32 devices in a mesh: section: 2 (over x), tensor: 4 (over y, core), dp: 4 (over z).
Axes of the slice: x: 2, y: 2, z: 4, core: 2. Of those that a mesh axis runs over, the one named last changes fastest.
Arguments:
- patches: bfloat16 [32, 102, 768], P('dp'), may hold values from -6 to 6
- cotangent: bfloat16 [32, 512, 512], P('dp'), may hold values from -6 to 6
- widths: int32 [32], P('dp'), may hold values from 4 to 8, as said below
- visible: int32 [32, 102], P('dp'), may hold values from 0 to 511, as said below
- window_shift: int32 [32, 2], P('dp'), may hold values from 0 to 3
- batch_order: int32 [4, 8], P('dp'), may hold values from 0 to 7, each once within a row
- encoder_qkv: bfloat16 [768, 3, 768], P(None, None, 'tensor'), may hold values from -0.21875 to 0.21875
- encoder_qvbias: bfloat16 [2, 768], P(None, 'tensor'), may hold values from -1.796875 to 1.796875
- encoder_proj: bfloat16 [768, 768], P('tensor'), may hold values from -0.625 to 0.625
- encoder_up: bfloat16 [768, 3072], P(None, 'tensor'), may hold values from -0.21875 to 0.21875
- encoder_upbias: bfloat16 [3072], P('tensor'), may hold values from -1.796875 to 1.796875
- encoder_down: bfloat16 [3072, 768], P('tensor'), may hold values from -0.109375 to 0.109375
- encoder_gains: bfloat16 [2, 768], replicated, may hold values from 0.099609375 to 1.8984375
- encoder_offsets: bfloat16 [4, 768], replicated, may hold values from -1.796875 to 1.796875
- decoder_qkv: bfloat16 [512, 3, 512], P(None, None, 'tensor'), may hold values from -0.25 to 0.25
- decoder_qvbias: bfloat16 [2, 512], P(None, 'tensor'), may hold values from -1.796875 to 1.796875
- decoder_proj: bfloat16 [512, 512], P('tensor'), may hold values from -0.5 to 0.5
- decoder_up: bfloat16 [512, 2048], P(None, 'tensor'), may hold values from -0.25 to 0.25
- decoder_upbias: bfloat16 [2048], P('tensor'), may hold values from -1.796875 to 1.796875
- decoder_down: bfloat16 [2048, 512], P('tensor'), may hold values from -0.125 to 0.125
- decoder_gains: bfloat16 [2, 512], replicated, may hold values from 0.099609375 to 1.8984375
- decoder_offsets: bfloat16 [4, 512], replicated, may hold values from -1.796875 to 1.796875
- embed_weight: bfloat16 [768, 512], replicated, may hold values from -0.21875 to 0.21875
- embed_vectors: bfloat16 [2, 512], replicated, may hold values from -3 to 3
Outputs:
- decoded: bfloat16 [32, 512, 512], P('dp', None, ('section', 'tensor'))
- patches_grad: bfloat16 [32, 102, 768], P('dp', None, ('section', 'tensor'))
- encoder_qkv_grad: float32 [768, 3, 768], P(None, None, 'tensor')
- encoder_qvbias_grad: float32 [2, 768], P(None, 'tensor')
- encoder_proj_grad: float32 [768, 768], P('tensor')
- encoder_up_grad: float32 [768, 3072], P(None, 'tensor')
- encoder_upbias_grad: float32 [3072], P('tensor')
- encoder_down_grad: float32 [3072, 768], P('tensor')
- encoder_gains_grad: float32 [2, 768], replicated
- encoder_offsets_grad: float32 [4, 768], replicated
- decoder_qkv_grad: float32 [512, 3, 512], P(None, None, 'tensor')
- decoder_qvbias_grad: float32 [2, 512], P(None, 'tensor')
- decoder_proj_grad: float32 [512, 512], P('tensor')
- decoder_up_grad: float32 [512, 2048], P(None, 'tensor')
- decoder_upbias_grad: float32 [2048], P('tensor')
- decoder_down_grad: float32 [2048, 512], P('tensor')
- decoder_gains_grad: float32 [2, 512], replicated
- decoder_offsets_grad: float32 [4, 512], replicated
- embed_weight_grad: float32 [768, 512], replicated
- embed_vectors_grad: float32 [2, 512], replicated
The draws below stay inside these ranges and needn't reach their ends.
Inputs may be any that keep to these rules, and one draw needn't show every extreme that they name: `widths`: each clip's grid is 64 rows by its width, which is 8 or 4. `visible`: within a clip the 102 entries are distinct. For a clip of width w the first 102 * w // 8 entries lie below 64 * w and the others at or above it. `batch_order`: each row is a permutation of the 8 clips of one index of dp.
All inputs are finite; a program needn't handle non-finite values.
Results may differ from the reference program's by a relative error of at most 0.025.
Values may be sent and summed in bfloat16 or wider, within the bound.
A program may use at most 256 MiB of HBM per device.

```python
import math
import jax
import jax.numpy as jnp
from jax import lax

D = 768
HEADS = 12
FF = 3072
DD = 512
DHEADS = 16
DFF = 2048
GRID_ROWS = 64
WIDE = 8
WIN = 4
VIS = 102
MB = 2
CPD = 8
CM = 4
GRID = 512
CLIPS = 32
N_DP = 4


def clip_widths(key):
    key = jax.random.fold_in(key, 7)
    pick = jax.random.randint(key, (CLIPS,), 0, 3)
    wide = jnp.where(pick > 0, WIDE, WIDE // 2).astype(jnp.int32)
    return wide.at[0].set(WIDE).at[1].set(WIDE // 2)


def draw_widths(key, part):
    shared = clip_widths(key)
    return shared


def draw_visible(key, part):
    shared = clip_widths(key)
    key = jax.random.fold_in(key, 2)

    def one(index):
        sub = jax.random.fold_in(key, index)
        whole = jax.random.permutation(jax.random.fold_in(sub, 0), GRID)[:VIS]
        lower = jax.random.permutation(jax.random.fold_in(sub, 1), GRID // 2)[:VIS // 2]
        upper = GRID // 2 + jax.random.permutation(jax.random.fold_in(sub, 2), GRID // 2)[:VIS // 2]
        return (whole.astype(jnp.int32), jnp.concatenate([lower, upper]).astype(jnp.int32))
    whole, narrow = jax.vmap(one)(jnp.arange(CLIPS, dtype=jnp.int32))
    return jnp.where((shared == WIDE)[:, None], whole, narrow).astype(jnp.int32)


def set_ends(result, own_key, least, high):
    dims = result.shape
    place = [jax.random.randint(jax.random.fold_in(own_key, axis), (), 0, dims[axis]) for axis in range(len(dims))]
    result = result.at[tuple(place)].set(least)
    longest = dims.index(max(dims))
    place[longest] = (place[longest] + 1) % dims[longest]
    return result.at[tuple(place)].set(high)


def steps_of(rng, dims, pieces, smallest, largest):
    level = 1.0
    for position, blocks in pieces:
        draws = jax.random.uniform(jax.random.fold_in(jax.random.fold_in(rng, 6), position), (blocks,), jnp.float32, smallest / len(pieces), largest / len(pieces))
        level = level * jnp.repeat(jnp.exp(draws), dims[position] // blocks).reshape((-1,) + (1,) * (len(dims) - 1 - position))
    return level


def gaussian(rng, extent, scale, limit, shards=(), kind=jnp.bfloat16):
    array = jax.random.normal(rng, extent, jnp.float32) * scale
    if len(shards) > 0:
        array = steps_of(rng, extent, shards, -0.22, 0.18) * array
    return jnp.clip(array, min=-limit, max=limit).astype(kind)


def setup_inputs(seed: int = 0) -> dict:
    streams_of = jax.random.split(jax.random.key(seed), 25)
    return {
        "patches": gaussian(streams_of[0], (CLIPS, VIS, D), 1.0, 6.0, ((0, 4),)),
        "cotangent": gaussian(streams_of[1], (CLIPS, GRID, DD), 1.0, 6.0, ((0, 4),)),
        "widths": draw_widths(jax.random.fold_in(streams_of[24], 71), 0),
        "visible": draw_visible(jax.random.fold_in(streams_of[24], 71), 0),
        "window_shift": set_ends(jax.random.randint(streams_of[4], (CLIPS, 2), 0, WIN), jax.random.fold_in(streams_of[4], 1), 0, WIN - 1).astype(jnp.int32),
        "batch_order": jax.vmap(lambda own: jax.random.permutation(own, CPD))(jax.random.split(streams_of[5], N_DP)).reshape((N_DP, CPD)).astype(jnp.int32),
        "encoder_qkv": gaussian(streams_of[6], (D, 3, D), D ** -0.5, 0.21875, ((2, 4),)),
        "encoder_qvbias": gaussian(streams_of[7], (2, D), 0.3, 1.796875, ((1, 4),)),
        "encoder_proj": gaussian(streams_of[8], (D, D), (D // 10) ** -0.5, 0.625, ((0, 4),)),
        "encoder_up": gaussian(streams_of[9], (D, FF), D ** -0.5, 0.21875, ((1, 4),)),
        "encoder_upbias": gaussian(streams_of[10], (FF,), 0.3, 1.796875, ((0, 4),)),
        "encoder_down": gaussian(streams_of[11], (FF, D), FF ** -0.5, 0.109375, ((0, 4),)),
        "encoder_gains": jnp.clip(1.0 + 0.18 * jax.random.normal(streams_of[12], (2, D), jnp.float32), 0.099609375, 1.8984375).astype(jnp.bfloat16),
        "encoder_offsets": gaussian(streams_of[13], (4, D), 0.3, 1.796875),
        "decoder_qkv": gaussian(streams_of[14], (DD, 3, DD), DD ** -0.5, 0.25, ((2, 4),)),
        "decoder_qvbias": gaussian(streams_of[15], (2, DD), 0.3, 1.796875, ((1, 4),)),
        "decoder_proj": gaussian(streams_of[16], (DD, DD), (DD // 4) ** -0.5, 0.5, ((0, 4),)),
        "decoder_up": gaussian(streams_of[17], (DD, DFF), DD ** -0.5, 0.25, ((1, 4),)),
        "decoder_upbias": gaussian(streams_of[18], (DFF,), 0.3, 1.796875, ((0, 4),)),
        "decoder_down": gaussian(streams_of[19], (DFF, DD), DFF ** -0.5, 0.125, ((0, 4),)),
        "decoder_gains": jnp.clip(1.0 + 0.18 * jax.random.normal(streams_of[20], (2, DD), jnp.float32), 0.099609375, 1.8984375).astype(jnp.bfloat16),
        "decoder_offsets": gaussian(streams_of[21], (4, DD), 0.3, 1.796875),
        "embed_weight": gaussian(streams_of[22], (D, DD), D ** -0.5, 0.21875),
        "embed_vectors": gaussian(streams_of[23], (2, DD), 0.5, 3.0),
    }


EPS = 1e-06
NEG = -10000.0
HIGHEST = lax.Precision.HIGHEST

@jax.custom_vjp
def low(v):
    return lax.optimization_barrier(v.astype(jnp.bfloat16)).astype(jnp.float32)

@jax.custom_vjp
def low_back(v):
    return v

def low_keep(v):
    return (low(v), None)

def low_pass(kept, grad):
    return (grad,)

def back_keep(v):
    return (v, None)

def back_low(kept, grad):
    return (low(grad),)
low.defvjp(low_keep, low_pass)
low_back.defvjp(back_keep, back_low)

def layer_norm(value, gain, offset):
    center = value - lax.optimization_barrier(jnp.mean(value, -1, keepdims=True))
    spread = lax.optimization_barrier(jnp.mean(center * center, -1, keepdims=True))
    return center * lax.rsqrt(spread + EPS) * gain + offset

def position_table(width):
    slot = jnp.arange(GRID, dtype=jnp.int32)
    row = (slot // width).astype(jnp.float32)[:, None]
    column = (slot % width).astype(jnp.float32)[:, None]
    quarter = DD // 4
    freq = jnp.exp(jnp.arange(quarter, dtype=jnp.float32) * (-math.log(10000.0) / quarter))[None, :]
    return jnp.concatenate([jnp.sin(row * freq), jnp.cos(row * freq), jnp.sin(column * freq), jnp.cos(column * freq)], 1)

def window_mask(width, shift):
    slot = jnp.arange(GRID, dtype=jnp.int32)
    row = slot // width
    column = slot % width
    valid = slot < GRID_ROWS * width
    band = (row + shift[0]) // WIN
    strip = (column + shift[1]) // WIN
    return (band[:, None] == band[None, :]) & (strip[:, None] == strip[None, :]) & valid[None, :]

def block(layer, value, mask, heads):
    qkv, qv_bias, proj, up_matrix, up_bias, down_matrix, gains, offsets = layer
    rows, width = value.shape
    size = width // heads
    normed = low(layer_norm(value, gains[0], offsets[0]))
    mixed_in = jnp.einsum('rd,dkc->rkc', normed, qkv, precision=HIGHEST)
    query = low(low_back(mixed_in[:, 0] + qv_bias[0])).reshape(rows, heads, size)
    keys = low(low_back(mixed_in[:, 1])).reshape(rows, heads, size)
    values = low(low_back(mixed_in[:, 2] + qv_bias[1])).reshape(rows, heads, size)
    raw = low_back(jnp.einsum('shd,thd->hst', query, keys, precision=HIGHEST))
    score = jnp.where(mask[None], raw * size ** (-0.5), NEG)
    top = lax.optimization_barrier(jnp.max(score, -1, keepdims=True))
    expo = jnp.exp(score - top)
    prob = expo / lax.optimization_barrier(jnp.sum(expo, -1, keepdims=True))
    mixed = jnp.einsum('hst,thd->shd', low(low_back(prob)), values, precision=HIGHEST).reshape(rows, width)
    attn = low_back(jnp.dot(low(low_back(mixed)), proj, precision=HIGHEST))
    first = value + attn + offsets[2]
    normed_two = low(layer_norm(first, gains[1], offsets[1]))
    hidden = low_back(jnp.dot(normed_two, up_matrix, precision=HIGHEST)) + up_bias
    active = low(low_back(jax.nn.gelu(hidden, approximate=False)))
    return first + low_back(jnp.dot(active, down_matrix, precision=HIGHEST)) + offsets[3]

def clip_forward(params, patch, width, slots, shift):
    enc_layer = params[0:8]
    dec_layer = params[8:16]
    embed_weight = params[16]
    embed_vectors = params[17]
    count = VIS * width // WIDE
    enc_mask = jnp.broadcast_to(jnp.arange(VIS, dtype=jnp.int32)[None, :] < count, (VIS, VIS))
    encoded = low(low_back(block(enc_layer, patch, enc_mask, HEADS)))
    embedded = jnp.dot(encoded, embed_weight, precision=HIGHEST) + embed_vectors[0]
    match = slots[:, None] == jnp.arange(GRID, dtype=jnp.int32)[None, :]
    hit = jnp.any(match, 0)
    source = lax.optimization_barrier(jnp.sum(jnp.where(match, jnp.arange(VIS, dtype=jnp.int32)[:, None], 0), 0)).astype(jnp.int32)
    filled = jnp.where(hit[:, None], embedded[source], embed_vectors[1][None, :])
    grid = low(low_back(filled))
    start = grid + position_table(width)
    out = block(dec_layer, start, window_mask(width, shift), DHEADS)
    valid = (jnp.arange(GRID, dtype=jnp.int32) < GRID_ROWS * width).astype(jnp.float32)
    return out * valid[:, None]

def reference(patches, cotangent, widths, visible, window_shift, batch_order, encoder_qkv, encoder_qvbias, encoder_proj, encoder_up, encoder_upbias, encoder_down, encoder_gains, encoder_offsets, decoder_qkv, decoder_qvbias, decoder_proj, decoder_up, decoder_upbias, decoder_down, decoder_gains, decoder_offsets, embed_weight, embed_vectors):
    weights = (encoder_qkv, encoder_qvbias, encoder_proj, encoder_up, encoder_upbias, encoder_down, encoder_gains, encoder_offsets, decoder_qkv, decoder_qvbias, decoder_proj, decoder_up, decoder_upbias, decoder_down, decoder_gains, decoder_offsets, embed_weight, embed_vectors)
    params = tuple((weight.astype(jnp.float32) for weight in weights))
    clip_ids = jnp.arange(N_DP, dtype=jnp.int32)[:, None] * CPD + batch_order
    grouped = widths[clip_ids].reshape(N_DP, MB, CM)
    counts = lax.optimization_barrier(jnp.sum(grouped, -1)) * GRID_ROWS
    factor_pos = jnp.repeat(CM * GRID / counts.astype(jnp.float32), CM, axis=1)
    factor = jnp.zeros((CLIPS,), jnp.float32).at[clip_ids.reshape(-1)].set(factor_pos.reshape(-1))

    def forward(params, source):

        def one(items):
            patch, width, slots, shift = items
            return clip_forward(params, patch, width, slots, shift)
        return lax.map(jax.checkpoint(one), (source, widths, visible, window_shift))
    source = patches.astype(jnp.float32)
    decoded, pullback = jax.vjp(forward, params, source)
    valid = (jnp.arange(GRID, dtype=jnp.int32)[None, :] < GRID_ROWS * widths[:, None]).astype(jnp.float32)
    loss_grad = cotangent.astype(jnp.float32) * valid[:, :, None] * factor[:, None, None]
    grads, source_grad = pullback(loss_grad)
    return (decoded.astype(jnp.bfloat16), source_grad.astype(jnp.bfloat16), grads[0], grads[1], grads[2], grads[3], grads[4], grads[5], grads[6], grads[7], grads[8], grads[9], grads[10], grads[11], grads[12], grads[13], grads[14], grads[15], grads[16], grads[17])
```

```python
import math

import jax
import jax.numpy as jnp
import numpy as np
from jax import lax
from jax.experimental import pallas as pl
from jax.experimental.pallas import tpu as pltpu
from jax.sharding import PartitionSpec as P

D = 768
HEADS = 12
DD = 512
DHEADS = 16
GRID_ROWS = 64
WIDE = 8
WIN = 4
VIS = 102
CM = 4
GRID = 512
LANES = 4
PAD = 128
EPS = 1e-06
NEG = -10000.0
F32 = jnp.float32
BF16 = jnp.bfloat16
VMEM_LIMIT = 60 * 1024 * 1024

VM = pl.BlockSpec(memory_space=pltpu.VMEM)
SM = pl.BlockSpec(memory_space=pltpu.SMEM)
ANY = pl.BlockSpec(memory_space=pl.ANY)


def nn(a, b):
    return lax.dot_general(a, b, (((1,), (0,)), ((), ())), preferred_element_type=F32)


def nt(a, b):
    return lax.dot_general(a, b, (((1,), (1,)), ((), ())), preferred_element_type=F32)


def tn(a, b):
    return lax.dot_general(a, b, (((0,), (0,)), ((), ())), preferred_element_type=F32)


def loop(count, body):
    def step(i, carry):
        body(i)
        return carry

    lax.fori_loop(0, count, step, 0)


def span(i, size):
    return pl.ds(pl.multiple_of(i * size, size), size)


def normal(x):
    center = x - jnp.mean(x, -1, keepdims=True)
    scale = lax.rsqrt(jnp.mean(center * center, -1, keepdims=True) + EPS)
    return center * scale, scale


def normal_back(dy, hat, scale, gain):
    d = dy * gain
    return scale * (
        d - jnp.mean(d, -1, keepdims=True) - hat * jnp.mean(d * hat, -1, keepdims=True)
    )


def gelu_both(h):
    bell = jnp.exp(h * h * -0.5)
    t = 1.0 / (1.0 + jnp.abs(h) * (0.3275911 * math.sqrt(0.5)))
    poly = t * (
        0.127414796
        + t * (-0.142248368 + t * (0.7107068705 + t * (-0.7265760135 + t * 0.5307027145)))
    )
    tail = poly * bell
    phi = jnp.where(h >= 0, 1.0 - tail, tail)
    return h * phi, phi + h * bell * (1.0 / math.sqrt(2.0 * math.pi))


def colsum(x):
    return jnp.sum(x, 0, keepdims=True)


def head_marks(width, size, dtype):
    lane = lax.broadcasted_iota(jnp.int32, (1, width), 1)
    return [((lane >= h * size) & (lane < (h + 1) * size)).astype(dtype) for h in range(width // size)]


def stacked(x, marks):
    return jnp.concatenate([x * m for m in marks], 0)


def softmax(s):
    e = jnp.exp(s - jnp.max(s, -1, keepdims=True))
    return e * (1.0 / jnp.sum(e, -1, keepdims=True))


def attend(q, k, v, marks, shape_scores):
    stack = stacked(k, marks)
    s = nt(q, stack)
    keys = k.shape[0]
    p = jnp.concatenate(
        [
            softmax(shape_scores(s[:, h * keys : (h + 1) * keys])).astype(BF16)
            for h in range(len(marks))
        ],
        1,
    )
    return p, nn(p, stacked(v, marks)).astype(BF16)


def attend_back(q, k, v, p, d_out, marks, marks32, scale):
    keys = k.shape[0]
    d_p = nt(d_out, stacked(v, marks))
    parts = []
    for h in range(len(marks)):
        cut = slice(h * keys, (h + 1) * keys)
        ph = p[:, cut].astype(F32)
        dh = d_p[:, cut]
        inner = jnp.sum(ph * dh, -1, keepdims=True)
        parts.append((ph * (dh - inner) * scale).astype(BF16))
    dr = jnp.concatenate(parts, 1)
    d_q = nn(dr, stacked(k, marks))
    d_k_all = tn(dr, q)
    d_v_all = tn(p, d_out)
    d_k = 0.0
    d_v = 0.0
    for h in range(len(marks)):
        cut = slice(h * keys, (h + 1) * keys)
        d_k += d_k_all[cut] * marks32[h]
        d_v += d_v_all[cut] * marks32[h]
    return d_q.astype(BF16), d_k.astype(BF16), d_v.astype(BF16)


ENC_SIZE = D // HEADS
ENC_SCALE = ENC_SIZE ** -0.5
DEC_SIZE = DD // DHEADS
DEC_SCALE = DEC_SIZE ** -0.5


def attend_flat(q, k, v, marks, rows32, allowed, scale):
    keys = k.shape[0]
    s = nt(stacked(k, marks), q)
    parts = []
    for h in range(len(marks)):
        x = jnp.where(allowed, s[h * keys : (h + 1) * keys] * scale, NEG)
        e = jnp.exp(x - jnp.max(x, 0, keepdims=True))
        parts.append((e * (1.0 / jnp.sum(e, 0, keepdims=True))).astype(BF16))
    p = jnp.concatenate(parts, 0)
    turned = jnp.transpose(v.astype(F32))
    wide = jnp.concatenate([(turned * m).astype(BF16) for m in rows32], 1)
    return p, nn(wide, p).astype(BF16)


def attend_flat_back(q, k, v, p, d_out, marks, marks32, rows32, scale):
    keys = k.shape[0]
    d_p = nt(stacked(v, marks), d_out)
    parts = []
    for h in range(len(marks)):
        cut = slice(h * keys, (h + 1) * keys)
        ph = p[cut].astype(F32)
        dh = d_p[cut]
        inner = jnp.sum(ph * dh, 0, keepdims=True)
        parts.append((ph * (dh - inner) * scale).astype(BF16))
    dr = jnp.concatenate(parts, 0)
    turned = jnp.transpose(k.astype(F32))
    wide = jnp.concatenate([(turned * m).astype(BF16) for m in rows32], 1)
    d_q = jnp.transpose(nn(wide, dr))
    d_k_all = nn(dr, q)
    d_v_all = nn(p, d_out)
    d_k = 0.0
    d_v = 0.0
    for h in range(len(marks)):
        cut = slice(h * keys, (h + 1) * keys)
        d_k += d_k_all[cut] * marks32[h]
        d_v += d_v_all[cut] * marks32[h]
    return d_q.astype(BF16), d_k.astype(BF16), d_v.astype(BF16)


MESH = pl.DeviceIdType.MESH


def far(src, dst, send, recv, peer):
    return pltpu.make_async_remote_copy(
        src_ref=src, dst_ref=dst, send_sem=send, recv_sem=recv, device_id=peer, device_id_type=MESH
    )


def forward_and_decoder(
    wid, shifts, order, vis, pat, gains, offs, b_qv, b_up, b_dqv, b_dup,
    h_qkv, h_proj, h_up, h_down, h_dqkv, h_dproj, h_dup, h_ddown,
    cot_hbm, ew, evec, table, dgains, doffs,
    o_x, o_x1, o_a, o_u, o_y, o_gp, o_qkv, o_p, o_o, o_w, o_wproj, o_wup, o_wdown, o_dec,
    d_enc, d_qvb, d_upb, d_small, dec_out,
    w_qkv, w_proj, w_up, w_down, bias, biases, qkv, proj, up, down,
    ex, ea, eu, ey, egp, eqkv, ep, eo, ex1, epart, esend, erecv, esend2, erecv2, eown,
    cot, x0, x1, a, acts, probs, o, u, ut, y, gp, g32, gb, gt, acc, e_ref, hot, buf, dsend,
    load_s, out_s, cot_s, w_s, w_r, bias_s, bias_r, dw_s, dw_r, ex_s, ex_r, ex2_s, ex2_r, do_s, do_r,
):
    sec = lax.axis_index("section")
    lane = lax.axis_index("tensor")
    mate = lane + 1 - 2 * lax.rem(lane, 2)
    over = lax.rem(lane + 2, LANES)
    cross = lax.rem(mate + 2, LANES)
    me = sec * LANES + lane
    devices = 2 * LANES
    clip = me
    clips = (me, sec * LANES + over)

    def group_peer(step):
        peer = lax.rem(me + step, devices)
        return peer, {"section": lax.div(peer, LANES), "tensor": lax.rem(peer, LANES)}

    own = [
        pltpu.make_async_copy(src, dst.at[0], load_s.at[n])
        for n, (src, dst) in enumerate(
            ((h_qkv, w_qkv), (h_proj, w_proj), (h_up, w_up), (h_down, w_down))
        )
    ]

    def place(n, shard):
        thick = (128, 128, 512, 512)[n]
        cut = pl.ds(pl.multiple_of(shard * thick, thick), thick)
        return (qkv.at[:, :, cut], proj.at[cut, :], up.at[:, cut], down.at[cut, :])[n]

    shards = (h_dqkv, h_dproj, h_dup, h_ddown)
    keep = [
        pltpu.make_async_copy(shards[n], place(n, lane), load_s.at[4 + n]) for n in range(4)
    ]
    for copy in own + keep:
        copy.start()
    fetch = pltpu.make_async_copy(cot_hbm.at[clip], cot, cot_s)
    fetch.start()

    barrier = pltpu.get_barrier_semaphore()
    for step in range(1, devices):
        pl.semaphore_signal(barrier, inc=1, device_id_type=MESH, device_id=group_peer(step)[1])
    bias[...] = jnp.zeros_like(bias)
    half = w_proj.shape[1]
    bias[0:1, :] = b_up[...].astype(F32).reshape(1, -1)
    bias[1:3, 0:half] = b_qv[...].astype(F32)
    bias[3:4, 0:512] = b_dup[...].astype(F32).reshape(1, -1)
    bias[4:6, 0:128] = b_dqv[...].astype(F32)
    biases[lane] = bias[...]
    pl.semaphore_wait(barrier, devices - 1)

    def enc_weight(n):
        src = (h_qkv, h_proj, h_up, h_down)[n]
        dst = (w_qkv, w_proj, w_up, w_down)[n]
        return far(src, dst.at[1], w_s.at[n], w_r.at[n], {"tensor": mate})

    def bias_copy(step):
        return far(
            bias, biases.at[lane], bias_s.at[step], bias_r.at[step],
            {"tensor": lax.rem(lane + step, LANES)},
        )

    def dec_weight(n, kind):
        peer = over if kind == 0 else mate
        src = shards[n] if kind < 2 else place(n, over)
        dst = place(n, lane if kind < 2 else over)
        return far(src, dst, dw_s.at[3 * n + kind], dw_r.at[3 * n + kind], {"tensor": peer})

    enc_weight(0).start()
    for step in range(1, LANES):
        bias_copy(step).start()
    enc_weight(1).start()
    for n in (0, 1):
        dec_weight(n, 0).start()
    enc_weight(2).start()
    enc_weight(3).start()
    for n in range(4):
        dec_weight(n, 1).start()

    def pass_on(n):
        dec_weight(n, 0).wait_recv()
        dec_weight(n, 2).start()

    def arrived(n):
        keep[n].wait()
        dec_weight(n, 1).wait_recv()
        dec_weight(n, 2).wait_recv()

    egain = gains[...].astype(F32)
    eoff = offs[...].astype(F32)
    stride = pat.shape[0] // VIS
    for c in range(2):
        row = lax.broadcasted_iota(jnp.int32, (PAD, pat.shape[0]), 0)
        col = lax.broadcasted_iota(jnp.int32, (PAD, pat.shape[0]), 1)
        pick = (col == row * stride + clips[c]).astype(F32).astype(BF16)
        ex[c * PAD : (c + 1) * PAD, :] = nn(pick, pat[...])

    def enc_norm(i):
        r = span(i, 64)
        hat, _ = normal(ex[r, :])
        ea[r, :] = (hat * egain[0:1] + eoff[0:1]).astype(BF16)

    loop(2 * PAD // 64, enc_norm)
    emarks = head_marks(half, ENC_SIZE, BF16)
    key = lax.broadcasted_iota(jnp.int32, (PAD, PAD), 1)
    floor = jnp.where(key < VIS, NEG, -1e30)
    for g, shard in enumerate((lane, mate)):
        if g == 0:
            own[0].wait()
            bq, bv = bias[1:2, 0:half], bias[2:3, 0:half]
        else:
            enc_weight(0).wait_recv()
            for step in range(1, LANES):
                bias_copy(step).wait_recv()
            bq, bv = biases[shard, 1:2, 0:half], biases[shard, 2:3, 0:half]
        eqkv[g, 0] = (nt(ea[...], w_qkv[g, 0]) + bq).astype(BF16)
        eqkv[g, 1] = nt(ea[...], w_qkv[g, 1]).astype(BF16)
        eqkv[g, 2] = (nt(ea[...], w_qkv[g, 2]) + bv).astype(BF16)
        for c in range(2):
            limit = (VIS * wid[clips[c]]) // WIDE
            rows = slice(c * PAD, (c + 1) * PAD)
            p, out = attend(
                eqkv[g, 0, rows], eqkv[g, 1, rows], eqkv[g, 2, rows], emarks,
                lambda s: jnp.where(key < limit, s * ENC_SCALE, floor),
            )
            ep[g, c] = p
            eo[g, rows] = out
    own[1].wait()
    enc_weight(1).wait_recv()

    def give_part(i, side):
        cut = span(i, 256)
        return far(
            esend.at[(1 - side) * PAD : (2 - side) * PAD, cut],
            erecv.at[side * PAD : (side + 1) * PAD, cut],
            ex_s.at[2 * i + side], ex_r.at[2 * i + side], {"tensor": over},
        )

    def enc_mix(i):
        c = span(i, 256)
        t = nn(eo[0], w_proj[0, :, c]) + nn(eo[1], w_proj[1, :, c])
        epart[:, c] = t
        esend[:, c] = t.astype(BF16)
        give_part(i, 0).start()
        give_part(i, 1).start()

    blocks = D // 256
    loop(blocks, enc_mix)
    pass_on(0)
    for i in range(blocks):
        give_part(i, 0).wait_recv()
        give_part(i, 1).wait_recv()
    dec_weight(2, 0).start()

    def enc_norm_two(i):
        r = span(i, 64)
        t = ex[r, :] + epart[r, :] + erecv[r, :].astype(F32) + eoff[2:3]
        ex1[r, :] = t
        hat, _ = normal(t)
        eu[r, :] = (hat * egain[1:2] + eoff[1:2]).astype(BF16)

    loop(2 * PAD // 64, enc_norm_two)
    own[2].wait()
    enc_weight(2).wait_recv()
    for g, shard in enumerate((lane, mate)):

        def enc_ff(i, g=g, shard=shard):
            c = span(i, 256)
            h = nn(eu[...], w_up[g, :, c]) + biases[shard, 0:1, c]
            act, slope = gelu_both(h)
            ey[g, :, c] = act.astype(BF16)
            egp[g, :, c] = slope.astype(BF16)

        loop(w_up.shape[2] // 256, enc_ff)
    own[3].wait()
    enc_weight(3).wait_recv()

    def give_last(i):
        cut = span(i, 256)
        return far(
            esend2.at[:, cut], erecv2.at[:, cut], ex2_s.at[i], ex2_r.at[i], {"tensor": over}
        )

    def enc_out(i):
        c = span(i, 256)
        t = nn(ey[0], w_down[0, :, c]) + nn(ey[1], w_down[1, :, c])
        eown[:, c] = t[:PAD]
        esend2[:, c] = t[PAD:].astype(BF16)
        give_last(i).start()

    loop(blocks, enc_out)
    outs = [
        pltpu.make_async_copy(src, dst, out_s.at[n])
        for n, (src, dst) in enumerate(
            (
                (ex.at[0:PAD, :], o_x), (ex1, o_x1), (ea, o_a), (eu, o_u), (ey, o_y), (egp, o_gp),
                (eqkv, o_qkv), (ep, o_p), (eo, o_o), (w_qkv.at[1], o_w), (w_proj.at[1], o_wproj),
                (w_up.at[1], o_wup), (w_down.at[1], o_wdown),
            )
        )
    ]
    for copy in outs:
        copy.start()
    pass_on(1)
    pass_on(2)
    for i in range(blocks):
        give_last(i).wait_recv()
    dec_weight(3, 0).start()

    width = wid[clip]
    bits = jnp.where(width == WIDE, 3, 2)
    turn = shifts[clip, 0] * width
    mod = GRID - 1
    spot = 0
    for i in range(order.shape[1]):
        spot = spot + jnp.where(order[0, i] == clip, i, 0)
    batch = spot // CM
    count = 0
    for i in range(order.shape[1]):
        count = count + jnp.where(batch == i // CM, wid[order[0, i]], 0)
    factor_rows = CM * GRID / (jnp.full((1, 1), count, jnp.int32) * GRID_ROWS).astype(F32)

    def slot_of(index):
        return (index - turn) & mod

    def code_of(slot):
        band = ((slot >> bits) + shifts[clip, 0]) >> 2
        strip = ((slot & (width - 1)) + shifts[clip, 1]) >> 2
        return band * 4 + strip

    e_ref[...] = (ex1[0:PAD, :] + eown[...] + erecv2[...].astype(F32) + eoff[3:4]).astype(BF16)
    vec = evec[...].astype(F32)
    m = (nn(e_ref[...], ew[...]) + vec[0:1]).astype(BF16)
    seen = vis[pl.ds(clip, 1), :]
    target = jnp.concatenate([(seen + turn) & mod, jnp.full((1, PAD - VIS), -1, jnp.int32)], 1)
    gain = dgains[...].astype(F32)
    offsets = doffs[...].astype(F32)

    def start(i):
        r = span(i, PAD)
        index = lax.broadcasted_iota(jnp.int32, (PAD, PAD), 0) + i * PAD
        column = lax.broadcasted_iota(jnp.int32, (PAD, PAD), 1)
        match = index == target
        oh = match.astype(F32).astype(BF16)
        hot[r, :] = oh
        hit = jnp.sum(match.astype(F32), -1, keepdims=True)
        grid = jnp.where(hit > 0, nn(oh, m), vec[1:2]).astype(BF16).astype(F32)
        slot = slot_of(index)
        by_row = ((slot >> bits) == column).astype(F32).astype(BF16)
        by_col = ((slot & (width - 1)) == column).astype(F32).astype(BF16)
        row_part = nn(by_row, table[0]) + nn(by_row, table[1])
        col_part = nn(by_col, table[0]) + nn(by_col, table[1])
        x = grid + jnp.concatenate([row_part, col_part], 1)
        x0[r, :] = x
        hat, _ = normal(x)
        a[r, :] = (hat * gain[0:1] + offsets[0:1]).astype(BF16)

    loop(GRID // PAD, start)
    arrived(0)

    def dec_bias(row, size):
        return jnp.concatenate([biases[k, row : row + 1, 0:size] for k in range(LANES)], 1)

    def project(i):
        r = span(i, 256)
        rows = a[r, :]
        acts[0, r, :] = (nn(rows, qkv[0]) + dec_bias(4, 128)).astype(BF16)
        acts[1, r, :] = nn(rows, qkv[1]).astype(BF16)
        acts[2, r, :] = (nn(rows, qkv[2]) + dec_bias(5, 128)).astype(BF16)

    loop(2, project)
    pass_on(3)
    marks = head_marks(128, DEC_SIZE, BF16)
    marks32 = head_marks(128, DEC_SIZE, F32)
    dim = lax.broadcasted_iota(jnp.int32, (128, 1), 0)
    rows32 = [
        ((dim >= h * DEC_SIZE) & (dim < (h + 1) * DEC_SIZE)).astype(F32) for h in range(len(marks))
    ]

    def attention(i):
        r = span(i, PAD)
        key_slot = slot_of(lax.broadcasted_iota(jnp.int32, (PAD, PAD), 0) + i * PAD)
        row_slot = slot_of(lax.broadcasted_iota(jnp.int32, (PAD, PAD), 1) + i * PAD)
        allowed = (code_of(row_slot) == code_of(key_slot)) & (key_slot < GRID_ROWS * width)
        for g in range(DD // 128):
            c = slice(g * 128, (g + 1) * 128)
            p, out = attend_flat(
                acts[0, r, c], acts[1, r, c], acts[2, r, c], marks, rows32, allowed, DEC_SCALE
            )
            probs[i, g * 512 : (g + 1) * 512, :] = p
            o[c, r] = out

    loop(GRID // PAD, attention)
    arrived(1)

    def mix(i):
        r = span(i, PAD)
        x = x0[r, :] + tn(o[:, r], proj[...]) + offsets[2:3]
        x1[r, :] = x
        hat, _ = normal(x)
        un = hat * gain[1:2] + offsets[1:2]
        u[r, :] = un.astype(BF16)
        ut[:, r] = jnp.transpose(un).astype(BF16)

    loop(GRID // PAD, mix)
    arrived(2)

    def ff(i):
        k = lax.div(i, 4)
        side = lax.rem(lax.div(i, 2), 2)
        c = span(lax.div(i, 2), 256)
        r = span(lax.rem(i, 2), 256)
        h = nn(u[r, :], up[:, c]) + biases[k, 3:4, span(side, 256)]
        act, slope = gelu_both(h)
        y[r, c] = act.astype(BF16)
        gp[r, c] = slope.astype(BF16)

    loop(2 * up.shape[1] // 256, ff)
    arrived(3)
    fetch.wait()
    slot_col = slot_of(lax.broadcasted_iota(jnp.int32, (GRID, 1), 0))
    valid = (slot_col < GRID_ROWS * width).astype(F32)
    rolled = slot_of(lax.broadcasted_iota(jnp.int32, (GRID, GRID), 0))
    perm = (rolled == lax.broadcasted_iota(jnp.int32, (GRID, GRID), 1)).astype(F32).astype(BF16)

    def out(i):
        r = span(lax.rem(i, 2), 256)
        c = span(lax.div(i, 2), 256)
        acc[r, c] = nn(y[r, :], down[:, c])

    loop(4, out)
    full = ((acc[...] + x1[...] + offsets[3:4]) * valid).astype(BF16)
    turned = tn(full, perm).astype(BF16)
    for k in range(devices):
        dsend[k] = turned[k * dsend.shape[1] : (k + 1) * dsend.shape[1]]

    def decoded_copy(step):
        peer, spot = group_peer(step)
        return far(dsend.at[peer], dec_out.at[me], do_s.at[step], do_r.at[step], spot)

    for step in range(1, devices):
        decoded_copy(step).start()
    dec_out[me] = dsend[me]
    g = nn(perm, cot[...]) * valid * factor_rows
    g32[...] = g
    gb[...] = g.astype(BF16)
    gt[...] = jnp.transpose(g).astype(BF16)
    d_small[0:5, :] = jnp.zeros((5, DD), F32)
    d_small[5:6, :] = colsum(g)
    d_small[6:8, :] = jnp.zeros((2, DD), F32)

    def ff_back(i):
        c = span(i, 256)
        shard = lax.div(i, 2)
        side = lax.rem(i, 2)
        buf[shard, side, 0:512, 512:768] = nn(gt[...], y[:, c]).astype(BF16)
        dh = nt(gb[...], down[c, :]) * gp[:, c].astype(F32)
        d_upb[:, c] = colsum(dh)
        du = dh.astype(BF16)
        gp[:, c] = du
        buf[shard, 0, 0:512, span(side, 256)] = nn(ut[...], du).astype(BF16)

    loop(up.shape[1] // 256, ff_back)
    early = pltpu.make_async_copy(buf.at[:, 0, 0:512, :], o_dec.at[:, 0, 0:512, :], out_s.at[13])
    early.start()

    def ff_in(i):
        r = span(lax.rem(i, 2), 256)
        c = span(lax.div(i, 2), 256)
        acc[r, c] = nt(gp[r, :], up[c, :])

    loop(4, ff_in)

    def mix_back(i):
        r = span(i, PAD)
        hat, scale = normal(x1[r, :])
        da = acc[r, :]
        dx = g32[r, :] + normal_back(da, hat, scale, gain[1:2])
        d_small[1:2, :] += colsum(da * hat)
        d_small[3:4, :] += colsum(da)
        d_small[4:5, :] += colsum(dx)
        g32[r, :] = dx
        dxb = dx.astype(BF16)
        gb[r, :] = dxb
        u[r, :] = nt(dxb, proj[...]).astype(BF16)

    loop(GRID // PAD, mix_back)
    d_proj = nn(o[...], gb[...]).astype(BF16)
    for k in range(LANES):
        for j in range(LANES):
            block = d_proj[k * 128 : (k + 1) * 128, j * 128 : (j + 1) * 128]
            buf[k, 1, j * 128 : (j + 1) * 128, 384:512] = block

    def attention_back(i):
        r = span(i, PAD)
        for k in range(DD // 128):
            c = slice(k * 128, (k + 1) * 128)
            dq, dk, dv = attend_flat_back(
                acts[0, r, c], acts[1, r, c], acts[2, r, c],
                probs[i, k * 512 : (k + 1) * 512, :], u[r, c], marks, marks32, rows32, DEC_SCALE,
            )
            acts[0, r, c] = dq
            acts[1, r, c] = dk
            acts[2, r, c] = dv

    loop(GRID // PAD, attention_back)
    d_qvb[0:1, :] = colsum(acts[0].astype(F32))
    d_qvb[1:2, :] = colsum(acts[2].astype(F32))

    def project_back(i):
        r = span(lax.rem(i, 2), 256)
        c = span(lax.div(i, 2), 256)
        acc[r, c] = (
            nt(acts[0, r, :], qkv[0, c, :])
            + nt(acts[1, r, :], qkv[1, c, :])
            + nt(acts[2, r, :], qkv[2, c, :])
        )

    loop(4, project_back)
    gt[...] = jnp.transpose(a[...].astype(F32)).astype(BF16)
    for j in range(3):
        d_qkv = nn(gt[...], acts[j]).astype(BF16)
        for k in range(LANES):
            buf[k, 1, 0:512, j * 128 : (j + 1) * 128] = d_qkv[:, k * 128 : (k + 1) * 128]

    def start_back(i):
        r = span(i, PAD)
        hat, scale = normal(x0[r, :])
        da = acc[r, :]
        dx = g32[r, :] + normal_back(da, hat, scale, gain[0:1])
        d_small[0:1, :] += colsum(da * hat)
        d_small[2:3, :] += colsum(da)
        dg = dx.astype(BF16)
        gb[r, :] = dg
        hit = jnp.sum(hot[r, :].astype(F32), -1, keepdims=True)
        d_small[7:8, :] += colsum(jnp.where(hit > 0, 0.0, dg.astype(F32)))

    loop(GRID // PAD, start_back)
    dm = tn(hot[...], gb[...])
    d_small[6:7, :] = colsum(dm)
    dmb = dm.astype(BF16)
    d_enc[...] = nt(dmb, ew[...]).astype(BF16)
    d_ew = tn(e_ref[...], dmb).astype(BF16)
    for k in range(LANES):
        for h in range(2):
            top = k * 192 + h * 64
            buf[k, h, 512:576, 0:512] = d_ew[top : top + 64]
            buf[k, h, 512:576, 512:768] = d_ew[k * 192 + 128 : (k + 1) * 192, h * 256 : (h + 1) * 256]

    rest = [
        pltpu.make_async_copy(buf.at[:, 1], o_dec.at[:, 1], out_s.at[14]),
        pltpu.make_async_copy(buf.at[:, 0, 512:576, :], o_dec.at[:, 0, 512:576, :], out_s.at[15]),
    ]
    for copy in rest:
        copy.start()
    for copy in outs + [early] + rest:
        copy.wait()
    for n in range(4):
        enc_weight(n).wait_send()
        for kind in range(3):
            dec_weight(n, kind).wait_send()
    for step in range(1, LANES):
        bias_copy(step).wait_send()
    for i in range(blocks):
        give_part(i, 0).wait_send()
        give_part(i, 1).wait_send()
        give_last(i).wait_send()
    for step in range(1, devices):
        decoded_copy(step).wait()


def forward_call(args, half, hid, dff):
    dma = lambda *s: pltpu.SemaphoreType.DMA(s)
    vm = lambda dtype, *shape: pltpu.VMEM(shape, dtype)
    rows = 2 * PAD
    keys = PAD * half // ENC_SIZE
    devices = 2 * LANES
    slab = DD // devices
    kept = [
        ((PAD, D), F32), ((rows, D), F32), ((rows, D), BF16), ((rows, D), BF16),
        ((2, rows, hid), BF16), ((2, rows, hid), BF16), ((2, 3, rows, half), BF16),
        ((2, 2, PAD, keys), BF16), ((2, rows, half), BF16),
        ((3, half, D), BF16), ((half, D), BF16), ((D, hid), BF16), ((hid, D), BF16),
        ((LANES, 2, DEC_ROWS, D), BF16),
    ]
    made = [
        ((PAD, D), BF16), ((2, DD), F32), ((1, dff), F32), ((8, DD), F32),
        ((devices, slab, GRID), BF16),
    ]
    return pl.pallas_call(
        forward_and_decoder,
        out_shape=[jax.ShapeDtypeStruct(s, d) for s, d in kept + made],
        in_specs=[SM, SM, SM] + [VM] * 8 + [ANY] * 9 + [VM] * 5,
        out_specs=[ANY] * len(kept) + [VM] * len(made),
        scratch_shapes=[
            vm(BF16, 2, 3, half, D), vm(BF16, 2, half, D), vm(BF16, 2, D, hid), vm(BF16, 2, hid, D),
            vm(F32, 8, D), vm(F32, LANES, 8, D),
            vm(BF16, 3, DD, DD), vm(BF16, DD, DD), vm(BF16, DD, dff), vm(BF16, dff, DD),
            vm(F32, rows, D), vm(BF16, rows, D), vm(BF16, rows, D), vm(BF16, 2, rows, hid),
            vm(BF16, 2, rows, hid), vm(BF16, 2, 3, rows, half), vm(BF16, 2, 2, PAD, keys),
            vm(BF16, 2, rows, half), vm(F32, rows, D), vm(F32, rows, D), vm(BF16, rows, D),
            vm(BF16, rows, D), vm(BF16, PAD, D), vm(BF16, PAD, D), vm(F32, PAD, D),
            vm(BF16, GRID, DD), vm(F32, GRID, DD), vm(F32, GRID, DD), vm(BF16, GRID, DD),
            vm(BF16, 3, GRID, DD), vm(BF16, GRID // PAD, DHEADS * PAD, PAD), vm(BF16, DD, GRID),
            vm(BF16, GRID, DD), vm(BF16, DD, GRID), vm(BF16, GRID, dff), vm(BF16, GRID, dff),
            vm(F32, GRID, DD), vm(BF16, GRID, DD), vm(BF16, DD, GRID), vm(F32, GRID, DD),
            vm(BF16, PAD, D), vm(BF16, GRID, PAD), vm(BF16, LANES, 2, DEC_ROWS, D),
            vm(BF16, devices, slab, GRID),
            dma(8), dma(16), pltpu.SemaphoreType.DMA, dma(4), dma(4), dma(LANES), dma(LANES),
            dma(12), dma(12), dma(6), dma(6), dma(3), dma(3), dma(devices), dma(devices),
        ],
        compiler_params=pltpu.CompilerParams(
            collective_id=0, has_side_effects=True, vmem_limit_bytes=VMEM_LIMIT
        ),
    )(*args)


CH = 64
DEC_ROWS = 576
ENC_A = 768
ENC_B = 384
DEC_K = DEC_ROWS // CH
B_K = (DEC_ROWS + ENC_A + ENC_B) // CH
ALL_K = B_K + 1
A_TOP = DEC_ROWS
B_TOP = DEC_ROWS + ENC_A
S_TOP = B_TOP + ENC_B
LAG = 2
LEAD = 4
MIXED = LEAD + 2 * (DEC_K - LEAD)


def add(x, y):
    return (x.astype(F32) + y.astype(F32)).astype(BF16)


def backward_and_sums(
    d_enc, x, x1, a, u, y, gp, qkv, p, o, gains, offs,
    w0, w1, proj0, proj1, up0, up1, down0, down1,
    dec, dec_qvb, dec_upb, dec_small,
    out, emb, dx_out,
    gb, gt, ut, part, send, recv, du, gx, dx1, d_o, d_acts, own, send1, recv1, dx32, dx,
    d_upb, d_qvb, d_small,
    acc, yacc, enc_mate, rcy, ry, rx, zl, zr, xc, cl, cr, small32, small,
    load_s, ex_s, ex_r,
    core_s, core_r, corey_s, corey_r, y_s, y_r, x_s, x_r, z_s, zl_r, zr_r,
    bl_s, br_s, b_r, a_s, a_r, emb_s, emb_r, dx_s, dx_r,
):
    sec = lax.axis_index("section")
    lane = lax.axis_index("tensor")
    pos = lax.axis_index("dp")
    count = lax.axis_size("dp")
    mate = lane + 1 - 2 * lax.rem(lane, 2)
    over = lax.rem(lane + 2, LANES)
    cross = lax.rem(mate + 2, LANES)
    first = pos == 0
    last = pos == count - 1
    me = sec * LANES + lane
    devices = 2 * LANES

    def group_peer(step):
        peer = lax.rem(me + step, devices)
        return peer, {"section": lax.div(peer, LANES), "tensor": lax.rem(peer, LANES)}

    barrier = pltpu.get_barrier_semaphore()
    for step in range(1, devices):
        pl.semaphore_signal(barrier, inc=1, device_id_type=MESH, device_id=group_peer(step)[1])

    @pl.when(pos > 0)
    def _():
        pl.semaphore_signal(barrier, inc=1, device_id={"dp": pos - 1}, device_id_type=MESH)

    @pl.when(pos < count - 1)
    def _():
        pl.semaphore_signal(barrier, inc=1, device_id={"dp": pos + 1}, device_id_type=MESH)

    loads = [
        pltpu.make_async_copy(dec.at[lane], acc.at[:, 0:DEC_ROWS, :], load_s.at[0]),
        pltpu.make_async_copy(dec.at[over], yacc.at[:, 0:DEC_ROWS, :], load_s.at[1]),
    ]
    for load in loads:
        load.start()
    small32[...] = jnp.zeros_like(small32)
    small[...] = jnp.zeros_like(small)
    d_small[...] = jnp.zeros_like(d_small)
    gb[0:PAD, :] = d_enc[...]
    ends = jnp.where(first, 0, 1) + jnp.where(last, 0, 1)
    pl.semaphore_wait(barrier, devices - 1 + ends)

    gain = gains[...].astype(F32)
    width = w0.shape[1]
    marks = head_marks(width, ENC_SIZE, BF16)
    marks32 = head_marks(width, ENC_SIZE, F32)

    def rows(k, size=CH):
        return pl.ds(pl.multiple_of(k * size, size), size)

    def give_enc():
        return far(d_enc, gb.at[PAD : 2 * PAD, :], ex_s.at[0], ex_r.at[0], {"tensor": over})

    def give_part(i, half):
        cut = rows(i, 256)
        n = 1 + 2 * i + half
        return far(
            send.at[(1 - half) * PAD : (2 - half) * PAD, cut],
            recv.at[half * PAD : (half + 1) * PAD, cut],
            ex_s.at[n], ex_r.at[n], {"tensor": over},
        )

    def give_last(i):
        cut = rows(i, 256)
        return far(send1.at[:, cut], recv1.at[:, cut], ex_s.at[7 + i], ex_r.at[7 + i], {"tensor": over})

    def ff_back(g, i, down):
        c = rows(i, 256)
        d_down = nn(gt[...], y[g, :, c]).astype(BF16)
        dh = nt(gb[...], down[c, :]) * gp[g, :, c].astype(F32)
        d_upb[g, :, c] = colsum(dh)
        dub = dh.astype(BF16)
        du[g, :, c] = dub
        d_up = nn(ut[...], dub).astype(BF16)
        if g == 0:
            acc[1, A_TOP:B_TOP, c] = d_down
            acc[0, A_TOP:B_TOP, c] = d_up
        else:
            enc_mate[1, 0:ENC_A, c] = d_down
            enc_mate[0, 0:ENC_A, c] = d_up

    def ff_in(i):
        c = rows(i, 256)
        t = nt(du[0], up0[c, :]) + nt(du[1], up1[c, :])
        part[:, c] = t
        send[:, c] = t.astype(BF16)
        give_part(i, 0).start()
        give_part(i, 1).start()

    def norm_two(i):
        del i
        for k in range(D // 256):
            give_part(k, 0).wait_recv()
            give_part(k, 1).wait_recv()

        def body(j):
            r = rows(j, 64)
            da = part[r, :] + recv[r, :].astype(F32)
            hat, scale = normal(x1[r, :])
            g = gb[r, :].astype(F32)
            d = g + normal_back(da, hat, scale, gain[1:2])
            gx[r, :] = d.astype(BF16)
            dx1[r, :] = d

            @pl.when(j < 2)
            def _():
                d_small[1:2, :] += colsum(da * hat)
                d_small[3:4, :] += colsum(da)
                d_small[4:5, :] += colsum(d)
                d_small[5:6, :] += colsum(g)

        loop(2 * PAD // 64, body)

    def attention(g, proj):
        d_proj = tn(o[g], gx[...]).astype(BF16)
        if g == 0:
            acc[1, B_TOP + width : S_TOP, :] = d_proj
        else:
            enc_mate[1, ENC_A + width : ENC_A + 2 * width, :] = d_proj
        d_o[...] = nt(gx[...], proj[...]).astype(BF16)
        for c in range(2):
            r = slice(c * PAD, (c + 1) * PAD)
            dq, dk, dv = attend_back(
                qkv[g, 0, r], qkv[g, 1, r], qkv[g, 2, r], p[g, c], d_o[r, :],
                marks, marks32, ENC_SCALE,
            )
            d_acts[g, 0, r] = dq
            d_acts[g, 1, r] = dk
            d_acts[g, 2, r] = dv
        d_qvb[g, 0:1, :] = colsum(d_acts[g, 0].astype(F32))
        d_qvb[g, 1:2, :] = colsum(d_acts[g, 2].astype(F32))

    def project_in(i):
        c = rows(i, 256)
        t = 0.0
        for g, w in enumerate((w0, w1)):
            for j in range(3):
                t += nn(d_acts[g, j], w[j, :, c])
        own[:, c] = t[:PAD]
        send1[:, c] = t[PAD:].astype(BF16)
        give_last(i).start()

    def project_grad(g):
        for j in range(3):
            row = (j % 2) * width
            d = tn(d_acts[g, j], a[...]).astype(BF16)
            if g == 0:
                acc[j // 2, B_TOP + row : B_TOP + row + width, :] = d
            else:
                enc_mate[j // 2, ENC_A + row : ENC_A + row + width, :] = d

    def norm_one(i):
        del i
        for k in range(D // 256):
            give_last(k).wait_recv()

        def body(j):
            r = rows(j, 64)
            da = own[r, :] + recv1[r, :].astype(F32)
            hat, scale = normal(x[r, :])
            d_small[0:1, :] += colsum(da * hat)
            d_small[2:3, :] += colsum(da)
            dx32[r, :] = dx1[r, :] + normal_back(da, hat, scale, gain[0:1])

        loop(PAD // 64, body)
        turned = jnp.transpose(dx32[...])
        cut = D // devices
        for k in range(devices):
            dx[k] = turned[k * cut : (k + 1) * cut, 0:VIS].astype(BF16)
        for r in range(LANES):
            small32[r, 0:1, 0:512] = dec_upb[:, r * 512 : (r + 1) * 512]
            small32[r, 1:2, 0:128] = dec_qvb[0:1, r * 128 : (r + 1) * 128]
            small32[r, 1:2, 128:256] = dec_qvb[1:2, r * 128 : (r + 1) * 128]
            small32[r, 8:16, 0:512] = dec_small[...]
            small32[r, 16:24, :] = d_small[...]
        for g, shard in enumerate((lane, mate)):
            small32[shard, 2:3, :] = d_upb[g]
            small32[shard, 3:4, 0:192] = d_qvb[g, 0:1]
            small32[shard, 3:4, 256:448] = d_qvb[g, 1:2]
        for r in range(LANES):
            small[r, 0, 0:32] = small32[r].astype(BF16)
        acc[:, S_TOP : S_TOP + CH, :] = small[lane]
        yacc[:, DEC_ROWS : DEC_ROWS + CH, :] = small[over]
        core_copy(ALL_K - 1, small.at[mate]).start()
        corey_copy(ALL_K - 1, small.at[cross]).start()
        for step in range(1, devices):
            dx_copy(step).start()
        dx_out[me] = dx[me]

    def core_enc(lo, hi):
        def body(m):
            block = block_of(m)

            @pl.when((block >= lo) & (block < hi))
            def _():
                src = pl.ds(pl.multiple_of(block * CH - DEC_ROWS, CH), CH)
                core_copy(m, enc_mate.at[:, src, :]).start()

        loop(ALL_K, body)

    def first_piece(i):
        del i
        ut[...] = jnp.transpose(u[...].astype(F32)).astype(BF16)
        give_enc().wait_recv()
        gt[...] = jnp.transpose(gb[...].astype(F32)).astype(BF16)

    pieces = [(0, 1, first_piece)]
    for g, down in enumerate((down0, down1)):
        pieces.append((0, 3, lambda i, g=g, down=down: ff_back(g, i, down)))
    pieces.append((3, 4, lambda i: core_enc(DEC_K, DEC_K + ENC_A // CH)))
    pieces.append((3, 4, lambda i: loop(D // 256, ff_in)))
    pieces.append((6, 7, norm_two))
    for g, proj in enumerate((proj0, proj1)):
        pieces.append((7 + g, 8 + g, lambda i, g=g, proj=proj: attention(g, proj)))
    pieces.append((9, 10, lambda i: loop(D // 256, project_in)))
    for g in range(2):
        pieces.append((10 + g, 11 + g, lambda i, g=g: project_grad(g)))
    pieces.append((12, 13, lambda i: core_enc(DEC_K + ENC_A // CH, B_K)))
    pieces.append((13, 14, norm_one))

    def dx_copy(step):
        peer, place = group_peer(step)
        return far(dx.at[peer], dx_out.at[me], dx_s.at[step], dx_r.at[step], place)

    def emb_copy(step):
        return far(
            out.at[:, pl.ds(512, CH), :], emb.at[lane], emb_s.at[step], emb_r.at[step],
            {"tensor": lax.rem(lane + step, LANES)},
        )

    def block_of(m):
        turn = jnp.where(lax.rem(m, 2) == 0, DEC_K + lax.div(m - LEAD, 2), LEAD + lax.div(m - LEAD - 1, 2))
        return jnp.where((m < LEAD) | (m >= MIXED), m, turn)

    def is_dec(m):
        return block_of(m) < DEC_K

    def with_y(m):
        return is_dec(m) | (m == ALL_K - 1)

    def at(m):
        return pl.ds(pl.multiple_of(block_of(m) * CH, CH), CH)

    def pair_at(m):
        return rows(lax.div(m, 2))

    def y_at(m):
        return rows(jnp.minimum(block_of(m), DEC_K))

    def core_copy(m, src):
        return far(src, out.at[:, at(m), :], core_s.at[m], core_r.at[m], {"tensor": mate})

    def corey_copy(m, src):
        return far(src, rcy.at[:, y_at(m), :], corey_s.at[m], corey_r.at[m], {"tensor": mate})

    def y_copy(m):
        cut = y_at(m)
        return far(
            yacc.at[:, cut, :], ry.at[:, cut, :], y_s.at[m], y_r.at[m], {"tensor": over}
        )

    def x_copy(m):
        return far(
            acc.at[1 - sec, at(m), :], rx.at[pair_at(m), :], x_s.at[m], x_r.at[m],
            {"section": 1 - sec},
        )

    def xc_copy(m):
        return far(
            acc.at[:, at(m), :], xc.at[:, pair_at(m), :], x_s.at[m], x_r.at[m],
            {"section": 1 - sec},
        )

    def z_copy(m, whole, right):
        if whole:
            src, dst = acc.at[:, at(m), :], (cl if right else cr).at[:, pair_at(m), :]
        else:
            src, dst = acc.at[sec, at(m), :], (zl if right else zr).at[pair_at(m), :]
        landed = zl_r if right else zr_r
        return far(src, dst, z_s.at[m], landed.at[m], {"dp": pos + 1 if right else pos - 1})

    def b_copy(m, whole, right):
        place = out.at[:, at(m), :] if whole else out.at[sec, at(m), :]
        sent = br_s if right else bl_s
        return far(place, place, sent.at[m], b_r.at[m], {"dp": pos + 1 if right else pos - 1})

    def a_copy(m):
        place = out.at[sec, at(m), :]
        return far(place, place, a_s.at[m], a_r.at[m], {"section": 1 - sec})

    def a_wait(m):
        place = out.at[1 - sec, at(m), :]
        far(place, place, a_s.at[m], a_r.at[m], {"section": 1 - sec}).wait_recv()

    give_enc().start()

    def start_core(m):
        @pl.when(is_dec(m))
        def _():
            core_copy(m, dec.at[mate, :, at(m), :]).start()
            corey_copy(m, dec.at[cross, :, at(m), :]).start()

    loop(MIXED, start_core)
    for load in loads:
        load.wait()

    def stage_c(m):
        core_copy(m, out.at[:, at(m), :]).wait_recv()
        acc[:, at(m), :] = add(acc[:, at(m), :], out[:, at(m), :])

        @pl.when(with_y(m))
        def _():
            corey_copy(m, rcy.at[:, y_at(m), :]).wait_recv()
            yacc[:, y_at(m), :] = add(yacc[:, y_at(m), :], rcy[:, y_at(m), :])
            y_copy(m).start()

    def finished(m):
        @pl.when(block_of(m) == DEC_K - 1)
        def _():
            for step in range(1, LANES):
                emb_copy(step).start()
            emb[lane] = out[:, 512 : 512 + CH, :]

    def line_of(root, whole):
        left = pos < root
        right = pos > root
        here = pos == root
        reach = max(root, count - 1 - root)
        level = jnp.where(left, pos, jnp.where(right, count - 1 - pos, reach))
        dist = jnp.where(left, root - pos, pos - root)

        def view(ref, m):
            return ref.at[:, at(m), :] if whole else ref.at[sec, at(m), :]

        def landed(ref, m):
            return ref.at[:, pair_at(m), :] if whole else ref.at[pair_at(m), :]

        from_left, from_right = (cl, cr) if whole else (zl, zr)

        def outer(m):
            @pl.when(left & first)
            def _():
                z_copy(m, whole, True).start()

            @pl.when(right & last)
            def _():
                z_copy(m, whole, False).start()

        def inward(m):
            @pl.when(left & (pos > 0))
            def _():
                z_copy(m, whole, True).wait_recv()
                view(acc, m)[...] = add(view(acc, m)[...], landed(from_left, m)[...])
                z_copy(m, whole, True).start()

            @pl.when(right & (pos < count - 1))
            def _():
                z_copy(m, whole, False).wait_recv()
                view(acc, m)[...] = add(view(acc, m)[...], landed(from_right, m)[...])
                z_copy(m, whole, False).start()

            @pl.when(here)
            def _():
                total = view(acc, m)[...].astype(F32)
                if root > 0:
                    z_copy(m, whole, True).wait_recv()
                    total = total + landed(from_left, m)[...].astype(F32)
                if root < count - 1:
                    z_copy(m, whole, False).wait_recv()
                    total = total + landed(from_right, m)[...].astype(F32)
                if whole:
                    view(acc, m)[...] = total.astype(BF16)
                    xc_copy(m).start()
                else:
                    view(out, m)[...] = total.astype(BF16)
                    spread(m)
                    a_copy(m).start()

        def spread(m):
            if root > 0:
                b_copy(m, whole, False).start()
            if root < count - 1:
                b_copy(m, whole, True).start()

        def crossed(m):
            xc_copy(m).wait_recv()
            view(out, m)[...] = add(view(acc, m)[...], landed(xc, m)[...])
            spread(m)
            finished(m)

        def outward(m):
            b_copy(m, whole, False).wait_recv()

            @pl.when(left & (pos > 0))
            def _():
                b_copy(m, whole, False).start()

            @pl.when(right & (pos < count - 1))
            def _():
                b_copy(m, whole, True).start()

            if whole:
                finished(m)
            else:
                a_copy(m).start()

        def sent(m):
            @pl.when(jnp.logical_not(here))
            def _():
                z_copy(m, whole, True).wait_send()

            @pl.when((pos <= root) & (pos > 0))
            def _():
                b_copy(m, whole, False).wait_send()

            @pl.when((pos >= root) & (pos < count - 1))
            def _():
                b_copy(m, whole, True).wait_send()

            if whole:
                @pl.when(here)
                def _():
                    xc_copy(m).wait_send()
            else:
                x_copy(m).wait_send()
                a_copy(m).wait_send()

        def add_y(m):
            @pl.when(with_y(m))
            def _():
                y_copy(m).wait_recv()
                acc[:, at(m), :] = add(acc[:, at(m), :], ry[:, y_at(m), :])

            if whole:
                outer(m)
            else:
                x_copy(m).start()

        def add_x(m):
            x_copy(m).wait_recv()
            acc[sec, at(m), :] = add(acc[sec, at(m), :], rx[pair_at(m), :])
            outer(m)

        def last_half(m):
            a_wait(m)
            finished(m)

        base = 1 if whole else 2
        back = base + reach + dist + (1 if whole else 0)
        steps = [(back, jnp.logical_not(here), outward), (base + level, level > 0, inward), (1, True, add_y)]
        if whole:
            steps.append((base + reach + 1, here, crossed))
        else:
            steps += [(back + 1, True, last_half), (2, True, add_x)]
        return steps, sent

    low_root = (count - 1) // 2
    high_root = min(low_root + 1, count - 1)
    lines = [
        (lambda m: lax.rem(m, 2) == 0, *line_of(low_root, False)),
        (lambda m: lax.rem(m, 4) == 1, *line_of(low_root, True)),
        (lambda m: lax.rem(m, 4) == 3, *line_of(high_root, True)),
    ]

    def tick(n):
        for low, high, piece in pieces:
            @pl.when((n >= low) & (n < high))
            def _(low=low, piece=piece):
                piece(n - low)

        for mine, steps, _ in lines:
            for offset, enabled, stage in steps:
                m = n - LAG * offset

                @pl.when((m >= 0) & (m < ALL_K) & mine(m) & enabled)
                def _(m=m, stage=stage):
                    stage(m)

        @pl.when(n < ALL_K)
        def _():
            stage_c(n)

    far_reach = max(low_root, count - 1 - low_root, high_root, count - 1 - high_root)
    loop(ALL_K + LAG * (3 + 2 * far_reach) + 1, tick)

    def finish(m):
        core_copy(m, out.at[:, at(m), :]).wait_send()

        @pl.when(with_y(m))
        def _():
            corey_copy(m, rcy.at[:, y_at(m), :]).wait_send()
            y_copy(m).wait_send()

        for mine, _, sent in lines:
            @pl.when(mine(m))
            def _(sent=sent):
                sent(m)

    loop(ALL_K, finish)
    for step in range(1, devices):
        dx_copy(step).wait()
    for step in range(1, LANES):
        emb_copy(step).wait()
    give_enc().wait_send()
    for k in range(D // 256):
        give_part(k, 0).wait_send()
        give_part(k, 1).wait_send()
        give_last(k).wait_send()


def backward_call(args, half, hid):
    dma = lambda *s: pltpu.SemaphoreType.DMA(s)
    vm = pltpu.VMEM
    full = ALL_K * CH
    y_half = DEC_ROWS + CH
    k = ALL_K
    rows = 2 * PAD
    cut = D // (2 * LANES)
    specs = [VM] * len(args)
    specs[20] = ANY
    return pl.pallas_call(
        backward_and_sums,
        out_shape=[
            jax.ShapeDtypeStruct((2, full, D), BF16),
            jax.ShapeDtypeStruct((LANES, 2, CH, D), BF16),
            jax.ShapeDtypeStruct((2 * LANES, cut, VIS), BF16),
        ],
        in_specs=specs,
        out_specs=[VM] * 3,
        scratch_shapes=[
            vm((rows, D), BF16), vm((D, rows), BF16), vm((D, rows), BF16),
            vm((rows, D), F32), vm((rows, D), BF16), vm((rows, D), BF16),
            vm((2, rows, hid), BF16), vm((rows, D), BF16), vm((rows, D), F32),
            vm((rows, half), BF16), vm((2, 3, rows, half), BF16),
            vm((PAD, D), F32), vm((PAD, D), BF16), vm((PAD, D), BF16), vm((PAD, D), F32),
            vm((2 * LANES, cut, VIS), BF16),
            vm((2, 1, hid), F32), vm((2, 2, half), F32), vm((8, D), F32),
            vm((2, full, D), BF16), vm((2, y_half, D), BF16), vm((2, ENC_A + ENC_B, D), BF16),
            vm((2, y_half, D), BF16), vm((2, y_half, D), BF16),
            vm((full // 2, D), BF16), vm((full // 2, D), BF16), vm((full // 2, D), BF16),
            vm((2, full // 2, D), BF16), vm((2, full // 2, D), BF16), vm((2, full // 2, D), BF16),
            vm((LANES, 32, D), F32), vm((LANES, 2, CH, D), BF16),
            dma(3), dma(10), dma(10),
            dma(k), dma(k), dma(k), dma(k), dma(k), dma(k),
            dma(k), dma(k), dma(k), dma(k), dma(k),
            dma(k), dma(k), dma(k), dma(k), dma(k), dma(LANES), dma(LANES),
            dma(2 * LANES), dma(2 * LANES),
        ],
        compiler_params=pltpu.CompilerParams(
            collective_id=1, has_side_effects=True, vmem_limit_bytes=VMEM_LIMIT
        ),
    )(*args)


def finish_grads(
    total, emb,
    e_qkv, e_qvb, e_proj, e_up, e_upb, e_down, e_gain, e_off,
    d_qkv, d_qvb, d_proj, d_up, d_upb, d_down, d_gain, d_off, d_ew, d_ev,
):
    half = e_proj.shape[0]
    e_up[...] = total[0, A_TOP:B_TOP, :].astype(F32)
    e_down[...] = jnp.transpose(total[1, A_TOP:B_TOP, :].astype(F32))
    e_qkv[0] = total[0, B_TOP : B_TOP + half, :].astype(F32)
    e_qkv[1] = total[0, B_TOP + half : S_TOP, :].astype(F32)
    e_qkv[2] = total[1, B_TOP : B_TOP + half, :].astype(F32)
    e_proj[...] = total[1, B_TOP + half : S_TOP, :].astype(F32)
    d_up[...] = total[0, 0:512, 0:512].astype(F32)
    d_down[0:256, :] = jnp.transpose(total[0, 0:512, 512:768].astype(F32))
    d_down[256:512, :] = jnp.transpose(total[1, 0:512, 512:768].astype(F32))
    for j in range(3):
        d_qkv[j] = total[1, 0:512, j * 128 : (j + 1) * 128].astype(F32)
    for j in range(LANES):
        cut = slice(j * 128, (j + 1) * 128)
        d_proj[:, cut] = total[1, cut, 384:512].astype(F32)
    for k in range(LANES):
        for h in range(2):
            top = k * 192 + h * 64
            d_ew[top : top + 64, :] = emb[k, h, :, 0:512].astype(F32)
            d_ew[k * 192 + 128 : (k + 1) * 192, h * 256 : (h + 1) * 256] = emb[
                k, h, :, 512:768
            ].astype(F32)
    little = total[0, S_TOP : S_TOP + 32, :].astype(F32)
    d_upb[...] = little[0:1, 0:512]
    d_qvb[0:1, :] = little[1:2, 0:128]
    d_qvb[1:2, :] = little[1:2, 128:256]
    e_upb[...] = little[2:3]
    e_qvb[0:1, :] = little[3:4, 0:192]
    e_qvb[1:2, :] = little[3:4, 256:448]
    d_gain[...] = little[8:10, 0:512]
    d_off[...] = little[10:14, 0:512]
    d_ev[...] = little[14:16, 0:512]
    e_gain[...] = little[16:18]
    e_off[...] = little[18:22]


def call(kernel, specs, shapes, scratch, args):
    return pl.pallas_call(
        kernel,
        out_shape=[jax.ShapeDtypeStruct(s, d) for s, d in shapes],
        in_specs=specs,
        out_specs=[VM] * len(shapes),
        scratch_shapes=scratch,
        compiler_params=pltpu.CompilerParams(vmem_limit_bytes=VMEM_LIMIT),
    )(*args)


def position_rows():
    quarter = DD // 4
    freq = np.exp(np.arange(quarter, dtype=np.float32) * np.float32(-math.log(10000.0) / quarter))
    angle = np.arange(PAD, dtype=np.float32)[:, None] * freq[None, :].astype(np.float32)
    both = np.concatenate([np.sin(angle), np.cos(angle)], 1).astype(np.float32)
    high = both.astype(jnp.bfloat16)
    low = (both - high.astype(np.float32)).astype(jnp.bfloat16)
    return np.stack([high, low])


def per_device(
    patches, cotangent, widths, visible, window_shift, batch_order,
    encoder_qkv, encoder_qvbias, encoder_proj, encoder_up, encoder_upbias, encoder_down,
    encoder_gains, encoder_offsets,
    decoder_qkv, decoder_qvbias, decoder_proj, decoder_up, decoder_upbias, decoder_down,
    decoder_gains, decoder_offsets, embed_weight, embed_vectors,
):
    qkv0 = encoder_qkv.transpose(1, 2, 0)
    half = qkv0.shape[1]
    hid = encoder_up.shape[1]
    dff = decoder_up.shape[1] * LANES
    flat = patches.transpose(1, 0, 2).reshape(-1, D)
    (
        x, x1, a, u, y, gp, qkv, p, o, qkv1, proj1, up1, down1, dec_buf,
        d_enc, d_dqvb, d_dupb, d_dsmall, out_all,
    ) = forward_call(
        (
            widths, window_shift, batch_order, visible, flat, encoder_gains, encoder_offsets,
            encoder_qvbias, encoder_upbias, decoder_qvbias, decoder_upbias,
            qkv0, encoder_proj, encoder_up, encoder_down,
            decoder_qkv.transpose(1, 0, 2), decoder_proj, decoder_up, decoder_down,
            cotangent, embed_weight, embed_vectors, jnp.asarray(position_rows()),
            decoder_gains, decoder_offsets,
        ),
        half, hid, dff,
    )
    total, emb, dx_all = backward_call(
        (
            d_enc, x, x1, a, u, y, gp, qkv, p, o, encoder_gains, encoder_offsets,
            qkv0, qkv1, encoder_proj, proj1, encoder_up, up1, encoder_down, down1,
            dec_buf, d_dqvb, d_dupb, d_dsmall,
        ),
        half, hid,
    )
    f = lambda *shape: (shape, F32)
    grads = call(
        finish_grads, [VM, VM],
        [
            f(3, half, D), f(2, half), f(half, D), f(D, hid), f(1, hid), f(hid, D), f(2, D), f(4, D),
            f(3, DD, 128), f(2, 128), f(128, DD), f(DD, 512), f(1, 512), f(512, DD), f(2, DD), f(4, DD),
            f(D, DD), f(2, DD),
        ],
        [], (total, emb),
    )
    grads = list(grads)
    grads[0] = grads[0].transpose(2, 0, 1)
    grads[4] = grads[4][0]
    grads[8] = grads[8].transpose(1, 0, 2)
    grads[12] = grads[12][0]
    return (out_all.swapaxes(1, 2), dx_all.swapaxes(1, 2), *grads)


def solution(mesh):
    weights = (
        P(None, None, "tensor"), P(None, "tensor"), P("tensor", None), P(None, "tensor"),
        P("tensor"), P("tensor", None), P(), P(),
    )
    split = P("dp", None, ("section", "tensor"))
    return jax.shard_map(
        per_device,
        mesh=mesh,
        in_specs=(
            P("dp", None, None), P("dp", None, None), P("dp"), P("dp", None), P("dp", None),
            P("dp", None),
        ) + weights + weights + (P(), P()),
        out_specs=(split, split) + weights + weights + (P(), P()),
        check_vma=False,
    )
```

```python
import math

import jax
import jax.numpy as jnp
import numpy as np
from jax import lax
from jax.experimental import pallas as pl
from jax.experimental.pallas import tpu as pltpu
from jax.sharding import PartitionSpec as P

D = 768
HEADS = 12
DD = 512
DHEADS = 16
GRID_ROWS = 64
WIDE = 8
WIN = 4
VIS = 102
CM = 4
GRID = 512
LANES = 4
PAD = 128
EPS = 1e-06
NEG = -10000.0
F32 = jnp.float32
BF16 = jnp.bfloat16
VMEM_LIMIT = 60 * 1024 * 1024

VM = pl.BlockSpec(memory_space=pltpu.VMEM)
SM = pl.BlockSpec(memory_space=pltpu.SMEM)
ANY = pl.BlockSpec(memory_space=pl.ANY)


def nn(a, b):
    return lax.dot_general(a, b, (((1,), (0,)), ((), ())), preferred_element_type=F32)


def nt(a, b):
    return lax.dot_general(a, b, (((1,), (1,)), ((), ())), preferred_element_type=F32)


def tn(a, b):
    return lax.dot_general(a, b, (((0,), (0,)), ((), ())), preferred_element_type=F32)


def loop(count, body):
    def step(i, carry):
        body(i)
        return carry

    lax.fori_loop(0, count, step, 0)


def span(i, size):
    return pl.ds(pl.multiple_of(i * size, size), size)


def normal(x):
    center = x - jnp.mean(x, -1, keepdims=True)
    scale = lax.rsqrt(jnp.mean(center * center, -1, keepdims=True) + EPS)
    return center * scale, scale


def normal_back(dy, hat, scale, gain):
    d = dy * gain
    return scale * (
        d - jnp.mean(d, -1, keepdims=True) - hat * jnp.mean(d * hat, -1, keepdims=True)
    )


def gelu_both(h):
    phi = 0.5 * lax.erf(h * math.sqrt(0.5)) + 0.5
    bell = jnp.exp2(h * h * (-0.5 * math.log2(math.e)))
    return h * phi, phi + h * bell * (1.0 / math.sqrt(2.0 * math.pi))


def colsum(x):
    return jnp.sum(x, 0, keepdims=True)


def head_marks(width, size, dtype):
    lane = lax.broadcasted_iota(jnp.int32, (1, width), 1)
    return [((lane >= h * size) & (lane < (h + 1) * size)).astype(dtype) for h in range(width // size)]


def stacked(x, marks):
    return jnp.concatenate([x * m for m in marks], 0)


def softmax(s):
    e = jnp.exp(s - jnp.max(s, -1, keepdims=True))
    return e * (1.0 / jnp.sum(e, -1, keepdims=True))


def attend(q, k, v, marks, shape_scores):
    stack = stacked(k, marks)
    s = nt(q, stack)
    keys = k.shape[0]
    p = jnp.concatenate(
        [
            softmax(shape_scores(s[:, h * keys : (h + 1) * keys])).astype(BF16)
            for h in range(len(marks))
        ],
        1,
    )
    return p, nn(p, stacked(v, marks)).astype(BF16)


def attend_back(q, k, v, p, d_out, marks, marks32, scale):
    keys = k.shape[0]
    d_p = nt(d_out, stacked(v, marks))
    parts = []
    for h in range(len(marks)):
        cut = slice(h * keys, (h + 1) * keys)
        ph = p[:, cut].astype(F32)
        dh = d_p[:, cut]
        inner = jnp.sum(ph * dh, -1, keepdims=True)
        parts.append((ph * (dh - inner) * scale).astype(BF16))
    dr = jnp.concatenate(parts, 1)
    d_q = nn(dr, stacked(k, marks))
    d_k_all = tn(dr, q)
    d_v_all = tn(p, d_out)
    d_k = 0.0
    d_v = 0.0
    for h in range(len(marks)):
        cut = slice(h * keys, (h + 1) * keys)
        d_k += d_k_all[cut] * marks32[h]
        d_v += d_v_all[cut] * marks32[h]
    return d_q.astype(BF16), d_k.astype(BF16), d_v.astype(BF16)


ENC_SIZE = D // HEADS
ENC_SCALE = ENC_SIZE ** -0.5
DEC_SIZE = DD // DHEADS
DEC_SCALE = DEC_SIZE ** -0.5


def attend_flat(q, k, v, marks, rows32, allowed, scale):
    keys = k.shape[0]
    s = nt(stacked(k, marks), q)
    parts = []
    for h in range(len(marks)):
        x = jnp.where(allowed, s[h * keys : (h + 1) * keys] * scale, NEG)
        e = jnp.exp(x - jnp.max(x, 0, keepdims=True))
        parts.append((e * (1.0 / jnp.sum(e, 0, keepdims=True))).astype(BF16))
    p = jnp.concatenate(parts, 0)
    turned = jnp.transpose(v.astype(F32))
    wide = jnp.concatenate([(turned * m).astype(BF16) for m in rows32], 1)
    return p, nn(wide, p).astype(BF16)


def attend_flat_back(q, k, v, p, d_out, marks, marks32, rows32, scale):
    keys = k.shape[0]
    d_p = nt(stacked(v, marks), d_out)
    parts = []
    for h in range(len(marks)):
        cut = slice(h * keys, (h + 1) * keys)
        ph = p[cut].astype(F32)
        dh = d_p[cut]
        inner = jnp.sum(ph * dh, 0, keepdims=True)
        parts.append((ph * (dh - inner) * scale).astype(BF16))
    dr = jnp.concatenate(parts, 0)
    turned = jnp.transpose(k.astype(F32))
    wide = jnp.concatenate([(turned * m).astype(BF16) for m in rows32], 1)
    d_q = jnp.transpose(nn(wide, dr))
    d_k_all = nn(dr, q)
    d_v_all = nn(p, d_out)
    d_k = 0.0
    d_v = 0.0
    for h in range(len(marks)):
        cut = slice(h * keys, (h + 1) * keys)
        d_k += d_k_all[cut] * marks32[h]
        d_v += d_v_all[cut] * marks32[h]
    return d_q.astype(BF16), d_k.astype(BF16), d_v.astype(BF16)


MESH = pl.DeviceIdType.MESH


def far(src, dst, send, recv, peer):
    return pltpu.make_async_remote_copy(
        src_ref=src, dst_ref=dst, send_sem=send, recv_sem=recv, device_id=peer, device_id_type=MESH
    )


def forward_and_decoder(
    wid, shifts, order, vis, pat, gains, offs, b_qv, b_up, b_dqv, b_dup,
    h_qkv, h_proj, h_up, h_down, h_dqkv, h_dproj, h_dup, h_ddown,
    cot_hbm, ew, evec, table, dgains, doffs,
    o_x, o_x1, o_a, o_u, o_y, o_gp, o_qkv, o_p, o_o, o_w, o_wproj, o_wup, o_wdown, o_dec,
    d_enc, d_qvb, d_upb, d_small, dec_out,
    w_qkv, w_proj, w_up, w_down, bias, biases, qkv, proj, up, down,
    ex, ea, eu, ey, egp, eqkv, ep, eo, ex1, epart, esend, erecv, esend2, erecv2, eown,
    cot, x0, x1, a, acts, probs, o, u, ut, y, gp, g32, gb, gt, acc, e_ref, hot, buf, dsend,
    load_s, out_s, cot_s, w_s, w_r, bias_s, bias_r, dw_s, dw_r, ex_s, ex_r, ex2_s, ex2_r, do_s, do_r,
):
    sec = lax.axis_index("section")
    lane = lax.axis_index("tensor")
    mate = lane + 1 - 2 * lax.rem(lane, 2)
    over = lax.rem(lane + 2, LANES)
    cross = lax.rem(mate + 2, LANES)
    me = sec * LANES + lane
    devices = 2 * LANES
    clip = me
    clips = (me, sec * LANES + over)

    def group_peer(step):
        peer = lax.rem(me + step, devices)
        return peer, {"section": lax.div(peer, LANES), "tensor": lax.rem(peer, LANES)}

    own = [
        pltpu.make_async_copy(src, dst.at[0], load_s.at[n])
        for n, (src, dst) in enumerate(
            ((h_qkv, w_qkv), (h_proj, w_proj), (h_up, w_up), (h_down, w_down))
        )
    ]

    def place(n, shard):
        thick = (128, 128, 512, 512)[n]
        cut = pl.ds(pl.multiple_of(shard * thick, thick), thick)
        return (qkv.at[:, :, cut], proj.at[cut, :], up.at[:, cut], down.at[cut, :])[n]

    shards = (h_dqkv, h_dproj, h_dup, h_ddown)
    keep = [
        pltpu.make_async_copy(shards[n], place(n, lane), load_s.at[4 + n]) for n in range(4)
    ]
    for copy in own + keep:
        copy.start()
    fetch = pltpu.make_async_copy(cot_hbm.at[clip], cot, cot_s)
    fetch.start()

    barrier = pltpu.get_barrier_semaphore()
    for step in range(1, devices):
        pl.semaphore_signal(barrier, inc=1, device_id_type=MESH, device_id=group_peer(step)[1])
    bias[...] = jnp.zeros_like(bias)
    half = w_proj.shape[1]
    bias[0:1, :] = b_up[...].astype(F32).reshape(1, -1)
    bias[1:3, 0:half] = b_qv[...].astype(F32)
    bias[3:4, 0:512] = b_dup[...].astype(F32).reshape(1, -1)
    bias[4:6, 0:128] = b_dqv[...].astype(F32)
    biases[lane] = bias[...]
    pl.semaphore_wait(barrier, devices - 1)

    def enc_weight(n):
        src = (h_qkv, h_proj, h_up, h_down)[n]
        dst = (w_qkv, w_proj, w_up, w_down)[n]
        return far(src, dst.at[1], w_s.at[n], w_r.at[n], {"tensor": mate})

    def bias_copy(step):
        return far(
            bias, biases.at[lane], bias_s.at[step], bias_r.at[step],
            {"tensor": lax.rem(lane + step, LANES)},
        )

    def dec_weight(n, kind):
        peer = over if kind == 0 else mate
        src = shards[n] if kind < 2 else place(n, over)
        dst = place(n, lane if kind < 2 else over)
        return far(src, dst, dw_s.at[3 * n + kind], dw_r.at[3 * n + kind], {"tensor": peer})

    enc_weight(0).start()
    for step in range(1, LANES):
        bias_copy(step).start()
    enc_weight(1).start()
    for n in (0, 1):
        dec_weight(n, 0).start()
    enc_weight(2).start()
    enc_weight(3).start()
    for n in range(4):
        dec_weight(n, 1).start()

    def pass_on(n):
        dec_weight(n, 0).wait_recv()
        dec_weight(n, 2).start()

    def arrived(n):
        keep[n].wait()
        dec_weight(n, 1).wait_recv()
        dec_weight(n, 2).wait_recv()

    egain = gains[...].astype(F32)
    eoff = offs[...].astype(F32)
    stride = pat.shape[0] // VIS
    for c in range(2):
        row = lax.broadcasted_iota(jnp.int32, (PAD, pat.shape[0]), 0)
        col = lax.broadcasted_iota(jnp.int32, (PAD, pat.shape[0]), 1)
        pick = (col == row * stride + clips[c]).astype(F32).astype(BF16)
        ex[c * PAD : (c + 1) * PAD, :] = nn(pick, pat[...])

    def enc_norm(i):
        r = span(i, 64)
        hat, _ = normal(ex[r, :])
        ea[r, :] = (hat * egain[0:1] + eoff[0:1]).astype(BF16)

    loop(2 * PAD // 64, enc_norm)
    emarks = head_marks(half, ENC_SIZE, BF16)
    key = lax.broadcasted_iota(jnp.int32, (PAD, PAD), 1)
    floor = jnp.where(key < VIS, NEG, -1e30)
    for g, shard in enumerate((lane, mate)):
        if g == 0:
            own[0].wait()
            bq, bv = bias[1:2, 0:half], bias[2:3, 0:half]
        else:
            enc_weight(0).wait_recv()
            for step in range(1, LANES):
                bias_copy(step).wait_recv()
            bq, bv = biases[shard, 1:2, 0:half], biases[shard, 2:3, 0:half]
        eqkv[g, 0] = (nt(ea[...], w_qkv[g, 0]) + bq).astype(BF16)
        eqkv[g, 1] = nt(ea[...], w_qkv[g, 1]).astype(BF16)
        eqkv[g, 2] = (nt(ea[...], w_qkv[g, 2]) + bv).astype(BF16)
        for c in range(2):
            limit = (VIS * wid[clips[c]]) // WIDE
            rows = slice(c * PAD, (c + 1) * PAD)
            p, out = attend(
                eqkv[g, 0, rows], eqkv[g, 1, rows], eqkv[g, 2, rows], emarks,
                lambda s: jnp.where(key < limit, s * ENC_SCALE, floor),
            )
            ep[g, c] = p
            eo[g, rows] = out
    own[1].wait()
    enc_weight(1).wait_recv()

    def give_part(i, side):
        cut = span(i, 256)
        return far(
            esend.at[(1 - side) * PAD : (2 - side) * PAD, cut],
            erecv.at[side * PAD : (side + 1) * PAD, cut],
            ex_s.at[2 * i + side], ex_r.at[2 * i + side], {"tensor": over},
        )

    def enc_mix(i):
        c = span(i, 256)
        t = nn(eo[0], w_proj[0, :, c]) + nn(eo[1], w_proj[1, :, c])
        epart[:, c] = t
        esend[:, c] = t.astype(BF16)
        give_part(i, 0).start()
        give_part(i, 1).start()

    blocks = D // 256
    loop(blocks, enc_mix)
    pass_on(0)
    for i in range(blocks):
        give_part(i, 0).wait_recv()
        give_part(i, 1).wait_recv()
    dec_weight(2, 0).start()

    def enc_norm_two(i):
        r = span(i, 64)
        t = ex[r, :] + epart[r, :] + erecv[r, :].astype(F32) + eoff[2:3]
        ex1[r, :] = t
        hat, _ = normal(t)
        eu[r, :] = (hat * egain[1:2] + eoff[1:2]).astype(BF16)

    loop(2 * PAD // 64, enc_norm_two)
    own[2].wait()
    enc_weight(2).wait_recv()
    for g, shard in enumerate((lane, mate)):

        def enc_ff(i, g=g, shard=shard):
            c = span(i, 256)
            h = nn(eu[...], w_up[g, :, c]) + biases[shard, 0:1, c]
            act, slope = gelu_both(h)
            ey[g, :, c] = act.astype(BF16)
            egp[g, :, c] = slope.astype(BF16)

        loop(w_up.shape[2] // 256, enc_ff)
    own[3].wait()
    enc_weight(3).wait_recv()

    def give_last(i):
        cut = span(i, 256)
        return far(
            esend2.at[:, cut], erecv2.at[:, cut], ex2_s.at[i], ex2_r.at[i], {"tensor": over}
        )

    def enc_out(i):
        c = span(i, 256)
        t = nn(ey[0], w_down[0, :, c]) + nn(ey[1], w_down[1, :, c])
        eown[:, c] = t[:PAD]
        esend2[:, c] = t[PAD:].astype(BF16)
        give_last(i).start()

    loop(blocks, enc_out)
    outs = [
        pltpu.make_async_copy(src, dst, out_s.at[n])
        for n, (src, dst) in enumerate(
            (
                (ex.at[0:PAD, :], o_x), (ex1, o_x1), (ea, o_a), (eu, o_u), (ey, o_y), (egp, o_gp),
                (eqkv, o_qkv), (ep, o_p), (eo, o_o), (w_qkv.at[1], o_w), (w_proj.at[1], o_wproj),
                (w_up.at[1], o_wup), (w_down.at[1], o_wdown),
            )
        )
    ]
    for copy in outs:
        copy.start()
    pass_on(1)
    pass_on(2)
    for i in range(blocks):
        give_last(i).wait_recv()
    dec_weight(3, 0).start()

    width = wid[clip]
    bits = jnp.where(width == WIDE, 3, 2)
    turn = shifts[clip, 0] * width
    mod = GRID - 1
    spot = 0
    for i in range(order.shape[1]):
        spot = spot + jnp.where(order[0, i] == clip, i, 0)
    batch = spot // CM
    count = 0
    for i in range(order.shape[1]):
        count = count + jnp.where(batch == i // CM, wid[order[0, i]], 0)
    factor_rows = CM * GRID / (jnp.full((1, 1), count, jnp.int32) * GRID_ROWS).astype(F32)

    def slot_of(index):
        return (index - turn) & mod

    def code_of(slot):
        band = ((slot >> bits) + shifts[clip, 0]) >> 2
        strip = ((slot & (width - 1)) + shifts[clip, 1]) >> 2
        return band * 4 + strip

    e_ref[...] = (ex1[0:PAD, :] + eown[...] + erecv2[...].astype(F32) + eoff[3:4]).astype(BF16)
    vec = evec[...].astype(F32)
    m = (nn(e_ref[...], ew[...]) + vec[0:1]).astype(BF16)
    seen = vis[pl.ds(clip, 1), :]
    target = jnp.concatenate([(seen + turn) & mod, jnp.full((1, PAD - VIS), -1, jnp.int32)], 1)
    gain = dgains[...].astype(F32)
    offsets = doffs[...].astype(F32)

    def start(i):
        r = span(i, PAD)
        index = lax.broadcasted_iota(jnp.int32, (PAD, PAD), 0) + i * PAD
        column = lax.broadcasted_iota(jnp.int32, (PAD, PAD), 1)
        match = index == target
        oh = match.astype(F32).astype(BF16)
        hot[r, :] = oh
        hit = jnp.sum(match.astype(F32), -1, keepdims=True)
        grid = jnp.where(hit > 0, nn(oh, m), vec[1:2]).astype(BF16).astype(F32)
        slot = slot_of(index)
        by_row = ((slot >> bits) == column).astype(F32).astype(BF16)
        by_col = ((slot & (width - 1)) == column).astype(F32).astype(BF16)
        row_part = nn(by_row, table[0]) + nn(by_row, table[1])
        col_part = nn(by_col, table[0]) + nn(by_col, table[1])
        x = grid + jnp.concatenate([row_part, col_part], 1)
        x0[r, :] = x
        hat, _ = normal(x)
        a[r, :] = (hat * gain[0:1] + offsets[0:1]).astype(BF16)

    loop(GRID // PAD, start)
    arrived(0)

    def dec_bias(row, size):
        return jnp.concatenate([biases[k, row : row + 1, 0:size] for k in range(LANES)], 1)

    def project(i):
        r = span(i, 256)
        rows = a[r, :]
        acts[0, r, :] = (nn(rows, qkv[0]) + dec_bias(4, 128)).astype(BF16)
        acts[1, r, :] = nn(rows, qkv[1]).astype(BF16)
        acts[2, r, :] = (nn(rows, qkv[2]) + dec_bias(5, 128)).astype(BF16)

    loop(2, project)
    pass_on(3)
    marks = head_marks(128, DEC_SIZE, BF16)
    marks32 = head_marks(128, DEC_SIZE, F32)
    dim = lax.broadcasted_iota(jnp.int32, (128, 1), 0)
    rows32 = [
        ((dim >= h * DEC_SIZE) & (dim < (h + 1) * DEC_SIZE)).astype(F32) for h in range(len(marks))
    ]

    def attention(i):
        r = span(i, PAD)
        key_slot = slot_of(lax.broadcasted_iota(jnp.int32, (PAD, PAD), 0) + i * PAD)
        row_slot = slot_of(lax.broadcasted_iota(jnp.int32, (PAD, PAD), 1) + i * PAD)
        allowed = (code_of(row_slot) == code_of(key_slot)) & (key_slot < GRID_ROWS * width)
        for g in range(DD // 128):
            c = slice(g * 128, (g + 1) * 128)
            p, out = attend_flat(
                acts[0, r, c], acts[1, r, c], acts[2, r, c], marks, rows32, allowed, DEC_SCALE
            )
            probs[i, g * 512 : (g + 1) * 512, :] = p
            o[c, r] = out

    loop(GRID // PAD, attention)
    arrived(1)

    def mix(i):
        r = span(i, PAD)
        x = x0[r, :] + tn(o[:, r], proj[...]) + offsets[2:3]
        x1[r, :] = x
        hat, _ = normal(x)
        un = hat * gain[1:2] + offsets[1:2]
        u[r, :] = un.astype(BF16)
        ut[:, r] = jnp.transpose(un).astype(BF16)

    loop(GRID // PAD, mix)
    arrived(2)

    def ff(i):
        k = lax.div(i, 4)
        side = lax.rem(lax.div(i, 2), 2)
        c = span(lax.div(i, 2), 256)
        r = span(lax.rem(i, 2), 256)
        h = nn(u[r, :], up[:, c]) + biases[k, 3:4, span(side, 256)]
        act, slope = gelu_both(h)
        y[r, c] = act.astype(BF16)
        gp[r, c] = slope.astype(BF16)

    loop(2 * up.shape[1] // 256, ff)
    arrived(3)
    fetch.wait()
    slot_col = slot_of(lax.broadcasted_iota(jnp.int32, (GRID, 1), 0))
    valid = (slot_col < GRID_ROWS * width).astype(F32)
    rolled = slot_of(lax.broadcasted_iota(jnp.int32, (GRID, GRID), 0))
    perm = (rolled == lax.broadcasted_iota(jnp.int32, (GRID, GRID), 1)).astype(F32).astype(BF16)

    def out(i):
        r = span(lax.rem(i, 2), 256)
        c = span(lax.div(i, 2), 256)
        acc[r, c] = nn(y[r, :], down[:, c])

    loop(4, out)
    full = ((acc[...] + x1[...] + offsets[3:4]) * valid).astype(BF16)
    turned = tn(full, perm).astype(BF16)
    for k in range(devices):
        dsend[k] = turned[k * dsend.shape[1] : (k + 1) * dsend.shape[1]]

    def decoded_copy(step):
        peer, spot = group_peer(step)
        return far(dsend.at[peer], dec_out.at[me], do_s.at[step], do_r.at[step], spot)

    for step in range(1, devices):
        decoded_copy(step).start()
    dec_out[me] = dsend[me]
    g = nn(perm, cot[...]) * valid * factor_rows
    g32[...] = g
    gb[...] = g.astype(BF16)
    gt[...] = jnp.transpose(g).astype(BF16)
    d_small[0:5, :] = jnp.zeros((5, DD), F32)
    d_small[5:6, :] = colsum(g)
    d_small[6:8, :] = jnp.zeros((2, DD), F32)

    def ff_back(i):
        c = span(i, 256)
        shard = lax.div(i, 2)
        side = lax.rem(i, 2)
        buf[shard, side, 0:512, 512:768] = nn(gt[...], y[:, c]).astype(BF16)
        dh = nt(gb[...], down[c, :]) * gp[:, c].astype(F32)
        d_upb[:, c] = colsum(dh)
        du = dh.astype(BF16)
        gp[:, c] = du
        buf[shard, 0, 0:512, span(side, 256)] = nn(ut[...], du).astype(BF16)

    loop(up.shape[1] // 256, ff_back)
    early = pltpu.make_async_copy(buf.at[:, 0, 0:512, :], o_dec.at[:, 0, 0:512, :], out_s.at[13])
    early.start()

    def ff_in(i):
        r = span(lax.rem(i, 2), 256)
        c = span(lax.div(i, 2), 256)
        acc[r, c] = nt(gp[r, :], up[c, :])

    loop(4, ff_in)

    def mix_back(i):
        r = span(i, PAD)
        hat, scale = normal(x1[r, :])
        da = acc[r, :]
        dx = g32[r, :] + normal_back(da, hat, scale, gain[1:2])
        d_small[1:2, :] += colsum(da * hat)
        d_small[3:4, :] += colsum(da)
        d_small[4:5, :] += colsum(dx)
        g32[r, :] = dx
        dxb = dx.astype(BF16)
        gb[r, :] = dxb
        u[r, :] = nt(dxb, proj[...]).astype(BF16)

    loop(GRID // PAD, mix_back)
    d_proj = nn(o[...], gb[...]).astype(BF16)
    for k in range(LANES):
        for j in range(LANES):
            block = d_proj[k * 128 : (k + 1) * 128, j * 128 : (j + 1) * 128]
            buf[k, 1, j * 128 : (j + 1) * 128, 384:512] = block

    def attention_back(i):
        r = span(i, PAD)
        for k in range(DD // 128):
            c = slice(k * 128, (k + 1) * 128)
            dq, dk, dv = attend_flat_back(
                acts[0, r, c], acts[1, r, c], acts[2, r, c],
                probs[i, k * 512 : (k + 1) * 512, :], u[r, c], marks, marks32, rows32, DEC_SCALE,
            )
            acts[0, r, c] = dq
            acts[1, r, c] = dk
            acts[2, r, c] = dv

    loop(GRID // PAD, attention_back)
    d_qvb[0:1, :] = colsum(acts[0].astype(F32))
    d_qvb[1:2, :] = colsum(acts[2].astype(F32))

    def project_back(i):
        r = span(lax.rem(i, 2), 256)
        c = span(lax.div(i, 2), 256)
        acc[r, c] = (
            nt(acts[0, r, :], qkv[0, c, :])
            + nt(acts[1, r, :], qkv[1, c, :])
            + nt(acts[2, r, :], qkv[2, c, :])
        )

    loop(4, project_back)
    gt[...] = jnp.transpose(a[...].astype(F32)).astype(BF16)
    for j in range(3):
        d_qkv = nn(gt[...], acts[j]).astype(BF16)
        for k in range(LANES):
            buf[k, 1, 0:512, j * 128 : (j + 1) * 128] = d_qkv[:, k * 128 : (k + 1) * 128]

    def start_back(i):
        r = span(i, PAD)
        hat, scale = normal(x0[r, :])
        da = acc[r, :]
        dx = g32[r, :] + normal_back(da, hat, scale, gain[0:1])
        d_small[0:1, :] += colsum(da * hat)
        d_small[2:3, :] += colsum(da)
        dg = dx.astype(BF16)
        gb[r, :] = dg
        hit = jnp.sum(hot[r, :].astype(F32), -1, keepdims=True)
        d_small[7:8, :] += colsum(jnp.where(hit > 0, 0.0, dg.astype(F32)))

    loop(GRID // PAD, start_back)
    dm = tn(hot[...], gb[...])
    d_small[6:7, :] = colsum(dm)
    dmb = dm.astype(BF16)
    d_enc[...] = nt(dmb, ew[...]).astype(BF16)
    d_ew = tn(e_ref[...], dmb).astype(BF16)
    for k in range(LANES):
        for h in range(2):
            top = k * 192 + h * 64
            buf[k, h, 512:576, 0:512] = d_ew[top : top + 64]
            buf[k, h, 512:576, 512:768] = d_ew[k * 192 + 128 : (k + 1) * 192, h * 256 : (h + 1) * 256]

    rest = [
        pltpu.make_async_copy(buf.at[:, 1], o_dec.at[:, 1], out_s.at[14]),
        pltpu.make_async_copy(buf.at[:, 0, 512:576, :], o_dec.at[:, 0, 512:576, :], out_s.at[15]),
    ]
    for copy in rest:
        copy.start()
    for copy in outs + [early] + rest:
        copy.wait()
    for n in range(4):
        enc_weight(n).wait_send()
        for kind in range(3):
            dec_weight(n, kind).wait_send()
    for step in range(1, LANES):
        bias_copy(step).wait_send()
    for i in range(blocks):
        give_part(i, 0).wait_send()
        give_part(i, 1).wait_send()
        give_last(i).wait_send()
    for step in range(1, devices):
        decoded_copy(step).wait()


def forward_call(args, half, hid, dff):
    dma = lambda *s: pltpu.SemaphoreType.DMA(s)
    vm = lambda dtype, *shape: pltpu.VMEM(shape, dtype)
    rows = 2 * PAD
    keys = PAD * half // ENC_SIZE
    devices = 2 * LANES
    slab = DD // devices
    kept = [
        ((PAD, D), F32), ((rows, D), F32), ((rows, D), BF16), ((rows, D), BF16),
        ((2, rows, hid), BF16), ((2, rows, hid), BF16), ((2, 3, rows, half), BF16),
        ((2, 2, PAD, keys), BF16), ((2, rows, half), BF16),
        ((3, half, D), BF16), ((half, D), BF16), ((D, hid), BF16), ((hid, D), BF16),
        ((LANES, 2, DEC_ROWS, D), BF16),
    ]
    made = [
        ((PAD, D), BF16), ((2, DD), F32), ((1, dff), F32), ((8, DD), F32),
        ((devices, slab, GRID), BF16),
    ]
    return pl.pallas_call(
        forward_and_decoder,
        out_shape=[jax.ShapeDtypeStruct(s, d) for s, d in kept + made],
        in_specs=[SM, SM, SM] + [VM] * 8 + [ANY] * 9 + [VM] * 5,
        out_specs=[ANY] * len(kept) + [VM] * len(made),
        scratch_shapes=[
            vm(BF16, 2, 3, half, D), vm(BF16, 2, half, D), vm(BF16, 2, D, hid), vm(BF16, 2, hid, D),
            vm(F32, 8, D), vm(F32, LANES, 8, D),
            vm(BF16, 3, DD, DD), vm(BF16, DD, DD), vm(BF16, DD, dff), vm(BF16, dff, DD),
            vm(F32, rows, D), vm(BF16, rows, D), vm(BF16, rows, D), vm(BF16, 2, rows, hid),
            vm(BF16, 2, rows, hid), vm(BF16, 2, 3, rows, half), vm(BF16, 2, 2, PAD, keys),
            vm(BF16, 2, rows, half), vm(F32, rows, D), vm(F32, rows, D), vm(BF16, rows, D),
            vm(BF16, rows, D), vm(BF16, PAD, D), vm(BF16, PAD, D), vm(F32, PAD, D),
            vm(BF16, GRID, DD), vm(F32, GRID, DD), vm(F32, GRID, DD), vm(BF16, GRID, DD),
            vm(BF16, 3, GRID, DD), vm(BF16, GRID // PAD, DHEADS * PAD, PAD), vm(BF16, DD, GRID),
            vm(BF16, GRID, DD), vm(BF16, DD, GRID), vm(BF16, GRID, dff), vm(BF16, GRID, dff),
            vm(F32, GRID, DD), vm(BF16, GRID, DD), vm(BF16, DD, GRID), vm(F32, GRID, DD),
            vm(BF16, PAD, D), vm(BF16, GRID, PAD), vm(BF16, LANES, 2, DEC_ROWS, D),
            vm(BF16, devices, slab, GRID),
            dma(8), dma(16), pltpu.SemaphoreType.DMA, dma(4), dma(4), dma(LANES), dma(LANES),
            dma(12), dma(12), dma(6), dma(6), dma(3), dma(3), dma(devices), dma(devices),
        ],
        compiler_params=pltpu.CompilerParams(
            collective_id=0, has_side_effects=True, vmem_limit_bytes=VMEM_LIMIT
        ),
    )(*args)


CH = 64
DEC_ROWS = 576
ENC_A = 768
ENC_B = 384
DEC_K = DEC_ROWS // CH
B_K = (DEC_ROWS + ENC_A + ENC_B) // CH
ALL_K = B_K + 1
A_TOP = DEC_ROWS
B_TOP = DEC_ROWS + ENC_A
S_TOP = B_TOP + ENC_B
LAG = 2
LEAD = 4
LATE = LEAD + 2 * (DEC_K - LEAD)


def add(x, y):
    return x + y


def backward_and_sums(
    d_enc, x, x1, a, u, y, gp, qkv, p, o, gains, offs,
    w0, w1, proj0, proj1, up0, up1, down0, down1,
    dec, dec_qvb, dec_upb, dec_small,
    out, emb, dx_out,
    gb, gt, ut, part, send, recv, du, gx, dx1, d_o, d_acts, own, send1, recv1, dx32, dx,
    d_upb, d_qvb, d_small,
    acc, yacc, enc_mate, rcy, ry, rx, zl, zr, xc, cl, cr, small32, small,
    load_s, ex_s, ex_r,
    core_s, core_r, corey_s, corey_r, y_s, y_r, x_s, x_r, z_s, zl_r, zr_r,
    bl_s, br_s, b_r, a_s, a_r, emb_s, emb_r, dx_s, dx_r,
):
    sec = lax.axis_index("section")
    lane = lax.axis_index("tensor")
    pos = lax.axis_index("dp")
    count = lax.axis_size("dp")
    mate = lane + 1 - 2 * lax.rem(lane, 2)
    over = lax.rem(lane + 2, LANES)
    cross = lax.rem(mate + 2, LANES)
    first = pos == 0
    last = pos == count - 1
    me = sec * LANES + lane
    devices = 2 * LANES

    def group_peer(step):
        peer = lax.rem(me + step, devices)
        return peer, {"section": lax.div(peer, LANES), "tensor": lax.rem(peer, LANES)}

    barrier = pltpu.get_barrier_semaphore()
    for step in range(1, devices):
        pl.semaphore_signal(barrier, inc=1, device_id_type=MESH, device_id=group_peer(step)[1])

    @pl.when(pos > 0)
    def _():
        pl.semaphore_signal(barrier, inc=1, device_id={"dp": pos - 1}, device_id_type=MESH)

    @pl.when(pos < count - 1)
    def _():
        pl.semaphore_signal(barrier, inc=1, device_id={"dp": pos + 1}, device_id_type=MESH)

    loads = [
        pltpu.make_async_copy(dec.at[lane], acc.at[:, 0:DEC_ROWS, :], load_s.at[0]),
        pltpu.make_async_copy(dec.at[over], yacc.at[:, 0:DEC_ROWS, :], load_s.at[1]),
    ]
    for load in loads:
        load.start()
    small32[...] = jnp.zeros_like(small32)
    small[...] = jnp.zeros_like(small)
    d_small[...] = jnp.zeros_like(d_small)
    gb[0:PAD, :] = d_enc[...]
    ends = jnp.where(first, 0, 1) + jnp.where(last, 0, 1)
    pl.semaphore_wait(barrier, devices - 1 + ends)

    gain = gains[...].astype(F32)
    width = w0.shape[1]
    marks = head_marks(width, ENC_SIZE, BF16)
    marks32 = head_marks(width, ENC_SIZE, F32)

    def rows(k, size=CH):
        return pl.ds(pl.multiple_of(k * size, size), size)

    def give_enc():
        return far(d_enc, gb.at[PAD : 2 * PAD, :], ex_s.at[0], ex_r.at[0], {"tensor": over})

    def give_part(i, half):
        cut = rows(i, 256)
        n = 1 + 2 * i + half
        return far(
            send.at[(1 - half) * PAD : (2 - half) * PAD, cut],
            recv.at[half * PAD : (half + 1) * PAD, cut],
            ex_s.at[n], ex_r.at[n], {"tensor": over},
        )

    def give_last(i):
        cut = rows(i, 256)
        return far(send1.at[:, cut], recv1.at[:, cut], ex_s.at[7 + i], ex_r.at[7 + i], {"tensor": over})

    def ff_back(g, i, down):
        c = rows(i, 256)
        d_down = nn(gt[...], y[g, :, c]).astype(BF16)
        dh = nt(gb[...], down[c, :]) * gp[g, :, c].astype(F32)
        d_upb[g, :, c] = colsum(dh)
        dub = dh.astype(BF16)
        du[g, :, c] = dub
        d_up = nn(ut[...], dub).astype(BF16)
        if g == 0:
            acc[1, A_TOP:B_TOP, c] = d_down
            acc[0, A_TOP:B_TOP, c] = d_up
        else:
            enc_mate[1, 0:ENC_A, c] = d_down
            enc_mate[0, 0:ENC_A, c] = d_up

    def ff_in(i):
        c = rows(i, 256)
        t = nt(du[0], up0[c, :]) + nt(du[1], up1[c, :])
        part[:, c] = t
        send[:, c] = t.astype(BF16)
        give_part(i, 0).start()
        give_part(i, 1).start()

    def norm_two(i):
        del i
        for k in range(D // 256):
            give_part(k, 0).wait_recv()
            give_part(k, 1).wait_recv()

        def body(j):
            r = rows(j, 64)
            da = part[r, :] + recv[r, :].astype(F32)
            hat, scale = normal(x1[r, :])
            g = gb[r, :].astype(F32)
            d = g + normal_back(da, hat, scale, gain[1:2])
            gx[r, :] = d.astype(BF16)
            dx1[r, :] = d

            @pl.when(j < 2)
            def _():
                d_small[1:2, :] += colsum(da * hat)
                d_small[3:4, :] += colsum(da)
                d_small[4:5, :] += colsum(d)
                d_small[5:6, :] += colsum(g)

        loop(2 * PAD // 64, body)

    def attention(g, proj):
        d_proj = tn(o[g], gx[...]).astype(BF16)
        if g == 0:
            acc[1, B_TOP + width : S_TOP, :] = d_proj
        else:
            enc_mate[1, ENC_A + width : ENC_A + 2 * width, :] = d_proj
        d_o[...] = nt(gx[...], proj[...]).astype(BF16)
        for c in range(2):
            r = slice(c * PAD, (c + 1) * PAD)
            dq, dk, dv = attend_back(
                qkv[g, 0, r], qkv[g, 1, r], qkv[g, 2, r], p[g, c], d_o[r, :],
                marks, marks32, ENC_SCALE,
            )
            d_acts[g, 0, r] = dq
            d_acts[g, 1, r] = dk
            d_acts[g, 2, r] = dv
        d_qvb[g, 0:1, :] = colsum(d_acts[g, 0].astype(F32))
        d_qvb[g, 1:2, :] = colsum(d_acts[g, 2].astype(F32))

    def project_in(i):
        c = rows(i, 256)
        t = 0.0
        for g, w in enumerate((w0, w1)):
            for j in range(3):
                t += nn(d_acts[g, j], w[j, :, c])
        own[:, c] = t[:PAD]
        send1[:, c] = t[PAD:].astype(BF16)
        give_last(i).start()

    def project_grad(g):
        for j in range(3):
            row = (j % 2) * width
            d = tn(d_acts[g, j], a[...]).astype(BF16)
            if g == 0:
                acc[j // 2, B_TOP + row : B_TOP + row + width, :] = d
            else:
                enc_mate[j // 2, ENC_A + row : ENC_A + row + width, :] = d

    def norm_one(i):
        del i
        for k in range(D // 256):
            give_last(k).wait_recv()

        def body(j):
            r = rows(j, 64)
            da = own[r, :] + recv1[r, :].astype(F32)
            hat, scale = normal(x[r, :])
            d_small[0:1, :] += colsum(da * hat)
            d_small[2:3, :] += colsum(da)
            dx32[r, :] = dx1[r, :] + normal_back(da, hat, scale, gain[0:1])

        loop(PAD // 64, body)
        turned = jnp.transpose(dx32[...])
        cut = D // devices
        for k in range(devices):
            dx[k] = turned[k * cut : (k + 1) * cut, 0:VIS].astype(BF16)
        for r in range(LANES):
            small32[r, 0:1, 0:512] = dec_upb[:, r * 512 : (r + 1) * 512]
            small32[r, 1:2, 0:128] = dec_qvb[0:1, r * 128 : (r + 1) * 128]
            small32[r, 1:2, 128:256] = dec_qvb[1:2, r * 128 : (r + 1) * 128]
            small32[r, 8:16, 0:512] = dec_small[...]
            small32[r, 16:24, :] = d_small[...]
        for g, shard in enumerate((lane, mate)):
            small32[shard, 2:3, :] = d_upb[g]
            small32[shard, 3:4, 0:192] = d_qvb[g, 0:1]
            small32[shard, 3:4, 256:448] = d_qvb[g, 1:2]
        for r in range(LANES):
            small[r, 0, 0:32] = small32[r].astype(BF16)
        acc[:, S_TOP : S_TOP + CH, :] = small[lane]
        yacc[:, DEC_ROWS : DEC_ROWS + CH, :] = small[over]
        core_copy(LATE, small.at[mate]).start()
        corey_copy(LATE, small.at[cross]).start()
        for step in range(1, devices):
            dx_copy(step).start()
        dx_out[me] = dx[me]

    def core_enc(lo, hi):
        def body(m):
            block = block_of(m)

            @pl.when((block >= lo) & (block < hi))
            def _():
                src = pl.ds(pl.multiple_of(block * CH - DEC_ROWS, CH), CH)
                core_copy(m, enc_mate.at[:, src, :]).start()

        loop(ALL_K, body)

    def first_piece(i):
        del i
        ut[...] = jnp.transpose(u[...].astype(F32)).astype(BF16)
        give_enc().wait_recv()
        gt[...] = jnp.transpose(gb[...].astype(F32)).astype(BF16)

    pieces = [(0, 1, first_piece)]
    for g, down in enumerate((down0, down1)):
        pieces.append((0, 3, lambda i, g=g, down=down: ff_back(g, i, down)))
    pieces.append((3, 4, lambda i: core_enc(DEC_K, DEC_K + ENC_A // CH)))
    pieces.append((3, 4, lambda i: loop(D // 256, ff_in)))
    pieces.append((6, 7, norm_two))
    for g, proj in enumerate((proj0, proj1)):
        pieces.append((7 + g, 8 + g, lambda i, g=g, proj=proj: attention(g, proj)))
    pieces.append((9, 10, lambda i: loop(D // 256, project_in)))
    for g in range(2):
        pieces.append((10 + g, 11 + g, lambda i, g=g: project_grad(g)))
    pieces.append((12, 13, lambda i: core_enc(DEC_K + ENC_A // CH, B_K)))
    pieces.append((13, 14, norm_one))

    def dx_copy(step):
        peer, place = group_peer(step)
        return far(dx.at[peer], dx_out.at[me], dx_s.at[step], dx_r.at[step], place)

    def emb_copy(step):
        return far(
            out.at[:, pl.ds(512, CH), :], emb.at[lane], emb_s.at[step], emb_r.at[step],
            {"tensor": lax.rem(lane + step, LANES)},
        )

    def block_of(m):
        turn = jnp.where(lax.rem(m, 2) == 0, DEC_K + lax.div(m - LEAD, 2), LEAD + lax.div(m - LEAD - 1, 2))
        late = jnp.where(m == LATE, ALL_K - 1, m - 1)
        return jnp.where(m < LEAD, m, jnp.where(m >= LATE, late, turn))

    def is_dec(m):
        return block_of(m) < DEC_K

    def with_y(m):
        return is_dec(m) | (m == LATE)

    def at(m):
        return pl.ds(pl.multiple_of(block_of(m) * CH, CH), CH)

    def pair_at(m):
        return rows(lax.div(m, 2))

    def y_at(m):
        return rows(jnp.minimum(block_of(m), DEC_K))

    def core_copy(m, src):
        return far(src, out.at[:, at(m), :], core_s.at[m], core_r.at[m], {"tensor": mate})

    def corey_copy(m, src):
        return far(src, rcy.at[:, y_at(m), :], corey_s.at[m], corey_r.at[m], {"tensor": mate})

    def y_copy(m):
        cut = y_at(m)
        return far(
            yacc.at[:, cut, :], ry.at[:, cut, :], y_s.at[m], y_r.at[m], {"tensor": over}
        )

    def x_copy(m):
        return far(
            acc.at[1 - sec, at(m), :], rx.at[pair_at(m), :], x_s.at[m], x_r.at[m],
            {"section": 1 - sec},
        )

    def xc_copy(m):
        return far(
            acc.at[:, at(m), :], xc.at[:, pair_at(m), :], x_s.at[m], x_r.at[m],
            {"section": 1 - sec},
        )

    def z_copy(m, whole, right):
        if whole:
            src, dst = acc.at[:, at(m), :], (cl if right else cr).at[:, pair_at(m), :]
        else:
            src, dst = acc.at[sec, at(m), :], (zl if right else zr).at[pair_at(m), :]
        landed = zl_r if right else zr_r
        return far(src, dst, z_s.at[m], landed.at[m], {"dp": pos + 1 if right else pos - 1})

    def b_copy(m, whole, right):
        place = out.at[:, at(m), :] if whole else out.at[sec, at(m), :]
        sent = br_s if right else bl_s
        return far(place, place, sent.at[m], b_r.at[m], {"dp": pos + 1 if right else pos - 1})

    def a_copy(m):
        place = out.at[sec, at(m), :]
        return far(place, place, a_s.at[m], a_r.at[m], {"section": 1 - sec})

    def a_wait(m):
        place = out.at[1 - sec, at(m), :]
        far(place, place, a_s.at[m], a_r.at[m], {"section": 1 - sec}).wait_recv()

    give_enc().start()

    def start_core(m):
        @pl.when(is_dec(m))
        def _():
            core_copy(m, dec.at[mate, :, at(m), :]).start()
            corey_copy(m, dec.at[cross, :, at(m), :]).start()

    loop(LATE, start_core)
    for load in loads:
        load.wait()

    def stage_c(m):
        core_copy(m, out.at[:, at(m), :]).wait_recv()
        acc[:, at(m), :] = add(acc[:, at(m), :], out[:, at(m), :])

        @pl.when(with_y(m))
        def _():
            corey_copy(m, rcy.at[:, y_at(m), :]).wait_recv()
            yacc[:, y_at(m), :] = add(yacc[:, y_at(m), :], rcy[:, y_at(m), :])
            y_copy(m).start()

    def finished(m):
        @pl.when(block_of(m) == DEC_K - 1)
        def _():
            for step in range(1, LANES):
                emb_copy(step).start()
            emb[lane] = out[:, 512 : 512 + CH, :]

    def line_of(root, whole):
        left = pos < root
        right = pos > root
        here = pos == root
        reach = max(root, count - 1 - root)
        level = jnp.where(left, pos, jnp.where(right, count - 1 - pos, reach))
        dist = jnp.where(left, root - pos, pos - root)

        def view(ref, m):
            return ref.at[:, at(m), :] if whole else ref.at[sec, at(m), :]

        def landed(ref, m):
            return ref.at[:, pair_at(m), :] if whole else ref.at[pair_at(m), :]

        from_left, from_right = (cl, cr) if whole else (zl, zr)

        def outer(m):
            @pl.when(left & first)
            def _():
                z_copy(m, whole, True).start()

            @pl.when(right & last)
            def _():
                z_copy(m, whole, False).start()

        def inward(m):
            @pl.when(left & (pos > 0))
            def _():
                z_copy(m, whole, True).wait_recv()
                view(acc, m)[...] = add(view(acc, m)[...], landed(from_left, m)[...])
                z_copy(m, whole, True).start()

            @pl.when(right & (pos < count - 1))
            def _():
                z_copy(m, whole, False).wait_recv()
                view(acc, m)[...] = add(view(acc, m)[...], landed(from_right, m)[...])
                z_copy(m, whole, False).start()

            @pl.when(here)
            def _():
                total = view(acc, m)[...].astype(F32)
                if root > 0:
                    z_copy(m, whole, True).wait_recv()
                    total = total + landed(from_left, m)[...].astype(F32)
                if root < count - 1:
                    z_copy(m, whole, False).wait_recv()
                    total = total + landed(from_right, m)[...].astype(F32)
                if whole:
                    view(acc, m)[...] = total.astype(BF16)
                    xc_copy(m).start()
                else:
                    view(out, m)[...] = total.astype(BF16)
                    spread(m)
                    a_copy(m).start()

        def spread(m):
            if root > 0:
                b_copy(m, whole, False).start()
            if root < count - 1:
                b_copy(m, whole, True).start()

        def crossed(m):
            xc_copy(m).wait_recv()
            view(out, m)[...] = add(view(acc, m)[...], landed(xc, m)[...])
            spread(m)
            finished(m)

        def outward(m):
            b_copy(m, whole, False).wait_recv()

            @pl.when(left & (pos > 0))
            def _():
                b_copy(m, whole, False).start()

            @pl.when(right & (pos < count - 1))
            def _():
                b_copy(m, whole, True).start()

            if whole:
                finished(m)
            else:
                a_copy(m).start()

        def sent(m):
            @pl.when(jnp.logical_not(here))
            def _():
                z_copy(m, whole, True).wait_send()

            @pl.when((pos <= root) & (pos > 0))
            def _():
                b_copy(m, whole, False).wait_send()

            @pl.when((pos >= root) & (pos < count - 1))
            def _():
                b_copy(m, whole, True).wait_send()

            if whole:
                @pl.when(here)
                def _():
                    xc_copy(m).wait_send()
            else:
                x_copy(m).wait_send()
                a_copy(m).wait_send()

        def add_y(m):
            @pl.when(with_y(m))
            def _():
                y_copy(m).wait_recv()
                acc[:, at(m), :] = add(acc[:, at(m), :], ry[:, y_at(m), :])

            if whole:
                outer(m)
            else:
                x_copy(m).start()

        def add_x(m):
            x_copy(m).wait_recv()
            acc[sec, at(m), :] = add(acc[sec, at(m), :], rx[pair_at(m), :])
            outer(m)

        def last_half(m):
            a_wait(m)
            finished(m)

        base = 1 if whole else 2
        back = base + reach + dist + (1 if whole else 0)
        steps = [(back, jnp.logical_not(here), outward), (base + level, level > 0, inward), (1, True, add_y)]
        if whole:
            steps.append((base + reach + 1, here, crossed))
        else:
            steps += [(back + 1, True, last_half), (2, True, add_x)]
        return steps, sent

    low_root = (count - 1) // 2
    high_root = min(low_root + 1, count - 1)
    lines = [
        (lambda m: lax.rem(m, 2) == 1, *line_of(low_root, False)),
        (lambda m: lax.rem(m, 4) == 0, *line_of(low_root, True)),
        (lambda m: lax.rem(m, 4) == 2, *line_of(high_root, True)),
    ]

    def tick(n):
        @pl.when(n < LATE)
        def _():
            for low, high, piece in pieces:
                @pl.when((n >= low) & (n < high))
                def _(low=low, piece=piece):
                    piece(n - low)

        for mine, steps, _ in lines:
            for offset, enabled, stage in steps:
                m = n - LAG * offset

                @pl.when((m >= 0) & (m < ALL_K) & mine(m) & enabled)
                def _(m=m, stage=stage):
                    stage(m)

        @pl.when(n < ALL_K)
        def _():
            stage_c(n)

    far_reach = max(low_root, count - 1 - low_root, high_root, count - 1 - high_root)
    loop(ALL_K + LAG * (3 + 2 * far_reach) + 1, tick)

    def finish(m):
        core_copy(m, out.at[:, at(m), :]).wait_send()

        @pl.when(with_y(m))
        def _():
            corey_copy(m, rcy.at[:, y_at(m), :]).wait_send()
            y_copy(m).wait_send()

        for mine, _, sent in lines:
            @pl.when(mine(m))
            def _(sent=sent):
                sent(m)

    loop(ALL_K, finish)
    for step in range(1, devices):
        dx_copy(step).wait()
    for step in range(1, LANES):
        emb_copy(step).wait()
    give_enc().wait_send()
    for k in range(D // 256):
        give_part(k, 0).wait_send()
        give_part(k, 1).wait_send()
        give_last(k).wait_send()


def backward_call(args, half, hid):
    dma = lambda *s: pltpu.SemaphoreType.DMA(s)
    vm = pltpu.VMEM
    full = ALL_K * CH
    y_half = DEC_ROWS + CH
    k = ALL_K
    rows = 2 * PAD
    cut = D // (2 * LANES)
    specs = [VM] * len(args)
    specs[20] = ANY
    return pl.pallas_call(
        backward_and_sums,
        out_shape=[
            jax.ShapeDtypeStruct((2, full, D), BF16),
            jax.ShapeDtypeStruct((LANES, 2, CH, D), BF16),
            jax.ShapeDtypeStruct((2 * LANES, cut, VIS), BF16),
        ],
        in_specs=specs,
        out_specs=[VM] * 3,
        scratch_shapes=[
            vm((rows, D), BF16), vm((D, rows), BF16), vm((D, rows), BF16),
            vm((rows, D), F32), vm((rows, D), BF16), vm((rows, D), BF16),
            vm((2, rows, hid), BF16), vm((rows, D), BF16), vm((rows, D), F32),
            vm((rows, half), BF16), vm((2, 3, rows, half), BF16),
            vm((PAD, D), F32), vm((PAD, D), BF16), vm((PAD, D), BF16), vm((PAD, D), F32),
            vm((2 * LANES, cut, VIS), BF16),
            vm((2, 1, hid), F32), vm((2, 2, half), F32), vm((8, D), F32),
            vm((2, full, D), BF16), vm((2, y_half, D), BF16), vm((2, ENC_A + ENC_B, D), BF16),
            vm((2, y_half, D), BF16), vm((2, y_half, D), BF16),
            vm((full // 2, D), BF16), vm((full // 2, D), BF16), vm((full // 2, D), BF16),
            vm((2, full // 2, D), BF16), vm((2, full // 2, D), BF16), vm((2, full // 2, D), BF16),
            vm((LANES, 32, D), F32), vm((LANES, 2, CH, D), BF16),
            dma(3), dma(10), dma(10),
            dma(k), dma(k), dma(k), dma(k), dma(k), dma(k),
            dma(k), dma(k), dma(k), dma(k), dma(k),
            dma(k), dma(k), dma(k), dma(k), dma(k), dma(LANES), dma(LANES),
            dma(2 * LANES), dma(2 * LANES),
        ],
        compiler_params=pltpu.CompilerParams(
            collective_id=1, has_side_effects=True, vmem_limit_bytes=VMEM_LIMIT
        ),
    )(*args)


def finish_grads(
    total, emb,
    e_qkv, e_qvb, e_proj, e_up, e_upb, e_down, e_gain, e_off,
    d_qkv, d_qvb, d_proj, d_up, d_upb, d_down, d_gain, d_off, d_ew, d_ev,
):
    half = e_proj.shape[0]
    e_up[...] = total[0, A_TOP:B_TOP, :].astype(F32)
    e_down[...] = jnp.transpose(total[1, A_TOP:B_TOP, :].astype(F32))
    e_qkv[0] = total[0, B_TOP : B_TOP + half, :].astype(F32)
    e_qkv[1] = total[0, B_TOP + half : S_TOP, :].astype(F32)
    e_qkv[2] = total[1, B_TOP : B_TOP + half, :].astype(F32)
    e_proj[...] = total[1, B_TOP + half : S_TOP, :].astype(F32)
    d_up[...] = total[0, 0:512, 0:512].astype(F32)
    d_down[0:256, :] = jnp.transpose(total[0, 0:512, 512:768].astype(F32))
    d_down[256:512, :] = jnp.transpose(total[1, 0:512, 512:768].astype(F32))
    for j in range(3):
        d_qkv[j] = total[1, 0:512, j * 128 : (j + 1) * 128].astype(F32)
    for j in range(LANES):
        cut = slice(j * 128, (j + 1) * 128)
        d_proj[:, cut] = total[1, cut, 384:512].astype(F32)
    for k in range(LANES):
        for h in range(2):
            top = k * 192 + h * 64
            d_ew[top : top + 64, :] = emb[k, h, :, 0:512].astype(F32)
            d_ew[k * 192 + 128 : (k + 1) * 192, h * 256 : (h + 1) * 256] = emb[
                k, h, :, 512:768
            ].astype(F32)
    little = total[0, S_TOP : S_TOP + 32, :].astype(F32)
    d_upb[...] = little[0:1, 0:512]
    d_qvb[0:1, :] = little[1:2, 0:128]
    d_qvb[1:2, :] = little[1:2, 128:256]
    e_upb[...] = little[2:3]
    e_qvb[0:1, :] = little[3:4, 0:192]
    e_qvb[1:2, :] = little[3:4, 256:448]
    d_gain[...] = little[8:10, 0:512]
    d_off[...] = little[10:14, 0:512]
    d_ev[...] = little[14:16, 0:512]
    e_gain[...] = little[16:18]
    e_off[...] = little[18:22]


def call(kernel, specs, shapes, scratch, args):
    return pl.pallas_call(
        kernel,
        out_shape=[jax.ShapeDtypeStruct(s, d) for s, d in shapes],
        in_specs=specs,
        out_specs=[VM] * len(shapes),
        scratch_shapes=scratch,
        compiler_params=pltpu.CompilerParams(vmem_limit_bytes=VMEM_LIMIT),
    )(*args)


def position_rows():
    quarter = DD // 4
    freq = np.exp(np.arange(quarter, dtype=np.float32) * np.float32(-math.log(10000.0) / quarter))
    angle = np.arange(PAD, dtype=np.float32)[:, None] * freq[None, :].astype(np.float32)
    both = np.concatenate([np.sin(angle), np.cos(angle)], 1).astype(np.float32)
    high = both.astype(jnp.bfloat16)
    low = (both - high.astype(np.float32)).astype(jnp.bfloat16)
    return np.stack([high, low])


def per_device(
    patches, cotangent, widths, visible, window_shift, batch_order,
    encoder_qkv, encoder_qvbias, encoder_proj, encoder_up, encoder_upbias, encoder_down,
    encoder_gains, encoder_offsets,
    decoder_qkv, decoder_qvbias, decoder_proj, decoder_up, decoder_upbias, decoder_down,
    decoder_gains, decoder_offsets, embed_weight, embed_vectors,
):
    qkv0 = encoder_qkv.transpose(1, 2, 0)
    half = qkv0.shape[1]
    hid = encoder_up.shape[1]
    dff = decoder_up.shape[1] * LANES
    flat = patches.transpose(1, 0, 2).reshape(-1, D)
    (
        x, x1, a, u, y, gp, qkv, p, o, qkv1, proj1, up1, down1, dec_buf,
        d_enc, d_dqvb, d_dupb, d_dsmall, out_all,
    ) = forward_call(
        (
            widths, window_shift, batch_order, visible, flat, encoder_gains, encoder_offsets,
            encoder_qvbias, encoder_upbias, decoder_qvbias, decoder_upbias,
            qkv0, encoder_proj, encoder_up, encoder_down,
            decoder_qkv.transpose(1, 0, 2), decoder_proj, decoder_up, decoder_down,
            cotangent, embed_weight, embed_vectors, jnp.asarray(position_rows()),
            decoder_gains, decoder_offsets,
        ),
        half, hid, dff,
    )
    total, emb, dx_all = backward_call(
        (
            d_enc, x, x1, a, u, y, gp, qkv, p, o, encoder_gains, encoder_offsets,
            qkv0, qkv1, encoder_proj, proj1, encoder_up, up1, encoder_down, down1,
            dec_buf, d_dqvb, d_dupb, d_dsmall,
        ),
        half, hid,
    )
    f = lambda *shape: (shape, F32)
    grads = call(
        finish_grads, [VM, VM],
        [
            f(3, half, D), f(2, half), f(half, D), f(D, hid), f(1, hid), f(hid, D), f(2, D), f(4, D),
            f(3, DD, 128), f(2, 128), f(128, DD), f(DD, 512), f(1, 512), f(512, DD), f(2, DD), f(4, DD),
            f(D, DD), f(2, DD),
        ],
        [], (total, emb),
    )
    grads = list(grads)
    grads[0] = grads[0].transpose(2, 0, 1)
    grads[4] = grads[4][0]
    grads[8] = grads[8].transpose(1, 0, 2)
    grads[12] = grads[12][0]
    return (out_all.swapaxes(1, 2), dx_all.swapaxes(1, 2), *grads)


def solution(mesh):
    weights = (
        P(None, None, "tensor"), P(None, "tensor"), P("tensor", None), P(None, "tensor"),
        P("tensor"), P("tensor", None), P(), P(),
    )
    split = P("dp", None, ("section", "tensor"))
    return jax.shard_map(
        per_device,
        mesh=mesh,
        in_specs=(
            P("dp", None, None), P("dp", None, None), P("dp"), P("dp", None), P("dp", None),
            P("dp", None),
        ) + weights + weights + (P(), P()),
        out_specs=(split, split) + weights + weights + (P(), P()),
        check_vma=False,
    )
```

```python
import math

import jax
import jax.numpy as jnp
import numpy as np
from jax import lax
from jax.experimental import pallas as pl
from jax.experimental.pallas import tpu as pltpu
from jax.sharding import PartitionSpec as P

D = 768
HEADS = 12
DD = 512
DHEADS = 16
GRID_ROWS = 64
WIDE = 8
WIN = 4
VIS = 102
CM = 4
GRID = 512
LANES = 4
PAD = 128
EPS = 1e-06
NEG = -10000.0
F32 = jnp.float32
BF16 = jnp.bfloat16
VMEM_LIMIT = 60 * 1024 * 1024

VM = pl.BlockSpec(memory_space=pltpu.VMEM)
SM = pl.BlockSpec(memory_space=pltpu.SMEM)
ANY = pl.BlockSpec(memory_space=pl.ANY)


def nn(a, b):
    return lax.dot_general(a, b, (((1,), (0,)), ((), ())), preferred_element_type=F32)


def nt(a, b):
    return lax.dot_general(a, b, (((1,), (1,)), ((), ())), preferred_element_type=F32)


def tn(a, b):
    return lax.dot_general(a, b, (((0,), (0,)), ((), ())), preferred_element_type=F32)


def loop(count, body, unroll=1):
    def step(i, carry):
        body(i)
        return carry

    lax.fori_loop(0, count, step, 0, unroll=unroll)


def span(i, size):
    return pl.ds(pl.multiple_of(i * size, size), size)


def normal(x):
    center = x - jnp.mean(x, -1, keepdims=True)
    scale = lax.rsqrt(jnp.mean(center * center, -1, keepdims=True) + EPS)
    return center * scale, scale


def normal_back(dy, hat, scale, gain):
    d = dy * gain
    return scale * (
        d - jnp.mean(d, -1, keepdims=True) - hat * jnp.mean(d * hat, -1, keepdims=True)
    )


def gelu_both(h):
    phi = 0.5 * lax.erf(h * math.sqrt(0.5)) + 0.5
    bell = jnp.exp2(h * h * (-0.5 * math.log2(math.e)))
    return h * phi, phi + h * bell * (1.0 / math.sqrt(2.0 * math.pi))


def colsum(x):
    return jnp.sum(x, 0, keepdims=True)


def head_marks(width, size, dtype):
    lane = lax.broadcasted_iota(jnp.int32, (1, width), 1)
    return [((lane >= h * size) & (lane < (h + 1) * size)).astype(dtype) for h in range(width // size)]


def stacked(x, marks):
    return jnp.concatenate([x * m for m in marks], 0)


def softmax(s):
    e = jnp.exp(s - jnp.max(s, -1, keepdims=True))
    return e * (1.0 / jnp.sum(e, -1, keepdims=True))


def attend(q, k, v, marks, shape_scores):
    stack = stacked(k, marks)
    s = nt(q, stack)
    keys = k.shape[0]
    p = jnp.concatenate(
        [
            softmax(shape_scores(s[:, h * keys : (h + 1) * keys])).astype(BF16)
            for h in range(len(marks))
        ],
        1,
    )
    return p, nn(p, stacked(v, marks)).astype(BF16)


def attend_back(q, k, v, p, d_out, marks, marks32, scale):
    keys = k.shape[0]
    d_p = nt(d_out, stacked(v, marks))
    parts = []
    for h in range(len(marks)):
        cut = slice(h * keys, (h + 1) * keys)
        ph = p[:, cut].astype(F32)
        dh = d_p[:, cut]
        inner = jnp.sum(ph * dh, -1, keepdims=True)
        parts.append((ph * (dh - inner) * scale).astype(BF16))
    dr = jnp.concatenate(parts, 1)
    d_q = nn(dr, stacked(k, marks))
    d_k_all = tn(dr, q)
    d_v_all = tn(p, d_out)
    d_k = 0.0
    d_v = 0.0
    for h in range(len(marks)):
        cut = slice(h * keys, (h + 1) * keys)
        d_k += d_k_all[cut] * marks32[h]
        d_v += d_v_all[cut] * marks32[h]
    return d_q.astype(BF16), d_k.astype(BF16), d_v.astype(BF16)


ENC_SIZE = D // HEADS
ENC_SCALE = ENC_SIZE ** -0.5
DEC_SIZE = DD // DHEADS
DEC_SCALE = DEC_SIZE ** -0.5


def attend_flat(q, k, v, marks, rows32, allowed, scale):
    keys = k.shape[0]
    s = nt(stacked(k, marks), q)
    parts = []
    for h in range(len(marks)):
        x = jnp.where(allowed, s[h * keys : (h + 1) * keys] * scale, NEG)
        e = jnp.exp(x - jnp.max(x, 0, keepdims=True))
        parts.append((e * (1.0 / jnp.sum(e, 0, keepdims=True))).astype(BF16))
    p = jnp.concatenate(parts, 0)
    turned = jnp.transpose(v.astype(F32))
    wide = jnp.concatenate([(turned * m).astype(BF16) for m in rows32], 1)
    return p, nn(wide, p).astype(BF16)


def attend_flat_back(q, k, v, p, d_out, marks, marks32, rows32, scale):
    keys = k.shape[0]
    d_p = nt(stacked(v, marks), d_out)
    parts = []
    for h in range(len(marks)):
        cut = slice(h * keys, (h + 1) * keys)
        ph = p[cut].astype(F32)
        dh = d_p[cut]
        inner = jnp.sum(ph * dh, 0, keepdims=True)
        parts.append((ph * (dh - inner) * scale).astype(BF16))
    dr = jnp.concatenate(parts, 0)
    turned = jnp.transpose(k.astype(F32))
    wide = jnp.concatenate([(turned * m).astype(BF16) for m in rows32], 1)
    d_q = jnp.transpose(nn(wide, dr))
    d_k_all = nn(dr, q)
    d_v_all = nn(p, d_out)
    d_k = 0.0
    d_v = 0.0
    for h in range(len(marks)):
        cut = slice(h * keys, (h + 1) * keys)
        d_k += d_k_all[cut] * marks32[h]
        d_v += d_v_all[cut] * marks32[h]
    return d_q.astype(BF16), d_k.astype(BF16), d_v.astype(BF16)


MESH = pl.DeviceIdType.MESH


def far(src, dst, send, recv, peer):
    return pltpu.make_async_remote_copy(
        src_ref=src, dst_ref=dst, send_sem=send, recv_sem=recv, device_id=peer, device_id_type=MESH
    )


def forward_and_decoder(
    wid, shifts, order, vis, pat, gains, offs, b_qv, b_up, b_dqv, b_dup,
    h_qkv, h_proj, h_up, h_down, h_dqkv, h_dproj, h_dup, h_ddown,
    cot_hbm, ew, evec, table, dgains, doffs,
    o_x, o_x1, o_a, o_u, o_y, o_gp, o_qkv, o_p, o_o, o_w, o_wproj, o_wup, o_wdown, o_dec,
    d_enc, d_qvb, d_upb, d_small, dec_out,
    w_qkv, w_proj, w_up, w_down, bias, biases, qkv, proj, up, down,
    ex, ea, eu, ey, egp, eqkv, ep, eo, ex1, epart, esend, erecv, esend2, erecv2, eown,
    cot, x0, x1, a, acts, probs, o, u, ut, y, gp, g32, gb, gt, acc, e_ref, hot, buf, dsend,
    load_s, out_s, cot_s, w_s, w_r, bias_s, bias_r, dw_s, dw_r, ex_s, ex_r, ex2_s, ex2_r, do_s, do_r,
):
    sec = lax.axis_index("section")
    lane = lax.axis_index("tensor")
    mate = lane + 1 - 2 * lax.rem(lane, 2)
    over = lax.rem(lane + 2, LANES)
    cross = lax.rem(mate + 2, LANES)
    me = sec * LANES + lane
    devices = 2 * LANES
    clip = me
    clips = (me, sec * LANES + over)

    def group_peer(step):
        peer = lax.rem(me + step, devices)
        return peer, {"section": lax.div(peer, LANES), "tensor": lax.rem(peer, LANES)}

    own = [
        pltpu.make_async_copy(src, dst.at[0], load_s.at[n])
        for n, (src, dst) in enumerate(
            ((h_qkv, w_qkv), (h_proj, w_proj), (h_up, w_up), (h_down, w_down))
        )
    ]

    def place(n, shard):
        thick = (128, 128, 512, 512)[n]
        cut = pl.ds(pl.multiple_of(shard * thick, thick), thick)
        return (qkv.at[:, :, cut], proj.at[cut, :], up.at[:, cut], down.at[cut, :])[n]

    shards = (h_dqkv, h_dproj, h_dup, h_ddown)
    keep = [
        pltpu.make_async_copy(shards[n], place(n, lane), load_s.at[4 + n]) for n in range(4)
    ]
    for copy in own + keep:
        copy.start()
    fetch = pltpu.make_async_copy(cot_hbm.at[clip], cot, cot_s)
    fetch.start()

    barrier = pltpu.get_barrier_semaphore()
    for step in range(1, devices):
        pl.semaphore_signal(barrier, inc=1, device_id_type=MESH, device_id=group_peer(step)[1])
    bias[...] = jnp.zeros_like(bias)
    half = w_proj.shape[1]
    bias[0:1, :] = b_up[...].astype(F32).reshape(1, -1)
    bias[1:3, 0:half] = b_qv[...].astype(F32)
    bias[3:4, 0:512] = b_dup[...].astype(F32).reshape(1, -1)
    bias[4:6, 0:128] = b_dqv[...].astype(F32)
    biases[lane] = bias[...]
    pl.semaphore_wait(barrier, devices - 1)

    def enc_weight(n):
        src = (h_qkv, h_proj, h_up, h_down)[n]
        dst = (w_qkv, w_proj, w_up, w_down)[n]
        return far(src, dst.at[1], w_s.at[n], w_r.at[n], {"tensor": mate})

    def bias_copy(step):
        return far(
            bias, biases.at[lane], bias_s.at[step], bias_r.at[step],
            {"tensor": lax.rem(lane + step, LANES)},
        )

    def dec_weight(n, kind):
        peer = over if kind == 0 else mate
        src = shards[n] if kind < 2 else place(n, over)
        dst = place(n, lane if kind < 2 else over)
        return far(src, dst, dw_s.at[3 * n + kind], dw_r.at[3 * n + kind], {"tensor": peer})

    enc_weight(0).start()
    for step in range(1, LANES):
        bias_copy(step).start()
    enc_weight(1).start()
    for n in (0, 1):
        dec_weight(n, 0).start()
    enc_weight(2).start()
    enc_weight(3).start()
    for n in range(4):
        dec_weight(n, 1).start()

    def pass_on(n):
        dec_weight(n, 0).wait_recv()
        dec_weight(n, 2).start()

    def arrived(n):
        keep[n].wait()
        dec_weight(n, 1).wait_recv()
        dec_weight(n, 2).wait_recv()

    egain = gains[...].astype(F32)
    eoff = offs[...].astype(F32)
    stride = pat.shape[0] // VIS
    for c in range(2):
        row = lax.broadcasted_iota(jnp.int32, (PAD, pat.shape[0]), 0)
        col = lax.broadcasted_iota(jnp.int32, (PAD, pat.shape[0]), 1)
        pick = (col == row * stride + clips[c]).astype(F32).astype(BF16)
        ex[c * PAD : (c + 1) * PAD, :] = nn(pick, pat[...])

    emarks = head_marks(half, ENC_SIZE, BF16)
    key = lax.broadcasted_iota(jnp.int32, (PAD, PAD), 1)
    floor = jnp.where(key < VIS, NEG, -1e30)
    blocks = D // 256

    def give_part(i, side):
        cut = span(i, 256)
        return far(
            esend.at[(1 - side) * PAD : (2 - side) * PAD, cut],
            erecv.at[side * PAD : (side + 1) * PAD, cut],
            ex_s.at[2 * i + side], ex_r.at[2 * i + side], {"tensor": over},
        )

    for c in range(2):
        rows = slice(c * PAD, (c + 1) * PAD)
        hat, _ = normal(ex[rows, :])
        ea[rows, :] = (hat * egain[0:1] + eoff[0:1]).astype(BF16)
        limit = (VIS * wid[clips[c]]) // WIDE
        for g, shard in enumerate((lane, mate)):
            if c == 0 and g == 0:
                own[0].wait()
            if c == 0 and g == 1:
                enc_weight(0).wait_recv()
                for step in range(1, LANES):
                    bias_copy(step).wait_recv()
            if g == 0:
                bq, bv = bias[1:2, 0:half], bias[2:3, 0:half]
            else:
                bq, bv = biases[shard, 1:2, 0:half], biases[shard, 2:3, 0:half]
            eqkv[g, 0, rows] = (nt(ea[rows, :], w_qkv[g, 0]) + bq).astype(BF16)
            eqkv[g, 1, rows] = nt(ea[rows, :], w_qkv[g, 1]).astype(BF16)
            eqkv[g, 2, rows] = (nt(ea[rows, :], w_qkv[g, 2]) + bv).astype(BF16)
            p, out = attend(
                eqkv[g, 0, rows], eqkv[g, 1, rows], eqkv[g, 2, rows], emarks,
                lambda s: jnp.where(key < limit, s * ENC_SCALE, floor),
            )
            ep[g, c] = p
            eo[g, rows] = out
        if c == 0:
            own[1].wait()
            enc_weight(1).wait_recv()
        for i in range(blocks):
            cut = slice(i * 256, (i + 1) * 256)
            t = nn(eo[0, rows], w_proj[0, :, cut]) + nn(eo[1, rows], w_proj[1, :, cut])
            epart[rows, cut] = t
            esend[rows, cut] = t.astype(BF16)
            give_part(i, 1 - c).start()
    pass_on(0)
    own[2].wait()
    enc_weight(2).wait_recv()

    def give_last(i):
        cut = span(i, 256)
        return far(
            esend2.at[:, cut], erecv2.at[:, cut], ex2_s.at[i], ex2_r.at[i], {"tensor": over}
        )

    for c in (1, 0):
        rows = slice(c * PAD, (c + 1) * PAD)
        for i in range(blocks):
            give_part(i, c).wait_recv()
        t = ex[rows, :] + epart[rows, :] + erecv[rows, :].astype(F32) + eoff[2:3]
        ex1[rows, :] = t
        hat, _ = normal(t)
        eu[rows, :] = (hat * egain[1:2] + eoff[1:2]).astype(BF16)
        if c == 0:
            dec_weight(2, 0).start()
        for g, shard in enumerate((lane, mate)):

            def enc_ff(i, g=g, shard=shard, rows=rows):
                cut = span(i, 256)
                h = nn(eu[rows, :], w_up[g, :, cut]) + biases[shard, 0:1, cut]
                act, slope = gelu_both(h)
                ey[g, rows, cut] = act.astype(BF16)
                egp[g, rows, cut] = slope.astype(BF16)

            loop(w_up.shape[2] // 256, enc_ff, unroll=3)
        if c == 1:
            own[3].wait()
            enc_weight(3).wait_recv()
        for i in range(blocks):
            cut = slice(i * 256, (i + 1) * 256)
            t = nn(ey[0, rows], w_down[0, :, cut]) + nn(ey[1, rows], w_down[1, :, cut])
            if c == 0:
                eown[:, cut] = t
            else:
                esend2[:, cut] = t.astype(BF16)
                give_last(i).start()
    outs = [
        pltpu.make_async_copy(src, dst, out_s.at[n])
        for n, (src, dst) in enumerate(
            (
                (ex.at[0:PAD, :], o_x), (ex1, o_x1), (ea, o_a), (eu, o_u), (ey, o_y), (egp, o_gp),
                (eqkv, o_qkv), (ep, o_p), (eo, o_o), (w_qkv.at[1], o_w), (w_proj.at[1], o_wproj),
                (w_up.at[1], o_wup), (w_down.at[1], o_wdown),
            )
        )
    ]
    for copy in outs:
        copy.start()
    pass_on(1)
    pass_on(2)
    for i in range(blocks):
        give_last(i).wait_recv()
    dec_weight(3, 0).start()

    width = wid[clip]
    bits = jnp.where(width == WIDE, 3, 2)
    turn = shifts[0, clip] * width
    mod = GRID - 1
    spot = 0
    for i in range(order.shape[1]):
        spot = spot + jnp.where(order[0, i] == clip, i, 0)
    batch = spot // CM
    count = 0
    for i in range(order.shape[1]):
        count = count + jnp.where(batch == i // CM, wid[order[0, i]], 0)
    factor_rows = CM * GRID / (jnp.full((1, 1), count, jnp.int32) * GRID_ROWS).astype(F32)

    def slot_of(index):
        return (index - turn) & mod

    def code_of(slot):
        band = ((slot >> bits) + shifts[0, clip]) >> 2
        strip = ((slot & (width - 1)) + shifts[1, clip]) >> 2
        return band * 4 + strip

    e_ref[...] = (ex1[0:PAD, :] + eown[...] + erecv2[...].astype(F32) + eoff[3:4]).astype(BF16)
    vec = evec[...].astype(F32)
    m = (nn(e_ref[...], ew[...]) + vec[0:1]).astype(BF16)
    seen = vis[pl.ds(clip, 1), :]
    target = jnp.concatenate([(seen + turn) & mod, jnp.full((1, PAD - VIS), -1, jnp.int32)], 1)
    gain = dgains[...].astype(F32)
    offsets = doffs[...].astype(F32)

    def start(i):
        r = span(i, PAD)
        index = lax.broadcasted_iota(jnp.int32, (PAD, PAD), 0) + i * PAD
        column = lax.broadcasted_iota(jnp.int32, (PAD, PAD), 1)
        match = index == target
        oh = match.astype(F32).astype(BF16)
        hot[r, :] = oh
        hit = jnp.sum(match.astype(F32), -1, keepdims=True)
        grid = jnp.where(hit > 0, nn(oh, m), vec[1:2]).astype(BF16).astype(F32)
        slot = slot_of(index)
        by_row = ((slot >> bits) == column).astype(F32).astype(BF16)
        by_col = ((slot & (width - 1)) == column).astype(F32).astype(BF16)
        row_part = nn(by_row, table[0]) + nn(by_row, table[1])
        col_part = nn(by_col, table[0]) + nn(by_col, table[1])
        x = grid + jnp.concatenate([row_part, col_part], 1)
        x0[r, :] = x
        hat, _ = normal(x)
        a[r, :] = (hat * gain[0:1] + offsets[0:1]).astype(BF16)

    loop(GRID // PAD, start)
    arrived(0)

    def dec_bias(row, size):
        return jnp.concatenate([biases[k, row : row + 1, 0:size] for k in range(LANES)], 1)

    def project(i):
        r = span(i, 256)
        rows = a[r, :]
        acts[0, r, :] = (nn(rows, qkv[0]) + dec_bias(4, 128)).astype(BF16)
        acts[1, r, :] = nn(rows, qkv[1]).astype(BF16)
        acts[2, r, :] = (nn(rows, qkv[2]) + dec_bias(5, 128)).astype(BF16)

    loop(2, project)
    pass_on(3)
    marks = head_marks(128, DEC_SIZE, BF16)
    marks32 = head_marks(128, DEC_SIZE, F32)
    dim = lax.broadcasted_iota(jnp.int32, (128, 1), 0)
    rows32 = [
        ((dim >= h * DEC_SIZE) & (dim < (h + 1) * DEC_SIZE)).astype(F32) for h in range(len(marks))
    ]

    def attention(i):
        r = span(i, PAD)
        key_slot = slot_of(lax.broadcasted_iota(jnp.int32, (PAD, PAD), 0) + i * PAD)
        row_slot = slot_of(lax.broadcasted_iota(jnp.int32, (PAD, PAD), 1) + i * PAD)
        allowed = (code_of(row_slot) == code_of(key_slot)) & (key_slot < GRID_ROWS * width)
        for g in range(DD // 128):
            c = slice(g * 128, (g + 1) * 128)
            p, out = attend_flat(
                acts[0, r, c], acts[1, r, c], acts[2, r, c], marks, rows32, allowed, DEC_SCALE
            )
            probs[i, g * 512 : (g + 1) * 512, :] = p
            o[c, r] = out

    loop(GRID // PAD, attention, unroll=2)
    arrived(1)

    def mix(i):
        r = span(i, PAD)
        x = x0[r, :] + tn(o[:, r], proj[...]) + offsets[2:3]
        x1[r, :] = x
        hat, _ = normal(x)
        un = hat * gain[1:2] + offsets[1:2]
        u[r, :] = un.astype(BF16)
        ut[:, r] = jnp.transpose(un).astype(BF16)

    loop(GRID // PAD, mix)
    arrived(2)

    def ff(i):
        k = lax.div(i, 4)
        side = lax.rem(lax.div(i, 2), 2)
        c = span(lax.div(i, 2), 256)
        r = span(lax.rem(i, 2), 256)
        h = nn(u[r, :], up[:, c]) + biases[k, 3:4, span(side, 256)]
        act, slope = gelu_both(h)
        y[r, c] = act.astype(BF16)
        gp[r, c] = slope.astype(BF16)

    loop(2 * up.shape[1] // 256, ff, unroll=2)
    arrived(3)
    fetch.wait()
    slot_col = slot_of(lax.broadcasted_iota(jnp.int32, (GRID, 1), 0))
    valid = (slot_col < GRID_ROWS * width).astype(F32)
    rolled = slot_of(lax.broadcasted_iota(jnp.int32, (GRID, GRID), 0))
    perm = (rolled == lax.broadcasted_iota(jnp.int32, (GRID, GRID), 1)).astype(F32).astype(BF16)

    def out(i):
        r = span(lax.rem(i, 2), 256)
        c = span(lax.div(i, 2), 256)
        acc[r, c] = nn(y[r, :], down[:, c])

    loop(4, out)
    full = ((acc[...] + x1[...] + offsets[3:4]) * valid).astype(BF16)
    turned = tn(full, perm).astype(BF16)
    for k in range(devices):
        dsend[k] = turned[k * dsend.shape[1] : (k + 1) * dsend.shape[1]]

    def decoded_copy(step):
        peer, spot = group_peer(step)
        return far(dsend.at[peer], dec_out.at[me], do_s.at[step], do_r.at[step], spot)

    for step in range(1, devices):
        decoded_copy(step).start()
    dec_out[me] = dsend[me]
    g = nn(perm, cot[...]) * valid * factor_rows
    g32[...] = g
    gb[...] = g.astype(BF16)
    gt[...] = jnp.transpose(g).astype(BF16)
    d_small[0:5, :] = jnp.zeros((5, DD), F32)
    d_small[5:6, :] = colsum(g)
    d_small[6:8, :] = jnp.zeros((2, DD), F32)

    def ff_back(i):
        c = span(i, 256)
        shard = lax.div(i, 2)
        side = lax.rem(i, 2)
        buf[shard, side, 0:512, 512:768] = nn(gt[...], y[:, c]).astype(BF16)
        dh = nt(gb[...], down[c, :]) * gp[:, c].astype(F32)
        d_upb[:, c] = colsum(dh)
        du = dh.astype(BF16)
        gp[:, c] = du
        buf[shard, 0, 0:512, span(side, 256)] = nn(ut[...], du).astype(BF16)

    loop(up.shape[1] // 256, ff_back, unroll=2)
    early = pltpu.make_async_copy(buf.at[:, 0, 0:512, :], o_dec.at[:, 0, 0:512, :], out_s.at[13])
    early.start()

    def ff_in(i):
        r = span(lax.rem(i, 2), 256)
        c = span(lax.div(i, 2), 256)
        acc[r, c] = nt(gp[r, :], up[c, :])

    loop(4, ff_in)

    def mix_back(i):
        r = span(i, PAD)
        hat, scale = normal(x1[r, :])
        da = acc[r, :]
        dx = g32[r, :] + normal_back(da, hat, scale, gain[1:2])
        d_small[1:2, :] += colsum(da * hat)
        d_small[3:4, :] += colsum(da)
        d_small[4:5, :] += colsum(dx)
        g32[r, :] = dx
        dxb = dx.astype(BF16)
        gb[r, :] = dxb
        u[r, :] = nt(dxb, proj[...]).astype(BF16)

    loop(GRID // PAD, mix_back)
    d_proj = nn(o[...], gb[...]).astype(BF16)
    for k in range(LANES):
        for j in range(LANES):
            block = d_proj[k * 128 : (k + 1) * 128, j * 128 : (j + 1) * 128]
            buf[k, 1, j * 128 : (j + 1) * 128, 384:512] = block

    def attention_back(i):
        r = span(i, PAD)
        for k in range(DD // 128):
            c = slice(k * 128, (k + 1) * 128)
            dq, dk, dv = attend_flat_back(
                acts[0, r, c], acts[1, r, c], acts[2, r, c],
                probs[i, k * 512 : (k + 1) * 512, :], u[r, c], marks, marks32, rows32, DEC_SCALE,
            )
            acts[0, r, c] = dq
            acts[1, r, c] = dk
            acts[2, r, c] = dv

    loop(GRID // PAD, attention_back, unroll=2)
    d_qvb[0:1, :] = colsum(acts[0].astype(F32))
    d_qvb[1:2, :] = colsum(acts[2].astype(F32))

    def project_back(i):
        r = span(lax.rem(i, 2), 256)
        c = span(lax.div(i, 2), 256)
        acc[r, c] = (
            nt(acts[0, r, :], qkv[0, c, :])
            + nt(acts[1, r, :], qkv[1, c, :])
            + nt(acts[2, r, :], qkv[2, c, :])
        )

    loop(4, project_back)
    gt[...] = jnp.transpose(a[...].astype(F32)).astype(BF16)
    for j in range(3):
        d_qkv = nn(gt[...], acts[j]).astype(BF16)
        for k in range(LANES):
            buf[k, 1, 0:512, j * 128 : (j + 1) * 128] = d_qkv[:, k * 128 : (k + 1) * 128]

    def start_back(i):
        r = span(i, PAD)
        hat, scale = normal(x0[r, :])
        da = acc[r, :]
        dx = g32[r, :] + normal_back(da, hat, scale, gain[0:1])
        d_small[0:1, :] += colsum(da * hat)
        d_small[2:3, :] += colsum(da)
        dg = dx.astype(BF16)
        gb[r, :] = dg
        hit = jnp.sum(hot[r, :].astype(F32), -1, keepdims=True)
        d_small[7:8, :] += colsum(jnp.where(hit > 0, 0.0, dg.astype(F32)))

    loop(GRID // PAD, start_back)
    dm = tn(hot[...], gb[...])
    d_small[6:7, :] = colsum(dm)
    dmb = dm.astype(BF16)
    d_enc[...] = nt(dmb, ew[...]).astype(BF16)
    d_ew = tn(e_ref[...], dmb).astype(BF16)
    for k in range(LANES):
        for h in range(2):
            top = k * 192 + h * 64
            buf[k, h, 512:576, 0:512] = d_ew[top : top + 64]
            buf[k, h, 512:576, 512:768] = d_ew[k * 192 + 128 : (k + 1) * 192, h * 256 : (h + 1) * 256]

    rest = [
        pltpu.make_async_copy(buf.at[:, 1], o_dec.at[:, 1], out_s.at[14]),
        pltpu.make_async_copy(buf.at[:, 0, 512:576, :], o_dec.at[:, 0, 512:576, :], out_s.at[15]),
    ]
    for copy in rest:
        copy.start()
    for copy in outs + [early] + rest:
        copy.wait()
    for n in range(4):
        enc_weight(n).wait_send()
        for kind in range(3):
            dec_weight(n, kind).wait_send()
    for step in range(1, LANES):
        bias_copy(step).wait_send()
    for i in range(blocks):
        give_part(i, 0).wait_send()
        give_part(i, 1).wait_send()
        give_last(i).wait_send()
    for step in range(1, devices):
        decoded_copy(step).wait()


def forward_call(args, half, hid, dff):
    dma = lambda *s: pltpu.SemaphoreType.DMA(s)
    vm = lambda dtype, *shape: pltpu.VMEM(shape, dtype)
    rows = 2 * PAD
    keys = PAD * half // ENC_SIZE
    devices = 2 * LANES
    slab = DD // devices
    kept = [
        ((PAD, D), F32), ((rows, D), F32), ((rows, D), BF16), ((rows, D), BF16),
        ((2, rows, hid), BF16), ((2, rows, hid), BF16), ((2, 3, rows, half), BF16),
        ((2, 2, PAD, keys), BF16), ((2, rows, half), BF16),
        ((3, half, D), BF16), ((half, D), BF16), ((D, hid), BF16), ((hid, D), BF16),
        ((LANES, 2, DEC_ROWS, D), BF16),
    ]
    made = [
        ((PAD, D), BF16), ((2, DD), F32), ((1, dff), F32), ((8, DD), F32),
        ((devices, slab, GRID), BF16),
    ]
    return pl.pallas_call(
        forward_and_decoder,
        out_shape=[jax.ShapeDtypeStruct(s, d) for s, d in kept + made],
        in_specs=[SM, SM, SM] + [VM] * 8 + [ANY] * 9 + [VM] * 5,
        out_specs=[ANY] * len(kept) + [VM] * len(made),
        scratch_shapes=[
            vm(BF16, 2, 3, half, D), vm(BF16, 2, half, D), vm(BF16, 2, D, hid), vm(BF16, 2, hid, D),
            vm(F32, 8, D), vm(F32, LANES, 8, D),
            vm(BF16, 3, DD, DD), vm(BF16, DD, DD), vm(BF16, DD, dff), vm(BF16, dff, DD),
            vm(F32, rows, D), vm(BF16, rows, D), vm(BF16, rows, D), vm(BF16, 2, rows, hid),
            vm(BF16, 2, rows, hid), vm(BF16, 2, 3, rows, half), vm(BF16, 2, 2, PAD, keys),
            vm(BF16, 2, rows, half), vm(F32, rows, D), vm(F32, rows, D), vm(BF16, rows, D),
            vm(BF16, rows, D), vm(BF16, PAD, D), vm(BF16, PAD, D), vm(F32, PAD, D),
            vm(BF16, GRID, DD), vm(F32, GRID, DD), vm(F32, GRID, DD), vm(BF16, GRID, DD),
            vm(BF16, 3, GRID, DD), vm(BF16, GRID // PAD, DHEADS * PAD, PAD), vm(BF16, DD, GRID),
            vm(BF16, GRID, DD), vm(BF16, DD, GRID), vm(BF16, GRID, dff), vm(BF16, GRID, dff),
            vm(F32, GRID, DD), vm(BF16, GRID, DD), vm(BF16, DD, GRID), vm(F32, GRID, DD),
            vm(BF16, PAD, D), vm(BF16, GRID, PAD), vm(BF16, LANES, 2, DEC_ROWS, D),
            vm(BF16, devices, slab, GRID),
            dma(8), dma(16), pltpu.SemaphoreType.DMA, dma(4), dma(4), dma(LANES), dma(LANES),
            dma(12), dma(12), dma(6), dma(6), dma(3), dma(3), dma(devices), dma(devices),
        ],
        compiler_params=pltpu.CompilerParams(
            collective_id=0, has_side_effects=True, vmem_limit_bytes=VMEM_LIMIT
        ),
    )(*args)


CH = 64
DEC_ROWS = 576
ENC_A = 768
ENC_B = 384
DEC_K = DEC_ROWS // CH
B_K = (DEC_ROWS + ENC_A + ENC_B) // CH
ALL_K = B_K + 1
A_TOP = DEC_ROWS
B_TOP = DEC_ROWS + ENC_A
S_TOP = B_TOP + ENC_B
LAG = 2
LEAD = 4
LATE = LEAD + 2 * (DEC_K - LEAD)
HALVED = ALL_K - 4


def add(x, y):
    return x + y


def backward_and_sums(
    d_enc, gains,
    h_u, h_y, h_gp, h_down0, h_down1, h_up0, h_up1,
    h_x, h_x1, h_a, h_qkv, h_p, h_o, h_w0, h_w1, h_proj0, h_proj1,
    dec, dec_qvb, dec_upb, dec_small,
    out, emb, dx_out,
    gb, gt, ut, part, send, recv, du, gx, dx1, d_o, d_acts, own, send1, recv1, dx32, dx,
    d_upb, d_qvb, d_small,
    acc, yacc, enc_mate, rcy, ry, rx, zl, zr, xc, cl, cr, small32, small,
    u, y, gp, down0, down1, up0, up1, x, x1, a, qkv, p, o, w0, w1, proj0, proj1, fetch_s,
    load_s, ex_s, ex_r,
    core_s, core_r, corey_s, corey_r, y_s, y_r, x_s, x_r, z_s, zl_r, zr_r,
    bl_s, br_s, b_r, a_s, a_r, emb_s, emb_r, dx_s, dx_r,
):
    sec = lax.axis_index("section")
    lane = lax.axis_index("tensor")
    pos = lax.axis_index("dp")
    count = lax.axis_size("dp")
    mate = lane + 1 - 2 * lax.rem(lane, 2)
    over = lax.rem(lane + 2, LANES)
    cross = lax.rem(mate + 2, LANES)
    first = pos == 0
    last = pos == count - 1
    me = sec * LANES + lane
    devices = 2 * LANES

    def group_peer(step):
        peer = lax.rem(me + step, devices)
        return peer, {"section": lax.div(peer, LANES), "tensor": lax.rem(peer, LANES)}

    barrier = pltpu.get_barrier_semaphore()
    for step in range(1, devices):
        pl.semaphore_signal(barrier, inc=1, device_id_type=MESH, device_id=group_peer(step)[1])

    @pl.when(pos > 0)
    def _():
        pl.semaphore_signal(barrier, inc=1, device_id={"dp": pos - 1}, device_id_type=MESH)

    @pl.when(pos < count - 1)
    def _():
        pl.semaphore_signal(barrier, inc=1, device_id={"dp": pos + 1}, device_id_type=MESH)

    fetches = [
        pltpu.make_async_copy(src, dst, fetch_s.at[n])
        for n, (src, dst) in enumerate(
            (
                (h_u, u), (h_y, y), (h_gp, gp), (h_down0, down0), (h_down1, down1), (h_up0, up0),
                (h_up1, up1), (h_x, x), (h_x1, x1), (h_a, a), (h_qkv, qkv), (h_p, p), (h_o, o),
                (h_w0, w0), (h_w1, w1), (h_proj0, proj0), (h_proj1, proj1),
            )
        )
    ]
    for fetch in fetches:
        fetch.start()
    loads = [
        pltpu.make_async_copy(dec.at[lane], acc.at[:, 0:DEC_ROWS, :], load_s.at[0]),
        pltpu.make_async_copy(dec.at[over], yacc.at[:, 0:DEC_ROWS, :], load_s.at[1]),
    ]
    for load in loads:
        load.start()
    small32[...] = jnp.zeros_like(small32)
    small[...] = jnp.zeros_like(small)
    d_small[...] = jnp.zeros_like(d_small)
    gb[0:PAD, :] = d_enc[...]
    ends = jnp.where(first, 0, 1) + jnp.where(last, 0, 1)
    pl.semaphore_wait(barrier, devices - 1 + ends)

    gain = gains[...].astype(F32)
    width = w0.shape[1]
    marks = head_marks(width, ENC_SIZE, BF16)
    marks32 = head_marks(width, ENC_SIZE, F32)

    def rows(k, size=CH):
        return pl.ds(pl.multiple_of(k * size, size), size)

    def give_enc():
        return far(d_enc, gb.at[PAD : 2 * PAD, :], ex_s.at[0], ex_r.at[0], {"tensor": over})

    def give_part(i, half):
        cut = rows(i, 256)
        n = 1 + 2 * i + half
        return far(
            send.at[(1 - half) * PAD : (2 - half) * PAD, cut],
            recv.at[half * PAD : (half + 1) * PAD, cut],
            ex_s.at[n], ex_r.at[n], {"tensor": over},
        )

    def give_last(i):
        cut = rows(i, 256)
        return far(send1.at[:, cut], recv1.at[:, cut], ex_s.at[7 + i], ex_r.at[7 + i], {"tensor": over})

    def ff_back(g, i, down):
        c = rows(i, 256)
        d_down = nn(gt[...], y[g, :, c]).astype(BF16)
        dh = nt(gb[...], down[c, :]) * gp[g, :, c].astype(F32)
        d_upb[g, :, c] = colsum(dh)
        dub = dh.astype(BF16)
        du[g, :, c] = dub
        d_up = nn(ut[...], dub).astype(BF16)
        if g == 0:
            acc[1, A_TOP:B_TOP, c] = d_down
            acc[0, A_TOP:B_TOP, c] = d_up
        else:
            enc_mate[1, 0:ENC_A, c] = d_down
            enc_mate[0, 0:ENC_A, c] = d_up

    def ff_in(i):
        c = rows(i, 256)
        t = nt(du[0], up0[c, :]) + nt(du[1], up1[c, :])
        part[:, c] = t
        send[:, c] = t.astype(BF16)
        give_part(i, 0).start()
        give_part(i, 1).start()

    def norm_two(i):
        del i
        for fetch in fetches[7:]:
            fetch.wait()
        for k in range(D // 256):
            give_part(k, 0).wait_recv()
            give_part(k, 1).wait_recv()

        def body(j):
            r = rows(j, 64)
            da = part[r, :] + recv[r, :].astype(F32)
            hat, scale = normal(x1[r, :])
            g = gb[r, :].astype(F32)
            d = g + normal_back(da, hat, scale, gain[1:2])
            gx[r, :] = d.astype(BF16)
            dx1[r, :] = d

            @pl.when(j < 2)
            def _():
                d_small[1:2, :] += colsum(da * hat)
                d_small[3:4, :] += colsum(da)
                d_small[4:5, :] += colsum(d)
                d_small[5:6, :] += colsum(g)

        loop(2 * PAD // 64, body)

    def attention(g, proj):
        d_proj = tn(o[g], gx[...]).astype(BF16)
        if g == 0:
            acc[1, B_TOP + width : S_TOP, :] = d_proj
        else:
            enc_mate[1, ENC_A + width : ENC_A + 2 * width, :] = d_proj
        d_o[...] = nt(gx[...], proj[...]).astype(BF16)
        for c in range(2):
            r = slice(c * PAD, (c + 1) * PAD)
            dq, dk, dv = attend_back(
                qkv[g, 0, r], qkv[g, 1, r], qkv[g, 2, r], p[g, c], d_o[r, :],
                marks, marks32, ENC_SCALE,
            )
            d_acts[g, 0, r] = dq
            d_acts[g, 1, r] = dk
            d_acts[g, 2, r] = dv
        d_qvb[g, 0:1, :] = colsum(d_acts[g, 0].astype(F32))
        d_qvb[g, 1:2, :] = colsum(d_acts[g, 2].astype(F32))

    def project_in(i):
        c = rows(i, 256)
        t = 0.0
        for g, w in enumerate((w0, w1)):
            for j in range(3):
                t += nn(d_acts[g, j], w[j, :, c])
        own[:, c] = t[:PAD]
        send1[:, c] = t[PAD:].astype(BF16)
        give_last(i).start()

    def project_grad(g):
        for j in range(3):
            row = (j % 2) * width
            d = tn(d_acts[g, j], a[...]).astype(BF16)
            if g == 0:
                acc[j // 2, B_TOP + row : B_TOP + row + width, :] = d
            else:
                enc_mate[j // 2, ENC_A + row : ENC_A + row + width, :] = d

    def norm_one(i):
        del i
        for k in range(D // 256):
            give_last(k).wait_recv()

        def body(j):
            r = rows(j, 64)
            da = own[r, :] + recv1[r, :].astype(F32)
            hat, scale = normal(x[r, :])
            d_small[0:1, :] += colsum(da * hat)
            d_small[2:3, :] += colsum(da)
            dx32[r, :] = dx1[r, :] + normal_back(da, hat, scale, gain[0:1])

        loop(PAD // 64, body)
        turned = jnp.transpose(dx32[...])
        cut = D // devices
        for k in range(devices):
            dx[k] = turned[k * cut : (k + 1) * cut, 0:VIS].astype(BF16)
        for r in range(LANES):
            small32[r, 0:1, 0:512] = dec_upb[:, r * 512 : (r + 1) * 512]
            small32[r, 1:2, 0:128] = dec_qvb[0:1, r * 128 : (r + 1) * 128]
            small32[r, 1:2, 128:256] = dec_qvb[1:2, r * 128 : (r + 1) * 128]
            small32[r, 8:16, 0:512] = dec_small[...]
            small32[r, 16:24, :] = d_small[...]
        for g, shard in enumerate((lane, mate)):
            small32[shard, 2:3, :] = d_upb[g]
            small32[shard, 3:4, 0:192] = d_qvb[g, 0:1]
            small32[shard, 3:4, 256:448] = d_qvb[g, 1:2]
        for r in range(LANES):
            small[r, 0, 0:32] = small32[r].astype(BF16)
        acc[:, S_TOP : S_TOP + CH, :] = small[lane]
        yacc[:, DEC_ROWS : DEC_ROWS + CH, :] = small[over]
        core_copy(LATE, small.at[mate]).start()
        corey_copy(LATE, small.at[cross]).start()
        for step in range(1, devices):
            dx_copy(step).start()
        dx_out[me] = dx[me]

    def core_enc(lo, hi):
        def body(m):
            block = block_of(m)

            @pl.when((block >= lo) & (block < hi))
            def _():
                src = pl.ds(pl.multiple_of(block * CH - DEC_ROWS, CH), CH)
                core_copy(m, enc_mate.at[:, src, :]).start()

        loop(ALL_K, body)

    def first_piece(i):
        del i
        for fetch in fetches[:7]:
            fetch.wait()
        ut[...] = jnp.transpose(u[...].astype(F32)).astype(BF16)
        give_enc().wait_recv()
        gt[...] = jnp.transpose(gb[...].astype(F32)).astype(BF16)

    pieces = [(0, 1, first_piece)]
    for g, down in enumerate((down0, down1)):
        pieces.append((0, 3, lambda i, g=g, down=down: ff_back(g, i, down)))
    pieces.append((3, 4, lambda i: core_enc(DEC_K, DEC_K + ENC_A // CH)))
    pieces.append((3, 4, lambda i: loop(D // 256, ff_in)))
    pieces.append((6, 7, norm_two))
    for g, proj in enumerate((proj0, proj1)):
        pieces.append((7 + g, 8 + g, lambda i, g=g, proj=proj: attention(g, proj)))
    pieces.append((9, 10, lambda i: loop(D // 256, project_in)))
    for g in range(2):
        pieces.append((10 + g, 11 + g, lambda i, g=g: project_grad(g)))
    pieces.append((12, 13, lambda i: core_enc(DEC_K + ENC_A // CH, B_K)))
    pieces.append((13, 14, norm_one))

    def dx_copy(step):
        peer, place = group_peer(step)
        return far(dx.at[peer], dx_out.at[me], dx_s.at[step], dx_r.at[step], place)

    def emb_copy(step):
        return far(
            out.at[:, pl.ds(512, CH), :], emb.at[lane], emb_s.at[step], emb_r.at[step],
            {"tensor": lax.rem(lane + step, LANES)},
        )

    def block_of(m):
        turn = jnp.where(lax.rem(m, 2) == 0, DEC_K + lax.div(m - LEAD, 2), LEAD + lax.div(m - LEAD - 1, 2))
        late = jnp.where(m == LATE, ALL_K - 1, m - 1)
        return jnp.where(m < LEAD, m, jnp.where(m >= LATE, late, turn))

    def is_dec(m):
        return block_of(m) < DEC_K

    def with_y(m):
        return is_dec(m) | (m == LATE)

    def at(m):
        return pl.ds(pl.multiple_of(block_of(m) * CH, CH), CH)

    def pair_at(m):
        return rows(jnp.where(m < HALVED, lax.div(m, 2), m - HALVED // 2))

    def y_at(m):
        return rows(jnp.minimum(block_of(m), DEC_K))

    def core_copy(m, src):
        return far(src, out.at[:, at(m), :], core_s.at[m], core_r.at[m], {"tensor": mate})

    def corey_copy(m, src):
        return far(src, rcy.at[:, y_at(m), :], corey_s.at[m], corey_r.at[m], {"tensor": mate})

    def y_copy(m):
        cut = y_at(m)
        return far(
            yacc.at[:, cut, :], ry.at[:, cut, :], y_s.at[m], y_r.at[m], {"tensor": over}
        )

    def x_copy(m):
        return far(
            acc.at[1 - sec, at(m), :], rx.at[pair_at(m), :], x_s.at[m], x_r.at[m],
            {"section": 1 - sec},
        )

    def xc_copy(m):
        return far(
            acc.at[:, at(m), :], xc.at[:, pair_at(m), :], x_s.at[m], x_r.at[m],
            {"section": 1 - sec},
        )

    def z_copy(m, whole, right):
        if whole:
            src, dst = acc.at[:, at(m), :], (cl if right else cr).at[:, pair_at(m), :]
        else:
            src, dst = acc.at[sec, at(m), :], (zl if right else zr).at[pair_at(m), :]
        landed = zl_r if right else zr_r
        return far(src, dst, z_s.at[m], landed.at[m], {"dp": pos + 1 if right else pos - 1})

    def b_copy(m, whole, right):
        place = out.at[:, at(m), :] if whole else out.at[sec, at(m), :]
        sent = br_s if right else bl_s
        return far(place, place, sent.at[m], b_r.at[m], {"dp": pos + 1 if right else pos - 1})

    def a_copy(m):
        place = out.at[sec, at(m), :]
        return far(place, place, a_s.at[m], a_r.at[m], {"section": 1 - sec})

    def a_wait(m):
        place = out.at[1 - sec, at(m), :]
        far(place, place, a_s.at[m], a_r.at[m], {"section": 1 - sec}).wait_recv()

    give_enc().start()

    def start_core(m):
        @pl.when(is_dec(m))
        def _():
            core_copy(m, dec.at[mate, :, at(m), :]).start()
            corey_copy(m, dec.at[cross, :, at(m), :]).start()

    loop(LATE, start_core)
    for load in loads:
        load.wait()

    def stage_c(m):
        core_copy(m, out.at[:, at(m), :]).wait_recv()
        acc[:, at(m), :] = add(acc[:, at(m), :], out[:, at(m), :])

        @pl.when(with_y(m))
        def _():
            corey_copy(m, rcy.at[:, y_at(m), :]).wait_recv()
            yacc[:, y_at(m), :] = add(yacc[:, y_at(m), :], rcy[:, y_at(m), :])
            y_copy(m).start()

    def finished(m):
        @pl.when(block_of(m) == DEC_K - 1)
        def _():
            for step in range(1, LANES):
                emb_copy(step).start()
            emb[lane] = out[:, 512 : 512 + CH, :]

    def line_of(root, whole):
        left = pos < root
        right = pos > root
        here = pos == root
        reach = max(root, count - 1 - root)
        level = jnp.where(left, pos, jnp.where(right, count - 1 - pos, reach))
        dist = jnp.where(left, root - pos, pos - root)

        def view(ref, m):
            return ref.at[:, at(m), :] if whole else ref.at[sec, at(m), :]

        def landed(ref, m):
            return ref.at[:, pair_at(m), :] if whole else ref.at[pair_at(m), :]

        from_left, from_right = (cl, cr) if whole else (zl, zr)

        def outer(m):
            @pl.when(left & first)
            def _():
                z_copy(m, whole, True).start()

            @pl.when(right & last)
            def _():
                z_copy(m, whole, False).start()

        def inward(m):
            @pl.when(left & (pos > 0))
            def _():
                z_copy(m, whole, True).wait_recv()
                view(acc, m)[...] = add(view(acc, m)[...], landed(from_left, m)[...])
                z_copy(m, whole, True).start()

            @pl.when(right & (pos < count - 1))
            def _():
                z_copy(m, whole, False).wait_recv()
                view(acc, m)[...] = add(view(acc, m)[...], landed(from_right, m)[...])
                z_copy(m, whole, False).start()

            @pl.when(here)
            def _():
                total = view(acc, m)[...].astype(F32)
                if root > 0:
                    z_copy(m, whole, True).wait_recv()
                    total = total + landed(from_left, m)[...].astype(F32)
                if root < count - 1:
                    z_copy(m, whole, False).wait_recv()
                    total = total + landed(from_right, m)[...].astype(F32)
                if whole:
                    view(acc, m)[...] = total.astype(BF16)
                    xc_copy(m).start()
                else:
                    view(out, m)[...] = total.astype(BF16)
                    spread(m)
                    a_copy(m).start()

        def spread(m):
            if root > 0:
                b_copy(m, whole, False).start()
            if root < count - 1:
                b_copy(m, whole, True).start()

        def crossed(m):
            xc_copy(m).wait_recv()
            view(out, m)[...] = add(view(acc, m)[...], landed(xc, m)[...])
            spread(m)
            finished(m)

        def outward(m):
            b_copy(m, whole, False).wait_recv()

            @pl.when(left & (pos > 0))
            def _():
                b_copy(m, whole, False).start()

            @pl.when(right & (pos < count - 1))
            def _():
                b_copy(m, whole, True).start()

            if whole:
                finished(m)
            else:
                a_copy(m).start()

        def sent(m):
            @pl.when(jnp.logical_not(here))
            def _():
                z_copy(m, whole, True).wait_send()

            @pl.when((pos <= root) & (pos > 0))
            def _():
                b_copy(m, whole, False).wait_send()

            @pl.when((pos >= root) & (pos < count - 1))
            def _():
                b_copy(m, whole, True).wait_send()

            if whole:
                @pl.when(here)
                def _():
                    xc_copy(m).wait_send()
            else:
                x_copy(m).wait_send()
                a_copy(m).wait_send()

        def add_y(m):
            @pl.when(with_y(m))
            def _():
                y_copy(m).wait_recv()
                acc[:, at(m), :] = add(acc[:, at(m), :], ry[:, y_at(m), :])

            if whole:
                outer(m)
            else:
                x_copy(m).start()

        def add_x(m):
            x_copy(m).wait_recv()
            acc[sec, at(m), :] = add(acc[sec, at(m), :], rx[pair_at(m), :])
            outer(m)

        def last_half(m):
            a_wait(m)
            finished(m)

        base = 1 if whole else 2
        back = base + reach + dist + (1 if whole else 0)
        steps = [(back, jnp.logical_not(here), outward), (base + level, level > 0, inward), (1, True, add_y)]
        if whole:
            steps.append((base + reach + 1, here, crossed))
        else:
            steps += [(back + 1, True, last_half), (2, True, add_x)]
        return steps, sent

    low_root = (count - 1) // 2
    high_root = min(low_root + 1, count - 1)
    lines = [
        (lambda m: (lax.rem(m, 2) == 1) | (m >= HALVED), *line_of(low_root, False)),
        (lambda m: (lax.rem(m, 4) == 0) & (m < HALVED), *line_of(low_root, True)),
        (lambda m: (lax.rem(m, 4) == 2) & (m < HALVED), *line_of(high_root, True)),
    ]

    def tick(n):
        @pl.when(n < LATE)
        def _():
            for low, high, piece in pieces:
                @pl.when((n >= low) & (n < high))
                def _(low=low, piece=piece):
                    piece(n - low)

        for mine, steps, _ in lines:
            for offset, enabled, stage in steps:
                m = n - LAG * offset

                @pl.when((m >= 0) & (m < ALL_K) & mine(m) & enabled)
                def _(m=m, stage=stage):
                    stage(m)

        @pl.when(n < ALL_K)
        def _():
            stage_c(n)

    far_reach = max(low_root, count - 1 - low_root, high_root, count - 1 - high_root)
    loop(ALL_K + LAG * (3 + 2 * far_reach) + 1, tick)

    def finish(m):
        core_copy(m, out.at[:, at(m), :]).wait_send()

        @pl.when(with_y(m))
        def _():
            corey_copy(m, rcy.at[:, y_at(m), :]).wait_send()
            y_copy(m).wait_send()

        for mine, _, sent in lines:
            @pl.when(mine(m))
            def _(sent=sent):
                sent(m)

    loop(ALL_K, finish)
    for step in range(1, devices):
        dx_copy(step).wait()
    for step in range(1, LANES):
        emb_copy(step).wait()
    give_enc().wait_send()
    for k in range(D // 256):
        give_part(k, 0).wait_send()
        give_part(k, 1).wait_send()
        give_last(k).wait_send()


def backward_call(args, half, hid):
    dma = lambda *s: pltpu.SemaphoreType.DMA(s)
    vm = pltpu.VMEM
    full = ALL_K * CH
    y_half = DEC_ROWS + CH
    whole = HALVED // 2 * CH
    by_half = full - whole
    k = ALL_K
    rows = 2 * PAD
    cut = D // (2 * LANES)
    specs = [VM, VM] + [ANY] * 18 + [VM] * 3
    return pl.pallas_call(
        backward_and_sums,
        out_shape=[
            jax.ShapeDtypeStruct((2, full, D), BF16),
            jax.ShapeDtypeStruct((LANES, 2, CH, D), BF16),
            jax.ShapeDtypeStruct((2 * LANES, cut, VIS), BF16),
        ],
        in_specs=specs,
        out_specs=[VM] * 3,
        scratch_shapes=[
            vm((rows, D), BF16), vm((D, rows), BF16), vm((D, rows), BF16),
            vm((rows, D), F32), vm((rows, D), BF16), vm((rows, D), BF16),
            vm((2, rows, hid), BF16), vm((rows, D), BF16), vm((rows, D), F32),
            vm((rows, half), BF16), vm((2, 3, rows, half), BF16),
            vm((PAD, D), F32), vm((PAD, D), BF16), vm((PAD, D), BF16), vm((PAD, D), F32),
            vm((2 * LANES, cut, VIS), BF16),
            vm((2, 1, hid), F32), vm((2, 2, half), F32), vm((8, D), F32),
            vm((2, full, D), BF16), vm((2, y_half, D), BF16), vm((2, ENC_A + ENC_B, D), BF16),
            vm((2, y_half, D), BF16), vm((2, y_half, D), BF16),
            vm((by_half, D), BF16), vm((by_half, D), BF16), vm((by_half, D), BF16),
            vm((2, whole, D), BF16), vm((2, whole, D), BF16), vm((2, whole, D), BF16),
            vm((LANES, 32, D), F32), vm((LANES, 2, CH, D), BF16),
            *[vm(v.shape, v.dtype) for v in args[2:19]], dma(17), dma(2), dma(10), dma(10),
            dma(k), dma(k), dma(k), dma(k), dma(k), dma(k),
            dma(k), dma(k), dma(k), dma(k), dma(k),
            dma(k), dma(k), dma(k), dma(k), dma(k), dma(LANES), dma(LANES),
            dma(2 * LANES), dma(2 * LANES),
        ],
        compiler_params=pltpu.CompilerParams(
            collective_id=1, has_side_effects=True, vmem_limit_bytes=VMEM_LIMIT
        ),
    )(*args)


def finish_grads(
    total, emb, decoded, dx, decoded_out, dx_out,
    e_qkv, e_qvb, e_proj, e_up, e_upb, e_down, e_gain, e_off,
    d_qkv, d_qvb, d_proj, d_up, d_upb, d_down, d_gain, d_off, d_ew, d_ev,
):
    half = e_proj.shape[0]
    decoded_out[...] = decoded[...]
    dx_out[...] = dx[...]
    e_up[...] = total[0, A_TOP:B_TOP, :].astype(F32)
    e_down[...] = jnp.transpose(total[1, A_TOP:B_TOP, :].astype(F32))
    e_qkv[0] = total[0, B_TOP : B_TOP + half, :].astype(F32)
    e_qkv[1] = total[0, B_TOP + half : S_TOP, :].astype(F32)
    e_qkv[2] = total[1, B_TOP : B_TOP + half, :].astype(F32)
    e_proj[...] = total[1, B_TOP + half : S_TOP, :].astype(F32)
    d_up[...] = total[0, 0:512, 0:512].astype(F32)
    d_down[0:256, :] = jnp.transpose(total[0, 0:512, 512:768].astype(F32))
    d_down[256:512, :] = jnp.transpose(total[1, 0:512, 512:768].astype(F32))
    for j in range(3):
        d_qkv[j] = total[1, 0:512, j * 128 : (j + 1) * 128].astype(F32)
    for j in range(LANES):
        cut = slice(j * 128, (j + 1) * 128)
        d_proj[:, cut] = total[1, cut, 384:512].astype(F32)
    for k in range(LANES):
        for h in range(2):
            top = k * 192 + h * 64
            d_ew[top : top + 64, :] = emb[k, h, :, 0:512].astype(F32)
            d_ew[k * 192 + 128 : (k + 1) * 192, h * 256 : (h + 1) * 256] = emb[
                k, h, :, 512:768
            ].astype(F32)
    little = total[0, S_TOP : S_TOP + 32, :].astype(F32)
    d_upb[...] = little[0, 0:512]
    d_qvb[0:1, :] = little[1:2, 0:128]
    d_qvb[1:2, :] = little[1:2, 128:256]
    e_upb[...] = little[2]
    e_qvb[0:1, :] = little[3:4, 0:192]
    e_qvb[1:2, :] = little[3:4, 256:448]
    d_gain[...] = little[8:10, 0:512]
    d_off[...] = little[10:14, 0:512]
    d_ev[...] = little[14:16, 0:512]
    e_gain[...] = little[16:18]
    e_off[...] = little[18:22]


def call(kernel, specs, shapes, scratch, args):
    return pl.pallas_call(
        kernel,
        out_shape=[jax.ShapeDtypeStruct(s, d) for s, d in shapes],
        in_specs=specs,
        out_specs=[VM] * len(shapes),
        scratch_shapes=scratch,
        compiler_params=pltpu.CompilerParams(vmem_limit_bytes=VMEM_LIMIT),
    )(*args)


def position_rows():
    quarter = DD // 4
    freq = np.exp(np.arange(quarter, dtype=np.float32) * np.float32(-math.log(10000.0) / quarter))
    angle = np.arange(PAD, dtype=np.float32)[:, None] * freq[None, :].astype(np.float32)
    both = np.concatenate([np.sin(angle), np.cos(angle)], 1).astype(np.float32)
    high = both.astype(jnp.bfloat16)
    low = (both - high.astype(np.float32)).astype(jnp.bfloat16)
    return np.stack([high, low])


def per_device(
    patches, cotangent, widths, visible, window_shift, batch_order,
    encoder_qkv, encoder_qvbias, encoder_proj, encoder_up, encoder_upbias, encoder_down,
    encoder_gains, encoder_offsets,
    decoder_qkv, decoder_qvbias, decoder_proj, decoder_up, decoder_upbias, decoder_down,
    decoder_gains, decoder_offsets, embed_weight, embed_vectors,
):
    qkv0 = encoder_qkv.transpose(1, 2, 0)
    half = qkv0.shape[1]
    hid = encoder_up.shape[1]
    dff = decoder_up.shape[1] * LANES
    flat = patches.transpose(1, 0, 2).reshape(-1, D)
    (
        x, x1, a, u, y, gp, qkv, p, o, qkv1, proj1, up1, down1, dec_buf,
        d_enc, d_dqvb, d_dupb, d_dsmall, out_all,
    ) = forward_call(
        (
            widths, window_shift.T, batch_order, visible, flat, encoder_gains, encoder_offsets,
            encoder_qvbias, encoder_upbias, decoder_qvbias, decoder_upbias,
            qkv0, encoder_proj, encoder_up, encoder_down,
            decoder_qkv.transpose(1, 0, 2), decoder_proj, decoder_up, decoder_down,
            cotangent, embed_weight, embed_vectors, jnp.asarray(position_rows()),
            decoder_gains, decoder_offsets,
        ),
        half, hid, dff,
    )
    total, emb, dx_all = backward_call(
        (
            d_enc, encoder_gains, u, y, gp, encoder_down, down1, encoder_up, up1,
            x, x1, a, qkv, p, o, qkv0, qkv1, encoder_proj, proj1,
            dec_buf, d_dqvb, d_dupb, d_dsmall,
        ),
        half, hid,
    )
    f = lambda *shape: (shape, F32)
    out_all, dx_all, *grads = call(
        finish_grads, [VM] * 4,
        [
            (out_all.shape, BF16), (dx_all.shape, BF16), f(3, half, D), f(2, half), f(half, D), f(D, hid), f(hid), f(hid, D), f(2, D), f(4, D),
            f(3, DD, 128), f(2, 128), f(128, DD), f(DD, 512), f(512), f(512, DD), f(2, DD), f(4, DD),
            f(D, DD), f(2, DD),
        ],
        [], (total, emb, out_all, dx_all),
    )
    grads[0] = grads[0].transpose(2, 0, 1)
    grads[8] = grads[8].transpose(1, 0, 2)
    return (out_all.swapaxes(1, 2), dx_all.swapaxes(1, 2), *grads)


def solution(mesh):
    weights = (
        P(None, None, "tensor"), P(None, "tensor"), P("tensor", None), P(None, "tensor"),
        P("tensor"), P("tensor", None), P(), P(),
    )
    split = P("dp", None, ("section", "tensor"))
    return jax.shard_map(
        per_device,
        mesh=mesh,
        in_specs=(
            P("dp", None, None), P("dp", None, None), P("dp"), P("dp", None), P("dp", None),
            P("dp", None),
        ) + weights + weights + (P(), P()),
        out_specs=(split, split) + weights + weights + (P(), P()),
        check_vma=False,
    )
```

```python
import math

import jax
import jax.numpy as jnp
import numpy as np
from jax import lax
from jax.experimental import pallas as pl
from jax.experimental.pallas import tpu as pltpu
from jax.sharding import PartitionSpec as P

D = 768
HEADS = 12
DD = 512
DHEADS = 16
GRID_ROWS = 64
WIDE = 8
WIN = 4
VIS = 102
CM = 4
GRID = 512
LANES = 4
PAD = 128
EPS = 1e-06
NEG = -10000.0
F32 = jnp.float32
BF16 = jnp.bfloat16
VMEM_LIMIT = 60 * 1024 * 1024

VM = pl.BlockSpec(memory_space=pltpu.VMEM)
SM = pl.BlockSpec(memory_space=pltpu.SMEM)
ANY = pl.BlockSpec(memory_space=pl.ANY)


def nn(a, b):
    return lax.dot_general(a, b, (((1,), (0,)), ((), ())), preferred_element_type=F32)


def nt(a, b):
    return lax.dot_general(a, b, (((1,), (1,)), ((), ())), preferred_element_type=F32)


def tn(a, b):
    return lax.dot_general(a, b, (((0,), (0,)), ((), ())), preferred_element_type=F32)


def loop(count, body, unroll=1):
    def step(i, carry):
        body(i)
        return carry

    lax.fori_loop(0, count, step, 0, unroll=unroll)


def span(i, size):
    return pl.ds(pl.multiple_of(i * size, size), size)


def normal(x):
    center = x - jnp.mean(x, -1, keepdims=True)
    scale = lax.rsqrt(jnp.mean(center * center, -1, keepdims=True) + EPS)
    return center * scale, scale


def normal_back(dy, hat, scale, gain):
    d = dy * gain
    return scale * (
        d - jnp.mean(d, -1, keepdims=True) - hat * jnp.mean(d * hat, -1, keepdims=True)
    )


def gelu_both(h):
    phi = 0.5 * lax.erf(h * math.sqrt(0.5)) + 0.5
    bell = jnp.exp2(h * h * (-0.5 * math.log2(math.e)))
    return h * phi, phi + h * bell * (1.0 / math.sqrt(2.0 * math.pi))


def colsum(x):
    return jnp.sum(x, 0, keepdims=True)


def head_marks(width, size, dtype):
    lane = lax.broadcasted_iota(jnp.int32, (1, width), 1)
    return [((lane >= h * size) & (lane < (h + 1) * size)).astype(dtype) for h in range(width // size)]


def stacked(x, marks):
    return jnp.concatenate([x * m for m in marks], 0)


LOG2E = math.log2(math.e)


def attend(q, k, v, marks, ones, masked, scale):
    keys = k.shape[0]
    s = nt(q, stacked(k, marks))
    parts = []
    for h in range(len(marks)):
        x = masked(s[:, h * keys : (h + 1) * keys] * (scale * LOG2E))
        parts.append(jnp.exp2(x - jnp.max(x, -1, keepdims=True)).astype(BF16))
    e = jnp.concatenate(parts, 1)
    width = q.shape[1]
    if width % 128:
        top, total = nn(e, stacked(v, marks)), nn(e, ones)
    else:
        both = nn(e, jnp.concatenate([stacked(v, marks), ones], 1))
        top, total = both[:, :width], both[:, width:]
    inverse = 1.0 / total
    return e, (top * inverse).astype(BF16), inverse


def attend_back(q, k, v, e, o, inverse, d_out, marks, marks32, rows32, ones, scale):
    keys = k.shape[0]
    width = q.shape[1]
    d_one = d_out.astype(F32) * inverse
    d_two = (d_one * o.astype(F32)).astype(BF16)
    d_one = d_one.astype(BF16)
    if width % 128:
        d_s = nt(d_one, stacked(v, marks)) - nt(d_two, ones)
    else:
        d_s = nt(
            jnp.concatenate([d_one, d_two], 1), jnp.concatenate([stacked(v, marks), -ones], 1)
        )
    dr = (e.astype(F32) * d_s * scale).astype(BF16)
    d_q = nn(dr, stacked(k, marks)).astype(BF16)
    if width % 128:
        d_k_all, d_v_all = tn(dr, q), tn(e, d_one)
        d_k = d_v = 0.0
        for h in range(len(marks)):
            cut = slice(h * keys, (h + 1) * keys)
            d_k += d_k_all[cut] * marks32[h]
            d_v += d_v_all[cut] * marks32[h]
        return d_q, d_k.astype(BF16), d_v.astype(BF16)
    d_k_all = nn(jnp.transpose(q.astype(F32)).astype(BF16), dr)
    d_v_all = nn(jnp.transpose(d_one.astype(F32)).astype(BF16), e)
    d_k = d_v = 0.0
    for h in range(len(marks)):
        cut = slice(h * keys, (h + 1) * keys)
        d_k += d_k_all[:, cut] * rows32[h]
        d_v += d_v_all[:, cut] * rows32[h]
    return d_q, jnp.transpose(d_k).astype(BF16), jnp.transpose(d_v).astype(BF16)


def ones_per_head(keys, marks):
    return jnp.concatenate([jnp.broadcast_to(m, (keys, m.shape[1])) for m in marks], 0)


ENC_SIZE = D // HEADS
ENC_SCALE = ENC_SIZE ** -0.5
DEC_SIZE = DD // DHEADS
DEC_SCALE = DEC_SIZE ** -0.5


MESH = pl.DeviceIdType.MESH


def far(src, dst, send, recv, peer):
    return pltpu.make_async_remote_copy(
        src_ref=src, dst_ref=dst, send_sem=send, recv_sem=recv, device_id=peer, device_id_type=MESH
    )


def forward_and_decoder(
    wid, shifts, order, vis, pat, gains, offs, b_qv, b_up, b_dqv, b_dup,
    h_qkv, h_proj, h_up, h_down, h_dqkv, h_dproj, h_dup, h_ddown,
    cot_hbm, ew, evec, table, dgains, doffs,
    o_x, o_x1, o_a, o_u, o_y, o_gp, o_qkv, o_p, o_o, o_w, o_wproj, o_wup, o_wdown, o_dec,
    d_enc, d_qvb, d_upb, d_small, dec_out,
    w_qkv, w_proj, w_up, w_down, bias, biases, qkv, proj, up, down,
    ex, ea, eu, ey, egp, eqkv, ep, eo, ex1, epart, esend, erecv, esend2, erecv2, eown,
    cot, x0, x1, a, acts, probs, o, inverse, u, ut, y, gp, g32, gb, gt, acc, e_ref, hot, buf, dsend,
    load_s, out_s, cot_s, w_s, w_r, bias_s, bias_r, dw_s, dw_r, ex_s, ex_r, ex2_s, ex2_r, do_s, do_r,
):
    sec = lax.axis_index("section")
    lane = lax.axis_index("tensor")
    mate = lane + 1 - 2 * lax.rem(lane, 2)
    over = lax.rem(lane + 2, LANES)
    cross = lax.rem(mate + 2, LANES)
    me = sec * LANES + lane
    devices = 2 * LANES
    clip = me
    clips = (me, sec * LANES + over)

    def group_peer(step):
        peer = lax.rem(me + step, devices)
        return peer, {"section": lax.div(peer, LANES), "tensor": lax.rem(peer, LANES)}

    own = [
        pltpu.make_async_copy(src, dst.at[0], load_s.at[n])
        for n, (src, dst) in enumerate(
            ((h_qkv, w_qkv), (h_proj, w_proj), (h_up, w_up), (h_down, w_down))
        )
    ]

    def place(n, shard):
        thick = (128, 128, 512, 512)[n]
        cut = pl.ds(pl.multiple_of(shard * thick, thick), thick)
        return (qkv.at[:, :, cut], proj.at[cut, :], up.at[:, cut], down.at[cut, :])[n]

    shards = (h_dqkv, h_dproj, h_dup, h_ddown)
    keep = [
        pltpu.make_async_copy(shards[n], place(n, lane), load_s.at[4 + n]) for n in range(4)
    ]
    for copy in own + keep:
        copy.start()
    fetch = pltpu.make_async_copy(cot_hbm.at[clip], cot, cot_s)
    fetch.start()

    barrier = pltpu.get_barrier_semaphore()
    for step in range(1, devices):
        pl.semaphore_signal(barrier, inc=1, device_id_type=MESH, device_id=group_peer(step)[1])
    bias[...] = jnp.zeros_like(bias)
    half = w_proj.shape[1]
    bias[0:1, :] = b_up[...].astype(F32).reshape(1, -1)
    bias[1:3, 0:half] = b_qv[...].astype(F32)
    bias[3:4, 0:512] = b_dup[...].astype(F32).reshape(1, -1)
    bias[4:6, 0:128] = b_dqv[...].astype(F32)
    biases[lane] = bias[...]
    pl.semaphore_wait(barrier, devices - 1)

    def enc_weight(n):
        src = (h_qkv, h_proj, h_up, h_down)[n]
        dst = (w_qkv, w_proj, w_up, w_down)[n]
        return far(src, dst.at[1], w_s.at[n], w_r.at[n], {"tensor": mate})

    def bias_copy(step):
        return far(
            bias, biases.at[lane], bias_s.at[step], bias_r.at[step],
            {"tensor": lax.rem(lane + step, LANES)},
        )

    def dec_weight(n, kind):
        peer = over if kind == 0 else mate
        src = shards[n] if kind < 2 else place(n, over)
        dst = place(n, lane if kind < 2 else over)
        return far(src, dst, dw_s.at[3 * n + kind], dw_r.at[3 * n + kind], {"tensor": peer})

    enc_weight(0).start()
    for step in range(1, LANES):
        bias_copy(step).start()
    enc_weight(1).start()
    for n in (0, 1):
        dec_weight(n, 0).start()
    enc_weight(2).start()
    enc_weight(3).start()
    for n in range(4):
        dec_weight(n, 1).start()

    def pass_on(n):
        dec_weight(n, 0).wait_recv()
        dec_weight(n, 2).start()

    def arrived(n):
        keep[n].wait()
        dec_weight(n, 1).wait_recv()
        dec_weight(n, 2).wait_recv()

    egain = gains[...].astype(F32)
    eoff = offs[...].astype(F32)
    stride = pat.shape[0] // VIS
    for c in range(2):
        row = lax.broadcasted_iota(jnp.int32, (PAD, pat.shape[0]), 0)
        col = lax.broadcasted_iota(jnp.int32, (PAD, pat.shape[0]), 1)
        pick = (col == row * stride + clips[c]).astype(F32).astype(BF16)
        ex[c * PAD : (c + 1) * PAD, :] = nn(pick, pat[...])

    emarks = head_marks(half, ENC_SIZE, BF16)
    key = lax.broadcasted_iota(jnp.int32, (PAD, PAD), 1)
    floor = jnp.where(key < VIS, NEG * LOG2E, -1e30)
    eones = ones_per_head(PAD, emarks)
    blocks = D // 256

    def give_part(i, side):
        cut = span(i, 256)
        return far(
            esend.at[(1 - side) * PAD : (2 - side) * PAD, cut],
            erecv.at[side * PAD : (side + 1) * PAD, cut],
            ex_s.at[2 * i + side], ex_r.at[2 * i + side], {"tensor": over},
        )

    for c in range(2):
        rows = slice(c * PAD, (c + 1) * PAD)
        hat, _ = normal(ex[rows, :])
        ea[rows, :] = (hat * egain[0:1] + eoff[0:1]).astype(BF16)
        limit = (VIS * wid[clips[c]]) // WIDE
        for g, shard in enumerate((lane, mate)):
            if c == 0 and g == 0:
                own[0].wait()
            if c == 0 and g == 1:
                enc_weight(0).wait_recv()
                for step in range(1, LANES):
                    bias_copy(step).wait_recv()
            if g == 0:
                bq, bv = bias[1:2, 0:half], bias[2:3, 0:half]
            else:
                bq, bv = biases[shard, 1:2, 0:half], biases[shard, 2:3, 0:half]
            eqkv[g, 0, rows] = (nt(ea[rows, :], w_qkv[g, 0]) + bq).astype(BF16)
            eqkv[g, 1, rows] = nt(ea[rows, :], w_qkv[g, 1]).astype(BF16)
            eqkv[g, 2, rows] = (nt(ea[rows, :], w_qkv[g, 2]) + bv).astype(BF16)
            p, out, _ = attend(
                eqkv[g, 0, rows], eqkv[g, 1, rows], eqkv[g, 2, rows], emarks, eones,
                lambda s: jnp.where(key < limit, s, floor), ENC_SCALE,
            )
            ep[g, c] = p
            eo[g, rows] = out
        if c == 0:
            own[1].wait()
            enc_weight(1).wait_recv()
        for i in range(blocks):
            cut = slice(i * 256, (i + 1) * 256)
            t = nn(eo[0, rows], w_proj[0, :, cut]) + nn(eo[1, rows], w_proj[1, :, cut])
            epart[rows, cut] = t
            esend[rows, cut] = t.astype(BF16)
            give_part(i, 1 - c).start()
    pass_on(0)
    own[2].wait()
    enc_weight(2).wait_recv()

    def give_last(i):
        cut = span(i, 256)
        return far(
            esend2.at[:, cut], erecv2.at[:, cut], ex2_s.at[i], ex2_r.at[i], {"tensor": over}
        )

    for c in (1, 0):
        rows = slice(c * PAD, (c + 1) * PAD)
        for i in range(blocks):
            give_part(i, c).wait_recv()
        t = ex[rows, :] + epart[rows, :] + erecv[rows, :].astype(F32) + eoff[2:3]
        ex1[rows, :] = t
        hat, _ = normal(t)
        eu[rows, :] = (hat * egain[1:2] + eoff[1:2]).astype(BF16)
        if c == 0:
            dec_weight(2, 0).start()
        for g, shard in enumerate((lane, mate)):

            def enc_ff(i, g=g, shard=shard, rows=rows):
                cut = span(i, 256)
                h = nn(eu[rows, :], w_up[g, :, cut]) + biases[shard, 0:1, cut]
                act, slope = gelu_both(h)
                ey[g, rows, cut] = act.astype(BF16)
                egp[g, rows, cut] = slope.astype(BF16)

            loop(w_up.shape[2] // 256, enc_ff, unroll=3)
        if c == 1:
            own[3].wait()
            enc_weight(3).wait_recv()
        for i in range(blocks):
            cut = slice(i * 256, (i + 1) * 256)
            t = nn(ey[0, rows], w_down[0, :, cut]) + nn(ey[1, rows], w_down[1, :, cut])
            if c == 0:
                eown[:, cut] = t
            else:
                esend2[:, cut] = t.astype(BF16)
                give_last(i).start()
    outs = [
        pltpu.make_async_copy(src, dst, out_s.at[n])
        for n, (src, dst) in enumerate(
            (
                (ex.at[0:PAD, :], o_x), (ex1, o_x1), (ea, o_a), (eu, o_u), (ey, o_y), (egp, o_gp),
                (eqkv, o_qkv), (ep, o_p), (eo, o_o), (w_qkv.at[1], o_w), (w_proj.at[1], o_wproj),
                (w_up.at[1], o_wup), (w_down.at[1], o_wdown),
            )
        )
    ]
    for copy in outs:
        copy.start()
    pass_on(1)
    for i in range(blocks):
        give_last(i).wait_recv()
    dec_weight(3, 0).start()

    width = wid[clip]
    bits = jnp.where(width == WIDE, 3, 2)
    turn = shifts[0, clip] * width
    mod = GRID - 1
    spot = 0
    for i in range(order.shape[1]):
        spot = spot + jnp.where(order[0, i] == clip, i, 0)
    batch = spot // CM
    count = 0
    for i in range(order.shape[1]):
        count = count + jnp.where(batch == i // CM, wid[order[0, i]], 0)
    factor_rows = CM * GRID / (jnp.full((1, 1), count, jnp.int32) * GRID_ROWS).astype(F32)

    def slot_of(index):
        return (index - turn) & mod

    def code_of(slot):
        band = ((slot >> bits) + shifts[0, clip]) >> 2
        strip = ((slot & (width - 1)) + shifts[1, clip]) >> 2
        return band * 4 + strip

    e_ref[...] = (ex1[0:PAD, :] + eown[...] + erecv2[...].astype(F32) + eoff[3:4]).astype(BF16)
    vec = evec[...].astype(F32)
    m = (nn(e_ref[...], ew[...]) + vec[0:1]).astype(BF16)
    seen = vis[pl.ds(clip, 1), :]
    target = jnp.concatenate([(seen + turn) & mod, jnp.full((1, PAD - VIS), -1, jnp.int32)], 1)
    gain = dgains[...].astype(F32)
    offsets = doffs[...].astype(F32)

    def start(i):
        r = span(i, PAD)
        index = lax.broadcasted_iota(jnp.int32, (PAD, PAD), 0) + i * PAD
        column = lax.broadcasted_iota(jnp.int32, (PAD, PAD), 1)
        match = index == target
        oh = match.astype(F32).astype(BF16)
        hot[r, :] = oh
        hit = jnp.sum(match.astype(F32), -1, keepdims=True)
        grid = jnp.where(hit > 0, nn(oh, m), vec[1:2]).astype(BF16).astype(F32)
        slot = slot_of(index)
        by_row = ((slot >> bits) == column).astype(F32).astype(BF16)
        by_col = ((slot & (width - 1)) == column).astype(F32).astype(BF16)
        row_part = nn(by_row, table[0]) + nn(by_row, table[1])
        col_part = nn(by_col, table[0]) + nn(by_col, table[1])
        x = grid + jnp.concatenate([row_part, col_part], 1)
        x0[r, :] = x
        hat, _ = normal(x)
        a[r, :] = (hat * gain[0:1] + offsets[0:1]).astype(BF16)

    loop(GRID // PAD, start)
    arrived(0)

    def dec_bias(row, size):
        return jnp.concatenate([biases[k, row : row + 1, 0:size] for k in range(LANES)], 1)

    def project(i):
        r = span(i, 256)
        rows = a[r, :]
        acts[0, r, :] = (nn(rows, qkv[0]) + dec_bias(4, 128)).astype(BF16)
        acts[1, r, :] = nn(rows, qkv[1]).astype(BF16)
        acts[2, r, :] = (nn(rows, qkv[2]) + dec_bias(5, 128)).astype(BF16)

    loop(2, project)
    pass_on(2)
    marks = head_marks(128, DEC_SIZE, BF16)
    marks32 = head_marks(128, DEC_SIZE, F32)
    dim = lax.broadcasted_iota(jnp.int32, (128, 1), 0)
    rows32 = [
        ((dim >= h * DEC_SIZE) & (dim < (h + 1) * DEC_SIZE)).astype(F32) for h in range(len(marks))
    ]

    ones = ones_per_head(PAD, marks)

    def attention(i):
        r = span(i, PAD)
        row_slot = slot_of(lax.broadcasted_iota(jnp.int32, (PAD, PAD), 0) + i * PAD)
        key_slot = slot_of(lax.broadcasted_iota(jnp.int32, (PAD, PAD), 1) + i * PAD)
        allowed = (code_of(row_slot) == code_of(key_slot)) & (key_slot < GRID_ROWS * width)
        for g in range(DD // 128):
            c = slice(g * 128, (g + 1) * 128)
            probs[i, :, g * 512 : (g + 1) * 512], o[r, c], inverse[r, c] = attend(
                acts[0, r, c], acts[1, r, c], acts[2, r, c], marks, ones,
                lambda s: jnp.where(allowed, s, NEG * LOG2E), DEC_SCALE,
            )

    loop(GRID // PAD, attention, unroll=2)
    arrived(1)
    pass_on(3)

    def mix(i):
        r = span(i, PAD)
        x = x0[r, :] + nn(o[r, :], proj[...]) + offsets[2:3]
        x1[r, :] = x
        hat, _ = normal(x)
        un = hat * gain[1:2] + offsets[1:2]
        u[r, :] = un.astype(BF16)
        ut[:, r] = jnp.transpose(un).astype(BF16)

    loop(GRID // PAD, mix)
    arrived(2)

    def ff(i):
        k = lax.div(i, 4)
        side = lax.rem(lax.div(i, 2), 2)
        c = span(lax.div(i, 2), 256)
        r = span(lax.rem(i, 2), 256)
        h = nn(u[r, :], up[:, c]) + biases[k, 3:4, span(side, 256)]
        act, slope = gelu_both(h)
        y[r, c] = act.astype(BF16)
        gp[r, c] = slope.astype(BF16)

    loop(2 * up.shape[1] // 256, ff, unroll=2)
    arrived(3)
    fetch.wait()
    slot_col = slot_of(lax.broadcasted_iota(jnp.int32, (GRID, 1), 0))
    valid = (slot_col < GRID_ROWS * width).astype(F32)
    rolled = slot_of(lax.broadcasted_iota(jnp.int32, (GRID, GRID), 0))
    perm = (rolled == lax.broadcasted_iota(jnp.int32, (GRID, GRID), 1)).astype(F32).astype(BF16)

    def out(i):
        r = span(lax.rem(i, 2), 256)
        c = span(lax.div(i, 2), 256)
        acc[r, c] = nn(y[r, :], down[:, c])

    loop(4, out)
    full = ((acc[...] + x1[...] + offsets[3:4]) * valid).astype(BF16)
    turned = tn(full, perm).astype(BF16)
    for k in range(devices):
        dsend[k] = turned[k * dsend.shape[1] : (k + 1) * dsend.shape[1]]

    def decoded_copy(step):
        peer, spot = group_peer(step)
        return far(dsend.at[peer], dec_out.at[me], do_s.at[step], do_r.at[step], spot)

    for step in range(1, devices):
        decoded_copy(step).start()
    dec_out[me] = dsend[me]
    g = nn(perm, cot[...]) * valid * factor_rows
    g32[...] = g
    gb[...] = g.astype(BF16)
    gt[...] = jnp.transpose(g).astype(BF16)
    d_small[0:5, :] = jnp.zeros((5, DD), F32)
    d_small[5:6, :] = colsum(g)
    d_small[6:8, :] = jnp.zeros((2, DD), F32)

    def ff_back(i):
        c = span(i, 256)
        shard = lax.div(i, 2)
        side = lax.rem(i, 2)
        buf[shard, side, 0:512, 512:768] = nn(gt[...], y[:, c]).astype(BF16)
        dh = nt(gb[...], down[c, :]) * gp[:, c].astype(F32)
        d_upb[:, c] = colsum(dh)
        du = dh.astype(BF16)
        gp[:, c] = du
        buf[shard, 0, 0:512, span(side, 256)] = nn(ut[...], du).astype(BF16)

    loop(up.shape[1] // 256, ff_back, unroll=2)
    early = pltpu.make_async_copy(buf.at[:, 0, 0:512, :], o_dec.at[:, 0, 0:512, :], out_s.at[13])
    early.start()

    def ff_in(i):
        r = span(lax.rem(i, 2), 256)
        c = span(lax.div(i, 2), 256)
        acc[r, c] = nt(gp[r, :], up[c, :])

    loop(4, ff_in)

    def mix_back(i):
        r = span(i, PAD)
        hat, scale = normal(x1[r, :])
        da = acc[r, :]
        dx = g32[r, :] + normal_back(da, hat, scale, gain[1:2])
        d_small[1:2, :] += colsum(da * hat)
        d_small[3:4, :] += colsum(da)
        d_small[4:5, :] += colsum(dx)
        g32[r, :] = dx
        dxb = dx.astype(BF16)
        gb[r, :] = dxb
        u[r, :] = nt(dxb, proj[...]).astype(BF16)

    loop(GRID // PAD, mix_back)
    d_proj = tn(o[...], gb[...]).astype(BF16)
    for k in range(LANES):
        for j in range(LANES):
            block = d_proj[k * 128 : (k + 1) * 128, j * 128 : (j + 1) * 128]
            buf[k, 1, j * 128 : (j + 1) * 128, 384:512] = block

    def attention_back(i):
        r = span(i, PAD)
        for k in range(DD // 128):
            c = slice(k * 128, (k + 1) * 128)
            acts[0, r, c], acts[1, r, c], acts[2, r, c] = attend_back(
                acts[0, r, c], acts[1, r, c], acts[2, r, c],
                probs[i, :, k * 512 : (k + 1) * 512], o[r, c], inverse[r, c], u[r, c],
                marks, marks32, rows32, ones, DEC_SCALE,
            )

    loop(GRID // PAD, attention_back, unroll=2)
    d_qvb[0:1, :] = colsum(acts[0].astype(F32))
    d_qvb[1:2, :] = colsum(acts[2].astype(F32))

    def project_back(i):
        r = span(lax.rem(i, 2), 256)
        c = span(lax.div(i, 2), 256)
        acc[r, c] = (
            nt(acts[0, r, :], qkv[0, c, :])
            + nt(acts[1, r, :], qkv[1, c, :])
            + nt(acts[2, r, :], qkv[2, c, :])
        )

    loop(4, project_back)
    gt[...] = jnp.transpose(a[...].astype(F32)).astype(BF16)
    for j in range(3):
        d_qkv = nn(gt[...], acts[j]).astype(BF16)
        for k in range(LANES):
            buf[k, 1, 0:512, j * 128 : (j + 1) * 128] = d_qkv[:, k * 128 : (k + 1) * 128]

    def start_back(i):
        r = span(i, PAD)
        hat, scale = normal(x0[r, :])
        da = acc[r, :]
        dx = g32[r, :] + normal_back(da, hat, scale, gain[0:1])
        d_small[0:1, :] += colsum(da * hat)
        d_small[2:3, :] += colsum(da)
        dg = dx.astype(BF16)
        gb[r, :] = dg
        hit = jnp.sum(hot[r, :].astype(F32), -1, keepdims=True)
        d_small[7:8, :] += colsum(jnp.where(hit > 0, 0.0, dg.astype(F32)))

    loop(GRID // PAD, start_back)
    dm = tn(hot[...], gb[...])
    d_small[6:7, :] = colsum(dm)
    dmb = dm.astype(BF16)
    d_enc[...] = nt(dmb, ew[...]).astype(BF16)
    d_ew = tn(e_ref[...], dmb).astype(BF16)
    for k in range(LANES):
        for h in range(2):
            top = k * 192 + h * 64
            buf[k, h, 512:576, 0:512] = d_ew[top : top + 64]
            buf[k, h, 512:576, 512:768] = d_ew[k * 192 + 128 : (k + 1) * 192, h * 256 : (h + 1) * 256]

    rest = [
        pltpu.make_async_copy(buf.at[:, 1], o_dec.at[:, 1], out_s.at[14]),
        pltpu.make_async_copy(buf.at[:, 0, 512:576, :], o_dec.at[:, 0, 512:576, :], out_s.at[15]),
    ]
    for copy in rest:
        copy.start()
    for copy in outs + [early] + rest:
        copy.wait()
    for n in range(4):
        enc_weight(n).wait_send()
        for kind in range(3):
            dec_weight(n, kind).wait_send()
    for step in range(1, LANES):
        bias_copy(step).wait_send()
    for i in range(blocks):
        give_part(i, 0).wait_send()
        give_part(i, 1).wait_send()
        give_last(i).wait_send()
    for step in range(1, devices):
        decoded_copy(step).wait()


def forward_call(args, half, hid, dff):
    dma = lambda *s: pltpu.SemaphoreType.DMA(s)
    vm = lambda dtype, *shape: pltpu.VMEM(shape, dtype)
    rows = 2 * PAD
    keys = PAD * half // ENC_SIZE
    devices = 2 * LANES
    slab = DD // devices
    kept = [
        ((PAD, D), F32), ((rows, D), F32), ((rows, D), BF16), ((rows, D), BF16),
        ((2, rows, hid), BF16), ((2, rows, hid), BF16), ((2, 3, rows, half), BF16),
        ((2, 2, PAD, keys), BF16), ((2, rows, half), BF16),
        ((3, half, D), BF16), ((half, D), BF16), ((D, hid), BF16), ((hid, D), BF16),
        ((LANES, 2, DEC_ROWS, D), BF16),
    ]
    made = [
        ((PAD, D), BF16), ((2, DD), F32), ((1, dff), F32), ((8, DD), F32),
        ((devices, slab, GRID), BF16),
    ]
    return pl.pallas_call(
        forward_and_decoder,
        out_shape=[jax.ShapeDtypeStruct(s, d) for s, d in kept + made],
        in_specs=[SM, SM, SM] + [VM] * 8 + [ANY] * 9 + [VM] * 5,
        out_specs=[ANY] * len(kept) + [VM] * len(made),
        scratch_shapes=[
            vm(BF16, 2, 3, half, D), vm(BF16, 2, half, D), vm(BF16, 2, D, hid), vm(BF16, 2, hid, D),
            vm(F32, 8, D), vm(F32, LANES, 8, D),
            vm(BF16, 3, DD, DD), vm(BF16, DD, DD), vm(BF16, DD, dff), vm(BF16, dff, DD),
            vm(F32, rows, D), vm(BF16, rows, D), vm(BF16, rows, D), vm(BF16, 2, rows, hid),
            vm(BF16, 2, rows, hid), vm(BF16, 2, 3, rows, half), vm(BF16, 2, 2, PAD, keys),
            vm(BF16, 2, rows, half), vm(F32, rows, D), vm(F32, rows, D), vm(BF16, rows, D),
            vm(BF16, rows, D), vm(BF16, PAD, D), vm(BF16, PAD, D), vm(F32, PAD, D),
            vm(BF16, GRID, DD), vm(F32, GRID, DD), vm(F32, GRID, DD), vm(BF16, GRID, DD),
            vm(BF16, 3, GRID, DD), vm(BF16, GRID // PAD, PAD, DHEADS * PAD), vm(BF16, GRID, DD),
            vm(F32, GRID, DD),
            vm(BF16, GRID, DD), vm(BF16, DD, GRID), vm(BF16, GRID, dff), vm(BF16, GRID, dff),
            vm(F32, GRID, DD), vm(BF16, GRID, DD), vm(BF16, DD, GRID), vm(F32, GRID, DD),
            vm(BF16, PAD, D), vm(BF16, GRID, PAD), vm(BF16, LANES, 2, DEC_ROWS, D),
            vm(BF16, devices, slab, GRID),
            dma(8), dma(16), pltpu.SemaphoreType.DMA, dma(4), dma(4), dma(LANES), dma(LANES),
            dma(12), dma(12), dma(6), dma(6), dma(3), dma(3), dma(devices), dma(devices),
        ],
        compiler_params=pltpu.CompilerParams(
            collective_id=0, has_side_effects=True, vmem_limit_bytes=VMEM_LIMIT
        ),
    )(*args)


CH = 64
DEC_ROWS = 576
ENC_A = 768
ENC_B = 384
DEC_K = DEC_ROWS // CH
B_K = (DEC_ROWS + ENC_A + ENC_B) // CH
ALL_K = B_K + 1
A_TOP = DEC_ROWS
B_TOP = DEC_ROWS + ENC_A
S_TOP = B_TOP + ENC_B
LAG = 2
LEAD = 4
LATE = LEAD + 2 * (DEC_K - LEAD)
HALVED = ALL_K - 4


def add(x, y):
    return x + y


def backward_and_sums(
    d_enc, gains,
    h_u, h_y, h_gp, h_down0, h_down1, h_up0, h_up1,
    h_x, h_x1, h_a, h_qkv, h_p, h_o, h_w0, h_w1, h_proj0, h_proj1,
    dec, dec_qvb, dec_upb, dec_small,
    out, emb, dx_out,
    gb, gt, ut, part, send, recv, du, gx, dx1, d_o, d_acts, own, send1, recv1, dx32, dx,
    d_upb, d_qvb, d_small,
    acc, yacc, enc_mate, rcy, ry, rx, zl, zr, xc, cl, cr, small32, small,
    u, y, gp, down0, down1, up0, up1, x, x1, a, qkv, p, o, w0, w1, proj0, proj1, fetch_s,
    load_s, ex_s, ex_r,
    core_s, core_r, corey_s, corey_r, y_s, y_r, x_s, x_r, z_s, zl_r, zr_r,
    bl_s, br_s, b_r, a_s, a_r, emb_s, emb_r, dx_s, dx_r,
):
    sec = lax.axis_index("section")
    lane = lax.axis_index("tensor")
    pos = lax.axis_index("dp")
    count = lax.axis_size("dp")
    mate = lane + 1 - 2 * lax.rem(lane, 2)
    over = lax.rem(lane + 2, LANES)
    cross = lax.rem(mate + 2, LANES)
    first = pos == 0
    last = pos == count - 1
    me = sec * LANES + lane
    devices = 2 * LANES

    def group_peer(step):
        peer = lax.rem(me + step, devices)
        return peer, {"section": lax.div(peer, LANES), "tensor": lax.rem(peer, LANES)}

    barrier = pltpu.get_barrier_semaphore()
    for step in range(1, devices):
        pl.semaphore_signal(barrier, inc=1, device_id_type=MESH, device_id=group_peer(step)[1])

    @pl.when(pos > 0)
    def _():
        pl.semaphore_signal(barrier, inc=1, device_id={"dp": pos - 1}, device_id_type=MESH)

    @pl.when(pos < count - 1)
    def _():
        pl.semaphore_signal(barrier, inc=1, device_id={"dp": pos + 1}, device_id_type=MESH)

    fetches = [
        pltpu.make_async_copy(src, dst, fetch_s.at[n])
        for n, (src, dst) in enumerate(
            (
                (h_u, u), (h_y, y), (h_gp, gp), (h_down0, down0), (h_down1, down1), (h_up0, up0),
                (h_up1, up1), (h_x, x), (h_x1, x1), (h_a, a), (h_qkv, qkv), (h_p, p), (h_o, o),
                (h_w0, w0), (h_w1, w1), (h_proj0, proj0), (h_proj1, proj1),
            )
        )
    ]
    for fetch in fetches:
        fetch.start()
    loads = [
        pltpu.make_async_copy(dec.at[lane], acc.at[:, 0:DEC_ROWS, :], load_s.at[0]),
        pltpu.make_async_copy(dec.at[over], yacc.at[:, 0:DEC_ROWS, :], load_s.at[1]),
    ]
    for load in loads:
        load.start()
    small32[...] = jnp.zeros_like(small32)
    small[...] = jnp.zeros_like(small)
    d_small[...] = jnp.zeros_like(d_small)
    gb[0:PAD, :] = d_enc[...]
    ends = jnp.where(first, 0, 1) + jnp.where(last, 0, 1)
    pl.semaphore_wait(barrier, devices - 1 + ends)

    gain = gains[...].astype(F32)
    width = w0.shape[1]
    marks = head_marks(width, ENC_SIZE, BF16)
    marks32 = head_marks(width, ENC_SIZE, F32)
    ones = ones_per_head(PAD, marks)

    def rows(k, size=CH):
        return pl.ds(pl.multiple_of(k * size, size), size)

    def give_enc():
        return far(d_enc, gb.at[PAD : 2 * PAD, :], ex_s.at[0], ex_r.at[0], {"tensor": over})

    def give_part(i, half):
        cut = rows(i, 256)
        n = 1 + 2 * i + half
        return far(
            send.at[(1 - half) * PAD : (2 - half) * PAD, cut],
            recv.at[half * PAD : (half + 1) * PAD, cut],
            ex_s.at[n], ex_r.at[n], {"tensor": over},
        )

    def give_last(i):
        cut = rows(i, 256)
        return far(send1.at[:, cut], recv1.at[:, cut], ex_s.at[7 + i], ex_r.at[7 + i], {"tensor": over})

    def ff_back(g, i, down):
        c = rows(i, 256)
        d_down = nn(gt[...], y[g, :, c]).astype(BF16)
        dh = nt(gb[...], down[c, :]) * gp[g, :, c].astype(F32)
        d_upb[g, :, c] = colsum(dh)
        dub = dh.astype(BF16)
        du[g, :, c] = dub
        d_up = nn(ut[...], dub).astype(BF16)
        if g == 0:
            acc[1, A_TOP:B_TOP, c] = d_down
            acc[0, A_TOP:B_TOP, c] = d_up
        else:
            enc_mate[1, 0:ENC_A, c] = d_down
            enc_mate[0, 0:ENC_A, c] = d_up

    def ff_in(i):
        c = rows(i, 256)
        t = nt(du[0], up0[c, :]) + nt(du[1], up1[c, :])
        part[:, c] = t
        send[:, c] = t.astype(BF16)
        give_part(i, 0).start()
        give_part(i, 1).start()

    def norm_two(i):
        del i
        for fetch in fetches[7:]:
            fetch.wait()
        for k in range(D // 256):
            give_part(k, 0).wait_recv()
            give_part(k, 1).wait_recv()

        def body(j):
            r = rows(j, 64)
            da = part[r, :] + recv[r, :].astype(F32)
            hat, scale = normal(x1[r, :])
            g = gb[r, :].astype(F32)
            d = g + normal_back(da, hat, scale, gain[1:2])
            gx[r, :] = d.astype(BF16)
            dx1[r, :] = d

            @pl.when(j < 2)
            def _():
                d_small[1:2, :] += colsum(da * hat)
                d_small[3:4, :] += colsum(da)
                d_small[4:5, :] += colsum(d)
                d_small[5:6, :] += colsum(g)

        loop(2 * PAD // 64, body)

    def attention(g, proj):
        d_proj = tn(o[g], gx[...]).astype(BF16)
        if g == 0:
            acc[1, B_TOP + width : S_TOP, :] = d_proj
        else:
            enc_mate[1, ENC_A + width : ENC_A + 2 * width, :] = d_proj
        d_o[...] = nt(gx[...], proj[...]).astype(BF16)
        for c in range(2):
            r = slice(c * PAD, (c + 1) * PAD)
            dq, dk, dv = attend_back(
                qkv[g, 0, r], qkv[g, 1, r], qkv[g, 2, r], p[g, c], o[g, r], 1.0 / nn(p[g, c], ones),
                d_o[r, :], marks, marks32, None, ones, ENC_SCALE,
            )
            d_acts[g, 0, r] = dq
            d_acts[g, 1, r] = dk
            d_acts[g, 2, r] = dv
        d_qvb[g, 0:1, :] = colsum(d_acts[g, 0].astype(F32))
        d_qvb[g, 1:2, :] = colsum(d_acts[g, 2].astype(F32))

    def project_in(i):
        c = rows(i, 256)
        t = 0.0
        for g, w in enumerate((w0, w1)):
            for j in range(3):
                t += nn(d_acts[g, j], w[j, :, c])
        own[:, c] = t[:PAD]
        send1[:, c] = t[PAD:].astype(BF16)
        give_last(i).start()

    def project_grad(g):
        for j in range(3):
            row = (j % 2) * width
            d = tn(d_acts[g, j], a[...]).astype(BF16)
            if g == 0:
                acc[j // 2, B_TOP + row : B_TOP + row + width, :] = d
            else:
                enc_mate[j // 2, ENC_A + row : ENC_A + row + width, :] = d

    def norm_one(i):
        del i
        for k in range(D // 256):
            give_last(k).wait_recv()

        def body(j):
            r = rows(j, 64)
            da = own[r, :] + recv1[r, :].astype(F32)
            hat, scale = normal(x[r, :])
            d_small[0:1, :] += colsum(da * hat)
            d_small[2:3, :] += colsum(da)
            dx32[r, :] = dx1[r, :] + normal_back(da, hat, scale, gain[0:1])

        loop(PAD // 64, body)
        turned = jnp.transpose(dx32[...])
        cut = D // devices
        for k in range(devices):
            dx[k] = turned[k * cut : (k + 1) * cut, 0:VIS].astype(BF16)
        for r in range(LANES):
            small32[r, 0:1, 0:512] = dec_upb[:, r * 512 : (r + 1) * 512]
            small32[r, 1:2, 0:128] = dec_qvb[0:1, r * 128 : (r + 1) * 128]
            small32[r, 1:2, 128:256] = dec_qvb[1:2, r * 128 : (r + 1) * 128]
            small32[r, 8:16, 0:512] = dec_small[...]
            small32[r, 16:24, :] = d_small[...]
        for g, shard in enumerate((lane, mate)):
            small32[shard, 2:3, :] = d_upb[g]
            small32[shard, 3:4, 0:192] = d_qvb[g, 0:1]
            small32[shard, 3:4, 256:448] = d_qvb[g, 1:2]
        for r in range(LANES):
            small[r, 0, 0:32] = small32[r].astype(BF16)
        acc[:, S_TOP : S_TOP + CH, :] = small[lane]
        yacc[:, DEC_ROWS : DEC_ROWS + CH, :] = small[over]
        core_copy(LATE, small.at[mate]).start()
        corey_copy(LATE, small.at[cross]).start()
        for step in range(1, devices):
            dx_copy(step).start()
        dx_out[me] = dx[me]

    def core_enc(lo, hi):
        def body(m):
            block = block_of(m)

            @pl.when((block >= lo) & (block < hi))
            def _():
                src = pl.ds(pl.multiple_of(block * CH - DEC_ROWS, CH), CH)
                core_copy(m, enc_mate.at[:, src, :]).start()

        loop(ALL_K, body)

    def first_piece(i):
        del i
        for fetch in fetches[:7]:
            fetch.wait()
        ut[...] = jnp.transpose(u[...].astype(F32)).astype(BF16)
        give_enc().wait_recv()
        gt[...] = jnp.transpose(gb[...].astype(F32)).astype(BF16)

    pieces = [(0, 1, first_piece)]
    for g, down in enumerate((down0, down1)):
        pieces.append((0, 3, lambda i, g=g, down=down: ff_back(g, i, down)))
    pieces.append((3, 4, lambda i: core_enc(DEC_K, DEC_K + ENC_A // CH)))
    pieces.append((3, 4, lambda i: loop(D // 256, ff_in)))
    pieces.append((6, 7, norm_two))
    for g, proj in enumerate((proj0, proj1)):
        pieces.append((7 + g, 8 + g, lambda i, g=g, proj=proj: attention(g, proj)))
    pieces.append((9, 10, lambda i: loop(D // 256, project_in)))
    for g in range(2):
        pieces.append((10 + g, 11 + g, lambda i, g=g: project_grad(g)))
    pieces.append((12, 13, lambda i: core_enc(DEC_K + ENC_A // CH, B_K)))
    pieces.append((13, 14, norm_one))

    def dx_copy(step):
        peer, place = group_peer(step)
        return far(dx.at[peer], dx_out.at[me], dx_s.at[step], dx_r.at[step], place)

    def emb_copy(step):
        return far(
            out.at[:, pl.ds(512, CH), :], emb.at[lane], emb_s.at[step], emb_r.at[step],
            {"tensor": lax.rem(lane + step, LANES)},
        )

    def block_of(m):
        turn = jnp.where(lax.rem(m, 2) == 0, DEC_K + lax.div(m - LEAD, 2), LEAD + lax.div(m - LEAD - 1, 2))
        late = jnp.where(m == LATE, ALL_K - 1, m - 1)
        return jnp.where(m < LEAD, m, jnp.where(m >= LATE, late, turn))

    def is_dec(m):
        return block_of(m) < DEC_K

    def with_y(m):
        return is_dec(m) | (m == LATE)

    def at(m):
        return pl.ds(pl.multiple_of(block_of(m) * CH, CH), CH)

    def pair_at(m):
        return rows(jnp.where(m < HALVED, lax.div(m, 2), m - HALVED // 2))

    def y_at(m):
        return rows(jnp.minimum(block_of(m), DEC_K))

    def core_copy(m, src):
        return far(src, out.at[:, at(m), :], core_s.at[m], core_r.at[m], {"tensor": mate})

    def corey_copy(m, src):
        return far(src, rcy.at[:, y_at(m), :], corey_s.at[m], corey_r.at[m], {"tensor": mate})

    def y_copy(m):
        cut = y_at(m)
        return far(
            yacc.at[:, cut, :], ry.at[:, cut, :], y_s.at[m], y_r.at[m], {"tensor": over}
        )

    def x_copy(m):
        return far(
            acc.at[1 - sec, at(m), :], rx.at[pair_at(m), :], x_s.at[m], x_r.at[m],
            {"section": 1 - sec},
        )

    def xc_copy(m):
        return far(
            acc.at[:, at(m), :], xc.at[:, pair_at(m), :], x_s.at[m], x_r.at[m],
            {"section": 1 - sec},
        )

    def z_copy(m, whole, right):
        if whole:
            src, dst = acc.at[:, at(m), :], (cl if right else cr).at[:, pair_at(m), :]
        else:
            src, dst = acc.at[sec, at(m), :], (zl if right else zr).at[pair_at(m), :]
        landed = zl_r if right else zr_r
        return far(src, dst, z_s.at[m], landed.at[m], {"dp": pos + 1 if right else pos - 1})

    def b_copy(m, whole, right):
        place = out.at[:, at(m), :] if whole else out.at[sec, at(m), :]
        sent = br_s if right else bl_s
        return far(place, place, sent.at[m], b_r.at[m], {"dp": pos + 1 if right else pos - 1})

    def a_copy(m):
        place = out.at[sec, at(m), :]
        return far(place, place, a_s.at[m], a_r.at[m], {"section": 1 - sec})

    def a_wait(m):
        place = out.at[1 - sec, at(m), :]
        far(place, place, a_s.at[m], a_r.at[m], {"section": 1 - sec}).wait_recv()

    give_enc().start()

    def start_core(m):
        @pl.when(is_dec(m))
        def _():
            core_copy(m, dec.at[mate, :, at(m), :]).start()
            corey_copy(m, dec.at[cross, :, at(m), :]).start()

    loop(LATE, start_core)
    for load in loads:
        load.wait()

    def stage_c(m):
        core_copy(m, out.at[:, at(m), :]).wait_recv()
        acc[:, at(m), :] = add(acc[:, at(m), :], out[:, at(m), :])

        @pl.when(with_y(m))
        def _():
            corey_copy(m, rcy.at[:, y_at(m), :]).wait_recv()
            yacc[:, y_at(m), :] = add(yacc[:, y_at(m), :], rcy[:, y_at(m), :])
            y_copy(m).start()

    def finished(m):
        @pl.when(block_of(m) == DEC_K - 1)
        def _():
            for step in range(1, LANES):
                emb_copy(step).start()
            emb[lane] = out[:, 512 : 512 + CH, :]

    def line_of(root, whole):
        left = pos < root
        right = pos > root
        here = pos == root
        reach = max(root, count - 1 - root)
        level = jnp.where(left, pos, jnp.where(right, count - 1 - pos, reach))
        dist = jnp.where(left, root - pos, pos - root)

        def view(ref, m):
            return ref.at[:, at(m), :] if whole else ref.at[sec, at(m), :]

        def landed(ref, m):
            return ref.at[:, pair_at(m), :] if whole else ref.at[pair_at(m), :]

        from_left, from_right = (cl, cr) if whole else (zl, zr)

        def outer(m):
            @pl.when(left & first)
            def _():
                z_copy(m, whole, True).start()

            @pl.when(right & last)
            def _():
                z_copy(m, whole, False).start()

        def inward(m):
            @pl.when(left & (pos > 0))
            def _():
                z_copy(m, whole, True).wait_recv()
                view(acc, m)[...] = add(view(acc, m)[...], landed(from_left, m)[...])
                z_copy(m, whole, True).start()

            @pl.when(right & (pos < count - 1))
            def _():
                z_copy(m, whole, False).wait_recv()
                view(acc, m)[...] = add(view(acc, m)[...], landed(from_right, m)[...])
                z_copy(m, whole, False).start()

            @pl.when(here)
            def _():
                total = view(acc, m)[...].astype(F32)
                if root > 0:
                    z_copy(m, whole, True).wait_recv()
                    total = total + landed(from_left, m)[...].astype(F32)
                if root < count - 1:
                    z_copy(m, whole, False).wait_recv()
                    total = total + landed(from_right, m)[...].astype(F32)
                if whole:
                    view(acc, m)[...] = total.astype(BF16)
                    xc_copy(m).start()
                else:
                    view(out, m)[...] = total.astype(BF16)
                    spread(m)
                    a_copy(m).start()

        def spread(m):
            if root > 0:
                b_copy(m, whole, False).start()
            if root < count - 1:
                b_copy(m, whole, True).start()

        def crossed(m):
            xc_copy(m).wait_recv()
            view(out, m)[...] = add(view(acc, m)[...], landed(xc, m)[...])
            spread(m)
            finished(m)

        def outward(m):
            b_copy(m, whole, False).wait_recv()

            @pl.when(left & (pos > 0))
            def _():
                b_copy(m, whole, False).start()

            @pl.when(right & (pos < count - 1))
            def _():
                b_copy(m, whole, True).start()

            if whole:
                finished(m)
            else:
                a_copy(m).start()

        def sent(m):
            @pl.when(jnp.logical_not(here))
            def _():
                z_copy(m, whole, True).wait_send()

            @pl.when((pos <= root) & (pos > 0))
            def _():
                b_copy(m, whole, False).wait_send()

            @pl.when((pos >= root) & (pos < count - 1))
            def _():
                b_copy(m, whole, True).wait_send()

            if whole:
                @pl.when(here)
                def _():
                    xc_copy(m).wait_send()
            else:
                x_copy(m).wait_send()
                a_copy(m).wait_send()

        def add_y(m):
            @pl.when(with_y(m))
            def _():
                y_copy(m).wait_recv()
                acc[:, at(m), :] = add(acc[:, at(m), :], ry[:, y_at(m), :])

            if whole:
                outer(m)
            else:
                x_copy(m).start()

        def add_x(m):
            x_copy(m).wait_recv()
            acc[sec, at(m), :] = add(acc[sec, at(m), :], rx[pair_at(m), :])
            outer(m)

        def last_half(m):
            a_wait(m)
            finished(m)

        base = 1 if whole else 2
        back = base + reach + dist + (1 if whole else 0)
        steps = [(back, jnp.logical_not(here), outward), (base + level, level > 0, inward), (1, True, add_y)]
        if whole:
            steps.append((base + reach + 1, here, crossed))
        else:
            steps += [(back + 1, True, last_half), (2, True, add_x)]
        return steps, sent

    low_root = (count - 1) // 2
    high_root = min(low_root + 1, count - 1)
    lines = [
        (lambda m: (lax.rem(m, 2) == 1) | (m >= HALVED), *line_of(low_root, False)),
        (lambda m: (lax.rem(m, 4) == 0) & (m < HALVED), *line_of(low_root, True)),
        (lambda m: (lax.rem(m, 4) == 2) & (m < HALVED), *line_of(high_root, True)),
    ]

    def tick(n):
        @pl.when(n < LATE)
        def _():
            for low, high, piece in pieces:
                @pl.when((n >= low) & (n < high))
                def _(low=low, piece=piece):
                    piece(n - low)

        for mine, steps, _ in lines:
            for offset, enabled, stage in steps:
                m = n - LAG * offset

                @pl.when((m >= 0) & (m < ALL_K) & mine(m) & enabled)
                def _(m=m, stage=stage):
                    stage(m)

        @pl.when(n < ALL_K)
        def _():
            stage_c(n)

    far_reach = max(low_root, count - 1 - low_root, high_root, count - 1 - high_root)
    loop(ALL_K + LAG * (3 + 2 * far_reach) + 1, tick)

    def finish(m):
        core_copy(m, out.at[:, at(m), :]).wait_send()

        @pl.when(with_y(m))
        def _():
            corey_copy(m, rcy.at[:, y_at(m), :]).wait_send()
            y_copy(m).wait_send()

        for mine, _, sent in lines:
            @pl.when(mine(m))
            def _(sent=sent):
                sent(m)

    loop(ALL_K, finish)
    for step in range(1, devices):
        dx_copy(step).wait()
    for step in range(1, LANES):
        emb_copy(step).wait()
    give_enc().wait_send()
    for k in range(D // 256):
        give_part(k, 0).wait_send()
        give_part(k, 1).wait_send()
        give_last(k).wait_send()


def backward_call(args, half, hid):
    dma = lambda *s: pltpu.SemaphoreType.DMA(s)
    vm = pltpu.VMEM
    full = ALL_K * CH
    y_half = DEC_ROWS + CH
    whole = HALVED // 2 * CH
    by_half = full - whole
    k = ALL_K
    rows = 2 * PAD
    cut = D // (2 * LANES)
    specs = [VM, VM] + [ANY] * 18 + [VM] * 3
    return pl.pallas_call(
        backward_and_sums,
        out_shape=[
            jax.ShapeDtypeStruct((2, full, D), BF16),
            jax.ShapeDtypeStruct((LANES, 2, CH, D), BF16),
            jax.ShapeDtypeStruct((2 * LANES, cut, VIS), BF16),
        ],
        in_specs=specs,
        out_specs=[VM] * 3,
        scratch_shapes=[
            vm((rows, D), BF16), vm((D, rows), BF16), vm((D, rows), BF16),
            vm((rows, D), F32), vm((rows, D), BF16), vm((rows, D), BF16),
            vm((2, rows, hid), BF16), vm((rows, D), BF16), vm((rows, D), F32),
            vm((rows, half), BF16), vm((2, 3, rows, half), BF16),
            vm((PAD, D), F32), vm((PAD, D), BF16), vm((PAD, D), BF16), vm((PAD, D), F32),
            vm((2 * LANES, cut, VIS), BF16),
            vm((2, 1, hid), F32), vm((2, 2, half), F32), vm((8, D), F32),
            vm((2, full, D), BF16), vm((2, y_half, D), BF16), vm((2, ENC_A + ENC_B, D), BF16),
            vm((2, y_half, D), BF16), vm((2, y_half, D), BF16),
            vm((by_half, D), BF16), vm((by_half, D), BF16), vm((by_half, D), BF16),
            vm((2, whole, D), BF16), vm((2, whole, D), BF16), vm((2, whole, D), BF16),
            vm((LANES, 32, D), F32), vm((LANES, 2, CH, D), BF16),
            *[vm(v.shape, v.dtype) for v in args[2:19]], dma(17), dma(2), dma(10), dma(10),
            dma(k), dma(k), dma(k), dma(k), dma(k), dma(k),
            dma(k), dma(k), dma(k), dma(k), dma(k),
            dma(k), dma(k), dma(k), dma(k), dma(k), dma(LANES), dma(LANES),
            dma(2 * LANES), dma(2 * LANES),
        ],
        compiler_params=pltpu.CompilerParams(
            collective_id=1, has_side_effects=True, vmem_limit_bytes=VMEM_LIMIT
        ),
    )(*args)


def finish_grads(
    total, emb, decoded, dx, decoded_out, dx_out,
    e_qkv, e_qvb, e_proj, e_up, e_upb, e_down, e_gain, e_off,
    d_qkv, d_qvb, d_proj, d_up, d_upb, d_down, d_gain, d_off, d_ew, d_ev,
):
    half = e_proj.shape[0]
    decoded_out[...] = decoded[...]
    dx_out[...] = dx[...]
    e_up[...] = total[0, A_TOP:B_TOP, :].astype(F32)
    e_down[...] = jnp.transpose(total[1, A_TOP:B_TOP, :].astype(F32))
    e_qkv[0] = total[0, B_TOP : B_TOP + half, :].astype(F32)
    e_qkv[1] = total[0, B_TOP + half : S_TOP, :].astype(F32)
    e_qkv[2] = total[1, B_TOP : B_TOP + half, :].astype(F32)
    e_proj[...] = total[1, B_TOP + half : S_TOP, :].astype(F32)
    d_up[...] = total[0, 0:512, 0:512].astype(F32)
    d_down[0:256, :] = jnp.transpose(total[0, 0:512, 512:768].astype(F32))
    d_down[256:512, :] = jnp.transpose(total[1, 0:512, 512:768].astype(F32))
    for j in range(3):
        d_qkv[j] = total[1, 0:512, j * 128 : (j + 1) * 128].astype(F32)
    for j in range(LANES):
        cut = slice(j * 128, (j + 1) * 128)
        d_proj[:, cut] = total[1, cut, 384:512].astype(F32)
    for k in range(LANES):
        for h in range(2):
            top = k * 192 + h * 64
            d_ew[top : top + 64, :] = emb[k, h, :, 0:512].astype(F32)
            d_ew[k * 192 + 128 : (k + 1) * 192, h * 256 : (h + 1) * 256] = emb[
                k, h, :, 512:768
            ].astype(F32)
    little = total[0, S_TOP : S_TOP + 32, :].astype(F32)
    d_upb[...] = little[0, 0:512]
    d_qvb[0:1, :] = little[1:2, 0:128]
    d_qvb[1:2, :] = little[1:2, 128:256]
    e_upb[...] = little[2]
    e_qvb[0:1, :] = little[3:4, 0:192]
    e_qvb[1:2, :] = little[3:4, 256:448]
    d_gain[...] = little[8:10, 0:512]
    d_off[...] = little[10:14, 0:512]
    d_ev[...] = little[14:16, 0:512]
    e_gain[...] = little[16:18]
    e_off[...] = little[18:22]


def call(kernel, specs, shapes, scratch, args):
    return pl.pallas_call(
        kernel,
        out_shape=[jax.ShapeDtypeStruct(s, d) for s, d in shapes],
        in_specs=specs,
        out_specs=[VM] * len(shapes),
        scratch_shapes=scratch,
        compiler_params=pltpu.CompilerParams(vmem_limit_bytes=VMEM_LIMIT),
    )(*args)


def position_rows():
    quarter = DD // 4
    freq = np.exp(np.arange(quarter, dtype=np.float32) * np.float32(-math.log(10000.0) / quarter))
    angle = np.arange(PAD, dtype=np.float32)[:, None] * freq[None, :].astype(np.float32)
    both = np.concatenate([np.sin(angle), np.cos(angle)], 1).astype(np.float32)
    high = both.astype(jnp.bfloat16)
    low = (both - high.astype(np.float32)).astype(jnp.bfloat16)
    return np.stack([high, low])


def per_device(
    patches, cotangent, widths, visible, window_shift, batch_order,
    encoder_qkv, encoder_qvbias, encoder_proj, encoder_up, encoder_upbias, encoder_down,
    encoder_gains, encoder_offsets,
    decoder_qkv, decoder_qvbias, decoder_proj, decoder_up, decoder_upbias, decoder_down,
    decoder_gains, decoder_offsets, embed_weight, embed_vectors,
):
    qkv0 = encoder_qkv.transpose(1, 2, 0)
    half = qkv0.shape[1]
    hid = encoder_up.shape[1]
    dff = decoder_up.shape[1] * LANES
    flat = patches.transpose(1, 0, 2).reshape(-1, D)
    (
        x, x1, a, u, y, gp, qkv, p, o, qkv1, proj1, up1, down1, dec_buf,
        d_enc, d_dqvb, d_dupb, d_dsmall, out_all,
    ) = forward_call(
        (
            widths, window_shift.T, batch_order, visible, flat, encoder_gains, encoder_offsets,
            encoder_qvbias, encoder_upbias, decoder_qvbias, decoder_upbias,
            qkv0, encoder_proj, encoder_up, encoder_down,
            decoder_qkv.transpose(1, 0, 2), decoder_proj, decoder_up, decoder_down,
            cotangent, embed_weight, embed_vectors, jnp.asarray(position_rows()),
            decoder_gains, decoder_offsets,
        ),
        half, hid, dff,
    )
    total, emb, dx_all = backward_call(
        (
            d_enc, encoder_gains, u, y, gp, encoder_down, down1, encoder_up, up1,
            x, x1, a, qkv, p, o, qkv0, qkv1, encoder_proj, proj1,
            dec_buf, d_dqvb, d_dupb, d_dsmall,
        ),
        half, hid,
    )
    f = lambda *shape: (shape, F32)
    out_all, dx_all, *grads = call(
        finish_grads, [VM] * 4,
        [
            (out_all.shape, BF16), (dx_all.shape, BF16), f(3, half, D), f(2, half), f(half, D), f(D, hid), f(hid), f(hid, D), f(2, D), f(4, D),
            f(3, DD, 128), f(2, 128), f(128, DD), f(DD, 512), f(512), f(512, DD), f(2, DD), f(4, DD),
            f(D, DD), f(2, DD),
        ],
        [], (total, emb, out_all, dx_all),
    )
    grads[0] = grads[0].transpose(2, 0, 1)
    grads[8] = grads[8].transpose(1, 0, 2)
    return (out_all.swapaxes(1, 2), dx_all.swapaxes(1, 2), *grads)


def solution(mesh):
    weights = (
        P(None, None, "tensor"), P(None, "tensor"), P("tensor", None), P(None, "tensor"),
        P("tensor"), P("tensor", None), P(), P(),
    )
    split = P("dp", None, ("section", "tensor"))
    return jax.shard_map(
        per_device,
        mesh=mesh,
        in_specs=(
            P("dp", None, None), P("dp", None, None), P("dp"), P("dp", None), P("dp", None),
            P("dp", None),
        ) + weights + weights + (P(), P()),
        out_specs=(split, split) + weights + weights + (P(), P()),
        check_vma=False,
    )
```

```python
import math

import jax
import jax.numpy as jnp
import numpy as np
from jax import lax
from jax.experimental import pallas as pl
from jax.experimental.pallas import tpu as pltpu
from jax.sharding import PartitionSpec as P

D = 768
HEADS = 12
DD = 512
DHEADS = 16
GRID_ROWS = 64
WIDE = 8
WIN = 4
VIS = 102
CM = 4
GRID = 512
LANES = 4
PAD = 128
EPS = 1e-06
NEG = -10000.0
F32 = jnp.float32
BF16 = jnp.bfloat16
VMEM_LIMIT = 60 * 1024 * 1024

VM = pl.BlockSpec(memory_space=pltpu.VMEM)
SM = pl.BlockSpec(memory_space=pltpu.SMEM)
ANY = pl.BlockSpec(memory_space=pl.ANY)


def nn(a, b):
    return lax.dot_general(a, b, (((1,), (0,)), ((), ())), preferred_element_type=F32)


def nt(a, b):
    return lax.dot_general(a, b, (((1,), (1,)), ((), ())), preferred_element_type=F32)


def tn(a, b):
    return lax.dot_general(a, b, (((0,), (0,)), ((), ())), preferred_element_type=F32)


def loop(count, body, unroll=1):
    def step(i, carry):
        body(i)
        return carry

    lax.fori_loop(0, count, step, 0, unroll=unroll)


def span(i, size):
    return pl.ds(pl.multiple_of(i * size, size), size)


def normal(x):
    center = x - jnp.mean(x, -1, keepdims=True)
    scale = lax.rsqrt(jnp.mean(center * center, -1, keepdims=True) + EPS)
    return center * scale, scale


def normal_back(dy, hat, scale, gain):
    d = dy * gain
    return scale * (
        d - jnp.mean(d, -1, keepdims=True) - hat * jnp.mean(d * hat, -1, keepdims=True)
    )


def gelu_both(h):
    phi = 0.5 * lax.erf(h * math.sqrt(0.5)) + 0.5
    bell = jnp.exp2(h * h * (-0.5 * math.log2(math.e)))
    return h * phi, phi + h * bell * (1.0 / math.sqrt(2.0 * math.pi))


def colsum(x):
    return jnp.sum(x, 0, keepdims=True)


def head_marks(width, size, dtype):
    lane = lax.broadcasted_iota(jnp.int32, (1, width), 1)
    return [((lane >= h * size) & (lane < (h + 1) * size)).astype(dtype) for h in range(width // size)]


def stacked(x, marks):
    return jnp.concatenate([x * m for m in marks], 0)


LOG2E = math.log2(math.e)


def attend(q, k, v, marks, ones, masked, scale):
    keys = k.shape[0]
    s = nt(q, stacked(k, marks))
    parts = []
    for h in range(len(marks)):
        x = masked(s[:, h * keys : (h + 1) * keys] * (scale * LOG2E))
        parts.append(jnp.exp2(x - jnp.max(x, -1, keepdims=True)).astype(BF16))
    e = jnp.concatenate(parts, 1)
    width = q.shape[1]
    if width % 128:
        top, total = nn(e, stacked(v, marks)), nn(e, ones)
    else:
        both = nn(e, jnp.concatenate([stacked(v, marks), ones], 1))
        top, total = both[:, :width], both[:, width:]
    inverse = 1.0 / total
    return e, (top * inverse).astype(BF16), inverse


def attend_back(q, k, v, e, o, inverse, d_out, marks, marks32, rows32, ones, scale):
    keys = k.shape[0]
    width = q.shape[1]
    d_one = d_out.astype(F32) * inverse
    d_two = (d_one * o.astype(F32)).astype(BF16)
    d_one = d_one.astype(BF16)
    if width % 128:
        d_s = nt(d_one, stacked(v, marks)) - nt(d_two, ones)
    else:
        d_s = nt(
            jnp.concatenate([d_one, d_two], 1), jnp.concatenate([stacked(v, marks), -ones], 1)
        )
    dr = (e.astype(F32) * d_s * scale).astype(BF16)
    d_q = nn(dr, stacked(k, marks)).astype(BF16)
    if width % 128:
        d_k_all, d_v_all = tn(dr, q), tn(e, d_one)
        d_k = d_v = 0.0
        for h in range(len(marks)):
            cut = slice(h * keys, (h + 1) * keys)
            d_k += d_k_all[cut] * marks32[h]
            d_v += d_v_all[cut] * marks32[h]
        return d_q, d_k.astype(BF16), d_v.astype(BF16)
    d_k_all = nn(jnp.transpose(q.astype(F32)).astype(BF16), dr)
    d_v_all = nn(jnp.transpose(d_one.astype(F32)).astype(BF16), e)
    d_k = d_v = 0.0
    for h in range(len(marks)):
        cut = slice(h * keys, (h + 1) * keys)
        d_k += d_k_all[:, cut] * rows32[h]
        d_v += d_v_all[:, cut] * rows32[h]
    return d_q, jnp.transpose(d_k).astype(BF16), jnp.transpose(d_v).astype(BF16)


def ones_per_head(keys, marks):
    return jnp.concatenate([jnp.broadcast_to(m, (keys, m.shape[1])) for m in marks], 0)


ENC_SIZE = D // HEADS
ENC_SCALE = ENC_SIZE ** -0.5
DEC_SIZE = DD // DHEADS
DEC_SCALE = DEC_SIZE ** -0.5


MESH = pl.DeviceIdType.MESH


def far(src, dst, send, recv, peer):
    return pltpu.make_async_remote_copy(
        src_ref=src, dst_ref=dst, send_sem=send, recv_sem=recv, device_id=peer, device_id_type=MESH
    )


def forward_and_decoder(
    wid, shifts, order, vis, pat, gains, offs, b_qv, b_up, b_dqv, b_dup,
    h_qkv, h_proj, h_up, h_down, h_dqkv, h_dproj, h_dup, h_ddown,
    cot_hbm, ew, evec, table, dgains, doffs,
    o_x, o_x1, o_a, o_u, o_y, o_gp, o_qkv, o_p, o_o, o_w, o_wproj, o_wup, o_wdown, o_dec,
    d_enc, d_qvb, d_upb, d_small, dec_out,
    w_qkv, w_proj, w_up, w_down, bias, biases, qkv, proj, up, down,
    ex, ea, eu, ey, egp, eqkv, ep, eo, ex1, epart, esend, erecv, esend2, erecv2, eown,
    cot, x0, x1, a, acts, probs, o, inverse, u, ut, y, gp, g32, gb, gt, acc, e_ref, hot, buf, dsend,
    load_s, out_s, cot_s, w_s, w_r, bias_s, bias_r, dw_s, dw_r, ex_s, ex_r, ex2_s, ex2_r, do_s, do_r,
):
    sec = lax.axis_index("section")
    lane = lax.axis_index("tensor")
    mate = lane + 1 - 2 * lax.rem(lane, 2)
    over = lax.rem(lane + 2, LANES)
    cross = lax.rem(mate + 2, LANES)
    me = sec * LANES + lane
    devices = 2 * LANES
    clip = me
    clips = (me, sec * LANES + over)

    def group_peer(step):
        peer = lax.rem(me + step, devices)
        return peer, {"section": lax.div(peer, LANES), "tensor": lax.rem(peer, LANES)}

    own = [
        pltpu.make_async_copy(src, dst.at[0], load_s.at[n])
        for n, (src, dst) in enumerate(
            ((h_qkv, w_qkv), (h_proj, w_proj), (h_up, w_up), (h_down, w_down))
        )
    ]

    def place(n, shard, part=None):
        thick = (128, 128, 512, 512)[n]
        base = shard * thick
        cut = pl.ds(pl.multiple_of(base, thick), thick)
        if part is None:
            return (qkv.at[:, :, cut], proj.at[cut, :], up.at[:, cut], down.at[cut, :])[n]
        some = span(part, (256, 64, 256, 256)[n])
        if n == 0:
            return qkv.at[:, some, cut]
        if n == 2:
            return up.at[some, cut]
        few = thick // 2
        rows = pl.ds(pl.multiple_of(base + part * few, few), few)
        return (proj if n == 1 else down).at[rows, :]

    shards = (h_dqkv, h_dproj, h_dup, h_ddown)
    keep = [
        pltpu.make_async_copy(shards[n], place(n, lane), load_s.at[4 + n]) for n in range(4)
    ]
    for copy in own + keep:
        copy.start()
    fetch = pltpu.make_async_copy(cot_hbm.at[clip], cot, cot_s)
    fetch.start()

    barrier = pltpu.get_barrier_semaphore()
    for step in range(1, devices):
        pl.semaphore_signal(barrier, inc=1, device_id_type=MESH, device_id=group_peer(step)[1])
    bias[...] = jnp.zeros_like(bias)
    half = w_proj.shape[1]
    bias[0:1, :] = b_up[...].astype(F32).reshape(1, -1)
    bias[1:3, 0:half] = b_qv[...].astype(F32)
    bias[3:4, 0:512] = b_dup[...].astype(F32).reshape(1, -1)
    bias[4:6, 0:128] = b_dqv[...].astype(F32)
    biases[lane] = bias[...]
    pl.semaphore_wait(barrier, devices - 1)

    def enc_weight(n):
        src = (h_qkv, h_proj, h_up, h_down)[n]
        dst = (w_qkv, w_proj, w_up, w_down)[n]
        return far(src, dst.at[1], w_s.at[n], w_r.at[n], {"tensor": mate})

    def bias_copy(step):
        return far(
            bias, biases.at[lane], bias_s.at[step], bias_r.at[step],
            {"tensor": lax.rem(lane + step, LANES)},
        )

    def half_of(n):
        some = span(sec, (256, 64, 256, 256)[n])
        return shards[n].at[:, some, :] if n == 0 else shards[n].at[some, :]

    def dec_weight(n, kind):
        peer = {"section": 1 - sec} if kind == 2 else {"tensor": over if kind == 0 else mate}
        if kind == 0:
            src, dst = half_of(n), place(n, lane, sec)
        elif kind == 1:
            src, dst = shards[n], place(n, lane)
        else:
            src = dst = place(n, over, 1 - sec if kind == 4 else sec)
        return far(src, dst, dw_s.at[5 * n + kind], dw_r.at[5 * n + kind], peer)

    enc_weight(0).start()
    for step in range(1, LANES):
        bias_copy(step).start()
    enc_weight(1).start()
    dec_weight(0, 0).start()
    enc_weight(2).start()
    enc_weight(3).start()
    for n in range(4):
        dec_weight(n, 1).start()

    def pass_on(n):
        dec_weight(n, 0).wait_recv()
        dec_weight(n, 2).start()
        dec_weight(n, 3).start()

    def pass_last(n):
        dec_weight(n, 2).wait_recv()
        dec_weight(n, 4).start()

    def arrived(n):
        keep[n].wait()
        dec_weight(n, 1).wait_recv()
        dec_weight(n, 3).wait_recv()
        dec_weight(n, 4).wait_recv()

    egain = gains[...].astype(F32)
    eoff = offs[...].astype(F32)
    stride = pat.shape[0] // VIS
    for c in range(2):
        row = lax.broadcasted_iota(jnp.int32, (PAD, pat.shape[0]), 0)
        col = lax.broadcasted_iota(jnp.int32, (PAD, pat.shape[0]), 1)
        pick = (col == row * stride + clips[c]).astype(F32).astype(BF16)
        ex[c * PAD : (c + 1) * PAD, :] = nn(pick, pat[...])

    emarks = head_marks(half, ENC_SIZE, BF16)
    key = lax.broadcasted_iota(jnp.int32, (PAD, PAD), 1)
    floor = jnp.where(key < VIS, NEG * LOG2E, -1e30)
    eones = ones_per_head(PAD, emarks)
    blocks = D // 256

    def give_part(i, side):
        cut = span(i, 256)
        return far(
            esend.at[(1 - side) * PAD : (2 - side) * PAD, cut],
            erecv.at[side * PAD : (side + 1) * PAD, cut],
            ex_s.at[2 * i + side], ex_r.at[2 * i + side], {"tensor": over},
        )

    for c in range(2):
        rows = slice(c * PAD, (c + 1) * PAD)
        hat, _ = normal(ex[rows, :])
        ea[rows, :] = (hat * egain[0:1] + eoff[0:1]).astype(BF16)
        limit = (VIS * wid[clips[c]]) // WIDE
        for g, shard in enumerate((lane, mate)):
            if c == 0 and g == 0:
                own[0].wait()
            if c == 0 and g == 1:
                enc_weight(0).wait_recv()
                for step in range(1, LANES):
                    bias_copy(step).wait_recv()
            if g == 0:
                bq, bv = bias[1:2, 0:half], bias[2:3, 0:half]
            else:
                bq, bv = biases[shard, 1:2, 0:half], biases[shard, 2:3, 0:half]
            eqkv[g, 0, rows] = (nt(ea[rows, :], w_qkv[g, 0]) + bq).astype(BF16)
            eqkv[g, 1, rows] = nt(ea[rows, :], w_qkv[g, 1]).astype(BF16)
            eqkv[g, 2, rows] = (nt(ea[rows, :], w_qkv[g, 2]) + bv).astype(BF16)
            p, out, _ = attend(
                eqkv[g, 0, rows], eqkv[g, 1, rows], eqkv[g, 2, rows], emarks, eones,
                lambda s: jnp.where(key < limit, s, floor), ENC_SCALE,
            )
            ep[g, c] = p
            eo[g, rows] = out
        if c == 0:
            own[1].wait()
            enc_weight(1).wait_recv()
        for i in range(blocks):
            cut = slice(i * 256, (i + 1) * 256)
            t = nn(eo[0, rows], w_proj[0, :, cut]) + nn(eo[1, rows], w_proj[1, :, cut])
            epart[rows, cut] = t
            esend[rows, cut] = t.astype(BF16)
            give_part(i, 1 - c).start()
    pass_on(0)
    own[2].wait()
    enc_weight(2).wait_recv()

    def give_last(i):
        cut = span(i, 256)
        return far(
            esend2.at[:, cut], erecv2.at[:, cut], ex2_s.at[i], ex2_r.at[i], {"tensor": over}
        )

    for c in (1, 0):
        rows = slice(c * PAD, (c + 1) * PAD)
        for i in range(blocks):
            give_part(i, c).wait_recv()
        t = ex[rows, :] + epart[rows, :] + erecv[rows, :].astype(F32) + eoff[2:3]
        ex1[rows, :] = t
        hat, _ = normal(t)
        eu[rows, :] = (hat * egain[1:2] + eoff[1:2]).astype(BF16)
        for g, shard in enumerate((lane, mate)):

            def enc_ff(i, g=g, shard=shard, rows=rows):
                cut = span(i, 256)
                h = nn(eu[rows, :], w_up[g, :, cut]) + biases[shard, 0:1, cut]
                act, slope = gelu_both(h)
                ey[g, rows, cut] = act.astype(BF16)
                egp[g, rows, cut] = slope.astype(BF16)

            loop(w_up.shape[2] // 256, enc_ff, unroll=3)
        if c == 1:
            own[3].wait()
            enc_weight(3).wait_recv()
        for i in range(blocks):
            cut = slice(i * 256, (i + 1) * 256)
            t = nn(ey[0, rows], w_down[0, :, cut]) + nn(ey[1, rows], w_down[1, :, cut])
            if c == 0:
                eown[:, cut] = t
            else:
                esend2[:, cut] = t.astype(BF16)
                give_last(i).start()
        if c == 1:
            for n in (1, 2, 3):
                dec_weight(n, 0).start()
            pass_last(0)
    outs = [
        pltpu.make_async_copy(src, dst, out_s.at[n])
        for n, (src, dst) in enumerate(
            (
                (ex.at[0:PAD, :], o_x), (ex1, o_x1), (ea, o_a), (eu, o_u), (ey, o_y), (egp, o_gp),
                (eqkv, o_qkv), (ep, o_p), (eo, o_o), (w_qkv.at[1], o_w), (w_proj.at[1], o_wproj),
                (w_up.at[1], o_wup), (w_down.at[1], o_wdown),
            )
        )
    ]
    for copy in outs:
        copy.start()
    for i in range(blocks):
        give_last(i).wait_recv()

    width = wid[clip]
    bits = jnp.where(width == WIDE, 3, 2)
    turn = shifts[0, clip] * width
    mod = GRID - 1
    spot = 0
    for i in range(order.shape[1]):
        spot = spot + jnp.where(order[0, i] == clip, i, 0)
    batch = spot // CM
    count = 0
    for i in range(order.shape[1]):
        count = count + jnp.where(batch == i // CM, wid[order[0, i]], 0)
    factor_rows = CM * GRID / (jnp.full((1, 1), count, jnp.int32) * GRID_ROWS).astype(F32)

    def slot_of(index):
        return (index - turn) & mod

    def code_of(slot):
        band = ((slot >> bits) + shifts[0, clip]) >> 2
        strip = ((slot & (width - 1)) + shifts[1, clip]) >> 2
        return band * 4 + strip

    e_ref[...] = (ex1[0:PAD, :] + eown[...] + erecv2[...].astype(F32) + eoff[3:4]).astype(BF16)
    vec = evec[...].astype(F32)
    m = (nn(e_ref[...], ew[...]) + vec[0:1]).astype(BF16)
    seen = vis[pl.ds(clip, 1), :]
    target = jnp.concatenate([(seen + turn) & mod, jnp.full((1, PAD - VIS), -1, jnp.int32)], 1)
    gain = dgains[...].astype(F32)
    offsets = doffs[...].astype(F32)

    def start(i):
        r = span(i, PAD)
        index = lax.broadcasted_iota(jnp.int32, (PAD, PAD), 0) + i * PAD
        column = lax.broadcasted_iota(jnp.int32, (PAD, PAD), 1)
        match = index == target
        oh = match.astype(F32).astype(BF16)
        hot[r, :] = oh
        hit = jnp.sum(match.astype(F32), -1, keepdims=True)
        grid = jnp.where(hit > 0, nn(oh, m), vec[1:2]).astype(BF16).astype(F32)
        slot = slot_of(index)
        by_row = ((slot >> bits) == column).astype(F32).astype(BF16)
        by_col = ((slot & (width - 1)) == column).astype(F32).astype(BF16)
        row_part = nn(by_row, table[0]) + nn(by_row, table[1])
        col_part = nn(by_col, table[0]) + nn(by_col, table[1])
        x = grid + jnp.concatenate([row_part, col_part], 1)
        x0[r, :] = x
        hat, _ = normal(x)
        a[r, :] = (hat * gain[0:1] + offsets[0:1]).astype(BF16)

    loop(GRID // PAD, start)
    arrived(0)

    def dec_bias(row, size):
        return jnp.concatenate([biases[k, row : row + 1, 0:size] for k in range(LANES)], 1)

    def project(i):
        r = span(i, 256)
        rows = a[r, :]
        acts[0, r, :] = (nn(rows, qkv[0]) + dec_bias(4, 128)).astype(BF16)
        acts[1, r, :] = nn(rows, qkv[1]).astype(BF16)
        acts[2, r, :] = (nn(rows, qkv[2]) + dec_bias(5, 128)).astype(BF16)

    loop(2, project)
    pass_on(1)
    pass_on(2)
    marks = head_marks(128, DEC_SIZE, BF16)
    marks32 = head_marks(128, DEC_SIZE, F32)
    dim = lax.broadcasted_iota(jnp.int32, (128, 1), 0)
    rows32 = [
        ((dim >= h * DEC_SIZE) & (dim < (h + 1) * DEC_SIZE)).astype(F32) for h in range(len(marks))
    ]

    ones = ones_per_head(PAD, marks)

    def attention(i):
        r = span(i, PAD)
        row_slot = slot_of(lax.broadcasted_iota(jnp.int32, (PAD, PAD), 0) + i * PAD)
        key_slot = slot_of(lax.broadcasted_iota(jnp.int32, (PAD, PAD), 1) + i * PAD)
        allowed = (code_of(row_slot) == code_of(key_slot)) & (key_slot < GRID_ROWS * width)
        for g in range(DD // 128):
            c = slice(g * 128, (g + 1) * 128)
            probs[i, :, g * 512 : (g + 1) * 512], o[r, c], inverse[r, c] = attend(
                acts[0, r, c], acts[1, r, c], acts[2, r, c], marks, ones,
                lambda s: jnp.where(allowed, s, NEG * LOG2E), DEC_SCALE,
            )

    loop(GRID // PAD, attention, unroll=2)
    pass_last(1)
    pass_last(2)
    pass_on(3)
    arrived(1)

    def mix(i):
        r = span(i, PAD)
        x = x0[r, :] + nn(o[r, :], proj[...]) + offsets[2:3]
        x1[r, :] = x
        hat, _ = normal(x)
        un = hat * gain[1:2] + offsets[1:2]
        u[r, :] = un.astype(BF16)
        ut[:, r] = jnp.transpose(un).astype(BF16)

    loop(GRID // PAD, mix)
    pass_last(3)
    arrived(2)

    def ff(i):
        k = lax.div(i, 4)
        side = lax.rem(lax.div(i, 2), 2)
        c = span(lax.div(i, 2), 256)
        r = span(lax.rem(i, 2), 256)
        h = nn(u[r, :], up[:, c]) + biases[k, 3:4, span(side, 256)]
        act, slope = gelu_both(h)
        y[r, c] = act.astype(BF16)
        gp[r, c] = slope.astype(BF16)

    loop(2 * up.shape[1] // 256, ff, unroll=2)
    arrived(3)
    fetch.wait()
    slot_col = slot_of(lax.broadcasted_iota(jnp.int32, (GRID, 1), 0))
    valid = (slot_col < GRID_ROWS * width).astype(F32)
    rolled = slot_of(lax.broadcasted_iota(jnp.int32, (GRID, GRID), 0))
    perm = (rolled == lax.broadcasted_iota(jnp.int32, (GRID, GRID), 1)).astype(F32).astype(BF16)

    def out(i):
        r = span(lax.rem(i, 2), 256)
        c = span(lax.div(i, 2), 256)
        acc[r, c] = nn(y[r, :], down[:, c])

    loop(4, out)
    full = ((acc[...] + x1[...] + offsets[3:4]) * valid).astype(BF16)
    turned = tn(full, perm).astype(BF16)
    for k in range(devices):
        dsend[k] = turned[k * dsend.shape[1] : (k + 1) * dsend.shape[1]]

    def decoded_copy(step):
        peer, spot = group_peer(step)
        return far(dsend.at[peer], dec_out.at[me], do_s.at[step], do_r.at[step], spot)

    for step in range(1, devices):
        decoded_copy(step).start()
    dec_out[me] = dsend[me]
    g = nn(perm, cot[...]) * valid * factor_rows
    g32[...] = g
    gb[...] = g.astype(BF16)
    gt[...] = jnp.transpose(g).astype(BF16)
    d_small[0:5, :] = jnp.zeros((5, DD), F32)
    d_small[5:6, :] = colsum(g)
    d_small[6:8, :] = jnp.zeros((2, DD), F32)

    def ff_back(i):
        c = span(i, 256)
        shard = lax.div(i, 2)
        side = lax.rem(i, 2)
        buf[shard, side, 0:512, 512:768] = nn(gt[...], y[:, c]).astype(BF16)
        dh = nt(gb[...], down[c, :]) * gp[:, c].astype(F32)
        d_upb[:, c] = colsum(dh)
        du = dh.astype(BF16)
        gp[:, c] = du
        buf[shard, 0, 0:512, span(side, 256)] = nn(ut[...], du).astype(BF16)

    loop(up.shape[1] // 256, ff_back, unroll=2)
    early = pltpu.make_async_copy(buf.at[:, 0, 0:512, :], o_dec.at[:, 0, 0:512, :], out_s.at[13])
    early.start()

    def ff_in(i):
        r = span(lax.rem(i, 2), 256)
        c = span(lax.div(i, 2), 256)
        acc[r, c] = nt(gp[r, :], up[c, :])

    loop(4, ff_in)

    def mix_back(i):
        r = span(i, PAD)
        hat, scale = normal(x1[r, :])
        da = acc[r, :]
        dx = g32[r, :] + normal_back(da, hat, scale, gain[1:2])
        d_small[1:2, :] += colsum(da * hat)
        d_small[3:4, :] += colsum(da)
        d_small[4:5, :] += colsum(dx)
        g32[r, :] = dx
        dxb = dx.astype(BF16)
        gb[r, :] = dxb
        u[r, :] = nt(dxb, proj[...]).astype(BF16)

    loop(GRID // PAD, mix_back)
    d_proj = tn(o[...], gb[...]).astype(BF16)
    for k in range(LANES):
        for j in range(LANES):
            block = d_proj[k * 128 : (k + 1) * 128, j * 128 : (j + 1) * 128]
            buf[k, 1, j * 128 : (j + 1) * 128, 384:512] = block

    def attention_back(i):
        r = span(i, PAD)
        for k in range(DD // 128):
            c = slice(k * 128, (k + 1) * 128)
            acts[0, r, c], acts[1, r, c], acts[2, r, c] = attend_back(
                acts[0, r, c], acts[1, r, c], acts[2, r, c],
                probs[i, :, k * 512 : (k + 1) * 512], o[r, c], inverse[r, c], u[r, c],
                marks, marks32, rows32, ones, DEC_SCALE,
            )

    loop(GRID // PAD, attention_back, unroll=2)
    d_qvb[0:1, :] = colsum(acts[0].astype(F32))
    d_qvb[1:2, :] = colsum(acts[2].astype(F32))

    def project_back(i):
        r = span(lax.rem(i, 2), 256)
        c = span(lax.div(i, 2), 256)
        acc[r, c] = (
            nt(acts[0, r, :], qkv[0, c, :])
            + nt(acts[1, r, :], qkv[1, c, :])
            + nt(acts[2, r, :], qkv[2, c, :])
        )

    loop(4, project_back)
    gt[...] = jnp.transpose(a[...].astype(F32)).astype(BF16)
    for j in range(3):
        d_qkv = nn(gt[...], acts[j]).astype(BF16)
        for k in range(LANES):
            buf[k, 1, 0:512, j * 128 : (j + 1) * 128] = d_qkv[:, k * 128 : (k + 1) * 128]

    def start_back(i):
        r = span(i, PAD)
        hat, scale = normal(x0[r, :])
        da = acc[r, :]
        dx = g32[r, :] + normal_back(da, hat, scale, gain[0:1])
        d_small[0:1, :] += colsum(da * hat)
        d_small[2:3, :] += colsum(da)
        dg = dx.astype(BF16)
        gb[r, :] = dg
        hit = jnp.sum(hot[r, :].astype(F32), -1, keepdims=True)
        d_small[7:8, :] += colsum(jnp.where(hit > 0, 0.0, dg.astype(F32)))

    loop(GRID // PAD, start_back)
    dm = tn(hot[...], gb[...])
    d_small[6:7, :] = colsum(dm)
    dmb = dm.astype(BF16)
    d_enc[...] = nt(dmb, ew[...]).astype(BF16)
    d_ew = tn(e_ref[...], dmb).astype(BF16)
    for k in range(LANES):
        for h in range(2):
            top = k * 192 + h * 64
            buf[k, h, 512:576, 0:512] = d_ew[top : top + 64]
            buf[k, h, 512:576, 512:768] = d_ew[k * 192 + 128 : (k + 1) * 192, h * 256 : (h + 1) * 256]

    rest = [
        pltpu.make_async_copy(buf.at[:, 1], o_dec.at[:, 1], out_s.at[14]),
        pltpu.make_async_copy(buf.at[:, 0, 512:576, :], o_dec.at[:, 0, 512:576, :], out_s.at[15]),
    ]
    for copy in rest:
        copy.start()
    for copy in outs + [early] + rest:
        copy.wait()
    for n in range(4):
        enc_weight(n).wait_send()
        for kind in range(5):
            dec_weight(n, kind).wait_send()
    for step in range(1, LANES):
        bias_copy(step).wait_send()
    for i in range(blocks):
        give_part(i, 0).wait_send()
        give_part(i, 1).wait_send()
        give_last(i).wait_send()
    for step in range(1, devices):
        decoded_copy(step).wait()


def forward_call(args, half, hid, dff):
    dma = lambda *s: pltpu.SemaphoreType.DMA(s)
    vm = lambda dtype, *shape: pltpu.VMEM(shape, dtype)
    rows = 2 * PAD
    keys = PAD * half // ENC_SIZE
    devices = 2 * LANES
    slab = DD // devices
    kept = [
        ((PAD, D), F32), ((rows, D), F32), ((rows, D), BF16), ((rows, D), BF16),
        ((2, rows, hid), BF16), ((2, rows, hid), BF16), ((2, 3, rows, half), BF16),
        ((2, 2, PAD, keys), BF16), ((2, rows, half), BF16),
        ((3, half, D), BF16), ((half, D), BF16), ((D, hid), BF16), ((hid, D), BF16),
        ((LANES, 2, DEC_ROWS, D), BF16),
    ]
    made = [
        ((PAD, D), BF16), ((2, DD), F32), ((1, dff), F32), ((8, DD), F32),
        ((devices, slab, GRID), BF16),
    ]
    return pl.pallas_call(
        forward_and_decoder,
        out_shape=[jax.ShapeDtypeStruct(s, d) for s, d in kept + made],
        in_specs=[SM, SM, SM] + [VM] * 8 + [ANY] * 9 + [VM] * 5,
        out_specs=[ANY] * len(kept) + [VM] * len(made),
        scratch_shapes=[
            vm(BF16, 2, 3, half, D), vm(BF16, 2, half, D), vm(BF16, 2, D, hid), vm(BF16, 2, hid, D),
            vm(F32, 8, D), vm(F32, LANES, 8, D),
            vm(BF16, 3, DD, DD), vm(BF16, DD, DD), vm(BF16, DD, dff), vm(BF16, dff, DD),
            vm(F32, rows, D), vm(BF16, rows, D), vm(BF16, rows, D), vm(BF16, 2, rows, hid),
            vm(BF16, 2, rows, hid), vm(BF16, 2, 3, rows, half), vm(BF16, 2, 2, PAD, keys),
            vm(BF16, 2, rows, half), vm(F32, rows, D), vm(F32, rows, D), vm(BF16, rows, D),
            vm(BF16, rows, D), vm(BF16, PAD, D), vm(BF16, PAD, D), vm(F32, PAD, D),
            vm(BF16, GRID, DD), vm(F32, GRID, DD), vm(F32, GRID, DD), vm(BF16, GRID, DD),
            vm(BF16, 3, GRID, DD), vm(BF16, GRID // PAD, PAD, DHEADS * PAD), vm(BF16, GRID, DD),
            vm(F32, GRID, DD),
            vm(BF16, GRID, DD), vm(BF16, DD, GRID), vm(BF16, GRID, dff), vm(BF16, GRID, dff),
            vm(F32, GRID, DD), vm(BF16, GRID, DD), vm(BF16, DD, GRID), vm(F32, GRID, DD),
            vm(BF16, PAD, D), vm(BF16, GRID, PAD), vm(BF16, LANES, 2, DEC_ROWS, D),
            vm(BF16, devices, slab, GRID),
            dma(8), dma(16), pltpu.SemaphoreType.DMA, dma(4), dma(4), dma(LANES), dma(LANES),
            dma(20), dma(20), dma(6), dma(6), dma(3), dma(3), dma(devices), dma(devices),
        ],
        compiler_params=pltpu.CompilerParams(
            collective_id=0, has_side_effects=True, vmem_limit_bytes=VMEM_LIMIT
        ),
    )(*args)


CH = 64
DEC_ROWS = 576
ENC_A = 768
ENC_B = 384
DEC_K = DEC_ROWS // CH
B_K = (DEC_ROWS + ENC_A + ENC_B) // CH
ALL_K = B_K + 1
A_TOP = DEC_ROWS
B_TOP = DEC_ROWS + ENC_A
S_TOP = B_TOP + ENC_B
LAG = 2
LEAD = 4
LATE = LEAD + 2 * (DEC_K - LEAD)
HALVED = ALL_K - 4


def add(x, y):
    return x + y


def backward_and_sums(
    d_enc, gains,
    h_u, h_y, h_gp, h_down0, h_down1, h_up0, h_up1,
    h_x, h_x1, h_a, h_qkv, h_p, h_o, h_w0, h_w1, h_proj0, h_proj1,
    dec, dec_qvb, dec_upb, dec_small,
    out, emb, dx_out,
    gb, gt, ut, part, send, recv, du, gx, dx1, d_o, d_acts, own, send1, recv1, dx32, dx,
    d_upb, d_qvb, d_small,
    acc, yacc, enc_mate, rcy, ry, rx, zl, zr, xc, cl, cr, small32, small,
    u, y, gp, down0, down1, up0, up1, x, x1, a, qkv, p, o, w0, w1, proj0, proj1, fetch_s,
    load_s, ex_s, ex_r,
    core_s, core_r, corey_s, corey_r, y_s, y_r, x_s, x_r, z_s, zl_r, zr_r,
    bl_s, br_s, b_r, a_s, a_r, emb_s, emb_r, dx_s, dx_r,
):
    sec = lax.axis_index("section")
    lane = lax.axis_index("tensor")
    pos = lax.axis_index("dp")
    count = lax.axis_size("dp")
    mate = lane + 1 - 2 * lax.rem(lane, 2)
    over = lax.rem(lane + 2, LANES)
    cross = lax.rem(mate + 2, LANES)
    first = pos == 0
    last = pos == count - 1
    me = sec * LANES + lane
    devices = 2 * LANES

    def group_peer(step):
        peer = lax.rem(me + step, devices)
        return peer, {"section": lax.div(peer, LANES), "tensor": lax.rem(peer, LANES)}

    barrier = pltpu.get_barrier_semaphore()
    for step in range(1, devices):
        pl.semaphore_signal(barrier, inc=1, device_id_type=MESH, device_id=group_peer(step)[1])

    @pl.when(pos > 0)
    def _():
        pl.semaphore_signal(barrier, inc=1, device_id={"dp": pos - 1}, device_id_type=MESH)

    @pl.when(pos < count - 1)
    def _():
        pl.semaphore_signal(barrier, inc=1, device_id={"dp": pos + 1}, device_id_type=MESH)

    fetches = [
        pltpu.make_async_copy(src, dst, fetch_s.at[n])
        for n, (src, dst) in enumerate(
            (
                (h_u, u), (h_y, y), (h_gp, gp), (h_down0, down0), (h_down1, down1), (h_up0, up0),
                (h_up1, up1), (h_x, x), (h_x1, x1), (h_a, a), (h_qkv, qkv), (h_p, p), (h_o, o),
                (h_w0, w0), (h_w1, w1), (h_proj0, proj0), (h_proj1, proj1),
            )
        )
    ]
    for fetch in fetches:
        fetch.start()
    loads = [
        pltpu.make_async_copy(dec.at[lane], acc.at[:, 0:DEC_ROWS, :], load_s.at[0]),
        pltpu.make_async_copy(dec.at[over], yacc.at[:, 0:DEC_ROWS, :], load_s.at[1]),
    ]
    for load in loads:
        load.start()
    small32[...] = jnp.zeros_like(small32)
    small[...] = jnp.zeros_like(small)
    d_small[...] = jnp.zeros_like(d_small)
    gb[0:PAD, :] = d_enc[...]
    ends = jnp.where(first, 0, 1) + jnp.where(last, 0, 1)
    pl.semaphore_wait(barrier, devices - 1 + ends)

    gain = gains[...].astype(F32)
    width = w0.shape[1]
    marks = head_marks(width, ENC_SIZE, BF16)
    marks32 = head_marks(width, ENC_SIZE, F32)
    ones = ones_per_head(PAD, marks)

    def rows(k, size=CH):
        return pl.ds(pl.multiple_of(k * size, size), size)

    def give_enc():
        return far(d_enc, gb.at[PAD : 2 * PAD, :], ex_s.at[0], ex_r.at[0], {"tensor": over})

    def give_part(i, half):
        cut = rows(i, 256)
        n = 1 + 2 * i + half
        return far(
            send.at[(1 - half) * PAD : (2 - half) * PAD, cut],
            recv.at[half * PAD : (half + 1) * PAD, cut],
            ex_s.at[n], ex_r.at[n], {"tensor": over},
        )

    def give_last(i):
        cut = rows(i, 256)
        return far(send1.at[:, cut], recv1.at[:, cut], ex_s.at[7 + i], ex_r.at[7 + i], {"tensor": over})

    def ff_back(g, i, down):
        c = rows(i, 256)
        d_down = nn(gt[...], y[g, :, c]).astype(BF16)
        dh = nt(gb[...], down[c, :]) * gp[g, :, c].astype(F32)
        d_upb[g, :, c] = colsum(dh)
        dub = dh.astype(BF16)
        du[g, :, c] = dub
        d_up = nn(ut[...], dub).astype(BF16)
        if g == 0:
            acc[1, A_TOP:B_TOP, c] = d_down
            acc[0, A_TOP:B_TOP, c] = d_up
        else:
            enc_mate[1, 0:ENC_A, c] = d_down
            enc_mate[0, 0:ENC_A, c] = d_up

    def ff_in(i):
        c = rows(i, 256)
        t = nt(du[0], up0[c, :]) + nt(du[1], up1[c, :])
        part[:, c] = t
        send[:, c] = t.astype(BF16)
        give_part(i, 0).start()
        give_part(i, 1).start()

    def norm_two(i):
        del i
        for fetch in fetches[7:]:
            fetch.wait()
        for k in range(D // 256):
            give_part(k, 0).wait_recv()
            give_part(k, 1).wait_recv()

        def body(j):
            r = rows(j, 64)
            da = part[r, :] + recv[r, :].astype(F32)
            hat, scale = normal(x1[r, :])
            g = gb[r, :].astype(F32)
            d = g + normal_back(da, hat, scale, gain[1:2])
            gx[r, :] = d.astype(BF16)
            dx1[r, :] = d

            @pl.when(j < 2)
            def _():
                d_small[1:2, :] += colsum(da * hat)
                d_small[3:4, :] += colsum(da)
                d_small[4:5, :] += colsum(d)
                d_small[5:6, :] += colsum(g)

        loop(2 * PAD // 64, body)

    def attention(g, proj):
        d_proj = tn(o[g], gx[...]).astype(BF16)
        if g == 0:
            acc[1, B_TOP + width : S_TOP, :] = d_proj
        else:
            enc_mate[1, ENC_A + width : ENC_A + 2 * width, :] = d_proj
        d_o[...] = nt(gx[...], proj[...]).astype(BF16)
        for c in range(2):
            r = slice(c * PAD, (c + 1) * PAD)
            dq, dk, dv = attend_back(
                qkv[g, 0, r], qkv[g, 1, r], qkv[g, 2, r], p[g, c], o[g, r], 1.0 / nn(p[g, c], ones),
                d_o[r, :], marks, marks32, None, ones, ENC_SCALE,
            )
            d_acts[g, 0, r] = dq
            d_acts[g, 1, r] = dk
            d_acts[g, 2, r] = dv
        d_qvb[g, 0:1, :] = colsum(d_acts[g, 0].astype(F32))
        d_qvb[g, 1:2, :] = colsum(d_acts[g, 2].astype(F32))

    def project_in(i):
        c = rows(i, 256)
        t = 0.0
        for g, w in enumerate((w0, w1)):
            for j in range(3):
                t += nn(d_acts[g, j], w[j, :, c])
        own[:, c] = t[:PAD]
        send1[:, c] = t[PAD:].astype(BF16)
        give_last(i).start()

    def project_grad(g):
        for j in range(3):
            row = (j % 2) * width
            d = tn(d_acts[g, j], a[...]).astype(BF16)
            if g == 0:
                acc[j // 2, B_TOP + row : B_TOP + row + width, :] = d
            else:
                enc_mate[j // 2, ENC_A + row : ENC_A + row + width, :] = d

    def norm_one(i):
        del i
        for k in range(D // 256):
            give_last(k).wait_recv()

        def body(j):
            r = rows(j, 64)
            da = own[r, :] + recv1[r, :].astype(F32)
            hat, scale = normal(x[r, :])
            d_small[0:1, :] += colsum(da * hat)
            d_small[2:3, :] += colsum(da)
            dx32[r, :] = dx1[r, :] + normal_back(da, hat, scale, gain[0:1])

        loop(PAD // 64, body)
        turned = jnp.transpose(dx32[...])
        cut = D // devices
        for k in range(devices):
            dx[k] = turned[k * cut : (k + 1) * cut, 0:VIS].astype(BF16)
        for r in range(LANES):
            small32[r, 0:1, 0:512] = dec_upb[:, r * 512 : (r + 1) * 512]
            small32[r, 1:2, 0:128] = dec_qvb[0:1, r * 128 : (r + 1) * 128]
            small32[r, 1:2, 128:256] = dec_qvb[1:2, r * 128 : (r + 1) * 128]
            small32[r, 8:16, 0:512] = dec_small[...]
            small32[r, 16:24, :] = d_small[...]
        for g, shard in enumerate((lane, mate)):
            small32[shard, 2:3, :] = d_upb[g]
            small32[shard, 3:4, 0:192] = d_qvb[g, 0:1]
            small32[shard, 3:4, 256:448] = d_qvb[g, 1:2]
        for r in range(LANES):
            small[r, 0, 0:32] = small32[r].astype(BF16)
        acc[:, S_TOP : S_TOP + CH, :] = small[lane]
        yacc[:, DEC_ROWS : DEC_ROWS + CH, :] = small[over]
        core_copy(LATE, small.at[mate]).start()
        corey_copy(LATE, small.at[cross]).start()
        for step in range(1, devices):
            dx_copy(step).start()
        dx_out[me] = dx[me]

    def core_enc(lo, hi):
        def body(m):
            block = block_of(m)

            @pl.when((block >= lo) & (block < hi))
            def _():
                src = pl.ds(pl.multiple_of(block * CH - DEC_ROWS, CH), CH)
                core_copy(m, enc_mate.at[:, src, :]).start()

        loop(ALL_K, body)

    def first_piece(i):
        del i
        for fetch in fetches[:7]:
            fetch.wait()
        ut[...] = jnp.transpose(u[...].astype(F32)).astype(BF16)
        give_enc().wait_recv()
        gt[...] = jnp.transpose(gb[...].astype(F32)).astype(BF16)

    pieces = [(0, 1, first_piece)]
    for g, down in enumerate((down0, down1)):
        pieces.append((0, 3, lambda i, g=g, down=down: ff_back(g, i, down)))
    pieces.append((3, 4, lambda i: core_enc(DEC_K, DEC_K + ENC_A // CH)))
    pieces.append((3, 4, lambda i: loop(D // 256, ff_in)))
    pieces.append((6, 7, norm_two))
    for g, proj in enumerate((proj0, proj1)):
        pieces.append((7 + g, 8 + g, lambda i, g=g, proj=proj: attention(g, proj)))
    pieces.append((9, 10, lambda i: loop(D // 256, project_in)))
    for g in range(2):
        pieces.append((10 + g, 11 + g, lambda i, g=g: project_grad(g)))
    pieces.append((12, 13, lambda i: core_enc(DEC_K + ENC_A // CH, B_K)))
    pieces.append((13, 14, norm_one))

    def dx_copy(step):
        peer, place = group_peer(step)
        return far(dx.at[peer], dx_out.at[me], dx_s.at[step], dx_r.at[step], place)

    def emb_copy(step):
        return far(
            out.at[:, pl.ds(512, CH), :], emb.at[lane], emb_s.at[step], emb_r.at[step],
            {"tensor": lax.rem(lane + step, LANES)},
        )

    def block_of(m):
        turn = jnp.where(lax.rem(m, 2) == 0, DEC_K + lax.div(m - LEAD, 2), LEAD + lax.div(m - LEAD - 1, 2))
        late = jnp.where(m == LATE, ALL_K - 1, m - 1)
        return jnp.where(m < LEAD, m, jnp.where(m >= LATE, late, turn))

    def is_dec(m):
        return block_of(m) < DEC_K

    def with_y(m):
        return is_dec(m) | (m == LATE)

    def at(m):
        return pl.ds(pl.multiple_of(block_of(m) * CH, CH), CH)

    def pair_at(m):
        return rows(jnp.where(m < HALVED, lax.div(m, 2), m - HALVED // 2))

    def y_at(m):
        return rows(jnp.minimum(block_of(m), DEC_K))

    def core_copy(m, src):
        return far(src, out.at[:, at(m), :], core_s.at[m], core_r.at[m], {"tensor": mate})

    def corey_copy(m, src):
        return far(src, rcy.at[:, y_at(m), :], corey_s.at[m], corey_r.at[m], {"tensor": mate})

    def y_copy(m):
        cut = y_at(m)
        return far(
            yacc.at[:, cut, :], ry.at[:, cut, :], y_s.at[m], y_r.at[m], {"tensor": over}
        )

    def x_copy(m):
        return far(
            acc.at[1 - sec, at(m), :], rx.at[pair_at(m), :], x_s.at[m], x_r.at[m],
            {"section": 1 - sec},
        )

    def xc_copy(m):
        return far(
            acc.at[:, at(m), :], xc.at[:, pair_at(m), :], x_s.at[m], x_r.at[m],
            {"section": 1 - sec},
        )

    def z_copy(m, whole, right):
        if whole:
            src, dst = acc.at[:, at(m), :], (cl if right else cr).at[:, pair_at(m), :]
        else:
            src, dst = acc.at[sec, at(m), :], (zl if right else zr).at[pair_at(m), :]
        landed = zl_r if right else zr_r
        return far(src, dst, z_s.at[m], landed.at[m], {"dp": pos + 1 if right else pos - 1})

    def b_copy(m, whole, right):
        place = out.at[:, at(m), :] if whole else out.at[sec, at(m), :]
        sent = br_s if right else bl_s
        return far(place, place, sent.at[m], b_r.at[m], {"dp": pos + 1 if right else pos - 1})

    def a_copy(m):
        place = out.at[sec, at(m), :]
        return far(place, place, a_s.at[m], a_r.at[m], {"section": 1 - sec})

    def a_wait(m):
        place = out.at[1 - sec, at(m), :]
        far(place, place, a_s.at[m], a_r.at[m], {"section": 1 - sec}).wait_recv()

    give_enc().start()

    def start_core(m):
        @pl.when(is_dec(m))
        def _():
            core_copy(m, dec.at[mate, :, at(m), :]).start()
            corey_copy(m, dec.at[cross, :, at(m), :]).start()

    loop(LATE, start_core)
    for load in loads:
        load.wait()

    def stage_c(m):
        core_copy(m, out.at[:, at(m), :]).wait_recv()
        acc[:, at(m), :] = add(acc[:, at(m), :], out[:, at(m), :])

        @pl.when(with_y(m))
        def _():
            corey_copy(m, rcy.at[:, y_at(m), :]).wait_recv()
            yacc[:, y_at(m), :] = add(yacc[:, y_at(m), :], rcy[:, y_at(m), :])
            y_copy(m).start()

    def finished(m):
        @pl.when(block_of(m) == DEC_K - 1)
        def _():
            for step in range(1, LANES):
                emb_copy(step).start()
            emb[lane] = out[:, 512 : 512 + CH, :]

    def line_of(root, whole):
        left = pos < root
        right = pos > root
        here = pos == root
        reach = max(root, count - 1 - root)
        level = jnp.where(left, pos, jnp.where(right, count - 1 - pos, reach))
        dist = jnp.where(left, root - pos, pos - root)

        def view(ref, m):
            return ref.at[:, at(m), :] if whole else ref.at[sec, at(m), :]

        def landed(ref, m):
            return ref.at[:, pair_at(m), :] if whole else ref.at[pair_at(m), :]

        from_left, from_right = (cl, cr) if whole else (zl, zr)

        def outer(m):
            @pl.when(left & first)
            def _():
                z_copy(m, whole, True).start()

            @pl.when(right & last)
            def _():
                z_copy(m, whole, False).start()

        def inward(m):
            @pl.when(left & (pos > 0))
            def _():
                z_copy(m, whole, True).wait_recv()
                view(acc, m)[...] = add(view(acc, m)[...], landed(from_left, m)[...])
                z_copy(m, whole, True).start()

            @pl.when(right & (pos < count - 1))
            def _():
                z_copy(m, whole, False).wait_recv()
                view(acc, m)[...] = add(view(acc, m)[...], landed(from_right, m)[...])
                z_copy(m, whole, False).start()

            @pl.when(here)
            def _():
                total = view(acc, m)[...].astype(F32)
                if root > 0:
                    z_copy(m, whole, True).wait_recv()
                    total = total + landed(from_left, m)[...].astype(F32)
                if root < count - 1:
                    z_copy(m, whole, False).wait_recv()
                    total = total + landed(from_right, m)[...].astype(F32)
                if whole:
                    view(acc, m)[...] = total.astype(BF16)
                    xc_copy(m).start()
                else:
                    view(out, m)[...] = total.astype(BF16)
                    spread(m)
                    a_copy(m).start()

        def spread(m):
            if root > 0:
                b_copy(m, whole, False).start()
            if root < count - 1:
                b_copy(m, whole, True).start()

        def crossed(m):
            xc_copy(m).wait_recv()
            view(out, m)[...] = add(view(acc, m)[...], landed(xc, m)[...])
            spread(m)
            finished(m)

        def outward(m):
            b_copy(m, whole, False).wait_recv()

            @pl.when(left & (pos > 0))
            def _():
                b_copy(m, whole, False).start()

            @pl.when(right & (pos < count - 1))
            def _():
                b_copy(m, whole, True).start()

            if whole:
                finished(m)
            else:
                a_copy(m).start()

        def sent(m):
            @pl.when(jnp.logical_not(here))
            def _():
                z_copy(m, whole, True).wait_send()

            @pl.when((pos <= root) & (pos > 0))
            def _():
                b_copy(m, whole, False).wait_send()

            @pl.when((pos >= root) & (pos < count - 1))
            def _():
                b_copy(m, whole, True).wait_send()

            if whole:
                @pl.when(here)
                def _():
                    xc_copy(m).wait_send()
            else:
                x_copy(m).wait_send()
                a_copy(m).wait_send()

        def add_y(m):
            @pl.when(with_y(m))
            def _():
                y_copy(m).wait_recv()
                acc[:, at(m), :] = add(acc[:, at(m), :], ry[:, y_at(m), :])

            if whole:
                outer(m)
            else:
                x_copy(m).start()

        def add_x(m):
            x_copy(m).wait_recv()
            acc[sec, at(m), :] = add(acc[sec, at(m), :], rx[pair_at(m), :])
            outer(m)

        def last_half(m):
            a_wait(m)
            finished(m)

        base = 1 if whole else 2
        back = base + reach + dist + (1 if whole else 0)
        steps = [(back, jnp.logical_not(here), outward), (base + level, level > 0, inward), (1, True, add_y)]
        if whole:
            steps.append((base + reach + 1, here, crossed))
        else:
            steps += [(back + 1, True, last_half), (2, True, add_x)]
        return steps, sent

    low_root = (count - 1) // 2
    high_root = min(low_root + 1, count - 1)
    lines = [
        (lambda m: (lax.rem(m, 2) == 1) | (m >= HALVED), *line_of(low_root, False)),
        (lambda m: (lax.rem(m, 4) == 0) & (m < HALVED), *line_of(low_root, True)),
        (lambda m: (lax.rem(m, 4) == 2) & (m < HALVED), *line_of(high_root, True)),
    ]

    def tick(n):
        @pl.when(n < LATE)
        def _():
            for low, high, piece in pieces:
                @pl.when((n >= low) & (n < high))
                def _(low=low, piece=piece):
                    piece(n - low)

        for mine, steps, _ in lines:
            for offset, enabled, stage in steps:
                m = n - LAG * offset

                @pl.when((m >= 0) & (m < ALL_K) & mine(m) & enabled)
                def _(m=m, stage=stage):
                    stage(m)

        @pl.when(n < ALL_K)
        def _():
            stage_c(n)

    far_reach = max(low_root, count - 1 - low_root, high_root, count - 1 - high_root)
    loop(ALL_K + LAG * (3 + 2 * far_reach) + 1, tick)

    def finish(m):
        core_copy(m, out.at[:, at(m), :]).wait_send()

        @pl.when(with_y(m))
        def _():
            corey_copy(m, rcy.at[:, y_at(m), :]).wait_send()
            y_copy(m).wait_send()

        for mine, _, sent in lines:
            @pl.when(mine(m))
            def _(sent=sent):
                sent(m)

    loop(ALL_K, finish)
    for step in range(1, devices):
        dx_copy(step).wait()
    for step in range(1, LANES):
        emb_copy(step).wait()
    give_enc().wait_send()
    for k in range(D // 256):
        give_part(k, 0).wait_send()
        give_part(k, 1).wait_send()
        give_last(k).wait_send()


def backward_call(args, half, hid):
    dma = lambda *s: pltpu.SemaphoreType.DMA(s)
    vm = pltpu.VMEM
    full = ALL_K * CH
    y_half = DEC_ROWS + CH
    whole = HALVED // 2 * CH
    by_half = full - whole
    k = ALL_K
    rows = 2 * PAD
    cut = D // (2 * LANES)
    specs = [VM, VM] + [ANY] * 18 + [VM] * 3
    return pl.pallas_call(
        backward_and_sums,
        out_shape=[
            jax.ShapeDtypeStruct((2, full, D), BF16),
            jax.ShapeDtypeStruct((LANES, 2, CH, D), BF16),
            jax.ShapeDtypeStruct((2 * LANES, cut, VIS), BF16),
        ],
        in_specs=specs,
        out_specs=[VM] * 3,
        scratch_shapes=[
            vm((rows, D), BF16), vm((D, rows), BF16), vm((D, rows), BF16),
            vm((rows, D), F32), vm((rows, D), BF16), vm((rows, D), BF16),
            vm((2, rows, hid), BF16), vm((rows, D), BF16), vm((rows, D), F32),
            vm((rows, half), BF16), vm((2, 3, rows, half), BF16),
            vm((PAD, D), F32), vm((PAD, D), BF16), vm((PAD, D), BF16), vm((PAD, D), F32),
            vm((2 * LANES, cut, VIS), BF16),
            vm((2, 1, hid), F32), vm((2, 2, half), F32), vm((8, D), F32),
            vm((2, full, D), BF16), vm((2, y_half, D), BF16), vm((2, ENC_A + ENC_B, D), BF16),
            vm((2, y_half, D), BF16), vm((2, y_half, D), BF16),
            vm((by_half, D), BF16), vm((by_half, D), BF16), vm((by_half, D), BF16),
            vm((2, whole, D), BF16), vm((2, whole, D), BF16), vm((2, whole, D), BF16),
            vm((LANES, 32, D), F32), vm((LANES, 2, CH, D), BF16),
            *[vm(v.shape, v.dtype) for v in args[2:19]], dma(17), dma(2), dma(10), dma(10),
            dma(k), dma(k), dma(k), dma(k), dma(k), dma(k),
            dma(k), dma(k), dma(k), dma(k), dma(k),
            dma(k), dma(k), dma(k), dma(k), dma(k), dma(LANES), dma(LANES),
            dma(2 * LANES), dma(2 * LANES),
        ],
        compiler_params=pltpu.CompilerParams(
            collective_id=1, has_side_effects=True, vmem_limit_bytes=VMEM_LIMIT
        ),
    )(*args)


def finish_grads(
    total, emb, decoded, dx, decoded_out, dx_out,
    e_qkv, e_qvb, e_proj, e_up, e_upb, e_down, e_gain, e_off,
    d_qkv, d_qvb, d_proj, d_up, d_upb, d_down, d_gain, d_off, d_ew, d_ev,
):
    half = e_proj.shape[0]
    decoded_out[...] = decoded[...]
    dx_out[...] = dx[...]
    e_up[...] = total[0, A_TOP:B_TOP, :].astype(F32)
    e_down[...] = jnp.transpose(total[1, A_TOP:B_TOP, :].astype(F32))
    e_qkv[0] = total[0, B_TOP : B_TOP + half, :].astype(F32)
    e_qkv[1] = total[0, B_TOP + half : S_TOP, :].astype(F32)
    e_qkv[2] = total[1, B_TOP : B_TOP + half, :].astype(F32)
    e_proj[...] = total[1, B_TOP + half : S_TOP, :].astype(F32)
    d_up[...] = total[0, 0:512, 0:512].astype(F32)
    d_down[0:256, :] = jnp.transpose(total[0, 0:512, 512:768].astype(F32))
    d_down[256:512, :] = jnp.transpose(total[1, 0:512, 512:768].astype(F32))
    for j in range(3):
        d_qkv[j] = total[1, 0:512, j * 128 : (j + 1) * 128].astype(F32)
    for j in range(LANES):
        cut = slice(j * 128, (j + 1) * 128)
        d_proj[:, cut] = total[1, cut, 384:512].astype(F32)
    for k in range(LANES):
        for h in range(2):
            top = k * 192 + h * 64
            d_ew[top : top + 64, :] = emb[k, h, :, 0:512].astype(F32)
            d_ew[k * 192 + 128 : (k + 1) * 192, h * 256 : (h + 1) * 256] = emb[
                k, h, :, 512:768
            ].astype(F32)
    little = total[0, S_TOP : S_TOP + 32, :].astype(F32)
    d_upb[...] = little[0, 0:512]
    d_qvb[0:1, :] = little[1:2, 0:128]
    d_qvb[1:2, :] = little[1:2, 128:256]
    e_upb[...] = little[2]
    e_qvb[0:1, :] = little[3:4, 0:192]
    e_qvb[1:2, :] = little[3:4, 256:448]
    d_gain[...] = little[8:10, 0:512]
    d_off[...] = little[10:14, 0:512]
    d_ev[...] = little[14:16, 0:512]
    e_gain[...] = little[16:18]
    e_off[...] = little[18:22]


def call(kernel, specs, shapes, scratch, args):
    return pl.pallas_call(
        kernel,
        out_shape=[jax.ShapeDtypeStruct(s, d) for s, d in shapes],
        in_specs=specs,
        out_specs=[VM] * len(shapes),
        scratch_shapes=scratch,
        compiler_params=pltpu.CompilerParams(vmem_limit_bytes=VMEM_LIMIT),
    )(*args)


def position_rows():
    quarter = DD // 4
    freq = np.exp(np.arange(quarter, dtype=np.float32) * np.float32(-math.log(10000.0) / quarter))
    angle = np.arange(PAD, dtype=np.float32)[:, None] * freq[None, :].astype(np.float32)
    both = np.concatenate([np.sin(angle), np.cos(angle)], 1).astype(np.float32)
    high = both.astype(jnp.bfloat16)
    low = (both - high.astype(np.float32)).astype(jnp.bfloat16)
    return np.stack([high, low])


def per_device(
    patches, cotangent, widths, visible, window_shift, batch_order,
    encoder_qkv, encoder_qvbias, encoder_proj, encoder_up, encoder_upbias, encoder_down,
    encoder_gains, encoder_offsets,
    decoder_qkv, decoder_qvbias, decoder_proj, decoder_up, decoder_upbias, decoder_down,
    decoder_gains, decoder_offsets, embed_weight, embed_vectors,
):
    qkv0 = encoder_qkv.transpose(1, 2, 0)
    half = qkv0.shape[1]
    hid = encoder_up.shape[1]
    dff = decoder_up.shape[1] * LANES
    flat = patches.transpose(1, 0, 2).reshape(-1, D)
    (
        x, x1, a, u, y, gp, qkv, p, o, qkv1, proj1, up1, down1, dec_buf,
        d_enc, d_dqvb, d_dupb, d_dsmall, out_all,
    ) = forward_call(
        (
            widths, window_shift.T, batch_order, visible, flat, encoder_gains, encoder_offsets,
            encoder_qvbias, encoder_upbias, decoder_qvbias, decoder_upbias,
            qkv0, encoder_proj, encoder_up, encoder_down,
            decoder_qkv.transpose(1, 0, 2), decoder_proj, decoder_up, decoder_down,
            cotangent, embed_weight, embed_vectors, jnp.asarray(position_rows()),
            decoder_gains, decoder_offsets,
        ),
        half, hid, dff,
    )
    total, emb, dx_all = backward_call(
        (
            d_enc, encoder_gains, u, y, gp, encoder_down, down1, encoder_up, up1,
            x, x1, a, qkv, p, o, qkv0, qkv1, encoder_proj, proj1,
            dec_buf, d_dqvb, d_dupb, d_dsmall,
        ),
        half, hid,
    )
    f = lambda *shape: (shape, F32)
    out_all, dx_all, *grads = call(
        finish_grads, [VM] * 4,
        [
            (out_all.shape, BF16), (dx_all.shape, BF16), f(3, half, D), f(2, half), f(half, D), f(D, hid), f(hid), f(hid, D), f(2, D), f(4, D),
            f(3, DD, 128), f(2, 128), f(128, DD), f(DD, 512), f(512), f(512, DD), f(2, DD), f(4, DD),
            f(D, DD), f(2, DD),
        ],
        [], (total, emb, out_all, dx_all),
    )
    grads[0] = grads[0].transpose(2, 0, 1)
    grads[8] = grads[8].transpose(1, 0, 2)
    return (out_all.swapaxes(1, 2), dx_all.swapaxes(1, 2), *grads)


def solution(mesh):
    weights = (
        P(None, None, "tensor"), P(None, "tensor"), P("tensor", None), P(None, "tensor"),
        P("tensor"), P("tensor", None), P(), P(),
    )
    split = P("dp", None, ("section", "tensor"))
    return jax.shard_map(
        per_device,
        mesh=mesh,
        in_specs=(
            P("dp", None, None), P("dp", None, None), P("dp"), P("dp", None), P("dp", None),
            P("dp", None),
        ) + weights + weights + (P(), P()),
        out_specs=(split, split) + weights + weights + (P(), P()),
        check_vma=False,
    )
```

```python
import math

import jax
import jax.numpy as jnp
import numpy as np
from jax import lax
from jax.experimental import pallas as pl
from jax.experimental.pallas import tpu as pltpu
from jax.sharding import PartitionSpec as P

D = 768
HEADS = 12
DD = 512
DHEADS = 16
GRID_ROWS = 64
WIDE = 8
WIN = 4
VIS = 102
CM = 4
GRID = 512
LANES = 4
PAD = 128
EPS = 1e-06
NEG = -10000.0
F32 = jnp.float32
BF16 = jnp.bfloat16
VMEM_LIMIT = 60 * 1024 * 1024

VM = pl.BlockSpec(memory_space=pltpu.VMEM)
SM = pl.BlockSpec(memory_space=pltpu.SMEM)
ANY = pl.BlockSpec(memory_space=pl.ANY)


def nn(a, b):
    return lax.dot_general(a, b, (((1,), (0,)), ((), ())), preferred_element_type=F32)


def nt(a, b):
    return lax.dot_general(a, b, (((1,), (1,)), ((), ())), preferred_element_type=F32)


def tn(a, b):
    return lax.dot_general(a, b, (((0,), (0,)), ((), ())), preferred_element_type=F32)


def loop(count, body, unroll=1):
    def step(i, carry):
        body(i)
        return carry

    lax.fori_loop(0, count, step, 0, unroll=unroll)


def span(i, size):
    return pl.ds(pl.multiple_of(i * size, size), size)


def normal(x):
    center = x - jnp.mean(x, -1, keepdims=True)
    scale = lax.rsqrt(jnp.mean(center * center, -1, keepdims=True) + EPS)
    return center * scale, scale


def normal_back(dy, hat, scale, gain):
    d = dy * gain
    return scale * (
        d - jnp.mean(d, -1, keepdims=True) - hat * jnp.mean(d * hat, -1, keepdims=True)
    )


def gelu_both(h):
    phi = 0.5 * lax.erf(h * math.sqrt(0.5)) + 0.5
    bell = jnp.exp2(h * h * (-0.5 * math.log2(math.e)))
    return h * phi, phi + h * bell * (1.0 / math.sqrt(2.0 * math.pi))


def colsum(x):
    return jnp.sum(x, 0, keepdims=True)


def head_marks(width, size, dtype):
    lane = lax.broadcasted_iota(jnp.int32, (1, width), 1)
    return [((lane >= h * size) & (lane < (h + 1) * size)).astype(dtype) for h in range(width // size)]


def stacked(x, marks):
    return jnp.concatenate([x * m for m in marks], 0)


LOG2E = math.log2(math.e)


def attend(q, k, v, marks, ones, masked, scale):
    keys = k.shape[0]
    s = nt(q, stacked(k, marks))
    parts = []
    for h in range(len(marks)):
        x = masked(s[:, h * keys : (h + 1) * keys] * (scale * LOG2E))
        parts.append(jnp.exp2(x - jnp.max(x, -1, keepdims=True)).astype(BF16))
    e = jnp.concatenate(parts, 1)
    width = q.shape[1]
    if width % 128:
        top, total = nn(e, stacked(v, marks)), nn(e, ones)
    else:
        both = nn(e, jnp.concatenate([stacked(v, marks), ones], 1))
        top, total = both[:, :width], both[:, width:]
    inverse = 1.0 / total
    return e, (top * inverse).astype(BF16), inverse


def attend_back(q, k, v, e, o, inverse, d_out, marks, marks32, rows32, ones, scale):
    keys = k.shape[0]
    width = q.shape[1]
    d_one = d_out.astype(F32) * inverse
    d_two = (d_one * o.astype(F32)).astype(BF16)
    d_one = d_one.astype(BF16)
    if width % 128:
        d_s = nt(d_one, stacked(v, marks)) - nt(d_two, ones)
    else:
        d_s = nt(
            jnp.concatenate([d_one, d_two], 1), jnp.concatenate([stacked(v, marks), -ones], 1)
        )
    dr = (e.astype(F32) * d_s * scale).astype(BF16)
    d_q = nn(dr, stacked(k, marks)).astype(BF16)
    if width % 128:
        d_k_all, d_v_all = tn(dr, q), tn(e, d_one)
        d_k = d_v = 0.0
        for h in range(len(marks)):
            cut = slice(h * keys, (h + 1) * keys)
            d_k += d_k_all[cut] * marks32[h]
            d_v += d_v_all[cut] * marks32[h]
        return d_q, d_k.astype(BF16), d_v.astype(BF16)
    d_k_all = nn(jnp.transpose(q.astype(F32)).astype(BF16), dr)
    d_v_all = nn(jnp.transpose(d_one.astype(F32)).astype(BF16), e)
    d_k = d_v = 0.0
    for h in range(len(marks)):
        cut = slice(h * keys, (h + 1) * keys)
        d_k += d_k_all[:, cut] * rows32[h]
        d_v += d_v_all[:, cut] * rows32[h]
    return d_q, jnp.transpose(d_k).astype(BF16), jnp.transpose(d_v).astype(BF16)


def ones_per_head(keys, marks):
    return jnp.concatenate([jnp.broadcast_to(m, (keys, m.shape[1])) for m in marks], 0)


ENC_SIZE = D // HEADS
ENC_SCALE = ENC_SIZE ** -0.5
DEC_SIZE = DD // DHEADS
DEC_SCALE = DEC_SIZE ** -0.5


CH = 64
DEC_ROWS = 576
ENC_A = 768
ENC_B = 384
DEC_K = DEC_ROWS // CH
B_K = (DEC_ROWS + ENC_A + ENC_B) // CH
ALL_K = B_K + 1
A_TOP = DEC_ROWS
B_TOP = DEC_ROWS + ENC_A
S_TOP = B_TOP + ENC_B
EARLY = 5
EARLY_ROWS = EARLY * CH
LAG = 2
MIXED = EARLY + 2 * (DEC_K - EARLY)
LATE = 16
HALVED = ALL_K - 4


def tile_of(number):
    place = number // 3
    return place % 2, place // 2 * CH, number % 3 * 256


MESH = pl.DeviceIdType.MESH


def far(src, dst, send, recv, peer):
    return pltpu.make_async_remote_copy(
        src_ref=src, dst_ref=dst, send_sem=send, recv_sem=recv, device_id=peer, device_id_type=MESH
    )


def forward_and_decoder(
    wid, shifts, order, vis, pat, gains, offs, b_qv, b_up, b_dqv, b_dup,
    h_qkv, h_proj, h_up, h_down, h_dqkv, h_dproj, h_dup, h_ddown,
    cot_hbm, ew, evec, table, dgains, doffs,
    o_x, o_x1, o_a, o_u, o_y, o_gp, o_qkv, o_p, o_o, o_w, o_wproj, o_wup, o_wdown, o_dec,
    d_enc, d_qvb, d_upb, d_small, dec_out,
    w_qkv, w_proj, w_up, w_down, bias, biases, qkv, proj, up, down,
    ex, ea, eu, ey, egp, eqkv, ep, eo, ex1, epart, esend, erecv, esend2, erecv2, eown,
    cot, x0, x1, a, acts, probs, o, inverse, u, ut, y, gp, g32, gb, gt, acc, e_ref, hot, buf, dsend, e_rc, e_rcy, e_ry,
    load_s, out_s, cot_s, w_s, w_r, bias_s, bias_r, dw_s, dw_r, ex_s, ex_r, ex2_s, ex2_r, do_s, do_r, e_s, e_r,
):
    sec = lax.axis_index("section")
    lane = lax.axis_index("tensor")
    mate = lane + 1 - 2 * lax.rem(lane, 2)
    over = lax.rem(lane + 2, LANES)
    cross = lax.rem(mate + 2, LANES)
    me = sec * LANES + lane
    devices = 2 * LANES
    clip = me
    clips = (me, sec * LANES + over)

    def group_peer(step):
        peer = lax.rem(me + step, devices)
        return peer, {"section": lax.div(peer, LANES), "tensor": lax.rem(peer, LANES)}

    own = [
        pltpu.make_async_copy(src, dst.at[0], load_s.at[n])
        for n, (src, dst) in enumerate(
            ((h_qkv, w_qkv), (h_proj, w_proj), (h_up, w_up), (h_down, w_down))
        )
    ]

    def place(n, shard, part=None):
        thick = (128, 128, 512, 512)[n]
        base = shard * thick
        cut = pl.ds(pl.multiple_of(base, thick), thick)
        if part is None:
            return (qkv.at[:, :, cut], proj.at[cut, :], up.at[:, cut], down.at[cut, :])[n]
        some = span(part, (256, 64, 256, 256)[n])
        if n == 0:
            return qkv.at[:, some, cut]
        if n == 2:
            return up.at[some, cut]
        few = thick // 2
        rows = pl.ds(pl.multiple_of(base + part * few, few), few)
        return (proj if n == 1 else down).at[rows, :]

    shards = (h_dqkv, h_dproj, h_dup, h_ddown)
    keep = [
        pltpu.make_async_copy(shards[n], place(n, lane), load_s.at[4 + n]) for n in range(4)
    ]
    for copy in own + keep:
        copy.start()
    fetch = pltpu.make_async_copy(cot_hbm.at[clip], cot, cot_s)
    fetch.start()

    barrier = pltpu.get_barrier_semaphore()
    for step in range(1, devices):
        pl.semaphore_signal(barrier, inc=1, device_id_type=MESH, device_id=group_peer(step)[1])
    bias[...] = jnp.zeros_like(bias)
    half = w_proj.shape[1]
    bias[0:1, :] = b_up[...].astype(F32).reshape(1, -1)
    bias[1:3, 0:half] = b_qv[...].astype(F32)
    bias[3:4, 0:512] = b_dup[...].astype(F32).reshape(1, -1)
    bias[4:6, 0:128] = b_dqv[...].astype(F32)
    biases[lane] = bias[...]
    pl.semaphore_wait(barrier, devices - 1)

    def enc_weight(n):
        src = (h_qkv, h_proj, h_up, h_down)[n]
        dst = (w_qkv, w_proj, w_up, w_down)[n]
        return far(src, dst.at[1], w_s.at[n], w_r.at[n], {"tensor": mate})

    def bias_copy(step):
        return far(
            bias, biases.at[lane], bias_s.at[step], bias_r.at[step],
            {"tensor": lax.rem(lane + step, LANES)},
        )

    def half_of(n):
        some = span(sec, (256, 64, 256, 256)[n])
        return shards[n].at[:, some, :] if n == 0 else shards[n].at[some, :]

    def dec_weight(n, kind):
        peer = {"section": 1 - sec} if kind == 2 else {"tensor": over if kind == 0 else mate}
        if kind == 0:
            src, dst = half_of(n), place(n, lane, sec)
        elif kind == 1:
            src, dst = shards[n], place(n, lane)
        else:
            src = dst = place(n, over, 1 - sec if kind == 4 else sec)
        return far(src, dst, dw_s.at[5 * n + kind], dw_r.at[5 * n + kind], peer)

    enc_weight(0).start()
    for step in range(1, LANES):
        bias_copy(step).start()
    enc_weight(1).start()
    dec_weight(0, 0).start()
    enc_weight(2).start()
    enc_weight(3).start()
    for n in range(4):
        dec_weight(n, 1).start()

    def pass_on(n):
        dec_weight(n, 0).wait_recv()
        dec_weight(n, 2).start()
        dec_weight(n, 3).start()

    def pass_last(n):
        dec_weight(n, 2).wait_recv()
        dec_weight(n, 4).start()

    def arrived(n):
        keep[n].wait()
        dec_weight(n, 1).wait_recv()
        dec_weight(n, 3).wait_recv()
        dec_weight(n, 4).wait_recv()

    egain = gains[...].astype(F32)
    eoff = offs[...].astype(F32)
    stride = pat.shape[0] // VIS
    for c in range(2):
        row = lax.broadcasted_iota(jnp.int32, (PAD, pat.shape[0]), 0)
        col = lax.broadcasted_iota(jnp.int32, (PAD, pat.shape[0]), 1)
        pick = (col == row * stride + clips[c]).astype(F32).astype(BF16)
        ex[c * PAD : (c + 1) * PAD, :] = nn(pick, pat[...])

    emarks = head_marks(half, ENC_SIZE, BF16)
    key = lax.broadcasted_iota(jnp.int32, (PAD, PAD), 1)
    floor = jnp.where(key < VIS, NEG * LOG2E, -1e30)
    eones = ones_per_head(PAD, emarks)
    blocks = D // 256

    def give_part(i, side):
        cut = span(i, 256)
        return far(
            esend.at[(1 - side) * PAD : (2 - side) * PAD, cut],
            erecv.at[side * PAD : (side + 1) * PAD, cut],
            ex_s.at[2 * i + side], ex_r.at[2 * i + side], {"tensor": over},
        )

    for c in range(2):
        rows = slice(c * PAD, (c + 1) * PAD)
        hat, _ = normal(ex[rows, :])
        ea[rows, :] = (hat * egain[0:1] + eoff[0:1]).astype(BF16)
        limit = (VIS * wid[clips[c]]) // WIDE
        for g, shard in enumerate((lane, mate)):
            if c == 0 and g == 0:
                own[0].wait()
            if c == 0 and g == 1:
                enc_weight(0).wait_recv()
                for step in range(1, LANES):
                    bias_copy(step).wait_recv()
            if g == 0:
                bq, bv = bias[1:2, 0:half], bias[2:3, 0:half]
            else:
                bq, bv = biases[shard, 1:2, 0:half], biases[shard, 2:3, 0:half]
            eqkv[g, 0, rows] = (nt(ea[rows, :], w_qkv[g, 0]) + bq).astype(BF16)
            eqkv[g, 1, rows] = nt(ea[rows, :], w_qkv[g, 1]).astype(BF16)
            eqkv[g, 2, rows] = (nt(ea[rows, :], w_qkv[g, 2]) + bv).astype(BF16)
            p, out, _ = attend(
                eqkv[g, 0, rows], eqkv[g, 1, rows], eqkv[g, 2, rows], emarks, eones,
                lambda s: jnp.where(key < limit, s, floor), ENC_SCALE,
            )
            ep[g, c] = p
            eo[g, rows] = out
        if c == 0:
            own[1].wait()
            enc_weight(1).wait_recv()
        for i in range(blocks):
            cut = slice(i * 256, (i + 1) * 256)
            t = nn(eo[0, rows], w_proj[0, :, cut]) + nn(eo[1, rows], w_proj[1, :, cut])
            epart[rows, cut] = t
            esend[rows, cut] = t.astype(BF16)
            give_part(i, 1 - c).start()
    pass_on(0)
    own[2].wait()
    enc_weight(2).wait_recv()

    def give_last(i):
        cut = span(i, 256)
        return far(
            esend2.at[:, cut], erecv2.at[:, cut], ex2_s.at[i], ex2_r.at[i], {"tensor": over}
        )

    for c in (1, 0):
        rows = slice(c * PAD, (c + 1) * PAD)
        for i in range(blocks):
            give_part(i, c).wait_recv()
        t = ex[rows, :] + epart[rows, :] + erecv[rows, :].astype(F32) + eoff[2:3]
        ex1[rows, :] = t
        hat, _ = normal(t)
        eu[rows, :] = (hat * egain[1:2] + eoff[1:2]).astype(BF16)
        for g, shard in enumerate((lane, mate)):

            def enc_ff(i, g=g, shard=shard, rows=rows):
                cut = span(i, 256)
                h = nn(eu[rows, :], w_up[g, :, cut]) + biases[shard, 0:1, cut]
                act, slope = gelu_both(h)
                ey[g, rows, cut] = act.astype(BF16)
                egp[g, rows, cut] = slope.astype(BF16)

            loop(w_up.shape[2] // 256, enc_ff, unroll=3)
        if c == 1:
            own[3].wait()
            enc_weight(3).wait_recv()
        for i in range(blocks):
            cut = slice(i * 256, (i + 1) * 256)
            t = nn(ey[0, rows], w_down[0, :, cut]) + nn(ey[1, rows], w_down[1, :, cut])
            if c == 0:
                eown[:, cut] = t
            else:
                esend2[:, cut] = t.astype(BF16)
                give_last(i).start()
        if c == 1:
            for n in (1, 2, 3):
                dec_weight(n, 0).start()
            pass_last(0)
    outs = [
        pltpu.make_async_copy(src, dst, out_s.at[n])
        for n, (src, dst) in enumerate(
            (
                (ex.at[0:PAD, :], o_x), (ex1, o_x1), (ea, o_a), (eu, o_u), (ey, o_y), (egp, o_gp),
                (eqkv, o_qkv), (ep, o_p), (eo, o_o), (w_qkv.at[1], o_w), (w_proj.at[1], o_wproj),
                (w_up.at[1], o_wup), (w_down.at[1], o_wdown),
            )
        )
    ]
    for copy in outs:
        copy.start()
    for i in range(blocks):
        give_last(i).wait_recv()

    width = wid[clip]
    bits = jnp.where(width == WIDE, 3, 2)
    turn = shifts[0, clip] * width
    mod = GRID - 1
    spot = 0
    for i in range(order.shape[1]):
        spot = spot + jnp.where(order[0, i] == clip, i, 0)
    batch = spot // CM
    count = 0
    for i in range(order.shape[1]):
        count = count + jnp.where(batch == i // CM, wid[order[0, i]], 0)
    factor_rows = CM * GRID / (jnp.full((1, 1), count, jnp.int32) * GRID_ROWS).astype(F32)

    def slot_of(index):
        return (index - turn) & mod

    def code_of(slot):
        band = ((slot >> bits) + shifts[0, clip]) >> 2
        strip = ((slot & (width - 1)) + shifts[1, clip]) >> 2
        return band * 4 + strip

    e_ref[...] = (ex1[0:PAD, :] + eown[...] + erecv2[...].astype(F32) + eoff[3:4]).astype(BF16)
    vec = evec[...].astype(F32)
    m = (nn(e_ref[...], ew[...]) + vec[0:1]).astype(BF16)
    seen = vis[pl.ds(clip, 1), :]
    target = jnp.concatenate([(seen + turn) & mod, jnp.full((1, PAD - VIS), -1, jnp.int32)], 1)
    gain = dgains[...].astype(F32)
    offsets = doffs[...].astype(F32)

    def start(i):
        r = span(i, PAD)
        index = lax.broadcasted_iota(jnp.int32, (PAD, PAD), 0) + i * PAD
        column = lax.broadcasted_iota(jnp.int32, (PAD, PAD), 1)
        match = index == target
        oh = match.astype(F32).astype(BF16)
        hot[r, :] = oh
        hit = jnp.sum(match.astype(F32), -1, keepdims=True)
        grid = jnp.where(hit > 0, nn(oh, m), vec[1:2]).astype(BF16).astype(F32)
        slot = slot_of(index)
        by_row = ((slot >> bits) == column).astype(F32).astype(BF16)
        by_col = ((slot & (width - 1)) == column).astype(F32).astype(BF16)
        row_part = nn(by_row, table[0]) + nn(by_row, table[1])
        col_part = nn(by_col, table[0]) + nn(by_col, table[1])
        x = grid + jnp.concatenate([row_part, col_part], 1)
        x0[r, :] = x
        hat, _ = normal(x)
        a[r, :] = (hat * gain[0:1] + offsets[0:1]).astype(BF16)

    loop(GRID // PAD, start)
    arrived(0)

    def dec_bias(row, size):
        return jnp.concatenate([biases[k, row : row + 1, 0:size] for k in range(LANES)], 1)

    def project(i):
        r = span(i, 256)
        rows = a[r, :]
        acts[0, r, :] = (nn(rows, qkv[0]) + dec_bias(4, 128)).astype(BF16)
        acts[1, r, :] = nn(rows, qkv[1]).astype(BF16)
        acts[2, r, :] = (nn(rows, qkv[2]) + dec_bias(5, 128)).astype(BF16)

    loop(2, project)
    pass_on(1)
    pass_on(2)
    marks = head_marks(128, DEC_SIZE, BF16)
    marks32 = head_marks(128, DEC_SIZE, F32)
    dim = lax.broadcasted_iota(jnp.int32, (128, 1), 0)
    rows32 = [
        ((dim >= h * DEC_SIZE) & (dim < (h + 1) * DEC_SIZE)).astype(F32) for h in range(len(marks))
    ]

    ones = ones_per_head(PAD, marks)

    def attention(i):
        r = span(i, PAD)
        row_slot = slot_of(lax.broadcasted_iota(jnp.int32, (PAD, PAD), 0) + i * PAD)
        key_slot = slot_of(lax.broadcasted_iota(jnp.int32, (PAD, PAD), 1) + i * PAD)
        allowed = (code_of(row_slot) == code_of(key_slot)) & (key_slot < GRID_ROWS * width)
        for g in range(DD // 128):
            c = slice(g * 128, (g + 1) * 128)
            probs[i, :, g * 512 : (g + 1) * 512], o[r, c], inverse[r, c] = attend(
                acts[0, r, c], acts[1, r, c], acts[2, r, c], marks, ones,
                lambda s: jnp.where(allowed, s, NEG * LOG2E), DEC_SCALE,
            )

    loop(GRID // PAD, attention, unroll=2)
    pass_last(1)
    pass_last(2)
    pass_on(3)
    arrived(1)

    def mix(i):
        r = span(i, PAD)
        x = x0[r, :] + nn(o[r, :], proj[...]) + offsets[2:3]
        x1[r, :] = x
        hat, _ = normal(x)
        un = hat * gain[1:2] + offsets[1:2]
        u[r, :] = un.astype(BF16)
        ut[:, r] = jnp.transpose(un).astype(BF16)

    loop(GRID // PAD, mix)
    pass_last(3)
    arrived(2)

    def ff(i):
        k = lax.div(i, 4)
        side = lax.rem(lax.div(i, 2), 2)
        c = span(lax.div(i, 2), 256)
        r = span(lax.rem(i, 2), 256)
        h = nn(u[r, :], up[:, c]) + biases[k, 3:4, span(side, 256)]
        act, slope = gelu_both(h)
        y[r, c] = act.astype(BF16)
        gp[r, c] = slope.astype(BF16)

    loop(2 * up.shape[1] // 256, ff, unroll=2)
    arrived(3)
    fetch.wait()
    slot_col = slot_of(lax.broadcasted_iota(jnp.int32, (GRID, 1), 0))
    valid = (slot_col < GRID_ROWS * width).astype(F32)
    rolled = slot_of(lax.broadcasted_iota(jnp.int32, (GRID, GRID), 0))
    perm = (rolled == lax.broadcasted_iota(jnp.int32, (GRID, GRID), 1)).astype(F32).astype(BF16)

    def out(i):
        r = span(lax.rem(i, 2), 256)
        c = span(lax.div(i, 2), 256)
        acc[r, c] = nn(y[r, :], down[:, c])

    loop(4, out)
    full = ((acc[...] + x1[...] + offsets[3:4]) * valid).astype(BF16)
    turned = tn(full, perm).astype(BF16)
    for k in range(devices):
        dsend[k] = turned[k * dsend.shape[1] : (k + 1) * dsend.shape[1]]

    def decoded_copy(step):
        peer, spot = group_peer(step)
        return far(dsend.at[peer], dec_out.at[me], do_s.at[step], do_r.at[step], spot)

    for step in range(1, devices):
        decoded_copy(step).start()
    dec_out[me] = dsend[me]
    g = nn(perm, cot[...]) * valid * factor_rows
    g32[...] = g
    gb[...] = g.astype(BF16)
    gt[...] = jnp.transpose(g).astype(BF16)
    d_small[0:5, :] = jnp.zeros((5, DD), F32)
    d_small[5:6, :] = colsum(g)
    d_small[6:8, :] = jnp.zeros((2, DD), F32)

    def ff_back(shard):
        for side in range(2):
            c = span(2 * shard + side, 256)
            d_down = nn(gt[...], y[:, c]).astype(BF16)
            dh = nt(gb[...], down[c, :]) * gp[:, c].astype(F32)
            d_upb[:, c] = colsum(dh)
            du = dh.astype(BF16)
            gp[:, c] = du
            d_up = nn(ut[...], du).astype(BF16)
            for block in range(GRID // CH):
                rows = slice(block * CH, (block + 1) * CH)
                h, top, col = tile_of(4 * block + side)
                buf[shard, h, top : top + CH, col : col + 256] = d_up[rows]
                h, top, col = tile_of(4 * block + 2 + side)
                buf[shard, h, top : top + CH, col : col + 256] = d_down[rows]

    def early_core(which):
        shard, land = ((mate, e_rc), (cross, e_rcy))[which]
        return far(
            buf.at[shard, :, 0:EARLY_ROWS, :], land, e_s.at[which], e_r.at[which], {"tensor": mate}
        )

    def early_y():
        return far(
            buf.at[over, :, 0:EARLY_ROWS, :], e_ry, e_s.at[2], e_r.at[2], {"tensor": over}
        )

    loop(2, lambda i: ff_back(jnp.where(i == 0, mate, cross)))
    early_core(1).start()
    early_core(0).start()
    loop(2, lambda i: ff_back(jnp.where(i == 0, over, lane)))
    early_core(1).wait_recv()

    def early_add(shard, land):
        def body(i):
            r = span(i, CH)
            buf[shard, :, r, :] = buf[shard, :, r, :] + land[:, r, :]

        loop(EARLY_ROWS // CH, body)

    early_add(over, e_rcy)
    early_y().start()

    def ff_in(i):
        r = span(lax.rem(i, 2), 256)
        c = span(lax.div(i, 2), 256)
        acc[r, c] = nt(gp[r, :], up[c, :])

    loop(4, ff_in)

    def mix_back(i):
        r = span(i, PAD)
        hat, scale = normal(x1[r, :])
        da = acc[r, :]
        dx = g32[r, :] + normal_back(da, hat, scale, gain[1:2])
        d_small[1:2, :] += colsum(da * hat)
        d_small[3:4, :] += colsum(da)
        d_small[4:5, :] += colsum(dx)
        g32[r, :] = dx
        dxb = dx.astype(BF16)
        gb[r, :] = dxb
        u[r, :] = nt(dxb, proj[...]).astype(BF16)

    loop(GRID // PAD, mix_back)
    early_core(0).wait_recv()
    early_add(lane, e_rc)
    d_proj = tn(o[...], gb[...]).astype(BF16)
    for block in range(GRID // CH):
        h, top, col = tile_of(33 + 2 * block)
        side = slice(block // 2 * 128, (block // 2 + 1) * 128)
        for k in range(LANES):
            row = k * 128 + block % 2 * CH
            buf[k, h, top : top + CH, col + 128 : col + 256] = d_proj[row : row + CH, side]

    def attention_back(i):
        r = span(i, PAD)
        for k in range(DD // 128):
            c = slice(k * 128, (k + 1) * 128)
            acts[0, r, c], acts[1, r, c], acts[2, r, c] = attend_back(
                acts[0, r, c], acts[1, r, c], acts[2, r, c],
                probs[i, :, k * 512 : (k + 1) * 512], o[r, c], inverse[r, c], u[r, c],
                marks, marks32, rows32, ones, DEC_SCALE,
            )

    loop(GRID // PAD, attention_back, unroll=2)
    d_qvb[0:1, :] = colsum(acts[0].astype(F32))
    d_qvb[1:2, :] = colsum(acts[2].astype(F32))

    def project_back(i):
        r = span(lax.rem(i, 2), 256)
        c = span(lax.div(i, 2), 256)
        acc[r, c] = (
            nt(acts[0, r, :], qkv[0, c, :])
            + nt(acts[1, r, :], qkv[1, c, :])
            + nt(acts[2, r, :], qkv[2, c, :])
        )

    loop(4, project_back)
    gt[...] = jnp.transpose(a[...].astype(F32)).astype(BF16)
    for j in range(3):
        d_qkv = nn(gt[...], acts[j]).astype(BF16)
        for block in range(GRID // CH):
            h, top, col = tile_of(32 + 2 * block + j // 2)
            col = col + j % 2 * 128
            rows = slice(block * CH, (block + 1) * CH)
            for k in range(LANES):
                buf[k, h, top : top + CH, col : col + 128] = d_qkv[rows, k * 128 : (k + 1) * 128]

    def start_back(i):
        r = span(i, PAD)
        hat, scale = normal(x0[r, :])
        da = acc[r, :]
        dx = g32[r, :] + normal_back(da, hat, scale, gain[0:1])
        d_small[0:1, :] += colsum(da * hat)
        d_small[2:3, :] += colsum(da)
        dg = dx.astype(BF16)
        gb[r, :] = dg
        hit = jnp.sum(hot[r, :].astype(F32), -1, keepdims=True)
        d_small[7:8, :] += colsum(jnp.where(hit > 0, 0.0, dg.astype(F32)))

    loop(GRID // PAD, start_back)
    dm = tn(hot[...], gb[...])
    d_small[6:7, :] = colsum(dm)
    dmb = dm.astype(BF16)
    d_enc[...] = nt(dmb, ew[...]).astype(BF16)
    d_ew = tn(e_ref[...], dmb).astype(BF16)
    for k in range(LANES):
        for h in range(2):
            top = k * 192 + h * 64
            buf[k, h, 512:576, 0:512] = d_ew[top : top + 64]
            buf[k, h, 512:576, 512:768] = d_ew[k * 192 + 128 : (k + 1) * 192, h * 256 : (h + 1) * 256]

    early_y().wait_recv()
    early_add(lane, e_ry)
    later = pl.ds(EARLY_ROWS, DEC_ROWS - EARLY_ROWS)
    rest = [pltpu.make_async_copy(buf.at[lane], o_dec.at[lane], out_s.at[13])] + [
        pltpu.make_async_copy(buf.at[k, :, later, :], o_dec.at[k, :, later, :], out_s.at[14 + n])
        for n, k in enumerate((mate, over, cross))
    ]
    for copy in rest:
        copy.start()
    for copy in outs + rest:
        copy.wait()
    for which in range(2):
        early_core(which).wait_send()
    early_y().wait_send()
    for n in range(4):
        enc_weight(n).wait_send()
        for kind in range(5):
            dec_weight(n, kind).wait_send()
    for step in range(1, LANES):
        bias_copy(step).wait_send()
    for i in range(blocks):
        give_part(i, 0).wait_send()
        give_part(i, 1).wait_send()
        give_last(i).wait_send()
    for step in range(1, devices):
        decoded_copy(step).wait()


def forward_call(args, half, hid, dff):
    dma = lambda *s: pltpu.SemaphoreType.DMA(s)
    vm = lambda dtype, *shape: pltpu.VMEM(shape, dtype)
    rows = 2 * PAD
    keys = PAD * half // ENC_SIZE
    devices = 2 * LANES
    slab = DD // devices
    kept = [
        ((PAD, D), F32), ((rows, D), F32), ((rows, D), BF16), ((rows, D), BF16),
        ((2, rows, hid), BF16), ((2, rows, hid), BF16), ((2, 3, rows, half), BF16),
        ((2, 2, PAD, keys), BF16), ((2, rows, half), BF16),
        ((3, half, D), BF16), ((half, D), BF16), ((D, hid), BF16), ((hid, D), BF16),
        ((LANES, 2, DEC_ROWS, D), BF16),
    ]
    made = [
        ((PAD, D), BF16), ((2, DD), F32), ((1, dff), F32), ((8, DD), F32),
        ((devices, slab, GRID), BF16),
    ]
    return pl.pallas_call(
        forward_and_decoder,
        out_shape=[jax.ShapeDtypeStruct(s, d) for s, d in kept + made],
        in_specs=[SM, SM, SM] + [VM] * 8 + [ANY] * 9 + [VM] * 5,
        out_specs=[ANY] * len(kept) + [VM] * len(made),
        scratch_shapes=[
            vm(BF16, 2, 3, half, D), vm(BF16, 2, half, D), vm(BF16, 2, D, hid), vm(BF16, 2, hid, D),
            vm(F32, 8, D), vm(F32, LANES, 8, D),
            vm(BF16, 3, DD, DD), vm(BF16, DD, DD), vm(BF16, DD, dff), vm(BF16, dff, DD),
            vm(F32, rows, D), vm(BF16, rows, D), vm(BF16, rows, D), vm(BF16, 2, rows, hid),
            vm(BF16, 2, rows, hid), vm(BF16, 2, 3, rows, half), vm(BF16, 2, 2, PAD, keys),
            vm(BF16, 2, rows, half), vm(F32, rows, D), vm(F32, rows, D), vm(BF16, rows, D),
            vm(BF16, rows, D), vm(BF16, PAD, D), vm(BF16, PAD, D), vm(F32, PAD, D),
            vm(BF16, GRID, DD), vm(F32, GRID, DD), vm(F32, GRID, DD), vm(BF16, GRID, DD),
            vm(BF16, 3, GRID, DD), vm(BF16, GRID // PAD, PAD, DHEADS * PAD), vm(BF16, GRID, DD),
            vm(F32, GRID, DD),
            vm(BF16, GRID, DD), vm(BF16, DD, GRID), vm(BF16, GRID, dff), vm(BF16, GRID, dff),
            vm(F32, GRID, DD), vm(BF16, GRID, DD), vm(BF16, DD, GRID), vm(F32, GRID, DD),
            vm(BF16, PAD, D), vm(BF16, GRID, PAD), vm(BF16, LANES, 2, DEC_ROWS, D),
            vm(BF16, devices, slab, GRID), *[vm(BF16, 2, EARLY_ROWS, D)] * 3,
            dma(8), dma(17), pltpu.SemaphoreType.DMA, dma(4), dma(4), dma(LANES), dma(LANES),
            dma(20), dma(20), dma(6), dma(6), dma(3), dma(3), dma(devices), dma(devices),
            dma(3), dma(3),
        ],
        compiler_params=pltpu.CompilerParams(
            collective_id=0, has_side_effects=True, vmem_limit_bytes=VMEM_LIMIT
        ),
    )(*args)


def add(x, y):
    return x + y


def backward_and_sums(
    d_enc, gains,
    h_u, h_y, h_gp, h_down0, h_down1, h_up0, h_up1,
    h_x, h_x1, h_a, h_qkv, h_p, h_o, h_w0, h_w1, h_proj0, h_proj1,
    dec, dec_qvb, dec_upb, dec_small,
    out, emb, dx_out,
    gb, gt, ut, part, send, recv, du, gx, dx1, d_o, d_acts, own, send1, recv1, dx32, dx,
    d_upb, d_qvb, d_small,
    acc, yacc, enc_mate, rcy, ry, rx, zl, zr, xc, cl, cr, small32, small,
    u, y, gp, down0, down1, up0, up1, x, x1, a, qkv, p, o, w0, w1, proj0, proj1, fetch_s,
    load_s, ex_s, ex_r,
    core_s, core_r, corey_s, corey_r, y_s, y_r, x_s, x_r, z_s, zl_r, zr_r,
    bl_s, br_s, b_r, a_s, a_r, emb_s, emb_r, dx_s, dx_r,
):
    sec = lax.axis_index("section")
    lane = lax.axis_index("tensor")
    pos = lax.axis_index("dp")
    count = lax.axis_size("dp")
    mate = lane + 1 - 2 * lax.rem(lane, 2)
    over = lax.rem(lane + 2, LANES)
    cross = lax.rem(mate + 2, LANES)
    first = pos == 0
    last = pos == count - 1
    me = sec * LANES + lane
    devices = 2 * LANES

    def group_peer(step):
        peer = lax.rem(me + step, devices)
        return peer, {"section": lax.div(peer, LANES), "tensor": lax.rem(peer, LANES)}

    barrier = pltpu.get_barrier_semaphore()
    for step in range(1, devices):
        pl.semaphore_signal(barrier, inc=1, device_id_type=MESH, device_id=group_peer(step)[1])

    @pl.when(pos > 0)
    def _():
        pl.semaphore_signal(barrier, inc=1, device_id={"dp": pos - 1}, device_id_type=MESH)

    @pl.when(pos < count - 1)
    def _():
        pl.semaphore_signal(barrier, inc=1, device_id={"dp": pos + 1}, device_id_type=MESH)

    fetches = [
        pltpu.make_async_copy(src, dst, fetch_s.at[n])
        for n, (src, dst) in enumerate(
            (
                (h_u, u), (h_y, y), (h_gp, gp), (h_down0, down0), (h_down1, down1), (h_up0, up0),
                (h_up1, up1), (h_x, x), (h_x1, x1), (h_a, a), (h_qkv, qkv), (h_p, p), (h_o, o),
                (h_w0, w0), (h_w1, w1), (h_proj0, proj0), (h_proj1, proj1),
            )
        )
    ]
    for fetch in fetches:
        fetch.start()
    loads = [
        pltpu.make_async_copy(dec.at[lane], acc.at[:, 0:DEC_ROWS, :], load_s.at[0]),
        pltpu.make_async_copy(
            dec.at[over, :, EARLY_ROWS:DEC_ROWS, :], yacc.at[:, 0 : DEC_ROWS - EARLY_ROWS, :],
            load_s.at[1],
        ),
    ]
    for load in loads:
        load.start()
    small32[...] = jnp.zeros_like(small32)
    small[...] = jnp.zeros_like(small)
    d_small[...] = jnp.zeros_like(d_small)
    gb[0:PAD, :] = d_enc[...]
    ends = jnp.where(first, 0, 1) + jnp.where(last, 0, 1)
    pl.semaphore_wait(barrier, devices - 1 + ends)

    gain = gains[...].astype(F32)
    width = w0.shape[1]
    marks = head_marks(width, ENC_SIZE, BF16)
    marks32 = head_marks(width, ENC_SIZE, F32)
    ones = ones_per_head(PAD, marks)

    def rows(k, size=CH):
        return pl.ds(pl.multiple_of(k * size, size), size)

    def give_enc():
        return far(d_enc, gb.at[PAD : 2 * PAD, :], ex_s.at[0], ex_r.at[0], {"tensor": over})

    def give_part(i, half):
        cut = rows(i, 256)
        n = 1 + 2 * i + half
        return far(
            send.at[(1 - half) * PAD : (2 - half) * PAD, cut],
            recv.at[half * PAD : (half + 1) * PAD, cut],
            ex_s.at[n], ex_r.at[n], {"tensor": over},
        )

    def give_last(i):
        cut = rows(i, 256)
        return far(send1.at[:, cut], recv1.at[:, cut], ex_s.at[7 + i], ex_r.at[7 + i], {"tensor": over})

    def ff_back(g, i, down):
        c = rows(i, 256)
        d_down = nn(gt[...], y[g, :, c]).astype(BF16)
        dh = nt(gb[...], down[c, :]) * gp[g, :, c].astype(F32)
        d_upb[g, :, c] = colsum(dh)
        dub = dh.astype(BF16)
        du[g, :, c] = dub
        d_up = nn(ut[...], dub).astype(BF16)
        if g == 0:
            acc[1, A_TOP:B_TOP, c] = d_down
            acc[0, A_TOP:B_TOP, c] = d_up
        else:
            enc_mate[1, 0:ENC_A, c] = d_down
            enc_mate[0, 0:ENC_A, c] = d_up

    def ff_in(i):
        c = rows(i, 256)
        t = nt(du[0], up0[c, :]) + nt(du[1], up1[c, :])
        part[:, c] = t
        send[:, c] = t.astype(BF16)
        give_part(i, 0).start()
        give_part(i, 1).start()

    def norm_two(i):
        del i
        for fetch in fetches[7:]:
            fetch.wait()
        for k in range(D // 256):
            give_part(k, 0).wait_recv()
            give_part(k, 1).wait_recv()

        def body(j):
            r = rows(j, 64)
            da = part[r, :] + recv[r, :].astype(F32)
            hat, scale = normal(x1[r, :])
            g = gb[r, :].astype(F32)
            d = g + normal_back(da, hat, scale, gain[1:2])
            gx[r, :] = d.astype(BF16)
            dx1[r, :] = d

            @pl.when(j < 2)
            def _():
                d_small[1:2, :] += colsum(da * hat)
                d_small[3:4, :] += colsum(da)
                d_small[4:5, :] += colsum(d)
                d_small[5:6, :] += colsum(g)

        loop(2 * PAD // 64, body)

    def attention(g, proj):
        d_proj = tn(o[g], gx[...]).astype(BF16)
        if g == 0:
            acc[1, B_TOP + width : S_TOP, :] = d_proj
        else:
            enc_mate[1, ENC_A + width : ENC_A + 2 * width, :] = d_proj
        d_o[...] = nt(gx[...], proj[...]).astype(BF16)
        for c in range(2):
            r = slice(c * PAD, (c + 1) * PAD)
            dq, dk, dv = attend_back(
                qkv[g, 0, r], qkv[g, 1, r], qkv[g, 2, r], p[g, c], o[g, r], 1.0 / nn(p[g, c], ones),
                d_o[r, :], marks, marks32, None, ones, ENC_SCALE,
            )
            d_acts[g, 0, r] = dq
            d_acts[g, 1, r] = dk
            d_acts[g, 2, r] = dv
        d_qvb[g, 0:1, :] = colsum(d_acts[g, 0].astype(F32))
        d_qvb[g, 1:2, :] = colsum(d_acts[g, 2].astype(F32))

    def project_in(i):
        c = rows(i, 256)
        t = 0.0
        for g, w in enumerate((w0, w1)):
            for j in range(3):
                t += nn(d_acts[g, j], w[j, :, c])
        own[:, c] = t[:PAD]
        send1[:, c] = t[PAD:].astype(BF16)
        give_last(i).start()

    def project_grad(g):
        for j in range(3):
            row = (j % 2) * width
            d = tn(d_acts[g, j], a[...]).astype(BF16)
            if g == 0:
                acc[j // 2, B_TOP + row : B_TOP + row + width, :] = d
            else:
                enc_mate[j // 2, ENC_A + row : ENC_A + row + width, :] = d

    def norm_one(i):
        del i
        for k in range(D // 256):
            give_last(k).wait_recv()

        def body(j):
            r = rows(j, 64)
            da = own[r, :] + recv1[r, :].astype(F32)
            hat, scale = normal(x[r, :])
            d_small[0:1, :] += colsum(da * hat)
            d_small[2:3, :] += colsum(da)
            dx32[r, :] = dx1[r, :] + normal_back(da, hat, scale, gain[0:1])

        loop(PAD // 64, body)
        turned = jnp.transpose(dx32[...])
        cut = D // devices
        for k in range(devices):
            dx[k] = turned[k * cut : (k + 1) * cut, 0:VIS].astype(BF16)
        for r in range(LANES):
            small32[r, 0:1, 0:512] = dec_upb[:, r * 512 : (r + 1) * 512]
            small32[r, 1:2, 0:128] = dec_qvb[0:1, r * 128 : (r + 1) * 128]
            small32[r, 1:2, 128:256] = dec_qvb[1:2, r * 128 : (r + 1) * 128]
            small32[r, 8:16, 0:512] = dec_small[...]
            small32[r, 16:24, :] = d_small[...]
        for g, shard in enumerate((lane, mate)):
            small32[shard, 2:3, :] = d_upb[g]
            small32[shard, 3:4, 0:192] = d_qvb[g, 0:1]
            small32[shard, 3:4, 256:448] = d_qvb[g, 1:2]
        for r in range(LANES):
            small[r, 0, 0:32] = small32[r].astype(BF16)
        acc[:, S_TOP : S_TOP + CH, :] = small[lane]
        yacc[:, DEC_ROWS - EARLY_ROWS :, :] = small[over]
        core_copy(LATE, small.at[mate]).start()
        corey_copy(LATE, small.at[cross]).start()
        for step in range(1, devices):
            dx_copy(step).start()
        dx_out[me] = dx[me]

    def core_enc(lo, hi):
        def body(m):
            block = block_of(m)

            @pl.when((block >= lo) & (block < hi))
            def _():
                src = pl.ds(pl.multiple_of(block * CH - DEC_ROWS, CH), CH)
                core_copy(m, enc_mate.at[:, src, :]).start()

        loop(ALL_K, body)

    def first_piece(i):
        del i
        for fetch in fetches[:7]:
            fetch.wait()
        ut[...] = jnp.transpose(u[...].astype(F32)).astype(BF16)
        give_enc().wait_recv()
        gt[...] = jnp.transpose(gb[...].astype(F32)).astype(BF16)

    pieces = [(0, 1, first_piece)]
    for g, down in enumerate((down0, down1)):
        pieces.append((0, 3, lambda i, g=g, down=down: ff_back(g, i, down)))
    pieces.append((3, 4, lambda i: core_enc(DEC_K, DEC_K + ENC_A // CH)))
    pieces.append((3, 4, lambda i: loop(D // 256, ff_in)))
    pieces.append((6, 7, norm_two))
    for g, proj in enumerate((proj0, proj1)):
        pieces.append((7 + g, 8 + g, lambda i, g=g, proj=proj: attention(g, proj)))
    pieces.append((9, 10, lambda i: loop(D // 256, project_in)))
    for g in range(2):
        pieces.append((10 + g, 11 + g, lambda i, g=g: project_grad(g)))
    pieces.append((12, 13, lambda i: core_enc(DEC_K + ENC_A // CH, B_K)))
    pieces.append((13, 14, norm_one))

    def dx_copy(step):
        peer, place = group_peer(step)
        return far(dx.at[peer], dx_out.at[me], dx_s.at[step], dx_r.at[step], place)

    def emb_copy(step):
        return far(
            out.at[:, pl.ds(512, CH), :], emb.at[lane], emb_s.at[step], emb_r.at[step],
            {"tensor": lax.rem(lane + step, LANES)},
        )

    def block_of(m):
        even = lax.rem(m - EARLY, 2) == 0
        turn = jnp.where(even, DEC_K + lax.div(m - EARLY, 2), EARLY + lax.div(m - EARLY - 1, 2))
        late = jnp.where(m == LATE, ALL_K - 1, jnp.where(m > LATE, m - 1, m))
        return jnp.where(m < EARLY, m, jnp.where(m >= MIXED, late, turn))

    def is_dec(m):
        return (block_of(m) < DEC_K) & (m >= EARLY)

    def with_y(m):
        return is_dec(m) | (m == LATE)

    def at(m):
        return pl.ds(pl.multiple_of(block_of(m) * CH, CH), CH)

    def pair_at(m):
        return rows(jnp.where(m < HALVED, lax.div(m, 2), m - HALVED // 2))

    def y_at(m):
        return rows(jnp.minimum(block_of(m), DEC_K) - EARLY)

    def core_copy(m, src):
        return far(src, out.at[:, at(m), :], core_s.at[m], core_r.at[m], {"tensor": mate})

    def corey_copy(m, src):
        return far(src, rcy.at[:, y_at(m), :], corey_s.at[m], corey_r.at[m], {"tensor": mate})

    def y_copy(m):
        cut = y_at(m)
        return far(
            yacc.at[:, cut, :], ry.at[:, cut, :], y_s.at[m], y_r.at[m], {"tensor": over}
        )

    def x_copy(m):
        return far(
            acc.at[1 - sec, at(m), :], rx.at[pair_at(m), :], x_s.at[m], x_r.at[m],
            {"section": 1 - sec},
        )

    def xc_copy(m):
        return far(
            acc.at[:, at(m), :], xc.at[:, pair_at(m), :], x_s.at[m], x_r.at[m],
            {"section": 1 - sec},
        )

    def z_copy(m, whole, right):
        if whole:
            src, dst = acc.at[:, at(m), :], (cl if right else cr).at[:, pair_at(m), :]
        else:
            src, dst = acc.at[sec, at(m), :], (zl if right else zr).at[pair_at(m), :]
        landed = zl_r if right else zr_r
        return far(src, dst, z_s.at[m], landed.at[m], {"dp": pos + 1 if right else pos - 1})

    def b_copy(m, whole, right):
        place = out.at[:, at(m), :] if whole else out.at[sec, at(m), :]
        sent = br_s if right else bl_s
        return far(place, place, sent.at[m], b_r.at[m], {"dp": pos + 1 if right else pos - 1})

    def a_copy(m):
        place = out.at[sec, at(m), :]
        return far(place, place, a_s.at[m], a_r.at[m], {"section": 1 - sec})

    def a_wait(m):
        place = out.at[1 - sec, at(m), :]
        far(place, place, a_s.at[m], a_r.at[m], {"section": 1 - sec}).wait_recv()

    give_enc().start()

    def start_core(m):
        @pl.when(is_dec(m))
        def _():
            core_copy(m, dec.at[mate, :, at(m), :]).start()
            corey_copy(m, dec.at[cross, :, at(m), :]).start()

    loop(MIXED, start_core)
    for load in loads:
        load.wait()

    def stage_c(m):
        @pl.when(m >= EARLY)
        def _():
            core_copy(m, out.at[:, at(m), :]).wait_recv()
            acc[:, at(m), :] = add(acc[:, at(m), :], out[:, at(m), :])

        @pl.when(with_y(m))
        def _():
            corey_copy(m, rcy.at[:, y_at(m), :]).wait_recv()
            yacc[:, y_at(m), :] = add(yacc[:, y_at(m), :], rcy[:, y_at(m), :])
            y_copy(m).start()

    def finished(m):
        @pl.when(block_of(m) == DEC_K - 1)
        def _():
            for step in range(1, LANES):
                emb_copy(step).start()
            emb[lane] = out[:, 512 : 512 + CH, :]

    def line_of(root, whole):
        left = pos < root
        right = pos > root
        here = pos == root
        reach = max(root, count - 1 - root)
        level = jnp.where(left, pos, jnp.where(right, count - 1 - pos, reach))
        dist = jnp.where(left, root - pos, pos - root)

        def view(ref, m):
            return ref.at[:, at(m), :] if whole else ref.at[sec, at(m), :]

        def landed(ref, m):
            return ref.at[:, pair_at(m), :] if whole else ref.at[pair_at(m), :]

        from_left, from_right = (cl, cr) if whole else (zl, zr)

        def outer(m):
            @pl.when(left & first)
            def _():
                z_copy(m, whole, True).start()

            @pl.when(right & last)
            def _():
                z_copy(m, whole, False).start()

        def inward(m):
            @pl.when(left & (pos > 0))
            def _():
                z_copy(m, whole, True).wait_recv()
                view(acc, m)[...] = add(view(acc, m)[...], landed(from_left, m)[...])
                z_copy(m, whole, True).start()

            @pl.when(right & (pos < count - 1))
            def _():
                z_copy(m, whole, False).wait_recv()
                view(acc, m)[...] = add(view(acc, m)[...], landed(from_right, m)[...])
                z_copy(m, whole, False).start()

            @pl.when(here)
            def _():
                total = view(acc, m)[...].astype(F32)
                if root > 0:
                    z_copy(m, whole, True).wait_recv()
                    total = total + landed(from_left, m)[...].astype(F32)
                if root < count - 1:
                    z_copy(m, whole, False).wait_recv()
                    total = total + landed(from_right, m)[...].astype(F32)
                if whole:
                    view(acc, m)[...] = total.astype(BF16)
                    xc_copy(m).start()
                else:
                    view(out, m)[...] = total.astype(BF16)
                    spread(m)
                    a_copy(m).start()

        def spread(m):
            if root > 0:
                b_copy(m, whole, False).start()
            if root < count - 1:
                b_copy(m, whole, True).start()

        def crossed(m):
            xc_copy(m).wait_recv()
            view(out, m)[...] = add(view(acc, m)[...], landed(xc, m)[...])
            spread(m)
            finished(m)

        def outward(m):
            b_copy(m, whole, False).wait_recv()

            @pl.when(left & (pos > 0))
            def _():
                b_copy(m, whole, False).start()

            @pl.when(right & (pos < count - 1))
            def _():
                b_copy(m, whole, True).start()

            if whole:
                finished(m)
            else:
                a_copy(m).start()

        def sent(m):
            @pl.when(jnp.logical_not(here))
            def _():
                z_copy(m, whole, True).wait_send()

            @pl.when((pos <= root) & (pos > 0))
            def _():
                b_copy(m, whole, False).wait_send()

            @pl.when((pos >= root) & (pos < count - 1))
            def _():
                b_copy(m, whole, True).wait_send()

            if whole:
                @pl.when(here)
                def _():
                    xc_copy(m).wait_send()
            else:
                x_copy(m).wait_send()
                a_copy(m).wait_send()

        def add_y(m):
            @pl.when(with_y(m))
            def _():
                y_copy(m).wait_recv()
                acc[:, at(m), :] = add(acc[:, at(m), :], ry[:, y_at(m), :])

            set_off(m)

        def set_off(m):
            if whole:
                outer(m)
            else:
                x_copy(m).start()

        def add_x(m):
            x_copy(m).wait_recv()
            acc[sec, at(m), :] = add(acc[sec, at(m), :], rx[pair_at(m), :])
            outer(m)

        def last_half(m):
            a_wait(m)
            finished(m)

        base = 1 if whole else 2
        back = base + reach + dist + (1 if whole else 0)
        steps = [(back, jnp.logical_not(here), outward), (base + level, level > 0, inward)]
        if whole:
            steps.append((base + reach + 1, here, crossed))
        else:
            steps += [(back + 1, True, last_half), (2, True, add_x)]
        return steps, sent, add_y, set_off

    low_root = (count - 1) // 2
    high_root = min(low_root + 1, count - 1)
    lines = [
        (lambda m: (lax.rem(m, 2) == 1) | (m >= HALVED), *line_of(low_root, False)),
        (lambda m: (lax.rem(m, 4) == 0) & (m < HALVED), *line_of(low_root, True)),
        (lambda m: (lax.rem(m, 4) == 2) & (m < HALVED), *line_of(high_root, True)),
    ]

    def tick(n):
        @pl.when(n < LATE)
        def _():
            for low, high, piece in pieces:
                @pl.when((n >= low) & (n < high))
                def _(low=low, piece=piece):
                    piece(n - low)

        for mine, steps, _, add_y, _ in lines:
            m = n - LAG

            @pl.when((m >= EARLY) & (m < ALL_K) & mine(m))
            def _(m=m, add_y=add_y):
                add_y(m)

            for offset, enabled, stage in steps:
                m = n - LAG * offset

                @pl.when((m >= 0) & (m < ALL_K) & mine(m) & enabled)
                def _(m=m, stage=stage):
                    stage(m)

        @pl.when(n < ALL_K)
        def _():
            stage_c(n)

    def set_off_early(m):
        for mine, _, _, _, set_off in lines:
            @pl.when(mine(m))
            def _(set_off=set_off):
                set_off(m)

    loop(EARLY, set_off_early)
    far_reach = max(low_root, count - 1 - low_root, high_root, count - 1 - high_root)
    loop(ALL_K + LAG * (3 + 2 * far_reach) + 1, tick)

    def finish(m):
        @pl.when(m >= EARLY)
        def _():
            core_copy(m, out.at[:, at(m), :]).wait_send()

        @pl.when(with_y(m))
        def _():
            corey_copy(m, rcy.at[:, y_at(m), :]).wait_send()
            y_copy(m).wait_send()

        for mine, _, sent, _, _ in lines:
            @pl.when(mine(m))
            def _(sent=sent):
                sent(m)

    loop(ALL_K, finish)
    for step in range(1, devices):
        dx_copy(step).wait()
    for step in range(1, LANES):
        emb_copy(step).wait()
    give_enc().wait_send()
    for k in range(D // 256):
        give_part(k, 0).wait_send()
        give_part(k, 1).wait_send()
        give_last(k).wait_send()


def backward_call(args, half, hid):
    dma = lambda *s: pltpu.SemaphoreType.DMA(s)
    vm = pltpu.VMEM
    full = ALL_K * CH
    y_half = DEC_ROWS - EARLY_ROWS + CH
    whole = HALVED // 2 * CH
    by_half = full - whole
    k = ALL_K
    rows = 2 * PAD
    cut = D // (2 * LANES)
    specs = [VM, VM] + [ANY] * 18 + [VM] * 3
    return pl.pallas_call(
        backward_and_sums,
        out_shape=[
            jax.ShapeDtypeStruct((2, full, D), BF16),
            jax.ShapeDtypeStruct((LANES, 2, CH, D), BF16),
            jax.ShapeDtypeStruct((2 * LANES, cut, VIS), BF16),
        ],
        in_specs=specs,
        out_specs=[VM] * 3,
        scratch_shapes=[
            vm((rows, D), BF16), vm((D, rows), BF16), vm((D, rows), BF16),
            vm((rows, D), F32), vm((rows, D), BF16), vm((rows, D), BF16),
            vm((2, rows, hid), BF16), vm((rows, D), BF16), vm((rows, D), F32),
            vm((rows, half), BF16), vm((2, 3, rows, half), BF16),
            vm((PAD, D), F32), vm((PAD, D), BF16), vm((PAD, D), BF16), vm((PAD, D), F32),
            vm((2 * LANES, cut, VIS), BF16),
            vm((2, 1, hid), F32), vm((2, 2, half), F32), vm((8, D), F32),
            vm((2, full, D), BF16), vm((2, y_half, D), BF16), vm((2, ENC_A + ENC_B, D), BF16),
            vm((2, y_half, D), BF16), vm((2, y_half, D), BF16),
            vm((by_half, D), BF16), vm((by_half, D), BF16), vm((by_half, D), BF16),
            vm((2, whole, D), BF16), vm((2, whole, D), BF16), vm((2, whole, D), BF16),
            vm((LANES, 32, D), F32), vm((LANES, 2, CH, D), BF16),
            *[vm(v.shape, v.dtype) for v in args[2:19]], dma(17), dma(2), dma(10), dma(10),
            dma(k), dma(k), dma(k), dma(k), dma(k), dma(k),
            dma(k), dma(k), dma(k), dma(k), dma(k),
            dma(k), dma(k), dma(k), dma(k), dma(k), dma(LANES), dma(LANES),
            dma(2 * LANES), dma(2 * LANES),
        ],
        compiler_params=pltpu.CompilerParams(
            collective_id=1, has_side_effects=True, vmem_limit_bytes=VMEM_LIMIT
        ),
    )(*args)


def finish_grads(
    total, emb, decoded, dx, decoded_out, dx_out,
    e_qkv, e_qvb, e_proj, e_up, e_upb, e_down, e_gain, e_off,
    d_qkv, d_qvb, d_proj, d_up, d_upb, d_down, d_gain, d_off, d_ew, d_ev,
):
    half = e_proj.shape[0]
    decoded_out[...] = decoded[...]
    dx_out[...] = dx[...]
    e_up[...] = total[0, A_TOP:B_TOP, :].astype(F32)
    e_down[...] = jnp.transpose(total[1, A_TOP:B_TOP, :].astype(F32))
    e_qkv[0] = total[0, B_TOP : B_TOP + half, :].astype(F32)
    e_qkv[1] = total[0, B_TOP + half : S_TOP, :].astype(F32)
    e_qkv[2] = total[1, B_TOP : B_TOP + half, :].astype(F32)
    e_proj[...] = total[1, B_TOP + half : S_TOP, :].astype(F32)

    def tile(number):
        h, top, col = tile_of(number)
        return total[h, top : top + CH, col : col + 256].astype(F32)

    for block in range(GRID // CH):
        rows = slice(block * CH, (block + 1) * CH)
        side = slice(block // 2 * 128, (block // 2 + 1) * 128)
        for k in range(2):
            d_up[rows, k * 256 : (k + 1) * 256] = tile(4 * block + k)
            if block % 2:
                both = jnp.concatenate([tile(4 * block - 2 + k), tile(4 * block + 2 + k)], 0)
                d_down[k * 256 : (k + 1) * 256, side] = jnp.transpose(both)
        one, two = tile(32 + 2 * block), tile(33 + 2 * block)
        d_qkv[0, rows, :] = one[:, 0:128]
        d_qkv[1, rows, :] = one[:, 128:256]
        d_qkv[2, rows, :] = two[:, 0:128]
        d_proj[block % 2 * CH : (block % 2 + 1) * CH, side] = two[:, 128:256]
    for k in range(LANES):
        for h in range(2):
            top = k * 192 + h * 64
            d_ew[top : top + 64, :] = emb[k, h, :, 0:512].astype(F32)
            d_ew[k * 192 + 128 : (k + 1) * 192, h * 256 : (h + 1) * 256] = emb[
                k, h, :, 512:768
            ].astype(F32)
    little = total[0, S_TOP : S_TOP + 32, :].astype(F32)
    d_upb[...] = little[0, 0:512]
    d_qvb[0:1, :] = little[1:2, 0:128]
    d_qvb[1:2, :] = little[1:2, 128:256]
    e_upb[...] = little[2]
    e_qvb[0:1, :] = little[3:4, 0:192]
    e_qvb[1:2, :] = little[3:4, 256:448]
    d_gain[...] = little[8:10, 0:512]
    d_off[...] = little[10:14, 0:512]
    d_ev[...] = little[14:16, 0:512]
    e_gain[...] = little[16:18]
    e_off[...] = little[18:22]


def call(kernel, specs, shapes, scratch, args):
    return pl.pallas_call(
        kernel,
        out_shape=[jax.ShapeDtypeStruct(s, d) for s, d in shapes],
        in_specs=specs,
        out_specs=[VM] * len(shapes),
        scratch_shapes=scratch,
        compiler_params=pltpu.CompilerParams(vmem_limit_bytes=VMEM_LIMIT),
    )(*args)


def position_rows():
    quarter = DD // 4
    freq = np.exp(np.arange(quarter, dtype=np.float32) * np.float32(-math.log(10000.0) / quarter))
    angle = np.arange(PAD, dtype=np.float32)[:, None] * freq[None, :].astype(np.float32)
    both = np.concatenate([np.sin(angle), np.cos(angle)], 1).astype(np.float32)
    high = both.astype(jnp.bfloat16)
    low = (both - high.astype(np.float32)).astype(jnp.bfloat16)
    return np.stack([high, low])


def per_device(
    patches, cotangent, widths, visible, window_shift, batch_order,
    encoder_qkv, encoder_qvbias, encoder_proj, encoder_up, encoder_upbias, encoder_down,
    encoder_gains, encoder_offsets,
    decoder_qkv, decoder_qvbias, decoder_proj, decoder_up, decoder_upbias, decoder_down,
    decoder_gains, decoder_offsets, embed_weight, embed_vectors,
):
    qkv0 = encoder_qkv.transpose(1, 2, 0)
    half = qkv0.shape[1]
    hid = encoder_up.shape[1]
    dff = decoder_up.shape[1] * LANES
    flat = patches.transpose(1, 0, 2).reshape(-1, D)
    (
        x, x1, a, u, y, gp, qkv, p, o, qkv1, proj1, up1, down1, dec_buf,
        d_enc, d_dqvb, d_dupb, d_dsmall, out_all,
    ) = forward_call(
        (
            widths, window_shift.T, batch_order, visible, flat, encoder_gains, encoder_offsets,
            encoder_qvbias, encoder_upbias, decoder_qvbias, decoder_upbias,
            qkv0, encoder_proj, encoder_up, encoder_down,
            decoder_qkv.transpose(1, 0, 2), decoder_proj, decoder_up, decoder_down,
            cotangent, embed_weight, embed_vectors, jnp.asarray(position_rows()),
            decoder_gains, decoder_offsets,
        ),
        half, hid, dff,
    )
    total, emb, dx_all = backward_call(
        (
            d_enc, encoder_gains, u, y, gp, encoder_down, down1, encoder_up, up1,
            x, x1, a, qkv, p, o, qkv0, qkv1, encoder_proj, proj1,
            dec_buf, d_dqvb, d_dupb, d_dsmall,
        ),
        half, hid,
    )
    f = lambda *shape: (shape, F32)
    out_all, dx_all, *grads = call(
        finish_grads, [VM] * 4,
        [
            (out_all.shape, BF16), (dx_all.shape, BF16), f(3, half, D), f(2, half), f(half, D), f(D, hid), f(hid), f(hid, D), f(2, D), f(4, D),
            f(3, DD, 128), f(2, 128), f(128, DD), f(DD, 512), f(512), f(512, DD), f(2, DD), f(4, DD),
            f(D, DD), f(2, DD),
        ],
        [], (total, emb, out_all, dx_all),
    )
    grads[0] = grads[0].transpose(2, 0, 1)
    grads[8] = grads[8].transpose(1, 0, 2)
    return (out_all.swapaxes(1, 2), dx_all.swapaxes(1, 2), *grads)


def solution(mesh):
    weights = (
        P(None, None, "tensor"), P(None, "tensor"), P("tensor", None), P(None, "tensor"),
        P("tensor"), P("tensor", None), P(), P(),
    )
    split = P("dp", None, ("section", "tensor"))
    return jax.shard_map(
        per_device,
        mesh=mesh,
        in_specs=(
            P("dp", None, None), P("dp", None, None), P("dp"), P("dp", None), P("dp", None),
            P("dp", None),
        ) + weights + weights + (P(), P()),
        out_specs=(split, split) + weights + weights + (P(), P()),
        check_vma=False,
    )
```

```python
import math

import jax
import jax.numpy as jnp
import numpy as np
from jax import lax
from jax.experimental import pallas as pl
from jax.experimental.pallas import tpu as pltpu
from jax.sharding import PartitionSpec as P

D = 768
HEADS = 12
DD = 512
DHEADS = 16
GRID_ROWS = 64
WIDE = 8
WIN = 4
VIS = 102
CM = 4
GRID = 512
LANES = 4
PAD = 128
EPS = 1e-06
NEG = -10000.0
F32 = jnp.float32
BF16 = jnp.bfloat16
VMEM_LIMIT = 60 * 1024 * 1024

VM = pl.BlockSpec(memory_space=pltpu.VMEM)
SM = pl.BlockSpec(memory_space=pltpu.SMEM)
ANY = pl.BlockSpec(memory_space=pl.ANY)


def nn(a, b):
    return lax.dot_general(a, b, (((1,), (0,)), ((), ())), preferred_element_type=F32)


def nt(a, b):
    return lax.dot_general(a, b, (((1,), (1,)), ((), ())), preferred_element_type=F32)


def tn(a, b):
    return lax.dot_general(a, b, (((0,), (0,)), ((), ())), preferred_element_type=F32)


def loop(count, body, unroll=1):
    def step(i, carry):
        body(i)
        return carry

    lax.fori_loop(0, count, step, 0, unroll=unroll)


def span(i, size):
    return pl.ds(pl.multiple_of(i * size, size), size)


def normal(x):
    center = x - jnp.mean(x, -1, keepdims=True)
    scale = lax.rsqrt(jnp.mean(center * center, -1, keepdims=True) + EPS)
    return center * scale, scale


def normal_back(dy, hat, scale, gain):
    d = dy * gain
    return scale * (
        d - jnp.mean(d, -1, keepdims=True) - hat * jnp.mean(d * hat, -1, keepdims=True)
    )


def gelu_both(h):
    phi = 0.5 * lax.erf(h * math.sqrt(0.5)) + 0.5
    bell = jnp.exp2(h * h * (-0.5 * math.log2(math.e)))
    return h * phi, phi + h * bell * (1.0 / math.sqrt(2.0 * math.pi))


def colsum(x):
    return jnp.sum(x, 0, keepdims=True)


def head_marks(width, size, dtype):
    lane = lax.broadcasted_iota(jnp.int32, (1, width), 1)
    return [((lane >= h * size) & (lane < (h + 1) * size)).astype(dtype) for h in range(width // size)]


def stacked(x, marks):
    return jnp.concatenate([x * m for m in marks], 0)


LOG2E = math.log2(math.e)


def attend(q, k, v, marks, ones, masked, scale):
    keys = k.shape[0]
    s = nt(q, stacked(k, marks))
    parts = []
    for h in range(len(marks)):
        x = masked(s[:, h * keys : (h + 1) * keys] * (scale * LOG2E))
        parts.append(jnp.exp2(x - jnp.max(x, -1, keepdims=True)).astype(BF16))
    e = jnp.concatenate(parts, 1)
    width = q.shape[1]
    if width % 128:
        top, total = nn(e, stacked(v, marks)), nn(e, ones)
    else:
        both = nn(e, jnp.concatenate([stacked(v, marks), ones], 1))
        top, total = both[:, :width], both[:, width:]
    inverse = 1.0 / total
    return e, (top * inverse).astype(BF16), inverse


def attend_back(q, k, v, e, o, inverse, d_out, marks, marks32, rows32, ones, scale):
    keys = k.shape[0]
    width = q.shape[1]
    d_one = d_out.astype(F32) * inverse
    d_two = (d_one * o.astype(F32)).astype(BF16)
    d_one = d_one.astype(BF16)
    if width % 128:
        d_s = nt(d_one, stacked(v, marks)) - nt(d_two, ones)
    else:
        d_s = nt(
            jnp.concatenate([d_one, d_two], 1), jnp.concatenate([stacked(v, marks), -ones], 1)
        )
    dr = (e.astype(F32) * d_s * scale).astype(BF16)
    d_q = nn(dr, stacked(k, marks)).astype(BF16)
    if width % 128:
        d_k_all, d_v_all = tn(dr, q), tn(e, d_one)
        d_k = d_v = 0.0
        for h in range(len(marks)):
            cut = slice(h * keys, (h + 1) * keys)
            d_k += d_k_all[cut] * marks32[h]
            d_v += d_v_all[cut] * marks32[h]
        return d_q, d_k.astype(BF16), d_v.astype(BF16)
    d_k_all = nn(jnp.transpose(q.astype(F32)).astype(BF16), dr)
    d_v_all = nn(jnp.transpose(d_one.astype(F32)).astype(BF16), e)
    d_k = d_v = 0.0
    for h in range(len(marks)):
        cut = slice(h * keys, (h + 1) * keys)
        d_k += d_k_all[:, cut] * rows32[h]
        d_v += d_v_all[:, cut] * rows32[h]
    return d_q, jnp.transpose(d_k).astype(BF16), jnp.transpose(d_v).astype(BF16)


def ones_per_head(keys, marks):
    return jnp.concatenate([jnp.broadcast_to(m, (keys, m.shape[1])) for m in marks], 0)


ENC_SIZE = D // HEADS
ENC_SCALE = ENC_SIZE ** -0.5
DEC_SIZE = DD // DHEADS
DEC_SCALE = DEC_SIZE ** -0.5


CH = 64
DEC_ROWS = 576
ENC_A = 768
ENC_B = 384
DEC_K = DEC_ROWS // CH
B_K = (DEC_ROWS + ENC_A + ENC_B) // CH
ALL_K = B_K + 1
A_TOP = DEC_ROWS
B_TOP = DEC_ROWS + ENC_A
S_TOP = B_TOP + ENC_B
EARLY = 4
EARLY_ROWS = EARLY * CH
LAG = 2
MIXED = EARLY + 2 * (DEC_K - EARLY)
WAIT = 2
LATE = 16
HALVED = ALL_K - 4


def tile_of(number):
    place = number // 3
    return place % 2, place // 2 * CH, number % 3 * 256


MESH = pl.DeviceIdType.MESH


def far(src, dst, send, recv, peer):
    return pltpu.make_async_remote_copy(
        src_ref=src, dst_ref=dst, send_sem=send, recv_sem=recv, device_id=peer, device_id_type=MESH
    )


def forward_and_decoder(
    wid, shifts, order, vis, pat, gains, offs, b_qv, b_up, b_dqv, b_dup,
    h_qkv, h_proj, h_up, h_down, h_dqkv, h_dproj, h_dup, h_ddown,
    cot_hbm, ew, evec, table, dgains, doffs,
    o_x, o_x1, o_a, o_u, o_y, o_gp, o_qkv, o_p, o_o, o_w, o_wproj, o_wup, o_wdown, o_dec,
    d_enc, d_qvb, d_upb, d_small, dec_out,
    w_qkv, w_proj, w_up, w_down, bias, biases, qkv, proj, up, down,
    ex, ea, eu, ey, egp, eqkv, ep, eo, ex1, epart, esend, erecv, esend2, erecv2, eown,
    cot, x0, x1, a, acts, probs, o, inverse, u, ut, y, gp, g32, gb, gt, acc, e_ref, hot, buf, dsend, e_rc, e_rcy, e_ry,
    load_s, out_s, cot_s, w_s, w_r, bias_s, bias_r, dw_s, dw_r, ex_s, ex_r, ex2_s, ex2_r, do_s, do_r, e_s, e_r,
):
    sec = lax.axis_index("section")
    lane = lax.axis_index("tensor")
    mate = lane + 1 - 2 * lax.rem(lane, 2)
    over = lax.rem(lane + 2, LANES)
    cross = lax.rem(mate + 2, LANES)
    me = sec * LANES + lane
    devices = 2 * LANES
    clip = me
    clips = (me, sec * LANES + over)

    def group_peer(step):
        peer = lax.rem(me + step, devices)
        return peer, {"section": lax.div(peer, LANES), "tensor": lax.rem(peer, LANES)}

    own = [
        pltpu.make_async_copy(src, dst.at[0], load_s.at[n])
        for n, (src, dst) in enumerate(
            ((h_qkv, w_qkv), (h_proj, w_proj), (h_up, w_up), (h_down, w_down))
        )
    ]

    def place(n, shard, part=None):
        thick = (128, 128, 512, 512)[n]
        base = shard * thick
        cut = pl.ds(pl.multiple_of(base, thick), thick)
        if part is None:
            return (qkv.at[:, :, cut], proj.at[cut, :], up.at[:, cut], down.at[cut, :])[n]
        some = span(part, (256, 64, 256, 256)[n])
        if n == 0:
            return qkv.at[:, some, cut]
        if n == 2:
            return up.at[some, cut]
        few = thick // 2
        rows = pl.ds(pl.multiple_of(base + part * few, few), few)
        return (proj if n == 1 else down).at[rows, :]

    shards = (h_dqkv, h_dproj, h_dup, h_ddown)
    keep = [
        pltpu.make_async_copy(shards[n], place(n, lane), load_s.at[4 + n]) for n in range(4)
    ]
    for copy in own + keep:
        copy.start()
    fetch = pltpu.make_async_copy(cot_hbm.at[clip], cot, cot_s)
    fetch.start()

    barrier = pltpu.get_barrier_semaphore()
    for step in range(1, devices):
        pl.semaphore_signal(barrier, inc=1, device_id_type=MESH, device_id=group_peer(step)[1])
    bias[...] = jnp.zeros_like(bias)
    half = w_proj.shape[1]
    bias[0:1, :] = b_up[...].astype(F32).reshape(1, -1)
    bias[1:3, 0:half] = b_qv[...].astype(F32)
    bias[3:4, 0:512] = b_dup[...].astype(F32).reshape(1, -1)
    bias[4:6, 0:128] = b_dqv[...].astype(F32)
    biases[lane] = bias[...]
    pl.semaphore_wait(barrier, devices - 1)

    def enc_weight(n):
        src = (h_qkv, h_proj, h_up, h_down)[n]
        dst = (w_qkv, w_proj, w_up, w_down)[n]
        return far(src, dst.at[1], w_s.at[n], w_r.at[n], {"tensor": mate})

    def bias_copy(step):
        return far(
            bias, biases.at[lane], bias_s.at[step], bias_r.at[step],
            {"tensor": lax.rem(lane + step, LANES)},
        )

    def half_of(n):
        some = span(sec, (256, 64, 256, 256)[n])
        return shards[n].at[:, some, :] if n == 0 else shards[n].at[some, :]

    def dec_weight(n, kind):
        peer = {"section": 1 - sec} if kind == 2 else {"tensor": over if kind == 0 else mate}
        if kind == 0:
            src, dst = half_of(n), place(n, lane, sec)
        elif kind == 1:
            src, dst = shards[n], place(n, lane)
        else:
            src = dst = place(n, over, 1 - sec if kind == 4 else sec)
        return far(src, dst, dw_s.at[5 * n + kind], dw_r.at[5 * n + kind], peer)

    enc_weight(0).start()
    for step in range(1, LANES):
        bias_copy(step).start()
    enc_weight(1).start()
    dec_weight(0, 0).start()
    enc_weight(2).start()
    enc_weight(3).start()
    for n in range(4):
        dec_weight(n, 1).start()

    def pass_on(n):
        dec_weight(n, 0).wait_recv()
        dec_weight(n, 2).start()
        dec_weight(n, 3).start()

    def pass_last(n):
        dec_weight(n, 2).wait_recv()
        dec_weight(n, 4).start()

    def arrived(n):
        keep[n].wait()
        dec_weight(n, 1).wait_recv()
        dec_weight(n, 3).wait_recv()
        dec_weight(n, 4).wait_recv()

    egain = gains[...].astype(F32)
    eoff = offs[...].astype(F32)
    stride = pat.shape[0] // VIS
    for c in range(2):
        row = lax.broadcasted_iota(jnp.int32, (PAD, pat.shape[0]), 0)
        col = lax.broadcasted_iota(jnp.int32, (PAD, pat.shape[0]), 1)
        pick = (col == row * stride + clips[c]).astype(F32).astype(BF16)
        ex[c * PAD : (c + 1) * PAD, :] = nn(pick, pat[...])

    emarks = head_marks(half, ENC_SIZE, BF16)
    key = lax.broadcasted_iota(jnp.int32, (PAD, PAD), 1)
    floor = jnp.where(key < VIS, NEG * LOG2E, -1e30)
    eones = ones_per_head(PAD, emarks)
    blocks = D // 256

    def give_part(i, side):
        cut = span(i, 256)
        return far(
            esend.at[(1 - side) * PAD : (2 - side) * PAD, cut],
            erecv.at[side * PAD : (side + 1) * PAD, cut],
            ex_s.at[2 * i + side], ex_r.at[2 * i + side], {"tensor": over},
        )

    for c in range(2):
        rows = slice(c * PAD, (c + 1) * PAD)
        hat, _ = normal(ex[rows, :])
        ea[rows, :] = (hat * egain[0:1] + eoff[0:1]).astype(BF16)
        limit = (VIS * wid[clips[c]]) // WIDE
        for g, shard in enumerate((lane, mate)):
            if c == 0 and g == 0:
                own[0].wait()
            if c == 0 and g == 1:
                enc_weight(0).wait_recv()
                for step in range(1, LANES):
                    bias_copy(step).wait_recv()
            if g == 0:
                bq, bv = bias[1:2, 0:half], bias[2:3, 0:half]
            else:
                bq, bv = biases[shard, 1:2, 0:half], biases[shard, 2:3, 0:half]
            eqkv[g, 0, rows] = (nt(ea[rows, :], w_qkv[g, 0]) + bq).astype(BF16)
            eqkv[g, 1, rows] = nt(ea[rows, :], w_qkv[g, 1]).astype(BF16)
            eqkv[g, 2, rows] = (nt(ea[rows, :], w_qkv[g, 2]) + bv).astype(BF16)
            p, out, _ = attend(
                eqkv[g, 0, rows], eqkv[g, 1, rows], eqkv[g, 2, rows], emarks, eones,
                lambda s: jnp.where(key < limit, s, floor), ENC_SCALE,
            )
            ep[g, c] = p
            eo[g, rows] = out
        if c == 0:
            own[1].wait()
            enc_weight(1).wait_recv()
        for i in range(blocks):
            cut = slice(i * 256, (i + 1) * 256)
            t = nn(eo[0, rows], w_proj[0, :, cut]) + nn(eo[1, rows], w_proj[1, :, cut])
            epart[rows, cut] = t
            esend[rows, cut] = t.astype(BF16)
            give_part(i, 1 - c).start()
    pass_on(0)
    own[2].wait()
    enc_weight(2).wait_recv()

    def give_last(i):
        cut = span(i, 256)
        return far(
            esend2.at[:, cut], erecv2.at[:, cut], ex2_s.at[i], ex2_r.at[i], {"tensor": over}
        )

    for c in (1, 0):
        rows = slice(c * PAD, (c + 1) * PAD)
        for i in range(blocks):
            give_part(i, c).wait_recv()
        t = ex[rows, :] + epart[rows, :] + erecv[rows, :].astype(F32) + eoff[2:3]
        ex1[rows, :] = t
        hat, _ = normal(t)
        eu[rows, :] = (hat * egain[1:2] + eoff[1:2]).astype(BF16)
        for g, shard in enumerate((lane, mate)):

            def enc_ff(i, g=g, shard=shard, rows=rows):
                cut = span(i, 256)
                h = nn(eu[rows, :], w_up[g, :, cut]) + biases[shard, 0:1, cut]
                act, slope = gelu_both(h)
                ey[g, rows, cut] = act.astype(BF16)
                egp[g, rows, cut] = slope.astype(BF16)

            loop(w_up.shape[2] // 256, enc_ff, unroll=3)
        if c == 1:
            own[3].wait()
            enc_weight(3).wait_recv()
        for i in range(blocks):
            cut = slice(i * 256, (i + 1) * 256)
            t = nn(ey[0, rows], w_down[0, :, cut]) + nn(ey[1, rows], w_down[1, :, cut])
            if c == 0:
                eown[:, cut] = t
            else:
                esend2[:, cut] = t.astype(BF16)
                give_last(i).start()
        if c == 1:
            for n in (1, 2, 3):
                dec_weight(n, 0).start()
            pass_last(0)
    outs = [
        pltpu.make_async_copy(src, dst, out_s.at[n])
        for n, (src, dst) in enumerate(
            (
                (ex.at[0:PAD, :], o_x), (ex1, o_x1), (ea, o_a), (eu, o_u), (ey, o_y), (egp, o_gp),
                (eqkv, o_qkv), (ep, o_p), (eo, o_o), (w_qkv.at[1], o_w), (w_proj.at[1], o_wproj),
                (w_up.at[1], o_wup), (w_down.at[1], o_wdown),
            )
        )
    ]
    for copy in outs:
        copy.start()
    for i in range(blocks):
        give_last(i).wait_recv()

    width = wid[clip]
    bits = jnp.where(width == WIDE, 3, 2)
    turn = shifts[0, clip] * width
    mod = GRID - 1
    spot = 0
    for i in range(order.shape[1]):
        spot = spot + jnp.where(order[0, i] == clip, i, 0)
    batch = spot // CM
    count = 0
    for i in range(order.shape[1]):
        count = count + jnp.where(batch == i // CM, wid[order[0, i]], 0)
    factor_rows = CM * GRID / (jnp.full((1, 1), count, jnp.int32) * GRID_ROWS).astype(F32)

    def slot_of(index):
        return (index - turn) & mod

    def code_of(slot):
        band = ((slot >> bits) + shifts[0, clip]) >> 2
        strip = ((slot & (width - 1)) + shifts[1, clip]) >> 2
        return band * 4 + strip

    e_ref[...] = (ex1[0:PAD, :] + eown[...] + erecv2[...].astype(F32) + eoff[3:4]).astype(BF16)
    vec = evec[...].astype(F32)
    m = (nn(e_ref[...], ew[...]) + vec[0:1]).astype(BF16)
    seen = vis[pl.ds(clip, 1), :]
    target = jnp.concatenate([(seen + turn) & mod, jnp.full((1, PAD - VIS), -1, jnp.int32)], 1)
    gain = dgains[...].astype(F32)
    offsets = doffs[...].astype(F32)

    def start(i):
        r = span(i, PAD)
        index = lax.broadcasted_iota(jnp.int32, (PAD, PAD), 0) + i * PAD
        column = lax.broadcasted_iota(jnp.int32, (PAD, PAD), 1)
        match = index == target
        oh = match.astype(F32).astype(BF16)
        hot[r, :] = oh
        hit = jnp.sum(match.astype(F32), -1, keepdims=True)
        grid = jnp.where(hit > 0, nn(oh, m), vec[1:2]).astype(BF16).astype(F32)
        slot = slot_of(index)
        by_row = ((slot >> bits) == column).astype(F32).astype(BF16)
        by_col = ((slot & (width - 1)) == column).astype(F32).astype(BF16)
        row_part = nn(by_row, table[0]) + nn(by_row, table[1])
        col_part = nn(by_col, table[0]) + nn(by_col, table[1])
        x = grid + jnp.concatenate([row_part, col_part], 1)
        x0[r, :] = x
        hat, _ = normal(x)
        a[r, :] = (hat * gain[0:1] + offsets[0:1]).astype(BF16)

    loop(GRID // PAD, start)
    arrived(0)

    def dec_bias(row, size):
        return jnp.concatenate([biases[k, row : row + 1, 0:size] for k in range(LANES)], 1)

    def project(i):
        r = span(i, 256)
        rows = a[r, :]
        acts[0, r, :] = (nn(rows, qkv[0]) + dec_bias(4, 128)).astype(BF16)
        acts[1, r, :] = nn(rows, qkv[1]).astype(BF16)
        acts[2, r, :] = (nn(rows, qkv[2]) + dec_bias(5, 128)).astype(BF16)

    loop(2, project)
    pass_on(1)
    pass_on(2)
    marks = head_marks(128, DEC_SIZE, BF16)
    marks32 = head_marks(128, DEC_SIZE, F32)
    dim = lax.broadcasted_iota(jnp.int32, (128, 1), 0)
    rows32 = [
        ((dim >= h * DEC_SIZE) & (dim < (h + 1) * DEC_SIZE)).astype(F32) for h in range(len(marks))
    ]

    ones = ones_per_head(PAD, marks)

    def attention(i):
        r = span(i, PAD)
        row_slot = slot_of(lax.broadcasted_iota(jnp.int32, (PAD, PAD), 0) + i * PAD)
        key_slot = slot_of(lax.broadcasted_iota(jnp.int32, (PAD, PAD), 1) + i * PAD)
        allowed = (code_of(row_slot) == code_of(key_slot)) & (key_slot < GRID_ROWS * width)
        for g in range(DD // 128):
            c = slice(g * 128, (g + 1) * 128)
            probs[i, :, g * 512 : (g + 1) * 512], o[r, c], inverse[r, c] = attend(
                acts[0, r, c], acts[1, r, c], acts[2, r, c], marks, ones,
                lambda s: jnp.where(allowed, s, NEG * LOG2E), DEC_SCALE,
            )

    loop(GRID // PAD, attention, unroll=2)
    pass_last(1)
    pass_last(2)
    pass_on(3)
    arrived(1)

    def mix(i):
        r = span(i, PAD)
        x = x0[r, :] + nn(o[r, :], proj[...]) + offsets[2:3]
        x1[r, :] = x
        hat, _ = normal(x)
        un = hat * gain[1:2] + offsets[1:2]
        u[r, :] = un.astype(BF16)
        ut[:, r] = jnp.transpose(un).astype(BF16)

    loop(GRID // PAD, mix)
    pass_last(3)
    arrived(2)

    def ff(i):
        k = lax.div(i, 4)
        side = lax.rem(lax.div(i, 2), 2)
        c = span(lax.div(i, 2), 256)
        r = span(lax.rem(i, 2), 256)
        h = nn(u[r, :], up[:, c]) + biases[k, 3:4, span(side, 256)]
        act, slope = gelu_both(h)
        y[r, c] = act.astype(BF16)
        gp[r, c] = slope.astype(BF16)

    loop(2 * up.shape[1] // 256, ff, unroll=2)
    arrived(3)
    fetch.wait()
    slot_col = slot_of(lax.broadcasted_iota(jnp.int32, (GRID, 1), 0))
    valid = (slot_col < GRID_ROWS * width).astype(F32)
    rolled = slot_of(lax.broadcasted_iota(jnp.int32, (GRID, GRID), 0))
    perm = (rolled == lax.broadcasted_iota(jnp.int32, (GRID, GRID), 1)).astype(F32).astype(BF16)

    def out(i):
        r = span(lax.rem(i, 2), 256)
        c = span(lax.div(i, 2), 256)
        acc[r, c] = nn(y[r, :], down[:, c])

    loop(4, out)
    full = ((acc[...] + x1[...] + offsets[3:4]) * valid).astype(BF16)
    turned = tn(full, perm).astype(BF16)
    for k in range(devices):
        dsend[k] = turned[k * dsend.shape[1] : (k + 1) * dsend.shape[1]]

    def decoded_copy(step):
        peer, spot = group_peer(step)
        return far(dsend.at[peer], dec_out.at[me], do_s.at[step], do_r.at[step], spot)

    for step in range(1, devices):
        decoded_copy(step).start()
    dec_out[me] = dsend[me]
    g = nn(perm, cot[...]) * valid * factor_rows
    g32[...] = g
    gb[...] = g.astype(BF16)
    gt[...] = jnp.transpose(g).astype(BF16)
    d_small[0:5, :] = jnp.zeros((5, DD), F32)
    d_small[5:6, :] = colsum(g)
    d_small[6:8, :] = jnp.zeros((2, DD), F32)

    def ff_back(shard):
        for side in range(2):
            c = span(2 * shard + side, 256)
            d_down = nn(gt[...], y[:, c]).astype(BF16)
            dh = nt(gb[...], down[c, :]) * gp[:, c].astype(F32)
            d_upb[:, c] = colsum(dh)
            du = dh.astype(BF16)
            gp[:, c] = du
            d_up = nn(ut[...], du).astype(BF16)
            for block in range(GRID // CH):
                rows = slice(block * CH, (block + 1) * CH)
                h, top, col = tile_of(4 * block + side)
                buf[shard, h, top : top + CH, col : col + 256] = d_up[rows]
                h, top, col = tile_of(4 * block + 2 + side)
                buf[shard, h, top : top + CH, col : col + 256] = d_down[rows]

    def early_core(which):
        shard, land = ((mate, e_rc), (cross, e_rcy))[which]
        return far(
            buf.at[shard, :, 0:EARLY_ROWS, :], land, e_s.at[which], e_r.at[which], {"tensor": mate}
        )

    def early_y():
        return far(
            buf.at[over, :, 0:EARLY_ROWS, :], e_ry, e_s.at[2], e_r.at[2], {"tensor": over}
        )

    def early_add(shard, land):
        def body(i):
            r = span(i, CH)
            buf[shard, :, r, :] = buf[shard, :, r, :] + land[:, r, :]

        loop(EARLY_ROWS // CH, body)

    def ff_step(i):
        ff_back(jnp.where(i == 0, cross, jnp.where(i == 1, over, jnp.where(i == 2, mate, lane))))

        @pl.when(i == 1)
        def _():
            early_core(1).start()

        @pl.when(i == 2)
        def _():
            early_core(0).start()
            early_core(1).wait_recv()
            early_add(over, e_rcy)
            early_y().start()

    loop(LANES, ff_step)

    def ff_in(i):
        r = span(lax.rem(i, 2), 256)
        c = span(lax.div(i, 2), 256)
        acc[r, c] = nt(gp[r, :], up[c, :])

    loop(4, ff_in)

    def mix_back(i):
        r = span(i, PAD)
        hat, scale = normal(x1[r, :])
        da = acc[r, :]
        dx = g32[r, :] + normal_back(da, hat, scale, gain[1:2])
        d_small[1:2, :] += colsum(da * hat)
        d_small[3:4, :] += colsum(da)
        d_small[4:5, :] += colsum(dx)
        g32[r, :] = dx
        dxb = dx.astype(BF16)
        gb[r, :] = dxb
        u[r, :] = nt(dxb, proj[...]).astype(BF16)

    loop(GRID // PAD, mix_back)
    early_core(0).wait_recv()
    early_add(lane, e_rc)
    d_proj = tn(o[...], gb[...]).astype(BF16)
    for block in range(GRID // CH):
        h, top, col = tile_of(33 + 2 * block)
        side = slice(block // 2 * 128, (block // 2 + 1) * 128)
        for k in range(LANES):
            row = k * 128 + block % 2 * CH
            buf[k, h, top : top + CH, col + 128 : col + 256] = d_proj[row : row + CH, side]

    def attention_back(i):
        r = span(i, PAD)
        for k in range(DD // 128):
            c = slice(k * 128, (k + 1) * 128)
            acts[0, r, c], acts[1, r, c], acts[2, r, c] = attend_back(
                acts[0, r, c], acts[1, r, c], acts[2, r, c],
                probs[i, :, k * 512 : (k + 1) * 512], o[r, c], inverse[r, c], u[r, c],
                marks, marks32, rows32, ones, DEC_SCALE,
            )

    loop(GRID // PAD, attention_back, unroll=2)
    d_qvb[0:1, :] = colsum(acts[0].astype(F32))
    d_qvb[1:2, :] = colsum(acts[2].astype(F32))

    def project_back(i):
        r = span(lax.rem(i, 2), 256)
        c = span(lax.div(i, 2), 256)
        acc[r, c] = (
            nt(acts[0, r, :], qkv[0, c, :])
            + nt(acts[1, r, :], qkv[1, c, :])
            + nt(acts[2, r, :], qkv[2, c, :])
        )

    loop(4, project_back)
    gt[...] = jnp.transpose(a[...].astype(F32)).astype(BF16)
    for j in range(3):
        d_qkv = nn(gt[...], acts[j]).astype(BF16)
        for block in range(GRID // CH):
            h, top, col = tile_of(32 + 2 * block + j // 2)
            col = col + j % 2 * 128
            rows = slice(block * CH, (block + 1) * CH)
            for k in range(LANES):
                buf[k, h, top : top + CH, col : col + 128] = d_qkv[rows, k * 128 : (k + 1) * 128]

    def start_back(i):
        r = span(i, PAD)
        hat, scale = normal(x0[r, :])
        da = acc[r, :]
        dx = g32[r, :] + normal_back(da, hat, scale, gain[0:1])
        d_small[0:1, :] += colsum(da * hat)
        d_small[2:3, :] += colsum(da)
        dg = dx.astype(BF16)
        gb[r, :] = dg
        hit = jnp.sum(hot[r, :].astype(F32), -1, keepdims=True)
        d_small[7:8, :] += colsum(jnp.where(hit > 0, 0.0, dg.astype(F32)))

    loop(GRID // PAD, start_back)
    dm = tn(hot[...], gb[...])
    d_small[6:7, :] = colsum(dm)
    dmb = dm.astype(BF16)
    d_enc[...] = nt(dmb, ew[...]).astype(BF16)
    d_ew = tn(e_ref[...], dmb).astype(BF16)
    for k in range(LANES):
        for h in range(2):
            top = k * 192 + h * 64
            buf[k, h, 512:576, 0:512] = d_ew[top : top + 64]
            buf[k, h, 512:576, 512:768] = d_ew[k * 192 + 128 : (k + 1) * 192, h * 256 : (h + 1) * 256]

    early_y().wait_recv()
    early_add(lane, e_ry)
    later = pl.ds(EARLY_ROWS, DEC_ROWS - EARLY_ROWS)
    rest = [pltpu.make_async_copy(buf.at[lane], o_dec.at[lane], out_s.at[13])] + [
        pltpu.make_async_copy(buf.at[k, :, later, :], o_dec.at[k, :, later, :], out_s.at[14 + n])
        for n, k in enumerate((mate, over, cross))
    ]
    for copy in rest:
        copy.start()
    for copy in outs + rest:
        copy.wait()
    for which in range(2):
        early_core(which).wait_send()
    early_y().wait_send()
    for n in range(4):
        enc_weight(n).wait_send()
        for kind in range(5):
            dec_weight(n, kind).wait_send()
    for step in range(1, LANES):
        bias_copy(step).wait_send()
    for i in range(blocks):
        give_part(i, 0).wait_send()
        give_part(i, 1).wait_send()
        give_last(i).wait_send()
    for step in range(1, devices):
        decoded_copy(step).wait()


def forward_call(args, half, hid, dff):
    dma = lambda *s: pltpu.SemaphoreType.DMA(s)
    vm = lambda dtype, *shape: pltpu.VMEM(shape, dtype)
    rows = 2 * PAD
    keys = PAD * half // ENC_SIZE
    devices = 2 * LANES
    slab = DD // devices
    kept = [
        ((PAD, D), F32), ((rows, D), F32), ((rows, D), BF16), ((rows, D), BF16),
        ((2, rows, hid), BF16), ((2, rows, hid), BF16), ((2, 3, rows, half), BF16),
        ((2, 2, PAD, keys), BF16), ((2, rows, half), BF16),
        ((3, half, D), BF16), ((half, D), BF16), ((D, hid), BF16), ((hid, D), BF16),
        ((LANES, 2, DEC_ROWS, D), BF16),
    ]
    made = [
        ((PAD, D), BF16), ((2, DD), F32), ((1, dff), F32), ((8, DD), F32),
        ((devices, slab, GRID), BF16),
    ]
    return pl.pallas_call(
        forward_and_decoder,
        out_shape=[jax.ShapeDtypeStruct(s, d) for s, d in kept + made],
        in_specs=[SM, SM, SM] + [VM] * 8 + [ANY] * 9 + [VM] * 5,
        out_specs=[ANY] * len(kept) + [VM] * len(made),
        scratch_shapes=[
            vm(BF16, 2, 3, half, D), vm(BF16, 2, half, D), vm(BF16, 2, D, hid), vm(BF16, 2, hid, D),
            vm(F32, 8, D), vm(F32, LANES, 8, D),
            vm(BF16, 3, DD, DD), vm(BF16, DD, DD), vm(BF16, DD, dff), vm(BF16, dff, DD),
            vm(F32, rows, D), vm(BF16, rows, D), vm(BF16, rows, D), vm(BF16, 2, rows, hid),
            vm(BF16, 2, rows, hid), vm(BF16, 2, 3, rows, half), vm(BF16, 2, 2, PAD, keys),
            vm(BF16, 2, rows, half), vm(F32, rows, D), vm(F32, rows, D), vm(BF16, rows, D),
            vm(BF16, rows, D), vm(BF16, PAD, D), vm(BF16, PAD, D), vm(F32, PAD, D),
            vm(BF16, GRID, DD), vm(F32, GRID, DD), vm(F32, GRID, DD), vm(BF16, GRID, DD),
            vm(BF16, 3, GRID, DD), vm(BF16, GRID // PAD, PAD, DHEADS * PAD), vm(BF16, GRID, DD),
            vm(F32, GRID, DD),
            vm(BF16, GRID, DD), vm(BF16, DD, GRID), vm(BF16, GRID, dff), vm(BF16, GRID, dff),
            vm(F32, GRID, DD), vm(BF16, GRID, DD), vm(BF16, DD, GRID), vm(F32, GRID, DD),
            vm(BF16, PAD, D), vm(BF16, GRID, PAD), vm(BF16, LANES, 2, DEC_ROWS, D),
            vm(BF16, devices, slab, GRID), *[vm(BF16, 2, EARLY_ROWS, D)] * 3,
            dma(8), dma(17), pltpu.SemaphoreType.DMA, dma(4), dma(4), dma(LANES), dma(LANES),
            dma(20), dma(20), dma(6), dma(6), dma(3), dma(3), dma(devices), dma(devices),
            dma(3), dma(3),
        ],
        compiler_params=pltpu.CompilerParams(
            collective_id=0, has_side_effects=True, vmem_limit_bytes=VMEM_LIMIT
        ),
    )(*args)


def add(x, y):
    return x + y


def backward_and_sums(
    d_enc, gains,
    h_u, h_y, h_gp, h_down0, h_down1, h_up0, h_up1,
    h_x, h_x1, h_a, h_qkv, h_p, h_o, h_w0, h_w1, h_proj0, h_proj1,
    dec, dec_qvb, dec_upb, dec_small,
    out, emb, dx_out,
    gb, gt, ut, part, send, recv, du, gx, dx1, d_o, d_acts, own, send1, recv1, dx32, dx,
    d_upb, d_qvb, d_small,
    acc, yacc, enc_mate, rcy, ry, rx, zl, zr, xc, cl, cr, small32, small,
    u, y, gp, down0, down1, up0, up1, x, x1, a, qkv, p, o, w0, w1, proj0, proj1, fetch_s,
    load_s, ex_s, ex_r,
    core_s, core_r, corey_s, corey_r, y_s, y_r, x_s, x_r, z_s, zl_r, zr_r,
    bl_s, br_s, b_r, a_s, a_r, emb_s, emb_r, dx_s, dx_r,
):
    sec = lax.axis_index("section")
    lane = lax.axis_index("tensor")
    pos = lax.axis_index("dp")
    count = lax.axis_size("dp")
    mate = lane + 1 - 2 * lax.rem(lane, 2)
    over = lax.rem(lane + 2, LANES)
    cross = lax.rem(mate + 2, LANES)
    first = pos == 0
    last = pos == count - 1
    me = sec * LANES + lane
    devices = 2 * LANES

    def group_peer(step):
        peer = lax.rem(me + step, devices)
        return peer, {"section": lax.div(peer, LANES), "tensor": lax.rem(peer, LANES)}

    barrier = pltpu.get_barrier_semaphore()
    for step in range(1, devices):
        pl.semaphore_signal(barrier, inc=1, device_id_type=MESH, device_id=group_peer(step)[1])

    @pl.when(pos > 0)
    def _():
        pl.semaphore_signal(barrier, inc=1, device_id={"dp": pos - 1}, device_id_type=MESH)

    @pl.when(pos < count - 1)
    def _():
        pl.semaphore_signal(barrier, inc=1, device_id={"dp": pos + 1}, device_id_type=MESH)

    fetches = [
        pltpu.make_async_copy(src, dst, fetch_s.at[n])
        for n, (src, dst) in enumerate(
            (
                (h_u, u), (h_y, y), (h_gp, gp), (h_down0, down0), (h_down1, down1), (h_up0, up0),
                (h_up1, up1), (h_x, x), (h_x1, x1), (h_a, a), (h_qkv, qkv), (h_p, p), (h_o, o),
                (h_w0, w0), (h_w1, w1), (h_proj0, proj0), (h_proj1, proj1),
            )
        )
    ]
    for fetch in fetches:
        fetch.start()
    loads = [
        pltpu.make_async_copy(dec.at[lane], acc.at[:, 0:DEC_ROWS, :], load_s.at[0]),
        pltpu.make_async_copy(
            dec.at[over, :, EARLY_ROWS:DEC_ROWS, :], yacc.at[:, 0 : DEC_ROWS - EARLY_ROWS, :],
            load_s.at[1],
        ),
    ]
    for load in loads:
        load.start()
    small32[...] = jnp.zeros_like(small32)
    small[...] = jnp.zeros_like(small)
    d_small[...] = jnp.zeros_like(d_small)
    gb[0:PAD, :] = d_enc[...]
    ends = jnp.where(first, 0, 1) + jnp.where(last, 0, 1)
    pl.semaphore_wait(barrier, devices - 1 + ends)

    gain = gains[...].astype(F32)
    width = w0.shape[1]
    marks = head_marks(width, ENC_SIZE, BF16)
    marks32 = head_marks(width, ENC_SIZE, F32)
    ones = ones_per_head(PAD, marks)

    def rows(k, size=CH):
        return pl.ds(pl.multiple_of(k * size, size), size)

    def give_enc():
        return far(d_enc, gb.at[PAD : 2 * PAD, :], ex_s.at[0], ex_r.at[0], {"tensor": over})

    def give_part(i, half):
        cut = rows(i, 256)
        n = 1 + 2 * i + half
        return far(
            send.at[(1 - half) * PAD : (2 - half) * PAD, cut],
            recv.at[half * PAD : (half + 1) * PAD, cut],
            ex_s.at[n], ex_r.at[n], {"tensor": over},
        )

    def give_last(i):
        cut = rows(i, 256)
        return far(send1.at[:, cut], recv1.at[:, cut], ex_s.at[7 + i], ex_r.at[7 + i], {"tensor": over})

    def ff_back(g, i, down):
        c = rows(i, 256)
        d_down = nn(gt[...], y[g, :, c]).astype(BF16)
        dh = nt(gb[...], down[c, :]) * gp[g, :, c].astype(F32)
        d_upb[g, :, c] = colsum(dh)
        dub = dh.astype(BF16)
        du[g, :, c] = dub
        d_up = nn(ut[...], dub).astype(BF16)
        if g == 0:
            acc[1, A_TOP:B_TOP, c] = d_down
            acc[0, A_TOP:B_TOP, c] = d_up
        else:
            enc_mate[1, 0:ENC_A, c] = d_down
            enc_mate[0, 0:ENC_A, c] = d_up

    def ff_in(i):
        c = rows(i, 256)
        t = nt(du[0], up0[c, :]) + nt(du[1], up1[c, :])
        part[:, c] = t
        send[:, c] = t.astype(BF16)
        give_part(i, 0).start()
        give_part(i, 1).start()

    def norm_two(i):
        del i
        for fetch in fetches[7:]:
            fetch.wait()
        for k in range(D // 256):
            give_part(k, 0).wait_recv()
            give_part(k, 1).wait_recv()

        def body(j):
            r = rows(j, 64)
            da = part[r, :] + recv[r, :].astype(F32)
            hat, scale = normal(x1[r, :])
            g = gb[r, :].astype(F32)
            d = g + normal_back(da, hat, scale, gain[1:2])
            gx[r, :] = d.astype(BF16)
            dx1[r, :] = d

            @pl.when(j < 2)
            def _():
                d_small[1:2, :] += colsum(da * hat)
                d_small[3:4, :] += colsum(da)
                d_small[4:5, :] += colsum(d)
                d_small[5:6, :] += colsum(g)

        loop(2 * PAD // 64, body)

    def attention(g, proj):
        d_proj = tn(o[g], gx[...]).astype(BF16)
        if g == 0:
            acc[1, B_TOP + width : S_TOP, :] = d_proj
        else:
            enc_mate[1, ENC_A + width : ENC_A + 2 * width, :] = d_proj
        d_o[...] = nt(gx[...], proj[...]).astype(BF16)
        for c in range(2):
            r = slice(c * PAD, (c + 1) * PAD)
            dq, dk, dv = attend_back(
                qkv[g, 0, r], qkv[g, 1, r], qkv[g, 2, r], p[g, c], o[g, r], 1.0 / nn(p[g, c], ones),
                d_o[r, :], marks, marks32, None, ones, ENC_SCALE,
            )
            d_acts[g, 0, r] = dq
            d_acts[g, 1, r] = dk
            d_acts[g, 2, r] = dv
        d_qvb[g, 0:1, :] = colsum(d_acts[g, 0].astype(F32))
        d_qvb[g, 1:2, :] = colsum(d_acts[g, 2].astype(F32))

    def project_in(i):
        c = rows(i, 256)
        t = 0.0
        for g, w in enumerate((w0, w1)):
            for j in range(3):
                t += nn(d_acts[g, j], w[j, :, c])
        own[:, c] = t[:PAD]
        send1[:, c] = t[PAD:].astype(BF16)
        give_last(i).start()

    def project_grad(g):
        for j in range(3):
            row = (j % 2) * width
            d = tn(d_acts[g, j], a[...]).astype(BF16)
            if g == 0:
                acc[j // 2, B_TOP + row : B_TOP + row + width, :] = d
            else:
                enc_mate[j // 2, ENC_A + row : ENC_A + row + width, :] = d

    def norm_one(i):
        del i
        for k in range(D // 256):
            give_last(k).wait_recv()

        def body(j):
            r = rows(j, 64)
            da = own[r, :] + recv1[r, :].astype(F32)
            hat, scale = normal(x[r, :])
            d_small[0:1, :] += colsum(da * hat)
            d_small[2:3, :] += colsum(da)
            dx32[r, :] = dx1[r, :] + normal_back(da, hat, scale, gain[0:1])

        loop(PAD // 64, body)
        turned = jnp.transpose(dx32[...])
        cut = D // devices
        for k in range(devices):
            dx[k] = turned[k * cut : (k + 1) * cut, 0:VIS].astype(BF16)
        for r in range(LANES):
            small32[r, 0:1, 0:512] = dec_upb[:, r * 512 : (r + 1) * 512]
            small32[r, 1:2, 0:128] = dec_qvb[0:1, r * 128 : (r + 1) * 128]
            small32[r, 1:2, 128:256] = dec_qvb[1:2, r * 128 : (r + 1) * 128]
            small32[r, 8:16, 0:512] = dec_small[...]
            small32[r, 16:24, :] = d_small[...]
        for g, shard in enumerate((lane, mate)):
            small32[shard, 2:3, :] = d_upb[g]
            small32[shard, 3:4, 0:192] = d_qvb[g, 0:1]
            small32[shard, 3:4, 256:448] = d_qvb[g, 1:2]
        for r in range(LANES):
            small[r, 0, 0:32] = small32[r].astype(BF16)
        acc[:, S_TOP : S_TOP + CH, :] = small[lane]
        yacc[:, DEC_ROWS - EARLY_ROWS :, :] = small[over]
        core_copy(LATE, small.at[mate]).start()
        corey_copy(LATE, small.at[cross]).start()
        for step in range(1, devices):
            dx_copy(step).start()
        dx_out[me] = dx[me]

    def core_enc(lo, hi):
        def body(m):
            block = block_of(m)

            @pl.when((block >= lo) & (block < hi))
            def _():
                src = pl.ds(pl.multiple_of(block * CH - DEC_ROWS, CH), CH)
                core_copy(m, enc_mate.at[:, src, :]).start()

        loop(ALL_K, body)

    def first_piece(i):
        del i
        for fetch in fetches[:7]:
            fetch.wait()
        ut[...] = jnp.transpose(u[...].astype(F32)).astype(BF16)
        give_enc().wait_recv()
        gt[...] = jnp.transpose(gb[...].astype(F32)).astype(BF16)

    pieces = [(WAIT, WAIT + 1, first_piece)]
    for g, down in enumerate((down0, down1)):
        pieces.append((WAIT, WAIT + 3, lambda i, g=g, down=down: ff_back(g, i, down)))
    pieces.append((WAIT + 3, WAIT + 4, lambda i: core_enc(DEC_K, DEC_K + ENC_A // CH)))
    pieces.append((WAIT + 3, WAIT + 4, lambda i: loop(D // 256, ff_in)))
    pieces.append((WAIT + 6, WAIT + 7, norm_two))
    for g, proj in enumerate((proj0, proj1)):
        low = WAIT + 7 + g
        pieces.append((low, low + 1, lambda i, g=g, proj=proj: attention(g, proj)))
    pieces.append((WAIT + 9, WAIT + 10, lambda i: loop(D // 256, project_in)))
    for g in range(2):
        low = WAIT + 10 + g
        pieces.append((low, low + 1, lambda i, g=g: project_grad(g)))
    pieces.append((WAIT + 12, WAIT + 13, lambda i: core_enc(DEC_K + ENC_A // CH, B_K)))
    pieces.append((WAIT + 13, WAIT + 14, norm_one))

    def dx_copy(step):
        peer, place = group_peer(step)
        return far(dx.at[peer], dx_out.at[me], dx_s.at[step], dx_r.at[step], place)

    def emb_copy(step):
        return far(
            out.at[:, pl.ds(512, CH), :], emb.at[lane], emb_s.at[step], emb_r.at[step],
            {"tensor": lax.rem(lane + step, LANES)},
        )

    def block_of(m):
        even = lax.rem(m - EARLY, 2) == 0
        turn = jnp.where(even, EARLY + lax.div(m - EARLY, 2), DEC_K + lax.div(m - EARLY - 1, 2))
        late = jnp.where(m == LATE, ALL_K - 1, jnp.where(m > LATE, m - 1, m))
        return jnp.where(m < EARLY, m, jnp.where(m >= MIXED, late, turn))

    def is_dec(m):
        return (block_of(m) < DEC_K) & (m >= EARLY)

    def with_y(m):
        return is_dec(m) | (m == LATE)

    def at(m):
        return pl.ds(pl.multiple_of(block_of(m) * CH, CH), CH)

    def pair_at(m):
        return rows(jnp.where(m < HALVED, lax.div(m, 2), m - HALVED // 2))

    def y_at(m):
        return rows(jnp.minimum(block_of(m), DEC_K) - EARLY)

    def core_copy(m, src):
        return far(src, out.at[:, at(m), :], core_s.at[m], core_r.at[m], {"tensor": mate})

    def corey_copy(m, src):
        return far(src, rcy.at[:, y_at(m), :], corey_s.at[m], corey_r.at[m], {"tensor": mate})

    def y_copy(m):
        cut = y_at(m)
        return far(
            yacc.at[:, cut, :], ry.at[:, cut, :], y_s.at[m], y_r.at[m], {"tensor": over}
        )

    def x_copy(m):
        return far(
            acc.at[1 - sec, at(m), :], rx.at[pair_at(m), :], x_s.at[m], x_r.at[m],
            {"section": 1 - sec},
        )

    def xc_copy(m):
        return far(
            acc.at[:, at(m), :], xc.at[:, pair_at(m), :], x_s.at[m], x_r.at[m],
            {"section": 1 - sec},
        )

    def z_copy(m, whole, right):
        if whole:
            src, dst = acc.at[:, at(m), :], (cl if right else cr).at[:, pair_at(m), :]
        else:
            src, dst = acc.at[sec, at(m), :], (zl if right else zr).at[pair_at(m), :]
        landed = zl_r if right else zr_r
        return far(src, dst, z_s.at[m], landed.at[m], {"dp": pos + 1 if right else pos - 1})

    def b_copy(m, whole, right):
        place = out.at[:, at(m), :] if whole else out.at[sec, at(m), :]
        sent = br_s if right else bl_s
        return far(place, place, sent.at[m], b_r.at[m], {"dp": pos + 1 if right else pos - 1})

    def a_copy(m):
        place = out.at[sec, at(m), :]
        return far(place, place, a_s.at[m], a_r.at[m], {"section": 1 - sec})

    def a_wait(m):
        place = out.at[1 - sec, at(m), :]
        far(place, place, a_s.at[m], a_r.at[m], {"section": 1 - sec}).wait_recv()

    give_enc().start()

    def start_core(m):
        @pl.when(is_dec(m))
        def _():
            core_copy(m, dec.at[mate, :, at(m), :]).start()
            corey_copy(m, dec.at[cross, :, at(m), :]).start()

    loop(MIXED, start_core)
    for load in loads:
        load.wait()

    def stage_c(m):
        @pl.when(m >= EARLY)
        def _():
            core_copy(m, out.at[:, at(m), :]).wait_recv()
            acc[:, at(m), :] = add(acc[:, at(m), :], out[:, at(m), :])

        @pl.when(with_y(m))
        def _():
            corey_copy(m, rcy.at[:, y_at(m), :]).wait_recv()
            yacc[:, y_at(m), :] = add(yacc[:, y_at(m), :], rcy[:, y_at(m), :])
            y_copy(m).start()

    def finished(m):
        @pl.when(block_of(m) == DEC_K - 1)
        def _():
            for step in range(1, LANES):
                emb_copy(step).start()
            emb[lane] = out[:, 512 : 512 + CH, :]

    def line_of(root, whole):
        left = pos < root
        right = pos > root
        here = pos == root
        reach = max(root, count - 1 - root)
        level = jnp.where(left, pos, jnp.where(right, count - 1 - pos, reach))
        dist = jnp.where(left, root - pos, pos - root)

        def view(ref, m):
            return ref.at[:, at(m), :] if whole else ref.at[sec, at(m), :]

        def landed(ref, m):
            return ref.at[:, pair_at(m), :] if whole else ref.at[pair_at(m), :]

        from_left, from_right = (cl, cr) if whole else (zl, zr)

        def outer(m):
            @pl.when(left & first)
            def _():
                z_copy(m, whole, True).start()

            @pl.when(right & last)
            def _():
                z_copy(m, whole, False).start()

        def inward(m):
            @pl.when(left & (pos > 0))
            def _():
                z_copy(m, whole, True).wait_recv()
                view(acc, m)[...] = add(view(acc, m)[...], landed(from_left, m)[...])
                z_copy(m, whole, True).start()

            @pl.when(right & (pos < count - 1))
            def _():
                z_copy(m, whole, False).wait_recv()
                view(acc, m)[...] = add(view(acc, m)[...], landed(from_right, m)[...])
                z_copy(m, whole, False).start()

            @pl.when(here)
            def _():
                total = view(acc, m)[...].astype(F32)
                if root > 0:
                    z_copy(m, whole, True).wait_recv()
                    total = total + landed(from_left, m)[...].astype(F32)
                if root < count - 1:
                    z_copy(m, whole, False).wait_recv()
                    total = total + landed(from_right, m)[...].astype(F32)
                if whole:
                    view(acc, m)[...] = total.astype(BF16)
                    xc_copy(m).start()
                else:
                    view(out, m)[...] = total.astype(BF16)
                    spread(m)
                    a_copy(m).start()

        def spread(m):
            if root > 0:
                b_copy(m, whole, False).start()
            if root < count - 1:
                b_copy(m, whole, True).start()

        def crossed(m):
            xc_copy(m).wait_recv()
            view(out, m)[...] = add(view(acc, m)[...], landed(xc, m)[...])
            spread(m)
            finished(m)

        def outward(m):
            b_copy(m, whole, False).wait_recv()

            @pl.when(left & (pos > 0))
            def _():
                b_copy(m, whole, False).start()

            @pl.when(right & (pos < count - 1))
            def _():
                b_copy(m, whole, True).start()

            if whole:
                finished(m)
            else:
                a_copy(m).start()

        def sent(m):
            @pl.when(jnp.logical_not(here))
            def _():
                z_copy(m, whole, True).wait_send()

            @pl.when((pos <= root) & (pos > 0))
            def _():
                b_copy(m, whole, False).wait_send()

            @pl.when((pos >= root) & (pos < count - 1))
            def _():
                b_copy(m, whole, True).wait_send()

            if whole:
                @pl.when(here)
                def _():
                    xc_copy(m).wait_send()
            else:
                x_copy(m).wait_send()
                a_copy(m).wait_send()

        def add_y(m):
            @pl.when(with_y(m))
            def _():
                y_copy(m).wait_recv()
                acc[:, at(m), :] = add(acc[:, at(m), :], ry[:, y_at(m), :])

            set_off(m)

        def set_off(m):
            if whole:
                outer(m)
            else:
                x_copy(m).start()

        def add_x(m):
            x_copy(m).wait_recv()
            acc[sec, at(m), :] = add(acc[sec, at(m), :], rx[pair_at(m), :])
            outer(m)

        def last_half(m):
            a_wait(m)
            finished(m)

        base = 1 if whole else 2
        back = base + reach + dist + (1 if whole else 0)
        steps = [(back, jnp.logical_not(here), outward), (base + level, level > 0, inward)]
        if whole:
            steps.append((base + reach + 1, here, crossed))
        else:
            steps += [(back + 1, True, last_half), (2, True, add_x)]
        return steps, sent, add_y, set_off

    low_root = (count - 1) // 2
    high_root = min(low_root + 1, count - 1)
    lines = [
        (lambda m: (lax.rem(m, 2) == 1) | (m >= HALVED), *line_of(low_root, False)),
        (lambda m: (lax.rem(m, 4) == 0) & (m < HALVED), *line_of(low_root, True)),
        (lambda m: (lax.rem(m, 4) == 2) & (m < HALVED), *line_of(high_root, True)),
    ]

    def finish(m):
        @pl.when(m >= EARLY)
        def _():
            core_copy(m, out.at[:, at(m), :]).wait_send()

        @pl.when(with_y(m))
        def _():
            corey_copy(m, rcy.at[:, y_at(m), :]).wait_send()
            y_copy(m).wait_send()

        for mine, _, sent, _, _ in lines:
            @pl.when(mine(m))
            def _(sent=sent):
                sent(m)

    far_reach = max(low_root, count - 1 - low_root, high_root, count - 1 - high_root)
    depth = LAG * (3 + 2 * far_reach) + 1

    def tick(n):
        @pl.when(n < LATE)
        def _():
            for low, high, piece in pieces:
                @pl.when((n >= low) & (n < high))
                def _(low=low, piece=piece):
                    piece(n - low)

        for mine, steps, _, add_y, _ in lines:
            m = n - LAG

            @pl.when((m >= EARLY) & (m < ALL_K) & mine(m))
            def _(m=m, add_y=add_y):
                add_y(m)

            for offset, enabled, stage in steps:
                m = n - LAG * offset

                @pl.when((m >= 0) & (m < ALL_K) & mine(m) & enabled)
                def _(m=m, stage=stage):
                    stage(m)

        @pl.when(n < ALL_K)
        def _():
            stage_c(n)

        @pl.when(n >= depth)
        def _():
            finish(n - depth)

    def set_off_early(m):
        for mine, _, _, _, set_off in lines:
            @pl.when(mine(m))
            def _(set_off=set_off):
                set_off(m)

    loop(EARLY, set_off_early)
    loop(ALL_K + depth, tick)

    for step in range(1, devices):
        dx_copy(step).wait()
    for step in range(1, LANES):
        emb_copy(step).wait()
    give_enc().wait_send()
    for k in range(D // 256):
        give_part(k, 0).wait_send()
        give_part(k, 1).wait_send()
        give_last(k).wait_send()


def backward_call(args, half, hid):
    dma = lambda *s: pltpu.SemaphoreType.DMA(s)
    vm = pltpu.VMEM
    full = ALL_K * CH
    y_half = DEC_ROWS - EARLY_ROWS + CH
    whole = HALVED // 2 * CH
    by_half = full - whole
    k = ALL_K
    rows = 2 * PAD
    cut = D // (2 * LANES)
    specs = [VM, VM] + [ANY] * 18 + [VM] * 3
    return pl.pallas_call(
        backward_and_sums,
        out_shape=[
            jax.ShapeDtypeStruct((2, full, D), BF16),
            jax.ShapeDtypeStruct((LANES, 2, CH, D), BF16),
            jax.ShapeDtypeStruct((2 * LANES, cut, VIS), BF16),
        ],
        in_specs=specs,
        out_specs=[VM] * 3,
        scratch_shapes=[
            vm((rows, D), BF16), vm((D, rows), BF16), vm((D, rows), BF16),
            vm((rows, D), F32), vm((rows, D), BF16), vm((rows, D), BF16),
            vm((2, rows, hid), BF16), vm((rows, D), BF16), vm((rows, D), F32),
            vm((rows, half), BF16), vm((2, 3, rows, half), BF16),
            vm((PAD, D), F32), vm((PAD, D), BF16), vm((PAD, D), BF16), vm((PAD, D), F32),
            vm((2 * LANES, cut, VIS), BF16),
            vm((2, 1, hid), F32), vm((2, 2, half), F32), vm((8, D), F32),
            vm((2, full, D), BF16), vm((2, y_half, D), BF16), vm((2, ENC_A + ENC_B, D), BF16),
            vm((2, y_half, D), BF16), vm((2, y_half, D), BF16),
            vm((by_half, D), BF16), vm((by_half, D), BF16), vm((by_half, D), BF16),
            vm((2, whole, D), BF16), vm((2, whole, D), BF16), vm((2, whole, D), BF16),
            vm((LANES, 32, D), F32), vm((LANES, 2, CH, D), BF16),
            *[vm(v.shape, v.dtype) for v in args[2:19]], dma(17), dma(2), dma(10), dma(10),
            dma(k), dma(k), dma(k), dma(k), dma(k), dma(k),
            dma(k), dma(k), dma(k), dma(k), dma(k),
            dma(k), dma(k), dma(k), dma(k), dma(k), dma(LANES), dma(LANES),
            dma(2 * LANES), dma(2 * LANES),
        ],
        compiler_params=pltpu.CompilerParams(
            collective_id=1, has_side_effects=True, vmem_limit_bytes=VMEM_LIMIT
        ),
    )(*args)


def finish_grads(
    total_h, emb_h, decoded, dx, *refs,
):
    (
        decoded_out, dx_out,
        e_qkv_h, e_qvb, e_proj_h, e_up_h, e_upb, e_down_h, e_gain, e_off,
        d_qkv_h, d_qvb, d_proj_h, d_up_h, d_upb, d_down_h, d_gain, d_off, d_ew_h, d_ev,
        total, emb, e_qkv, e_proj, e_up, e_down, d_qkv, d_proj, d_up, d_down, d_ew, in_s, out_s,
    ) = refs
    half = e_proj.shape[0]
    spots = ((A_TOP, B_TOP), (B_TOP, S_TOP + CH), (0, A_TOP))
    loads = [
        pltpu.make_async_copy(
            total_h.at[:, low:high, :], total.at[:, low:high, :], in_s.at[n]
        )
        for n, (low, high) in enumerate(spots)
    ] + [pltpu.make_async_copy(emb_h, emb, in_s.at[3])]
    for load in loads:
        load.start()
    stores = []

    def store(src, dst):
        copy = pltpu.make_async_copy(src, dst, out_s.at[len(stores)])
        copy.start()
        stores.append(copy)

    store(decoded, decoded_out)
    store(dx, dx_out)
    loads[0].wait()
    e_up[...] = total[0, A_TOP:B_TOP, :].astype(F32)
    store(e_up, e_up_h)
    e_down[...] = jnp.transpose(total[1, A_TOP:B_TOP, :].astype(F32))
    store(e_down, e_down_h)
    loads[1].wait()
    e_qkv[0] = total[0, B_TOP : B_TOP + half, :].astype(F32)
    e_qkv[1] = total[0, B_TOP + half : S_TOP, :].astype(F32)
    e_qkv[2] = total[1, B_TOP : B_TOP + half, :].astype(F32)
    store(e_qkv, e_qkv_h)
    e_proj[...] = total[1, B_TOP + half : S_TOP, :].astype(F32)
    store(e_proj, e_proj_h)
    loads[3].wait()
    for k in range(LANES):
        for h in range(2):
            top = k * 192 + h * 64
            d_ew[top : top + 64, :] = emb[k, h, :, 0:512].astype(F32)
            d_ew[k * 192 + 128 : (k + 1) * 192, h * 256 : (h + 1) * 256] = emb[
                k, h, :, 512:768
            ].astype(F32)
    store(d_ew, d_ew_h)
    loads[2].wait()

    def tile(number):
        h, top, col = tile_of(number)
        return total[h, top : top + CH, col : col + 256].astype(F32)

    for block in range(GRID // CH):
        rows = slice(block * CH, (block + 1) * CH)
        side = slice(block // 2 * 128, (block // 2 + 1) * 128)
        for k in range(2):
            d_up[rows, k * 256 : (k + 1) * 256] = tile(4 * block + k)
            if block % 2:
                both = jnp.concatenate([tile(4 * block - 2 + k), tile(4 * block + 2 + k)], 0)
                d_down[k * 256 : (k + 1) * 256, side] = jnp.transpose(both)
        one, two = tile(32 + 2 * block), tile(33 + 2 * block)
        d_qkv[0, rows, :] = one[:, 0:128]
        d_qkv[1, rows, :] = one[:, 128:256]
        d_qkv[2, rows, :] = two[:, 0:128]
        d_proj[block % 2 * CH : (block % 2 + 1) * CH, side] = two[:, 128:256]
    for src, dst in ((d_up, d_up_h), (d_down, d_down_h), (d_qkv, d_qkv_h), (d_proj, d_proj_h)):
        store(src, dst)
    little = total[0, S_TOP : S_TOP + 32, :].astype(F32)
    d_upb[...] = little[0, 0:512]
    d_qvb[0:1, :] = little[1:2, 0:128]
    d_qvb[1:2, :] = little[1:2, 128:256]
    e_upb[...] = little[2]
    e_qvb[0:1, :] = little[3:4, 0:192]
    e_qvb[1:2, :] = little[3:4, 256:448]
    d_gain[...] = little[8:10, 0:512]
    d_off[...] = little[10:14, 0:512]
    d_ev[...] = little[14:16, 0:512]
    e_gain[...] = little[16:18]
    e_off[...] = little[18:22]
    for copy in stores:
        copy.wait()


def finish_call(total, emb, decoded, dx, shapes):
    large = (0, 2, 3, 5, 8, 10, 11, 13, 16)
    order = (0, 2, 3, 5, 8, 10, 11, 13, 16)
    vm = pltpu.VMEM
    return pl.pallas_call(
        finish_grads,
        out_shape=[jax.ShapeDtypeStruct(v.shape, v.dtype) for v in (decoded, dx)]
        + [jax.ShapeDtypeStruct(s, F32) for s in shapes],
        in_specs=[ANY] * 4,
        out_specs=[ANY, ANY] + [ANY if n in large else VM for n in range(len(shapes))],
        scratch_shapes=[vm(total.shape, BF16), vm(emb.shape, BF16)]
        + [vm(shapes[n], F32) for n in order]
        + [pltpu.SemaphoreType.DMA((4,)), pltpu.SemaphoreType.DMA((11,))],
        compiler_params=pltpu.CompilerParams(vmem_limit_bytes=VMEM_LIMIT),
    )(total, emb, decoded, dx)


def position_rows():
    quarter = DD // 4
    freq = np.exp(np.arange(quarter, dtype=np.float32) * np.float32(-math.log(10000.0) / quarter))
    angle = np.arange(PAD, dtype=np.float32)[:, None] * freq[None, :].astype(np.float32)
    both = np.concatenate([np.sin(angle), np.cos(angle)], 1).astype(np.float32)
    high = both.astype(jnp.bfloat16)
    low = (both - high.astype(np.float32)).astype(jnp.bfloat16)
    return np.stack([high, low])


def per_device(
    patches, cotangent, widths, visible, window_shift, batch_order,
    encoder_qkv, encoder_qvbias, encoder_proj, encoder_up, encoder_upbias, encoder_down,
    encoder_gains, encoder_offsets,
    decoder_qkv, decoder_qvbias, decoder_proj, decoder_up, decoder_upbias, decoder_down,
    decoder_gains, decoder_offsets, embed_weight, embed_vectors,
):
    qkv0 = encoder_qkv.transpose(1, 2, 0)
    half = qkv0.shape[1]
    hid = encoder_up.shape[1]
    dff = decoder_up.shape[1] * LANES
    flat = patches.transpose(1, 0, 2).reshape(-1, D)
    (
        x, x1, a, u, y, gp, qkv, p, o, qkv1, proj1, up1, down1, dec_buf,
        d_enc, d_dqvb, d_dupb, d_dsmall, out_all,
    ) = forward_call(
        (
            widths, window_shift.T, batch_order, visible, flat, encoder_gains, encoder_offsets,
            encoder_qvbias, encoder_upbias, decoder_qvbias, decoder_upbias,
            qkv0, encoder_proj, encoder_up, encoder_down,
            decoder_qkv.transpose(1, 0, 2), decoder_proj, decoder_up, decoder_down,
            cotangent, embed_weight, embed_vectors, jnp.asarray(position_rows()),
            decoder_gains, decoder_offsets,
        ),
        half, hid, dff,
    )
    total, emb, dx_all = backward_call(
        (
            d_enc, encoder_gains, u, y, gp, encoder_down, down1, encoder_up, up1,
            x, x1, a, qkv, p, o, qkv0, qkv1, encoder_proj, proj1,
            dec_buf, d_dqvb, d_dupb, d_dsmall,
        ),
        half, hid,
    )
    out_all, dx_all, *grads = finish_call(
        total, emb, out_all, dx_all,
        [
            (3, half, D), (2, half), (half, D), (D, hid), (hid,), (hid, D), (2, D), (4, D),
            (3, DD, 128), (2, 128), (128, DD), (DD, 512), (512,), (512, DD), (2, DD), (4, DD),
            (D, DD), (2, DD),
        ],
    )
    grads[0] = grads[0].transpose(2, 0, 1)
    grads[8] = grads[8].transpose(1, 0, 2)
    return (out_all.swapaxes(1, 2), dx_all.swapaxes(1, 2), *grads)


def solution(mesh):
    weights = (
        P(None, None, "tensor"), P(None, "tensor"), P("tensor", None), P(None, "tensor"),
        P("tensor"), P("tensor", None), P(), P(),
    )
    split = P("dp", None, ("section", "tensor"))
    return jax.shard_map(
        per_device,
        mesh=mesh,
        in_specs=(
            P("dp", None, None), P("dp", None, None), P("dp"), P("dp", None), P("dp", None),
            P("dp", None),
        ) + weights + weights + (P(), P()),
        out_specs=(split, split) + weights + weights + (P(), P()),
        check_vma=False,
    )
```

```python
import math

import jax
import jax.numpy as jnp
import numpy as np
from jax import lax
from jax.experimental import pallas as pl
from jax.experimental.pallas import tpu as pltpu
from jax.sharding import PartitionSpec as P

D = 768
HEADS = 12
DD = 512
DHEADS = 16
GRID_ROWS = 64
WIDE = 8
WIN = 4
VIS = 102
CM = 4
GRID = 512
LANES = 4
PAD = 128
EPS = 1e-06
NEG = -10000.0
F32 = jnp.float32
BF16 = jnp.bfloat16
VMEM_LIMIT = 60 * 1024 * 1024

VM = pl.BlockSpec(memory_space=pltpu.VMEM)
SM = pl.BlockSpec(memory_space=pltpu.SMEM)
ANY = pl.BlockSpec(memory_space=pl.ANY)


def nn(a, b):
    return lax.dot_general(a, b, (((1,), (0,)), ((), ())), preferred_element_type=F32)


def nt(a, b):
    return lax.dot_general(a, b, (((1,), (1,)), ((), ())), preferred_element_type=F32)


def tn(a, b):
    return lax.dot_general(a, b, (((0,), (0,)), ((), ())), preferred_element_type=F32)


def loop(count, body, unroll=1):
    def step(i, carry):
        body(i)
        return carry

    lax.fori_loop(0, count, step, 0, unroll=unroll)


def span(i, size):
    return pl.ds(pl.multiple_of(i * size, size), size)


def normal(x):
    center = x - jnp.mean(x, -1, keepdims=True)
    scale = lax.rsqrt(jnp.mean(center * center, -1, keepdims=True) + EPS)
    return center * scale, scale


def normal_back(dy, hat, scale, gain):
    d = dy * gain
    return scale * (
        d - jnp.mean(d, -1, keepdims=True) - hat * jnp.mean(d * hat, -1, keepdims=True)
    )


def gelu_both(h):
    phi = 0.5 * lax.erf(h * math.sqrt(0.5)) + 0.5
    bell = jnp.exp2(h * h * (-0.5 * math.log2(math.e)))
    return h * phi, phi + h * bell * (1.0 / math.sqrt(2.0 * math.pi))


def colsum(x):
    return jnp.sum(x, 0, keepdims=True)


def head_marks(width, size, dtype):
    lane = lax.broadcasted_iota(jnp.int32, (1, width), 1)
    return [((lane >= h * size) & (lane < (h + 1) * size)).astype(dtype) for h in range(width // size)]


def stacked(x, marks):
    return jnp.concatenate([x * m for m in marks], 0)


LOG2E = math.log2(math.e)


def attend(q, k, v, marks, ones, masked, scale):
    keys = k.shape[0]
    s = nt(q, stacked(k, marks))
    parts = []
    for h in range(len(marks)):
        x = masked(s[:, h * keys : (h + 1) * keys] * (scale * LOG2E))
        parts.append(jnp.exp2(x - jnp.max(x, -1, keepdims=True)).astype(BF16))
    e = jnp.concatenate(parts, 1)
    width = q.shape[1]
    if width % 128:
        top, total = nn(e, stacked(v, marks)), nn(e, ones)
    else:
        both = nn(e, jnp.concatenate([stacked(v, marks), ones], 1))
        top, total = both[:, :width], both[:, width:]
    inverse = 1.0 / total
    return e, (top * inverse).astype(BF16), inverse


def attend_back(q, k, v, e, o, inverse, d_out, marks, marks32, rows32, ones, scale):
    keys = k.shape[0]
    width = q.shape[1]
    d_one = d_out.astype(F32) * inverse
    d_two = (d_one * o.astype(F32)).astype(BF16)
    d_one = d_one.astype(BF16)
    if width % 128:
        d_s = nt(d_one, stacked(v, marks)) - nt(d_two, ones)
    else:
        d_s = nt(
            jnp.concatenate([d_one, d_two], 1), jnp.concatenate([stacked(v, marks), -ones], 1)
        )
    dr = (e.astype(F32) * d_s * scale).astype(BF16)
    d_q = nn(dr, stacked(k, marks)).astype(BF16)
    if width % 128:
        d_k_all, d_v_all = tn(dr, q), tn(e, d_one)
        d_k = d_v = 0.0
        for h in range(len(marks)):
            cut = slice(h * keys, (h + 1) * keys)
            d_k += d_k_all[cut] * marks32[h]
            d_v += d_v_all[cut] * marks32[h]
        return d_q, d_k.astype(BF16), d_v.astype(BF16)
    d_k_all = nn(jnp.transpose(q.astype(F32)).astype(BF16), dr)
    d_v_all = nn(jnp.transpose(d_one.astype(F32)).astype(BF16), e)
    d_k = d_v = 0.0
    for h in range(len(marks)):
        cut = slice(h * keys, (h + 1) * keys)
        d_k += d_k_all[:, cut] * rows32[h]
        d_v += d_v_all[:, cut] * rows32[h]
    return d_q, jnp.transpose(d_k).astype(BF16), jnp.transpose(d_v).astype(BF16)


def ones_per_head(keys, marks):
    return jnp.concatenate([jnp.broadcast_to(m, (keys, m.shape[1])) for m in marks], 0)


ENC_SIZE = D // HEADS
ENC_SCALE = ENC_SIZE ** -0.5
DEC_SIZE = DD // DHEADS
DEC_SCALE = DEC_SIZE ** -0.5


CH = 64
DEC_ROWS = 576
ENC_A = 768
ENC_B = 384
DEC_K = DEC_ROWS // CH
B_K = (DEC_ROWS + ENC_A + ENC_B) // CH
ALL_K = B_K + 1
A_TOP = DEC_ROWS
B_TOP = DEC_ROWS + ENC_A
S_TOP = B_TOP + ENC_B
EARLY = 4
EARLY_ROWS = EARLY * CH
LAG = 2
MIXED = EARLY + 2 * (DEC_K - EARLY)
WAIT = 2
LATE = 16
HALVED = ALL_K - 4


def tile_of(number):
    place = number // 3
    return place % 2, place // 2 * CH, number % 3 * 256


MESH = pl.DeviceIdType.MESH


def far(src, dst, send, recv, peer):
    return pltpu.make_async_remote_copy(
        src_ref=src, dst_ref=dst, send_sem=send, recv_sem=recv, device_id=peer, device_id_type=MESH
    )


def forward_and_decoder(
    wid, shifts, order, vis, pat, gains, offs, b_qv, b_up, b_dqv, b_dup,
    h_qkv, h_proj, h_up, h_down, h_dqkv, h_dproj, h_dup, h_ddown,
    cot_hbm, ew, evec, table, dgains, doffs,
    o_x, o_x1, o_a, o_u, o_y, o_gp, o_qkv, o_p, o_o, o_w, o_wproj, o_wup, o_wdown, o_dec,
    d_enc, d_qvb, d_upb, d_small, dec_out,
    w_qkv, w_proj, w_up, w_down, bias, biases, qkv, proj, up, down,
    ex, ea, eu, ey, egp, eqkv, ep, eo, ex1, epart, esend, erecv, esend2, erecv2, eown,
    cot, x0, x1, a, acts, probs, o, inverse, u, ut, y, gp, g32, gb, gt, acc, e_ref, hot, perm, buf, dsend, e_rc, e_rcy, e_ry,
    load_s, out_s, cot_s, w_s, w_r, bias_s, bias_r, dw_s, dw_r, ex_s, ex_r, ex2_s, ex2_r, do_s, do_r, e_s, e_r,
):
    sec = lax.axis_index("section")
    lane = lax.axis_index("tensor")
    mate = lane + 1 - 2 * lax.rem(lane, 2)
    over = lax.rem(lane + 2, LANES)
    cross = lax.rem(mate + 2, LANES)
    me = sec * LANES + lane
    devices = 2 * LANES
    clip = me
    clips = (me, sec * LANES + over)

    def group_peer(step):
        peer = lax.rem(me + step, devices)
        return peer, {"section": lax.div(peer, LANES), "tensor": lax.rem(peer, LANES)}

    own = [
        pltpu.make_async_copy(src, dst.at[0], load_s.at[n])
        for n, (src, dst) in enumerate(
            ((h_qkv, w_qkv), (h_proj, w_proj), (h_up, w_up), (h_down, w_down))
        )
    ]

    def place(n, shard, part=None):
        thick = (128, 128, 512, 512)[n]
        base = shard * thick
        cut = pl.ds(pl.multiple_of(base, thick), thick)
        if part is None:
            return (qkv.at[:, :, cut], proj.at[cut, :], up.at[:, cut], down.at[cut, :])[n]
        some = span(part, (256, 64, 256, 256)[n])
        if n == 0:
            return qkv.at[:, some, cut]
        if n == 2:
            return up.at[some, cut]
        few = thick // 2
        rows = pl.ds(pl.multiple_of(base + part * few, few), few)
        return (proj if n == 1 else down).at[rows, :]

    shards = (h_dqkv, h_dproj, h_dup, h_ddown)
    keep = [
        pltpu.make_async_copy(shards[n], place(n, lane), load_s.at[4 + n]) for n in range(4)
    ]
    for copy in own + keep:
        copy.start()
    fetch = pltpu.make_async_copy(cot_hbm.at[clip], cot, cot_s)
    fetch.start()

    barrier = pltpu.get_barrier_semaphore()
    for step in range(1, devices):
        pl.semaphore_signal(barrier, inc=1, device_id_type=MESH, device_id=group_peer(step)[1])
    bias[...] = jnp.zeros_like(bias)
    half = w_proj.shape[1]
    bias[0:1, :] = b_up[...].astype(F32).reshape(1, -1)
    bias[1:3, 0:half] = b_qv[...].astype(F32)
    bias[3:4, 0:512] = b_dup[...].astype(F32).reshape(1, -1)
    bias[4:6, 0:128] = b_dqv[...].astype(F32)
    biases[lane] = bias[...]
    pl.semaphore_wait(barrier, devices - 1)

    def enc_weight(n):
        src = (h_qkv, h_proj, h_up, h_down)[n]
        dst = (w_qkv, w_proj, w_up, w_down)[n]
        return far(src, dst.at[1], w_s.at[n], w_r.at[n], {"tensor": mate})

    def bias_copy(step):
        return far(
            bias, biases.at[lane], bias_s.at[step], bias_r.at[step],
            {"tensor": lax.rem(lane + step, LANES)},
        )

    def half_of(n):
        some = span(sec, (256, 64, 256, 256)[n])
        return shards[n].at[:, some, :] if n == 0 else shards[n].at[some, :]

    def dec_weight(n, kind):
        peer = {"section": 1 - sec} if kind == 2 else {"tensor": over if kind == 0 else mate}
        if kind == 0:
            src, dst = half_of(n), place(n, lane, sec)
        elif kind == 1:
            src, dst = shards[n], place(n, lane)
        else:
            src = dst = place(n, over, 1 - sec if kind == 4 else sec)
        return far(src, dst, dw_s.at[5 * n + kind], dw_r.at[5 * n + kind], peer)

    enc_weight(0).start()
    for step in range(1, LANES):
        bias_copy(step).start()
    enc_weight(1).start()
    dec_weight(0, 0).start()
    enc_weight(2).start()
    enc_weight(3).start()
    for n in range(4):
        dec_weight(n, 1).start()

    def pass_on(n):
        dec_weight(n, 0).wait_recv()
        dec_weight(n, 2).start()
        dec_weight(n, 3).start()

    def pass_last(n):
        dec_weight(n, 2).wait_recv()
        dec_weight(n, 4).start()

    def arrived(n):
        keep[n].wait()
        dec_weight(n, 1).wait_recv()
        dec_weight(n, 3).wait_recv()
        dec_weight(n, 4).wait_recv()

    width = wid[clip]
    bits = jnp.where(width == WIDE, 3, 2)
    turn = shifts[0, clip] * width
    mod = GRID - 1
    spot = 0
    for i in range(order.shape[1]):
        spot = spot + jnp.where(order[0, i] == clip, i, 0)
    batch = spot // CM
    count = 0
    for i in range(order.shape[1]):
        count = count + jnp.where(batch == i // CM, wid[order[0, i]], 0)
    factor_rows = CM * GRID / (jnp.full((1, 1), count, jnp.int32) * GRID_ROWS).astype(F32)

    def slot_of(index):
        return (index - turn) & mod

    def code_of(slot):
        band = ((slot >> bits) + shifts[0, clip]) >> 2
        strip = ((slot & (width - 1)) + shifts[1, clip]) >> 2
        return band * 4 + strip

    def valid_rows():
        slot = slot_of(lax.broadcasted_iota(jnp.int32, (GRID, 1), 0))
        return (slot < GRID_ROWS * width).astype(F32)

    def clip_gradient():
        fetch.wait()
        rolled = slot_of(lax.broadcasted_iota(jnp.int32, (GRID, GRID), 0))
        column = lax.broadcasted_iota(jnp.int32, (GRID, GRID), 1)
        perm[...] = (rolled == column).astype(F32).astype(BF16)
        g = nn(perm[...], cot[...]) * valid_rows() * factor_rows
        g32[...] = g
        gb[...] = g.astype(BF16)
        gt[...] = jnp.transpose(g).astype(BF16)
        d_small[...] = jnp.zeros_like(d_small)
        d_small[5:6, :] = colsum(g)

    seen = vis[pl.ds(clip, 1), :]
    target = jnp.concatenate([(seen + turn) & mod, jnp.full((1, PAD - VIS), -1, jnp.int32)], 1)

    def places(i):
        r = span(i, PAD)
        index = lax.broadcasted_iota(jnp.int32, (PAD, PAD), 0) + i * PAD
        column = lax.broadcasted_iota(jnp.int32, (PAD, PAD), 1)
        hot[r, :] = (index == target).astype(F32).astype(BF16)
        slot = slot_of(index)
        by_row = ((slot >> bits) == column).astype(F32).astype(BF16)
        by_col = ((slot & (width - 1)) == column).astype(F32).astype(BF16)
        row_part = nn(by_row, table[0]) + nn(by_row, table[1])
        col_part = nn(by_col, table[0]) + nn(by_col, table[1])
        x0[r, :] = jnp.concatenate([row_part, col_part], 1)

    egain = gains[...].astype(F32)
    eoff = offs[...].astype(F32)
    stride = pat.shape[0] // VIS
    for c in range(2):
        row = lax.broadcasted_iota(jnp.int32, (PAD, pat.shape[0]), 0)
        col = lax.broadcasted_iota(jnp.int32, (PAD, pat.shape[0]), 1)
        pick = (col == row * stride + clips[c]).astype(F32).astype(BF16)
        ex[c * PAD : (c + 1) * PAD, :] = nn(pick, pat[...])

    emarks = head_marks(half, ENC_SIZE, BF16)
    key = lax.broadcasted_iota(jnp.int32, (PAD, PAD), 1)
    floor = jnp.where(key < VIS, NEG * LOG2E, -1e30)
    eones = ones_per_head(PAD, emarks)
    blocks = D // 256

    def give_part(i, side):
        cut = span(i, 256)
        return far(
            esend.at[(1 - side) * PAD : (2 - side) * PAD, cut],
            erecv.at[side * PAD : (side + 1) * PAD, cut],
            ex_s.at[2 * i + side], ex_r.at[2 * i + side], {"tensor": over},
        )

    for c in range(2):
        rows = slice(c * PAD, (c + 1) * PAD)
        hat, _ = normal(ex[rows, :])
        ea[rows, :] = (hat * egain[0:1] + eoff[0:1]).astype(BF16)
        limit = (VIS * wid[clips[c]]) // WIDE
        for g, shard in enumerate((lane, mate)):
            if c == 0 and g == 0:
                own[0].wait()
            if c == 0 and g == 1:
                enc_weight(0).wait_recv()
                for step in range(1, LANES):
                    bias_copy(step).wait_recv()
            if g == 0:
                bq, bv = bias[1:2, 0:half], bias[2:3, 0:half]
            else:
                bq, bv = biases[shard, 1:2, 0:half], biases[shard, 2:3, 0:half]
            eqkv[g, 0, rows] = (nt(ea[rows, :], w_qkv[g, 0]) + bq).astype(BF16)
            eqkv[g, 1, rows] = nt(ea[rows, :], w_qkv[g, 1]).astype(BF16)
            eqkv[g, 2, rows] = (nt(ea[rows, :], w_qkv[g, 2]) + bv).astype(BF16)
            p, out, _ = attend(
                eqkv[g, 0, rows], eqkv[g, 1, rows], eqkv[g, 2, rows], emarks, eones,
                lambda s: jnp.where(key < limit, s, floor), ENC_SCALE,
            )
            ep[g, c] = p
            eo[g, rows] = out
        if c == 0:
            own[1].wait()
            enc_weight(1).wait_recv()
        for i in range(blocks):
            cut = slice(i * 256, (i + 1) * 256)
            t = nn(eo[0, rows], w_proj[0, :, cut]) + nn(eo[1, rows], w_proj[1, :, cut])
            epart[rows, cut] = t
            esend[rows, cut] = t.astype(BF16)
            give_part(i, 1 - c).start()
    pass_on(0)
    clip_gradient()
    own[2].wait()
    enc_weight(2).wait_recv()

    def give_last(i):
        cut = span(i, 256)
        return far(
            esend2.at[:, cut], erecv2.at[:, cut], ex2_s.at[i], ex2_r.at[i], {"tensor": over}
        )

    for c in (1, 0):
        rows = slice(c * PAD, (c + 1) * PAD)
        for i in range(blocks):
            give_part(i, c).wait_recv()
        t = ex[rows, :] + epart[rows, :] + erecv[rows, :].astype(F32) + eoff[2:3]
        ex1[rows, :] = t
        hat, _ = normal(t)
        eu[rows, :] = (hat * egain[1:2] + eoff[1:2]).astype(BF16)
        for g, shard in enumerate((lane, mate)):

            def enc_ff(i, g=g, shard=shard, rows=rows):
                cut = span(i, 256)
                h = nn(eu[rows, :], w_up[g, :, cut]) + biases[shard, 0:1, cut]
                act, slope = gelu_both(h)
                ey[g, rows, cut] = act.astype(BF16)
                egp[g, rows, cut] = slope.astype(BF16)

            loop(w_up.shape[2] // 256, enc_ff, unroll=3)
        if c == 1:
            own[3].wait()
            enc_weight(3).wait_recv()
        for i in range(blocks):
            cut = slice(i * 256, (i + 1) * 256)
            t = nn(ey[0, rows], w_down[0, :, cut]) + nn(ey[1, rows], w_down[1, :, cut])
            if c == 0:
                eown[:, cut] = t
            else:
                esend2[:, cut] = t.astype(BF16)
                give_last(i).start()
        if c == 1:
            for n in (1, 2, 3):
                dec_weight(n, 0).start()
            pass_last(0)
    outs = [
        pltpu.make_async_copy(src, dst, out_s.at[n])
        for n, (src, dst) in enumerate(
            (
                (ex.at[0:PAD, :], o_x), (ex1, o_x1), (ea, o_a), (eu, o_u), (ey, o_y), (egp, o_gp),
                (eqkv, o_qkv), (ep, o_p), (eo, o_o), (w_qkv.at[1], o_w), (w_proj.at[1], o_wproj),
                (w_up.at[1], o_wup), (w_down.at[1], o_wdown),
            )
        )
    ]
    for copy in outs:
        copy.start()
    loop(GRID // PAD, places, unroll=2)
    for i in range(blocks):
        give_last(i).wait_recv()

    e_ref[...] = (ex1[0:PAD, :] + eown[...] + erecv2[...].astype(F32) + eoff[3:4]).astype(BF16)
    vec = evec[...].astype(F32)
    m = (nn(e_ref[...], ew[...]) + vec[0:1]).astype(BF16)
    gain = dgains[...].astype(F32)
    offsets = doffs[...].astype(F32)

    def start(i):
        r = span(i, PAD)
        oh = hot[r, :]
        hit = jnp.sum(oh.astype(F32), -1, keepdims=True)
        x = jnp.where(hit > 0, nn(oh, m), vec[1:2]).astype(BF16).astype(F32) + x0[r, :]
        x0[r, :] = x
        hat, _ = normal(x)
        a[r, :] = (hat * gain[0:1] + offsets[0:1]).astype(BF16)

    loop(GRID // PAD, start, unroll=2)
    arrived(0)

    def dec_bias(row, size):
        return jnp.concatenate([biases[k, row : row + 1, 0:size] for k in range(LANES)], 1)

    def project(i):
        r = span(i, 256)
        rows = a[r, :]
        acts[0, r, :] = (nn(rows, qkv[0]) + dec_bias(4, 128)).astype(BF16)
        acts[1, r, :] = nn(rows, qkv[1]).astype(BF16)
        acts[2, r, :] = (nn(rows, qkv[2]) + dec_bias(5, 128)).astype(BF16)

    loop(2, project)
    pass_on(1)
    pass_on(2)
    marks = head_marks(128, DEC_SIZE, BF16)
    marks32 = head_marks(128, DEC_SIZE, F32)
    dim = lax.broadcasted_iota(jnp.int32, (128, 1), 0)
    rows32 = [
        ((dim >= h * DEC_SIZE) & (dim < (h + 1) * DEC_SIZE)).astype(F32) for h in range(len(marks))
    ]

    ones = ones_per_head(PAD, marks)

    def attention(i):
        r = span(i, PAD)
        row_slot = slot_of(lax.broadcasted_iota(jnp.int32, (PAD, PAD), 0) + i * PAD)
        key_slot = slot_of(lax.broadcasted_iota(jnp.int32, (PAD, PAD), 1) + i * PAD)
        allowed = (code_of(row_slot) == code_of(key_slot)) & (key_slot < GRID_ROWS * width)
        for g in range(DD // 128):
            c = slice(g * 128, (g + 1) * 128)
            probs[i, :, g * 512 : (g + 1) * 512], o[r, c], inverse[r, c] = attend(
                acts[0, r, c], acts[1, r, c], acts[2, r, c], marks, ones,
                lambda s: jnp.where(allowed, s, NEG * LOG2E), DEC_SCALE,
            )

    loop(GRID // PAD, attention, unroll=2)
    pass_last(1)
    pass_last(2)
    pass_on(3)
    arrived(1)

    def mix(i):
        r = span(i, PAD)
        x = x0[r, :] + nn(o[r, :], proj[...]) + offsets[2:3]
        x1[r, :] = x
        hat, _ = normal(x)
        un = hat * gain[1:2] + offsets[1:2]
        u[r, :] = un.astype(BF16)
        ut[:, r] = jnp.transpose(un).astype(BF16)

    loop(GRID // PAD, mix, unroll=2)
    pass_last(3)
    arrived(2)

    def ff(i):
        k = lax.div(i, 4)
        side = lax.rem(lax.div(i, 2), 2)
        c = span(lax.div(i, 2), 256)
        r = span(lax.rem(i, 2), 256)
        h = nn(u[r, :], up[:, c]) + biases[k, 3:4, span(side, 256)]
        act, slope = gelu_both(h)
        y[r, c] = act.astype(BF16)
        gp[r, c] = slope.astype(BF16)

    loop(2 * up.shape[1] // 256, ff, unroll=2)
    arrived(3)
    def out(i):
        r = span(lax.rem(i, 2), 256)
        c = span(lax.div(i, 2), 256)
        acc[r, c] = nn(y[r, :], down[:, c])

    loop(4, out, unroll=2)
    full = ((acc[...] + x1[...] + offsets[3:4]) * valid_rows()).astype(BF16)
    turned = tn(full, perm[...]).astype(BF16)
    for k in range(devices):
        dsend[k] = turned[k * dsend.shape[1] : (k + 1) * dsend.shape[1]]

    def decoded_copy(step):
        peer, spot = group_peer(step)
        return far(dsend.at[peer], dec_out.at[me], do_s.at[step], do_r.at[step], spot)

    for step in range(1, devices):
        decoded_copy(step).start()
    dec_out[me] = dsend[me]

    def ff_back(shard):
        for side in range(2):
            c = span(2 * shard + side, 256)
            d_down = nn(gt[...], y[:, c]).astype(BF16)
            dh = nt(gb[...], down[c, :]) * gp[:, c].astype(F32)
            d_upb[:, c] = colsum(dh)
            du = dh.astype(BF16)
            gp[:, c] = du
            d_up = nn(ut[...], du).astype(BF16)
            for block in range(GRID // CH):
                rows = slice(block * CH, (block + 1) * CH)
                h, top, col = tile_of(4 * block + side)
                buf[shard, h, top : top + CH, col : col + 256] = d_up[rows]
                h, top, col = tile_of(4 * block + 2 + side)
                buf[shard, h, top : top + CH, col : col + 256] = d_down[rows]

    def early_core(which):
        shard, land = ((mate, e_rc), (cross, e_rcy))[which]
        return far(
            buf.at[shard, :, 0:EARLY_ROWS, :], land, e_s.at[which], e_r.at[which], {"tensor": mate}
        )

    def early_y():
        return far(
            buf.at[over, :, 0:EARLY_ROWS, :], e_ry, e_s.at[2], e_r.at[2], {"tensor": over}
        )

    def early_add(shard, land):
        def body(i):
            r = span(i, CH)
            buf[shard, :, r, :] = buf[shard, :, r, :] + land[:, r, :]

        loop(EARLY_ROWS // CH, body)

    def ff_step(i):
        ff_back(jnp.where(i == 0, cross, jnp.where(i == 1, over, jnp.where(i == 2, mate, lane))))

        @pl.when(i == 1)
        def _():
            early_core(1).start()

        @pl.when(i == 2)
        def _():
            early_core(0).start()
            early_core(1).wait_recv()
            early_add(over, e_rcy)
            early_y().start()

    loop(LANES, ff_step)

    def ff_in(i):
        r = span(lax.rem(i, 2), 256)
        c = span(lax.div(i, 2), 256)
        acc[r, c] = nt(gp[r, :], up[c, :])

    loop(4, ff_in, unroll=2)

    def mix_back(i):
        r = span(i, PAD)
        hat, scale = normal(x1[r, :])
        da = acc[r, :]
        dx = g32[r, :] + normal_back(da, hat, scale, gain[1:2])
        d_small[1:2, :] += colsum(da * hat)
        d_small[3:4, :] += colsum(da)
        d_small[4:5, :] += colsum(dx)
        g32[r, :] = dx
        dxb = dx.astype(BF16)
        gb[r, :] = dxb
        u[r, :] = nt(dxb, proj[...]).astype(BF16)

    loop(GRID // PAD, mix_back, unroll=2)
    early_core(0).wait_recv()
    early_add(lane, e_rc)
    d_proj = tn(o[...], gb[...]).astype(BF16)
    for block in range(GRID // CH):
        h, top, col = tile_of(33 + 2 * block)
        side = slice(block // 2 * 128, (block // 2 + 1) * 128)
        for k in range(LANES):
            row = k * 128 + block % 2 * CH
            buf[k, h, top : top + CH, col + 128 : col + 256] = d_proj[row : row + CH, side]

    def attention_back(i):
        r = span(i, PAD)
        for k in range(DD // 128):
            c = slice(k * 128, (k + 1) * 128)
            acts[0, r, c], acts[1, r, c], acts[2, r, c] = attend_back(
                acts[0, r, c], acts[1, r, c], acts[2, r, c],
                probs[i, :, k * 512 : (k + 1) * 512], o[r, c], inverse[r, c], u[r, c],
                marks, marks32, rows32, ones, DEC_SCALE,
            )

    loop(GRID // PAD, attention_back, unroll=2)
    d_qvb[0:1, :] = colsum(acts[0].astype(F32))
    d_qvb[1:2, :] = colsum(acts[2].astype(F32))

    def project_back(i):
        r = span(lax.rem(i, 2), 256)
        c = span(lax.div(i, 2), 256)
        acc[r, c] = (
            nt(acts[0, r, :], qkv[0, c, :])
            + nt(acts[1, r, :], qkv[1, c, :])
            + nt(acts[2, r, :], qkv[2, c, :])
        )

    loop(4, project_back, unroll=2)
    gt[...] = jnp.transpose(a[...].astype(F32)).astype(BF16)
    for j in range(3):
        d_qkv = nn(gt[...], acts[j]).astype(BF16)
        for block in range(GRID // CH):
            h, top, col = tile_of(32 + 2 * block + j // 2)
            col = col + j % 2 * 128
            rows = slice(block * CH, (block + 1) * CH)
            for k in range(LANES):
                buf[k, h, top : top + CH, col : col + 128] = d_qkv[rows, k * 128 : (k + 1) * 128]

    def start_back(i):
        r = span(i, PAD)
        hat, scale = normal(x0[r, :])
        da = acc[r, :]
        dx = g32[r, :] + normal_back(da, hat, scale, gain[0:1])
        d_small[0:1, :] += colsum(da * hat)
        d_small[2:3, :] += colsum(da)
        dg = dx.astype(BF16)
        gb[r, :] = dg
        hit = jnp.sum(hot[r, :].astype(F32), -1, keepdims=True)
        d_small[7:8, :] += colsum(jnp.where(hit > 0, 0.0, dg.astype(F32)))

    loop(GRID // PAD, start_back, unroll=2)
    dm = tn(hot[...], gb[...])
    d_small[6:7, :] = colsum(dm)
    dmb = dm.astype(BF16)
    d_enc[...] = nt(dmb, ew[...]).astype(BF16)
    d_ew = tn(e_ref[...], dmb).astype(BF16)
    for k in range(LANES):
        for h in range(2):
            top = k * 192 + h * 64
            buf[k, h, 512:576, 0:512] = d_ew[top : top + 64]
            buf[k, h, 512:576, 512:768] = d_ew[k * 192 + 128 : (k + 1) * 192, h * 256 : (h + 1) * 256]

    early_y().wait_recv()
    early_add(lane, e_ry)
    later = pl.ds(EARLY_ROWS, DEC_ROWS - EARLY_ROWS)
    rest = [pltpu.make_async_copy(buf.at[lane], o_dec.at[lane], out_s.at[13])] + [
        pltpu.make_async_copy(buf.at[k, :, later, :], o_dec.at[k, :, later, :], out_s.at[14 + n])
        for n, k in enumerate((mate, over, cross))
    ]
    for copy in rest:
        copy.start()
    for copy in outs + rest:
        copy.wait()
    for which in range(2):
        early_core(which).wait_send()
    early_y().wait_send()
    for n in range(4):
        enc_weight(n).wait_send()
        for kind in range(5):
            dec_weight(n, kind).wait_send()
    for step in range(1, LANES):
        bias_copy(step).wait_send()
    for i in range(blocks):
        give_part(i, 0).wait_send()
        give_part(i, 1).wait_send()
        give_last(i).wait_send()
    for step in range(1, devices):
        decoded_copy(step).wait()


def forward_call(args, half, hid, dff):
    dma = lambda *s: pltpu.SemaphoreType.DMA(s)
    vm = lambda dtype, *shape: pltpu.VMEM(shape, dtype)
    rows = 2 * PAD
    keys = PAD * half // ENC_SIZE
    devices = 2 * LANES
    slab = DD // devices
    kept = [
        ((PAD, D), F32), ((rows, D), F32), ((rows, D), BF16), ((rows, D), BF16),
        ((2, rows, hid), BF16), ((2, rows, hid), BF16), ((2, 3, rows, half), BF16),
        ((2, 2, PAD, keys), BF16), ((2, rows, half), BF16),
        ((3, half, D), BF16), ((half, D), BF16), ((D, hid), BF16), ((hid, D), BF16),
        ((LANES, 2, DEC_ROWS, D), BF16),
    ]
    made = [
        ((PAD, D), BF16), ((2, DD), F32), ((1, dff), F32), ((8, DD), F32),
        ((devices, slab, GRID), BF16),
    ]
    return pl.pallas_call(
        forward_and_decoder,
        out_shape=[jax.ShapeDtypeStruct(s, d) for s, d in kept + made],
        in_specs=[SM, SM, SM] + [VM] * 8 + [ANY] * 9 + [VM] * 5,
        out_specs=[ANY] * len(kept) + [VM] * len(made),
        scratch_shapes=[
            vm(BF16, 2, 3, half, D), vm(BF16, 2, half, D), vm(BF16, 2, D, hid), vm(BF16, 2, hid, D),
            vm(F32, 8, D), vm(F32, LANES, 8, D),
            vm(BF16, 3, DD, DD), vm(BF16, DD, DD), vm(BF16, DD, dff), vm(BF16, dff, DD),
            vm(F32, rows, D), vm(BF16, rows, D), vm(BF16, rows, D), vm(BF16, 2, rows, hid),
            vm(BF16, 2, rows, hid), vm(BF16, 2, 3, rows, half), vm(BF16, 2, 2, PAD, keys),
            vm(BF16, 2, rows, half), vm(F32, rows, D), vm(F32, rows, D), vm(BF16, rows, D),
            vm(BF16, rows, D), vm(BF16, PAD, D), vm(BF16, PAD, D), vm(F32, PAD, D),
            vm(BF16, GRID, DD), vm(F32, GRID, DD), vm(F32, GRID, DD), vm(BF16, GRID, DD),
            vm(BF16, 3, GRID, DD), vm(BF16, GRID // PAD, PAD, DHEADS * PAD), vm(BF16, GRID, DD),
            vm(F32, GRID, DD),
            vm(BF16, GRID, DD), vm(BF16, DD, GRID), vm(BF16, GRID, dff), vm(BF16, GRID, dff),
            vm(F32, GRID, DD), vm(BF16, GRID, DD), vm(BF16, DD, GRID), vm(F32, GRID, DD),
            vm(BF16, PAD, D), vm(BF16, GRID, PAD), vm(BF16, GRID, GRID),
            vm(BF16, LANES, 2, DEC_ROWS, D),
            vm(BF16, devices, slab, GRID), *[vm(BF16, 2, EARLY_ROWS, D)] * 3,
            dma(8), dma(17), pltpu.SemaphoreType.DMA, dma(4), dma(4), dma(LANES), dma(LANES),
            dma(20), dma(20), dma(6), dma(6), dma(3), dma(3), dma(devices), dma(devices),
            dma(3), dma(3),
        ],
        compiler_params=pltpu.CompilerParams(
            collective_id=0, has_side_effects=True, vmem_limit_bytes=VMEM_LIMIT
        ),
    )(*args)


def add(x, y):
    return x + y


def backward_and_sums(
    d_enc, gains,
    h_u, h_y, h_gp, h_down0, h_down1, h_up0, h_up1,
    h_x, h_x1, h_a, h_qkv, h_p, h_o, h_w0, h_w1, h_proj0, h_proj1,
    dec, dec_qvb, dec_upb, dec_small,
    out, emb, dx_out,
    gb, gt, ut, part, send, recv, du, gx, dx1, d_o, d_acts, own, send1, recv1, dx32, dx,
    d_upb, d_qvb, d_small,
    acc, yacc, enc_mate, rcy, ry, rx, zl, zr, xc, cl, cr, small32, small,
    u, y, gp, down0, down1, up0, up1, x, x1, a, qkv, p, o, w0, w1, proj0, proj1, fetch_s,
    load_s, ex_s, ex_r,
    core_s, core_r, corey_s, corey_r, y_s, y_r, x_s, x_r, z_s, zl_r, zr_r,
    bl_s, br_s, b_r, a_s, a_r, emb_s, emb_r, dx_s, dx_r,
):
    sec = lax.axis_index("section")
    lane = lax.axis_index("tensor")
    pos = lax.axis_index("dp")
    count = lax.axis_size("dp")
    mate = lane + 1 - 2 * lax.rem(lane, 2)
    over = lax.rem(lane + 2, LANES)
    cross = lax.rem(mate + 2, LANES)
    first = pos == 0
    last = pos == count - 1
    me = sec * LANES + lane
    devices = 2 * LANES

    def group_peer(step):
        peer = lax.rem(me + step, devices)
        return peer, {"section": lax.div(peer, LANES), "tensor": lax.rem(peer, LANES)}

    barrier = pltpu.get_barrier_semaphore()
    for step in range(1, devices):
        pl.semaphore_signal(barrier, inc=1, device_id_type=MESH, device_id=group_peer(step)[1])

    @pl.when(pos > 0)
    def _():
        pl.semaphore_signal(barrier, inc=1, device_id={"dp": pos - 1}, device_id_type=MESH)

    @pl.when(pos < count - 1)
    def _():
        pl.semaphore_signal(barrier, inc=1, device_id={"dp": pos + 1}, device_id_type=MESH)

    fetches = [
        pltpu.make_async_copy(src, dst, fetch_s.at[n])
        for n, (src, dst) in enumerate(
            (
                (h_u, u), (h_y, y), (h_gp, gp), (h_down0, down0), (h_down1, down1), (h_up0, up0),
                (h_up1, up1), (h_x, x), (h_x1, x1), (h_a, a), (h_qkv, qkv), (h_p, p), (h_o, o),
                (h_w0, w0), (h_w1, w1), (h_proj0, proj0), (h_proj1, proj1),
            )
        )
    ]
    for fetch in fetches:
        fetch.start()
    loads = [
        pltpu.make_async_copy(dec.at[lane], acc.at[:, 0:DEC_ROWS, :], load_s.at[0]),
        pltpu.make_async_copy(
            dec.at[over, :, EARLY_ROWS:DEC_ROWS, :], yacc.at[:, 0 : DEC_ROWS - EARLY_ROWS, :],
            load_s.at[1],
        ),
    ]
    for load in loads:
        load.start()
    small32[...] = jnp.zeros_like(small32)
    small[...] = jnp.zeros_like(small)
    d_small[...] = jnp.zeros_like(d_small)
    gb[0:PAD, :] = d_enc[...]
    ends = jnp.where(first, 0, 1) + jnp.where(last, 0, 1)
    pl.semaphore_wait(barrier, devices - 1 + ends)

    gain = gains[...].astype(F32)
    width = w0.shape[1]
    marks = head_marks(width, ENC_SIZE, BF16)
    marks32 = head_marks(width, ENC_SIZE, F32)
    ones = ones_per_head(PAD, marks)

    def rows(k, size=CH):
        return pl.ds(pl.multiple_of(k * size, size), size)

    def give_enc():
        return far(d_enc, gb.at[PAD : 2 * PAD, :], ex_s.at[0], ex_r.at[0], {"tensor": over})

    def give_part(i, half):
        cut = rows(i, 256)
        n = 1 + 2 * i + half
        return far(
            send.at[(1 - half) * PAD : (2 - half) * PAD, cut],
            recv.at[half * PAD : (half + 1) * PAD, cut],
            ex_s.at[n], ex_r.at[n], {"tensor": over},
        )

    def give_last(i):
        cut = rows(i, 256)
        return far(send1.at[:, cut], recv1.at[:, cut], ex_s.at[7 + i], ex_r.at[7 + i], {"tensor": over})

    def ff_back(g, i, down):
        c = rows(i, 256)
        d_down = nn(gt[...], y[g, :, c]).astype(BF16)
        dh = nt(gb[...], down[c, :]) * gp[g, :, c].astype(F32)
        d_upb[g, :, c] = colsum(dh)
        dub = dh.astype(BF16)
        du[g, :, c] = dub
        d_up = nn(ut[...], dub).astype(BF16)
        if g == 0:
            acc[1, A_TOP:B_TOP, c] = d_down
            acc[0, A_TOP:B_TOP, c] = d_up
        else:
            enc_mate[1, 0:ENC_A, c] = d_down
            enc_mate[0, 0:ENC_A, c] = d_up

    def ff_in(i):
        c = rows(i, 256)
        t = nt(du[0], up0[c, :]) + nt(du[1], up1[c, :])
        part[:, c] = t
        send[:, c] = t.astype(BF16)
        give_part(i, 0).start()
        give_part(i, 1).start()

    def norm_two(i):
        del i
        for fetch in fetches[7:]:
            fetch.wait()
        for k in range(D // 256):
            give_part(k, 0).wait_recv()
            give_part(k, 1).wait_recv()

        def body(j):
            r = rows(j, 64)
            da = part[r, :] + recv[r, :].astype(F32)
            hat, scale = normal(x1[r, :])
            g = gb[r, :].astype(F32)
            d = g + normal_back(da, hat, scale, gain[1:2])
            gx[r, :] = d.astype(BF16)
            dx1[r, :] = d

            @pl.when(j < 2)
            def _():
                d_small[1:2, :] += colsum(da * hat)
                d_small[3:4, :] += colsum(da)
                d_small[4:5, :] += colsum(d)
                d_small[5:6, :] += colsum(g)

        loop(2 * PAD // 64, body)

    def attention(g, proj):
        d_proj = tn(o[g], gx[...]).astype(BF16)
        if g == 0:
            acc[1, B_TOP + width : S_TOP, :] = d_proj
        else:
            enc_mate[1, ENC_A + width : ENC_A + 2 * width, :] = d_proj
        d_o[...] = nt(gx[...], proj[...]).astype(BF16)
        for c in range(2):
            r = slice(c * PAD, (c + 1) * PAD)
            dq, dk, dv = attend_back(
                qkv[g, 0, r], qkv[g, 1, r], qkv[g, 2, r], p[g, c], o[g, r], 1.0 / nn(p[g, c], ones),
                d_o[r, :], marks, marks32, None, ones, ENC_SCALE,
            )
            d_acts[g, 0, r] = dq
            d_acts[g, 1, r] = dk
            d_acts[g, 2, r] = dv
        d_qvb[g, 0:1, :] = colsum(d_acts[g, 0].astype(F32))
        d_qvb[g, 1:2, :] = colsum(d_acts[g, 2].astype(F32))

    def project_in(i):
        c = rows(i, 256)
        t = 0.0
        for g, w in enumerate((w0, w1)):
            for j in range(3):
                t += nn(d_acts[g, j], w[j, :, c])
        own[:, c] = t[:PAD]
        send1[:, c] = t[PAD:].astype(BF16)
        give_last(i).start()

    def project_grad(g):
        for j in range(3):
            row = (j % 2) * width
            d = tn(d_acts[g, j], a[...]).astype(BF16)
            if g == 0:
                acc[j // 2, B_TOP + row : B_TOP + row + width, :] = d
            else:
                enc_mate[j // 2, ENC_A + row : ENC_A + row + width, :] = d

    def norm_one(i):
        del i
        for k in range(D // 256):
            give_last(k).wait_recv()

        def body(j):
            r = rows(j, 64)
            da = own[r, :] + recv1[r, :].astype(F32)
            hat, scale = normal(x[r, :])
            d_small[0:1, :] += colsum(da * hat)
            d_small[2:3, :] += colsum(da)
            dx32[r, :] = dx1[r, :] + normal_back(da, hat, scale, gain[0:1])

        loop(PAD // 64, body)
        turned = jnp.transpose(dx32[...])
        cut = D // devices
        for k in range(devices):
            dx[k] = turned[k * cut : (k + 1) * cut, 0:VIS].astype(BF16)
        for r in range(LANES):
            small32[r, 0:1, 0:512] = dec_upb[:, r * 512 : (r + 1) * 512]
            small32[r, 1:2, 0:128] = dec_qvb[0:1, r * 128 : (r + 1) * 128]
            small32[r, 1:2, 128:256] = dec_qvb[1:2, r * 128 : (r + 1) * 128]
            small32[r, 8:16, 0:512] = dec_small[...]
            small32[r, 16:24, :] = d_small[...]
        for g, shard in enumerate((lane, mate)):
            small32[shard, 2:3, :] = d_upb[g]
            small32[shard, 3:4, 0:192] = d_qvb[g, 0:1]
            small32[shard, 3:4, 256:448] = d_qvb[g, 1:2]
        for r in range(LANES):
            small[r, 0, 0:32] = small32[r].astype(BF16)
        acc[:, S_TOP : S_TOP + CH, :] = small[lane]
        yacc[:, DEC_ROWS - EARLY_ROWS :, :] = small[over]
        core_copy(LATE, small.at[mate]).start()
        corey_copy(LATE, small.at[cross]).start()
        for step in range(1, devices):
            dx_copy(step).start()
        dx_out[me] = dx[me]

    def core_enc(lo, hi):
        def body(m):
            block = block_of(m)

            @pl.when((block >= lo) & (block < hi))
            def _():
                src = pl.ds(pl.multiple_of(block * CH - DEC_ROWS, CH), CH)
                core_copy(m, enc_mate.at[:, src, :]).start()

        loop(ALL_K, body)

    def first_piece(i):
        del i
        for fetch in fetches[:7]:
            fetch.wait()
        ut[...] = jnp.transpose(u[...].astype(F32)).astype(BF16)
        give_enc().wait_recv()
        gt[...] = jnp.transpose(gb[...].astype(F32)).astype(BF16)

    pieces = [(WAIT, WAIT + 1, first_piece)]
    for g, down in enumerate((down0, down1)):
        pieces.append((WAIT, WAIT + 3, lambda i, g=g, down=down: ff_back(g, i, down)))
    pieces.append((WAIT + 3, WAIT + 4, lambda i: core_enc(DEC_K, DEC_K + ENC_A // CH)))
    pieces.append((WAIT + 3, WAIT + 4, lambda i: loop(D // 256, ff_in)))
    pieces.append((WAIT + 6, WAIT + 7, norm_two))
    for g, proj in enumerate((proj0, proj1)):
        low = WAIT + 7 + g
        pieces.append((low, low + 1, lambda i, g=g, proj=proj: attention(g, proj)))
    pieces.append((WAIT + 9, WAIT + 10, lambda i: loop(D // 256, project_in)))
    for g in range(2):
        low = WAIT + 10 + g
        pieces.append((low, low + 1, lambda i, g=g: project_grad(g)))
    pieces.append((WAIT + 12, WAIT + 13, lambda i: core_enc(DEC_K + ENC_A // CH, B_K)))
    pieces.append((WAIT + 13, WAIT + 14, norm_one))

    def dx_copy(step):
        peer, place = group_peer(step)
        return far(dx.at[peer], dx_out.at[me], dx_s.at[step], dx_r.at[step], place)

    def emb_copy(step):
        return far(
            out.at[:, pl.ds(512, CH), :], emb.at[lane], emb_s.at[step], emb_r.at[step],
            {"tensor": lax.rem(lane + step, LANES)},
        )

    def block_of(m):
        even = lax.rem(m - EARLY, 2) == 0
        turn = jnp.where(even, EARLY + lax.div(m - EARLY, 2), DEC_K + lax.div(m - EARLY - 1, 2))
        late = jnp.where(m == LATE, ALL_K - 1, jnp.where(m > LATE, m - 1, m))
        return jnp.where(m < EARLY, m, jnp.where(m >= MIXED, late, turn))

    def is_dec(m):
        return (block_of(m) < DEC_K) & (m >= EARLY)

    def with_y(m):
        return is_dec(m) | (m == LATE)

    def at(m):
        return pl.ds(pl.multiple_of(block_of(m) * CH, CH), CH)

    def pair_at(m):
        return rows(jnp.where(m < HALVED, lax.div(m, 2), m - HALVED // 2))

    def y_at(m):
        return rows(jnp.minimum(block_of(m), DEC_K) - EARLY)

    def core_copy(m, src):
        return far(src, out.at[:, at(m), :], core_s.at[m], core_r.at[m], {"tensor": mate})

    def corey_copy(m, src):
        return far(src, rcy.at[:, y_at(m), :], corey_s.at[m], corey_r.at[m], {"tensor": mate})

    def y_copy(m):
        cut = y_at(m)
        return far(
            yacc.at[:, cut, :], ry.at[:, cut, :], y_s.at[m], y_r.at[m], {"tensor": over}
        )

    def x_copy(m):
        return far(
            acc.at[1 - sec, at(m), :], rx.at[pair_at(m), :], x_s.at[m], x_r.at[m],
            {"section": 1 - sec},
        )

    def xc_copy(m):
        return far(
            acc.at[:, at(m), :], xc.at[:, pair_at(m), :], x_s.at[m], x_r.at[m],
            {"section": 1 - sec},
        )

    def z_copy(m, whole, right):
        if whole:
            src, dst = acc.at[:, at(m), :], (cl if right else cr).at[:, pair_at(m), :]
        else:
            src, dst = acc.at[sec, at(m), :], (zl if right else zr).at[pair_at(m), :]
        landed = zl_r if right else zr_r
        return far(src, dst, z_s.at[m], landed.at[m], {"dp": pos + 1 if right else pos - 1})

    def b_copy(m, whole, right):
        place = out.at[:, at(m), :] if whole else out.at[sec, at(m), :]
        sent = br_s if right else bl_s
        return far(place, place, sent.at[m], b_r.at[m], {"dp": pos + 1 if right else pos - 1})

    def a_copy(m):
        place = out.at[sec, at(m), :]
        return far(place, place, a_s.at[m], a_r.at[m], {"section": 1 - sec})

    def a_wait(m):
        place = out.at[1 - sec, at(m), :]
        far(place, place, a_s.at[m], a_r.at[m], {"section": 1 - sec}).wait_recv()

    give_enc().start()

    def start_core(m):
        @pl.when(is_dec(m))
        def _():
            core_copy(m, dec.at[mate, :, at(m), :]).start()
            corey_copy(m, dec.at[cross, :, at(m), :]).start()

    loop(MIXED, start_core)
    for load in loads:
        load.wait()

    def stage_c(m):
        @pl.when(m >= EARLY)
        def _():
            core_copy(m, out.at[:, at(m), :]).wait_recv()
            acc[:, at(m), :] = add(acc[:, at(m), :], out[:, at(m), :])

        @pl.when(with_y(m))
        def _():
            corey_copy(m, rcy.at[:, y_at(m), :]).wait_recv()
            yacc[:, y_at(m), :] = add(yacc[:, y_at(m), :], rcy[:, y_at(m), :])
            y_copy(m).start()

    def finished(m):
        @pl.when(block_of(m) == DEC_K - 1)
        def _():
            for step in range(1, LANES):
                emb_copy(step).start()
            emb[lane] = out[:, 512 : 512 + CH, :]

    def line_of(root, whole):
        left = pos < root
        right = pos > root
        here = pos == root
        reach = max(root, count - 1 - root)
        level = jnp.where(left, pos, jnp.where(right, count - 1 - pos, reach))
        dist = jnp.where(left, root - pos, pos - root)

        def view(ref, m):
            return ref.at[:, at(m), :] if whole else ref.at[sec, at(m), :]

        def landed(ref, m):
            return ref.at[:, pair_at(m), :] if whole else ref.at[pair_at(m), :]

        from_left, from_right = (cl, cr) if whole else (zl, zr)

        def outer(m):
            @pl.when(left & first)
            def _():
                z_copy(m, whole, True).start()

            @pl.when(right & last)
            def _():
                z_copy(m, whole, False).start()

        def inward(m):
            @pl.when(left & (pos > 0))
            def _():
                z_copy(m, whole, True).wait_recv()
                view(acc, m)[...] = add(view(acc, m)[...], landed(from_left, m)[...])
                z_copy(m, whole, True).start()

            @pl.when(right & (pos < count - 1))
            def _():
                z_copy(m, whole, False).wait_recv()
                view(acc, m)[...] = add(view(acc, m)[...], landed(from_right, m)[...])
                z_copy(m, whole, False).start()

            @pl.when(here)
            def _():
                total = view(acc, m)[...].astype(F32)
                if root > 0:
                    z_copy(m, whole, True).wait_recv()
                    total = total + landed(from_left, m)[...].astype(F32)
                if root < count - 1:
                    z_copy(m, whole, False).wait_recv()
                    total = total + landed(from_right, m)[...].astype(F32)
                if whole:
                    view(acc, m)[...] = total.astype(BF16)
                    xc_copy(m).start()
                else:
                    view(out, m)[...] = total.astype(BF16)
                    spread(m)
                    a_copy(m).start()

        def spread(m):
            if root > 0:
                b_copy(m, whole, False).start()
            if root < count - 1:
                b_copy(m, whole, True).start()

        def crossed(m):
            xc_copy(m).wait_recv()
            view(out, m)[...] = add(view(acc, m)[...], landed(xc, m)[...])
            spread(m)
            finished(m)

        def outward(m):
            b_copy(m, whole, False).wait_recv()

            @pl.when(left & (pos > 0))
            def _():
                b_copy(m, whole, False).start()

            @pl.when(right & (pos < count - 1))
            def _():
                b_copy(m, whole, True).start()

            if whole:
                finished(m)
            else:
                a_copy(m).start()

        def sent(m):
            @pl.when(jnp.logical_not(here))
            def _():
                z_copy(m, whole, True).wait_send()

            @pl.when((pos <= root) & (pos > 0))
            def _():
                b_copy(m, whole, False).wait_send()

            @pl.when((pos >= root) & (pos < count - 1))
            def _():
                b_copy(m, whole, True).wait_send()

            if whole:
                @pl.when(here)
                def _():
                    xc_copy(m).wait_send()
            else:
                x_copy(m).wait_send()
                a_copy(m).wait_send()

        def add_y(m):
            @pl.when(with_y(m))
            def _():
                y_copy(m).wait_recv()
                acc[:, at(m), :] = add(acc[:, at(m), :], ry[:, y_at(m), :])

            set_off(m)

        def set_off(m):
            if whole:
                outer(m)
            else:
                x_copy(m).start()

        def add_x(m):
            x_copy(m).wait_recv()
            acc[sec, at(m), :] = add(acc[sec, at(m), :], rx[pair_at(m), :])
            outer(m)

        def last_half(m):
            a_wait(m)
            finished(m)

        base = 1 if whole else 2
        back = base + reach + dist + (1 if whole else 0)
        steps = [(back, jnp.logical_not(here), outward), (base + level, level > 0, inward)]
        if whole:
            steps.append((base + reach + 1, here, crossed))
        else:
            steps += [(back + 1, True, last_half), (2, True, add_x)]
        return steps, sent, add_y, set_off

    low_root = (count - 1) // 2
    high_root = min(low_root + 1, count - 1)
    lines = [
        (lambda m: (lax.rem(m, 2) == 1) | (m >= HALVED), *line_of(low_root, False)),
        (lambda m: (lax.rem(m, 4) == 0) & (m < HALVED), *line_of(low_root, True)),
        (lambda m: (lax.rem(m, 4) == 2) & (m < HALVED), *line_of(high_root, True)),
    ]

    def finish(m):
        @pl.when(m >= EARLY)
        def _():
            core_copy(m, out.at[:, at(m), :]).wait_send()

        @pl.when(with_y(m))
        def _():
            corey_copy(m, rcy.at[:, y_at(m), :]).wait_send()
            y_copy(m).wait_send()

        for mine, _, sent, _, _ in lines:
            @pl.when(mine(m))
            def _(sent=sent):
                sent(m)

    far_reach = max(low_root, count - 1 - low_root, high_root, count - 1 - high_root)
    depth = LAG * (3 + 2 * far_reach) + 1

    def tick(n):
        @pl.when(n < LATE)
        def _():
            for low, high, piece in pieces:
                @pl.when((n >= low) & (n < high))
                def _(low=low, piece=piece):
                    piece(n - low)

        for mine, steps, _, add_y, _ in lines:
            m = n - LAG

            @pl.when((m >= EARLY) & (m < ALL_K) & mine(m))
            def _(m=m, add_y=add_y):
                add_y(m)

            for offset, enabled, stage in steps:
                m = n - LAG * offset

                @pl.when((m >= 0) & (m < ALL_K) & mine(m) & enabled)
                def _(m=m, stage=stage):
                    stage(m)

        @pl.when(n < ALL_K)
        def _():
            stage_c(n)

        @pl.when(n >= depth)
        def _():
            finish(n - depth)

    def set_off_early(m):
        for mine, _, _, _, set_off in lines:
            @pl.when(mine(m))
            def _(set_off=set_off):
                set_off(m)

    loop(EARLY, set_off_early)
    loop(ALL_K + depth, tick)

    for step in range(1, devices):
        dx_copy(step).wait()
    for step in range(1, LANES):
        emb_copy(step).wait()
    give_enc().wait_send()
    for k in range(D // 256):
        give_part(k, 0).wait_send()
        give_part(k, 1).wait_send()
        give_last(k).wait_send()


def backward_call(args, half, hid):
    dma = lambda *s: pltpu.SemaphoreType.DMA(s)
    vm = pltpu.VMEM
    full = ALL_K * CH
    y_half = DEC_ROWS - EARLY_ROWS + CH
    whole = HALVED // 2 * CH
    by_half = full - whole
    k = ALL_K
    rows = 2 * PAD
    cut = D // (2 * LANES)
    specs = [VM, VM] + [ANY] * 18 + [VM] * 3
    return pl.pallas_call(
        backward_and_sums,
        out_shape=[
            jax.ShapeDtypeStruct((2, full, D), BF16),
            jax.ShapeDtypeStruct((LANES, 2, CH, D), BF16),
            jax.ShapeDtypeStruct((2 * LANES, cut, VIS), BF16),
        ],
        in_specs=specs,
        out_specs=[VM] * 3,
        scratch_shapes=[
            vm((rows, D), BF16), vm((D, rows), BF16), vm((D, rows), BF16),
            vm((rows, D), F32), vm((rows, D), BF16), vm((rows, D), BF16),
            vm((2, rows, hid), BF16), vm((rows, D), BF16), vm((rows, D), F32),
            vm((rows, half), BF16), vm((2, 3, rows, half), BF16),
            vm((PAD, D), F32), vm((PAD, D), BF16), vm((PAD, D), BF16), vm((PAD, D), F32),
            vm((2 * LANES, cut, VIS), BF16),
            vm((2, 1, hid), F32), vm((2, 2, half), F32), vm((8, D), F32),
            vm((2, full, D), BF16), vm((2, y_half, D), BF16), vm((2, ENC_A + ENC_B, D), BF16),
            vm((2, y_half, D), BF16), vm((2, y_half, D), BF16),
            vm((by_half, D), BF16), vm((by_half, D), BF16), vm((by_half, D), BF16),
            vm((2, whole, D), BF16), vm((2, whole, D), BF16), vm((2, whole, D), BF16),
            vm((LANES, 32, D), F32), vm((LANES, 2, CH, D), BF16),
            *[vm(v.shape, v.dtype) for v in args[2:19]], dma(17), dma(2), dma(10), dma(10),
            dma(k), dma(k), dma(k), dma(k), dma(k), dma(k),
            dma(k), dma(k), dma(k), dma(k), dma(k),
            dma(k), dma(k), dma(k), dma(k), dma(k), dma(LANES), dma(LANES),
            dma(2 * LANES), dma(2 * LANES),
        ],
        compiler_params=pltpu.CompilerParams(
            collective_id=1, has_side_effects=True, vmem_limit_bytes=VMEM_LIMIT
        ),
    )(*args)


def finish_grads(
    total_h, emb_h, decoded, dx, *refs,
):
    (
        decoded_out, dx_out,
        e_qkv_h, e_qvb, e_proj_h, e_up_h, e_upb, e_down_h, e_gain, e_off,
        d_qkv_h, d_qvb, d_proj_h, d_up_h, d_upb, d_down_h, d_gain, d_off, d_ew_h, d_ev,
        total, emb, e_qkv, e_proj, e_up, e_down, d_qkv, d_proj, d_up, d_down, d_ew, in_s, out_s,
    ) = refs
    half = e_proj.shape[0]
    spots = ((A_TOP, B_TOP), (B_TOP, S_TOP + CH), (0, A_TOP))
    loads = [
        pltpu.make_async_copy(
            total_h.at[:, low:high, :], total.at[:, low:high, :], in_s.at[n]
        )
        for n, (low, high) in enumerate(spots)
    ] + [pltpu.make_async_copy(emb_h, emb, in_s.at[3])]
    for load in loads:
        load.start()
    stores = []

    def store(src, dst):
        copy = pltpu.make_async_copy(src, dst, out_s.at[len(stores)])
        copy.start()
        stores.append(copy)

    decoded_out[...] = decoded[...]
    dx_out[...] = dx[...]
    loads[0].wait()
    e_up[...] = total[0, A_TOP:B_TOP, :].astype(F32)
    store(e_up, e_up_h)
    e_down[...] = jnp.transpose(total[1, A_TOP:B_TOP, :].astype(F32))
    store(e_down, e_down_h)
    loads[1].wait()
    e_qkv[0] = total[0, B_TOP : B_TOP + half, :].astype(F32)
    e_qkv[1] = total[0, B_TOP + half : S_TOP, :].astype(F32)
    e_qkv[2] = total[1, B_TOP : B_TOP + half, :].astype(F32)
    store(e_qkv, e_qkv_h)
    e_proj[...] = total[1, B_TOP + half : S_TOP, :].astype(F32)
    store(e_proj, e_proj_h)
    loads[3].wait()
    for k in range(LANES):
        for h in range(2):
            top = k * 192 + h * 64
            d_ew[top : top + 64, :] = emb[k, h, :, 0:512].astype(F32)
            d_ew[k * 192 + 128 : (k + 1) * 192, h * 256 : (h + 1) * 256] = emb[
                k, h, :, 512:768
            ].astype(F32)
    store(d_ew, d_ew_h)
    loads[2].wait()

    def tile(number):
        h, top, col = tile_of(number)
        return total[h, top : top + CH, col : col + 256].astype(F32)

    for block in range(GRID // CH):
        rows = slice(block * CH, (block + 1) * CH)
        side = slice(block // 2 * 128, (block // 2 + 1) * 128)
        for k in range(2):
            d_up[rows, k * 256 : (k + 1) * 256] = tile(4 * block + k)
            if block % 2:
                both = jnp.concatenate([tile(4 * block - 2 + k), tile(4 * block + 2 + k)], 0)
                d_down[k * 256 : (k + 1) * 256, side] = jnp.transpose(both)
        one, two = tile(32 + 2 * block), tile(33 + 2 * block)
        d_qkv[0, rows, :] = one[:, 0:128]
        d_qkv[1, rows, :] = one[:, 128:256]
        d_qkv[2, rows, :] = two[:, 0:128]
        d_proj[block % 2 * CH : (block % 2 + 1) * CH, side] = two[:, 128:256]
    for src, dst in ((d_up, d_up_h), (d_down, d_down_h), (d_qkv, d_qkv_h), (d_proj, d_proj_h)):
        store(src, dst)
    little = total[0, S_TOP : S_TOP + 32, :].astype(F32)
    d_upb[...] = little[0, 0:512]
    d_qvb[0:1, :] = little[1:2, 0:128]
    d_qvb[1:2, :] = little[1:2, 128:256]
    e_upb[...] = little[2]
    e_qvb[0:1, :] = little[3:4, 0:192]
    e_qvb[1:2, :] = little[3:4, 256:448]
    d_gain[...] = little[8:10, 0:512]
    d_off[...] = little[10:14, 0:512]
    d_ev[...] = little[14:16, 0:512]
    e_gain[...] = little[16:18]
    e_off[...] = little[18:22]
    for copy in stores:
        copy.wait()


def finish_call(total, emb, decoded, dx, shapes):
    large = (0, 2, 3, 5, 8, 10, 11, 13, 16)
    order = (0, 2, 3, 5, 8, 10, 11, 13, 16)
    vm = pltpu.VMEM
    return pl.pallas_call(
        finish_grads,
        out_shape=[jax.ShapeDtypeStruct(v.shape, v.dtype) for v in (decoded, dx)]
        + [jax.ShapeDtypeStruct(s, F32) for s in shapes],
        in_specs=[ANY, ANY, VM, VM],
        out_specs=[VM, VM] + [ANY if n in large else VM for n in range(len(shapes))],
        scratch_shapes=[vm(total.shape, BF16), vm(emb.shape, BF16)]
        + [vm(shapes[n], F32) for n in order]
        + [pltpu.SemaphoreType.DMA((4,)), pltpu.SemaphoreType.DMA((9,))],
        compiler_params=pltpu.CompilerParams(vmem_limit_bytes=VMEM_LIMIT),
    )(total, emb, decoded, dx)


def position_rows():
    quarter = DD // 4
    freq = np.exp(np.arange(quarter, dtype=np.float32) * np.float32(-math.log(10000.0) / quarter))
    angle = np.arange(PAD, dtype=np.float32)[:, None] * freq[None, :].astype(np.float32)
    both = np.concatenate([np.sin(angle), np.cos(angle)], 1).astype(np.float32)
    high = both.astype(jnp.bfloat16)
    low = (both - high.astype(np.float32)).astype(jnp.bfloat16)
    return np.stack([high, low])


def per_device(
    patches, cotangent, widths, visible, window_shift, batch_order,
    encoder_qkv, encoder_qvbias, encoder_proj, encoder_up, encoder_upbias, encoder_down,
    encoder_gains, encoder_offsets,
    decoder_qkv, decoder_qvbias, decoder_proj, decoder_up, decoder_upbias, decoder_down,
    decoder_gains, decoder_offsets, embed_weight, embed_vectors,
):
    qkv0 = encoder_qkv.transpose(1, 2, 0)
    half = qkv0.shape[1]
    hid = encoder_up.shape[1]
    dff = decoder_up.shape[1] * LANES
    flat = patches.transpose(1, 0, 2).reshape(-1, D)
    (
        x, x1, a, u, y, gp, qkv, p, o, qkv1, proj1, up1, down1, dec_buf,
        d_enc, d_dqvb, d_dupb, d_dsmall, out_all,
    ) = forward_call(
        (
            widths, window_shift.T, batch_order, visible, flat, encoder_gains, encoder_offsets,
            encoder_qvbias, encoder_upbias, decoder_qvbias, decoder_upbias,
            qkv0, encoder_proj, encoder_up, encoder_down,
            decoder_qkv.transpose(1, 0, 2), decoder_proj, decoder_up, decoder_down,
            cotangent, embed_weight, embed_vectors, jnp.asarray(position_rows()),
            decoder_gains, decoder_offsets,
        ),
        half, hid, dff,
    )
    total, emb, dx_all = backward_call(
        (
            d_enc, encoder_gains, u, y, gp, encoder_down, down1, encoder_up, up1,
            x, x1, a, qkv, p, o, qkv0, qkv1, encoder_proj, proj1,
            dec_buf, d_dqvb, d_dupb, d_dsmall,
        ),
        half, hid,
    )
    out_all, dx_all, *grads = finish_call(
        total, emb, out_all, dx_all,
        [
            (3, half, D), (2, half), (half, D), (D, hid), (hid,), (hid, D), (2, D), (4, D),
            (3, DD, 128), (2, 128), (128, DD), (DD, 512), (512,), (512, DD), (2, DD), (4, DD),
            (D, DD), (2, DD),
        ],
    )
    grads[0] = grads[0].transpose(2, 0, 1)
    grads[8] = grads[8].transpose(1, 0, 2)
    return (out_all.swapaxes(1, 2), dx_all.swapaxes(1, 2), *grads)


def solution(mesh):
    weights = (
        P(None, None, "tensor"), P(None, "tensor"), P("tensor", None), P(None, "tensor"),
        P("tensor"), P("tensor", None), P(), P(),
    )
    split = P("dp", None, ("section", "tensor"))
    return jax.shard_map(
        per_device,
        mesh=mesh,
        in_specs=(
            P("dp", None, None), P("dp", None, None), P("dp"), P("dp", None), P("dp", None),
            P("dp", None),
        ) + weights + weights + (P(), P()),
        out_specs=(split, split) + weights + weights + (P(), P()),
        check_vma=False,
    )
```

```python
import math

import jax
import jax.numpy as jnp
import numpy as np
from jax import lax
from jax.experimental import pallas as pl
from jax.experimental.pallas import tpu as pltpu
from jax.sharding import PartitionSpec as P

D = 768
HEADS = 12
DD = 512
DHEADS = 16
GRID_ROWS = 64
WIDE = 8
WIN = 4
VIS = 102
CM = 4
GRID = 512
LANES = 4
PAD = 128
EPS = 1e-06
NEG = -10000.0
F32 = jnp.float32
BF16 = jnp.bfloat16
VMEM_LIMIT = 60 * 1024 * 1024

VM = pl.BlockSpec(memory_space=pltpu.VMEM)
SM = pl.BlockSpec(memory_space=pltpu.SMEM)
ANY = pl.BlockSpec(memory_space=pl.ANY)


def nn(a, b):
    return lax.dot_general(a, b, (((1,), (0,)), ((), ())), preferred_element_type=F32)


def nt(a, b):
    return lax.dot_general(a, b, (((1,), (1,)), ((), ())), preferred_element_type=F32)


def tn(a, b):
    return lax.dot_general(a, b, (((0,), (0,)), ((), ())), preferred_element_type=F32)


def loop(count, body, unroll=1):
    def step(i, carry):
        body(i)
        return carry

    lax.fori_loop(0, count, step, 0, unroll=unroll)


def span(i, size):
    return pl.ds(pl.multiple_of(i * size, size), size)


def normal(x):
    center = x - jnp.mean(x, -1, keepdims=True)
    scale = lax.rsqrt(jnp.mean(center * center, -1, keepdims=True) + EPS)
    return center * scale, scale


def normal_back(dy, hat, scale, gain):
    d = dy * gain
    return scale * (
        d - jnp.mean(d, -1, keepdims=True) - hat * jnp.mean(d * hat, -1, keepdims=True)
    )


def gelu_both(h):
    phi = 0.5 * lax.erf(h * math.sqrt(0.5)) + 0.5
    bell = jnp.exp2(h * h * (-0.5 * math.log2(math.e)))
    return h * phi, phi + h * bell * (1.0 / math.sqrt(2.0 * math.pi))


def colsum(x):
    return jnp.sum(x, 0, keepdims=True)


def head_marks(width, size, dtype):
    lane = lax.broadcasted_iota(jnp.int32, (1, width), 1)
    return [((lane >= h * size) & (lane < (h + 1) * size)).astype(dtype) for h in range(width // size)]


def stacked(x, marks):
    return jnp.concatenate([x * m for m in marks], 0)


LOG2E = math.log2(math.e)


def attend(q, k, v, marks, ones, masked, scale):
    keys = k.shape[0]
    s = nt(q, stacked(k, marks))
    parts = []
    for h in range(len(marks)):
        x = masked(s[:, h * keys : (h + 1) * keys] * (scale * LOG2E))
        parts.append(jnp.exp2(x - jnp.max(x, -1, keepdims=True)).astype(BF16))
    e = jnp.concatenate(parts, 1)
    width = q.shape[1]
    if width % 128:
        top, total = nn(e, stacked(v, marks)), nn(e, ones)
    else:
        both = nn(e, jnp.concatenate([stacked(v, marks), ones], 1))
        top, total = both[:, :width], both[:, width:]
    inverse = 1.0 / total
    return e, (top * inverse).astype(BF16), inverse


def attend_back(q, k, v, e, o, inverse, d_out, marks, marks32, rows32, ones, scale):
    keys = k.shape[0]
    width = q.shape[1]
    d_one = d_out.astype(F32) * inverse
    d_two = (d_one * o.astype(F32)).astype(BF16)
    d_one = d_one.astype(BF16)
    if width % 128:
        d_s = nt(d_one, stacked(v, marks)) - nt(d_two, ones)
    else:
        d_s = nt(
            jnp.concatenate([d_one, d_two], 1), jnp.concatenate([stacked(v, marks), -ones], 1)
        )
    dr = (e.astype(F32) * d_s * scale).astype(BF16)
    d_q = nn(dr, stacked(k, marks)).astype(BF16)
    if width % 128:
        d_k_all, d_v_all = tn(dr, q), tn(e, d_one)
        d_k = d_v = 0.0
        for h in range(len(marks)):
            cut = slice(h * keys, (h + 1) * keys)
            d_k += d_k_all[cut] * marks32[h]
            d_v += d_v_all[cut] * marks32[h]
        return d_q, d_k.astype(BF16), d_v.astype(BF16)
    d_k_all = nn(jnp.transpose(q.astype(F32)).astype(BF16), dr)
    d_v_all = nn(jnp.transpose(d_one.astype(F32)).astype(BF16), e)
    d_k = d_v = 0.0
    for h in range(len(marks)):
        cut = slice(h * keys, (h + 1) * keys)
        d_k += d_k_all[:, cut] * rows32[h]
        d_v += d_v_all[:, cut] * rows32[h]
    return d_q, jnp.transpose(d_k).astype(BF16), jnp.transpose(d_v).astype(BF16)


def ones_per_head(keys, marks):
    return jnp.concatenate([jnp.broadcast_to(m, (keys, m.shape[1])) for m in marks], 0)


ENC_SIZE = D // HEADS
ENC_SCALE = ENC_SIZE ** -0.5
DEC_SIZE = DD // DHEADS
DEC_SCALE = DEC_SIZE ** -0.5


CH = 64
DEC_ROWS = 576
ENC_A = 768
ENC_B = 384
DEC_K = DEC_ROWS // CH
B_K = (DEC_ROWS + ENC_A + ENC_B) // CH
ALL_K = B_K + 1
A_TOP = DEC_ROWS
B_TOP = DEC_ROWS + ENC_A
S_TOP = B_TOP + ENC_B
EARLY = 4
EARLY_ROWS = EARLY * CH
LAG = 2
ORDER = (0, 1, 2, 3, 4, 9, 10, 11, 12, 13, 14, 15, 16, 5, 17, 6, 7, 18, 19, 8, 21, 22, 23, 27, 20, 24, 25, 26)
PIECES = (0, 0, 0, 2, 2, 4, 4, 5, 5, 11, 11, 13, 15, 15, 15, 17, 17, 17, 17, 17, 17, 19, 20)
LATE = ORDER.index(B_K)
HALVED = ALL_K - 4


def tile_of(number):
    place = number // 3
    return place % 2, place // 2 * CH, number % 3 * 256


MESH = pl.DeviceIdType.MESH


def far(src, dst, send, recv, peer):
    return pltpu.make_async_remote_copy(
        src_ref=src, dst_ref=dst, send_sem=send, recv_sem=recv, device_id=peer, device_id_type=MESH
    )


def forward_and_decoder(
    wid, shifts, order, vis, pat, gains, offs, b_qv, b_up, b_dqv, b_dup,
    h_qkv, h_proj, h_up, h_down, h_dqkv, h_dproj, h_dup, h_ddown,
    cot_hbm, ew, evec, table, dgains, doffs,
    o_x, o_x1, o_a, o_u, o_y, o_gp, o_qkv, o_p, o_o, o_w, o_wproj, o_wup, o_wdown, o_dec,
    d_enc, d_qvb, d_upb, d_small, dec_out,
    w_qkv, w_proj, w_up, w_down, bias, biases, qkv, proj, up, down,
    ex, ea, eu, ey, egp, eqkv, ep, eo, ex1, epart, esend, erecv, esend2, erecv2, eown,
    cot, x0, x1, a, acts, probs, o, inverse, u, ut, y, gp, g32, gb, gt, acc, e_ref, hot, perm, buf, dsend, e_rc, e_rcy, e_ry,
    load_s, out_s, cot_s, w_s, w_r, bias_s, bias_r, dw_s, dw_r, ex_s, ex_r, ex2_s, ex2_r, do_s, do_r, e_s, e_r,
):
    sec = lax.axis_index("section")
    lane = lax.axis_index("tensor")
    mate = lane + 1 - 2 * lax.rem(lane, 2)
    over = lax.rem(lane + 2, LANES)
    cross = lax.rem(mate + 2, LANES)
    me = sec * LANES + lane
    devices = 2 * LANES
    clip = me
    clips = (me, sec * LANES + over)

    def group_peer(step):
        peer = lax.rem(me + step, devices)
        return peer, {"section": lax.div(peer, LANES), "tensor": lax.rem(peer, LANES)}

    own = [
        pltpu.make_async_copy(src, dst.at[0], load_s.at[n])
        for n, (src, dst) in enumerate(
            ((h_qkv, w_qkv), (h_proj, w_proj), (h_up, w_up), (h_down, w_down))
        )
    ]

    def place(n, shard, part=None):
        thick = (128, 128, 512, 512)[n]
        base = shard * thick
        cut = pl.ds(pl.multiple_of(base, thick), thick)
        if part is None:
            return (qkv.at[:, :, cut], proj.at[cut, :], up.at[:, cut], down.at[cut, :])[n]
        some = span(part, (256, 64, 256, 256)[n])
        if n == 0:
            return qkv.at[:, some, cut]
        if n == 2:
            return up.at[some, cut]
        few = thick // 2
        rows = pl.ds(pl.multiple_of(base + part * few, few), few)
        return (proj if n == 1 else down).at[rows, :]

    shards = (h_dqkv, h_dproj, h_dup, h_ddown)
    keep = [
        pltpu.make_async_copy(shards[n], place(n, lane), load_s.at[4 + n]) for n in range(4)
    ]
    for copy in own + keep:
        copy.start()
    fetch = pltpu.make_async_copy(cot_hbm.at[clip], cot, cot_s)
    fetch.start()

    barrier = pltpu.get_barrier_semaphore()
    for step in range(1, devices):
        pl.semaphore_signal(barrier, inc=1, device_id_type=MESH, device_id=group_peer(step)[1])
    bias[...] = jnp.zeros_like(bias)
    half = w_proj.shape[1]
    bias[0:1, :] = b_up[...].astype(F32).reshape(1, -1)
    bias[1:3, 0:half] = b_qv[...].astype(F32)
    bias[3:4, 0:512] = b_dup[...].astype(F32).reshape(1, -1)
    bias[4:6, 0:128] = b_dqv[...].astype(F32)
    biases[lane] = bias[...]
    pl.semaphore_wait(barrier, devices - 1)

    def enc_weight(n):
        src = (h_qkv, h_proj, h_up, h_down)[n]
        dst = (w_qkv, w_proj, w_up, w_down)[n]
        return far(src, dst.at[1], w_s.at[n], w_r.at[n], {"tensor": mate})

    def bias_copy(step):
        return far(
            bias, biases.at[lane], bias_s.at[step], bias_r.at[step],
            {"tensor": lax.rem(lane + step, LANES)},
        )

    def half_of(n):
        some = span(sec, (256, 64, 256, 256)[n])
        return shards[n].at[:, some, :] if n == 0 else shards[n].at[some, :]

    def dec_weight(n, kind):
        peer = {"section": 1 - sec} if kind == 2 else {"tensor": over if kind == 0 else mate}
        if kind == 0:
            src, dst = half_of(n), place(n, lane, sec)
        elif kind == 1:
            src, dst = shards[n], place(n, lane)
        else:
            src = dst = place(n, over, 1 - sec if kind == 4 else sec)
        return far(src, dst, dw_s.at[5 * n + kind], dw_r.at[5 * n + kind], peer)

    enc_weight(0).start()
    for step in range(1, LANES):
        bias_copy(step).start()
    enc_weight(1).start()
    dec_weight(0, 0).start()
    enc_weight(2).start()
    enc_weight(3).start()
    for n in range(4):
        dec_weight(n, 1).start()

    def pass_on(n):
        dec_weight(n, 0).wait_recv()
        dec_weight(n, 2).start()
        dec_weight(n, 3).start()

    def pass_last(n):
        dec_weight(n, 2).wait_recv()
        dec_weight(n, 4).start()

    def arrived(n):
        keep[n].wait()
        dec_weight(n, 1).wait_recv()
        dec_weight(n, 3).wait_recv()
        dec_weight(n, 4).wait_recv()

    width = wid[clip]
    bits = jnp.where(width == WIDE, 3, 2)
    turn = shifts[0, clip] * width
    mod = GRID - 1
    spot = 0
    for i in range(order.shape[1]):
        spot = spot + jnp.where(order[0, i] == clip, i, 0)
    batch = spot // CM
    count = 0
    for i in range(order.shape[1]):
        count = count + jnp.where(batch == i // CM, wid[order[0, i]], 0)
    factor_rows = CM * GRID / (jnp.full((1, 1), count, jnp.int32) * GRID_ROWS).astype(F32)

    def slot_of(index):
        return (index - turn) & mod

    def code_of(slot):
        band = ((slot >> bits) + shifts[0, clip]) >> 2
        strip = ((slot & (width - 1)) + shifts[1, clip]) >> 2
        return band * 4 + strip

    def valid_rows():
        slot = slot_of(lax.broadcasted_iota(jnp.int32, (GRID, 1), 0))
        return (slot < GRID_ROWS * width).astype(F32)

    def clip_gradient():
        fetch.wait()
        rolled = slot_of(lax.broadcasted_iota(jnp.int32, (GRID, GRID), 0))
        column = lax.broadcasted_iota(jnp.int32, (GRID, GRID), 1)
        perm[...] = (rolled == column).astype(F32).astype(BF16)
        g = nn(perm[...], cot[...]) * valid_rows() * factor_rows
        g32[...] = g
        gb[...] = g.astype(BF16)
        gt[...] = jnp.transpose(g).astype(BF16)
        d_small[...] = jnp.zeros_like(d_small)
        d_small[5:6, :] = colsum(g)

    seen = vis[pl.ds(clip, 1), :]
    target = jnp.concatenate([(seen + turn) & mod, jnp.full((1, PAD - VIS), -1, jnp.int32)], 1)

    def places(i):
        r = span(i, PAD)
        index = lax.broadcasted_iota(jnp.int32, (PAD, PAD), 0) + i * PAD
        column = lax.broadcasted_iota(jnp.int32, (PAD, PAD), 1)
        hot[r, :] = (index == target).astype(F32).astype(BF16)
        slot = slot_of(index)
        by_row = ((slot >> bits) == column).astype(F32).astype(BF16)
        by_col = ((slot & (width - 1)) == column).astype(F32).astype(BF16)
        row_part = nn(by_row, table[0]) + nn(by_row, table[1])
        col_part = nn(by_col, table[0]) + nn(by_col, table[1])
        x0[r, :] = jnp.concatenate([row_part, col_part], 1)

    egain = gains[...].astype(F32)
    eoff = offs[...].astype(F32)
    stride = pat.shape[0] // VIS
    for c in range(2):
        row = lax.broadcasted_iota(jnp.int32, (PAD, pat.shape[0]), 0)
        col = lax.broadcasted_iota(jnp.int32, (PAD, pat.shape[0]), 1)
        pick = (col == row * stride + clips[c]).astype(F32).astype(BF16)
        ex[c * PAD : (c + 1) * PAD, :] = nn(pick, pat[...])

    emarks = head_marks(half, ENC_SIZE, BF16)
    key = lax.broadcasted_iota(jnp.int32, (PAD, PAD), 1)
    floor = jnp.where(key < VIS, NEG * LOG2E, -1e30)
    eones = ones_per_head(PAD, emarks)
    blocks = D // 256

    def give_part(i, side):
        cut = span(i, 256)
        return far(
            esend.at[(1 - side) * PAD : (2 - side) * PAD, cut],
            erecv.at[side * PAD : (side + 1) * PAD, cut],
            ex_s.at[2 * i + side], ex_r.at[2 * i + side], {"tensor": over},
        )

    for c in range(2):
        rows = slice(c * PAD, (c + 1) * PAD)
        hat, _ = normal(ex[rows, :])
        ea[rows, :] = (hat * egain[0:1] + eoff[0:1]).astype(BF16)
        limit = (VIS * wid[clips[c]]) // WIDE
        for g, shard in enumerate((lane, mate)):
            if c == 0 and g == 0:
                own[0].wait()
            if c == 0 and g == 1:
                enc_weight(0).wait_recv()
                for step in range(1, LANES):
                    bias_copy(step).wait_recv()
            if g == 0:
                bq, bv = bias[1:2, 0:half], bias[2:3, 0:half]
            else:
                bq, bv = biases[shard, 1:2, 0:half], biases[shard, 2:3, 0:half]
            eqkv[g, 0, rows] = (nt(ea[rows, :], w_qkv[g, 0]) + bq).astype(BF16)
            eqkv[g, 1, rows] = nt(ea[rows, :], w_qkv[g, 1]).astype(BF16)
            eqkv[g, 2, rows] = (nt(ea[rows, :], w_qkv[g, 2]) + bv).astype(BF16)
            p, out, _ = attend(
                eqkv[g, 0, rows], eqkv[g, 1, rows], eqkv[g, 2, rows], emarks, eones,
                lambda s: jnp.where(key < limit, s, floor), ENC_SCALE,
            )
            ep[g, c] = p
            eo[g, rows] = out
        if c == 0:
            own[1].wait()
            enc_weight(1).wait_recv()
        for i in range(blocks):
            cut = slice(i * 256, (i + 1) * 256)
            t = nn(eo[0, rows], w_proj[0, :, cut]) + nn(eo[1, rows], w_proj[1, :, cut])
            epart[rows, cut] = t
            esend[rows, cut] = t.astype(BF16)
            give_part(i, 1 - c).start()
    pass_on(0)
    clip_gradient()
    own[2].wait()
    enc_weight(2).wait_recv()

    def give_last(i):
        cut = span(i, 256)
        return far(
            esend2.at[:, cut], erecv2.at[:, cut], ex2_s.at[i], ex2_r.at[i], {"tensor": over}
        )

    for c in (1, 0):
        rows = slice(c * PAD, (c + 1) * PAD)
        for i in range(blocks):
            give_part(i, c).wait_recv()
        t = ex[rows, :] + epart[rows, :] + erecv[rows, :].astype(F32) + eoff[2:3]
        ex1[rows, :] = t
        hat, _ = normal(t)
        eu[rows, :] = (hat * egain[1:2] + eoff[1:2]).astype(BF16)
        for g, shard in enumerate((lane, mate)):

            def enc_ff(i, g=g, shard=shard, rows=rows):
                cut = span(i, 256)
                h = nn(eu[rows, :], w_up[g, :, cut]) + biases[shard, 0:1, cut]
                act, slope = gelu_both(h)
                ey[g, rows, cut] = act.astype(BF16)
                egp[g, rows, cut] = slope.astype(BF16)

            loop(w_up.shape[2] // 256, enc_ff, unroll=3)
        if c == 1:
            own[3].wait()
            enc_weight(3).wait_recv()
        for i in range(blocks):
            cut = slice(i * 256, (i + 1) * 256)
            t = nn(ey[0, rows], w_down[0, :, cut]) + nn(ey[1, rows], w_down[1, :, cut])
            if c == 0:
                eown[:, cut] = t
            else:
                esend2[:, cut] = t.astype(BF16)
                give_last(i).start()
        if c == 1:
            for n in (1, 2, 3):
                dec_weight(n, 0).start()
            pass_last(0)
    outs = [
        pltpu.make_async_copy(src, dst, out_s.at[n])
        for n, (src, dst) in enumerate(
            (
                (ex.at[0:PAD, :], o_x), (ex1, o_x1), (ea, o_a), (eu, o_u), (ey, o_y), (egp, o_gp),
                (eqkv, o_qkv), (ep, o_p), (eo, o_o), (w_qkv.at[1], o_w), (w_proj.at[1], o_wproj),
                (w_up.at[1], o_wup), (w_down.at[1], o_wdown),
            )
        )
    ]
    for copy in outs:
        copy.start()
    loop(GRID // PAD, places, unroll=2)
    for i in range(blocks):
        give_last(i).wait_recv()

    e_ref[...] = (ex1[0:PAD, :] + eown[...] + erecv2[...].astype(F32) + eoff[3:4]).astype(BF16)
    vec = evec[...].astype(F32)
    m = (nn(e_ref[...], ew[...]) + vec[0:1]).astype(BF16)
    gain = dgains[...].astype(F32)
    offsets = doffs[...].astype(F32)

    def start(i):
        r = span(i, PAD)
        oh = hot[r, :]
        hit = jnp.sum(oh.astype(F32), -1, keepdims=True)
        x = jnp.where(hit > 0, nn(oh, m), vec[1:2]).astype(BF16).astype(F32) + x0[r, :]
        x0[r, :] = x
        hat, _ = normal(x)
        a[r, :] = (hat * gain[0:1] + offsets[0:1]).astype(BF16)

    loop(GRID // PAD, start, unroll=2)
    arrived(0)

    def dec_bias(row, size):
        return jnp.concatenate([biases[k, row : row + 1, 0:size] for k in range(LANES)], 1)

    acts[0] = (nn(a[...], qkv[0]) + dec_bias(4, 128)).astype(BF16)
    acts[1] = nn(a[...], qkv[1]).astype(BF16)
    acts[2] = (nn(a[...], qkv[2]) + dec_bias(5, 128)).astype(BF16)
    pass_on(1)
    pass_on(2)
    marks = head_marks(128, DEC_SIZE, BF16)
    marks32 = head_marks(128, DEC_SIZE, F32)
    dim = lax.broadcasted_iota(jnp.int32, (128, 1), 0)
    rows32 = [
        ((dim >= h * DEC_SIZE) & (dim < (h + 1) * DEC_SIZE)).astype(F32) for h in range(len(marks))
    ]

    ones = ones_per_head(PAD, marks)

    def attention(i):
        r = span(i, PAD)
        row_slot = slot_of(lax.broadcasted_iota(jnp.int32, (PAD, PAD), 0) + i * PAD)
        key_slot = slot_of(lax.broadcasted_iota(jnp.int32, (PAD, PAD), 1) + i * PAD)
        allowed = (code_of(row_slot) == code_of(key_slot)) & (key_slot < GRID_ROWS * width)
        for g in range(DD // 128):
            c = slice(g * 128, (g + 1) * 128)
            probs[i, :, g * 512 : (g + 1) * 512], o[r, c], inverse[r, c] = attend(
                acts[0, r, c], acts[1, r, c], acts[2, r, c], marks, ones,
                lambda s: jnp.where(allowed, s, NEG * LOG2E), DEC_SCALE,
            )

    loop(GRID // PAD, attention, unroll=2)
    pass_last(1)
    pass_last(2)
    pass_on(3)
    arrived(1)

    def mix(i):
        r = span(i, 256)
        x = x0[r, :] + nn(o[r, :], proj[...]) + offsets[2:3]
        x1[r, :] = x
        hat, _ = normal(x)
        un = hat * gain[1:2] + offsets[1:2]
        u[r, :] = un.astype(BF16)
        ut[:, r] = jnp.transpose(un).astype(BF16)

    loop(2, mix)
    pass_last(3)
    arrived(2)

    def ff(i):
        c = span(i, 256)
        h = nn(u[...], up[:, c]) + biases[lax.div(i, 2), 3:4, span(lax.rem(i, 2), 256)]
        act, slope = gelu_both(h)
        y[:, c] = act.astype(BF16)
        gp[:, c] = slope.astype(BF16)

    loop(up.shape[1] // 256, ff, unroll=2)
    arrived(3)
    def out(i):
        c = span(i, 256)
        acc[:, c] = nn(y[...], down[:, c])

    loop(2, out)
    full = ((acc[...] + x1[...] + offsets[3:4]) * valid_rows()).astype(BF16)
    turned = tn(full, perm[...]).astype(BF16)
    for k in range(devices):
        dsend[k] = turned[k * dsend.shape[1] : (k + 1) * dsend.shape[1]]

    def decoded_copy(step):
        peer, spot = group_peer(step)
        return far(dsend.at[peer], dec_out.at[me], do_s.at[step], do_r.at[step], spot)

    for step in range(1, devices):
        decoded_copy(step).start()
    dec_out[me] = dsend[me]

    def ff_back(shard):
        for side in range(2):
            c = span(2 * shard + side, 256)
            d_down = nn(gt[...], y[:, c]).astype(BF16)
            dh = nt(gb[...], down[c, :]) * gp[:, c].astype(F32)
            d_upb[:, c] = colsum(dh)
            du = dh.astype(BF16)
            gp[:, c] = du
            d_up = nn(ut[...], du).astype(BF16)
            for block in range(GRID // CH):
                rows = slice(block * CH, (block + 1) * CH)
                h, top, col = tile_of(4 * block + side)
                buf[shard, h, top : top + CH, col : col + 256] = d_up[rows]
                h, top, col = tile_of(4 * block + 2 + side)
                buf[shard, h, top : top + CH, col : col + 256] = d_down[rows]

    def early_core(which):
        shard, land = ((mate, e_rc), (cross, e_rcy))[which]
        return far(
            buf.at[shard, :, 0:EARLY_ROWS, :], land, e_s.at[which], e_r.at[which], {"tensor": mate}
        )

    def early_y():
        return far(
            buf.at[over, :, 0:EARLY_ROWS, :], e_ry, e_s.at[2], e_r.at[2], {"tensor": over}
        )

    def early_add(shard, land):
        def body(i):
            r = span(i, CH)
            buf[shard, :, r, :] = buf[shard, :, r, :] + land[:, r, :]

        loop(EARLY_ROWS // CH, body)

    def ff_step(i):
        ff_back(jnp.where(i == 0, cross, jnp.where(i == 1, over, jnp.where(i == 2, mate, lane))))

        @pl.when(i == 1)
        def _():
            early_core(1).start()

        @pl.when(i == 2)
        def _():
            early_core(0).start()
            early_core(1).wait_recv()
            early_add(over, e_rcy)
            early_y().start()

    loop(LANES, ff_step)

    def ff_in(i):
        c = span(i, 256)
        acc[:, c] = nt(gp[...], up[c, :])

    loop(2, ff_in)

    def mix_back(i):
        r = span(i, 256)
        hat, scale = normal(x1[r, :])
        da = acc[r, :]
        dx = g32[r, :] + normal_back(da, hat, scale, gain[1:2])
        d_small[1:2, :] += colsum(da * hat)
        d_small[3:4, :] += colsum(da)
        d_small[4:5, :] += colsum(dx)
        g32[r, :] = dx
        dxb = dx.astype(BF16)
        gb[r, :] = dxb
        u[r, :] = nt(dxb, proj[...]).astype(BF16)

    loop(2, mix_back)
    early_core(0).wait_recv()
    early_add(lane, e_rc)
    d_proj = tn(o[...], gb[...]).astype(BF16)
    for block in range(GRID // CH):
        h, top, col = tile_of(33 + 2 * block)
        side = slice(block // 2 * 128, (block // 2 + 1) * 128)
        for k in range(LANES):
            row = k * 128 + block % 2 * CH
            buf[k, h, top : top + CH, col + 128 : col + 256] = d_proj[row : row + CH, side]

    def attention_back(i):
        r = span(i, PAD)
        for k in range(DD // 128):
            c = slice(k * 128, (k + 1) * 128)
            acts[0, r, c], acts[1, r, c], acts[2, r, c] = attend_back(
                acts[0, r, c], acts[1, r, c], acts[2, r, c],
                probs[i, :, k * 512 : (k + 1) * 512], o[r, c], inverse[r, c], u[r, c],
                marks, marks32, rows32, ones, DEC_SCALE,
            )

    loop(GRID // PAD, attention_back, unroll=2)
    d_qvb[0:1, :] = colsum(acts[0].astype(F32))
    d_qvb[1:2, :] = colsum(acts[2].astype(F32))

    def project_back(i):
        c = span(i, 256)
        acc[:, c] = (
            nt(acts[0], qkv[0, c, :]) + nt(acts[1], qkv[1, c, :]) + nt(acts[2], qkv[2, c, :])
        )

    loop(2, project_back)
    gt[...] = jnp.transpose(a[...].astype(F32)).astype(BF16)
    for j in range(3):
        d_qkv = nn(gt[...], acts[j]).astype(BF16)
        for block in range(GRID // CH):
            h, top, col = tile_of(32 + 2 * block + j // 2)
            col = col + j % 2 * 128
            rows = slice(block * CH, (block + 1) * CH)
            for k in range(LANES):
                buf[k, h, top : top + CH, col : col + 128] = d_qkv[rows, k * 128 : (k + 1) * 128]

    def start_back(i):
        r = span(i, PAD)
        hat, scale = normal(x0[r, :])
        da = acc[r, :]
        dx = g32[r, :] + normal_back(da, hat, scale, gain[0:1])
        d_small[0:1, :] += colsum(da * hat)
        d_small[2:3, :] += colsum(da)
        dg = dx.astype(BF16)
        gb[r, :] = dg
        hit = jnp.sum(hot[r, :].astype(F32), -1, keepdims=True)
        d_small[7:8, :] += colsum(jnp.where(hit > 0, 0.0, dg.astype(F32)))

    loop(GRID // PAD, start_back, unroll=2)
    dm = tn(hot[...], gb[...])
    d_small[6:7, :] = colsum(dm)
    dmb = dm.astype(BF16)
    d_enc[...] = nt(dmb, ew[...]).astype(BF16)
    d_ew = tn(e_ref[...], dmb).astype(BF16)
    for k in range(LANES):
        for h in range(2):
            top = k * 192 + h * 64
            buf[k, h, 512:576, 0:512] = d_ew[top : top + 64]
            buf[k, h, 512:576, 512:768] = d_ew[k * 192 + 128 : (k + 1) * 192, h * 256 : (h + 1) * 256]

    early_y().wait_recv()
    early_add(lane, e_ry)
    later = pl.ds(EARLY_ROWS, DEC_ROWS - EARLY_ROWS)
    rest = [pltpu.make_async_copy(buf.at[lane], o_dec.at[lane], out_s.at[13])] + [
        pltpu.make_async_copy(buf.at[k, :, later, :], o_dec.at[k, :, later, :], out_s.at[14 + n])
        for n, k in enumerate((mate, over, cross))
    ]
    for copy in rest:
        copy.start()
    for copy in outs + rest:
        copy.wait()
    for which in range(2):
        early_core(which).wait_send()
    early_y().wait_send()
    for n in range(4):
        enc_weight(n).wait_send()
        for kind in range(5):
            dec_weight(n, kind).wait_send()
    for step in range(1, LANES):
        bias_copy(step).wait_send()
    for i in range(blocks):
        give_part(i, 0).wait_send()
        give_part(i, 1).wait_send()
        give_last(i).wait_send()
    for step in range(1, devices):
        decoded_copy(step).wait()


def forward_call(args, half, hid, dff):
    dma = lambda *s: pltpu.SemaphoreType.DMA(s)
    vm = lambda dtype, *shape: pltpu.VMEM(shape, dtype)
    rows = 2 * PAD
    keys = PAD * half // ENC_SIZE
    devices = 2 * LANES
    slab = DD // devices
    kept = [
        ((PAD, D), F32), ((rows, D), F32), ((rows, D), BF16), ((rows, D), BF16),
        ((2, rows, hid), BF16), ((2, rows, hid), BF16), ((2, 3, rows, half), BF16),
        ((2, 2, PAD, keys), BF16), ((2, rows, half), BF16),
        ((3, half, D), BF16), ((half, D), BF16), ((D, hid), BF16), ((hid, D), BF16),
        ((LANES, 2, DEC_ROWS, D), BF16),
    ]
    made = [
        ((PAD, D), BF16), ((2, DD), F32), ((1, dff), F32), ((8, DD), F32),
        ((devices, slab, GRID), BF16),
    ]
    return pl.pallas_call(
        forward_and_decoder,
        out_shape=[jax.ShapeDtypeStruct(s, d) for s, d in kept + made],
        in_specs=[SM, SM, SM] + [VM] * 8 + [ANY] * 9 + [VM] * 5,
        out_specs=[ANY] * len(kept) + [VM] * len(made),
        scratch_shapes=[
            vm(BF16, 2, 3, half, D), vm(BF16, 2, half, D), vm(BF16, 2, D, hid), vm(BF16, 2, hid, D),
            vm(F32, 8, D), vm(F32, LANES, 8, D),
            vm(BF16, 3, DD, DD), vm(BF16, DD, DD), vm(BF16, DD, dff), vm(BF16, dff, DD),
            vm(F32, rows, D), vm(BF16, rows, D), vm(BF16, rows, D), vm(BF16, 2, rows, hid),
            vm(BF16, 2, rows, hid), vm(BF16, 2, 3, rows, half), vm(BF16, 2, 2, PAD, keys),
            vm(BF16, 2, rows, half), vm(F32, rows, D), vm(F32, rows, D), vm(BF16, rows, D),
            vm(BF16, rows, D), vm(BF16, PAD, D), vm(BF16, PAD, D), vm(F32, PAD, D),
            vm(BF16, GRID, DD), vm(F32, GRID, DD), vm(F32, GRID, DD), vm(BF16, GRID, DD),
            vm(BF16, 3, GRID, DD), vm(BF16, GRID // PAD, PAD, DHEADS * PAD), vm(BF16, GRID, DD),
            vm(F32, GRID, DD),
            vm(BF16, GRID, DD), vm(BF16, DD, GRID), vm(BF16, GRID, dff), vm(BF16, GRID, dff),
            vm(F32, GRID, DD), vm(BF16, GRID, DD), vm(BF16, DD, GRID), vm(F32, GRID, DD),
            vm(BF16, PAD, D), vm(BF16, GRID, PAD), vm(BF16, GRID, GRID),
            vm(BF16, LANES, 2, DEC_ROWS, D),
            vm(BF16, devices, slab, GRID), *[vm(BF16, 2, EARLY_ROWS, D)] * 3,
            dma(8), dma(17), pltpu.SemaphoreType.DMA, dma(4), dma(4), dma(LANES), dma(LANES),
            dma(20), dma(20), dma(6), dma(6), dma(3), dma(3), dma(devices), dma(devices),
            dma(3), dma(3),
        ],
        compiler_params=pltpu.CompilerParams(
            collective_id=0, has_side_effects=True, vmem_limit_bytes=VMEM_LIMIT
        ),
    )(*args)


def add(x, y):
    return x + y


def backward_and_sums(
    d_enc, gains,
    h_u, h_y, h_gp, h_down0, h_down1, h_up0, h_up1,
    h_x, h_x1, h_a, h_qkv, h_p, h_o, h_w0, h_w1, h_proj0, h_proj1,
    dec, dec_qvb, dec_upb, dec_small,
    out, emb, dx_out,
    gb, gt, ut, part, send, recv, du, gx, dx1, d_o, d_acts, own, send1, recv1, dx32, dx,
    d_upb, d_qvb, d_small,
    acc, yacc, enc_mate, rcy, ry, rx, zl, zr, xc, cl, cr, small32, small,
    u, y, gp, down0, down1, up0, up1, x, x1, a, qkv, p, o, w0, w1, proj0, proj1, fetch_s,
    load_s, ex_s, ex_r,
    core_s, core_r, corey_s, corey_r, y_s, y_r, x_s, x_r, z_s, zl_r, zr_r,
    bl_s, br_s, b_r, a_s, a_r, emb_s, emb_r, dx_s, dx_r,
):
    sec = lax.axis_index("section")
    lane = lax.axis_index("tensor")
    pos = lax.axis_index("dp")
    count = lax.axis_size("dp")
    mate = lane + 1 - 2 * lax.rem(lane, 2)
    over = lax.rem(lane + 2, LANES)
    cross = lax.rem(mate + 2, LANES)
    first = pos == 0
    last = pos == count - 1
    me = sec * LANES + lane
    devices = 2 * LANES

    def group_peer(step):
        peer = lax.rem(me + step, devices)
        return peer, {"section": lax.div(peer, LANES), "tensor": lax.rem(peer, LANES)}

    barrier = pltpu.get_barrier_semaphore()
    for step in range(1, devices):
        pl.semaphore_signal(barrier, inc=1, device_id_type=MESH, device_id=group_peer(step)[1])

    @pl.when(pos > 0)
    def _():
        pl.semaphore_signal(barrier, inc=1, device_id={"dp": pos - 1}, device_id_type=MESH)

    @pl.when(pos < count - 1)
    def _():
        pl.semaphore_signal(barrier, inc=1, device_id={"dp": pos + 1}, device_id_type=MESH)

    fetches = [
        pltpu.make_async_copy(src, dst, fetch_s.at[n])
        for n, (src, dst) in enumerate(
            (
                (h_u, u), (h_y, y), (h_gp, gp), (h_down0, down0), (h_down1, down1), (h_up0, up0),
                (h_up1, up1), (h_x, x), (h_x1, x1), (h_a, a), (h_qkv, qkv), (h_p, p), (h_o, o),
                (h_w0, w0), (h_w1, w1), (h_proj0, proj0), (h_proj1, proj1),
            )
        )
    ]
    for fetch in fetches:
        fetch.start()
    loads = [
        pltpu.make_async_copy(dec.at[lane], acc.at[:, 0:DEC_ROWS, :], load_s.at[0]),
        pltpu.make_async_copy(
            dec.at[over, :, EARLY_ROWS:DEC_ROWS, :], yacc.at[:, 0 : DEC_ROWS - EARLY_ROWS, :],
            load_s.at[1],
        ),
    ]
    for load in loads:
        load.start()
    small32[...] = jnp.zeros_like(small32)
    small[...] = jnp.zeros_like(small)
    d_small[...] = jnp.zeros_like(d_small)
    gb[0:PAD, :] = d_enc[...]
    ends = jnp.where(first, 0, 1) + jnp.where(last, 0, 1)
    pl.semaphore_wait(barrier, devices - 1 + ends)

    gain = gains[...].astype(F32)
    width = w0.shape[1]
    marks = head_marks(width, ENC_SIZE, BF16)
    marks32 = head_marks(width, ENC_SIZE, F32)
    ones = ones_per_head(PAD, marks)

    def rows(k, size=CH):
        return pl.ds(pl.multiple_of(k * size, size), size)

    def give_enc():
        return far(d_enc, gb.at[PAD : 2 * PAD, :], ex_s.at[0], ex_r.at[0], {"tensor": over})

    def give_part(i, half):
        cut = rows(i, 256)
        n = 1 + 2 * i + half
        return far(
            send.at[(1 - half) * PAD : (2 - half) * PAD, cut],
            recv.at[half * PAD : (half + 1) * PAD, cut],
            ex_s.at[n], ex_r.at[n], {"tensor": over},
        )

    def give_last(i):
        cut = rows(i, 256)
        return far(send1.at[:, cut], recv1.at[:, cut], ex_s.at[7 + i], ex_r.at[7 + i], {"tensor": over})

    def ff_back(g, i, down):
        c = rows(i, 256)
        d_down = nn(gt[...], y[g, :, c]).astype(BF16)
        dh = nt(gb[...], down[c, :]) * gp[g, :, c].astype(F32)
        d_upb[g, :, c] = colsum(dh)
        dub = dh.astype(BF16)
        du[g, :, c] = dub
        d_up = nn(ut[...], dub).astype(BF16)
        if g == 0:
            acc[1, A_TOP:B_TOP, c] = d_down
            acc[0, A_TOP:B_TOP, c] = d_up
        else:
            enc_mate[1, 0:ENC_A, c] = d_down
            enc_mate[0, 0:ENC_A, c] = d_up

    def ff_in(i):
        c = rows(i, 256)
        t = nt(du[0], up0[c, :]) + nt(du[1], up1[c, :])
        part[:, c] = t
        send[:, c] = t.astype(BF16)
        give_part(i, 0).start()
        give_part(i, 1).start()

    def norm_two():
        for fetch in fetches[7:]:
            fetch.wait()
        for k in range(D // 256):
            give_part(k, 0).wait_recv()
            give_part(k, 1).wait_recv()

        def body(j):
            r = rows(j, 64)
            da = part[r, :] + recv[r, :].astype(F32)
            hat, scale = normal(x1[r, :])
            g = gb[r, :].astype(F32)
            d = g + normal_back(da, hat, scale, gain[1:2])
            gx[r, :] = d.astype(BF16)
            dx1[r, :] = d

            @pl.when(j < 2)
            def _():
                d_small[1:2, :] += colsum(da * hat)
                d_small[3:4, :] += colsum(da)
                d_small[4:5, :] += colsum(d)
                d_small[5:6, :] += colsum(g)

        loop(2 * PAD // 64, body)

    def attention(g, c):
        if c == 0:
            d_proj = tn(o[g], gx[...]).astype(BF16)
            if g == 0:
                acc[1, B_TOP + width : S_TOP, :] = d_proj
            else:
                enc_mate[1, ENC_A + width : ENC_A + 2 * width, :] = d_proj
            d_o[...] = nt(gx[...], (proj0, proj1)[g][...]).astype(BF16)
        r = slice(c * PAD, (c + 1) * PAD)
        d_acts[g, 0, r], d_acts[g, 1, r], d_acts[g, 2, r] = attend_back(
            qkv[g, 0, r], qkv[g, 1, r], qkv[g, 2, r], p[g, c], o[g, r], 1.0 / nn(p[g, c], ones),
            d_o[r, :], marks, marks32, None, ones, ENC_SCALE,
        )
        if c == 1:
            d_qvb[g, 0:1, :] = colsum(d_acts[g, 0].astype(F32))
            d_qvb[g, 1:2, :] = colsum(d_acts[g, 2].astype(F32))

    def project_in(i):
        c = rows(i, 256)
        t = 0.0
        for g, w in enumerate((w0, w1)):
            for j in range(3):
                t += nn(d_acts[g, j], w[j, :, c])
        own[:, c] = t[:PAD]
        send1[:, c] = t[PAD:].astype(BF16)
        give_last(i).start()

    def project_grad(g):
        for j in range(3):
            row = (j % 2) * width
            d = tn(d_acts[g, j], a[...]).astype(BF16)
            if g == 0:
                acc[j // 2, B_TOP + row : B_TOP + row + width, :] = d
            else:
                enc_mate[j // 2, ENC_A + row : ENC_A + row + width, :] = d

    def norm_one():
        for k in range(D // 256):
            give_last(k).wait_recv()

        def body(j):
            r = rows(j, 64)
            da = own[r, :] + recv1[r, :].astype(F32)
            hat, scale = normal(x[r, :])
            d_small[0:1, :] += colsum(da * hat)
            d_small[2:3, :] += colsum(da)
            dx32[r, :] = dx1[r, :] + normal_back(da, hat, scale, gain[0:1])

        loop(PAD // 64, body)
        turned = jnp.transpose(dx32[...])
        cut = D // devices
        for k in range(devices):
            dx[k] = turned[k * cut : (k + 1) * cut, 0:VIS].astype(BF16)
        for r in range(LANES):
            small32[r, 0:1, 0:512] = dec_upb[:, r * 512 : (r + 1) * 512]
            small32[r, 1:2, 0:128] = dec_qvb[0:1, r * 128 : (r + 1) * 128]
            small32[r, 1:2, 128:256] = dec_qvb[1:2, r * 128 : (r + 1) * 128]
            small32[r, 8:16, 0:512] = dec_small[...]
            small32[r, 16:24, :] = d_small[...]
        for g, shard in enumerate((lane, mate)):
            small32[shard, 2:3, :] = d_upb[g]
            small32[shard, 3:4, 0:192] = d_qvb[g, 0:1]
            small32[shard, 3:4, 256:448] = d_qvb[g, 1:2]
        for r in range(LANES):
            small[r, 0, 0:32] = small32[r].astype(BF16)
        acc[:, S_TOP : S_TOP + CH, :] = small[lane]
        yacc[:, DEC_ROWS - EARLY_ROWS :, :] = small[over]
        core_copy(LATE, small.at[mate]).start()
        corey_copy(LATE, small.at[cross]).start()
        for step in range(1, devices):
            dx_copy(step).start()
        dx_out[me] = dx[me]

    def core_enc(lo, hi):
        def body(m):
            block = block_of(m)

            @pl.when((block >= lo) & (block < hi))
            def _():
                src = pl.ds(pl.multiple_of(block * CH - DEC_ROWS, CH), CH)
                core_copy(m, enc_mate.at[:, src, :]).start()

        loop(ALL_K, body)

    def first_piece():
        for fetch in fetches[:7]:
            fetch.wait()
        ut[...] = jnp.transpose(u[...].astype(F32)).astype(BF16)
        give_enc().wait_recv()
        gt[...] = jnp.transpose(gb[...].astype(F32)).astype(BF16)

    def ff_step(k):
        for g, down in enumerate((down0, down1)):
            @pl.when(lax.rem(k, 2) == g)
            def _(g=g, down=down):
                ff_back(g, lax.div(k, 2), down)

    def run_pieces(n):
        def several(low, high, body):
            begin = sum(jnp.where(n > t, 1, 0) for t in PIECES[low:high])
            end = sum(jnp.where(n >= t, 1, 0) for t in PIECES[low:high])
            lax.fori_loop(begin, end, lambda k, c: (body(k), c)[1], 0)

        def single(k, body):
            @pl.when(n == PIECES[k])
            def _():
                body()

        single(0, first_piece)
        several(1, 7, ff_step)
        single(7, lambda: core_enc(DEC_K, DEC_K + ENC_A // CH))
        several(8, 11, ff_in)
        single(11, norm_two)
        for k in range(4):
            single(12 + k, lambda k=k: attention(k // 2, k % 2))
        several(16, 19, project_in)
        for g in range(2):
            single(19 + g, lambda g=g: project_grad(g))
        single(21, lambda: core_enc(DEC_K + ENC_A // CH, B_K))
        single(22, norm_one)

    def dx_copy(step):
        peer, place = group_peer(step)
        return far(dx.at[peer], dx_out.at[me], dx_s.at[step], dx_r.at[step], place)

    def emb_copy(step):
        return far(
            out.at[:, pl.ds(512, CH), :], emb.at[lane], emb_s.at[step], emb_r.at[step],
            {"tensor": lax.rem(lane + step, LANES)},
        )

    def block_of(m):
        shift = 0
        for k in range(1, ALL_K):
            if ORDER[k] - k != ORDER[k - 1] - k + 1:
                shift = jnp.where(m >= k, ORDER[k] - k, shift)
        return m + shift

    def is_dec(m):
        return (block_of(m) < DEC_K) & (m >= EARLY)

    def with_y(m):
        return is_dec(m) | (m == LATE)

    def at(m):
        return pl.ds(pl.multiple_of(block_of(m) * CH, CH), CH)

    def slot_at(m):
        return rows(jnp.where(m < HALVED, lax.div(m, 2), m - HALVED // 2))

    def y_at(m):
        return rows(jnp.minimum(block_of(m), DEC_K) - EARLY)

    def core_copy(m, src):
        return far(src, out.at[:, at(m), :], core_s.at[m], core_r.at[m], {"tensor": mate})

    def corey_copy(m, src):
        return far(src, rcy.at[:, y_at(m), :], corey_s.at[m], corey_r.at[m], {"tensor": mate})

    def y_copy(m):
        cut = y_at(m)
        return far(
            yacc.at[:, cut, :], ry.at[:, cut, :], y_s.at[m], y_r.at[m], {"tensor": over}
        )

    def x_copy(m):
        return far(
            acc.at[1 - sec, at(m), :], rx.at[slot_at(m), :], x_s.at[m], x_r.at[m],
            {"section": 1 - sec},
        )

    def xc_copy(m):
        return far(
            acc.at[:, at(m), :], xc.at[:, slot_at(m), :], x_s.at[m], x_r.at[m],
            {"section": 1 - sec},
        )

    def z_copy(m, whole, right):
        if whole:
            src, dst = acc.at[:, at(m), :], (cl if right else cr).at[:, slot_at(m), :]
        else:
            src, dst = acc.at[sec, at(m), :], (zl if right else zr).at[slot_at(m), :]
        landed = zl_r if right else zr_r
        return far(src, dst, z_s.at[m], landed.at[m], {"dp": pos + 1 if right else pos - 1})

    def b_copy(m, whole, right):
        place = out.at[:, at(m), :] if whole else out.at[sec, at(m), :]
        sent = br_s if right else bl_s
        return far(place, place, sent.at[m], b_r.at[m], {"dp": pos + 1 if right else pos - 1})

    def a_copy(m):
        place = out.at[sec, at(m), :]
        return far(place, place, a_s.at[m], a_r.at[m], {"section": 1 - sec})

    def a_wait(m):
        place = out.at[1 - sec, at(m), :]
        far(place, place, a_s.at[m], a_r.at[m], {"section": 1 - sec}).wait_recv()

    give_enc().start()

    def start_core(m):
        @pl.when(is_dec(m))
        def _():
            core_copy(m, dec.at[mate, :, at(m), :]).start()
            corey_copy(m, dec.at[cross, :, at(m), :]).start()

    loop(ALL_K, start_core)
    for load in loads:
        load.wait()

    def stage_c(m):
        @pl.when(m >= EARLY)
        def _():
            core_copy(m, out.at[:, at(m), :]).wait_recv()
            acc[:, at(m), :] = add(acc[:, at(m), :], out[:, at(m), :])

        @pl.when(with_y(m))
        def _():
            corey_copy(m, rcy.at[:, y_at(m), :]).wait_recv()
            yacc[:, y_at(m), :] = add(yacc[:, y_at(m), :], rcy[:, y_at(m), :])
            y_copy(m).start()

    def finished(m):
        @pl.when(block_of(m) == DEC_K - 1)
        def _():
            for step in range(1, LANES):
                emb_copy(step).start()
            emb[lane] = out[:, 512 : 512 + CH, :]

    def line_of(root, whole):
        left = pos < root
        right = pos > root
        here = pos == root
        reach = max(root, count - 1 - root)
        level = jnp.where(left, pos, jnp.where(right, count - 1 - pos, reach))
        dist = jnp.where(left, root - pos, pos - root)

        def view(ref, m):
            return ref.at[:, at(m), :] if whole else ref.at[sec, at(m), :]

        def landed(ref, m):
            return ref.at[:, slot_at(m), :] if whole else ref.at[slot_at(m), :]

        from_left, from_right = (cl, cr) if whole else (zl, zr)

        def outer(m):
            @pl.when(left & first)
            def _():
                z_copy(m, whole, True).start()

            @pl.when(right & last)
            def _():
                z_copy(m, whole, False).start()

        def inward(m):
            @pl.when(left & (pos > 0))
            def _():
                z_copy(m, whole, True).wait_recv()
                view(acc, m)[...] = add(view(acc, m)[...], landed(from_left, m)[...])
                z_copy(m, whole, True).start()

            @pl.when(right & (pos < count - 1))
            def _():
                z_copy(m, whole, False).wait_recv()
                view(acc, m)[...] = add(view(acc, m)[...], landed(from_right, m)[...])
                z_copy(m, whole, False).start()

            @pl.when(here)
            def _():
                total = view(acc, m)[...].astype(F32)
                if root > 0:
                    z_copy(m, whole, True).wait_recv()
                    total = total + landed(from_left, m)[...].astype(F32)
                if root < count - 1:
                    z_copy(m, whole, False).wait_recv()
                    total = total + landed(from_right, m)[...].astype(F32)
                if whole:
                    view(acc, m)[...] = total.astype(BF16)
                    xc_copy(m).start()
                else:
                    view(out, m)[...] = total.astype(BF16)
                    spread(m)
                    a_copy(m).start()

        def spread(m):
            if root > 0:
                b_copy(m, whole, False).start()
            if root < count - 1:
                b_copy(m, whole, True).start()

        def crossed(m):
            xc_copy(m).wait_recv()
            view(out, m)[...] = add(view(acc, m)[...], landed(xc, m)[...])
            spread(m)
            finished(m)

        def outward(m):
            b_copy(m, whole, False).wait_recv()

            @pl.when(left & (pos > 0))
            def _():
                b_copy(m, whole, False).start()

            @pl.when(right & (pos < count - 1))
            def _():
                b_copy(m, whole, True).start()

            if whole:
                finished(m)
            else:
                a_copy(m).start()

        def sent(m):
            @pl.when(jnp.logical_not(here))
            def _():
                z_copy(m, whole, True).wait_send()

            @pl.when((pos <= root) & (pos > 0))
            def _():
                b_copy(m, whole, False).wait_send()

            @pl.when((pos >= root) & (pos < count - 1))
            def _():
                b_copy(m, whole, True).wait_send()

            if whole:
                @pl.when(here)
                def _():
                    xc_copy(m).wait_send()
            else:
                x_copy(m).wait_send()
                a_copy(m).wait_send()

        def add_y(m):
            @pl.when(with_y(m))
            def _():
                y_copy(m).wait_recv()
                acc[:, at(m), :] = add(acc[:, at(m), :], ry[:, y_at(m), :])

            set_off(m)

        def set_off(m):
            if whole:
                outer(m)
            else:
                x_copy(m).start()

        def add_x(m):
            x_copy(m).wait_recv()
            acc[sec, at(m), :] = add(acc[sec, at(m), :], rx[slot_at(m), :])
            outer(m)

        def last_half(m):
            a_wait(m)
            finished(m)

        base = 1 if whole else 2
        back = base + reach + dist + (1 if whole else 0)
        steps = [(back, jnp.logical_not(here), outward), (base + level, level > 0, inward)]
        if whole:
            steps.append((base + reach + 1, here, crossed))
        else:
            steps += [(back + 1, True, last_half), (2, True, add_x)]
        return steps, sent, add_y, set_off

    low_root = (count - 1) // 2
    high_root = min(low_root + 1, count - 1)
    lines = [
        (lambda m: (lax.rem(m, 2) == 1) | (m >= HALVED), *line_of(low_root, False)),
        (lambda m: (lax.rem(m, 4) == 0) & (m < HALVED), *line_of(low_root, True)),
        (lambda m: (lax.rem(m, 4) == 2) & (m < HALVED), *line_of(high_root, True)),
    ]

    def finish(m):
        @pl.when(m >= EARLY)
        def _():
            core_copy(m, out.at[:, at(m), :]).wait_send()

        @pl.when(with_y(m))
        def _():
            corey_copy(m, rcy.at[:, y_at(m), :]).wait_send()
            y_copy(m).wait_send()

        for mine, _, sent, _, _ in lines:
            @pl.when(mine(m))
            def _(sent=sent):
                sent(m)

    far_reach = max(low_root, count - 1 - low_root, high_root, count - 1 - high_root)
    depth = LAG * (3 + 2 * far_reach) + 1

    def tick(n):
        @pl.when(n <= PIECES[-1])
        def _():
            run_pieces(n)

        for mine, steps, _, add_y, _ in lines:
            m = n - LAG

            @pl.when((m >= EARLY) & (m < ALL_K))
            def _(m=m, mine=mine, add_y=add_y):
                @pl.when(mine(m))
                def _():
                    add_y(m)

            for offset, enabled, stage in steps:
                m = n - LAG * offset

                @pl.when((m >= 0) & (m < ALL_K) & enabled)
                def _(m=m, mine=mine, stage=stage):
                    @pl.when(mine(m))
                    def _():
                        stage(m)

        @pl.when(n < ALL_K)
        def _():
            stage_c(n)

        @pl.when(n >= depth)
        def _():
            finish(n - depth)

    def set_off_early(m):
        for mine, _, _, _, set_off in lines:
            @pl.when(mine(m))
            def _(set_off=set_off):
                set_off(m)

    loop(EARLY, set_off_early)
    loop(ALL_K + depth, tick)

    for step in range(1, devices):
        dx_copy(step).wait()
    for step in range(1, LANES):
        emb_copy(step).wait()
    give_enc().wait_send()
    for k in range(D // 256):
        give_part(k, 0).wait_send()
        give_part(k, 1).wait_send()
        give_last(k).wait_send()


def backward_call(args, half, hid):
    dma = lambda *s: pltpu.SemaphoreType.DMA(s)
    vm = pltpu.VMEM
    full = ALL_K * CH
    y_half = DEC_ROWS - EARLY_ROWS + CH
    whole = HALVED // 2 * CH
    by_half = full - whole
    k = ALL_K
    rows = 2 * PAD
    cut = D // (2 * LANES)
    specs = [VM, VM] + [ANY] * 18 + [VM] * 3
    return pl.pallas_call(
        backward_and_sums,
        out_shape=[
            jax.ShapeDtypeStruct((2, full, D), BF16),
            jax.ShapeDtypeStruct((LANES, 2, CH, D), BF16),
            jax.ShapeDtypeStruct((2 * LANES, cut, VIS), BF16),
        ],
        in_specs=specs,
        out_specs=[VM] * 3,
        scratch_shapes=[
            vm((rows, D), BF16), vm((D, rows), BF16), vm((D, rows), BF16),
            vm((rows, D), F32), vm((rows, D), BF16), vm((rows, D), BF16),
            vm((2, rows, hid), BF16), vm((rows, D), BF16), vm((rows, D), F32),
            vm((rows, half), BF16), vm((2, 3, rows, half), BF16),
            vm((PAD, D), F32), vm((PAD, D), BF16), vm((PAD, D), BF16), vm((PAD, D), F32),
            vm((2 * LANES, cut, VIS), BF16),
            vm((2, 1, hid), F32), vm((2, 2, half), F32), vm((8, D), F32),
            vm((2, full, D), BF16), vm((2, y_half, D), BF16), vm((2, ENC_A + ENC_B, D), BF16),
            vm((2, y_half, D), BF16), vm((2, y_half, D), BF16),
            vm((by_half, D), BF16), vm((by_half, D), BF16), vm((by_half, D), BF16),
            vm((2, whole, D), BF16), vm((2, whole, D), BF16), vm((2, whole, D), BF16),
            vm((LANES, 32, D), F32), vm((LANES, 2, CH, D), BF16),
            *[vm(v.shape, v.dtype) for v in args[2:19]],
            dma(17), dma(2), dma(10), dma(10),
            dma(k), dma(k), dma(k), dma(k), dma(k), dma(k),
            dma(k), dma(k), dma(k), dma(k), dma(k),
            dma(k), dma(k), dma(k), dma(k), dma(k), dma(LANES), dma(LANES),
            dma(2 * LANES), dma(2 * LANES),
        ],
        compiler_params=pltpu.CompilerParams(
            collective_id=1, has_side_effects=True, vmem_limit_bytes=VMEM_LIMIT
        ),
    )(*args)


def finish_grads(
    total, emb, decoded, dx, decoded_out, dx_out,
    e_qkv, e_qvb, e_proj, e_up, e_upb, e_down, e_gain, e_off,
    d_qkv, d_qvb, d_proj, d_up, d_upb, d_down, d_gain, d_off, d_ew, d_ev,
):
    half = e_proj.shape[0]
    decoded_out[...] = decoded[...]
    dx_out[...] = dx[...]
    e_up[...] = total[0, A_TOP:B_TOP, :].astype(F32)
    e_down[...] = jnp.transpose(total[1, A_TOP:B_TOP, :].astype(F32))
    e_qkv[0] = total[0, B_TOP : B_TOP + half, :].astype(F32)
    e_qkv[1] = total[0, B_TOP + half : S_TOP, :].astype(F32)
    e_qkv[2] = total[1, B_TOP : B_TOP + half, :].astype(F32)
    e_proj[...] = total[1, B_TOP + half : S_TOP, :].astype(F32)

    def tile(number):
        h, top, col = tile_of(number)
        return total[h, top : top + CH, col : col + 256].astype(F32)

    for block in range(GRID // CH):
        rows = slice(block * CH, (block + 1) * CH)
        side = slice(block // 2 * 128, (block // 2 + 1) * 128)
        for k in range(2):
            d_up[rows, k * 256 : (k + 1) * 256] = tile(4 * block + k)
            if block % 2:
                both = jnp.concatenate([tile(4 * block - 2 + k), tile(4 * block + 2 + k)], 0)
                d_down[k * 256 : (k + 1) * 256, side] = jnp.transpose(both)
        one, two = tile(32 + 2 * block), tile(33 + 2 * block)
        d_qkv[0, rows, :] = one[:, 0:128]
        d_qkv[1, rows, :] = one[:, 128:256]
        d_qkv[2, rows, :] = two[:, 0:128]
        d_proj[block % 2 * CH : (block % 2 + 1) * CH, side] = two[:, 128:256]
    for k in range(LANES):
        for h in range(2):
            top = k * 192 + h * 64
            d_ew[top : top + 64, :] = emb[k, h, :, 0:512].astype(F32)
            d_ew[k * 192 + 128 : (k + 1) * 192, h * 256 : (h + 1) * 256] = emb[
                k, h, :, 512:768
            ].astype(F32)
    little = total[0, S_TOP : S_TOP + 32, :].astype(F32)
    d_upb[...] = little[0, 0:512]
    d_qvb[0:1, :] = little[1:2, 0:128]
    d_qvb[1:2, :] = little[1:2, 128:256]
    e_upb[...] = little[2]
    e_qvb[0:1, :] = little[3:4, 0:192]
    e_qvb[1:2, :] = little[3:4, 256:448]
    d_gain[...] = little[8:10, 0:512]
    d_off[...] = little[10:14, 0:512]
    d_ev[...] = little[14:16, 0:512]
    e_gain[...] = little[16:18]
    e_off[...] = little[18:22]


def call(kernel, specs, shapes, scratch, args):
    return pl.pallas_call(
        kernel,
        out_shape=[jax.ShapeDtypeStruct(s, d) for s, d in shapes],
        in_specs=specs,
        out_specs=[VM] * len(shapes),
        scratch_shapes=scratch,
        compiler_params=pltpu.CompilerParams(vmem_limit_bytes=VMEM_LIMIT),
    )(*args)


def position_rows():
    quarter = DD // 4
    freq = np.exp(np.arange(quarter, dtype=np.float32) * np.float32(-math.log(10000.0) / quarter))
    angle = np.arange(PAD, dtype=np.float32)[:, None] * freq[None, :].astype(np.float32)
    both = np.concatenate([np.sin(angle), np.cos(angle)], 1).astype(np.float32)
    high = both.astype(jnp.bfloat16)
    low = (both - high.astype(np.float32)).astype(jnp.bfloat16)
    return np.stack([high, low])


def per_device(
    patches, cotangent, widths, visible, window_shift, batch_order,
    encoder_qkv, encoder_qvbias, encoder_proj, encoder_up, encoder_upbias, encoder_down,
    encoder_gains, encoder_offsets,
    decoder_qkv, decoder_qvbias, decoder_proj, decoder_up, decoder_upbias, decoder_down,
    decoder_gains, decoder_offsets, embed_weight, embed_vectors,
):
    qkv0 = encoder_qkv.transpose(1, 2, 0)
    half = qkv0.shape[1]
    hid = encoder_up.shape[1]
    dff = decoder_up.shape[1] * LANES
    flat = patches.transpose(1, 0, 2).reshape(-1, D)
    (
        x, x1, a, u, y, gp, qkv, p, o, qkv1, proj1, up1, down1, dec_buf,
        d_enc, d_dqvb, d_dupb, d_dsmall, out_all,
    ) = forward_call(
        (
            widths, window_shift.T, batch_order, visible, flat, encoder_gains, encoder_offsets,
            encoder_qvbias, encoder_upbias, decoder_qvbias, decoder_upbias,
            qkv0, encoder_proj, encoder_up, encoder_down,
            decoder_qkv.transpose(1, 0, 2), decoder_proj, decoder_up, decoder_down,
            cotangent, embed_weight, embed_vectors, jnp.asarray(position_rows()),
            decoder_gains, decoder_offsets,
        ),
        half, hid, dff,
    )
    total, emb, dx_all = backward_call(
        (
            d_enc, encoder_gains, u, y, gp, encoder_down, down1, encoder_up, up1,
            x, x1, a, qkv, p, o, qkv0, qkv1, encoder_proj, proj1,
            dec_buf, d_dqvb, d_dupb, d_dsmall,
        ),
        half, hid,
    )
    f = lambda *shape: (shape, F32)
    out_all, dx_all, *grads = call(
        finish_grads, [VM] * 4,
        [
            (out_all.shape, BF16), (dx_all.shape, BF16), f(3, half, D), f(2, half), f(half, D), f(D, hid), f(hid), f(hid, D), f(2, D), f(4, D),
            f(3, DD, 128), f(2, 128), f(128, DD), f(DD, 512), f(512), f(512, DD), f(2, DD), f(4, DD),
            f(D, DD), f(2, DD),
        ],
        [], (total, emb, out_all, dx_all),
    )
    grads[0] = grads[0].transpose(2, 0, 1)
    grads[8] = grads[8].transpose(1, 0, 2)
    return (out_all.swapaxes(1, 2), dx_all.swapaxes(1, 2), *grads)


def solution(mesh):
    weights = (
        P(None, None, "tensor"), P(None, "tensor"), P("tensor", None), P(None, "tensor"),
        P("tensor"), P("tensor", None), P(), P(),
    )
    split = P("dp", None, ("section", "tensor"))
    return jax.shard_map(
        per_device,
        mesh=mesh,
        in_specs=(
            P("dp", None, None), P("dp", None, None), P("dp"), P("dp", None), P("dp", None),
            P("dp", None),
        ) + weights + weights + (P(), P()),
        out_specs=(split, split) + weights + weights + (P(), P()),
        check_vma=False,
    )
```

```python
import math

import jax
import jax.numpy as jnp
import numpy as np
from jax import lax
from jax.experimental import pallas as pl
from jax.experimental.pallas import tpu as pltpu
from jax.sharding import PartitionSpec as P

D = 768
HEADS = 12
DD = 512
DHEADS = 16
GRID_ROWS = 64
WIDE = 8
WIN = 4
VIS = 102
CM = 4
GRID = 512
LANES = 4
PAD = 128
EPS = 1e-06
NEG = -10000.0
F32 = jnp.float32
BF16 = jnp.bfloat16
VMEM_LIMIT = 60 * 1024 * 1024

VM = pl.BlockSpec(memory_space=pltpu.VMEM)
SM = pl.BlockSpec(memory_space=pltpu.SMEM)
ANY = pl.BlockSpec(memory_space=pl.ANY)


def nn(a, b):
    return lax.dot_general(a, b, (((1,), (0,)), ((), ())), preferred_element_type=F32)


def nt(a, b):
    return lax.dot_general(a, b, (((1,), (1,)), ((), ())), preferred_element_type=F32)


def tn(a, b):
    return lax.dot_general(a, b, (((0,), (0,)), ((), ())), preferred_element_type=F32)


def loop(count, body, unroll=1):
    def step(i, carry):
        body(i)
        return carry

    lax.fori_loop(0, count, step, 0, unroll=unroll)


def span(i, size):
    return pl.ds(pl.multiple_of(i * size, size), size)


def normal(x):
    center = x - jnp.mean(x, -1, keepdims=True)
    scale = lax.rsqrt(jnp.mean(center * center, -1, keepdims=True) + EPS)
    return center * scale, scale


def normal_back(dy, hat, scale, gain):
    d = dy * gain
    return scale * (
        d - jnp.mean(d, -1, keepdims=True) - hat * jnp.mean(d * hat, -1, keepdims=True)
    )


def gelu_both(h):
    phi = 0.5 * lax.erf(h * math.sqrt(0.5)) + 0.5
    bell = jnp.exp2(h * h * (-0.5 * math.log2(math.e)))
    return h * phi, phi + h * bell * (1.0 / math.sqrt(2.0 * math.pi))


def colsum(x):
    return jnp.sum(x, 0, keepdims=True)


def head_marks(width, size, dtype):
    lane = lax.broadcasted_iota(jnp.int32, (1, width), 1)
    return [((lane >= h * size) & (lane < (h + 1) * size)).astype(dtype) for h in range(width // size)]


def stacked(x, marks):
    return jnp.concatenate([x * m for m in marks], 0)


LOG2E = math.log2(math.e)


def attend(q, k, v, marks, ones, masked, scale):
    keys = k.shape[0]
    s = nt(q, stacked(k, marks))
    parts = []
    for h in range(len(marks)):
        x = masked(s[:, h * keys : (h + 1) * keys] * (scale * LOG2E))
        parts.append(jnp.exp2(x - jnp.max(x, -1, keepdims=True)).astype(BF16))
    e = jnp.concatenate(parts, 1)
    width = q.shape[1]
    if width % 128:
        top, total = nn(e, stacked(v, marks)), nn(e, ones)
    else:
        both = nn(e, jnp.concatenate([stacked(v, marks), ones], 1))
        top, total = both[:, :width], both[:, width:]
    inverse = 1.0 / total
    return e, (top * inverse).astype(BF16), inverse


def attend_back(q, k, v, e, o, inverse, d_out, marks, marks32, rows32, ones, scale):
    keys = k.shape[0]
    width = q.shape[1]
    d_one = d_out.astype(F32) * inverse
    d_two = (d_one * o.astype(F32)).astype(BF16)
    d_one = d_one.astype(BF16)
    if width % 128:
        d_s = nt(d_one, stacked(v, marks)) - nt(d_two, ones)
    else:
        d_s = nt(
            jnp.concatenate([d_one, d_two], 1), jnp.concatenate([stacked(v, marks), -ones], 1)
        )
    dr = (e.astype(F32) * d_s * scale).astype(BF16)
    d_q = nn(dr, stacked(k, marks)).astype(BF16)
    if width % 128:
        d_k_all, d_v_all = tn(dr, q), tn(e, d_one)
        d_k = d_v = 0.0
        for h in range(len(marks)):
            cut = slice(h * keys, (h + 1) * keys)
            d_k += d_k_all[cut] * marks32[h]
            d_v += d_v_all[cut] * marks32[h]
        return d_q, d_k.astype(BF16), d_v.astype(BF16)
    d_k_all = nn(jnp.transpose(q.astype(F32)).astype(BF16), dr)
    d_v_all = nn(jnp.transpose(d_one.astype(F32)).astype(BF16), e)
    d_k = d_v = 0.0
    for h in range(len(marks)):
        cut = slice(h * keys, (h + 1) * keys)
        d_k += d_k_all[:, cut] * rows32[h]
        d_v += d_v_all[:, cut] * rows32[h]
    return d_q, jnp.transpose(d_k).astype(BF16), jnp.transpose(d_v).astype(BF16)


def ones_per_head(keys, marks):
    return jnp.concatenate([jnp.broadcast_to(m, (keys, m.shape[1])) for m in marks], 0)


ENC_SIZE = D // HEADS
ENC_SCALE = ENC_SIZE ** -0.5
DEC_SIZE = DD // DHEADS
DEC_SCALE = DEC_SIZE ** -0.5


CH = 64
DEC_ROWS = 576
ENC_A = 768
ENC_B = 384
DEC_K = DEC_ROWS // CH
B_K = (DEC_ROWS + ENC_A + ENC_B) // CH
ALL_K = B_K + 1
A_TOP = DEC_ROWS
B_TOP = DEC_ROWS + ENC_A
S_TOP = B_TOP + ENC_B
EARLY = 4
XFIRST = True
EARLY_ROWS = EARLY * CH
LAG = 2
ORDER = (0, 1, 2, 3, 9, 10, 11, 12, 13, 14, 15, 16, 17, 4, 18, 5, 19, 20, 6, 8, 21, 22, 23, 24, 27, 25, 26, 7)
PIECES = (2, 2, 3, 3, 3, 3, 3, 3, 3, 3, 3, 10, 10, 11, 12, 12, 13, 15, 15, 16, 16, 18, 20)
LATE = ORDER.index(B_K)
WHOLE_LOW = 6
WHOLE_HIGH = 22
SMALL = 16


def tile_of(number):
    place = number // 3
    return place % 2, place // 2 * CH, number % 3 * 256


MESH = pl.DeviceIdType.MESH


def far(src, dst, send, recv, peer):
    return pltpu.make_async_remote_copy(
        src_ref=src, dst_ref=dst, send_sem=send, recv_sem=recv, device_id=peer, device_id_type=MESH
    )


def forward_and_decoder(
    wid, shifts, order, vis, pat, gains, offs, b_qv, b_up, b_dqv, b_dup,
    h_qkv, h_proj, h_up, h_down, h_dqkv, h_dproj, h_dup, h_ddown,
    cot_hbm, ew, evec, table, dgains, doffs,
    o_x, o_x1, o_a, o_u, o_y, o_gp, o_qkv, o_p, o_o, o_w, o_wproj, o_wup, o_wdown, o_dec,
    d_enc, d_qvb, d_upb, d_small, dec_out,
    w_qkv, w_proj, w_up, w_down, bias, biases, qkv, proj, up, down,
    ex, ea, eu, ey, egp, eqkv, ep, eo, ex1, epart, esend, erecv, esend2, erecv2, eown,
    cot, x0, x1, a, acts, probs, o, inverse, u, ut, y, gp, g32, gb, gt, acc, e_ref, hot, perm, buf, dsend, e_rc, e_rcy, e_rx, e_ry,
    load_s, out_s, cot_s, w_s, w_r, bias_s, bias_r, dw_s, dw_r, ex_s, ex_r, ex2_s, ex2_r, do_s, do_r, e_s, e_r,
):
    sec = lax.axis_index("section")
    lane = lax.axis_index("tensor")
    mate = lane + 1 - 2 * lax.rem(lane, 2)
    over = lax.rem(lane + 2, LANES)
    cross = lax.rem(mate + 2, LANES)
    me = sec * LANES + lane
    devices = 2 * LANES
    clip = me
    clips = (me, sec * LANES + over)

    def group_peer(step):
        peer = lax.rem(me + step, devices)
        return peer, {"section": lax.div(peer, LANES), "tensor": lax.rem(peer, LANES)}

    own = [
        pltpu.make_async_copy(src, dst.at[0], load_s.at[n])
        for n, (src, dst) in enumerate(
            ((h_qkv, w_qkv), (h_proj, w_proj), (h_up, w_up), (h_down, w_down))
        )
    ]

    def place(n, shard, part=None):
        thick = (128, 128, 512, 512)[n]
        base = shard * thick
        cut = pl.ds(pl.multiple_of(base, thick), thick)
        if part is None:
            return (qkv.at[:, :, cut], proj.at[cut, :], up.at[:, cut], down.at[cut, :])[n]
        some = span(part, (256, 64, 256, 256)[n])
        if n == 0:
            return qkv.at[:, some, cut]
        if n == 2:
            return up.at[some, cut]
        few = thick // 2
        rows = pl.ds(pl.multiple_of(base + part * few, few), few)
        return (proj if n == 1 else down).at[rows, :]

    shards = (h_dqkv, h_dproj, h_dup, h_ddown)
    keep = [
        pltpu.make_async_copy(shards[n], place(n, lane), load_s.at[4 + n]) for n in range(4)
    ]
    for copy in own + keep:
        copy.start()
    fetch = pltpu.make_async_copy(cot_hbm.at[clip], cot, cot_s)
    fetch.start()

    barrier = pltpu.get_barrier_semaphore()
    for step in range(1, devices):
        pl.semaphore_signal(barrier, inc=1, device_id_type=MESH, device_id=group_peer(step)[1])
    bias[...] = jnp.zeros_like(bias)
    half = w_proj.shape[1]
    bias[0:1, :] = b_up[...].astype(F32).reshape(1, -1)
    bias[1:3, 0:half] = b_qv[...].astype(F32)
    bias[3:4, 0:512] = b_dup[...].astype(F32).reshape(1, -1)
    bias[4:6, 0:128] = b_dqv[...].astype(F32)
    biases[lane] = bias[...]
    pl.semaphore_wait(barrier, devices - 1)

    def enc_weight(n):
        src = (h_qkv, h_proj, h_up, h_down)[n]
        dst = (w_qkv, w_proj, w_up, w_down)[n]
        return far(src, dst.at[1], w_s.at[n], w_r.at[n], {"tensor": mate})

    def bias_copy(step):
        return far(
            bias, biases.at[lane], bias_s.at[step], bias_r.at[step],
            {"tensor": lax.rem(lane + step, LANES)},
        )

    def half_of(n):
        some = span(sec, (256, 64, 256, 256)[n])
        return shards[n].at[:, some, :] if n == 0 else shards[n].at[some, :]

    def dec_weight(n, kind):
        peer = {"section": 1 - sec} if kind == 2 else {"tensor": over if kind == 0 else mate}
        if kind == 0:
            src, dst = half_of(n), place(n, lane, sec)
        elif kind == 1:
            src, dst = shards[n], place(n, lane)
        else:
            src = dst = place(n, over, 1 - sec if kind == 4 else sec)
        return far(src, dst, dw_s.at[5 * n + kind], dw_r.at[5 * n + kind], peer)

    enc_weight(0).start()
    for step in range(1, LANES):
        bias_copy(step).start()
    enc_weight(1).start()
    dec_weight(0, 0).start()
    enc_weight(2).start()
    enc_weight(3).start()
    for n in range(4):
        dec_weight(n, 1).start()

    def pass_on(n):
        dec_weight(n, 0).wait_recv()
        dec_weight(n, 2).start()
        dec_weight(n, 3).start()

    def pass_last(n):
        dec_weight(n, 2).wait_recv()
        dec_weight(n, 4).start()

    def arrived(n):
        keep[n].wait()
        dec_weight(n, 1).wait_recv()
        dec_weight(n, 3).wait_recv()
        dec_weight(n, 4).wait_recv()

    width = wid[clip]
    bits = jnp.where(width == WIDE, 3, 2)
    turn = shifts[0, clip] * width
    mod = GRID - 1
    spot = 0
    for i in range(order.shape[1]):
        spot = spot + jnp.where(order[0, i] == clip, i, 0)
    batch = spot // CM
    count = 0
    for i in range(order.shape[1]):
        count = count + jnp.where(batch == i // CM, wid[order[0, i]], 0)
    factor_rows = CM * GRID / (jnp.full((1, 1), count, jnp.int32) * GRID_ROWS).astype(F32)

    def slot_of(index):
        return (index - turn) & mod

    def code_of(slot):
        band = ((slot >> bits) + shifts[0, clip]) >> 2
        strip = ((slot & (width - 1)) + shifts[1, clip]) >> 2
        return band * 4 + strip

    def valid_rows():
        slot = slot_of(lax.broadcasted_iota(jnp.int32, (GRID, 1), 0))
        return (slot < GRID_ROWS * width).astype(F32)

    def clip_gradient():
        fetch.wait()
        rolled = slot_of(lax.broadcasted_iota(jnp.int32, (GRID, GRID), 0))
        column = lax.broadcasted_iota(jnp.int32, (GRID, GRID), 1)
        perm[...] = (rolled == column).astype(F32).astype(BF16)
        g = nn(perm[...], cot[...]) * valid_rows() * factor_rows
        g32[...] = g
        gb[...] = g.astype(BF16)
        gt[...] = jnp.transpose(g).astype(BF16)
        d_small[...] = jnp.zeros_like(d_small)
        d_small[5:6, :] = colsum(g)

    seen = vis[pl.ds(clip, 1), :]
    target = jnp.concatenate([(seen + turn) & mod, jnp.full((1, PAD - VIS), -1, jnp.int32)], 1)

    def places(i):
        r = span(i, PAD)
        index = lax.broadcasted_iota(jnp.int32, (PAD, PAD), 0) + i * PAD
        column = lax.broadcasted_iota(jnp.int32, (PAD, PAD), 1)
        hot[r, :] = (index == target).astype(F32).astype(BF16)
        slot = slot_of(index)
        by_row = ((slot >> bits) == column).astype(F32).astype(BF16)
        by_col = ((slot & (width - 1)) == column).astype(F32).astype(BF16)
        row_part = nn(by_row, table[0]) + nn(by_row, table[1])
        col_part = nn(by_col, table[0]) + nn(by_col, table[1])
        x0[r, :] = jnp.concatenate([row_part, col_part], 1)

    egain = gains[...].astype(F32)
    eoff = offs[...].astype(F32)
    stride = pat.shape[0] // VIS
    for c in range(2):
        row = lax.broadcasted_iota(jnp.int32, (PAD, pat.shape[0]), 0)
        col = lax.broadcasted_iota(jnp.int32, (PAD, pat.shape[0]), 1)
        pick = (col == row * stride + clips[c]).astype(F32).astype(BF16)
        ex[c * PAD : (c + 1) * PAD, :] = nn(pick, pat[...])

    emarks = head_marks(half, ENC_SIZE, BF16)
    key = lax.broadcasted_iota(jnp.int32, (PAD, PAD), 1)
    floor = jnp.where(key < VIS, NEG * LOG2E, -1e30)
    eones = ones_per_head(PAD, emarks)
    blocks = D // 256

    def give_part(i, side):
        cut = span(i, 256)
        return far(
            esend.at[(1 - side) * PAD : (2 - side) * PAD, cut],
            erecv.at[side * PAD : (side + 1) * PAD, cut],
            ex_s.at[2 * i + side], ex_r.at[2 * i + side], {"tensor": over},
        )

    for c in range(2):
        rows = slice(c * PAD, (c + 1) * PAD)
        hat, _ = normal(ex[rows, :])
        ea[rows, :] = (hat * egain[0:1] + eoff[0:1]).astype(BF16)
        limit = (VIS * wid[clips[c]]) // WIDE
        for g, shard in enumerate((lane, mate)):
            if c == 0 and g == 0:
                own[0].wait()
            if c == 0 and g == 1:
                enc_weight(0).wait_recv()
                for step in range(1, LANES):
                    bias_copy(step).wait_recv()
            if g == 0:
                bq, bv = bias[1:2, 0:half], bias[2:3, 0:half]
            else:
                bq, bv = biases[shard, 1:2, 0:half], biases[shard, 2:3, 0:half]
            eqkv[g, 0, rows] = (nt(ea[rows, :], w_qkv[g, 0]) + bq).astype(BF16)
            eqkv[g, 1, rows] = nt(ea[rows, :], w_qkv[g, 1]).astype(BF16)
            eqkv[g, 2, rows] = (nt(ea[rows, :], w_qkv[g, 2]) + bv).astype(BF16)
            p, out, _ = attend(
                eqkv[g, 0, rows], eqkv[g, 1, rows], eqkv[g, 2, rows], emarks, eones,
                lambda s: jnp.where(key < limit, s, floor), ENC_SCALE,
            )
            ep[g, c] = p
            eo[g, rows] = out
        if c == 0:
            own[1].wait()
            enc_weight(1).wait_recv()
        for i in range(blocks):
            cut = slice(i * 256, (i + 1) * 256)
            t = nn(eo[0, rows], w_proj[0, :, cut]) + nn(eo[1, rows], w_proj[1, :, cut])
            epart[rows, cut] = t
            esend[rows, cut] = t.astype(BF16)
            give_part(i, 1 - c).start()
    pass_on(0)
    clip_gradient()
    own[2].wait()
    enc_weight(2).wait_recv()

    def give_last(i):
        cut = span(i, 256)
        return far(
            esend2.at[:, cut], erecv2.at[:, cut], ex2_s.at[i], ex2_r.at[i], {"tensor": over}
        )

    for c in (1, 0):
        rows = slice(c * PAD, (c + 1) * PAD)
        for i in range(blocks):
            give_part(i, c).wait_recv()
        t = ex[rows, :] + epart[rows, :] + erecv[rows, :].astype(F32) + eoff[2:3]
        ex1[rows, :] = t
        hat, _ = normal(t)
        eu[rows, :] = (hat * egain[1:2] + eoff[1:2]).astype(BF16)
        for g, shard in enumerate((lane, mate)):

            def enc_ff(i, g=g, shard=shard, rows=rows):
                cut = span(i, 256)
                h = nn(eu[rows, :], w_up[g, :, cut]) + biases[shard, 0:1, cut]
                act, slope = gelu_both(h)
                ey[g, rows, cut] = act.astype(BF16)
                egp[g, rows, cut] = slope.astype(BF16)

            loop(w_up.shape[2] // 256, enc_ff, unroll=3)
        if c == 1:
            own[3].wait()
            enc_weight(3).wait_recv()
        for i in range(blocks):
            cut = slice(i * 256, (i + 1) * 256)
            t = nn(ey[0, rows], w_down[0, :, cut]) + nn(ey[1, rows], w_down[1, :, cut])
            if c == 0:
                eown[:, cut] = t
            else:
                esend2[:, cut] = t.astype(BF16)
                give_last(i).start()
        if c == 1:
            for n in (1, 2, 3):
                dec_weight(n, 0).start()
            pass_last(0)
    outs = [
        pltpu.make_async_copy(src, dst, out_s.at[n])
        for n, (src, dst) in enumerate(
            (
                (ex.at[0:PAD, :], o_x), (ex1, o_x1), (ea, o_a), (eu, o_u), (ey, o_y), (egp, o_gp),
                (eqkv, o_qkv), (ep, o_p), (eo, o_o), (w_qkv.at[1], o_w), (w_proj.at[1], o_wproj),
                (w_up.at[1], o_wup), (w_down.at[1], o_wdown),
            )
        )
    ]
    for copy in outs:
        copy.start()
    loop(GRID // PAD, places, unroll=2)
    for i in range(blocks):
        give_last(i).wait_recv()

    e_ref[...] = (ex1[0:PAD, :] + eown[...] + erecv2[...].astype(F32) + eoff[3:4]).astype(BF16)
    vec = evec[...].astype(F32)
    m = (nn(e_ref[...], ew[...]) + vec[0:1]).astype(BF16)
    gain = dgains[...].astype(F32)
    offsets = doffs[...].astype(F32)

    def start(i):
        r = span(i, PAD)
        oh = hot[r, :]
        hit = jnp.sum(oh.astype(F32), -1, keepdims=True)
        x = jnp.where(hit > 0, nn(oh, m), vec[1:2]).astype(BF16).astype(F32) + x0[r, :]
        x0[r, :] = x
        hat, _ = normal(x)
        a[r, :] = (hat * gain[0:1] + offsets[0:1]).astype(BF16)

    loop(GRID // PAD, start, unroll=2)
    arrived(0)

    def dec_bias(row, size):
        return jnp.concatenate([biases[k, row : row + 1, 0:size] for k in range(LANES)], 1)

    acts[0] = (nn(a[...], qkv[0]) + dec_bias(4, 128)).astype(BF16)
    acts[1] = nn(a[...], qkv[1]).astype(BF16)
    acts[2] = (nn(a[...], qkv[2]) + dec_bias(5, 128)).astype(BF16)
    pass_on(1)
    pass_on(2)
    marks = head_marks(128, DEC_SIZE, BF16)
    marks32 = head_marks(128, DEC_SIZE, F32)
    dim = lax.broadcasted_iota(jnp.int32, (128, 1), 0)
    rows32 = [
        ((dim >= h * DEC_SIZE) & (dim < (h + 1) * DEC_SIZE)).astype(F32) for h in range(len(marks))
    ]

    ones = ones_per_head(PAD, marks)

    def attention(i):
        r = span(i, PAD)
        row_slot = slot_of(lax.broadcasted_iota(jnp.int32, (PAD, PAD), 0) + i * PAD)
        key_slot = slot_of(lax.broadcasted_iota(jnp.int32, (PAD, PAD), 1) + i * PAD)
        allowed = (code_of(row_slot) == code_of(key_slot)) & (key_slot < GRID_ROWS * width)
        for g in range(DD // 128):
            c = slice(g * 128, (g + 1) * 128)
            probs[i, :, g * 512 : (g + 1) * 512], o[r, c], inverse[r, c] = attend(
                acts[0, r, c], acts[1, r, c], acts[2, r, c], marks, ones,
                lambda s: jnp.where(allowed, s, NEG * LOG2E), DEC_SCALE,
            )

    loop(GRID // PAD, attention, unroll=2)
    pass_last(1)
    pass_last(2)
    pass_on(3)
    arrived(1)

    def mix(i):
        r = span(i, 256)
        x = x0[r, :] + nn(o[r, :], proj[...]) + offsets[2:3]
        x1[r, :] = x
        hat, _ = normal(x)
        un = hat * gain[1:2] + offsets[1:2]
        u[r, :] = un.astype(BF16)
        ut[:, r] = jnp.transpose(un).astype(BF16)

    loop(2, mix)
    pass_last(3)
    arrived(2)

    def ff(i):
        c = span(i, 256)
        h = nn(u[...], up[:, c]) + biases[lax.div(i, 2), 3:4, span(lax.rem(i, 2), 256)]
        act, slope = gelu_both(h)
        y[:, c] = act.astype(BF16)
        gp[:, c] = slope.astype(BF16)

    loop(up.shape[1] // 256, ff, unroll=2)
    arrived(3)
    def out(i):
        c = span(i, 256)
        acc[:, c] = nn(y[...], down[:, c])

    loop(2, out)
    full = ((acc[...] + x1[...] + offsets[3:4]) * valid_rows()).astype(BF16)
    turned = tn(full, perm[...]).astype(BF16)
    for k in range(devices):
        dsend[k] = turned[k * dsend.shape[1] : (k + 1) * dsend.shape[1]]

    def decoded_copy(step):
        peer, spot = group_peer(step)
        return far(dsend.at[peer], dec_out.at[me], do_s.at[step], do_r.at[step], spot)

    for step in range(1, devices):
        decoded_copy(step).start()
    dec_out[me] = dsend[me]

    def ff_back(shard):
        for side in range(2):
            c = span(2 * shard + side, 256)
            d_down = nn(gt[...], y[:, c]).astype(BF16)
            dh = nt(gb[...], down[c, :]) * gp[:, c].astype(F32)
            d_upb[:, c] = colsum(dh)
            du = dh.astype(BF16)
            gp[:, c] = du
            d_up = nn(ut[...], du).astype(BF16)
            for block in range(GRID // CH):
                rows = slice(block * CH, (block + 1) * CH)
                h, top, col = tile_of(4 * block + side)
                buf[shard, h, top : top + CH, col : col + 256] = d_up[rows]
                h, top, col = tile_of(4 * block + 2 + side)
                buf[shard, h, top : top + CH, col : col + 256] = d_down[rows]

    def early_core(which):
        shard, land = ((mate, e_rc), (cross, e_rcy))[which]
        return far(
            buf.at[shard, :, 0:EARLY_ROWS, :], land, e_s.at[which], e_r.at[which], {"tensor": mate}
        )

    def early_x(which):
        return far(
            buf.at[(over, lane)[which], 1 - sec, 0:EARLY_ROWS, :], e_rx.at[which],
            e_s.at[2 + which], e_r.at[2 + which], {"section": 1 - sec},
        )

    def early_y():
        return far(
            buf.at[over, sec, 0:EARLY_ROWS, :], e_ry, e_s.at[4], e_r.at[4], {"tensor": over}
        )

    def early_add(shard, land):
        def body(i):
            r = span(i, CH)
            buf[shard, :, r, :] = buf[shard, :, r, :] + land[:, r, :]

        loop(EARLY_ROWS // CH, body)

    def early_half(shard, land):
        buf[shard, sec, 0:EARLY_ROWS, :] = buf[shard, sec, 0:EARLY_ROWS, :] + land

    def ff_step(i):
        ff_back(jnp.where(i == 0, cross, jnp.where(i == 1, over, jnp.where(i == 2, mate, lane))))

        @pl.when(i == 1)
        def _():
            early_core(1).start()

        @pl.when(i == 2)
        def _():
            early_core(0).start()
            early_core(1).wait_recv()
            early_add(over, e_rcy)
            early_x(0).start()

    loop(LANES, ff_step)

    def ff_in(i):
        c = span(i, 256)
        acc[:, c] = nt(gp[...], up[c, :])

    loop(2, ff_in)
    early_core(0).wait_recv()
    early_add(lane, e_rc)
    early_x(1).start()

    def mix_back(i):
        r = span(i, 256)
        hat, scale = normal(x1[r, :])
        da = acc[r, :]
        dx = g32[r, :] + normal_back(da, hat, scale, gain[1:2])
        d_small[1:2, :] += colsum(da * hat)
        d_small[3:4, :] += colsum(da)
        d_small[4:5, :] += colsum(dx)
        g32[r, :] = dx
        dxb = dx.astype(BF16)
        gb[r, :] = dxb
        u[r, :] = nt(dxb, proj[...]).astype(BF16)

    loop(2, mix_back)
    d_proj = tn(o[...], gb[...]).astype(BF16)
    for block in range(GRID // CH):
        h, top, col = tile_of(33 + 2 * block)
        side = slice(block // 2 * 128, (block // 2 + 1) * 128)
        for k in range(LANES):
            row = k * 128 + block % 2 * CH
            buf[k, h, top : top + CH, col + 128 : col + 256] = d_proj[row : row + CH, side]

    def attention_back(i):
        r = span(i, PAD)
        for k in range(DD // 128):
            c = slice(k * 128, (k + 1) * 128)
            acts[0, r, c], acts[1, r, c], acts[2, r, c] = attend_back(
                acts[0, r, c], acts[1, r, c], acts[2, r, c],
                probs[i, :, k * 512 : (k + 1) * 512], o[r, c], inverse[r, c], u[r, c],
                marks, marks32, rows32, ones, DEC_SCALE,
            )

    loop(GRID // PAD, attention_back, unroll=2)
    early_x(0).wait_recv()
    early_half(over, e_rx[0])
    early_y().start()
    d_qvb[0:1, :] = colsum(acts[0].astype(F32))
    d_qvb[1:2, :] = colsum(acts[2].astype(F32))

    def project_back(i):
        c = span(i, 256)
        acc[:, c] = (
            nt(acts[0], qkv[0, c, :]) + nt(acts[1], qkv[1, c, :]) + nt(acts[2], qkv[2, c, :])
        )

    loop(2, project_back)
    gt[...] = jnp.transpose(a[...].astype(F32)).astype(BF16)
    for j in range(3):
        d_qkv = nn(gt[...], acts[j]).astype(BF16)
        for block in range(GRID // CH):
            h, top, col = tile_of(32 + 2 * block + j // 2)
            col = col + j % 2 * 128
            rows = slice(block * CH, (block + 1) * CH)
            for k in range(LANES):
                buf[k, h, top : top + CH, col : col + 128] = d_qkv[rows, k * 128 : (k + 1) * 128]

    def start_back(i):
        r = span(i, PAD)
        hat, scale = normal(x0[r, :])
        da = acc[r, :]
        dx = g32[r, :] + normal_back(da, hat, scale, gain[0:1])
        d_small[0:1, :] += colsum(da * hat)
        d_small[2:3, :] += colsum(da)
        dg = dx.astype(BF16)
        gb[r, :] = dg
        hit = jnp.sum(hot[r, :].astype(F32), -1, keepdims=True)
        d_small[7:8, :] += colsum(jnp.where(hit > 0, 0.0, dg.astype(F32)))

    loop(GRID // PAD, start_back, unroll=2)
    dm = tn(hot[...], gb[...])
    d_small[6:7, :] = colsum(dm)
    dmb = dm.astype(BF16)
    d_enc[...] = nt(dmb, ew[...]).astype(BF16)
    d_ew = tn(e_ref[...], dmb).astype(BF16)
    for k in range(LANES):
        for h in range(2):
            top = k * 192 + h * 64
            buf[k, h, 512:576, 0:512] = d_ew[top : top + 64]
            buf[k, h, 512:576, 512:768] = d_ew[k * 192 + 128 : (k + 1) * 192, h * 256 : (h + 1) * 256]

    early_x(1).wait_recv()
    early_half(lane, e_rx[1])
    early_y().wait_recv()
    early_half(lane, e_ry[...])
    later = pl.ds(EARLY_ROWS, DEC_ROWS - EARLY_ROWS)
    rest = [pltpu.make_async_copy(buf.at[lane], o_dec.at[lane], out_s.at[13])] + [
        pltpu.make_async_copy(buf.at[k, :, later, :], o_dec.at[k, :, later, :], out_s.at[14 + n])
        for n, k in enumerate((mate, over, cross))
    ]
    for copy in rest:
        copy.start()
    for copy in outs + rest:
        copy.wait()
    for which in range(2):
        early_core(which).wait_send()
        early_x(which).wait_send()
    early_y().wait_send()
    for n in range(4):
        enc_weight(n).wait_send()
        for kind in range(5):
            dec_weight(n, kind).wait_send()
    for step in range(1, LANES):
        bias_copy(step).wait_send()
    for i in range(blocks):
        give_part(i, 0).wait_send()
        give_part(i, 1).wait_send()
        give_last(i).wait_send()
    for step in range(1, devices):
        decoded_copy(step).wait()


def forward_call(args, half, hid, dff):
    dma = lambda *s: pltpu.SemaphoreType.DMA(s)
    vm = lambda dtype, *shape: pltpu.VMEM(shape, dtype)
    rows = 2 * PAD
    keys = PAD * half // ENC_SIZE
    devices = 2 * LANES
    slab = DD // devices
    kept = [
        ((PAD, D), F32), ((rows, D), F32), ((rows, D), BF16), ((rows, D), BF16),
        ((2, rows, hid), BF16), ((2, rows, hid), BF16), ((2, 3, rows, half), BF16),
        ((2, 2, PAD, keys), BF16), ((2, rows, half), BF16),
        ((3, half, D), BF16), ((half, D), BF16), ((D, hid), BF16), ((hid, D), BF16),
        ((LANES, 2, DEC_ROWS, D), BF16),
    ]
    made = [
        ((PAD, D), BF16), ((2, DD), F32), ((1, dff), F32), ((8, DD), F32),
        ((devices, slab, GRID), BF16),
    ]
    return pl.pallas_call(
        forward_and_decoder,
        out_shape=[jax.ShapeDtypeStruct(s, d) for s, d in kept + made],
        in_specs=[SM, SM, SM] + [VM] * 8 + [ANY] * 9 + [VM] * 5,
        out_specs=[ANY] * len(kept) + [VM] * len(made),
        scratch_shapes=[
            vm(BF16, 2, 3, half, D), vm(BF16, 2, half, D), vm(BF16, 2, D, hid), vm(BF16, 2, hid, D),
            vm(F32, 8, D), vm(F32, LANES, 8, D),
            vm(BF16, 3, DD, DD), vm(BF16, DD, DD), vm(BF16, DD, dff), vm(BF16, dff, DD),
            vm(F32, rows, D), vm(BF16, rows, D), vm(BF16, rows, D), vm(BF16, 2, rows, hid),
            vm(BF16, 2, rows, hid), vm(BF16, 2, 3, rows, half), vm(BF16, 2, 2, PAD, keys),
            vm(BF16, 2, rows, half), vm(F32, rows, D), vm(F32, rows, D), vm(BF16, rows, D),
            vm(BF16, rows, D), vm(BF16, PAD, D), vm(BF16, PAD, D), vm(F32, PAD, D),
            vm(BF16, GRID, DD), vm(F32, GRID, DD), vm(F32, GRID, DD), vm(BF16, GRID, DD),
            vm(BF16, 3, GRID, DD), vm(BF16, GRID // PAD, PAD, DHEADS * PAD), vm(BF16, GRID, DD),
            vm(F32, GRID, DD),
            vm(BF16, GRID, DD), vm(BF16, DD, GRID), vm(BF16, GRID, dff), vm(BF16, GRID, dff),
            vm(F32, GRID, DD), vm(BF16, GRID, DD), vm(BF16, DD, GRID), vm(F32, GRID, DD),
            vm(BF16, PAD, D), vm(BF16, GRID, PAD), vm(BF16, GRID, GRID),
            vm(BF16, LANES, 2, DEC_ROWS, D),
            vm(BF16, devices, slab, GRID), *[vm(BF16, 2, EARLY_ROWS, D)] * 3, vm(BF16, EARLY_ROWS, D),
            dma(8), dma(17), pltpu.SemaphoreType.DMA, dma(4), dma(4), dma(LANES), dma(LANES),
            dma(20), dma(20), dma(6), dma(6), dma(3), dma(3), dma(devices), dma(devices),
            dma(5), dma(5),
        ],
        compiler_params=pltpu.CompilerParams(
            collective_id=0, has_side_effects=True, vmem_limit_bytes=VMEM_LIMIT
        ),
    )(*args)


def add(x, y):
    return x + y


def backward_and_sums(
    d_enc, gains,
    h_u, h_y, h_gp, h_down0, h_down1, h_up0, h_up1,
    h_x, h_x1, h_a, h_qkv, h_p, h_o, h_w0, h_w1, h_proj0, h_proj1,
    dec, dec_qvb, dec_upb, dec_small,
    out, emb, dx_out,
    gb, gt, ut, part, send, recv, du, gx, dx1, d_o, d_acts, own, send1, recv1, dx32, dx,
    d_upb, d_qvb, d_small,
    acc, yacc, enc_mate, rcy, ry, land_x, land_l, land_r, small32, small,
    u, y, gp, down0, down1, up0, up1, x, x1, a, qkv, p, o, w0, w1, proj0, proj1, fetch_s,
    load_s, ex_s, ex_r,
    core_s, core_r, corey_s, corey_r, y_s, y_r, x_s, x_r, z_s, zl_r, zr_r,
    bl_s, br_s, b_r, a_s, a_r, emb_s, emb_r, dx_s, dx_r,
):
    sec = lax.axis_index("section")
    lane = lax.axis_index("tensor")
    pos = lax.axis_index("dp")
    count = lax.axis_size("dp")
    mate = lane + 1 - 2 * lax.rem(lane, 2)
    over = lax.rem(lane + 2, LANES)
    cross = lax.rem(mate + 2, LANES)
    first = pos == 0
    last = pos == count - 1
    me = sec * LANES + lane
    devices = 2 * LANES

    def group_peer(step):
        peer = lax.rem(me + step, devices)
        return peer, {"section": lax.div(peer, LANES), "tensor": lax.rem(peer, LANES)}

    barrier = pltpu.get_barrier_semaphore()
    for step in range(1, devices):
        pl.semaphore_signal(barrier, inc=1, device_id_type=MESH, device_id=group_peer(step)[1])

    @pl.when(pos > 0)
    def _():
        pl.semaphore_signal(barrier, inc=1, device_id={"dp": pos - 1}, device_id_type=MESH)

    @pl.when(pos < count - 1)
    def _():
        pl.semaphore_signal(barrier, inc=1, device_id={"dp": pos + 1}, device_id_type=MESH)

    loads = [
        pltpu.make_async_copy(dec.at[lane], acc.at[:, 0:DEC_ROWS, :], load_s.at[0]),
        pltpu.make_async_copy(
            dec.at[over, :, EARLY_ROWS:DEC_ROWS, :], yacc.at[:, 0 : DEC_ROWS - EARLY_ROWS, :],
            load_s.at[1],
        ),
    ]
    for load in loads:
        load.start()
    fetches = [
        pltpu.make_async_copy(src, dst, fetch_s.at[n])
        for n, (src, dst) in enumerate(
            (
                (h_u, u), (h_y, y), (h_gp, gp), (h_down0, down0), (h_down1, down1), (h_up0, up0),
                (h_up1, up1), (h_x, x), (h_x1, x1), (h_a, a), (h_qkv, qkv), (h_p, p), (h_o, o),
                (h_w0, w0), (h_w1, w1), (h_proj0, proj0), (h_proj1, proj1),
            )
        )
    ]
    for fetch in fetches:
        fetch.start()
    small32[...] = jnp.zeros_like(small32)
    d_small[...] = jnp.zeros_like(d_small)
    gb[0:PAD, :] = d_enc[...]
    ends = jnp.where(first, 0, 1) + jnp.where(last, 0, 1)
    pl.semaphore_wait(barrier, devices - 1 + ends)

    gain = gains[...].astype(F32)
    width = w0.shape[1]
    marks = head_marks(width, ENC_SIZE, BF16)
    marks32 = head_marks(width, ENC_SIZE, F32)
    ones = ones_per_head(PAD, marks)

    def rows(k, size=CH):
        return pl.ds(pl.multiple_of(k * size, size), size)

    def give_enc():
        return far(d_enc, gb.at[PAD : 2 * PAD, :], ex_s.at[0], ex_r.at[0], {"tensor": over})

    def give_part(i, half):
        cut = rows(i, 256)
        n = 1 + 2 * i + half
        return far(
            send.at[(1 - half) * PAD : (2 - half) * PAD, cut],
            recv.at[half * PAD : (half + 1) * PAD, cut],
            ex_s.at[n], ex_r.at[n], {"tensor": over},
        )

    def give_last(i):
        cut = rows(i, 256)
        return far(send1.at[:, cut], recv1.at[:, cut], ex_s.at[7 + i], ex_r.at[7 + i], {"tensor": over})

    def ff_back(g, i, down):
        c = rows(i, 256)
        d_down = nn(gt[...], y[g, :, c]).astype(BF16)
        dh = nt(gb[...], down[c, :]) * gp[g, :, c].astype(F32)
        d_upb[g, :, c] = colsum(dh)
        dub = dh.astype(BF16)
        du[g, :, c] = dub
        d_up = nn(ut[...], dub).astype(BF16)
        if g == 0:
            acc[1, A_TOP:B_TOP, c] = d_down
            acc[0, A_TOP:B_TOP, c] = d_up
        else:
            enc_mate[1, 0:ENC_A, c] = d_down
            enc_mate[0, 0:ENC_A, c] = d_up

    def ff_in(i):
        c = rows(i, 256)
        t = nt(du[0], up0[c, :]) + nt(du[1], up1[c, :])
        part[:, c] = t
        send[:, c] = t.astype(BF16)
        give_part(i, 0).start()
        give_part(i, 1).start()

    def norm_two():
        for fetch in fetches[7:]:
            fetch.wait()
        for k in range(D // 256):
            give_part(k, 0).wait_recv()
            give_part(k, 1).wait_recv()

        def body(j):
            r = rows(j, 64)
            da = part[r, :] + recv[r, :].astype(F32)
            hat, scale = normal(x1[r, :])
            g = gb[r, :].astype(F32)
            d = g + normal_back(da, hat, scale, gain[1:2])
            gx[r, :] = d.astype(BF16)
            dx1[r, :] = d

            @pl.when(j < 2)
            def _():
                d_small[1:2, :] += colsum(da * hat)
                d_small[3:4, :] += colsum(da)
                d_small[4:5, :] += colsum(d)
                d_small[5:6, :] += colsum(g)

        loop(2 * PAD // 64, body)

    def attention(g, c):
        if c == 0:
            d_proj = tn(o[g], gx[...]).astype(BF16)
            if g == 0:
                acc[1, B_TOP + width : S_TOP, :] = d_proj
            else:
                enc_mate[1, ENC_A + width : ENC_A + 2 * width, :] = d_proj
            d_o[...] = nt(gx[...], (proj0, proj1)[g][...]).astype(BF16)
        r = slice(c * PAD, (c + 1) * PAD)
        d_acts[g, 0, r], d_acts[g, 1, r], d_acts[g, 2, r] = attend_back(
            qkv[g, 0, r], qkv[g, 1, r], qkv[g, 2, r], p[g, c], o[g, r], 1.0 / nn(p[g, c], ones),
            d_o[r, :], marks, marks32, None, ones, ENC_SCALE,
        )
        if c == 1:
            d_qvb[g, 0:1, :] = colsum(d_acts[g, 0].astype(F32))
            d_qvb[g, 1:2, :] = colsum(d_acts[g, 2].astype(F32))

    def project_in(i):
        c = rows(i, 256)
        t = 0.0
        for g, w in enumerate((w0, w1)):
            for j in range(3):
                t += nn(d_acts[g, j], w[j, :, c])
        own[:, c] = t[:PAD]
        send1[:, c] = t[PAD:].astype(BF16)
        give_last(i).start()

    def project_grad(g):
        for j in range(3):
            row = (j % 2) * width
            d = tn(d_acts[g, j], a[...]).astype(BF16)
            if g == 0:
                acc[j // 2, B_TOP + row : B_TOP + row + width, :] = d
            else:
                enc_mate[j // 2, ENC_A + row : ENC_A + row + width, :] = d

    def norm_one():
        for k in range(D // 256):
            give_last(k).wait_recv()

        def body(j):
            r = rows(j, 64)
            da = own[r, :] + recv1[r, :].astype(F32)
            hat, scale = normal(x[r, :])
            d_small[0:1, :] += colsum(da * hat)
            d_small[2:3, :] += colsum(da)
            dx32[r, :] = dx1[r, :] + normal_back(da, hat, scale, gain[0:1])

        loop(PAD // 64, body)
        turned = jnp.transpose(dx32[...])
        cut = D // devices
        for k in range(devices):
            dx[k] = turned[k * cut : (k + 1) * cut, 0:VIS].astype(BF16)
        for r in range(LANES):
            small32[r, 8:9, 0:512] = dec_upb[:, r * 512 : (r + 1) * 512]
            small32[r, 9:10, 0:128] = dec_qvb[0:1, r * 128 : (r + 1) * 128]
            small32[r, 9:10, 128:256] = dec_qvb[1:2, r * 128 : (r + 1) * 128]
            small32[r, 0:8, 0:512] = dec_small[...]
            small32[r, 16:24, :] = d_small[...]
        for g, shard in enumerate((lane, mate)):
            small32[shard, 10:11, :] = d_upb[g]
            small32[shard, 11:12, 0:192] = d_qvb[g, 0:1]
            small32[shard, 11:12, 256:448] = d_qvb[g, 1:2]
        for r in range(LANES):
            for h in range(2):
                small[r, h] = small32[r, h * SMALL : (h + 1) * SMALL].astype(BF16)
        acc[:, S_TOP : S_TOP + SMALL, :] = small[lane]
        yacc[:, DEC_ROWS - EARLY_ROWS :, :] = small[over]
        core_copy(LATE, small.at[mate], SMALL).start()
        corey_copy(LATE, small.at[cross], SMALL).start()
        for step in range(1, devices):
            dx_copy(step).start()
        dx_out[me] = dx[me]

    def core_enc(lo, hi):
        def body(m):
            block = block_of(m)

            @pl.when((block >= lo) & (block < hi))
            def _():
                src = pl.ds(pl.multiple_of(block * CH - DEC_ROWS, CH), CH)
                core_copy(m, enc_mate.at[:, src, :]).start()

        loop(ALL_K, body)

    def first_piece():
        for fetch in fetches[:7]:
            fetch.wait()
        ut[...] = jnp.transpose(u[...].astype(F32)).astype(BF16)
        give_enc().wait_recv()
        gt[...] = jnp.transpose(gb[...].astype(F32)).astype(BF16)

    def ff_step(k):
        for g, down in enumerate((down0, down1)):
            @pl.when(lax.rem(k, 2) == g)
            def _(g=g, down=down):
                ff_back(g, lax.div(k, 2), down)

    def run_pieces(n):
        def several(low, high, body):
            begin = sum(jnp.where(n > t, 1, 0) for t in PIECES[low:high])
            end = sum(jnp.where(n >= t, 1, 0) for t in PIECES[low:high])
            lax.fori_loop(begin, end, lambda k, c: (body(k), c)[1], 0)

        def single(k, body):
            @pl.when(n == PIECES[k])
            def _():
                body()

        single(0, first_piece)
        several(1, 7, ff_step)
        single(7, lambda: core_enc(DEC_K, DEC_K + ENC_A // CH))
        several(8, 11, ff_in)
        single(11, norm_two)
        for k in range(4):
            single(12 + k, lambda k=k: attention(k // 2, k % 2))
        several(16, 19, project_in)
        for g in range(2):
            single(19 + g, lambda g=g: project_grad(g))
        single(21, lambda: core_enc(DEC_K + ENC_A // CH, B_K))
        single(22, norm_one)

    def dx_copy(step):
        peer, place = group_peer(step)
        return far(dx.at[peer], dx_out.at[me], dx_s.at[step], dx_r.at[step], place)

    def emb_copy(step):
        return far(
            out.at[:, pl.ds(512, CH), :], emb.at[lane], emb_s.at[step], emb_r.at[step],
            {"tensor": lax.rem(lane + step, LANES)},
        )

    def block_of(m):
        shift = 0
        for k in range(1, ALL_K):
            if ORDER[k] - k != ORDER[k - 1] - k + 1:
                shift = jnp.where(m >= k, ORDER[k] - k, shift)
        return m + shift

    def is_dec(m):
        return (block_of(m) < DEC_K) & (m >= EARLY)

    def at(m, size=CH):
        return pl.ds(pl.multiple_of(block_of(m) * CH, CH), size)

    def slot(m, size=CH):
        return pl.ds(pl.multiple_of(m * CH, CH), size)

    def y_at(m, size=CH):
        return pl.ds(pl.multiple_of((jnp.minimum(block_of(m), DEC_K) - EARLY) * CH, CH), size)

    def core_copy(m, src, size=CH):
        return far(src, out.at[:, at(m, size), :], core_s.at[m], core_r.at[m], {"tensor": mate})

    def corey_copy(m, src, size=CH):
        return far(src, rcy.at[:, y_at(m, size), :], corey_s.at[m], corey_r.at[m], {"tensor": mate})

    def y_copy(m, size=CH):
        cut = y_at(m, size)
        return far(
            yacc.at[:, cut, :], ry.at[:, cut, :], y_s.at[m], y_r.at[m], {"tensor": over}
        )

    def x_copy(m, size=CH):
        return far(
            acc.at[1 - sec, at(m, size), :], land_x.at[0, slot(m, size), :], x_s.at[m], x_r.at[m],
            {"section": 1 - sec},
        )

    def xc_copy(m):
        return far(
            acc.at[:, at(m), :], land_x.at[:, slot(m), :], x_s.at[m], x_r.at[m],
            {"section": 1 - sec},
        )

    def z_copy(m, whole, right, size=CH):
        land = land_l if right else land_r
        if whole:
            src, dst = acc.at[:, at(m), :], land.at[:, slot(m), :]
        else:
            src, dst = acc.at[sec, at(m, size), :], land.at[0, slot(m, size), :]
        landed = zl_r if right else zr_r
        return far(src, dst, z_s.at[m], landed.at[m], {"dp": pos + 1 if right else pos - 1})

    def b_copy(m, whole, right, size=CH):
        place = out.at[:, at(m), :] if whole else out.at[sec, at(m, size), :]
        sent = br_s if right else bl_s
        return far(place, place, sent.at[m], b_r.at[m], {"dp": pos + 1 if right else pos - 1})

    def a_copy(m, size=CH):
        place = out.at[sec, at(m, size), :]
        return far(place, place, a_s.at[m], a_r.at[m], {"section": 1 - sec})

    def a_wait(m, size=CH):
        place = out.at[1 - sec, at(m, size), :]
        far(place, place, a_s.at[m], a_r.at[m], {"section": 1 - sec}).wait_recv()

    give_enc().start()

    def start_core(m):
        @pl.when(is_dec(m))
        def _():
            core_copy(m, dec.at[mate, :, at(m), :]).start()
            corey_copy(m, dec.at[cross, :, at(m), :]).start()

    loop(ALL_K, start_core)
    for load in loads:
        load.wait()

    def join_core(m, size):
        core_copy(m, out.at[:, at(m, size), :], size).wait_recv()
        acc[:, at(m, size), :] = add(acc[:, at(m, size), :], out[:, at(m, size), :])

    def join_core_y(m, size):
        corey_copy(m, rcy.at[:, y_at(m, size), :], size).wait_recv()
        yacc[:, y_at(m, size), :] = add(yacc[:, y_at(m, size), :], rcy[:, y_at(m, size), :])
        y_copy(m, size).start()

    def stage_c(m):
        @pl.when((m >= EARLY) & (m != LATE))
        def _():
            join_core(m, CH)

            @pl.when(is_dec(m))
            def _():
                join_core_y(m, CH)

        @pl.when(m == LATE)
        def _():
            join_core(m, SMALL)
            join_core_y(m, SMALL)

    def finished(m):
        @pl.when(block_of(m) == DEC_K - 1)
        def _():
            for step in range(1, LANES):
                emb_copy(step).start()
            emb[lane] = out[:, 512 : 512 + CH, :]

    def line_of(root, whole, size=CH):
        left = pos < root
        right = pos > root
        here = pos == root
        reach = max(root, count - 1 - root)
        level = jnp.where(left, pos, jnp.where(right, count - 1 - pos, reach))
        dist = jnp.where(left, root - pos, pos - root)

        def view(ref, m):
            return ref.at[:, at(m), :] if whole else ref.at[sec, at(m, size), :]

        def landed(ref, m):
            return ref.at[:, slot(m), :] if whole else ref.at[0, slot(m, size), :]

        def hop(m, rightward):
            return z_copy(m, whole, rightward, size)

        def back_hop(m, rightward):
            return b_copy(m, whole, rightward, size)

        def outer(m):
            @pl.when(left & first)
            def _():
                hop(m, True).start()

            @pl.when(right & last)
            def _():
                hop(m, False).start()

        def inward(m):
            @pl.when(left & (pos > 0))
            def _():
                hop(m, True).wait_recv()
                view(acc, m)[...] = add(view(acc, m)[...], landed(land_l, m)[...])
                hop(m, True).start()

            @pl.when(right & (pos < count - 1))
            def _():
                hop(m, False).wait_recv()
                view(acc, m)[...] = add(view(acc, m)[...], landed(land_r, m)[...])
                hop(m, False).start()

            @pl.when(here)
            def _():
                total = view(acc, m)[...].astype(F32)
                if root > 0:
                    hop(m, True).wait_recv()
                    total = total + landed(land_l, m)[...].astype(F32)
                if root < count - 1:
                    hop(m, False).wait_recv()
                    total = total + landed(land_r, m)[...].astype(F32)
                if whole:
                    view(acc, m)[...] = total.astype(BF16)
                    xc_copy(m).start()
                else:
                    view(out, m)[...] = total.astype(BF16)
                    spread(m)
                    a_copy(m, size).start()

        def spread(m):
            if root > 0:
                back_hop(m, False).start()
            if root < count - 1:
                back_hop(m, True).start()

        def crossed(m):
            xc_copy(m).wait_recv()
            view(out, m)[...] = add(view(acc, m)[...], landed(land_x, m)[...])
            spread(m)
            finished(m)

        def outward(m):
            back_hop(m, False).wait_recv()

            @pl.when(left & (pos > 0))
            def _():
                back_hop(m, False).start()

            @pl.when(right & (pos < count - 1))
            def _():
                back_hop(m, True).start()

            if whole:
                finished(m)
            else:
                a_copy(m, size).start()

        def sent(m):
            @pl.when(jnp.logical_not(here))
            def _():
                hop(m, True).wait_send()

            @pl.when((pos <= root) & (pos > 0))
            def _():
                back_hop(m, False).wait_send()

            @pl.when((pos >= root) & (pos < count - 1))
            def _():
                back_hop(m, True).wait_send()

            if whole:
                @pl.when(here)
                def _():
                    xc_copy(m).wait_send()
            else:
                a_copy(m, size).wait_send()

                @pl.when(crosses_first(m))
                def _():
                    x_copy(m, size).wait_send()

        def crosses_first(m):
            return m >= EARLY if XFIRST else m >= 0

        def set_off(m):
            if whole:
                outer(m)
            else:
                x_copy(m, size).start()

        def set_off_early(m):
            if XFIRST:
                outer(m)
            else:
                set_off(m)

        def add_y(m):
            def joined():
                y_copy(m, size).wait_recv()
                acc[:, at(m, size), :] = add(acc[:, at(m, size), :], ry[:, y_at(m, size), :])

            if size == CH:
                pl.when(is_dec(m))(joined)
            else:
                joined()
            set_off(m)

        def add_x(m):
            @pl.when(crosses_first(m))
            def _():
                x_copy(m, size).wait_recv()
                acc[sec, at(m, size), :] = add(
                    acc[sec, at(m, size), :], land_x[0, slot(m, size), :]
                )
                outer(m)

        def last_half(m):
            a_wait(m, size)
            finished(m)

        base = 1 if whole else 2
        back = base + reach + dist + (1 if whole else 0)
        steps = [(back, jnp.logical_not(here), outward), (base + level, level > 0, inward)]
        if whole:
            steps.append((base + reach + 1, here, crossed))
        else:
            steps += [(back + 1, True, last_half), (2, True, add_x)]
        return steps, sent, add_y, set_off_early

    low_root = (count - 1) // 2
    high_root = min(low_root + 1, count - 1)
    def is_whole(m):
        return (lax.rem(m, 2) == 0) & (m >= WHOLE_LOW) & (m < WHOLE_HIGH)

    roots = (high_root, count - 1, low_root, 0)
    lines = [
        (lambda m, part=part: is_whole(m) & (lax.rem(m, 8) == part), *line_of(root, True))
        for part, root in zip((0, 2, 4, 6), roots)
    ] + [
        (lambda m: jnp.logical_not(is_whole(m)) & (m != LATE), *line_of(low_root, False)),
        (lambda m: m == LATE, *line_of(low_root, False, SMALL)),
    ]

    def finish(m):
        @pl.when((m >= EARLY) & (m != LATE))
        def _():
            core_copy(m, out.at[:, at(m), :]).wait_send()

            @pl.when(is_dec(m))
            def _():
                corey_copy(m, rcy.at[:, y_at(m), :]).wait_send()
                y_copy(m).wait_send()

        @pl.when(m == LATE)
        def _():
            core_copy(m, out.at[:, at(m, SMALL), :], SMALL).wait_send()
            corey_copy(m, rcy.at[:, y_at(m, SMALL), :], SMALL).wait_send()
            y_copy(m, SMALL).wait_send()

        for mine, _, sent, _, _ in lines:
            @pl.when(mine(m))
            def _(sent=sent):
                sent(m)

    def set_off_early(m):
        for mine, _, _, _, set_off in lines:
            @pl.when(mine(m))
            def _(set_off=set_off):
                set_off(m)

    loop(EARLY, set_off_early)
    far_reach = max(max(root, count - 1 - root) for root in roots)
    depth = LAG * (3 + 2 * far_reach) + 1

    def tick(n):
        @pl.when(n <= PIECES[-1])
        def _():
            run_pieces(n)

        for mine, steps, _, add_y, _ in lines:
            m = n - LAG

            @pl.when((m >= EARLY) & (m < ALL_K))
            def _(m=m, mine=mine, add_y=add_y):
                @pl.when(mine(m))
                def _():
                    add_y(m)

            for offset, enabled, stage in steps:
                m = n - LAG * offset

                @pl.when((m >= 0) & (m < ALL_K) & enabled)
                def _(m=m, mine=mine, stage=stage):
                    @pl.when(mine(m))
                    def _():
                        stage(m)

        @pl.when(n < ALL_K)
        def _():
            stage_c(n)

        @pl.when(n >= depth)
        def _():
            finish(n - depth)

    loop(ALL_K + depth, tick)

    for step in range(1, devices):
        dx_copy(step).wait()
    for step in range(1, LANES):
        emb_copy(step).wait()
    give_enc().wait_send()
    for k in range(D // 256):
        give_part(k, 0).wait_send()
        give_part(k, 1).wait_send()
        give_last(k).wait_send()


def backward_call(args, half, hid):
    dma = lambda *s: pltpu.SemaphoreType.DMA(s)
    vm = pltpu.VMEM
    full = ALL_K * CH
    y_half = DEC_ROWS - EARLY_ROWS + SMALL
    k = ALL_K
    rows = 2 * PAD
    cut = D // (2 * LANES)
    specs = [VM, VM] + [ANY] * 18 + [VM] * 3
    return pl.pallas_call(
        backward_and_sums,
        out_shape=[
            jax.ShapeDtypeStruct((2, full, D), BF16),
            jax.ShapeDtypeStruct((LANES, 2, CH, D), BF16),
            jax.ShapeDtypeStruct((2 * LANES, cut, VIS), BF16),
        ],
        in_specs=specs,
        out_specs=[VM] * 3,
        scratch_shapes=[
            vm((rows, D), BF16), vm((D, rows), BF16), vm((D, rows), BF16),
            vm((rows, D), F32), vm((rows, D), BF16), vm((rows, D), BF16),
            vm((2, rows, hid), BF16), vm((rows, D), BF16), vm((rows, D), F32),
            vm((rows, half), BF16), vm((2, 3, rows, half), BF16),
            vm((PAD, D), F32), vm((PAD, D), BF16), vm((PAD, D), BF16), vm((PAD, D), F32),
            vm((2 * LANES, cut, VIS), BF16),
            vm((2, 1, hid), F32), vm((2, 2, half), F32), vm((8, D), F32),
            vm((2, full, D), BF16), vm((2, y_half, D), BF16), vm((2, ENC_A + ENC_B, D), BF16),
            vm((2, y_half, D), BF16), vm((2, y_half, D), BF16),
            *[vm((2, full, D), BF16)] * 3,
            vm((LANES, 32, D), F32), vm((LANES, 2, SMALL, D), BF16),
            *[vm(v.shape, v.dtype) for v in args[2:19]],
            dma(17), dma(2), dma(10), dma(10),
            dma(k), dma(k), dma(k), dma(k), dma(k), dma(k),
            dma(k), dma(k), dma(k), dma(k), dma(k),
            dma(k), dma(k), dma(k), dma(k), dma(k), dma(LANES), dma(LANES),
            dma(2 * LANES), dma(2 * LANES),
        ],
        compiler_params=pltpu.CompilerParams(
            collective_id=1, has_side_effects=True, vmem_limit_bytes=VMEM_LIMIT
        ),
    )(*args)


def finish_grads(
    total, emb, decoded, dx, decoded_out, dx_out,
    e_qkv, e_qvb, e_proj, e_up, e_upb, e_down, e_gain, e_off,
    d_qkv, d_qvb, d_proj, d_up, d_upb, d_down, d_gain, d_off, d_ew, d_ev,
):
    half = e_proj.shape[0]
    decoded_out[...] = decoded[...]
    dx_out[...] = dx[...]
    e_up[...] = total[0, A_TOP:B_TOP, :].astype(F32)
    e_down[...] = jnp.transpose(total[1, A_TOP:B_TOP, :].astype(F32))
    e_qkv[0] = total[0, B_TOP : B_TOP + half, :].astype(F32)
    e_qkv[1] = total[0, B_TOP + half : S_TOP, :].astype(F32)
    e_qkv[2] = total[1, B_TOP : B_TOP + half, :].astype(F32)
    e_proj[...] = total[1, B_TOP + half : S_TOP, :].astype(F32)

    def tile(number):
        h, top, col = tile_of(number)
        return total[h, top : top + CH, col : col + 256].astype(F32)

    for block in range(GRID // CH):
        rows = slice(block * CH, (block + 1) * CH)
        side = slice(block // 2 * 128, (block // 2 + 1) * 128)
        for k in range(2):
            d_up[rows, k * 256 : (k + 1) * 256] = tile(4 * block + k)
            if block % 2:
                both = jnp.concatenate([tile(4 * block - 2 + k), tile(4 * block + 2 + k)], 0)
                d_down[k * 256 : (k + 1) * 256, side] = jnp.transpose(both)
        one, two = tile(32 + 2 * block), tile(33 + 2 * block)
        d_qkv[0, rows, :] = one[:, 0:128]
        d_qkv[1, rows, :] = one[:, 128:256]
        d_qkv[2, rows, :] = two[:, 0:128]
        d_proj[block % 2 * CH : (block % 2 + 1) * CH, side] = two[:, 128:256]
    for k in range(LANES):
        for h in range(2):
            top = k * 192 + h * 64
            d_ew[top : top + 64, :] = emb[k, h, :, 0:512].astype(F32)
            d_ew[k * 192 + 128 : (k + 1) * 192, h * 256 : (h + 1) * 256] = emb[
                k, h, :, 512:768
            ].astype(F32)
    little = total[0, S_TOP : S_TOP + SMALL, :].astype(F32)
    d_gain[...] = little[0:2, 0:512]
    d_off[...] = little[2:6, 0:512]
    d_ev[...] = little[6:8, 0:512]
    d_upb[...] = little[8, 0:512]
    d_qvb[0:1, :] = little[9:10, 0:128]
    d_qvb[1:2, :] = little[9:10, 128:256]
    e_upb[...] = little[10]
    e_qvb[0:1, :] = little[11:12, 0:192]
    e_qvb[1:2, :] = little[11:12, 256:448]
    little = total[1, S_TOP : S_TOP + SMALL, :].astype(F32)
    e_gain[...] = little[0:2]
    e_off[...] = little[2:6]


def call(kernel, specs, shapes, scratch, args):
    return pl.pallas_call(
        kernel,
        out_shape=[jax.ShapeDtypeStruct(s, d) for s, d in shapes],
        in_specs=specs,
        out_specs=[VM] * len(shapes),
        scratch_shapes=scratch,
        compiler_params=pltpu.CompilerParams(vmem_limit_bytes=VMEM_LIMIT),
    )(*args)


def position_rows():
    quarter = DD // 4
    freq = np.exp(np.arange(quarter, dtype=np.float32) * np.float32(-math.log(10000.0) / quarter))
    angle = np.arange(PAD, dtype=np.float32)[:, None] * freq[None, :].astype(np.float32)
    both = np.concatenate([np.sin(angle), np.cos(angle)], 1).astype(np.float32)
    high = both.astype(jnp.bfloat16)
    low = (both - high.astype(np.float32)).astype(jnp.bfloat16)
    return np.stack([high, low])


def per_device(
    patches, cotangent, widths, visible, window_shift, batch_order,
    encoder_qkv, encoder_qvbias, encoder_proj, encoder_up, encoder_upbias, encoder_down,
    encoder_gains, encoder_offsets,
    decoder_qkv, decoder_qvbias, decoder_proj, decoder_up, decoder_upbias, decoder_down,
    decoder_gains, decoder_offsets, embed_weight, embed_vectors,
):
    qkv0 = encoder_qkv.transpose(1, 2, 0)
    half = qkv0.shape[1]
    hid = encoder_up.shape[1]
    dff = decoder_up.shape[1] * LANES
    flat = patches.transpose(1, 0, 2).reshape(-1, D)
    (
        x, x1, a, u, y, gp, qkv, p, o, qkv1, proj1, up1, down1, dec_buf,
        d_enc, d_dqvb, d_dupb, d_dsmall, out_all,
    ) = forward_call(
        (
            widths, window_shift.T, batch_order, visible, flat, encoder_gains, encoder_offsets,
            encoder_qvbias, encoder_upbias, decoder_qvbias, decoder_upbias,
            qkv0, encoder_proj, encoder_up, encoder_down,
            decoder_qkv.transpose(1, 0, 2), decoder_proj, decoder_up, decoder_down,
            cotangent, embed_weight, embed_vectors, jnp.asarray(position_rows()),
            decoder_gains, decoder_offsets,
        ),
        half, hid, dff,
    )
    total, emb, dx_all = backward_call(
        (
            d_enc, encoder_gains, u, y, gp, encoder_down, down1, encoder_up, up1,
            x, x1, a, qkv, p, o, qkv0, qkv1, encoder_proj, proj1,
            dec_buf, d_dqvb, d_dupb, d_dsmall,
        ),
        half, hid,
    )
    f = lambda *shape: (shape, F32)
    out_all, dx_all, *grads = call(
        finish_grads, [VM] * 4,
        [
            (out_all.shape, BF16), (dx_all.shape, BF16), f(3, half, D), f(2, half), f(half, D), f(D, hid), f(hid), f(hid, D), f(2, D), f(4, D),
            f(3, DD, 128), f(2, 128), f(128, DD), f(DD, 512), f(512), f(512, DD), f(2, DD), f(4, DD),
            f(D, DD), f(2, DD),
        ],
        [], (total, emb, out_all, dx_all),
    )
    grads[0] = grads[0].transpose(2, 0, 1)
    grads[8] = grads[8].transpose(1, 0, 2)
    return (out_all.swapaxes(1, 2), dx_all.swapaxes(1, 2), *grads)


def solution(mesh):
    weights = (
        P(None, None, "tensor"), P(None, "tensor"), P("tensor", None), P(None, "tensor"),
        P("tensor"), P("tensor", None), P(), P(),
    )
    split = P("dp", None, ("section", "tensor"))
    return jax.shard_map(
        per_device,
        mesh=mesh,
        in_specs=(
            P("dp", None, None), P("dp", None, None), P("dp"), P("dp", None), P("dp", None),
            P("dp", None),
        ) + weights + weights + (P(), P()),
        out_specs=(split, split) + weights + weights + (P(), P()),
        check_vma=False,
    )
```

```python
import math

import jax
import jax.numpy as jnp
import numpy as np
from jax import lax
from jax.experimental import pallas as pl
from jax.experimental.pallas import tpu as pltpu
from jax.sharding import PartitionSpec as P

D = 768
HEADS = 12
DD = 512
DHEADS = 16
GRID_ROWS = 64
WIDE = 8
WIN = 4
VIS = 102
CM = 4
GRID = 512
LANES = 4
PAD = 128
EPS = 1e-06
NEG = -10000.0
F32 = jnp.float32
BF16 = jnp.bfloat16
VMEM_LIMIT = 60 * 1024 * 1024

VM = pl.BlockSpec(memory_space=pltpu.VMEM)
SM = pl.BlockSpec(memory_space=pltpu.SMEM)
ANY = pl.BlockSpec(memory_space=pl.ANY)


def nn(a, b):
    return lax.dot_general(a, b, (((1,), (0,)), ((), ())), preferred_element_type=F32)


def nt(a, b):
    return lax.dot_general(a, b, (((1,), (1,)), ((), ())), preferred_element_type=F32)


def tn(a, b):
    return lax.dot_general(a, b, (((0,), (0,)), ((), ())), preferred_element_type=F32)


def loop(count, body, unroll=1):
    def step(i, carry):
        body(i)
        return carry

    lax.fori_loop(0, count, step, 0, unroll=unroll)


def span(i, size):
    return pl.ds(pl.multiple_of(i * size, size), size)


def normal(x):
    center = x - jnp.mean(x, -1, keepdims=True)
    scale = lax.rsqrt(jnp.mean(center * center, -1, keepdims=True) + EPS)
    return center * scale, scale


def normal_back(dy, hat, scale, gain):
    d = dy * gain
    return scale * (
        d - jnp.mean(d, -1, keepdims=True) - hat * jnp.mean(d * hat, -1, keepdims=True)
    )


def gelu_both(h):
    phi = 0.5 * lax.erf(h * math.sqrt(0.5)) + 0.5
    bell = jnp.exp2(h * h * (-0.5 * math.log2(math.e)))
    return h * phi, phi + h * bell * (1.0 / math.sqrt(2.0 * math.pi))


def colsum(x):
    return jnp.sum(x, 0, keepdims=True)


def head_marks(width, size, dtype):
    lane = lax.broadcasted_iota(jnp.int32, (1, width), 1)
    return [((lane >= h * size) & (lane < (h + 1) * size)).astype(dtype) for h in range(width // size)]


def stacked(x, marks):
    return jnp.concatenate([x * m for m in marks], 0)


LOG2E = math.log2(math.e)


def attend(q, k, v, marks, ones, masked, scale):
    keys = k.shape[0]
    s = nt(q, stacked(k, marks))
    parts = []
    for h in range(len(marks)):
        x = masked(s[:, h * keys : (h + 1) * keys] * (scale * LOG2E))
        parts.append(jnp.exp2(x - jnp.max(x, -1, keepdims=True)).astype(BF16))
    e = jnp.concatenate(parts, 1)
    width = q.shape[1]
    if width % 128:
        top, total = nn(e, stacked(v, marks)), nn(e, ones)
    else:
        both = nn(e, jnp.concatenate([stacked(v, marks), ones], 1))
        top, total = both[:, :width], both[:, width:]
    inverse = 1.0 / total
    return e, (top * inverse).astype(BF16), inverse


def attend_back(q, k, v, e, o, inverse, d_out, marks, marks32, rows32, ones, scale):
    keys = k.shape[0]
    width = q.shape[1]
    d_one = d_out.astype(F32) * inverse
    d_two = (d_one * o.astype(F32)).astype(BF16)
    d_one = d_one.astype(BF16)
    if width % 128:
        d_s = nt(d_one, stacked(v, marks)) - nt(d_two, ones)
    else:
        d_s = nt(
            jnp.concatenate([d_one, d_two], 1), jnp.concatenate([stacked(v, marks), -ones], 1)
        )
    dr = (e.astype(F32) * d_s * scale).astype(BF16)
    d_q = nn(dr, stacked(k, marks)).astype(BF16)
    if width % 128:
        d_k_all, d_v_all = tn(dr, q), tn(e, d_one)
        d_k = d_v = 0.0
        for h in range(len(marks)):
            cut = slice(h * keys, (h + 1) * keys)
            d_k += d_k_all[cut] * marks32[h]
            d_v += d_v_all[cut] * marks32[h]
        return d_q, d_k.astype(BF16), d_v.astype(BF16)
    d_k_all = nn(jnp.transpose(q.astype(F32)).astype(BF16), dr)
    d_v_all = nn(jnp.transpose(d_one.astype(F32)).astype(BF16), e)
    d_k = d_v = 0.0
    for h in range(len(marks)):
        cut = slice(h * keys, (h + 1) * keys)
        d_k += d_k_all[:, cut] * rows32[h]
        d_v += d_v_all[:, cut] * rows32[h]
    return d_q, jnp.transpose(d_k).astype(BF16), jnp.transpose(d_v).astype(BF16)


def ones_per_head(keys, marks):
    return jnp.concatenate([jnp.broadcast_to(m, (keys, m.shape[1])) for m in marks], 0)


ENC_SIZE = D // HEADS
ENC_SCALE = ENC_SIZE ** -0.5
DEC_SIZE = DD // DHEADS
DEC_SCALE = DEC_SIZE ** -0.5


CH = 64
DEC_ROWS = 576
ENC_A = 768
ENC_B = 384
DEC_K = DEC_ROWS // CH
B_K = (DEC_ROWS + ENC_A + ENC_B) // CH
ALL_K = B_K + 1
A_TOP = DEC_ROWS
B_TOP = DEC_ROWS + ENC_A
S_TOP = B_TOP + ENC_B
EARLY = 4
XFIRST = True
EARLY_ROWS = EARLY * CH
LAG = 2
ORDER = (0, 1, 2, 3, 9, 10, 11, 12, 13, 14, 15, 16, 17, 4, 18, 5, 19, 20, 6, 8, 21, 22, 23, 24, 27, 25, 26, 7)
PIECES = (2, 2, 3, 3, 3, 3, 3, 3, 3, 3, 3, 10, 10, 11, 12, 12, 13, 15, 15, 16, 16, 18, 20)
LATE = ORDER.index(B_K)
WHOLE_LOW = 6
WHOLE_HIGH = 22
SMALL = 16


def tile_of(number):
    place = number // 3
    return place % 2, place // 2 * CH, number % 3 * 256


MESH = pl.DeviceIdType.MESH


def far(src, dst, send, recv, peer):
    return pltpu.make_async_remote_copy(
        src_ref=src, dst_ref=dst, send_sem=send, recv_sem=recv, device_id=peer, device_id_type=MESH
    )


def forward_and_decoder(
    wid, shifts, order, vis, pat, gains, offs, b_qv, b_up, b_dqv, b_dup,
    h_qkv, h_proj, h_up, h_down, h_dqkv, h_dproj, h_dup, h_ddown,
    cot_hbm, ew, evec, table, dgains, doffs,
    o_x, o_x1, o_a, o_u, o_y, o_gp, o_qkv, o_p, o_o, o_w, o_wproj, o_wup, o_wdown, o_dec, o_slabs,
    d_enc, d_qvb, d_upb, d_small,
    w_qkv, w_proj, w_up, w_down, bias, biases, qkv, proj, up, down,
    ex, ea, eu, ey, egp, eqkv, ep, eo, ex1, epart, esend, erecv, esend2, erecv2, eown,
    cot, x0, x1, a, acts, probs, o, inverse, u, ut, y, gp, g32, gb, gt, acc, e_ref, hot, perm, buf, dsend, e_rc, e_rcy, e_rx, e_ry,
    load_s, out_s, cot_s, w_s, w_r, bias_s, bias_r, dw_s, dw_r, ex_s, ex_r, ex2_s, ex2_r, e_s, e_r,
):
    sec = lax.axis_index("section")
    lane = lax.axis_index("tensor")
    mate = lane + 1 - 2 * lax.rem(lane, 2)
    over = lax.rem(lane + 2, LANES)
    cross = lax.rem(mate + 2, LANES)
    me = sec * LANES + lane
    devices = 2 * LANES
    clip = me
    clips = (me, sec * LANES + over)

    def group_peer(step):
        peer = lax.rem(me + step, devices)
        return peer, {"section": lax.div(peer, LANES), "tensor": lax.rem(peer, LANES)}

    own = [
        pltpu.make_async_copy(src, dst.at[0], load_s.at[n])
        for n, (src, dst) in enumerate(
            ((h_qkv, w_qkv), (h_proj, w_proj), (h_up, w_up), (h_down, w_down))
        )
    ]

    def place(n, shard, part=None):
        thick = (128, 128, 512, 512)[n]
        base = shard * thick
        cut = pl.ds(pl.multiple_of(base, thick), thick)
        if part is None:
            return (qkv.at[:, :, cut], proj.at[cut, :], up.at[:, cut], down.at[cut, :])[n]
        some = span(part, (256, 64, 256, 256)[n])
        if n == 0:
            return qkv.at[:, some, cut]
        if n == 2:
            return up.at[some, cut]
        few = thick // 2
        rows = pl.ds(pl.multiple_of(base + part * few, few), few)
        return (proj if n == 1 else down).at[rows, :]

    shards = (h_dqkv, h_dproj, h_dup, h_ddown)
    keep = [
        pltpu.make_async_copy(shards[n], place(n, lane), load_s.at[4 + n]) for n in range(4)
    ]
    for copy in own + keep:
        copy.start()
    fetch = pltpu.make_async_copy(cot_hbm.at[clip], cot, cot_s)
    fetch.start()

    barrier = pltpu.get_barrier_semaphore()
    for step in range(1, devices):
        pl.semaphore_signal(barrier, inc=1, device_id_type=MESH, device_id=group_peer(step)[1])
    bias[...] = jnp.zeros_like(bias)
    half = w_proj.shape[1]
    bias[0:1, :] = b_up[...].astype(F32).reshape(1, -1)
    bias[1:3, 0:half] = b_qv[...].astype(F32)
    bias[3:4, 0:512] = b_dup[...].astype(F32).reshape(1, -1)
    bias[4:6, 0:128] = b_dqv[...].astype(F32)
    biases[lane] = bias[...]
    pl.semaphore_wait(barrier, devices - 1)

    def enc_weight(n):
        src = (h_qkv, h_proj, h_up, h_down)[n]
        dst = (w_qkv, w_proj, w_up, w_down)[n]
        return far(src, dst.at[1], w_s.at[n], w_r.at[n], {"tensor": mate})

    def bias_copy(step):
        return far(
            bias, biases.at[lane], bias_s.at[step], bias_r.at[step],
            {"tensor": lax.rem(lane + step, LANES)},
        )

    def half_of(n):
        some = span(sec, (256, 64, 256, 256)[n])
        return shards[n].at[:, some, :] if n == 0 else shards[n].at[some, :]

    def dec_weight(n, kind):
        peer = {"section": 1 - sec} if kind == 2 else {"tensor": over if kind == 0 else mate}
        if kind == 0:
            src, dst = half_of(n), place(n, lane, sec)
        elif kind == 1:
            src, dst = shards[n], place(n, lane)
        else:
            src = dst = place(n, over, 1 - sec if kind == 4 else sec)
        return far(src, dst, dw_s.at[5 * n + kind], dw_r.at[5 * n + kind], peer)

    enc_weight(0).start()
    for step in range(1, LANES):
        bias_copy(step).start()
    enc_weight(1).start()
    dec_weight(0, 0).start()
    enc_weight(2).start()
    enc_weight(3).start()
    for n in range(4):
        dec_weight(n, 1).start()

    def pass_on(n):
        dec_weight(n, 0).wait_recv()
        dec_weight(n, 2).start()
        dec_weight(n, 3).start()

    def pass_last(n):
        dec_weight(n, 2).wait_recv()
        dec_weight(n, 4).start()

    def arrived(n):
        keep[n].wait()
        dec_weight(n, 1).wait_recv()
        dec_weight(n, 3).wait_recv()
        dec_weight(n, 4).wait_recv()

    width = wid[clip]
    bits = jnp.where(width == WIDE, 3, 2)
    turn = shifts[0, clip] * width
    mod = GRID - 1
    spot = 0
    for i in range(order.shape[1]):
        spot = spot + jnp.where(order[0, i] == clip, i, 0)
    batch = spot // CM
    count = 0
    for i in range(order.shape[1]):
        count = count + jnp.where(batch == i // CM, wid[order[0, i]], 0)
    factor_rows = CM * GRID / (jnp.full((1, 1), count, jnp.int32) * GRID_ROWS).astype(F32)

    def slot_of(index):
        return (index - turn) & mod

    def code_of(slot):
        band = ((slot >> bits) + shifts[0, clip]) >> 2
        strip = ((slot & (width - 1)) + shifts[1, clip]) >> 2
        return band * 4 + strip

    def valid_rows():
        slot = slot_of(lax.broadcasted_iota(jnp.int32, (GRID, 1), 0))
        return (slot < GRID_ROWS * width).astype(F32)

    def clip_gradient():
        fetch.wait()
        rolled = slot_of(lax.broadcasted_iota(jnp.int32, (GRID, GRID), 0))
        column = lax.broadcasted_iota(jnp.int32, (GRID, GRID), 1)
        perm[...] = (rolled == column).astype(F32).astype(BF16)
        g = nn(perm[...], cot[...]) * valid_rows() * factor_rows
        g32[...] = g
        gb[...] = g.astype(BF16)
        gt[...] = jnp.transpose(g).astype(BF16)
        d_small[...] = jnp.zeros_like(d_small)
        d_small[5:6, :] = colsum(g)

    seen = vis[pl.ds(clip, 1), :]
    target = jnp.concatenate([(seen + turn) & mod, jnp.full((1, PAD - VIS), -1, jnp.int32)], 1)

    def places(i):
        r = span(i, PAD)
        index = lax.broadcasted_iota(jnp.int32, (PAD, PAD), 0) + i * PAD
        column = lax.broadcasted_iota(jnp.int32, (PAD, PAD), 1)
        hot[r, :] = (index == target).astype(F32).astype(BF16)
        slot = slot_of(index)
        by_row = ((slot >> bits) == column).astype(F32).astype(BF16)
        by_col = ((slot & (width - 1)) == column).astype(F32).astype(BF16)
        row_part = nn(by_row, table[0]) + nn(by_row, table[1])
        col_part = nn(by_col, table[0]) + nn(by_col, table[1])
        x0[r, :] = jnp.concatenate([row_part, col_part], 1)

    egain = gains[...].astype(F32)
    eoff = offs[...].astype(F32)
    stride = pat.shape[0] // VIS
    for c in range(2):
        row = lax.broadcasted_iota(jnp.int32, (PAD, pat.shape[0]), 0)
        col = lax.broadcasted_iota(jnp.int32, (PAD, pat.shape[0]), 1)
        pick = (col == row * stride + clips[c]).astype(F32).astype(BF16)
        ex[c * PAD : (c + 1) * PAD, :] = nn(pick, pat[...])

    emarks = head_marks(half, ENC_SIZE, BF16)
    key = lax.broadcasted_iota(jnp.int32, (PAD, PAD), 1)
    floor = jnp.where(key < VIS, NEG * LOG2E, -1e30)
    eones = ones_per_head(PAD, emarks)
    blocks = D // 256

    def give_part(i, side):
        cut = span(i, 256)
        return far(
            esend.at[(1 - side) * PAD : (2 - side) * PAD, cut],
            erecv.at[side * PAD : (side + 1) * PAD, cut],
            ex_s.at[2 * i + side], ex_r.at[2 * i + side], {"tensor": over},
        )

    for c in range(2):
        rows = slice(c * PAD, (c + 1) * PAD)
        hat, _ = normal(ex[rows, :])
        ea[rows, :] = (hat * egain[0:1] + eoff[0:1]).astype(BF16)
        limit = (VIS * wid[clips[c]]) // WIDE
        for g, shard in enumerate((lane, mate)):
            if c == 0 and g == 0:
                own[0].wait()
            if c == 0 and g == 1:
                enc_weight(0).wait_recv()
                for step in range(1, LANES):
                    bias_copy(step).wait_recv()
            if g == 0:
                bq, bv = bias[1:2, 0:half], bias[2:3, 0:half]
            else:
                bq, bv = biases[shard, 1:2, 0:half], biases[shard, 2:3, 0:half]
            eqkv[g, 0, rows] = (nt(ea[rows, :], w_qkv[g, 0]) + bq).astype(BF16)
            eqkv[g, 1, rows] = nt(ea[rows, :], w_qkv[g, 1]).astype(BF16)
            eqkv[g, 2, rows] = (nt(ea[rows, :], w_qkv[g, 2]) + bv).astype(BF16)
            p, out, _ = attend(
                eqkv[g, 0, rows], eqkv[g, 1, rows], eqkv[g, 2, rows], emarks, eones,
                lambda s: jnp.where(key < limit, s, floor), ENC_SCALE,
            )
            ep[g, c] = p
            eo[g, rows] = out
        if c == 0:
            own[1].wait()
            enc_weight(1).wait_recv()
        for i in range(blocks):
            cut = slice(i * 256, (i + 1) * 256)
            t = nn(eo[0, rows], w_proj[0, :, cut]) + nn(eo[1, rows], w_proj[1, :, cut])
            epart[rows, cut] = t
            esend[rows, cut] = t.astype(BF16)
            give_part(i, 1 - c).start()
    pass_on(0)
    clip_gradient()
    own[2].wait()
    enc_weight(2).wait_recv()

    def give_last(i):
        cut = span(i, 256)
        return far(
            esend2.at[:, cut], erecv2.at[:, cut], ex2_s.at[i], ex2_r.at[i], {"tensor": over}
        )

    for c in (1, 0):
        rows = slice(c * PAD, (c + 1) * PAD)
        for i in range(blocks):
            give_part(i, c).wait_recv()
        t = ex[rows, :] + epart[rows, :] + erecv[rows, :].astype(F32) + eoff[2:3]
        ex1[rows, :] = t
        hat, _ = normal(t)
        eu[rows, :] = (hat * egain[1:2] + eoff[1:2]).astype(BF16)
        for g, shard in enumerate((lane, mate)):

            def enc_ff(i, g=g, shard=shard, rows=rows):
                cut = span(i, 256)
                h = nn(eu[rows, :], w_up[g, :, cut]) + biases[shard, 0:1, cut]
                act, slope = gelu_both(h)
                ey[g, rows, cut] = act.astype(BF16)
                egp[g, rows, cut] = slope.astype(BF16)

            loop(w_up.shape[2] // 256, enc_ff, unroll=3)
        if c == 1:
            own[3].wait()
            enc_weight(3).wait_recv()
        for i in range(blocks):
            cut = slice(i * 256, (i + 1) * 256)
            t = nn(ey[0, rows], w_down[0, :, cut]) + nn(ey[1, rows], w_down[1, :, cut])
            if c == 0:
                eown[:, cut] = t
            else:
                esend2[:, cut] = t.astype(BF16)
                give_last(i).start()
        if c == 1:
            for n in (1, 2, 3):
                dec_weight(n, 0).start()
            pass_last(0)
    outs = [
        pltpu.make_async_copy(src, dst, out_s.at[n])
        for n, (src, dst) in enumerate(
            (
                (ex.at[0:PAD, :], o_x), (ex1, o_x1), (ea, o_a), (eu, o_u), (ey, o_y), (egp, o_gp),
                (eqkv, o_qkv), (ep, o_p), (eo, o_o), (w_qkv.at[1], o_w), (w_proj.at[1], o_wproj),
                (w_up.at[1], o_wup), (w_down.at[1], o_wdown),
            )
        )
    ]
    for copy in outs:
        copy.start()
    loop(GRID // PAD, places, unroll=2)
    for i in range(blocks):
        give_last(i).wait_recv()

    e_ref[...] = (ex1[0:PAD, :] + eown[...] + erecv2[...].astype(F32) + eoff[3:4]).astype(BF16)
    vec = evec[...].astype(F32)
    m = (nn(e_ref[...], ew[...]) + vec[0:1]).astype(BF16)
    gain = dgains[...].astype(F32)
    offsets = doffs[...].astype(F32)

    def start(i):
        r = span(i, PAD)
        oh = hot[r, :]
        hit = jnp.sum(oh.astype(F32), -1, keepdims=True)
        x = jnp.where(hit > 0, nn(oh, m), vec[1:2]).astype(BF16).astype(F32) + x0[r, :]
        x0[r, :] = x
        hat, _ = normal(x)
        a[r, :] = (hat * gain[0:1] + offsets[0:1]).astype(BF16)

    loop(GRID // PAD, start, unroll=2)
    arrived(0)

    def dec_bias(row, size):
        return jnp.concatenate([biases[k, row : row + 1, 0:size] for k in range(LANES)], 1)

    acts[0] = (nn(a[...], qkv[0]) + dec_bias(4, 128)).astype(BF16)
    acts[1] = nn(a[...], qkv[1]).astype(BF16)
    acts[2] = (nn(a[...], qkv[2]) + dec_bias(5, 128)).astype(BF16)
    pass_on(1)
    pass_on(2)
    marks = head_marks(128, DEC_SIZE, BF16)
    marks32 = head_marks(128, DEC_SIZE, F32)
    dim = lax.broadcasted_iota(jnp.int32, (128, 1), 0)
    rows32 = [
        ((dim >= h * DEC_SIZE) & (dim < (h + 1) * DEC_SIZE)).astype(F32) for h in range(len(marks))
    ]

    ones = ones_per_head(PAD, marks)

    def attention(i):
        r = span(i, PAD)
        row_slot = slot_of(lax.broadcasted_iota(jnp.int32, (PAD, PAD), 0) + i * PAD)
        key_slot = slot_of(lax.broadcasted_iota(jnp.int32, (PAD, PAD), 1) + i * PAD)
        allowed = (code_of(row_slot) == code_of(key_slot)) & (key_slot < GRID_ROWS * width)
        for g in range(DD // 128):
            c = slice(g * 128, (g + 1) * 128)
            probs[i, :, g * 512 : (g + 1) * 512], o[r, c], inverse[r, c] = attend(
                acts[0, r, c], acts[1, r, c], acts[2, r, c], marks, ones,
                lambda s: jnp.where(allowed, s, NEG * LOG2E), DEC_SCALE,
            )

    loop(GRID // PAD, attention, unroll=2)
    pass_last(1)
    pass_last(2)
    pass_on(3)
    arrived(1)

    def mix(i):
        r = span(i, 256)
        x = x0[r, :] + nn(o[r, :], proj[...]) + offsets[2:3]
        x1[r, :] = x
        hat, _ = normal(x)
        un = hat * gain[1:2] + offsets[1:2]
        u[r, :] = un.astype(BF16)
        ut[:, r] = jnp.transpose(un).astype(BF16)

    loop(2, mix)
    pass_last(3)
    arrived(2)

    def ff(i):
        c = span(i, 256)
        h = nn(u[...], up[:, c]) + biases[lax.div(i, 2), 3:4, span(lax.rem(i, 2), 256)]
        act, slope = gelu_both(h)
        y[:, c] = act.astype(BF16)
        gp[:, c] = slope.astype(BF16)

    loop(up.shape[1] // 256, ff, unroll=2)
    arrived(3)
    def out(i):
        c = span(i, 256)
        acc[:, c] = nn(y[...], down[:, c])

    loop(2, out)
    full = ((acc[...] + x1[...] + offsets[3:4]) * valid_rows()).astype(BF16)
    turned = tn(full, perm[...]).astype(BF16)
    for k in range(devices):
        dsend[k] = turned[k * dsend.shape[1] : (k + 1) * dsend.shape[1]]

    slabs = pltpu.make_async_copy(dsend, o_slabs, out_s.at[17])
    slabs.start()

    def ff_back(shard):
        for side in range(2):
            c = span(2 * shard + side, 256)
            d_down = nn(gt[...], y[:, c]).astype(BF16)
            dh = nt(gb[...], down[c, :]) * gp[:, c].astype(F32)
            d_upb[:, c] = colsum(dh)
            du = dh.astype(BF16)
            gp[:, c] = du
            d_up = nn(ut[...], du).astype(BF16)
            for block in range(GRID // CH):
                rows = slice(block * CH, (block + 1) * CH)
                h, top, col = tile_of(4 * block + side)
                buf[shard, h, top : top + CH, col : col + 256] = d_up[rows]
                h, top, col = tile_of(4 * block + 2 + side)
                buf[shard, h, top : top + CH, col : col + 256] = d_down[rows]

    def early_core(which):
        shard, land = ((mate, e_rc), (cross, e_rcy))[which]
        return far(
            buf.at[shard, :, 0:EARLY_ROWS, :], land, e_s.at[which], e_r.at[which], {"tensor": mate}
        )

    def early_x(which):
        return far(
            buf.at[(over, lane)[which], 1 - sec, 0:EARLY_ROWS, :], e_rx.at[which],
            e_s.at[2 + which], e_r.at[2 + which], {"section": 1 - sec},
        )

    def early_y():
        return far(
            buf.at[over, sec, 0:EARLY_ROWS, :], e_ry, e_s.at[4], e_r.at[4], {"tensor": over}
        )

    def early_add(shard, land):
        def body(i):
            r = span(i, CH)
            buf[shard, :, r, :] = buf[shard, :, r, :] + land[:, r, :]

        loop(EARLY_ROWS // CH, body)

    def early_half(shard, land):
        buf[shard, sec, 0:EARLY_ROWS, :] = buf[shard, sec, 0:EARLY_ROWS, :] + land

    def ff_step(i):
        ff_back(jnp.where(i == 0, cross, jnp.where(i == 1, over, jnp.where(i == 2, mate, lane))))

        @pl.when(i == 1)
        def _():
            early_core(1).start()

        @pl.when(i == 2)
        def _():
            early_core(0).start()
            early_core(1).wait_recv()
            early_add(over, e_rcy)
            early_x(0).start()

    loop(LANES, ff_step)

    def ff_in(i):
        c = span(i, 256)
        acc[:, c] = nt(gp[...], up[c, :])

    loop(2, ff_in)
    early_core(0).wait_recv()
    early_add(lane, e_rc)
    early_x(1).start()

    def mix_back(i):
        r = span(i, 256)
        hat, scale = normal(x1[r, :])
        da = acc[r, :]
        dx = g32[r, :] + normal_back(da, hat, scale, gain[1:2])
        d_small[1:2, :] += colsum(da * hat)
        d_small[3:4, :] += colsum(da)
        d_small[4:5, :] += colsum(dx)
        g32[r, :] = dx
        dxb = dx.astype(BF16)
        gb[r, :] = dxb
        u[r, :] = nt(dxb, proj[...]).astype(BF16)

    loop(2, mix_back)
    d_proj = tn(o[...], gb[...]).astype(BF16)
    for block in range(GRID // CH):
        h, top, col = tile_of(33 + 2 * block)
        side = slice(block // 2 * 128, (block // 2 + 1) * 128)
        for k in range(LANES):
            row = k * 128 + block % 2 * CH
            buf[k, h, top : top + CH, col + 128 : col + 256] = d_proj[row : row + CH, side]

    def attention_back(i):
        r = span(i, PAD)
        for k in range(DD // 128):
            c = slice(k * 128, (k + 1) * 128)
            acts[0, r, c], acts[1, r, c], acts[2, r, c] = attend_back(
                acts[0, r, c], acts[1, r, c], acts[2, r, c],
                probs[i, :, k * 512 : (k + 1) * 512], o[r, c], inverse[r, c], u[r, c],
                marks, marks32, rows32, ones, DEC_SCALE,
            )

    loop(GRID // PAD, attention_back, unroll=2)
    early_x(0).wait_recv()
    early_half(over, e_rx[0])
    early_y().start()
    d_qvb[0:1, :] = colsum(acts[0].astype(F32))
    d_qvb[1:2, :] = colsum(acts[2].astype(F32))

    def project_back(i):
        c = span(i, 256)
        acc[:, c] = (
            nt(acts[0], qkv[0, c, :]) + nt(acts[1], qkv[1, c, :]) + nt(acts[2], qkv[2, c, :])
        )

    loop(2, project_back)
    gt[...] = jnp.transpose(a[...].astype(F32)).astype(BF16)
    for j in range(3):
        d_qkv = nn(gt[...], acts[j]).astype(BF16)
        for block in range(GRID // CH):
            h, top, col = tile_of(32 + 2 * block + j // 2)
            col = col + j % 2 * 128
            rows = slice(block * CH, (block + 1) * CH)
            for k in range(LANES):
                buf[k, h, top : top + CH, col : col + 128] = d_qkv[rows, k * 128 : (k + 1) * 128]

    def start_back(i):
        r = span(i, PAD)
        hat, scale = normal(x0[r, :])
        da = acc[r, :]
        dx = g32[r, :] + normal_back(da, hat, scale, gain[0:1])
        d_small[0:1, :] += colsum(da * hat)
        d_small[2:3, :] += colsum(da)
        dg = dx.astype(BF16)
        gb[r, :] = dg
        hit = jnp.sum(hot[r, :].astype(F32), -1, keepdims=True)
        d_small[7:8, :] += colsum(jnp.where(hit > 0, 0.0, dg.astype(F32)))

    loop(GRID // PAD, start_back, unroll=2)
    dm = tn(hot[...], gb[...])
    d_small[6:7, :] = colsum(dm)
    dmb = dm.astype(BF16)
    d_enc[...] = nt(dmb, ew[...]).astype(BF16)
    d_ew = tn(e_ref[...], dmb).astype(BF16)
    for k in range(LANES):
        for h in range(2):
            top = k * 192 + h * 64
            buf[k, h, 512:576, 0:512] = d_ew[top : top + 64]
            buf[k, h, 512:576, 512:768] = d_ew[k * 192 + 128 : (k + 1) * 192, h * 256 : (h + 1) * 256]

    early_x(1).wait_recv()
    early_half(lane, e_rx[1])
    early_y().wait_recv()
    early_half(lane, e_ry[...])
    later = pl.ds(EARLY_ROWS, DEC_ROWS - EARLY_ROWS)
    rest = [pltpu.make_async_copy(buf.at[lane], o_dec.at[lane], out_s.at[13])] + [
        pltpu.make_async_copy(buf.at[k, :, later, :], o_dec.at[k, :, later, :], out_s.at[14 + n])
        for n, k in enumerate((mate, over, cross))
    ]
    for copy in rest:
        copy.start()
    for copy in outs + rest + [slabs]:
        copy.wait()
    for which in range(2):
        early_core(which).wait_send()
        early_x(which).wait_send()
    early_y().wait_send()
    for n in range(4):
        enc_weight(n).wait_send()
        for kind in range(5):
            dec_weight(n, kind).wait_send()
    for step in range(1, LANES):
        bias_copy(step).wait_send()
    for i in range(blocks):
        give_part(i, 0).wait_send()
        give_part(i, 1).wait_send()
        give_last(i).wait_send()


def forward_call(args, half, hid, dff):
    dma = lambda *s: pltpu.SemaphoreType.DMA(s)
    vm = lambda dtype, *shape: pltpu.VMEM(shape, dtype)
    rows = 2 * PAD
    keys = PAD * half // ENC_SIZE
    devices = 2 * LANES
    slab = DD // devices
    kept = [
        ((PAD, D), F32), ((rows, D), F32), ((rows, D), BF16), ((rows, D), BF16),
        ((2, rows, hid), BF16), ((2, rows, hid), BF16), ((2, 3, rows, half), BF16),
        ((2, 2, PAD, keys), BF16), ((2, rows, half), BF16),
        ((3, half, D), BF16), ((half, D), BF16), ((D, hid), BF16), ((hid, D), BF16),
        ((LANES, 2, DEC_ROWS, D), BF16), ((devices, slab, GRID), BF16),
    ]
    made = [((PAD, D), BF16), ((2, DD), F32), ((1, dff), F32), ((8, DD), F32)]
    return pl.pallas_call(
        forward_and_decoder,
        out_shape=[jax.ShapeDtypeStruct(s, d) for s, d in kept + made],
        in_specs=[SM, SM, SM] + [VM] * 8 + [ANY] * 9 + [VM] * 5,
        out_specs=[ANY] * len(kept) + [VM] * len(made),
        scratch_shapes=[
            vm(BF16, 2, 3, half, D), vm(BF16, 2, half, D), vm(BF16, 2, D, hid), vm(BF16, 2, hid, D),
            vm(F32, 8, D), vm(F32, LANES, 8, D),
            vm(BF16, 3, DD, DD), vm(BF16, DD, DD), vm(BF16, DD, dff), vm(BF16, dff, DD),
            vm(F32, rows, D), vm(BF16, rows, D), vm(BF16, rows, D), vm(BF16, 2, rows, hid),
            vm(BF16, 2, rows, hid), vm(BF16, 2, 3, rows, half), vm(BF16, 2, 2, PAD, keys),
            vm(BF16, 2, rows, half), vm(F32, rows, D), vm(F32, rows, D), vm(BF16, rows, D),
            vm(BF16, rows, D), vm(BF16, PAD, D), vm(BF16, PAD, D), vm(F32, PAD, D),
            vm(BF16, GRID, DD), vm(F32, GRID, DD), vm(F32, GRID, DD), vm(BF16, GRID, DD),
            vm(BF16, 3, GRID, DD), vm(BF16, GRID // PAD, PAD, DHEADS * PAD), vm(BF16, GRID, DD),
            vm(F32, GRID, DD),
            vm(BF16, GRID, DD), vm(BF16, DD, GRID), vm(BF16, GRID, dff), vm(BF16, GRID, dff),
            vm(F32, GRID, DD), vm(BF16, GRID, DD), vm(BF16, DD, GRID), vm(F32, GRID, DD),
            vm(BF16, PAD, D), vm(BF16, GRID, PAD), vm(BF16, GRID, GRID),
            vm(BF16, LANES, 2, DEC_ROWS, D),
            vm(BF16, devices, slab, GRID), *[vm(BF16, 2, EARLY_ROWS, D)] * 3, vm(BF16, EARLY_ROWS, D),
            dma(8), dma(18), pltpu.SemaphoreType.DMA, dma(4), dma(4), dma(LANES), dma(LANES),
            dma(20), dma(20), dma(6), dma(6), dma(3), dma(3),
            dma(5), dma(5),
        ],
        compiler_params=pltpu.CompilerParams(
            collective_id=0, has_side_effects=True, vmem_limit_bytes=VMEM_LIMIT
        ),
    )(*args)


def add(x, y):
    return x + y


def backward_and_sums(
    d_enc, gains,
    h_u, h_y, h_gp, h_down0, h_down1, h_up0, h_up1,
    h_x, h_x1, h_a, h_qkv, h_p, h_o, h_w0, h_w1, h_proj0, h_proj1,
    dec, slabs, dec_qvb, dec_upb, dec_small,
    out, emb, dec_out, dx_out,
    gb, gt, ut, part, send, recv, du, gx, dx1, d_o, d_acts, own, send1, recv1, dx32, dx,
    d_upb, d_qvb, d_small,
    acc, yacc, enc_mate, rcy, ry, land_x, land_l, land_r, small32, small,
    u, y, gp, down0, down1, up0, up1, x, x1, a, qkv, p, o, w0, w1, proj0, proj1, fetch_s,
    load_s, ex_s, ex_r,
    core_s, core_r, corey_s, corey_r, y_s, y_r, x_s, x_r, z_s, zl_r, zr_r,
    bl_s, br_s, b_r, a_s, a_r, emb_s, emb_r, dx_s, dx_r, do_s, do_r,
):
    sec = lax.axis_index("section")
    lane = lax.axis_index("tensor")
    pos = lax.axis_index("dp")
    count = lax.axis_size("dp")
    mate = lane + 1 - 2 * lax.rem(lane, 2)
    over = lax.rem(lane + 2, LANES)
    cross = lax.rem(mate + 2, LANES)
    first = pos == 0
    last = pos == count - 1
    me = sec * LANES + lane
    devices = 2 * LANES

    def group_peer(step):
        peer = lax.rem(me + step, devices)
        return peer, {"section": lax.div(peer, LANES), "tensor": lax.rem(peer, LANES)}

    barrier = pltpu.get_barrier_semaphore()
    for step in range(1, devices):
        pl.semaphore_signal(barrier, inc=1, device_id_type=MESH, device_id=group_peer(step)[1])

    @pl.when(pos > 0)
    def _():
        pl.semaphore_signal(barrier, inc=1, device_id={"dp": pos - 1}, device_id_type=MESH)

    @pl.when(pos < count - 1)
    def _():
        pl.semaphore_signal(barrier, inc=1, device_id={"dp": pos + 1}, device_id_type=MESH)

    me = sec * LANES + lane
    loads = [
        pltpu.make_async_copy(slabs.at[me], dec_out.at[me], load_s.at[2]),
        pltpu.make_async_copy(dec.at[lane], acc.at[:, 0:DEC_ROWS, :], load_s.at[0]),
        pltpu.make_async_copy(
            dec.at[over, :, EARLY_ROWS:DEC_ROWS, :], yacc.at[:, 0 : DEC_ROWS - EARLY_ROWS, :],
            load_s.at[1],
        ),
    ]
    for load in loads:
        load.start()
    fetches = [
        pltpu.make_async_copy(src, dst, fetch_s.at[n])
        for n, (src, dst) in enumerate(
            (
                (h_u, u), (h_y, y), (h_gp, gp), (h_down0, down0), (h_down1, down1), (h_up0, up0),
                (h_up1, up1), (h_x, x), (h_x1, x1), (h_a, a), (h_qkv, qkv), (h_p, p), (h_o, o),
                (h_w0, w0), (h_w1, w1), (h_proj0, proj0), (h_proj1, proj1),
            )
        )
    ]
    for fetch in fetches:
        fetch.start()
    small32[...] = jnp.zeros_like(small32)
    d_small[...] = jnp.zeros_like(d_small)
    gb[0:PAD, :] = d_enc[...]
    ends = jnp.where(first, 0, 1) + jnp.where(last, 0, 1)
    pl.semaphore_wait(barrier, devices - 1 + ends)

    gain = gains[...].astype(F32)
    width = w0.shape[1]
    marks = head_marks(width, ENC_SIZE, BF16)
    marks32 = head_marks(width, ENC_SIZE, F32)
    ones = ones_per_head(PAD, marks)

    def rows(k, size=CH):
        return pl.ds(pl.multiple_of(k * size, size), size)

    def give_enc():
        return far(d_enc, gb.at[PAD : 2 * PAD, :], ex_s.at[0], ex_r.at[0], {"tensor": over})

    def give_part(i, half):
        cut = rows(i, 256)
        n = 1 + 2 * i + half
        return far(
            send.at[(1 - half) * PAD : (2 - half) * PAD, cut],
            recv.at[half * PAD : (half + 1) * PAD, cut],
            ex_s.at[n], ex_r.at[n], {"tensor": over},
        )

    def give_last(i):
        cut = rows(i, 256)
        return far(send1.at[:, cut], recv1.at[:, cut], ex_s.at[7 + i], ex_r.at[7 + i], {"tensor": over})

    def ff_back(g, i, down):
        c = rows(i, 256)
        d_down = nn(gt[...], y[g, :, c]).astype(BF16)
        dh = nt(gb[...], down[c, :]) * gp[g, :, c].astype(F32)
        d_upb[g, :, c] = colsum(dh)
        dub = dh.astype(BF16)
        du[g, :, c] = dub
        d_up = nn(ut[...], dub).astype(BF16)
        if g == 0:
            acc[1, A_TOP:B_TOP, c] = d_down
            acc[0, A_TOP:B_TOP, c] = d_up
        else:
            enc_mate[1, 0:ENC_A, c] = d_down
            enc_mate[0, 0:ENC_A, c] = d_up

    def ff_in(i):
        c = rows(i, 256)
        t = nt(du[0], up0[c, :]) + nt(du[1], up1[c, :])
        part[:, c] = t
        send[:, c] = t.astype(BF16)
        give_part(i, 0).start()
        give_part(i, 1).start()

    def norm_two():
        for fetch in fetches[7:]:
            fetch.wait()
        for k in range(D // 256):
            give_part(k, 0).wait_recv()
            give_part(k, 1).wait_recv()

        def body(j):
            r = rows(j, 64)
            da = part[r, :] + recv[r, :].astype(F32)
            hat, scale = normal(x1[r, :])
            g = gb[r, :].astype(F32)
            d = g + normal_back(da, hat, scale, gain[1:2])
            gx[r, :] = d.astype(BF16)
            dx1[r, :] = d

            @pl.when(j < 2)
            def _():
                d_small[1:2, :] += colsum(da * hat)
                d_small[3:4, :] += colsum(da)
                d_small[4:5, :] += colsum(d)
                d_small[5:6, :] += colsum(g)

        loop(2 * PAD // 64, body)

    def attention(g, c):
        if c == 0:
            d_proj = tn(o[g], gx[...]).astype(BF16)
            if g == 0:
                acc[1, B_TOP + width : S_TOP, :] = d_proj
            else:
                enc_mate[1, ENC_A + width : ENC_A + 2 * width, :] = d_proj
            d_o[...] = nt(gx[...], (proj0, proj1)[g][...]).astype(BF16)
        r = slice(c * PAD, (c + 1) * PAD)
        d_acts[g, 0, r], d_acts[g, 1, r], d_acts[g, 2, r] = attend_back(
            qkv[g, 0, r], qkv[g, 1, r], qkv[g, 2, r], p[g, c], o[g, r], 1.0 / nn(p[g, c], ones),
            d_o[r, :], marks, marks32, None, ones, ENC_SCALE,
        )
        if c == 1:
            d_qvb[g, 0:1, :] = colsum(d_acts[g, 0].astype(F32))
            d_qvb[g, 1:2, :] = colsum(d_acts[g, 2].astype(F32))

    def project_in(i):
        c = rows(i, 256)
        t = 0.0
        for g, w in enumerate((w0, w1)):
            for j in range(3):
                t += nn(d_acts[g, j], w[j, :, c])
        own[:, c] = t[:PAD]
        send1[:, c] = t[PAD:].astype(BF16)
        give_last(i).start()

    def project_grad(g):
        for j in range(3):
            row = (j % 2) * width
            d = tn(d_acts[g, j], a[...]).astype(BF16)
            if g == 0:
                acc[j // 2, B_TOP + row : B_TOP + row + width, :] = d
            else:
                enc_mate[j // 2, ENC_A + row : ENC_A + row + width, :] = d

    def norm_one():
        for k in range(D // 256):
            give_last(k).wait_recv()

        def body(j):
            r = rows(j, 64)
            da = own[r, :] + recv1[r, :].astype(F32)
            hat, scale = normal(x[r, :])
            d_small[0:1, :] += colsum(da * hat)
            d_small[2:3, :] += colsum(da)
            dx32[r, :] = dx1[r, :] + normal_back(da, hat, scale, gain[0:1])

        loop(PAD // 64, body)
        turned = jnp.transpose(dx32[...])
        cut = D // devices
        for k in range(devices):
            dx[k] = turned[k * cut : (k + 1) * cut, 0:VIS].astype(BF16)
        for r in range(LANES):
            small32[r, 8:9, 0:512] = dec_upb[:, r * 512 : (r + 1) * 512]
            small32[r, 9:10, 0:128] = dec_qvb[0:1, r * 128 : (r + 1) * 128]
            small32[r, 9:10, 128:256] = dec_qvb[1:2, r * 128 : (r + 1) * 128]
            small32[r, 0:8, 0:512] = dec_small[...]
            small32[r, 16:24, :] = d_small[...]
        for g, shard in enumerate((lane, mate)):
            small32[shard, 10:11, :] = d_upb[g]
            small32[shard, 11:12, 0:192] = d_qvb[g, 0:1]
            small32[shard, 11:12, 256:448] = d_qvb[g, 1:2]
        for r in range(LANES):
            for h in range(2):
                small[r, h] = small32[r, h * SMALL : (h + 1) * SMALL].astype(BF16)
        acc[:, S_TOP : S_TOP + SMALL, :] = small[lane]
        yacc[:, DEC_ROWS - EARLY_ROWS :, :] = small[over]
        core_copy(LATE, small.at[mate], SMALL).start()
        corey_copy(LATE, small.at[cross], SMALL).start()
        for step in range(1, devices):
            dx_copy(step).start()
        dx_out[me] = dx[me]

    def core_enc(lo, hi):
        def body(m):
            block = block_of(m)

            @pl.when((block >= lo) & (block < hi))
            def _():
                src = pl.ds(pl.multiple_of(block * CH - DEC_ROWS, CH), CH)
                core_copy(m, enc_mate.at[:, src, :]).start()

        loop(ALL_K, body)

    def first_piece():
        for fetch in fetches[:7]:
            fetch.wait()
        ut[...] = jnp.transpose(u[...].astype(F32)).astype(BF16)
        give_enc().wait_recv()
        gt[...] = jnp.transpose(gb[...].astype(F32)).astype(BF16)

    def ff_step(k):
        for g, down in enumerate((down0, down1)):
            @pl.when(lax.rem(k, 2) == g)
            def _(g=g, down=down):
                ff_back(g, lax.div(k, 2), down)

    def run_pieces(n):
        def several(low, high, body):
            begin = sum(jnp.where(n > t, 1, 0) for t in PIECES[low:high])
            end = sum(jnp.where(n >= t, 1, 0) for t in PIECES[low:high])
            lax.fori_loop(begin, end, lambda k, c: (body(k), c)[1], 0)

        def single(k, body):
            @pl.when(n == PIECES[k])
            def _():
                body()

        single(0, first_piece)
        several(1, 7, ff_step)
        single(7, lambda: core_enc(DEC_K, DEC_K + ENC_A // CH))
        several(8, 11, ff_in)
        single(11, norm_two)
        for k in range(4):
            single(12 + k, lambda k=k: attention(k // 2, k % 2))
        several(16, 19, project_in)
        for g in range(2):
            single(19 + g, lambda g=g: project_grad(g))
        single(21, lambda: core_enc(DEC_K + ENC_A // CH, B_K))
        single(22, norm_one)

    def dx_copy(step):
        peer, place = group_peer(step)
        return far(dx.at[peer], dx_out.at[me], dx_s.at[step], dx_r.at[step], place)

    def decoded_copy(step):
        peer, place = group_peer(step)
        return far(slabs.at[peer], dec_out.at[me], do_s.at[step], do_r.at[step], place)

    def emb_copy(step):
        return far(
            out.at[:, pl.ds(512, CH), :], emb.at[lane], emb_s.at[step], emb_r.at[step],
            {"tensor": lax.rem(lane + step, LANES)},
        )

    def block_of(m):
        shift = 0
        for k in range(1, ALL_K):
            if ORDER[k] - k != ORDER[k - 1] - k + 1:
                shift = jnp.where(m >= k, ORDER[k] - k, shift)
        return m + shift

    def is_dec(m):
        return (block_of(m) < DEC_K) & (m >= EARLY)

    def at(m, size=CH):
        return pl.ds(pl.multiple_of(block_of(m) * CH, CH), size)

    def slot(m, size=CH):
        return pl.ds(pl.multiple_of(m * CH, CH), size)

    def y_at(m, size=CH):
        return pl.ds(pl.multiple_of((jnp.minimum(block_of(m), DEC_K) - EARLY) * CH, CH), size)

    def core_copy(m, src, size=CH):
        return far(src, out.at[:, at(m, size), :], core_s.at[m], core_r.at[m], {"tensor": mate})

    def corey_copy(m, src, size=CH):
        return far(src, rcy.at[:, y_at(m, size), :], corey_s.at[m], corey_r.at[m], {"tensor": mate})

    def y_copy(m, size=CH):
        cut = y_at(m, size)
        return far(
            yacc.at[:, cut, :], ry.at[:, cut, :], y_s.at[m], y_r.at[m], {"tensor": over}
        )

    def x_copy(m, size=CH):
        return far(
            acc.at[1 - sec, at(m, size), :], land_x.at[0, slot(m, size), :], x_s.at[m], x_r.at[m],
            {"section": 1 - sec},
        )

    def xc_copy(m):
        return far(
            acc.at[:, at(m), :], land_x.at[:, slot(m), :], x_s.at[m], x_r.at[m],
            {"section": 1 - sec},
        )

    def z_copy(m, whole, right, size=CH):
        land = land_l if right else land_r
        if whole:
            src, dst = acc.at[:, at(m), :], land.at[:, slot(m), :]
        else:
            src, dst = acc.at[sec, at(m, size), :], land.at[0, slot(m, size), :]
        landed = zl_r if right else zr_r
        return far(src, dst, z_s.at[m], landed.at[m], {"dp": pos + 1 if right else pos - 1})

    def b_copy(m, whole, right, size=CH):
        place = out.at[:, at(m), :] if whole else out.at[sec, at(m, size), :]
        sent = br_s if right else bl_s
        return far(place, place, sent.at[m], b_r.at[m], {"dp": pos + 1 if right else pos - 1})

    def a_copy(m, size=CH):
        place = out.at[sec, at(m, size), :]
        return far(place, place, a_s.at[m], a_r.at[m], {"section": 1 - sec})

    def a_wait(m, size=CH):
        place = out.at[1 - sec, at(m, size), :]
        far(place, place, a_s.at[m], a_r.at[m], {"section": 1 - sec}).wait_recv()

    give_enc().start()

    def start_core(m):
        @pl.when(is_dec(m))
        def _():
            core_copy(m, dec.at[mate, :, at(m), :]).start()
            corey_copy(m, dec.at[cross, :, at(m), :]).start()

    loop(ALL_K, start_core)
    for step in range(1, devices):
        decoded_copy(step).start()
    for load in loads:
        load.wait()

    def join_core(m, size):
        core_copy(m, out.at[:, at(m, size), :], size).wait_recv()
        acc[:, at(m, size), :] = add(acc[:, at(m, size), :], out[:, at(m, size), :])

    def join_core_y(m, size):
        corey_copy(m, rcy.at[:, y_at(m, size), :], size).wait_recv()
        yacc[:, y_at(m, size), :] = add(yacc[:, y_at(m, size), :], rcy[:, y_at(m, size), :])
        y_copy(m, size).start()

    def stage_c(m):
        @pl.when((m >= EARLY) & (m != LATE))
        def _():
            join_core(m, CH)

            @pl.when(is_dec(m))
            def _():
                join_core_y(m, CH)

        @pl.when(m == LATE)
        def _():
            join_core(m, SMALL)
            join_core_y(m, SMALL)

    def finished(m):
        @pl.when(block_of(m) == DEC_K - 1)
        def _():
            for step in range(1, LANES):
                emb_copy(step).start()
            emb[lane] = out[:, 512 : 512 + CH, :]

    def line_of(root, whole, size=CH):
        left = pos < root
        right = pos > root
        here = pos == root
        reach = max(root, count - 1 - root)
        level = jnp.where(left, pos, jnp.where(right, count - 1 - pos, reach))
        dist = jnp.where(left, root - pos, pos - root)

        def view(ref, m):
            return ref.at[:, at(m), :] if whole else ref.at[sec, at(m, size), :]

        def landed(ref, m):
            return ref.at[:, slot(m), :] if whole else ref.at[0, slot(m, size), :]

        def hop(m, rightward):
            return z_copy(m, whole, rightward, size)

        def back_hop(m, rightward):
            return b_copy(m, whole, rightward, size)

        def outer(m):
            @pl.when(left & first)
            def _():
                hop(m, True).start()

            @pl.when(right & last)
            def _():
                hop(m, False).start()

        def inward(m):
            @pl.when(left & (pos > 0))
            def _():
                hop(m, True).wait_recv()
                view(acc, m)[...] = add(view(acc, m)[...], landed(land_l, m)[...])
                hop(m, True).start()

            @pl.when(right & (pos < count - 1))
            def _():
                hop(m, False).wait_recv()
                view(acc, m)[...] = add(view(acc, m)[...], landed(land_r, m)[...])
                hop(m, False).start()

            @pl.when(here)
            def _():
                total = view(acc, m)[...].astype(F32)
                if root > 0:
                    hop(m, True).wait_recv()
                    total = total + landed(land_l, m)[...].astype(F32)
                if root < count - 1:
                    hop(m, False).wait_recv()
                    total = total + landed(land_r, m)[...].astype(F32)
                if whole:
                    view(acc, m)[...] = total.astype(BF16)
                    xc_copy(m).start()
                else:
                    view(out, m)[...] = total.astype(BF16)
                    spread(m)
                    a_copy(m, size).start()

        def spread(m):
            if root > 0:
                back_hop(m, False).start()
            if root < count - 1:
                back_hop(m, True).start()

        def crossed(m):
            xc_copy(m).wait_recv()
            view(out, m)[...] = add(view(acc, m)[...], landed(land_x, m)[...])
            spread(m)
            finished(m)

        def outward(m):
            back_hop(m, False).wait_recv()

            @pl.when(left & (pos > 0))
            def _():
                back_hop(m, False).start()

            @pl.when(right & (pos < count - 1))
            def _():
                back_hop(m, True).start()

            if whole:
                finished(m)
            else:
                a_copy(m, size).start()

        def sent(m):
            @pl.when(jnp.logical_not(here))
            def _():
                hop(m, True).wait_send()

            @pl.when((pos <= root) & (pos > 0))
            def _():
                back_hop(m, False).wait_send()

            @pl.when((pos >= root) & (pos < count - 1))
            def _():
                back_hop(m, True).wait_send()

            if whole:
                @pl.when(here)
                def _():
                    xc_copy(m).wait_send()
            else:
                a_copy(m, size).wait_send()

                @pl.when(crosses_first(m))
                def _():
                    x_copy(m, size).wait_send()

        def crosses_first(m):
            return m >= EARLY if XFIRST else m >= 0

        def set_off(m):
            if whole:
                outer(m)
            else:
                x_copy(m, size).start()

        def set_off_early(m):
            if XFIRST:
                outer(m)
            else:
                set_off(m)

        def add_y(m):
            def joined():
                y_copy(m, size).wait_recv()
                acc[:, at(m, size), :] = add(acc[:, at(m, size), :], ry[:, y_at(m, size), :])

            if size == CH:
                pl.when(is_dec(m))(joined)
            else:
                joined()
            set_off(m)

        def add_x(m):
            @pl.when(crosses_first(m))
            def _():
                x_copy(m, size).wait_recv()
                acc[sec, at(m, size), :] = add(
                    acc[sec, at(m, size), :], land_x[0, slot(m, size), :]
                )
                outer(m)

        def last_half(m):
            a_wait(m, size)
            finished(m)

        base = 1 if whole else 2
        back = base + reach + dist + (1 if whole else 0)
        steps = [(back, jnp.logical_not(here), outward), (base + level, level > 0, inward)]
        if whole:
            steps.append((base + reach + 1, here, crossed))
        else:
            steps += [(back + 1, True, last_half), (2, True, add_x)]
        return steps, sent, add_y, set_off_early

    low_root = (count - 1) // 2
    high_root = min(low_root + 1, count - 1)
    def is_whole(m):
        return (lax.rem(m, 2) == 0) & (m >= WHOLE_LOW) & (m < WHOLE_HIGH)

    roots = (high_root, count - 1, low_root, 0)
    lines = [
        (lambda m, part=part: is_whole(m) & (lax.rem(m, 8) == part), *line_of(root, True))
        for part, root in zip((0, 2, 4, 6), roots)
    ] + [
        (lambda m: jnp.logical_not(is_whole(m)) & (m != LATE), *line_of(low_root, False)),
        (lambda m: m == LATE, *line_of(low_root, False, SMALL)),
    ]

    def finish(m):
        @pl.when((m >= EARLY) & (m != LATE))
        def _():
            core_copy(m, out.at[:, at(m), :]).wait_send()

            @pl.when(is_dec(m))
            def _():
                corey_copy(m, rcy.at[:, y_at(m), :]).wait_send()
                y_copy(m).wait_send()

        @pl.when(m == LATE)
        def _():
            core_copy(m, out.at[:, at(m, SMALL), :], SMALL).wait_send()
            corey_copy(m, rcy.at[:, y_at(m, SMALL), :], SMALL).wait_send()
            y_copy(m, SMALL).wait_send()

        for mine, _, sent, _, _ in lines:
            @pl.when(mine(m))
            def _(sent=sent):
                sent(m)

    def set_off_early(m):
        for mine, _, _, _, set_off in lines:
            @pl.when(mine(m))
            def _(set_off=set_off):
                set_off(m)

    loop(EARLY, set_off_early)
    far_reach = max(max(root, count - 1 - root) for root in roots)
    depth = LAG * (3 + 2 * far_reach) + 1

    def tick(n):
        @pl.when(n <= PIECES[-1])
        def _():
            run_pieces(n)

        for mine, steps, _, add_y, _ in lines:
            m = n - LAG

            @pl.when((m >= EARLY) & (m < ALL_K))
            def _(m=m, mine=mine, add_y=add_y):
                @pl.when(mine(m))
                def _():
                    add_y(m)

            for offset, enabled, stage in steps:
                m = n - LAG * offset

                @pl.when((m >= 0) & (m < ALL_K) & enabled)
                def _(m=m, mine=mine, stage=stage):
                    @pl.when(mine(m))
                    def _():
                        stage(m)

        @pl.when(n < ALL_K)
        def _():
            stage_c(n)

        @pl.when(n >= depth)
        def _():
            finish(n - depth)

    loop(ALL_K + depth, tick)

    for step in range(1, devices):
        dx_copy(step).wait()
        decoded_copy(step).wait()
    for step in range(1, LANES):
        emb_copy(step).wait()
    give_enc().wait_send()
    for k in range(D // 256):
        give_part(k, 0).wait_send()
        give_part(k, 1).wait_send()
        give_last(k).wait_send()


def backward_call(args, half, hid):
    dma = lambda *s: pltpu.SemaphoreType.DMA(s)
    vm = pltpu.VMEM
    full = ALL_K * CH
    y_half = DEC_ROWS - EARLY_ROWS + SMALL
    k = ALL_K
    rows = 2 * PAD
    cut = D // (2 * LANES)
    specs = [VM, VM] + [ANY] * 19 + [VM] * 3
    return pl.pallas_call(
        backward_and_sums,
        out_shape=[
            jax.ShapeDtypeStruct((2, full, D), BF16),
            jax.ShapeDtypeStruct((LANES, 2, CH, D), BF16),
            jax.ShapeDtypeStruct((2 * LANES, DD // (2 * LANES), GRID), BF16),
            jax.ShapeDtypeStruct((2 * LANES, cut, VIS), BF16),
        ],
        in_specs=specs,
        out_specs=[VM] * 4,
        scratch_shapes=[
            vm((rows, D), BF16), vm((D, rows), BF16), vm((D, rows), BF16),
            vm((rows, D), F32), vm((rows, D), BF16), vm((rows, D), BF16),
            vm((2, rows, hid), BF16), vm((rows, D), BF16), vm((rows, D), F32),
            vm((rows, half), BF16), vm((2, 3, rows, half), BF16),
            vm((PAD, D), F32), vm((PAD, D), BF16), vm((PAD, D), BF16), vm((PAD, D), F32),
            vm((2 * LANES, cut, VIS), BF16),
            vm((2, 1, hid), F32), vm((2, 2, half), F32), vm((8, D), F32),
            vm((2, full, D), BF16), vm((2, y_half, D), BF16), vm((2, ENC_A + ENC_B, D), BF16),
            vm((2, y_half, D), BF16), vm((2, y_half, D), BF16),
            *[vm((2, full, D), BF16)] * 3,
            vm((LANES, 32, D), F32), vm((LANES, 2, SMALL, D), BF16),
            *[vm(v.shape, v.dtype) for v in args[2:19]],
            dma(17), dma(3), dma(10), dma(10),
            dma(k), dma(k), dma(k), dma(k), dma(k), dma(k),
            dma(k), dma(k), dma(k), dma(k), dma(k),
            dma(k), dma(k), dma(k), dma(k), dma(k), dma(LANES), dma(LANES),
            dma(2 * LANES), dma(2 * LANES), dma(2 * LANES), dma(2 * LANES),
        ],
        compiler_params=pltpu.CompilerParams(
            collective_id=1, has_side_effects=True, vmem_limit_bytes=VMEM_LIMIT
        ),
    )(*args)


def finish_grads(
    total, emb, decoded, dx, decoded_out, dx_out,
    e_qkv, e_qvb, e_proj, e_up, e_upb, e_down, e_gain, e_off,
    d_qkv, d_qvb, d_proj, d_up, d_upb, d_down, d_gain, d_off, d_ew, d_ev,
):
    half = e_proj.shape[0]
    decoded_out[...] = decoded[...]
    dx_out[...] = dx[...]
    e_up[...] = total[0, A_TOP:B_TOP, :].astype(F32)
    e_down[...] = jnp.transpose(total[1, A_TOP:B_TOP, :].astype(F32))
    e_qkv[0] = total[0, B_TOP : B_TOP + half, :].astype(F32)
    e_qkv[1] = total[0, B_TOP + half : S_TOP, :].astype(F32)
    e_qkv[2] = total[1, B_TOP : B_TOP + half, :].astype(F32)
    e_proj[...] = total[1, B_TOP + half : S_TOP, :].astype(F32)

    def tile(number):
        h, top, col = tile_of(number)
        return total[h, top : top + CH, col : col + 256].astype(F32)

    for block in range(GRID // CH):
        rows = slice(block * CH, (block + 1) * CH)
        side = slice(block // 2 * 128, (block // 2 + 1) * 128)
        for k in range(2):
            d_up[rows, k * 256 : (k + 1) * 256] = tile(4 * block + k)
            if block % 2:
                both = jnp.concatenate([tile(4 * block - 2 + k), tile(4 * block + 2 + k)], 0)
                d_down[k * 256 : (k + 1) * 256, side] = jnp.transpose(both)
        one, two = tile(32 + 2 * block), tile(33 + 2 * block)
        d_qkv[0, rows, :] = one[:, 0:128]
        d_qkv[1, rows, :] = one[:, 128:256]
        d_qkv[2, rows, :] = two[:, 0:128]
        d_proj[block % 2 * CH : (block % 2 + 1) * CH, side] = two[:, 128:256]
    for k in range(LANES):
        for h in range(2):
            top = k * 192 + h * 64
            d_ew[top : top + 64, :] = emb[k, h, :, 0:512].astype(F32)
            d_ew[k * 192 + 128 : (k + 1) * 192, h * 256 : (h + 1) * 256] = emb[
                k, h, :, 512:768
            ].astype(F32)
    little = total[0, S_TOP : S_TOP + SMALL, :].astype(F32)
    d_gain[...] = little[0:2, 0:512]
    d_off[...] = little[2:6, 0:512]
    d_ev[...] = little[6:8, 0:512]
    d_upb[...] = little[8, 0:512]
    d_qvb[0:1, :] = little[9:10, 0:128]
    d_qvb[1:2, :] = little[9:10, 128:256]
    e_upb[...] = little[10]
    e_qvb[0:1, :] = little[11:12, 0:192]
    e_qvb[1:2, :] = little[11:12, 256:448]
    little = total[1, S_TOP : S_TOP + SMALL, :].astype(F32)
    e_gain[...] = little[0:2]
    e_off[...] = little[2:6]


def call(kernel, specs, shapes, scratch, args):
    return pl.pallas_call(
        kernel,
        out_shape=[jax.ShapeDtypeStruct(s, d) for s, d in shapes],
        in_specs=specs,
        out_specs=[VM] * len(shapes),
        scratch_shapes=scratch,
        compiler_params=pltpu.CompilerParams(vmem_limit_bytes=VMEM_LIMIT),
    )(*args)


def position_rows():
    quarter = DD // 4
    freq = np.exp(np.arange(quarter, dtype=np.float32) * np.float32(-math.log(10000.0) / quarter))
    angle = np.arange(PAD, dtype=np.float32)[:, None] * freq[None, :].astype(np.float32)
    both = np.concatenate([np.sin(angle), np.cos(angle)], 1).astype(np.float32)
    high = both.astype(jnp.bfloat16)
    low = (both - high.astype(np.float32)).astype(jnp.bfloat16)
    return np.stack([high, low])


def per_device(
    patches, cotangent, widths, visible, window_shift, batch_order,
    encoder_qkv, encoder_qvbias, encoder_proj, encoder_up, encoder_upbias, encoder_down,
    encoder_gains, encoder_offsets,
    decoder_qkv, decoder_qvbias, decoder_proj, decoder_up, decoder_upbias, decoder_down,
    decoder_gains, decoder_offsets, embed_weight, embed_vectors,
):
    qkv0 = encoder_qkv.transpose(1, 2, 0)
    half = qkv0.shape[1]
    hid = encoder_up.shape[1]
    dff = decoder_up.shape[1] * LANES
    flat = patches.transpose(1, 0, 2).reshape(-1, D)
    (
        x, x1, a, u, y, gp, qkv, p, o, qkv1, proj1, up1, down1, dec_buf,
        slabs, d_enc, d_dqvb, d_dupb, d_dsmall,
    ) = forward_call(
        (
            widths, window_shift.T, batch_order, visible, flat, encoder_gains, encoder_offsets,
            encoder_qvbias, encoder_upbias, decoder_qvbias, decoder_upbias,
            qkv0, encoder_proj, encoder_up, encoder_down,
            decoder_qkv.transpose(1, 0, 2), decoder_proj, decoder_up, decoder_down,
            cotangent, embed_weight, embed_vectors, jnp.asarray(position_rows()),
            decoder_gains, decoder_offsets,
        ),
        half, hid, dff,
    )
    total, emb, out_all, dx_all = backward_call(
        (
            d_enc, encoder_gains, u, y, gp, encoder_down, down1, encoder_up, up1,
            x, x1, a, qkv, p, o, qkv0, qkv1, encoder_proj, proj1,
            dec_buf, slabs, d_dqvb, d_dupb, d_dsmall,
        ),
        half, hid,
    )
    f = lambda *shape: (shape, F32)
    out_all, dx_all, *grads = call(
        finish_grads, [VM] * 4,
        [
            (out_all.shape, BF16), (dx_all.shape, BF16), f(3, half, D), f(2, half), f(half, D), f(D, hid), f(hid), f(hid, D), f(2, D), f(4, D),
            f(3, DD, 128), f(2, 128), f(128, DD), f(DD, 512), f(512), f(512, DD), f(2, DD), f(4, DD),
            f(D, DD), f(2, DD),
        ],
        [], (total, emb, out_all, dx_all),
    )
    grads[0] = grads[0].transpose(2, 0, 1)
    grads[8] = grads[8].transpose(1, 0, 2)
    return (out_all.swapaxes(1, 2), dx_all.swapaxes(1, 2), *grads)


def solution(mesh):
    weights = (
        P(None, None, "tensor"), P(None, "tensor"), P("tensor", None), P(None, "tensor"),
        P("tensor"), P("tensor", None), P(), P(),
    )
    split = P("dp", None, ("section", "tensor"))
    return jax.shard_map(
        per_device,
        mesh=mesh,
        in_specs=(
            P("dp", None, None), P("dp", None, None), P("dp"), P("dp", None), P("dp", None),
            P("dp", None),
        ) + weights + weights + (P(), P()),
        out_specs=(split, split) + weights + weights + (P(), P()),
        check_vma=False,
    )
```

```python
import math

import jax
import jax.numpy as jnp
import numpy as np
from jax import lax
from jax.experimental import pallas as pl
from jax.experimental.pallas import tpu as pltpu
from jax.sharding import PartitionSpec as P

D = 768
HEADS = 12
DD = 512
DHEADS = 16
GRID_ROWS = 64
WIDE = 8
WIN = 4
VIS = 102
CM = 4
GRID = 512
LANES = 4
PAD = 128
EPS = 1e-06
NEG = -10000.0
F32 = jnp.float32
BF16 = jnp.bfloat16
VMEM_LIMIT = 60 * 1024 * 1024

VM = pl.BlockSpec(memory_space=pltpu.VMEM)
SM = pl.BlockSpec(memory_space=pltpu.SMEM)
ANY = pl.BlockSpec(memory_space=pl.ANY)


def nn(a, b):
    return lax.dot_general(a, b, (((1,), (0,)), ((), ())), preferred_element_type=F32)


def nt(a, b):
    return lax.dot_general(a, b, (((1,), (1,)), ((), ())), preferred_element_type=F32)


def tn(a, b):
    return lax.dot_general(a, b, (((0,), (0,)), ((), ())), preferred_element_type=F32)


def loop(count, body, unroll=1):
    def step(i, carry):
        body(i)
        return carry

    lax.fori_loop(0, count, step, 0, unroll=unroll)


def span(i, size):
    return pl.ds(pl.multiple_of(i * size, size), size)


def normal(x):
    center = x - jnp.mean(x, -1, keepdims=True)
    scale = lax.rsqrt(jnp.mean(center * center, -1, keepdims=True) + EPS)
    return center * scale, scale


def normal_back(dy, hat, scale, gain):
    d = dy * gain
    return scale * (
        d - jnp.mean(d, -1, keepdims=True) - hat * jnp.mean(d * hat, -1, keepdims=True)
    )


def gelu_both(h):
    phi = 0.5 * lax.erf(h * math.sqrt(0.5)) + 0.5
    bell = jnp.exp2(h * h * (-0.5 * math.log2(math.e)))
    return h * phi, phi + h * bell * (1.0 / math.sqrt(2.0 * math.pi))


def colsum(x):
    return jnp.sum(x, 0, keepdims=True)


def head_marks(width, size, dtype):
    lane = lax.broadcasted_iota(jnp.int32, (1, width), 1)
    return [((lane >= h * size) & (lane < (h + 1) * size)).astype(dtype) for h in range(width // size)]


def stacked(x, marks):
    return jnp.concatenate([x * m for m in marks], 0)


LOG2E = math.log2(math.e)


def attend(q, k, v, marks, ones, masked, scale):
    keys = k.shape[0]
    s = nt(q, stacked(k, marks))
    parts = []
    for h in range(len(marks)):
        x = masked(s[:, h * keys : (h + 1) * keys] * (scale * LOG2E))
        parts.append(jnp.exp2(x - jnp.max(x, -1, keepdims=True)).astype(BF16))
    e = jnp.concatenate(parts, 1)
    width = q.shape[1]
    if width % 128:
        top, total = nn(e, stacked(v, marks)), nn(e, ones)
    else:
        both = nn(e, jnp.concatenate([stacked(v, marks), ones], 1))
        top, total = both[:, :width], both[:, width:]
    inverse = 1.0 / total
    return e, (top * inverse).astype(BF16), inverse


def attend_back(q, k, v, e, o, inverse, d_out, marks, marks32, rows32, ones, scale):
    keys = k.shape[0]
    width = q.shape[1]
    d_one = d_out.astype(F32) * inverse
    d_two = (d_one * o.astype(F32)).astype(BF16)
    d_one = d_one.astype(BF16)
    if width % 128:
        d_s = nt(d_one, stacked(v, marks)) - nt(d_two, ones)
    else:
        d_s = nt(
            jnp.concatenate([d_one, d_two], 1), jnp.concatenate([stacked(v, marks), -ones], 1)
        )
    dr = (e.astype(F32) * d_s * scale).astype(BF16)
    d_q = nn(dr, stacked(k, marks)).astype(BF16)
    if width % 128:
        d_k_all, d_v_all = tn(dr, q), tn(e, d_one)
        d_k = d_v = 0.0
        for h in range(len(marks)):
            cut = slice(h * keys, (h + 1) * keys)
            d_k += d_k_all[cut] * marks32[h]
            d_v += d_v_all[cut] * marks32[h]
        return d_q, d_k.astype(BF16), d_v.astype(BF16)
    d_k_all = nn(jnp.transpose(q), dr)
    d_v_all = nn(jnp.transpose(d_one), e)
    d_k = d_v = 0.0
    for h in range(len(marks)):
        cut = slice(h * keys, (h + 1) * keys)
        d_k += d_k_all[:, cut] * rows32[h]
        d_v += d_v_all[:, cut] * rows32[h]
    return d_q, jnp.transpose(d_k.astype(BF16)), jnp.transpose(d_v.astype(BF16))


def ones_per_head(keys, marks):
    return jnp.concatenate([jnp.broadcast_to(m, (keys, m.shape[1])) for m in marks], 0)


ENC_SIZE = D // HEADS
ENC_SCALE = ENC_SIZE ** -0.5
DEC_SIZE = DD // DHEADS
DEC_SCALE = DEC_SIZE ** -0.5


CH = 64
DEC_ROWS = 576
ENC_A = 768
ENC_B = 384
DEC_K = DEC_ROWS // CH
B_K = (DEC_ROWS + ENC_A + ENC_B) // CH
ALL_K = B_K + 1
A_TOP = DEC_ROWS
B_TOP = DEC_ROWS + ENC_A
S_TOP = B_TOP + ENC_B
EARLY = 4
XFIRST = True
EARLY_ROWS = EARLY * CH
LAG = 2
ORDER = (0, 1, 2, 3, 9, 10, 11, 12, 13, 14, 15, 16, 17, 4, 18, 5, 19, 20, 6, 8, 21, 22, 23, 24, 27, 25, 26, 7)
PIECES = (2, 2, 3, 3, 3, 3, 3, 3, 3, 3, 3, 10, 10, 11, 12, 12, 13, 15, 15, 16, 16, 18, 20)
LATE = ORDER.index(B_K)
WHOLE_LOW = 6
WHOLE_HIGH = 22
SMALL = 16


def tile_of(number):
    place = number // 3
    return place % 2, place // 2 * CH, number % 3 * 256


MESH = pl.DeviceIdType.MESH


def far(src, dst, send, recv, peer):
    return pltpu.make_async_remote_copy(
        src_ref=src, dst_ref=dst, send_sem=send, recv_sem=recv, device_id=peer, device_id_type=MESH
    )


def forward_and_decoder(
    wid, shifts, order, vis, pat, gains, offs, b_qv, b_up, b_dqv, b_dup,
    h_qkv, h_proj, h_up, h_down, h_dqkv, h_dproj, h_dup, h_ddown,
    cot_hbm, ew, evec, table, dgains, doffs,
    o_x, o_x1, o_a, o_u, o_y, o_gp, o_qkv, o_p, o_o, o_w, o_wproj, o_wup, o_wdown, o_dec,
    d_enc, d_qvb, d_upb, d_small, dec_out,
    w_qkv, w_proj, w_up, w_down, bias, biases, qkv, proj, up, down,
    ex, ea, eu, ey, egp, eqkv, ep, eo, ex1, epart, esend, erecv, esend2, erecv2, eown,
    cot, x0, x1, a, acts, probs, o, inverse, u, ut, y, gp, g32, gb, gt, acc, e_ref, hot, perm, buf, dsend, e_rc, e_rcy, e_rx, e_ry,
    load_s, out_s, cot_s, w_s, w_r, bias_s, bias_r, dw_s, dw_r, ex_s, ex_r, ex2_s, ex2_r, do_s, do_r, e_s, e_r,
):
    sec = lax.axis_index("section")
    lane = lax.axis_index("tensor")
    mate = lane + 1 - 2 * lax.rem(lane, 2)
    over = lax.rem(lane + 2, LANES)
    cross = lax.rem(mate + 2, LANES)
    me = sec * LANES + lane
    devices = 2 * LANES
    clip = me
    clips = (me, sec * LANES + over)

    def group_peer(step):
        peer = lax.rem(me + step, devices)
        return peer, {"section": lax.div(peer, LANES), "tensor": lax.rem(peer, LANES)}

    own = [
        pltpu.make_async_copy(src, dst.at[0], load_s.at[n])
        for n, (src, dst) in enumerate(
            ((h_qkv, w_qkv), (h_proj, w_proj), (h_up, w_up), (h_down, w_down))
        )
    ]

    def place(n, shard, part=None):
        thick = (128, 128, 512, 512)[n]
        base = shard * thick
        cut = pl.ds(pl.multiple_of(base, thick), thick)
        if part is None:
            return (qkv.at[:, :, cut], proj.at[cut, :], up.at[:, cut], down.at[cut, :])[n]
        some = span(part, (256, 64, 256, 256)[n])
        if n == 0:
            return qkv.at[:, some, cut]
        if n == 2:
            return up.at[some, cut]
        few = thick // 2
        rows = pl.ds(pl.multiple_of(base + part * few, few), few)
        return (proj if n == 1 else down).at[rows, :]

    shards = (h_dqkv, h_dproj, h_dup, h_ddown)
    keep = [
        pltpu.make_async_copy(shards[n], place(n, lane), load_s.at[4 + n]) for n in range(4)
    ]
    for copy in own + keep:
        copy.start()
    fetch = pltpu.make_async_copy(cot_hbm.at[clip], cot, cot_s)
    fetch.start()

    barrier = pltpu.get_barrier_semaphore()
    for step in range(1, devices):
        pl.semaphore_signal(barrier, inc=1, device_id_type=MESH, device_id=group_peer(step)[1])
    bias[...] = jnp.zeros_like(bias)
    half = w_proj.shape[1]
    bias[0:1, :] = b_up[...].astype(F32).reshape(1, -1)
    bias[1:3, 0:half] = b_qv[...].astype(F32)
    bias[3:4, 0:512] = b_dup[...].astype(F32).reshape(1, -1)
    bias[4:6, 0:128] = b_dqv[...].astype(F32)
    biases[lane] = bias[...]
    stride = pat.shape[0] // VIS
    for c in range(2):
        row = lax.broadcasted_iota(jnp.int32, (PAD, pat.shape[0]), 0)
        col = lax.broadcasted_iota(jnp.int32, (PAD, pat.shape[0]), 1)
        pick = (col == row * stride + clips[c]).astype(F32).astype(BF16)
        ex[c * PAD : (c + 1) * PAD, :] = nn(pick, pat[...])

    pl.semaphore_wait(barrier, devices - 1)

    def enc_weight(n):
        src = (h_qkv, h_proj, h_up, h_down)[n]
        dst = (w_qkv, w_proj, w_up, w_down)[n]
        return far(src, dst.at[1], w_s.at[n], w_r.at[n], {"tensor": mate})

    def bias_copy(step):
        return far(
            bias, biases.at[lane], bias_s.at[step], bias_r.at[step],
            {"tensor": lax.rem(lane + step, LANES)},
        )

    def half_of(n):
        some = span(sec, (256, 64, 256, 256)[n])
        return shards[n].at[:, some, :] if n == 0 else shards[n].at[some, :]

    def dec_weight(n, kind):
        peer = {"section": 1 - sec} if kind == 2 else {"tensor": over if kind == 0 else mate}
        if kind == 0:
            src, dst = half_of(n), place(n, lane, sec)
        elif kind == 1:
            src, dst = shards[n], place(n, lane)
        else:
            src = dst = place(n, over, 1 - sec if kind == 4 else sec)
        return far(src, dst, dw_s.at[5 * n + kind], dw_r.at[5 * n + kind], peer)

    enc_weight(0).start()
    for step in range(1, LANES):
        bias_copy(step).start()
    enc_weight(1).start()
    dec_weight(0, 0).start()
    enc_weight(2).start()
    enc_weight(3).start()
    for n in range(4):
        dec_weight(n, 1).start()

    def pass_on(n):
        dec_weight(n, 0).wait_recv()
        dec_weight(n, 2).start()
        dec_weight(n, 3).start()

    def pass_last(n):
        dec_weight(n, 2).wait_recv()
        dec_weight(n, 4).start()

    def arrived(n):
        keep[n].wait()
        dec_weight(n, 1).wait_recv()
        dec_weight(n, 3).wait_recv()
        dec_weight(n, 4).wait_recv()

    width = wid[clip]
    bits = jnp.where(width == WIDE, 3, 2)
    turn = shifts[0, clip] * width
    mod = GRID - 1
    spot = 0
    for i in range(order.shape[1]):
        spot = spot + jnp.where(order[0, i] == clip, i, 0)
    batch = spot // CM
    count = 0
    for i in range(order.shape[1]):
        count = count + jnp.where(batch == i // CM, wid[order[0, i]], 0)
    factor_rows = CM * GRID / (jnp.full((1, 1), count, jnp.int32) * GRID_ROWS).astype(F32)

    def slot_of(index):
        return (index - turn) & mod

    def code_of(slot):
        band = ((slot >> bits) + shifts[0, clip]) >> 2
        strip = ((slot & (width - 1)) + shifts[1, clip]) >> 2
        return band * 4 + strip

    def valid_rows():
        slot = slot_of(lax.broadcasted_iota(jnp.int32, (GRID, 1), 0))
        return (slot < GRID_ROWS * width).astype(F32)

    def clip_gradient():
        fetch.wait()
        rolled = slot_of(lax.broadcasted_iota(jnp.int32, (GRID, GRID), 0))
        column = lax.broadcasted_iota(jnp.int32, (GRID, GRID), 1)
        perm[...] = (rolled == column).astype(F32).astype(BF16)
        g = nn(perm[...], cot[...]) * valid_rows() * factor_rows
        g32[...] = g
        gb[...] = g.astype(BF16)
        gt[...] = jnp.transpose(g.astype(BF16))
        d_small[...] = jnp.zeros_like(d_small)
        d_small[5:6, :] = colsum(g)

    seen = vis[pl.ds(clip, 1), :]
    target = jnp.concatenate([(seen + turn) & mod, jnp.full((1, PAD - VIS), -1, jnp.int32)], 1)

    def places(i):
        r = span(i, PAD)
        index = lax.broadcasted_iota(jnp.int32, (PAD, PAD), 0) + i * PAD
        column = lax.broadcasted_iota(jnp.int32, (PAD, PAD), 1)
        hot[r, :] = (index == target).astype(F32).astype(BF16)
        slot = slot_of(index)
        by_row = ((slot >> bits) == column).astype(F32).astype(BF16)
        by_col = ((slot & (width - 1)) == column).astype(F32).astype(BF16)
        row_part = nn(by_row, table[0]) + nn(by_row, table[1])
        col_part = nn(by_col, table[0]) + nn(by_col, table[1])
        x0[r, :] = jnp.concatenate([row_part, col_part], 1)

    egain = gains[...].astype(F32)
    eoff = offs[...].astype(F32)
    emarks = head_marks(half, ENC_SIZE, BF16)
    key = lax.broadcasted_iota(jnp.int32, (PAD, PAD), 1)
    floor = jnp.where(key < VIS, NEG * LOG2E, -1e30)
    eones = ones_per_head(PAD, emarks)
    blocks = D // 256

    def give_part(i, side):
        cut = span(i, 256)
        return far(
            esend.at[(1 - side) * PAD : (2 - side) * PAD, cut],
            erecv.at[side * PAD : (side + 1) * PAD, cut],
            ex_s.at[2 * i + side], ex_r.at[2 * i + side], {"tensor": over},
        )

    for c in range(2):
        rows = slice(c * PAD, (c + 1) * PAD)
        hat, _ = normal(ex[rows, :])
        ea[rows, :] = (hat * egain[0:1] + eoff[0:1]).astype(BF16)
        limit = (VIS * wid[clips[c]]) // WIDE
        for g, shard in enumerate((lane, mate)):
            if c == 0 and g == 0:
                own[0].wait()
            if c == 0 and g == 1:
                enc_weight(0).wait_recv()
                for step in range(1, LANES):
                    bias_copy(step).wait_recv()
            if g == 0:
                bq, bv = bias[1:2, 0:half], bias[2:3, 0:half]
            else:
                bq, bv = biases[shard, 1:2, 0:half], biases[shard, 2:3, 0:half]
            eqkv[g, 0, rows] = (nt(ea[rows, :], w_qkv[g, 0]) + bq).astype(BF16)
            eqkv[g, 1, rows] = nt(ea[rows, :], w_qkv[g, 1]).astype(BF16)
            eqkv[g, 2, rows] = (nt(ea[rows, :], w_qkv[g, 2]) + bv).astype(BF16)
            p, out, _ = attend(
                eqkv[g, 0, rows], eqkv[g, 1, rows], eqkv[g, 2, rows], emarks, eones,
                lambda s: jnp.where(key < limit, s, floor), ENC_SCALE,
            )
            ep[g, c] = p
            eo[g, rows] = out
        if c == 0:
            own[1].wait()
            enc_weight(1).wait_recv()
        for i in range(blocks):
            cut = slice(i * 256, (i + 1) * 256)
            t = nn(eo[0, rows], w_proj[0, :, cut]) + nn(eo[1, rows], w_proj[1, :, cut])
            epart[rows, cut] = t
            esend[rows, cut] = t.astype(BF16)
            give_part(i, 1 - c).start()
    pass_on(0)
    clip_gradient()
    own[2].wait()
    enc_weight(2).wait_recv()

    def give_last(i):
        cut = span(i, 256)
        return far(
            esend2.at[:, cut], erecv2.at[:, cut], ex2_s.at[i], ex2_r.at[i], {"tensor": over}
        )

    for c in (1, 0):
        rows = slice(c * PAD, (c + 1) * PAD)
        for i in range(blocks):
            give_part(i, c).wait_recv()
        t = ex[rows, :] + epart[rows, :] + erecv[rows, :].astype(F32) + eoff[2:3]
        ex1[rows, :] = t
        hat, _ = normal(t)
        eu[rows, :] = (hat * egain[1:2] + eoff[1:2]).astype(BF16)
        for g, shard in enumerate((lane, mate)):

            def enc_ff(i, g=g, shard=shard, rows=rows):
                cut = span(i, 256)
                h = nn(eu[rows, :], w_up[g, :, cut]) + biases[shard, 0:1, cut]
                act, slope = gelu_both(h)
                ey[g, rows, cut] = act.astype(BF16)
                egp[g, rows, cut] = slope.astype(BF16)

            loop(w_up.shape[2] // 256, enc_ff, unroll=3)
        if c == 1:
            own[3].wait()
            enc_weight(3).wait_recv()
        for i in range(blocks):
            cut = slice(i * 256, (i + 1) * 256)
            t = nn(ey[0, rows], w_down[0, :, cut]) + nn(ey[1, rows], w_down[1, :, cut])
            if c == 0:
                eown[:, cut] = t
            else:
                esend2[:, cut] = t.astype(BF16)
                give_last(i).start()
        if c == 1:
            for n in (1, 2, 3):
                dec_weight(n, 0).start()
            pass_last(0)
    outs = [
        pltpu.make_async_copy(src, dst, out_s.at[n])
        for n, (src, dst) in enumerate(
            (
                (ex.at[0:PAD, :], o_x), (ex1, o_x1), (ea, o_a), (eu, o_u), (ey, o_y), (egp, o_gp),
                (eqkv, o_qkv), (ep, o_p), (eo, o_o), (w_qkv.at[1], o_w), (w_proj.at[1], o_wproj),
                (w_up.at[1], o_wup), (w_down.at[1], o_wdown),
            )
        )
    ]
    for copy in outs:
        copy.start()
    loop(GRID // PAD, places, unroll=2)
    for i in range(blocks):
        give_last(i).wait_recv()

    e_ref[...] = (ex1[0:PAD, :] + eown[...] + erecv2[...].astype(F32) + eoff[3:4]).astype(BF16)
    vec = evec[...].astype(F32)
    m = (nn(e_ref[...], ew[...]) + vec[0:1]).astype(BF16)
    gain = dgains[...].astype(F32)
    offsets = doffs[...].astype(F32)

    def start(i):
        r = span(i, PAD)
        oh = hot[r, :]
        hit = jnp.sum(oh.astype(F32), -1, keepdims=True)
        x = jnp.where(hit > 0, nn(oh, m), vec[1:2]).astype(BF16).astype(F32) + x0[r, :]
        x0[r, :] = x
        hat, _ = normal(x)
        a[r, :] = (hat * gain[0:1] + offsets[0:1]).astype(BF16)

    loop(GRID // PAD, start, unroll=2)
    arrived(0)

    def dec_bias(row, size):
        return jnp.concatenate([biases[k, row : row + 1, 0:size] for k in range(LANES)], 1)

    acts[0] = (nn(a[...], qkv[0]) + dec_bias(4, 128)).astype(BF16)
    acts[1] = nn(a[...], qkv[1]).astype(BF16)
    acts[2] = (nn(a[...], qkv[2]) + dec_bias(5, 128)).astype(BF16)
    pass_on(1)
    pass_on(2)
    marks = head_marks(128, DEC_SIZE, BF16)
    marks32 = head_marks(128, DEC_SIZE, F32)
    dim = lax.broadcasted_iota(jnp.int32, (128, 1), 0)
    rows32 = [
        ((dim >= h * DEC_SIZE) & (dim < (h + 1) * DEC_SIZE)).astype(F32) for h in range(len(marks))
    ]

    ones = ones_per_head(PAD, marks)

    def attention(i):
        r = span(i, PAD)
        row_slot = slot_of(lax.broadcasted_iota(jnp.int32, (PAD, PAD), 0) + i * PAD)
        key_slot = slot_of(lax.broadcasted_iota(jnp.int32, (PAD, PAD), 1) + i * PAD)
        allowed = (code_of(row_slot) == code_of(key_slot)) & (key_slot < GRID_ROWS * width)
        for g in range(DD // 128):
            c = slice(g * 128, (g + 1) * 128)
            probs[i, :, g * 512 : (g + 1) * 512], o[r, c], inverse[r, c] = attend(
                acts[0, r, c], acts[1, r, c], acts[2, r, c], marks, ones,
                lambda s: jnp.where(allowed, s, NEG * LOG2E), DEC_SCALE,
            )

    loop(GRID // PAD, attention, unroll=2)
    pass_last(1)
    pass_last(2)
    pass_on(3)
    arrived(1)

    def mix(i):
        r = span(i, 256)
        x = x0[r, :] + nn(o[r, :], proj[...]) + offsets[2:3]
        x1[r, :] = x
        hat, _ = normal(x)
        un = hat * gain[1:2] + offsets[1:2]
        u[r, :] = un.astype(BF16)
        ut[:, r] = jnp.transpose(un.astype(BF16))

    loop(2, mix)
    pass_last(3)
    arrived(2)

    def ff(i):
        c = span(i, 256)
        h = nn(u[...], up[:, c]) + biases[lax.div(i, 2), 3:4, span(lax.rem(i, 2), 256)]
        act, slope = gelu_both(h)
        y[:, c] = act.astype(BF16)
        gp[:, c] = slope.astype(BF16)

    loop(up.shape[1] // 256, ff, unroll=2)
    arrived(3)
    def out(i):
        c = span(i, 256)
        acc[:, c] = nn(y[...], down[:, c])

    loop(2, out)
    full = ((acc[...] + x1[...] + offsets[3:4]) * valid_rows()).astype(BF16)
    turned = tn(full, perm[...]).astype(BF16)
    for k in range(devices):
        dsend[k] = turned[k * dsend.shape[1] : (k + 1) * dsend.shape[1]]

    def decoded_copy(step):
        peer, spot = group_peer(step)
        return far(dsend.at[peer], dec_out.at[me], do_s.at[step], do_r.at[step], spot)

    for step in range(1, devices):
        decoded_copy(step).start()
    dec_out[me] = dsend[me]

    def ff_back(shard):
        for side in range(2):
            c = span(2 * shard + side, 256)
            d_down = nn(gt[...], y[:, c]).astype(BF16)
            dh = nt(gb[...], down[c, :]) * gp[:, c].astype(F32)
            d_upb[:, c] = colsum(dh)
            du = dh.astype(BF16)
            gp[:, c] = du
            d_up = nn(ut[...], du).astype(BF16)
            for block in range(GRID // CH):
                rows = slice(block * CH, (block + 1) * CH)
                h, top, col = tile_of(4 * block + side)
                buf[shard, h, top : top + CH, col : col + 256] = d_up[rows]
                h, top, col = tile_of(4 * block + 2 + side)
                buf[shard, h, top : top + CH, col : col + 256] = d_down[rows]

    def early_core(which):
        shard, land = ((mate, e_rc), (cross, e_rcy))[which]
        return far(
            buf.at[shard, :, 0:EARLY_ROWS, :], land, e_s.at[which], e_r.at[which], {"tensor": mate}
        )

    def early_x(which):
        return far(
            buf.at[(over, lane)[which], 1 - sec, 0:EARLY_ROWS, :], e_rx.at[which],
            e_s.at[2 + which], e_r.at[2 + which], {"section": 1 - sec},
        )

    def early_y():
        return far(
            buf.at[over, sec, 0:EARLY_ROWS, :], e_ry, e_s.at[4], e_r.at[4], {"tensor": over}
        )

    def early_add(shard, land):
        def body(i):
            r = span(i, CH)
            buf[shard, :, r, :] = buf[shard, :, r, :] + land[:, r, :]

        loop(EARLY_ROWS // CH, body)

    def early_half(shard, land):
        buf[shard, sec, 0:EARLY_ROWS, :] = buf[shard, sec, 0:EARLY_ROWS, :] + land

    def ff_step(i):
        ff_back(jnp.where(i == 0, cross, jnp.where(i == 1, over, jnp.where(i == 2, mate, lane))))

        @pl.when(i == 1)
        def _():
            early_core(1).start()

        @pl.when(i == 2)
        def _():
            early_core(0).start()

    loop(LANES, ff_step)
    early_core(1).wait_recv()
    early_add(over, e_rcy)
    early_x(0).start()

    def ff_in(i):
        c = span(i, 256)
        acc[:, c] = nt(gp[...], up[c, :])

    loop(2, ff_in)
    early_core(0).wait_recv()
    early_add(lane, e_rc)
    early_x(1).start()

    def mix_back(i):
        r = span(i, 256)
        hat, scale = normal(x1[r, :])
        da = acc[r, :]
        dx = g32[r, :] + normal_back(da, hat, scale, gain[1:2])
        d_small[1:2, :] += colsum(da * hat)
        d_small[3:4, :] += colsum(da)
        d_small[4:5, :] += colsum(dx)
        g32[r, :] = dx
        dxb = dx.astype(BF16)
        gb[r, :] = dxb
        u[r, :] = nt(dxb, proj[...]).astype(BF16)

    loop(2, mix_back)
    d_proj = tn(o[...], gb[...]).astype(BF16)
    for block in range(GRID // CH):
        h, top, col = tile_of(33 + 2 * block)
        side = slice(block // 2 * 128, (block // 2 + 1) * 128)
        for k in range(LANES):
            row = k * 128 + block % 2 * CH
            buf[k, h, top : top + CH, col + 128 : col + 256] = d_proj[row : row + CH, side]

    def attention_back(i):
        r = span(i, PAD)
        for k in range(DD // 128):
            c = slice(k * 128, (k + 1) * 128)
            acts[0, r, c], acts[1, r, c], acts[2, r, c] = attend_back(
                acts[0, r, c], acts[1, r, c], acts[2, r, c],
                probs[i, :, k * 512 : (k + 1) * 512], o[r, c], inverse[r, c], u[r, c],
                marks, marks32, rows32, ones, DEC_SCALE,
            )

    loop(GRID // PAD, attention_back, unroll=2)
    early_x(0).wait_recv()
    early_half(over, e_rx[0])
    early_y().start()
    d_qvb[0:1, :] = colsum(acts[0].astype(F32))
    d_qvb[1:2, :] = colsum(acts[2].astype(F32))

    def project_back(i):
        c = span(i, 256)
        acc[:, c] = (
            nt(acts[0], qkv[0, c, :]) + nt(acts[1], qkv[1, c, :]) + nt(acts[2], qkv[2, c, :])
        )

    loop(2, project_back)
    gt[...] = jnp.transpose(a[...])
    for j in range(3):
        d_qkv = nn(gt[...], acts[j]).astype(BF16)
        for block in range(GRID // CH):
            h, top, col = tile_of(32 + 2 * block + j // 2)
            col = col + j % 2 * 128
            rows = slice(block * CH, (block + 1) * CH)
            for k in range(LANES):
                buf[k, h, top : top + CH, col : col + 128] = d_qkv[rows, k * 128 : (k + 1) * 128]

    def start_back(i):
        r = span(i, PAD)
        hat, scale = normal(x0[r, :])
        da = acc[r, :]
        dx = g32[r, :] + normal_back(da, hat, scale, gain[0:1])
        d_small[0:1, :] += colsum(da * hat)
        d_small[2:3, :] += colsum(da)
        dg = dx.astype(BF16)
        gb[r, :] = dg
        hit = jnp.sum(hot[r, :].astype(F32), -1, keepdims=True)
        d_small[7:8, :] += colsum(jnp.where(hit > 0, 0.0, dg.astype(F32)))

    loop(GRID // PAD, start_back, unroll=2)
    dm = tn(hot[...], gb[...])
    d_small[6:7, :] = colsum(dm)
    dmb = dm.astype(BF16)
    d_enc[...] = nt(dmb, ew[...]).astype(BF16)
    d_ew = tn(e_ref[...], dmb).astype(BF16)
    for k in range(LANES):
        for h in range(2):
            top = k * 192 + h * 64
            buf[k, h, 512:576, 0:512] = d_ew[top : top + 64]
            buf[k, h, 512:576, 512:768] = d_ew[k * 192 + 128 : (k + 1) * 192, h * 256 : (h + 1) * 256]

    early_x(1).wait_recv()
    early_half(lane, e_rx[1])
    early_y().wait_recv()
    early_half(lane, e_ry[...])
    later = pl.ds(EARLY_ROWS, DEC_ROWS - EARLY_ROWS)
    rest = [pltpu.make_async_copy(buf.at[lane], o_dec.at[lane], out_s.at[13])] + [
        pltpu.make_async_copy(buf.at[k, :, later, :], o_dec.at[k, :, later, :], out_s.at[14 + n])
        for n, k in enumerate((mate, over, cross))
    ]
    for copy in rest:
        copy.start()
    for copy in outs + rest:
        copy.wait()
    for which in range(2):
        early_core(which).wait_send()
        early_x(which).wait_send()
    early_y().wait_send()
    for n in range(4):
        enc_weight(n).wait_send()
        for kind in range(5):
            dec_weight(n, kind).wait_send()
    for step in range(1, LANES):
        bias_copy(step).wait_send()
    for i in range(blocks):
        give_part(i, 0).wait_send()
        give_part(i, 1).wait_send()
        give_last(i).wait_send()
    for step in range(1, devices):
        decoded_copy(step).wait()


def forward_call(args, half, hid, dff):
    dma = lambda *s: pltpu.SemaphoreType.DMA(s)
    vm = lambda dtype, *shape: pltpu.VMEM(shape, dtype)
    rows = 2 * PAD
    keys = PAD * half // ENC_SIZE
    devices = 2 * LANES
    slab = DD // devices
    kept = [
        ((PAD, D), F32), ((rows, D), F32), ((rows, D), BF16), ((rows, D), BF16),
        ((2, rows, hid), BF16), ((2, rows, hid), BF16), ((2, 3, rows, half), BF16),
        ((2, 2, PAD, keys), BF16), ((2, rows, half), BF16),
        ((3, half, D), BF16), ((half, D), BF16), ((D, hid), BF16), ((hid, D), BF16),
        ((LANES, 2, DEC_ROWS, D), BF16),
    ]
    made = [
        ((PAD, D), BF16), ((2, DD), F32), ((1, dff), F32), ((8, DD), F32),
        ((devices, slab, GRID), BF16),
    ]
    return pl.pallas_call(
        forward_and_decoder,
        out_shape=[jax.ShapeDtypeStruct(s, d) for s, d in kept + made],
        in_specs=[SM, SM, SM] + [VM] * 8 + [ANY] * 9 + [VM] * 5,
        out_specs=[ANY] * len(kept) + [VM] * len(made),
        scratch_shapes=[
            vm(BF16, 2, 3, half, D), vm(BF16, 2, half, D), vm(BF16, 2, D, hid), vm(BF16, 2, hid, D),
            vm(F32, 8, D), vm(F32, LANES, 8, D),
            vm(BF16, 3, DD, DD), vm(BF16, DD, DD), vm(BF16, DD, dff), vm(BF16, dff, DD),
            vm(F32, rows, D), vm(BF16, rows, D), vm(BF16, rows, D), vm(BF16, 2, rows, hid),
            vm(BF16, 2, rows, hid), vm(BF16, 2, 3, rows, half), vm(BF16, 2, 2, PAD, keys),
            vm(BF16, 2, rows, half), vm(F32, rows, D), vm(F32, rows, D), vm(BF16, rows, D),
            vm(BF16, rows, D), vm(BF16, PAD, D), vm(BF16, PAD, D), vm(F32, PAD, D),
            vm(BF16, GRID, DD), vm(F32, GRID, DD), vm(F32, GRID, DD), vm(BF16, GRID, DD),
            vm(BF16, 3, GRID, DD), vm(BF16, GRID // PAD, PAD, DHEADS * PAD), vm(BF16, GRID, DD),
            vm(F32, GRID, DD),
            vm(BF16, GRID, DD), vm(BF16, DD, GRID), vm(BF16, GRID, dff), vm(BF16, GRID, dff),
            vm(F32, GRID, DD), vm(BF16, GRID, DD), vm(BF16, DD, GRID), vm(F32, GRID, DD),
            vm(BF16, PAD, D), vm(BF16, GRID, PAD), vm(BF16, GRID, GRID),
            vm(BF16, LANES, 2, DEC_ROWS, D),
            vm(BF16, devices, slab, GRID), *[vm(BF16, 2, EARLY_ROWS, D)] * 3, vm(BF16, EARLY_ROWS, D),
            dma(8), dma(17), pltpu.SemaphoreType.DMA, dma(4), dma(4), dma(LANES), dma(LANES),
            dma(20), dma(20), dma(6), dma(6), dma(3), dma(3), dma(devices), dma(devices),
            dma(5), dma(5),
        ],
        compiler_params=pltpu.CompilerParams(
            collective_id=0, has_side_effects=True, vmem_limit_bytes=VMEM_LIMIT
        ),
    )(*args)


def add(x, y):
    return x + y


def backward_and_sums(
    d_enc, gains,
    h_u, h_y, h_gp, h_down0, h_down1, h_up0, h_up1,
    h_x, h_x1, h_a, h_qkv, h_p, h_o, h_w0, h_w1, h_proj0, h_proj1,
    dec, dec_qvb, dec_upb, dec_small,
    out, emb, dx_out,
    gb, gt, ut, part, send, recv, du, gx, dx1, d_o, d_acts, own, send1, recv1, dx32, dx,
    d_upb, d_qvb, d_small,
    acc, yacc, enc_mate, rcy, ry, land_x, land_l, land_r, small32, small,
    u, y, gp, down0, down1, up0, up1, x, x1, a, qkv, p, o, w0, w1, proj0, proj1, fetch_s,
    load_s, ex_s, ex_r,
    core_s, core_r, corey_s, corey_r, y_s, y_r, x_s, x_r, z_s, zl_r, zr_r,
    bl_s, br_s, b_r, a_s, a_r, emb_s, emb_r, dx_s, dx_r,
):
    sec = lax.axis_index("section")
    lane = lax.axis_index("tensor")
    pos = lax.axis_index("dp")
    count = lax.axis_size("dp")
    mate = lane + 1 - 2 * lax.rem(lane, 2)
    over = lax.rem(lane + 2, LANES)
    cross = lax.rem(mate + 2, LANES)
    first = pos == 0
    last = pos == count - 1
    me = sec * LANES + lane
    devices = 2 * LANES

    def group_peer(step):
        peer = lax.rem(me + step, devices)
        return peer, {"section": lax.div(peer, LANES), "tensor": lax.rem(peer, LANES)}

    barrier = pltpu.get_barrier_semaphore()
    for step in range(1, devices):
        pl.semaphore_signal(barrier, inc=1, device_id_type=MESH, device_id=group_peer(step)[1])

    @pl.when(pos > 0)
    def _():
        pl.semaphore_signal(barrier, inc=1, device_id={"dp": pos - 1}, device_id_type=MESH)

    @pl.when(pos < count - 1)
    def _():
        pl.semaphore_signal(barrier, inc=1, device_id={"dp": pos + 1}, device_id_type=MESH)

    loads = [
        pltpu.make_async_copy(dec.at[lane], acc.at[:, 0:DEC_ROWS, :], load_s.at[0]),
        pltpu.make_async_copy(
            dec.at[over, :, EARLY_ROWS:DEC_ROWS, :], yacc.at[:, 0 : DEC_ROWS - EARLY_ROWS, :],
            load_s.at[1],
        ),
    ]
    for load in loads:
        load.start()
    fetches = [
        pltpu.make_async_copy(src, dst, fetch_s.at[n])
        for n, (src, dst) in enumerate(
            (
                (h_u, u), (h_y, y), (h_gp, gp), (h_down0, down0), (h_down1, down1), (h_up0, up0),
                (h_up1, up1), (h_x, x), (h_x1, x1), (h_a, a), (h_qkv, qkv), (h_p, p), (h_o, o),
                (h_w0, w0), (h_w1, w1), (h_proj0, proj0), (h_proj1, proj1),
            )
        )
    ]
    for fetch in fetches:
        fetch.start()
    small32[...] = jnp.zeros_like(small32)
    d_small[...] = jnp.zeros_like(d_small)
    gb[0:PAD, :] = d_enc[...]
    ends = jnp.where(first, 0, 1) + jnp.where(last, 0, 1)
    pl.semaphore_wait(barrier, devices - 1 + ends)

    gain = gains[...].astype(F32)
    width = w0.shape[1]
    marks = head_marks(width, ENC_SIZE, BF16)
    marks32 = head_marks(width, ENC_SIZE, F32)
    ones = ones_per_head(PAD, marks)

    def rows(k, size=CH):
        return pl.ds(pl.multiple_of(k * size, size), size)

    def give_enc():
        return far(d_enc, gb.at[PAD : 2 * PAD, :], ex_s.at[0], ex_r.at[0], {"tensor": over})

    def give_part(i, half):
        cut = rows(i, 256)
        n = 1 + 2 * i + half
        return far(
            send.at[(1 - half) * PAD : (2 - half) * PAD, cut],
            recv.at[half * PAD : (half + 1) * PAD, cut],
            ex_s.at[n], ex_r.at[n], {"tensor": over},
        )

    def give_last(i):
        cut = rows(i, 256)
        return far(send1.at[:, cut], recv1.at[:, cut], ex_s.at[7 + i], ex_r.at[7 + i], {"tensor": over})

    def ff_back(g, i, down):
        c = rows(i, 256)
        d_down = nn(gt[...], y[g, :, c]).astype(BF16)
        dh = nt(gb[...], down[c, :]) * gp[g, :, c].astype(F32)
        d_upb[g, :, c] = colsum(dh)
        dub = dh.astype(BF16)
        du[g, :, c] = dub
        d_up = nn(ut[...], dub).astype(BF16)
        if g == 0:
            acc[1, A_TOP:B_TOP, c] = d_down
            acc[0, A_TOP:B_TOP, c] = d_up
        else:
            enc_mate[1, 0:ENC_A, c] = d_down
            enc_mate[0, 0:ENC_A, c] = d_up

    def ff_in(i):
        c = rows(i, 256)
        t = nt(du[0], up0[c, :]) + nt(du[1], up1[c, :])
        part[:, c] = t
        send[:, c] = t.astype(BF16)
        give_part(i, 0).start()
        give_part(i, 1).start()

    def norm_two():
        for fetch in fetches[7:]:
            fetch.wait()
        for k in range(D // 256):
            give_part(k, 0).wait_recv()
            give_part(k, 1).wait_recv()

        def body(j):
            r = rows(j, 64)
            da = part[r, :] + recv[r, :].astype(F32)
            hat, scale = normal(x1[r, :])
            g = gb[r, :].astype(F32)
            d = g + normal_back(da, hat, scale, gain[1:2])
            gx[r, :] = d.astype(BF16)
            dx1[r, :] = d

            @pl.when(j < 2)
            def _():
                d_small[1:2, :] += colsum(da * hat)
                d_small[3:4, :] += colsum(da)
                d_small[4:5, :] += colsum(d)
                d_small[5:6, :] += colsum(g)

        loop(2 * PAD // 64, body)

    def attention(g, c):
        if c == 0:
            d_proj = tn(o[g], gx[...]).astype(BF16)
            if g == 0:
                acc[1, B_TOP + width : S_TOP, :] = d_proj
            else:
                enc_mate[1, ENC_A + width : ENC_A + 2 * width, :] = d_proj
            d_o[...] = nt(gx[...], (proj0, proj1)[g][...]).astype(BF16)
        r = slice(c * PAD, (c + 1) * PAD)
        d_acts[g, 0, r], d_acts[g, 1, r], d_acts[g, 2, r] = attend_back(
            qkv[g, 0, r], qkv[g, 1, r], qkv[g, 2, r], p[g, c], o[g, r], 1.0 / nn(p[g, c], ones),
            d_o[r, :], marks, marks32, None, ones, ENC_SCALE,
        )
        if c == 1:
            d_qvb[g, 0:1, :] = colsum(d_acts[g, 0].astype(F32))
            d_qvb[g, 1:2, :] = colsum(d_acts[g, 2].astype(F32))

    def project_in(i):
        c = rows(i, 256)
        t = 0.0
        for g, w in enumerate((w0, w1)):
            for j in range(3):
                t += nn(d_acts[g, j], w[j, :, c])
        own[:, c] = t[:PAD]
        send1[:, c] = t[PAD:].astype(BF16)
        give_last(i).start()

    def project_grad(g):
        for j in range(3):
            row = (j % 2) * width
            d = tn(d_acts[g, j], a[...]).astype(BF16)
            if g == 0:
                acc[j // 2, B_TOP + row : B_TOP + row + width, :] = d
            else:
                enc_mate[j // 2, ENC_A + row : ENC_A + row + width, :] = d

    def norm_one():
        for k in range(D // 256):
            give_last(k).wait_recv()

        def body(j):
            r = rows(j, 64)
            da = own[r, :] + recv1[r, :].astype(F32)
            hat, scale = normal(x[r, :])
            d_small[0:1, :] += colsum(da * hat)
            d_small[2:3, :] += colsum(da)
            dx32[r, :] = dx1[r, :] + normal_back(da, hat, scale, gain[0:1])

        loop(PAD // 64, body)
        turned = jnp.transpose(dx32[...])
        cut = D // devices
        for k in range(devices):
            dx[k] = turned[k * cut : (k + 1) * cut, 0:VIS].astype(BF16)
        for r in range(LANES):
            small32[r, 8:9, 0:512] = dec_upb[:, r * 512 : (r + 1) * 512]
            small32[r, 9:10, 0:128] = dec_qvb[0:1, r * 128 : (r + 1) * 128]
            small32[r, 9:10, 128:256] = dec_qvb[1:2, r * 128 : (r + 1) * 128]
            small32[r, 0:8, 0:512] = dec_small[...]
            small32[r, 16:24, :] = d_small[...]
        for g, shard in enumerate((lane, mate)):
            small32[shard, 10:11, :] = d_upb[g]
            small32[shard, 11:12, 0:192] = d_qvb[g, 0:1]
            small32[shard, 11:12, 256:448] = d_qvb[g, 1:2]
        for r in range(LANES):
            for h in range(2):
                small[r, h] = small32[r, h * SMALL : (h + 1) * SMALL].astype(BF16)
        acc[:, S_TOP : S_TOP + SMALL, :] = small[lane]
        yacc[:, DEC_ROWS - EARLY_ROWS :, :] = small[over]
        core_copy(LATE, small.at[mate], SMALL).start()
        corey_copy(LATE, small.at[cross], SMALL).start()
        for step in range(1, devices):
            dx_copy(step).start()
        dx_out[me] = dx[me]

    def core_enc(lo, hi):
        def body(m):
            block = block_of(m)

            @pl.when((block >= lo) & (block < hi))
            def _():
                src = pl.ds(pl.multiple_of(block * CH - DEC_ROWS, CH), CH)
                core_copy(m, enc_mate.at[:, src, :]).start()

        loop(ALL_K, body)

    def first_piece():
        for fetch in fetches[:7]:
            fetch.wait()
        ut[...] = jnp.transpose(u[...])
        give_enc().wait_recv()
        gt[...] = jnp.transpose(gb[...])

    def ff_step(k):
        for g, down in enumerate((down0, down1)):
            @pl.when(lax.rem(k, 2) == g)
            def _(g=g, down=down):
                ff_back(g, lax.div(k, 2), down)

    def run_pieces(n):
        def several(low, high, body):
            begin = sum(jnp.where(n > t, 1, 0) for t in PIECES[low:high])
            end = sum(jnp.where(n >= t, 1, 0) for t in PIECES[low:high])
            lax.fori_loop(begin, end, lambda k, c: (body(k), c)[1], 0)

        def single(k, body):
            @pl.when(n == PIECES[k])
            def _():
                body()

        single(0, first_piece)
        several(1, 7, ff_step)
        single(7, lambda: core_enc(DEC_K, DEC_K + ENC_A // CH))
        several(8, 11, ff_in)
        single(11, norm_two)
        for k in range(4):
            single(12 + k, lambda k=k: attention(k // 2, k % 2))
        several(16, 19, project_in)
        for g in range(2):
            single(19 + g, lambda g=g: project_grad(g))
        single(21, lambda: core_enc(DEC_K + ENC_A // CH, B_K))
        single(22, norm_one)

    def dx_copy(step):
        peer, place = group_peer(step)
        return far(dx.at[peer], dx_out.at[me], dx_s.at[step], dx_r.at[step], place)

    def emb_copy(step):
        return far(
            out.at[:, pl.ds(512, CH), :], emb.at[lane], emb_s.at[step], emb_r.at[step],
            {"tensor": lax.rem(lane + step, LANES)},
        )

    def block_of(m):
        shift = 0
        for k in range(1, ALL_K):
            if ORDER[k] - k != ORDER[k - 1] - k + 1:
                shift = jnp.where(m >= k, ORDER[k] - k, shift)
        return m + shift

    def is_dec(m):
        return (block_of(m) < DEC_K) & (m >= EARLY)

    def at(m, size=CH):
        return pl.ds(pl.multiple_of(block_of(m) * CH, CH), size)

    def slot(m, size=CH):
        return pl.ds(pl.multiple_of(m * CH, CH), size)

    def y_at(m, size=CH):
        return pl.ds(pl.multiple_of((jnp.minimum(block_of(m), DEC_K) - EARLY) * CH, CH), size)

    def core_copy(m, src, size=CH):
        return far(src, out.at[:, at(m, size), :], core_s.at[m], core_r.at[m], {"tensor": mate})

    def corey_copy(m, src, size=CH):
        return far(src, rcy.at[:, y_at(m, size), :], corey_s.at[m], corey_r.at[m], {"tensor": mate})

    def y_copy(m, size=CH):
        cut = y_at(m, size)
        return far(
            yacc.at[:, cut, :], ry.at[:, cut, :], y_s.at[m], y_r.at[m], {"tensor": over}
        )

    def x_copy(m, size=CH):
        return far(
            acc.at[1 - sec, at(m, size), :], land_x.at[0, slot(m, size), :], x_s.at[m], x_r.at[m],
            {"section": 1 - sec},
        )

    def xc_copy(m):
        return far(
            acc.at[:, at(m), :], land_x.at[:, slot(m), :], x_s.at[m], x_r.at[m],
            {"section": 1 - sec},
        )

    def z_copy(m, whole, right, size=CH):
        land = land_l if right else land_r
        if whole:
            src, dst = acc.at[:, at(m), :], land.at[:, slot(m), :]
        else:
            src, dst = acc.at[sec, at(m, size), :], land.at[0, slot(m, size), :]
        landed = zl_r if right else zr_r
        return far(src, dst, z_s.at[m], landed.at[m], {"dp": pos + 1 if right else pos - 1})

    def b_copy(m, whole, right, size=CH):
        place = out.at[:, at(m), :] if whole else out.at[sec, at(m, size), :]
        sent = br_s if right else bl_s
        return far(place, place, sent.at[m], b_r.at[m], {"dp": pos + 1 if right else pos - 1})

    def a_copy(m, size=CH):
        place = out.at[sec, at(m, size), :]
        return far(place, place, a_s.at[m], a_r.at[m], {"section": 1 - sec})

    def a_wait(m, size=CH):
        place = out.at[1 - sec, at(m, size), :]
        far(place, place, a_s.at[m], a_r.at[m], {"section": 1 - sec}).wait_recv()

    give_enc().start()

    def start_core(m):
        @pl.when(is_dec(m))
        def _():
            core_copy(m, dec.at[mate, :, at(m), :]).start()
            corey_copy(m, dec.at[cross, :, at(m), :]).start()

    loop(ALL_K, start_core)
    for load in loads:
        load.wait()

    def join_core(m, size):
        core_copy(m, out.at[:, at(m, size), :], size).wait_recv()
        acc[:, at(m, size), :] = add(acc[:, at(m, size), :], out[:, at(m, size), :])

    def join_core_y(m, size):
        corey_copy(m, rcy.at[:, y_at(m, size), :], size).wait_recv()
        yacc[:, y_at(m, size), :] = add(yacc[:, y_at(m, size), :], rcy[:, y_at(m, size), :])
        y_copy(m, size).start()

    def stage_c(m):
        @pl.when((m >= EARLY) & (m != LATE))
        def _():
            join_core(m, CH)

            @pl.when(is_dec(m))
            def _():
                join_core_y(m, CH)

        @pl.when(m == LATE)
        def _():
            join_core(m, SMALL)
            join_core_y(m, SMALL)

    def finished(m):
        @pl.when(block_of(m) == DEC_K - 1)
        def _():
            for step in range(1, LANES):
                emb_copy(step).start()
            emb[lane] = out[:, 512 : 512 + CH, :]

    def line_of(root, whole, size=CH):
        left = pos < root
        right = pos > root
        here = pos == root
        reach = max(root, count - 1 - root)
        level = jnp.where(left, pos, jnp.where(right, count - 1 - pos, reach))
        dist = jnp.where(left, root - pos, pos - root)

        def view(ref, m):
            return ref.at[:, at(m), :] if whole else ref.at[sec, at(m, size), :]

        def landed(ref, m):
            return ref.at[:, slot(m), :] if whole else ref.at[0, slot(m, size), :]

        def hop(m, rightward):
            return z_copy(m, whole, rightward, size)

        def back_hop(m, rightward):
            return b_copy(m, whole, rightward, size)

        def outer(m):
            @pl.when(left & first)
            def _():
                hop(m, True).start()

            @pl.when(right & last)
            def _():
                hop(m, False).start()

        def inward(m):
            @pl.when(left & (pos > 0))
            def _():
                hop(m, True).wait_recv()
                view(acc, m)[...] = add(view(acc, m)[...], landed(land_l, m)[...])
                hop(m, True).start()

            @pl.when(right & (pos < count - 1))
            def _():
                hop(m, False).wait_recv()
                view(acc, m)[...] = add(view(acc, m)[...], landed(land_r, m)[...])
                hop(m, False).start()

            @pl.when(here)
            def _():
                total = view(acc, m)[...].astype(F32)
                if root > 0:
                    hop(m, True).wait_recv()
                    total = total + landed(land_l, m)[...].astype(F32)
                if root < count - 1:
                    hop(m, False).wait_recv()
                    total = total + landed(land_r, m)[...].astype(F32)
                if whole:
                    view(acc, m)[...] = total.astype(BF16)
                    xc_copy(m).start()
                else:
                    view(out, m)[...] = total.astype(BF16)
                    spread(m)
                    a_copy(m, size).start()

        def spread(m):
            if root > 0:
                back_hop(m, False).start()
            if root < count - 1:
                back_hop(m, True).start()

        def crossed(m):
            xc_copy(m).wait_recv()
            view(out, m)[...] = add(view(acc, m)[...], landed(land_x, m)[...])
            spread(m)
            finished(m)

        def outward(m):
            back_hop(m, False).wait_recv()

            @pl.when(left & (pos > 0))
            def _():
                back_hop(m, False).start()

            @pl.when(right & (pos < count - 1))
            def _():
                back_hop(m, True).start()

            if whole:
                finished(m)
            else:
                a_copy(m, size).start()

        def sent(m):
            @pl.when(jnp.logical_not(here))
            def _():
                hop(m, True).wait_send()

            @pl.when((pos <= root) & (pos > 0))
            def _():
                back_hop(m, False).wait_send()

            @pl.when((pos >= root) & (pos < count - 1))
            def _():
                back_hop(m, True).wait_send()

            if whole:
                @pl.when(here)
                def _():
                    xc_copy(m).wait_send()
            else:
                a_copy(m, size).wait_send()

                @pl.when(crosses_first(m))
                def _():
                    x_copy(m, size).wait_send()

        def crosses_first(m):
            return m >= EARLY if XFIRST else m >= 0

        def set_off(m):
            if whole:
                outer(m)
            else:
                x_copy(m, size).start()

        def set_off_early(m):
            if XFIRST:
                outer(m)
            else:
                set_off(m)

        def add_y(m):
            def joined():
                y_copy(m, size).wait_recv()
                acc[:, at(m, size), :] = add(acc[:, at(m, size), :], ry[:, y_at(m, size), :])

            if size == CH:
                pl.when(is_dec(m))(joined)
            else:
                joined()
            set_off(m)

        def add_x(m):
            @pl.when(crosses_first(m))
            def _():
                x_copy(m, size).wait_recv()
                acc[sec, at(m, size), :] = add(
                    acc[sec, at(m, size), :], land_x[0, slot(m, size), :]
                )
                outer(m)

        def last_half(m):
            a_wait(m, size)
            finished(m)

        base = 1 if whole else 2
        back = base + reach + dist + (1 if whole else 0)
        steps = [(back, jnp.logical_not(here), outward), (base + level, level > 0, inward)]
        if whole:
            steps.append((base + reach + 1, here, crossed))
        else:
            steps += [(back + 1, True, last_half), (2, True, add_x)]
        return steps, sent, add_y, set_off_early

    low_root = (count - 1) // 2
    high_root = min(low_root + 1, count - 1)
    def is_whole(m):
        return (lax.rem(m, 2) == 0) & (m >= WHOLE_LOW) & (m < WHOLE_HIGH)

    roots = (high_root, count - 1, low_root, 0)
    lines = [
        (lambda m, part=part: is_whole(m) & (lax.rem(m, 8) == part), *line_of(root, True))
        for part, root in zip((0, 2, 4, 6), roots)
    ] + [
        (lambda m: jnp.logical_not(is_whole(m)) & (m != LATE), *line_of(low_root, False)),
        (lambda m: m == LATE, *line_of(low_root, False, SMALL)),
    ]

    def finish(m):
        @pl.when((m >= EARLY) & (m != LATE))
        def _():
            core_copy(m, out.at[:, at(m), :]).wait_send()

            @pl.when(is_dec(m))
            def _():
                corey_copy(m, rcy.at[:, y_at(m), :]).wait_send()
                y_copy(m).wait_send()

        @pl.when(m == LATE)
        def _():
            core_copy(m, out.at[:, at(m, SMALL), :], SMALL).wait_send()
            corey_copy(m, rcy.at[:, y_at(m, SMALL), :], SMALL).wait_send()
            y_copy(m, SMALL).wait_send()

        for mine, _, sent, _, _ in lines:
            @pl.when(mine(m))
            def _(sent=sent):
                sent(m)

    def set_off_early(m):
        for mine, _, _, _, set_off in lines:
            @pl.when(mine(m))
            def _(set_off=set_off):
                set_off(m)

    loop(EARLY, set_off_early)
    far_reach = max(max(root, count - 1 - root) for root in roots)
    depth = (LAG + 1) * (3 + 2 * far_reach) + 1

    lag = LAG + lax.rem(lane, 2)

    def tick(n):
        @pl.when(n <= PIECES[-1])
        def _():
            run_pieces(n)

        for mine, steps, _, add_y, _ in lines:
            m = n - lag

            @pl.when((m >= EARLY) & (m < ALL_K))
            def _(m=m, mine=mine, add_y=add_y):
                @pl.when(mine(m))
                def _():
                    add_y(m)

            for offset, enabled, stage in steps:
                m = n - lag * offset

                @pl.when((m >= 0) & (m < ALL_K) & enabled)
                def _(m=m, mine=mine, stage=stage):
                    @pl.when(mine(m))
                    def _():
                        stage(m)

        @pl.when(n < ALL_K)
        def _():
            stage_c(n)

        @pl.when(n >= depth)
        def _():
            finish(n - depth)

    loop(ALL_K + depth, tick)

    for step in range(1, devices):
        dx_copy(step).wait()
    for step in range(1, LANES):
        emb_copy(step).wait()
    give_enc().wait_send()
    for k in range(D // 256):
        give_part(k, 0).wait_send()
        give_part(k, 1).wait_send()
        give_last(k).wait_send()


def backward_call(args, half, hid):
    dma = lambda *s: pltpu.SemaphoreType.DMA(s)
    vm = pltpu.VMEM
    full = ALL_K * CH
    y_half = DEC_ROWS - EARLY_ROWS + SMALL
    k = ALL_K
    rows = 2 * PAD
    cut = D // (2 * LANES)
    specs = [VM, VM] + [ANY] * 18 + [VM] * 3
    return pl.pallas_call(
        backward_and_sums,
        out_shape=[
            jax.ShapeDtypeStruct((2, full, D), BF16),
            jax.ShapeDtypeStruct((LANES, 2, CH, D), BF16),
            jax.ShapeDtypeStruct((2 * LANES, cut, VIS), BF16),
        ],
        in_specs=specs,
        out_specs=[VM] * 3,
        scratch_shapes=[
            vm((rows, D), BF16), vm((D, rows), BF16), vm((D, rows), BF16),
            vm((rows, D), F32), vm((rows, D), BF16), vm((rows, D), BF16),
            vm((2, rows, hid), BF16), vm((rows, D), BF16), vm((rows, D), F32),
            vm((rows, half), BF16), vm((2, 3, rows, half), BF16),
            vm((PAD, D), F32), vm((PAD, D), BF16), vm((PAD, D), BF16), vm((PAD, D), F32),
            vm((2 * LANES, cut, VIS), BF16),
            vm((2, 1, hid), F32), vm((2, 2, half), F32), vm((8, D), F32),
            vm((2, full, D), BF16), vm((2, y_half, D), BF16), vm((2, ENC_A + ENC_B, D), BF16),
            vm((2, y_half, D), BF16), vm((2, y_half, D), BF16),
            *[vm((2, full, D), BF16)] * 3,
            vm((LANES, 32, D), F32), vm((LANES, 2, SMALL, D), BF16),
            *[vm(v.shape, v.dtype) for v in args[2:19]],
            dma(17), dma(2), dma(10), dma(10),
            dma(k), dma(k), dma(k), dma(k), dma(k), dma(k),
            dma(k), dma(k), dma(k), dma(k), dma(k),
            dma(k), dma(k), dma(k), dma(k), dma(k), dma(LANES), dma(LANES),
            dma(2 * LANES), dma(2 * LANES),
        ],
        compiler_params=pltpu.CompilerParams(
            collective_id=1, has_side_effects=True, vmem_limit_bytes=VMEM_LIMIT
        ),
    )(*args)


def finish_grads(
    total, emb, decoded, dx, decoded_out, dx_out,
    e_qkv, e_qvb, e_proj, e_up, e_upb, e_down, e_gain, e_off,
    d_qkv, d_qvb, d_proj, d_up, d_upb, d_down, d_gain, d_off, d_ew, d_ev,
):
    half = e_proj.shape[0]
    decoded_out[...] = decoded[...]
    dx_out[...] = dx[...]
    e_up[...] = total[0, A_TOP:B_TOP, :].astype(F32)
    e_down[...] = jnp.transpose(total[1, A_TOP:B_TOP, :].astype(F32))
    e_qkv[0] = total[0, B_TOP : B_TOP + half, :].astype(F32)
    e_qkv[1] = total[0, B_TOP + half : S_TOP, :].astype(F32)
    e_qkv[2] = total[1, B_TOP : B_TOP + half, :].astype(F32)
    e_proj[...] = total[1, B_TOP + half : S_TOP, :].astype(F32)

    def tile(number):
        h, top, col = tile_of(number)
        return total[h, top : top + CH, col : col + 256].astype(F32)

    for block in range(GRID // CH):
        rows = slice(block * CH, (block + 1) * CH)
        side = slice(block // 2 * 128, (block // 2 + 1) * 128)
        for k in range(2):
            d_up[rows, k * 256 : (k + 1) * 256] = tile(4 * block + k)
            if block % 2:
                both = jnp.concatenate([tile(4 * block - 2 + k), tile(4 * block + 2 + k)], 0)
                d_down[k * 256 : (k + 1) * 256, side] = jnp.transpose(both)
        one, two = tile(32 + 2 * block), tile(33 + 2 * block)
        d_qkv[0, rows, :] = one[:, 0:128]
        d_qkv[1, rows, :] = one[:, 128:256]
        d_qkv[2, rows, :] = two[:, 0:128]
        d_proj[block % 2 * CH : (block % 2 + 1) * CH, side] = two[:, 128:256]
    for k in range(LANES):
        for h in range(2):
            top = k * 192 + h * 64
            d_ew[top : top + 64, :] = emb[k, h, :, 0:512].astype(F32)
            d_ew[k * 192 + 128 : (k + 1) * 192, h * 256 : (h + 1) * 256] = emb[
                k, h, :, 512:768
            ].astype(F32)
    little = total[0, S_TOP : S_TOP + SMALL, :].astype(F32)
    d_gain[...] = little[0:2, 0:512]
    d_off[...] = little[2:6, 0:512]
    d_ev[...] = little[6:8, 0:512]
    d_upb[...] = little[8, 0:512]
    d_qvb[0:1, :] = little[9:10, 0:128]
    d_qvb[1:2, :] = little[9:10, 128:256]
    e_upb[...] = little[10]
    e_qvb[0:1, :] = little[11:12, 0:192]
    e_qvb[1:2, :] = little[11:12, 256:448]
    little = total[1, S_TOP : S_TOP + SMALL, :].astype(F32)
    e_gain[...] = little[0:2]
    e_off[...] = little[2:6]


def call(kernel, specs, shapes, scratch, args):
    return pl.pallas_call(
        kernel,
        out_shape=[jax.ShapeDtypeStruct(s, d) for s, d in shapes],
        in_specs=specs,
        out_specs=[VM] * len(shapes),
        scratch_shapes=scratch,
        compiler_params=pltpu.CompilerParams(vmem_limit_bytes=VMEM_LIMIT),
    )(*args)


def position_rows():
    quarter = DD // 4
    freq = np.exp(np.arange(quarter, dtype=np.float32) * np.float32(-math.log(10000.0) / quarter))
    angle = np.arange(PAD, dtype=np.float32)[:, None] * freq[None, :].astype(np.float32)
    both = np.concatenate([np.sin(angle), np.cos(angle)], 1).astype(np.float32)
    high = both.astype(jnp.bfloat16)
    low = (both - high.astype(np.float32)).astype(jnp.bfloat16)
    return np.stack([high, low])


def per_device(
    patches, cotangent, widths, visible, window_shift, batch_order,
    encoder_qkv, encoder_qvbias, encoder_proj, encoder_up, encoder_upbias, encoder_down,
    encoder_gains, encoder_offsets,
    decoder_qkv, decoder_qvbias, decoder_proj, decoder_up, decoder_upbias, decoder_down,
    decoder_gains, decoder_offsets, embed_weight, embed_vectors,
):
    qkv0 = encoder_qkv.transpose(1, 2, 0)
    half = qkv0.shape[1]
    hid = encoder_up.shape[1]
    dff = decoder_up.shape[1] * LANES
    flat = patches.transpose(1, 0, 2).reshape(-1, D)
    (
        x, x1, a, u, y, gp, qkv, p, o, qkv1, proj1, up1, down1, dec_buf,
        d_enc, d_dqvb, d_dupb, d_dsmall, out_all,
    ) = forward_call(
        (
            widths, window_shift.T, batch_order, visible, flat, encoder_gains, encoder_offsets,
            encoder_qvbias, encoder_upbias, decoder_qvbias, decoder_upbias,
            qkv0, encoder_proj, encoder_up, encoder_down,
            decoder_qkv.transpose(1, 0, 2), decoder_proj, decoder_up, decoder_down,
            cotangent, embed_weight, embed_vectors, jnp.asarray(position_rows()),
            decoder_gains, decoder_offsets,
        ),
        half, hid, dff,
    )
    total, emb, dx_all = backward_call(
        (
            d_enc, encoder_gains, u, y, gp, encoder_down, down1, encoder_up, up1,
            x, x1, a, qkv, p, o, qkv0, qkv1, encoder_proj, proj1,
            dec_buf, d_dqvb, d_dupb, d_dsmall,
        ),
        half, hid,
    )
    f = lambda *shape: (shape, F32)
    out_all, dx_all, *grads = call(
        finish_grads, [VM] * 4,
        [
            (out_all.shape, BF16), (dx_all.shape, BF16), f(3, half, D), f(2, half), f(half, D), f(D, hid), f(hid), f(hid, D), f(2, D), f(4, D),
            f(3, DD, 128), f(2, 128), f(128, DD), f(DD, 512), f(512), f(512, DD), f(2, DD), f(4, DD),
            f(D, DD), f(2, DD),
        ],
        [], (total, emb, out_all, dx_all),
    )
    grads[0] = grads[0].transpose(2, 0, 1)
    grads[8] = grads[8].transpose(1, 0, 2)
    return (out_all.swapaxes(1, 2), dx_all.swapaxes(1, 2), *grads)


def solution(mesh):
    weights = (
        P(None, None, "tensor"), P(None, "tensor"), P("tensor", None), P(None, "tensor"),
        P("tensor"), P("tensor", None), P(), P(),
    )
    split = P("dp", None, ("section", "tensor"))
    return jax.shard_map(
        per_device,
        mesh=mesh,
        in_specs=(
            P("dp", None, None), P("dp", None, None), P("dp"), P("dp", None), P("dp", None),
            P("dp", None),
        ) + weights + weights + (P(), P()),
        out_specs=(split, split) + weights + weights + (P(), P()),
        check_vma=False,
    )
```

```python
import math

import jax
import jax.numpy as jnp
import numpy as np
from jax import lax
from jax.experimental import pallas as pl
from jax.experimental.pallas import tpu as pltpu
from jax.sharding import PartitionSpec as P

D = 768
HEADS = 12
DD = 512
DHEADS = 16
GRID_ROWS = 64
WIDE = 8
WIN = 4
VIS = 102
CM = 4
GRID = 512
LANES = 4
PAD = 128
EPS = 1e-06
NEG = -10000.0
F32 = jnp.float32
BF16 = jnp.bfloat16
VMEM_LIMIT = 60 * 1024 * 1024

VM = pl.BlockSpec(memory_space=pltpu.VMEM)
SM = pl.BlockSpec(memory_space=pltpu.SMEM)
ANY = pl.BlockSpec(memory_space=pl.ANY)


def nn(a, b):
    return lax.dot_general(a, b, (((1,), (0,)), ((), ())), preferred_element_type=F32)


def nt(a, b):
    return lax.dot_general(a, b, (((1,), (1,)), ((), ())), preferred_element_type=F32)


def tn(a, b):
    return lax.dot_general(a, b, (((0,), (0,)), ((), ())), preferred_element_type=F32)


def loop(count, body, unroll=1):
    def step(i, carry):
        body(i)
        return carry

    lax.fori_loop(0, count, step, 0, unroll=unroll)


def span(i, size):
    return pl.ds(pl.multiple_of(i * size, size), size)


def normal(x):
    center = x - jnp.mean(x, -1, keepdims=True)
    scale = lax.rsqrt(jnp.mean(center * center, -1, keepdims=True) + EPS)
    return center * scale, scale


def normal_back(dy, hat, scale, gain):
    d = dy * gain
    return scale * (
        d - jnp.mean(d, -1, keepdims=True) - hat * jnp.mean(d * hat, -1, keepdims=True)
    )


def gelu_both(h):
    phi = 0.5 * lax.erf(h * math.sqrt(0.5)) + 0.5
    bell = jnp.exp2(h * h * (-0.5 * math.log2(math.e)))
    return h * phi, phi + h * bell * (1.0 / math.sqrt(2.0 * math.pi))


def colsum(x):
    return jnp.sum(x, 0, keepdims=True)


def head_marks(width, size, dtype):
    lane = lax.broadcasted_iota(jnp.int32, (1, width), 1)
    return [((lane >= h * size) & (lane < (h + 1) * size)).astype(dtype) for h in range(width // size)]


def stacked(x, marks):
    return jnp.concatenate([x * m for m in marks], 0)


LOG2E = math.log2(math.e)


def attend(q, k, v, marks, ones, masked, scale):
    keys = k.shape[0]
    s = nt(q, stacked(k, marks))
    parts = []
    for h in range(len(marks)):
        x = masked(s[:, h * keys : (h + 1) * keys] * (scale * LOG2E))
        parts.append(jnp.exp2(x - jnp.max(x, -1, keepdims=True)).astype(BF16))
    e = jnp.concatenate(parts, 1)
    width = q.shape[1]
    if width % 128:
        top, total = nn(e, stacked(v, marks)), nn(e, ones)
    else:
        both = nn(e, jnp.concatenate([stacked(v, marks), ones], 1))
        top, total = both[:, :width], both[:, width:]
    inverse = 1.0 / total
    return e, (top * inverse).astype(BF16), inverse


def attend_back(q, k, v, e, o, inverse, d_out, marks, marks32, rows32, ones, scale):
    keys = k.shape[0]
    width = q.shape[1]
    d_one = d_out.astype(F32) * inverse
    d_two = (d_one * o.astype(F32)).astype(BF16)
    d_one = d_one.astype(BF16)
    if width % 128:
        d_s = nt(d_one, stacked(v, marks)) - nt(d_two, ones)
    else:
        d_s = nt(
            jnp.concatenate([d_one, d_two], 1), jnp.concatenate([stacked(v, marks), -ones], 1)
        )
    dr = (e.astype(F32) * d_s * scale).astype(BF16)
    d_q = nn(dr, stacked(k, marks)).astype(BF16)
    if width % 128:
        d_k_all, d_v_all = tn(dr, q), tn(e, d_one)
        d_k = d_v = 0.0
        for h in range(len(marks)):
            cut = slice(h * keys, (h + 1) * keys)
            d_k += d_k_all[cut] * marks32[h]
            d_v += d_v_all[cut] * marks32[h]
        return d_q, d_k.astype(BF16), d_v.astype(BF16)
    d_k_all = nn(jnp.transpose(q), dr)
    d_v_all = nn(jnp.transpose(d_one), e)
    d_k = d_v = 0.0
    for h in range(len(marks)):
        cut = slice(h * keys, (h + 1) * keys)
        d_k += d_k_all[:, cut] * rows32[h]
        d_v += d_v_all[:, cut] * rows32[h]
    return d_q, jnp.transpose(d_k.astype(BF16)), jnp.transpose(d_v.astype(BF16))


def ones_per_head(keys, marks):
    return jnp.concatenate([jnp.broadcast_to(m, (keys, m.shape[1])) for m in marks], 0)


ENC_SIZE = D // HEADS
ENC_SCALE = ENC_SIZE ** -0.5
DEC_SIZE = DD // DHEADS
DEC_SCALE = DEC_SIZE ** -0.5


CH = 64
DEC_ROWS = 576
ENC_A = 768
ENC_B = 384
DEC_K = DEC_ROWS // CH
B_K = (DEC_ROWS + ENC_A + ENC_B) // CH
ALL_K = B_K + 1
A_TOP = DEC_ROWS
B_TOP = DEC_ROWS + ENC_A
S_TOP = B_TOP + ENC_B
EARLY = 4
XFIRST = True
EARLY_ROWS = EARLY * CH
LAG = 2
ORDER = (0, 1, 2, 3, 9, 10, 11, 12, 13, 14, 15, 16, 17, 4, 18, 5, 19, 20, 6, 8, 21, 22, 23, 24, 27, 25, 26, 7)
PIECES = (2, 2, 3, 3, 3, 3, 3, 3, 3, 3, 3, 10, 10, 11, 12, 12, 13, 15, 15, 16, 16, 18, 20)
LATE = ORDER.index(B_K)
WHOLE_LOW = 6
WHOLE_HIGH = 22
SMALL = 16


def tile_of(number):
    place = number // 3
    return place % 2, place // 2 * CH, number % 3 * 256


MESH = pl.DeviceIdType.MESH


def far(src, dst, send, recv, peer):
    return pltpu.make_async_remote_copy(
        src_ref=src, dst_ref=dst, send_sem=send, recv_sem=recv, device_id=peer, device_id_type=MESH
    )


def forward_and_decoder(
    wid, shifts, order, vis, pat, gains, offs, b_qv, b_up, b_dqv, b_dup,
    h_qkv, h_proj, h_up, h_down, h_dqkv, h_dproj, h_dup, h_ddown,
    cot_hbm, ew, evec, table, dgains, doffs,
    o_x, o_x1, o_a, o_u, o_y, o_gp, o_qkv, o_p, o_o, o_w, o_wproj, o_wup, o_wdown, o_dec,
    d_enc, d_qvb, d_upb, d_small, dec_out,
    w_qkv, w_proj, w_up, w_down, bias, biases, qkv, proj, up, down,
    ex, ea, eu, ey, egp, eqkv, ep, eo, ex1, epart, esend, erecv, esend2, erecv2, eown,
    cot, x0, x1, a, acts, probs, o, inverse, u, ut, y, gp, g32, gb, gt, acc, e_ref, hot, perm, buf, dsend, e_rc, e_rcy, e_rx, e_ry,
    load_s, out_s, cot_s, w_s, w_r, bias_s, bias_r, dw_s, dw_r, ex_s, ex_r, ex2_s, ex2_r, do_s, do_r, e_s, e_r,
):
    sec = lax.axis_index("section")
    lane = lax.axis_index("tensor")
    mate = lane + 1 - 2 * lax.rem(lane, 2)
    over = lax.rem(lane + 2, LANES)
    cross = lax.rem(mate + 2, LANES)
    me = sec * LANES + lane
    devices = 2 * LANES
    clip = me
    clips = (me, sec * LANES + over)

    def group_peer(step):
        peer = lax.rem(me + step, devices)
        return peer, {"section": lax.div(peer, LANES), "tensor": lax.rem(peer, LANES)}

    own = [
        pltpu.make_async_copy(src, dst.at[0], load_s.at[n])
        for n, (src, dst) in enumerate(
            ((h_qkv, w_qkv), (h_proj, w_proj), (h_up, w_up), (h_down, w_down))
        )
    ]

    def place(n, shard, part=None):
        thick = (128, 128, 512, 512)[n]
        base = shard * thick
        cut = pl.ds(pl.multiple_of(base, thick), thick)
        if part is None:
            return (qkv.at[:, :, cut], proj.at[cut, :], up.at[:, cut], down.at[cut, :])[n]
        some = span(part, (256, 64, 256, 256)[n])
        if n == 0:
            return qkv.at[:, some, cut]
        if n == 2:
            return up.at[some, cut]
        few = thick // 2
        rows = pl.ds(pl.multiple_of(base + part * few, few), few)
        return (proj if n == 1 else down).at[rows, :]

    shards = (h_dqkv, h_dproj, h_dup, h_ddown)
    keep = [
        pltpu.make_async_copy(shards[n], place(n, lane), load_s.at[4 + n]) for n in range(4)
    ]
    for copy in own + keep:
        copy.start()
    fetch = pltpu.make_async_copy(cot_hbm.at[clip], cot, cot_s)
    fetch.start()

    barrier = pltpu.get_barrier_semaphore()
    for step in range(1, devices):
        pl.semaphore_signal(barrier, inc=1, device_id_type=MESH, device_id=group_peer(step)[1])
    bias[...] = jnp.zeros_like(bias)
    half = w_proj.shape[1]
    bias[0:1, :] = b_up[...].astype(F32).reshape(1, -1)
    bias[1:3, 0:half] = b_qv[...].astype(F32)
    bias[3:4, 0:512] = b_dup[...].astype(F32).reshape(1, -1)
    bias[4:6, 0:128] = b_dqv[...].astype(F32)
    biases[lane] = bias[...]
    stride = pat.shape[0] // VIS
    for c in range(2):
        row = lax.broadcasted_iota(jnp.int32, (PAD, pat.shape[0]), 0)
        col = lax.broadcasted_iota(jnp.int32, (PAD, pat.shape[0]), 1)
        pick = (col == row * stride + clips[c]).astype(F32).astype(BF16)
        ex[c * PAD : (c + 1) * PAD, :] = nn(pick, pat[...])

    pl.semaphore_wait(barrier, devices - 1)

    def enc_weight(n):
        src = (h_qkv, h_proj, h_up, h_down)[n]
        dst = (w_qkv, w_proj, w_up, w_down)[n]
        return far(src, dst.at[1], w_s.at[n], w_r.at[n], {"tensor": mate})

    def bias_copy(step):
        return far(
            bias, biases.at[lane], bias_s.at[step], bias_r.at[step],
            {"tensor": lax.rem(lane + step, LANES)},
        )

    def half_of(n):
        some = span(sec, (256, 64, 256, 256)[n])
        return shards[n].at[:, some, :] if n == 0 else shards[n].at[some, :]

    def dec_weight(n, kind):
        peer = {"section": 1 - sec} if kind == 2 else {"tensor": over if kind == 0 else mate}
        if kind == 0:
            src, dst = half_of(n), place(n, lane, sec)
        elif kind == 1:
            src, dst = shards[n], place(n, lane)
        else:
            src = dst = place(n, over, 1 - sec if kind == 4 else sec)
        return far(src, dst, dw_s.at[5 * n + kind], dw_r.at[5 * n + kind], peer)

    enc_weight(0).start()
    for step in range(1, LANES):
        bias_copy(step).start()
    enc_weight(1).start()
    dec_weight(0, 0).start()
    enc_weight(2).start()
    enc_weight(3).start()
    for n in range(4):
        dec_weight(n, 1).start()

    def pass_on(n):
        dec_weight(n, 0).wait_recv()
        dec_weight(n, 2).start()
        dec_weight(n, 3).start()

    def pass_last(n):
        dec_weight(n, 2).wait_recv()
        dec_weight(n, 4).start()

    def arrived(n):
        keep[n].wait()
        dec_weight(n, 1).wait_recv()
        dec_weight(n, 3).wait_recv()
        dec_weight(n, 4).wait_recv()

    width = wid[clip]
    bits = jnp.where(width == WIDE, 3, 2)
    turn = shifts[0, clip] * width
    mod = GRID - 1
    spot = 0
    for i in range(order.shape[1]):
        spot = spot + jnp.where(order[0, i] == clip, i, 0)
    batch = spot // CM
    count = 0
    for i in range(order.shape[1]):
        count = count + jnp.where(batch == i // CM, wid[order[0, i]], 0)
    factor_rows = CM * GRID / (jnp.full((1, 1), count, jnp.int32) * GRID_ROWS).astype(F32)

    def slot_of(index):
        return (index - turn) & mod

    def code_of(slot):
        band = ((slot >> bits) + shifts[0, clip]) >> 2
        strip = ((slot & (width - 1)) + shifts[1, clip]) >> 2
        return band * 4 + strip

    def valid_rows():
        slot = slot_of(lax.broadcasted_iota(jnp.int32, (GRID, 1), 0))
        return (slot < GRID_ROWS * width).astype(F32)

    def clip_gradient():
        fetch.wait()
        rolled = slot_of(lax.broadcasted_iota(jnp.int32, (GRID, GRID), 0))
        column = lax.broadcasted_iota(jnp.int32, (GRID, GRID), 1)
        perm[...] = (rolled == column).astype(F32).astype(BF16)
        g = nn(perm[...], cot[...]) * valid_rows() * factor_rows
        g32[...] = g
        gb[...] = g.astype(BF16)
        gt[...] = jnp.transpose(g.astype(BF16))
        d_small[...] = jnp.zeros_like(d_small)
        d_small[5:6, :] = colsum(g)

    seen = vis[pl.ds(clip, 1), :]
    target = jnp.concatenate([(seen + turn) & mod, jnp.full((1, PAD - VIS), -1, jnp.int32)], 1)

    def places(i):
        r = span(i, PAD)
        index = lax.broadcasted_iota(jnp.int32, (PAD, PAD), 0) + i * PAD
        column = lax.broadcasted_iota(jnp.int32, (PAD, PAD), 1)
        hot[r, :] = (index == target).astype(F32).astype(BF16)
        slot = slot_of(index)
        by_row = ((slot >> bits) == column).astype(F32).astype(BF16)
        by_col = ((slot & (width - 1)) == column).astype(F32).astype(BF16)
        row_part = nn(by_row, table[0]) + nn(by_row, table[1])
        col_part = nn(by_col, table[0]) + nn(by_col, table[1])
        x0[r, :] = jnp.concatenate([row_part, col_part], 1)

    egain = gains[...].astype(F32)
    eoff = offs[...].astype(F32)
    emarks = head_marks(half, ENC_SIZE, BF16)
    key = lax.broadcasted_iota(jnp.int32, (PAD, PAD), 1)
    floor = jnp.where(key < VIS, NEG * LOG2E, -1e30)
    eones = ones_per_head(PAD, emarks)
    blocks = D // 256

    def give_part(i, side):
        cut = span(i, 256)
        return far(
            esend.at[(1 - side) * PAD : (2 - side) * PAD, cut],
            erecv.at[side * PAD : (side + 1) * PAD, cut],
            ex_s.at[2 * i + side], ex_r.at[2 * i + side], {"tensor": over},
        )

    for c in range(2):
        rows = slice(c * PAD, (c + 1) * PAD)
        hat, _ = normal(ex[rows, :])
        ea[rows, :] = (hat * egain[0:1] + eoff[0:1]).astype(BF16)
        limit = (VIS * wid[clips[c]]) // WIDE
        for g, shard in enumerate((lane, mate)):
            if c == 0 and g == 0:
                own[0].wait()
            if c == 0 and g == 1:
                enc_weight(0).wait_recv()
                for step in range(1, LANES):
                    bias_copy(step).wait_recv()
            if g == 0:
                bq, bv = bias[1:2, 0:half], bias[2:3, 0:half]
            else:
                bq, bv = biases[shard, 1:2, 0:half], biases[shard, 2:3, 0:half]
            eqkv[g, 0, rows] = (nt(ea[rows, :], w_qkv[g, 0]) + bq).astype(BF16)
            eqkv[g, 1, rows] = nt(ea[rows, :], w_qkv[g, 1]).astype(BF16)
            eqkv[g, 2, rows] = (nt(ea[rows, :], w_qkv[g, 2]) + bv).astype(BF16)
            p, out, _ = attend(
                eqkv[g, 0, rows], eqkv[g, 1, rows], eqkv[g, 2, rows], emarks, eones,
                lambda s: jnp.where(key < limit, s, floor), ENC_SCALE,
            )
            ep[g, c] = p
            eo[g, rows] = out
        if c == 0:
            own[1].wait()
            enc_weight(1).wait_recv()
        for i in range(blocks):
            cut = slice(i * 256, (i + 1) * 256)
            t = nn(eo[0, rows], w_proj[0, :, cut]) + nn(eo[1, rows], w_proj[1, :, cut])
            epart[rows, cut] = t
            esend[rows, cut] = t.astype(BF16)
            give_part(i, 1 - c).start()
    pass_on(0)
    clip_gradient()
    own[2].wait()
    enc_weight(2).wait_recv()

    def give_last(i):
        cut = span(i, 256)
        return far(
            esend2.at[:, cut], erecv2.at[:, cut], ex2_s.at[i], ex2_r.at[i], {"tensor": over}
        )

    for c in (1, 0):
        rows = slice(c * PAD, (c + 1) * PAD)
        for i in range(blocks):
            give_part(i, c).wait_recv()
        t = ex[rows, :] + epart[rows, :] + erecv[rows, :].astype(F32) + eoff[2:3]
        ex1[rows, :] = t
        hat, _ = normal(t)
        eu[rows, :] = (hat * egain[1:2] + eoff[1:2]).astype(BF16)
        for g, shard in enumerate((lane, mate)):

            def enc_ff(i, g=g, shard=shard, rows=rows):
                cut = span(i, 256)
                h = nn(eu[rows, :], w_up[g, :, cut]) + biases[shard, 0:1, cut]
                act, slope = gelu_both(h)
                ey[g, rows, cut] = act.astype(BF16)
                egp[g, rows, cut] = slope.astype(BF16)

            loop(w_up.shape[2] // 256, enc_ff, unroll=3)
        if c == 1:
            own[3].wait()
            enc_weight(3).wait_recv()
        for i in range(blocks):
            cut = slice(i * 256, (i + 1) * 256)
            t = nn(ey[0, rows], w_down[0, :, cut]) + nn(ey[1, rows], w_down[1, :, cut])
            if c == 0:
                eown[:, cut] = t
            else:
                esend2[:, cut] = t.astype(BF16)
                give_last(i).start()
        if c == 1:
            for n in (1, 2, 3):
                dec_weight(n, 0).start()
            pass_last(0)
    outs = [
        pltpu.make_async_copy(src, dst, out_s.at[n])
        for n, (src, dst) in enumerate(
            (
                (ex.at[0:PAD, :], o_x), (ex1, o_x1), (ea, o_a), (eu, o_u), (ey, o_y), (egp, o_gp),
                (eqkv, o_qkv), (ep, o_p), (eo, o_o), (w_qkv.at[1], o_w), (w_proj.at[1], o_wproj),
                (w_up.at[1], o_wup), (w_down.at[1], o_wdown),
            )
        )
    ]
    for copy in outs:
        copy.start()
    loop(GRID // PAD, places, unroll=2)
    for i in range(blocks):
        give_last(i).wait_recv()

    e_ref[...] = (ex1[0:PAD, :] + eown[...] + erecv2[...].astype(F32) + eoff[3:4]).astype(BF16)
    vec = evec[...].astype(F32)
    m = (nn(e_ref[...], ew[...]) + vec[0:1]).astype(BF16)
    gain = dgains[...].astype(F32)
    offsets = doffs[...].astype(F32)

    def start(i):
        r = span(i, PAD)
        oh = hot[r, :]
        hit = jnp.sum(oh.astype(F32), -1, keepdims=True)
        x = jnp.where(hit > 0, nn(oh, m), vec[1:2]).astype(BF16).astype(F32) + x0[r, :]
        x0[r, :] = x
        hat, _ = normal(x)
        a[r, :] = (hat * gain[0:1] + offsets[0:1]).astype(BF16)

    loop(GRID // PAD, start, unroll=2)
    arrived(0)

    def dec_bias(row, size):
        return jnp.concatenate([biases[k, row : row + 1, 0:size] for k in range(LANES)], 1)

    acts[0] = (nn(a[...], qkv[0]) + dec_bias(4, 128)).astype(BF16)
    acts[1] = nn(a[...], qkv[1]).astype(BF16)
    acts[2] = (nn(a[...], qkv[2]) + dec_bias(5, 128)).astype(BF16)
    pass_on(1)
    pass_on(2)
    marks = head_marks(128, DEC_SIZE, BF16)
    marks32 = head_marks(128, DEC_SIZE, F32)
    dim = lax.broadcasted_iota(jnp.int32, (128, 1), 0)
    rows32 = [
        ((dim >= h * DEC_SIZE) & (dim < (h + 1) * DEC_SIZE)).astype(F32) for h in range(len(marks))
    ]

    ones = ones_per_head(PAD, marks)

    def attention(i):
        r = span(i, PAD)
        row_slot = slot_of(lax.broadcasted_iota(jnp.int32, (PAD, PAD), 0) + i * PAD)
        key_slot = slot_of(lax.broadcasted_iota(jnp.int32, (PAD, PAD), 1) + i * PAD)
        allowed = (code_of(row_slot) == code_of(key_slot)) & (key_slot < GRID_ROWS * width)
        for g in range(DD // 128):
            c = slice(g * 128, (g + 1) * 128)
            probs[i, :, g * 512 : (g + 1) * 512], o[r, c], inverse[r, c] = attend(
                acts[0, r, c], acts[1, r, c], acts[2, r, c], marks, ones,
                lambda s: jnp.where(allowed, s, NEG * LOG2E), DEC_SCALE,
            )

    loop(GRID // PAD, attention, unroll=2)
    pass_last(1)
    pass_last(2)
    pass_on(3)
    arrived(1)

    def mix(i):
        r = span(i, 256)
        x = x0[r, :] + nn(o[r, :], proj[...]) + offsets[2:3]
        x1[r, :] = x
        hat, _ = normal(x)
        un = hat * gain[1:2] + offsets[1:2]
        u[r, :] = un.astype(BF16)
        ut[:, r] = jnp.transpose(un.astype(BF16))

    loop(2, mix)
    pass_last(3)
    arrived(2)

    def ff(i):
        c = span(i, 256)
        h = nn(u[...], up[:, c]) + biases[lax.div(i, 2), 3:4, span(lax.rem(i, 2), 256)]
        act, slope = gelu_both(h)
        y[:, c] = act.astype(BF16)
        gp[:, c] = slope.astype(BF16)

    loop(up.shape[1] // 256, ff, unroll=2)
    arrived(3)
    def out(i):
        c = span(i, 256)
        acc[:, c] = nn(y[...], down[:, c])

    loop(2, out)
    full = ((acc[...] + x1[...] + offsets[3:4]) * valid_rows()).astype(BF16)
    turned = tn(full, perm[...]).astype(BF16)
    for k in range(devices):
        dsend[k] = turned[k * dsend.shape[1] : (k + 1) * dsend.shape[1]]

    def decoded_copy(step):
        peer, spot = group_peer(step)
        return far(dsend.at[peer], dec_out.at[me], do_s.at[step], do_r.at[step], spot)

    for step in range(1, devices):
        decoded_copy(step).start()
    dec_out[me] = dsend[me]

    def ff_back(shard):
        for side in range(2):
            c = span(2 * shard + side, 256)
            d_down = nn(gt[...], y[:, c]).astype(BF16)
            dh = nt(gb[...], down[c, :]) * gp[:, c].astype(F32)
            d_upb[:, c] = colsum(dh)
            du = dh.astype(BF16)
            gp[:, c] = du
            d_up = nn(ut[...], du).astype(BF16)
            for block in range(GRID // CH):
                rows = slice(block * CH, (block + 1) * CH)
                h, top, col = tile_of(4 * block + side)
                buf[shard, h, top : top + CH, col : col + 256] = d_up[rows]
                h, top, col = tile_of(4 * block + 2 + side)
                buf[shard, h, top : top + CH, col : col + 256] = d_down[rows]

    def early_core(which):
        shard, land = ((mate, e_rc), (cross, e_rcy))[which]
        return far(
            buf.at[shard, :, 0:EARLY_ROWS, :], land, e_s.at[which], e_r.at[which], {"tensor": mate}
        )

    def early_x(which):
        return far(
            buf.at[(over, lane)[which], 1 - sec, 0:EARLY_ROWS, :], e_rx.at[which],
            e_s.at[2 + which], e_r.at[2 + which], {"section": 1 - sec},
        )

    def early_y():
        return far(
            buf.at[over, sec, 0:EARLY_ROWS, :], e_ry, e_s.at[4], e_r.at[4], {"tensor": over}
        )

    def early_add(shard, land):
        def body(i):
            r = span(i, CH)
            buf[shard, :, r, :] = buf[shard, :, r, :] + land[:, r, :]

        loop(EARLY_ROWS // CH, body)

    def early_half(shard, land):
        buf[shard, sec, 0:EARLY_ROWS, :] = buf[shard, sec, 0:EARLY_ROWS, :] + land

    def ff_step(i):
        ff_back(jnp.where(i == 0, cross, jnp.where(i == 1, over, jnp.where(i == 2, mate, lane))))

        @pl.when(i == 1)
        def _():
            early_core(1).start()

        @pl.when(i == 2)
        def _():
            early_core(0).start()

    loop(LANES, ff_step)
    early_core(1).wait_recv()
    early_add(over, e_rcy)
    early_x(0).start()

    def ff_in(i):
        c = span(i, 256)
        acc[:, c] = nt(gp[...], up[c, :])

    loop(2, ff_in)
    early_core(0).wait_recv()
    early_add(lane, e_rc)
    early_x(1).start()

    def mix_back(i):
        r = span(i, 256)
        hat, scale = normal(x1[r, :])
        da = acc[r, :]
        dx = g32[r, :] + normal_back(da, hat, scale, gain[1:2])
        d_small[1:2, :] += colsum(da * hat)
        d_small[3:4, :] += colsum(da)
        d_small[4:5, :] += colsum(dx)
        g32[r, :] = dx
        dxb = dx.astype(BF16)
        gb[r, :] = dxb
        u[r, :] = nt(dxb, proj[...]).astype(BF16)

    loop(2, mix_back)
    d_proj = tn(o[...], gb[...]).astype(BF16)
    for block in range(GRID // CH):
        h, top, col = tile_of(33 + 2 * block)
        side = slice(block // 2 * 128, (block // 2 + 1) * 128)
        for k in range(LANES):
            row = k * 128 + block % 2 * CH
            buf[k, h, top : top + CH, col + 128 : col + 256] = d_proj[row : row + CH, side]

    def attention_back(i):
        r = span(i, PAD)
        for k in range(DD // 128):
            c = slice(k * 128, (k + 1) * 128)
            acts[0, r, c], acts[1, r, c], acts[2, r, c] = attend_back(
                acts[0, r, c], acts[1, r, c], acts[2, r, c],
                probs[i, :, k * 512 : (k + 1) * 512], o[r, c], inverse[r, c], u[r, c],
                marks, marks32, rows32, ones, DEC_SCALE,
            )

    loop(GRID // PAD, attention_back, unroll=2)
    early_x(0).wait_recv()
    early_half(over, e_rx[0])
    early_y().start()
    d_qvb[0:1, :] = colsum(acts[0].astype(F32))
    d_qvb[1:2, :] = colsum(acts[2].astype(F32))

    def project_back(i):
        c = span(i, 256)
        acc[:, c] = (
            nt(acts[0], qkv[0, c, :]) + nt(acts[1], qkv[1, c, :]) + nt(acts[2], qkv[2, c, :])
        )

    loop(2, project_back)
    gt[...] = jnp.transpose(a[...])
    for j in range(3):
        d_qkv = nn(gt[...], acts[j]).astype(BF16)
        for block in range(GRID // CH):
            h, top, col = tile_of(32 + 2 * block + j // 2)
            col = col + j % 2 * 128
            rows = slice(block * CH, (block + 1) * CH)
            for k in range(LANES):
                buf[k, h, top : top + CH, col : col + 128] = d_qkv[rows, k * 128 : (k + 1) * 128]

    def start_back(i):
        r = span(i, PAD)
        hat, scale = normal(x0[r, :])
        da = acc[r, :]
        dx = g32[r, :] + normal_back(da, hat, scale, gain[0:1])
        d_small[0:1, :] += colsum(da * hat)
        d_small[2:3, :] += colsum(da)
        dg = dx.astype(BF16)
        gb[r, :] = dg
        hit = jnp.sum(hot[r, :].astype(F32), -1, keepdims=True)
        d_small[7:8, :] += colsum(jnp.where(hit > 0, 0.0, dg.astype(F32)))

    loop(GRID // PAD, start_back, unroll=2)
    dm = tn(hot[...], gb[...])
    d_small[6:7, :] = colsum(dm)
    dmb = dm.astype(BF16)
    d_enc[...] = nt(dmb, ew[...]).astype(BF16)
    d_ew = tn(e_ref[...], dmb).astype(BF16)
    for k in range(LANES):
        for h in range(2):
            top = k * 192 + h * 64
            buf[k, h, 512:576, 0:512] = d_ew[top : top + 64]
            buf[k, h, 512:576, 512:768] = d_ew[k * 192 + 128 : (k + 1) * 192, h * 256 : (h + 1) * 256]

    early_x(1).wait_recv()
    early_half(lane, e_rx[1])
    early_y().wait_recv()
    early_half(lane, e_ry[...])
    later = pl.ds(EARLY_ROWS, DEC_ROWS - EARLY_ROWS)
    rest = [pltpu.make_async_copy(buf.at[lane], o_dec.at[lane], out_s.at[13])] + [
        pltpu.make_async_copy(buf.at[k, :, later, :], o_dec.at[k, :, later, :], out_s.at[14 + n])
        for n, k in enumerate((mate, over, cross))
    ]
    for copy in rest:
        copy.start()
    for copy in outs + rest:
        copy.wait()
    for which in range(2):
        early_core(which).wait_send()
        early_x(which).wait_send()
    early_y().wait_send()
    for n in range(4):
        enc_weight(n).wait_send()
        for kind in range(5):
            dec_weight(n, kind).wait_send()
    for step in range(1, LANES):
        bias_copy(step).wait_send()
    for i in range(blocks):
        give_part(i, 0).wait_send()
        give_part(i, 1).wait_send()
        give_last(i).wait_send()
    for step in range(1, devices):
        decoded_copy(step).wait()


def forward_call(args, half, hid, dff):
    dma = lambda *s: pltpu.SemaphoreType.DMA(s)
    vm = lambda dtype, *shape: pltpu.VMEM(shape, dtype)
    rows = 2 * PAD
    keys = PAD * half // ENC_SIZE
    devices = 2 * LANES
    slab = DD // devices
    kept = [
        ((PAD, D), F32), ((rows, D), F32), ((rows, D), BF16), ((rows, D), BF16),
        ((2, rows, hid), BF16), ((2, rows, hid), BF16), ((2, 3, rows, half), BF16),
        ((2, 2, PAD, keys), BF16), ((2, rows, half), BF16),
        ((3, half, D), BF16), ((half, D), BF16), ((D, hid), BF16), ((hid, D), BF16),
        ((LANES, 2, DEC_ROWS, D), BF16),
    ]
    made = [
        ((PAD, D), BF16), ((2, DD), F32), ((1, dff), F32), ((8, DD), F32),
        ((devices, slab, GRID), BF16),
    ]
    return pl.pallas_call(
        forward_and_decoder,
        out_shape=[jax.ShapeDtypeStruct(s, d) for s, d in kept + made],
        in_specs=[SM, SM, SM] + [VM] * 8 + [ANY] * 9 + [VM] * 5,
        out_specs=[ANY] * len(kept) + [VM] * len(made),
        scratch_shapes=[
            vm(BF16, 2, 3, half, D), vm(BF16, 2, half, D), vm(BF16, 2, D, hid), vm(BF16, 2, hid, D),
            vm(F32, 8, D), vm(F32, LANES, 8, D),
            vm(BF16, 3, DD, DD), vm(BF16, DD, DD), vm(BF16, DD, dff), vm(BF16, dff, DD),
            vm(F32, rows, D), vm(BF16, rows, D), vm(BF16, rows, D), vm(BF16, 2, rows, hid),
            vm(BF16, 2, rows, hid), vm(BF16, 2, 3, rows, half), vm(BF16, 2, 2, PAD, keys),
            vm(BF16, 2, rows, half), vm(F32, rows, D), vm(F32, rows, D), vm(BF16, rows, D),
            vm(BF16, rows, D), vm(BF16, PAD, D), vm(BF16, PAD, D), vm(F32, PAD, D),
            vm(BF16, GRID, DD), vm(F32, GRID, DD), vm(F32, GRID, DD), vm(BF16, GRID, DD),
            vm(BF16, 3, GRID, DD), vm(BF16, GRID // PAD, PAD, DHEADS * PAD), vm(BF16, GRID, DD),
            vm(F32, GRID, DD),
            vm(BF16, GRID, DD), vm(BF16, DD, GRID), vm(BF16, GRID, dff), vm(BF16, GRID, dff),
            vm(F32, GRID, DD), vm(BF16, GRID, DD), vm(BF16, DD, GRID), vm(F32, GRID, DD),
            vm(BF16, PAD, D), vm(BF16, GRID, PAD), vm(BF16, GRID, GRID),
            vm(BF16, LANES, 2, DEC_ROWS, D),
            vm(BF16, devices, slab, GRID), *[vm(BF16, 2, EARLY_ROWS, D)] * 3, vm(BF16, EARLY_ROWS, D),
            dma(8), dma(17), pltpu.SemaphoreType.DMA, dma(4), dma(4), dma(LANES), dma(LANES),
            dma(20), dma(20), dma(6), dma(6), dma(3), dma(3), dma(devices), dma(devices),
            dma(5), dma(5),
        ],
        compiler_params=pltpu.CompilerParams(
            collective_id=0, has_side_effects=True, vmem_limit_bytes=VMEM_LIMIT
        ),
    )(*args)


def add(x, y):
    return x + y


def backward_and_sums(
    d_enc, gains,
    h_u, h_y, h_gp, h_down0, h_down1, h_up0, h_up1,
    h_x, h_x1, h_a, h_qkv, h_p, h_o, h_w0, h_w1, h_proj0, h_proj1,
    dec, dec_qvb, dec_upb, dec_small,
    total, emb, dx_out,
    gb, gt, ut, part, send, recv, du, gx, dx1, d_o, d_acts, own, send1, recv1, dx32, dx,
    d_upb, d_qvb, d_small,
    acc, yacc, enc_mate, out, rcy, ry, land_x, land_l, land_r, small32, small,
    u, y, gp, down0, down1, up0, up1, x, x1, a, qkv, p, o, w0, w1, proj0, proj1, fetch_s,
    load_s, flush_s, ex_s, ex_r,
    core_s, core_r, corey_s, corey_r, y_s, y_r, x_s, x_r, z_s, zl_r, zr_r,
    bl_s, br_s, b_r, a_s, a_r, emb_s, emb_r, dx_s, dx_r,
):
    sec = lax.axis_index("section")
    lane = lax.axis_index("tensor")
    pos = lax.axis_index("dp")
    count = lax.axis_size("dp")
    mate = lane + 1 - 2 * lax.rem(lane, 2)
    over = lax.rem(lane + 2, LANES)
    cross = lax.rem(mate + 2, LANES)
    first = pos == 0
    last = pos == count - 1
    me = sec * LANES + lane
    devices = 2 * LANES

    def group_peer(step):
        peer = lax.rem(me + step, devices)
        return peer, {"section": lax.div(peer, LANES), "tensor": lax.rem(peer, LANES)}

    barrier = pltpu.get_barrier_semaphore()
    for step in range(1, devices):
        pl.semaphore_signal(barrier, inc=1, device_id_type=MESH, device_id=group_peer(step)[1])

    @pl.when(pos > 0)
    def _():
        pl.semaphore_signal(barrier, inc=1, device_id={"dp": pos - 1}, device_id_type=MESH)

    @pl.when(pos < count - 1)
    def _():
        pl.semaphore_signal(barrier, inc=1, device_id={"dp": pos + 1}, device_id_type=MESH)

    loads = [
        pltpu.make_async_copy(dec.at[lane], acc.at[:, 0:DEC_ROWS, :], load_s.at[0]),
        pltpu.make_async_copy(
            dec.at[over, :, EARLY_ROWS:DEC_ROWS, :], yacc.at[:, 0 : DEC_ROWS - EARLY_ROWS, :],
            load_s.at[1],
        ),
    ]
    for load in loads:
        load.start()
    fetches = [
        pltpu.make_async_copy(src, dst, fetch_s.at[n])
        for n, (src, dst) in enumerate(
            (
                (h_u, u), (h_y, y), (h_gp, gp), (h_down0, down0), (h_down1, down1), (h_up0, up0),
                (h_up1, up1), (h_x, x), (h_x1, x1), (h_a, a), (h_qkv, qkv), (h_p, p), (h_o, o),
                (h_w0, w0), (h_w1, w1), (h_proj0, proj0), (h_proj1, proj1),
            )
        )
    ]
    for fetch in fetches:
        fetch.start()
    small32[...] = jnp.zeros_like(small32)
    d_small[...] = jnp.zeros_like(d_small)
    gb[0:PAD, :] = d_enc[...]
    ends = jnp.where(first, 0, 1) + jnp.where(last, 0, 1)
    pl.semaphore_wait(barrier, devices - 1 + ends)

    gain = gains[...].astype(F32)
    width = w0.shape[1]
    marks = head_marks(width, ENC_SIZE, BF16)
    marks32 = head_marks(width, ENC_SIZE, F32)
    ones = ones_per_head(PAD, marks)

    def rows(k, size=CH):
        return pl.ds(pl.multiple_of(k * size, size), size)

    def give_enc():
        return far(d_enc, gb.at[PAD : 2 * PAD, :], ex_s.at[0], ex_r.at[0], {"tensor": over})

    def give_part(i, half):
        cut = rows(i, 256)
        n = 1 + 2 * i + half
        return far(
            send.at[(1 - half) * PAD : (2 - half) * PAD, cut],
            recv.at[half * PAD : (half + 1) * PAD, cut],
            ex_s.at[n], ex_r.at[n], {"tensor": over},
        )

    def give_last(i):
        cut = rows(i, 256)
        return far(send1.at[:, cut], recv1.at[:, cut], ex_s.at[7 + i], ex_r.at[7 + i], {"tensor": over})

    def ff_back(g, i, down):
        c = rows(i, 256)
        d_down = nn(gt[...], y[g, :, c]).astype(BF16)
        dh = nt(gb[...], down[c, :]) * gp[g, :, c].astype(F32)
        d_upb[g, :, c] = colsum(dh)
        dub = dh.astype(BF16)
        du[g, :, c] = dub
        d_up = nn(ut[...], dub).astype(BF16)
        if g == 0:
            acc[1, A_TOP:B_TOP, c] = d_down
            acc[0, A_TOP:B_TOP, c] = d_up
        else:
            enc_mate[1, 0:ENC_A, c] = d_down
            enc_mate[0, 0:ENC_A, c] = d_up

    def ff_in(i):
        c = rows(i, 256)
        t = nt(du[0], up0[c, :]) + nt(du[1], up1[c, :])
        part[:, c] = t
        send[:, c] = t.astype(BF16)
        give_part(i, 0).start()
        give_part(i, 1).start()

    def norm_two():
        for fetch in fetches[7:]:
            fetch.wait()
        for k in range(D // 256):
            give_part(k, 0).wait_recv()
            give_part(k, 1).wait_recv()

        def body(j):
            r = rows(j, 64)
            da = part[r, :] + recv[r, :].astype(F32)
            hat, scale = normal(x1[r, :])
            g = gb[r, :].astype(F32)
            d = g + normal_back(da, hat, scale, gain[1:2])
            gx[r, :] = d.astype(BF16)
            dx1[r, :] = d

            @pl.when(j < 2)
            def _():
                d_small[1:2, :] += colsum(da * hat)
                d_small[3:4, :] += colsum(da)
                d_small[4:5, :] += colsum(d)
                d_small[5:6, :] += colsum(g)

        loop(2 * PAD // 64, body)

    def attention(g, c):
        if c == 0:
            d_proj = tn(o[g], gx[...]).astype(BF16)
            if g == 0:
                acc[1, B_TOP + width : S_TOP, :] = d_proj
            else:
                enc_mate[1, ENC_A + width : ENC_A + 2 * width, :] = d_proj
            d_o[...] = nt(gx[...], (proj0, proj1)[g][...]).astype(BF16)
        r = slice(c * PAD, (c + 1) * PAD)
        d_acts[g, 0, r], d_acts[g, 1, r], d_acts[g, 2, r] = attend_back(
            qkv[g, 0, r], qkv[g, 1, r], qkv[g, 2, r], p[g, c], o[g, r], 1.0 / nn(p[g, c], ones),
            d_o[r, :], marks, marks32, None, ones, ENC_SCALE,
        )
        if c == 1:
            d_qvb[g, 0:1, :] = colsum(d_acts[g, 0].astype(F32))
            d_qvb[g, 1:2, :] = colsum(d_acts[g, 2].astype(F32))

    def project_in(i):
        c = rows(i, 256)
        t = 0.0
        for g, w in enumerate((w0, w1)):
            for j in range(3):
                t += nn(d_acts[g, j], w[j, :, c])
        own[:, c] = t[:PAD]
        send1[:, c] = t[PAD:].astype(BF16)
        give_last(i).start()

    def project_grad(g):
        for j in range(3):
            row = (j % 2) * width
            d = tn(d_acts[g, j], a[...]).astype(BF16)
            if g == 0:
                acc[j // 2, B_TOP + row : B_TOP + row + width, :] = d
            else:
                enc_mate[j // 2, ENC_A + row : ENC_A + row + width, :] = d

    def norm_one():
        for k in range(D // 256):
            give_last(k).wait_recv()

        def body(j):
            r = rows(j, 64)
            da = own[r, :] + recv1[r, :].astype(F32)
            hat, scale = normal(x[r, :])
            d_small[0:1, :] += colsum(da * hat)
            d_small[2:3, :] += colsum(da)
            dx32[r, :] = dx1[r, :] + normal_back(da, hat, scale, gain[0:1])

        loop(PAD // 64, body)
        turned = jnp.transpose(dx32[...])
        cut = D // devices
        for k in range(devices):
            dx[k] = turned[k * cut : (k + 1) * cut, 0:VIS].astype(BF16)
        for r in range(LANES):
            small32[r, 8:9, 0:512] = dec_upb[:, r * 512 : (r + 1) * 512]
            small32[r, 9:10, 0:128] = dec_qvb[0:1, r * 128 : (r + 1) * 128]
            small32[r, 9:10, 128:256] = dec_qvb[1:2, r * 128 : (r + 1) * 128]
            small32[r, 0:8, 0:512] = dec_small[...]
            small32[r, 16:24, :] = d_small[...]
        for g, shard in enumerate((lane, mate)):
            small32[shard, 10:11, :] = d_upb[g]
            small32[shard, 11:12, 0:192] = d_qvb[g, 0:1]
            small32[shard, 11:12, 256:448] = d_qvb[g, 1:2]
        for r in range(LANES):
            for h in range(2):
                small[r, h] = small32[r, h * SMALL : (h + 1) * SMALL].astype(BF16)
        acc[:, S_TOP : S_TOP + SMALL, :] = small[lane]
        yacc[:, DEC_ROWS - EARLY_ROWS :, :] = small[over]
        core_copy(LATE, small.at[mate], SMALL).start()
        corey_copy(LATE, small.at[cross], SMALL).start()
        for step in range(1, devices):
            dx_copy(step).start()
        dx_out[me] = dx[me]

    def core_enc(lo, hi):
        def body(m):
            block = block_of(m)

            @pl.when((block >= lo) & (block < hi))
            def _():
                src = pl.ds(pl.multiple_of(block * CH - DEC_ROWS, CH), CH)
                core_copy(m, enc_mate.at[:, src, :]).start()

        loop(ALL_K, body)

    def first_piece():
        for fetch in fetches[:7]:
            fetch.wait()
        ut[...] = jnp.transpose(u[...])
        give_enc().wait_recv()
        gt[...] = jnp.transpose(gb[...])

    def ff_step(k):
        for g, down in enumerate((down0, down1)):
            @pl.when(lax.rem(k, 2) == g)
            def _(g=g, down=down):
                ff_back(g, lax.div(k, 2), down)

    def run_pieces(n):
        def several(low, high, body):
            begin = sum(jnp.where(n > t, 1, 0) for t in PIECES[low:high])
            end = sum(jnp.where(n >= t, 1, 0) for t in PIECES[low:high])
            lax.fori_loop(begin, end, lambda k, c: (body(k), c)[1], 0)

        def single(k, body):
            @pl.when(n == PIECES[k])
            def _():
                body()

        single(0, first_piece)
        several(1, 7, ff_step)
        single(7, lambda: core_enc(DEC_K, DEC_K + ENC_A // CH))
        several(8, 11, ff_in)
        single(11, norm_two)
        for k in range(4):
            single(12 + k, lambda k=k: attention(k // 2, k % 2))
        several(16, 19, project_in)
        for g in range(2):
            single(19 + g, lambda g=g: project_grad(g))
        single(21, lambda: core_enc(DEC_K + ENC_A // CH, B_K))
        single(22, norm_one)

    def dx_copy(step):
        peer, place = group_peer(step)
        return far(dx.at[peer], dx_out.at[me], dx_s.at[step], dx_r.at[step], place)

    def emb_copy(step):
        return far(
            out.at[:, pl.ds(512, CH), :], emb.at[lane], emb_s.at[step], emb_r.at[step],
            {"tensor": lax.rem(lane + step, LANES)},
        )

    def block_of(m):
        shift = 0
        for k in range(1, ALL_K):
            if ORDER[k] - k != ORDER[k - 1] - k + 1:
                shift = jnp.where(m >= k, ORDER[k] - k, shift)
        return m + shift

    def is_dec(m):
        return (block_of(m) < DEC_K) & (m >= EARLY)

    def at(m, size=CH):
        return pl.ds(pl.multiple_of(block_of(m) * CH, CH), size)

    def slot(m, size=CH):
        return pl.ds(pl.multiple_of(m * CH, CH), size)

    def y_at(m, size=CH):
        return pl.ds(pl.multiple_of((jnp.minimum(block_of(m), DEC_K) - EARLY) * CH, CH), size)

    def core_copy(m, src, size=CH):
        return far(src, out.at[:, at(m, size), :], core_s.at[m], core_r.at[m], {"tensor": mate})

    def corey_copy(m, src, size=CH):
        return far(src, rcy.at[:, y_at(m, size), :], corey_s.at[m], corey_r.at[m], {"tensor": mate})

    def y_copy(m, size=CH):
        cut = y_at(m, size)
        return far(
            yacc.at[:, cut, :], ry.at[:, cut, :], y_s.at[m], y_r.at[m], {"tensor": over}
        )

    def x_copy(m, size=CH):
        return far(
            acc.at[1 - sec, at(m, size), :], land_x.at[0, slot(m, size), :], x_s.at[m], x_r.at[m],
            {"section": 1 - sec},
        )

    def xc_copy(m):
        return far(
            acc.at[:, at(m), :], land_x.at[:, slot(m), :], x_s.at[m], x_r.at[m],
            {"section": 1 - sec},
        )

    def z_copy(m, whole, right, size=CH):
        land = land_l if right else land_r
        if whole:
            src, dst = acc.at[:, at(m), :], land.at[:, slot(m), :]
        else:
            src, dst = acc.at[sec, at(m, size), :], land.at[0, slot(m, size), :]
        landed = zl_r if right else zr_r
        return far(src, dst, z_s.at[m], landed.at[m], {"dp": pos + 1 if right else pos - 1})

    def b_copy(m, whole, right, size=CH):
        place = out.at[:, at(m), :] if whole else out.at[sec, at(m, size), :]
        sent = br_s if right else bl_s
        return far(place, place, sent.at[m], b_r.at[m], {"dp": pos + 1 if right else pos - 1})

    def a_copy(m, size=CH):
        place = out.at[sec, at(m, size), :]
        return far(place, place, a_s.at[m], a_r.at[m], {"section": 1 - sec})

    def a_wait(m, size=CH):
        place = out.at[1 - sec, at(m, size), :]
        far(place, place, a_s.at[m], a_r.at[m], {"section": 1 - sec}).wait_recv()

    give_enc().start()

    def start_core(m):
        @pl.when(is_dec(m))
        def _():
            core_copy(m, dec.at[mate, :, at(m), :]).start()
            corey_copy(m, dec.at[cross, :, at(m), :]).start()

    loop(ALL_K, start_core)
    for load in loads:
        load.wait()

    def join_core(m, size):
        core_copy(m, out.at[:, at(m, size), :], size).wait_recv()
        acc[:, at(m, size), :] = add(acc[:, at(m, size), :], out[:, at(m, size), :])

    def join_core_y(m, size):
        corey_copy(m, rcy.at[:, y_at(m, size), :], size).wait_recv()
        yacc[:, y_at(m, size), :] = add(yacc[:, y_at(m, size), :], rcy[:, y_at(m, size), :])
        y_copy(m, size).start()

    def stage_c(m):
        @pl.when((m >= EARLY) & (m != LATE))
        def _():
            join_core(m, CH)

            @pl.when(is_dec(m))
            def _():
                join_core_y(m, CH)

        @pl.when(m == LATE)
        def _():
            join_core(m, SMALL)
            join_core_y(m, SMALL)

    def flush(m):
        return pltpu.make_async_copy(
            out.at[:, at(m), :], total.at[:, at(m), :], flush_s.at[m]
        )

    def finished(m):
        flush(m).start()

        @pl.when(block_of(m) == DEC_K - 1)
        def _():
            for step in range(1, LANES):
                emb_copy(step).start()
            emb[lane] = out[:, 512 : 512 + CH, :]

    def line_of(root, whole, size=CH):
        left = pos < root
        right = pos > root
        here = pos == root
        reach = max(root, count - 1 - root)
        level = jnp.where(left, pos, jnp.where(right, count - 1 - pos, reach))
        dist = jnp.where(left, root - pos, pos - root)

        def view(ref, m):
            return ref.at[:, at(m), :] if whole else ref.at[sec, at(m, size), :]

        def landed(ref, m):
            return ref.at[:, slot(m), :] if whole else ref.at[0, slot(m, size), :]

        def hop(m, rightward):
            return z_copy(m, whole, rightward, size)

        def back_hop(m, rightward):
            return b_copy(m, whole, rightward, size)

        def outer(m):
            @pl.when(left & first)
            def _():
                hop(m, True).start()

            @pl.when(right & last)
            def _():
                hop(m, False).start()

        def inward(m):
            @pl.when(left & (pos > 0))
            def _():
                hop(m, True).wait_recv()
                view(acc, m)[...] = add(view(acc, m)[...], landed(land_l, m)[...])
                hop(m, True).start()

            @pl.when(right & (pos < count - 1))
            def _():
                hop(m, False).wait_recv()
                view(acc, m)[...] = add(view(acc, m)[...], landed(land_r, m)[...])
                hop(m, False).start()

            @pl.when(here)
            def _():
                total = view(acc, m)[...].astype(F32)
                if root > 0:
                    hop(m, True).wait_recv()
                    total = total + landed(land_l, m)[...].astype(F32)
                if root < count - 1:
                    hop(m, False).wait_recv()
                    total = total + landed(land_r, m)[...].astype(F32)
                if whole:
                    view(acc, m)[...] = total.astype(BF16)
                    xc_copy(m).start()
                else:
                    view(out, m)[...] = total.astype(BF16)
                    spread(m)
                    a_copy(m, size).start()

        def spread(m):
            if root > 0:
                back_hop(m, False).start()
            if root < count - 1:
                back_hop(m, True).start()

        def crossed(m):
            xc_copy(m).wait_recv()
            view(out, m)[...] = add(view(acc, m)[...], landed(land_x, m)[...])
            spread(m)
            finished(m)

        def outward(m):
            back_hop(m, False).wait_recv()

            @pl.when(left & (pos > 0))
            def _():
                back_hop(m, False).start()

            @pl.when(right & (pos < count - 1))
            def _():
                back_hop(m, True).start()

            if whole:
                finished(m)
            else:
                a_copy(m, size).start()

        def sent(m):
            @pl.when(jnp.logical_not(here))
            def _():
                hop(m, True).wait_send()

            @pl.when((pos <= root) & (pos > 0))
            def _():
                back_hop(m, False).wait_send()

            @pl.when((pos >= root) & (pos < count - 1))
            def _():
                back_hop(m, True).wait_send()

            if whole:
                @pl.when(here)
                def _():
                    xc_copy(m).wait_send()
            else:
                a_copy(m, size).wait_send()

                @pl.when(crosses_first(m))
                def _():
                    x_copy(m, size).wait_send()

        def crosses_first(m):
            return m >= EARLY if XFIRST else m >= 0

        def set_off(m):
            if whole:
                outer(m)
            else:
                x_copy(m, size).start()

        def set_off_early(m):
            if XFIRST:
                outer(m)
            else:
                set_off(m)

        def add_y(m):
            def joined():
                y_copy(m, size).wait_recv()
                acc[:, at(m, size), :] = add(acc[:, at(m, size), :], ry[:, y_at(m, size), :])

            if size == CH:
                pl.when(is_dec(m))(joined)
            else:
                joined()
            set_off(m)

        def add_x(m):
            @pl.when(crosses_first(m))
            def _():
                x_copy(m, size).wait_recv()
                acc[sec, at(m, size), :] = add(
                    acc[sec, at(m, size), :], land_x[0, slot(m, size), :]
                )
                outer(m)

        def last_half(m):
            a_wait(m, size)
            finished(m)

        base = 1 if whole else 2
        back = base + reach + dist + (1 if whole else 0)
        steps = [(back, jnp.logical_not(here), outward), (base + level, level > 0, inward)]
        if whole:
            steps.append((base + reach + 1, here, crossed))
        else:
            steps += [(back + 1, True, last_half), (2, True, add_x)]
        return steps, sent, add_y, set_off_early

    low_root = (count - 1) // 2
    high_root = min(low_root + 1, count - 1)
    def is_whole(m):
        return (lax.rem(m, 2) == 0) & (m >= WHOLE_LOW) & (m < WHOLE_HIGH)

    roots = (high_root, count - 1, low_root, 0)
    lines = [
        (lambda m, part=part: is_whole(m) & (lax.rem(m, 8) == part), *line_of(root, True))
        for part, root in zip((0, 2, 4, 6), roots)
    ] + [
        (lambda m: jnp.logical_not(is_whole(m)) & (m != LATE), *line_of(low_root, False)),
        (lambda m: m == LATE, *line_of(low_root, False, SMALL)),
    ]

    def finish(m):
        @pl.when((m >= EARLY) & (m != LATE))
        def _():
            core_copy(m, out.at[:, at(m), :]).wait_send()

            @pl.when(is_dec(m))
            def _():
                corey_copy(m, rcy.at[:, y_at(m), :]).wait_send()
                y_copy(m).wait_send()

        @pl.when(m == LATE)
        def _():
            core_copy(m, out.at[:, at(m, SMALL), :], SMALL).wait_send()
            corey_copy(m, rcy.at[:, y_at(m, SMALL), :], SMALL).wait_send()
            y_copy(m, SMALL).wait_send()

        for mine, _, sent, _, _ in lines:
            @pl.when(mine(m))
            def _(sent=sent):
                sent(m)

    def set_off_early(m):
        for mine, _, _, _, set_off in lines:
            @pl.when(mine(m))
            def _(set_off=set_off):
                set_off(m)

    loop(EARLY, set_off_early)
    far_reach = max(max(root, count - 1 - root) for root in roots)
    depth = LAG * (3 + 2 * far_reach) + 1

    def tick(n):
        @pl.when(n <= PIECES[-1])
        def _():
            run_pieces(n)

        for mine, steps, _, add_y, _ in lines:
            m = n - LAG

            @pl.when((m >= EARLY) & (m < ALL_K))
            def _(m=m, mine=mine, add_y=add_y):
                @pl.when(mine(m))
                def _():
                    add_y(m)

            for offset, enabled, stage in steps:
                m = n - LAG * offset

                @pl.when((m >= 0) & (m < ALL_K) & enabled)
                def _(m=m, mine=mine, stage=stage):
                    @pl.when(mine(m))
                    def _():
                        stage(m)

        @pl.when(n < ALL_K)
        def _():
            stage_c(n)

        @pl.when(n >= depth)
        def _():
            finish(n - depth)

    loop(ALL_K + depth, tick)
    loop(ALL_K, lambda m: flush(m).wait())
    for step in range(1, devices):
        dx_copy(step).wait()
    for step in range(1, LANES):
        emb_copy(step).wait()
    give_enc().wait_send()
    for k in range(D // 256):
        give_part(k, 0).wait_send()
        give_part(k, 1).wait_send()
        give_last(k).wait_send()


def backward_call(args, half, hid):
    dma = lambda *s: pltpu.SemaphoreType.DMA(s)
    vm = pltpu.VMEM
    full = ALL_K * CH
    y_half = DEC_ROWS - EARLY_ROWS + SMALL
    k = ALL_K
    rows = 2 * PAD
    cut = D // (2 * LANES)
    specs = [VM, VM] + [ANY] * 18 + [VM] * 3
    return pl.pallas_call(
        backward_and_sums,
        out_shape=[
            jax.ShapeDtypeStruct((2, full, D), BF16),
            jax.ShapeDtypeStruct((LANES, 2, CH, D), BF16),
            jax.ShapeDtypeStruct((2 * LANES, cut, VIS), BF16),
        ],
        in_specs=specs,
        out_specs=[ANY, VM, VM],
        scratch_shapes=[
            vm((rows, D), BF16), vm((D, rows), BF16), vm((D, rows), BF16),
            vm((rows, D), F32), vm((rows, D), BF16), vm((rows, D), BF16),
            vm((2, rows, hid), BF16), vm((rows, D), BF16), vm((rows, D), F32),
            vm((rows, half), BF16), vm((2, 3, rows, half), BF16),
            vm((PAD, D), F32), vm((PAD, D), BF16), vm((PAD, D), BF16), vm((PAD, D), F32),
            vm((2 * LANES, cut, VIS), BF16),
            vm((2, 1, hid), F32), vm((2, 2, half), F32), vm((8, D), F32),
            vm((2, full, D), BF16), vm((2, y_half, D), BF16), vm((2, ENC_A + ENC_B, D), BF16),
            vm((2, full, D), BF16),
            vm((2, y_half, D), BF16), vm((2, y_half, D), BF16),
            *[vm((2, full, D), BF16)] * 3,
            vm((LANES, 32, D), F32), vm((LANES, 2, SMALL, D), BF16),
            *[vm(v.shape, v.dtype) for v in args[2:19]],
            dma(17), dma(2), dma(k), dma(10), dma(10),
            dma(k), dma(k), dma(k), dma(k), dma(k), dma(k),
            dma(k), dma(k), dma(k), dma(k), dma(k),
            dma(k), dma(k), dma(k), dma(k), dma(k), dma(LANES), dma(LANES),
            dma(2 * LANES), dma(2 * LANES),
        ],
        compiler_params=pltpu.CompilerParams(
            collective_id=1, has_side_effects=True, vmem_limit_bytes=VMEM_LIMIT
        ),
    )(*args)


STEPS = 6


def finish_grads(
    total, emb, decoded, dx, decoded_out, dx_out,
    e_qkv, e_qvb, e_proj, e_up, e_upb, e_down, e_gain, e_off,
    d_qkv, d_qvb, d_proj, d_up, d_upb, d_down, d_gain, d_off, d_ew, d_ev,
):
    i = pl.program_id(0)

    def rows(size):
        return pl.ds(pl.multiple_of(i * size, size), size)

    cut = rows(128)
    e_up[...] = total[0, pl.ds(pl.multiple_of(A_TOP + i * 128, 64), 128), :].astype(F32)
    e_down[...] = jnp.transpose(total[1, A_TOP:B_TOP, cut].astype(F32))
    third = e_qkv.shape[0]

    @pl.when(i < 4)
    def _():
        e_qkv[...] = total[0, pl.ds(pl.multiple_of(B_TOP + i * third, 32), third), :].astype(F32)

    @pl.when(i >= 4)
    def _():
        e_qkv[...] = total[
            1, pl.ds(pl.multiple_of(B_TOP + (i - 4) * third, 32), third), :
        ].astype(F32)

    size = e_proj.shape[0]
    start = B_TOP + 2 * third
    e_proj[...] = total[1, pl.ds(pl.multiple_of(start + i * size, 32), size), :].astype(F32)

    def tile(number, top, height, left, width):
        place = lax.div(number, 3)
        row = lax.div(place, 2) * CH + top
        col = lax.rem(number, 3) * 256 + left
        return total[
            lax.rem(place, 2),
            pl.ds(pl.multiple_of(row, 32), height),
            pl.ds(pl.multiple_of(col, 128), width),
        ].astype(F32)

    @pl.when(i < LANES)
    def _():
        decoded_out[...] = decoded[...]
        dx_out[...] = dx[...]
        side, part = lax.div(i, 2), lax.rem(i, 2)
        for n in range(2):
            block = 2 * i + n
            cut = slice(n * CH, (n + 1) * CH)
            for k in range(2):
                d_up[cut, k * 256 : (k + 1) * 256] = tile(4 * block + k, 0, CH, 0, 256)
            d_qkv[0, cut, :] = tile(32 + 2 * block, 0, CH, 0, 128)
            d_qkv[1, cut, :] = tile(32 + 2 * block, 0, CH, 128, 128)
            d_qkv[2, cut, :] = tile(33 + 2 * block, 0, CH, 0, 128)
        for k in range(LANES):
            pair = [tile(4 * (2 * k + n) + 2 + side, 0, CH, part * 128, 128) for n in range(2)]
            d_down[:, k * 128 : (k + 1) * 128] = jnp.transpose(jnp.concatenate(pair, 0))
            number = 33 + 2 * (2 * k + side)
            d_proj[:, k * 128 : (k + 1) * 128] = tile(number, part * 32, 32, 128, 128)
        for h in range(2):
            d_ew[h * 64 : (h + 1) * 64, :] = emb[i, h, :, 0:512].astype(F32)
            d_ew[128:192, h * 256 : (h + 1) * 256] = emb[i, h, :, 512:768].astype(F32)

    @pl.when(i == 0)
    def _():
        little = total[0, S_TOP : S_TOP + SMALL, :].astype(F32)
        d_gain[...] = little[0:2, 0:512]
        d_off[...] = little[2:6, 0:512]
        d_ev[...] = little[6:8, 0:512]
        d_upb[...] = little[8, 0:512]
        d_qvb[0:1, :] = little[9:10, 0:128]
        d_qvb[1:2, :] = little[9:10, 128:256]
        e_upb[...] = little[10]
        e_qvb[0:1, :] = little[11:12, 0:192]
        e_qvb[1:2, :] = little[11:12, 256:448]
        other = total[1, S_TOP : S_TOP + SMALL, :].astype(F32)
        e_gain[...] = other[0:2]
        e_off[...] = other[2:6]


def finish_call(total, emb, decoded, dx, half, hid):
    def whole(*shape):
        return shape, pl.BlockSpec(shape, lambda i: (0,) * len(shape))

    def split(*shape):
        block = (shape[0] // STEPS,) + shape[1:]
        return shape, pl.BlockSpec(block, lambda i: (i,) + (0,) * (len(shape) - 1))

    def fourth(*shape):
        block = (shape[0] // LANES,) + shape[1:]
        return shape, pl.BlockSpec(
            block, lambda i: (jnp.minimum(i, LANES - 1),) + (0,) * (len(shape) - 1)
        )

    middle = (3, DD, 128), pl.BlockSpec(
        (3, DD // LANES, 128), lambda i: (0, jnp.minimum(i, LANES - 1), 0)
    )
    outs = [
        split(3 * half, D), whole(2, half), split(half, D), split(D, hid), whole(hid),
        split(hid, D), whole(2, D), whole(4, D),
        middle, whole(2, 128), fourth(128, DD), fourth(DD, 512), whole(512),
        fourth(512, DD), whole(2, DD), whole(4, DD),
        fourth(D, DD), whole(2, DD),
    ]
    slabs = [fourth(*decoded.shape), fourth(*dx.shape)]
    return pl.pallas_call(
        finish_grads,
        grid=(STEPS,),
        out_shape=[jax.ShapeDtypeStruct(s, BF16) for s, _ in slabs]
        + [jax.ShapeDtypeStruct(s, F32) for s, _ in outs],
        in_specs=[whole(*total.shape)[1], whole(*emb.shape)[1]] + [spec for _, spec in slabs],
        out_specs=[spec for _, spec in slabs + outs],
        compiler_params=pltpu.CompilerParams(vmem_limit_bytes=VMEM_LIMIT),
    )(total, emb, decoded, dx)


def position_rows():
    quarter = DD // 4
    freq = np.exp(np.arange(quarter, dtype=np.float32) * np.float32(-math.log(10000.0) / quarter))
    angle = np.arange(PAD, dtype=np.float32)[:, None] * freq[None, :].astype(np.float32)
    both = np.concatenate([np.sin(angle), np.cos(angle)], 1).astype(np.float32)
    high = both.astype(jnp.bfloat16)
    low = (both - high.astype(np.float32)).astype(jnp.bfloat16)
    return np.stack([high, low])


def per_device(
    patches, cotangent, widths, visible, window_shift, batch_order,
    encoder_qkv, encoder_qvbias, encoder_proj, encoder_up, encoder_upbias, encoder_down,
    encoder_gains, encoder_offsets,
    decoder_qkv, decoder_qvbias, decoder_proj, decoder_up, decoder_upbias, decoder_down,
    decoder_gains, decoder_offsets, embed_weight, embed_vectors,
):
    qkv0 = encoder_qkv.transpose(1, 2, 0)
    half = qkv0.shape[1]
    hid = encoder_up.shape[1]
    dff = decoder_up.shape[1] * LANES
    flat = patches.transpose(1, 0, 2).reshape(-1, D)
    (
        x, x1, a, u, y, gp, qkv, p, o, qkv1, proj1, up1, down1, dec_buf,
        d_enc, d_dqvb, d_dupb, d_dsmall, out_all,
    ) = forward_call(
        (
            widths, window_shift.T, batch_order, visible, flat, encoder_gains, encoder_offsets,
            encoder_qvbias, encoder_upbias, decoder_qvbias, decoder_upbias,
            qkv0, encoder_proj, encoder_up, encoder_down,
            decoder_qkv.transpose(1, 0, 2), decoder_proj, decoder_up, decoder_down,
            cotangent, embed_weight, embed_vectors, jnp.asarray(position_rows()),
            decoder_gains, decoder_offsets,
        ),
        half, hid, dff,
    )
    total, emb, dx_all = backward_call(
        (
            d_enc, encoder_gains, u, y, gp, encoder_down, down1, encoder_up, up1,
            x, x1, a, qkv, p, o, qkv0, qkv1, encoder_proj, proj1,
            dec_buf, d_dqvb, d_dupb, d_dsmall,
        ),
        half, hid,
    )
    out_all, dx_all, *grads = finish_call(total, emb, out_all, dx_all, half, hid)
    grads[0] = grads[0].reshape(3, half, D)
    grads[0] = grads[0].transpose(2, 0, 1)
    grads[8] = grads[8].transpose(1, 0, 2)
    return (out_all.swapaxes(1, 2), dx_all.swapaxes(1, 2), *grads)


def solution(mesh):
    weights = (
        P(None, None, "tensor"), P(None, "tensor"), P("tensor", None), P(None, "tensor"),
        P("tensor"), P("tensor", None), P(), P(),
    )
    split = P("dp", None, ("section", "tensor"))
    return jax.shard_map(
        per_device,
        mesh=mesh,
        in_specs=(
            P("dp", None, None), P("dp", None, None), P("dp"), P("dp", None), P("dp", None),
            P("dp", None),
        ) + weights + weights + (P(), P()),
        out_specs=(split, split) + weights + weights + (P(), P()),
        check_vma=False,
    )
```

```python
import math

import jax
import jax.numpy as jnp
import numpy as np
from jax import lax
from jax.experimental import pallas as pl
from jax.experimental.pallas import tpu as pltpu
from jax.sharding import PartitionSpec as P

D = 768
HEADS = 12
DD = 512
DHEADS = 16
GRID_ROWS = 64
WIDE = 8
WIN = 4
VIS = 102
CM = 4
GRID = 512
LANES = 4
PAD = 128
EPS = 1e-06
NEG = -10000.0
F32 = jnp.float32
BF16 = jnp.bfloat16
VMEM_LIMIT = 60 * 1024 * 1024

VM = pl.BlockSpec(memory_space=pltpu.VMEM)
SM = pl.BlockSpec(memory_space=pltpu.SMEM)
ANY = pl.BlockSpec(memory_space=pl.ANY)


def nn(a, b):
    return lax.dot_general(a, b, (((1,), (0,)), ((), ())), preferred_element_type=F32)


def nt(a, b):
    return lax.dot_general(a, b, (((1,), (1,)), ((), ())), preferred_element_type=F32)


def tn(a, b):
    return lax.dot_general(a, b, (((0,), (0,)), ((), ())), preferred_element_type=F32)


def loop(count, body, unroll=1):
    def step(i, carry):
        body(i)
        return carry

    lax.fori_loop(0, count, step, 0, unroll=unroll)


def span(i, size):
    return pl.ds(pl.multiple_of(i * size, size), size)


def normal(x):
    center = x - jnp.mean(x, -1, keepdims=True)
    scale = lax.rsqrt(jnp.mean(center * center, -1, keepdims=True) + EPS)
    return center * scale, scale


def normal_back(dy, hat, scale, gain):
    d = dy * gain
    return scale * (
        d - jnp.mean(d, -1, keepdims=True) - hat * jnp.mean(d * hat, -1, keepdims=True)
    )


def gelu_both(h):
    phi = 0.5 * lax.erf(h * math.sqrt(0.5)) + 0.5
    bell = jnp.exp2(h * h * (-0.5 * math.log2(math.e)))
    return h * phi, phi + h * bell * (1.0 / math.sqrt(2.0 * math.pi))


def colsum(x):
    return jnp.sum(x, 0, keepdims=True)


def head_marks(width, size, dtype):
    lane = lax.broadcasted_iota(jnp.int32, (1, width), 1)
    return [((lane >= h * size) & (lane < (h + 1) * size)).astype(dtype) for h in range(width // size)]


def stacked(x, marks):
    return jnp.concatenate([x * m for m in marks], 0)


LOG2E = math.log2(math.e)


def attend(q, k, v, marks, ones, masked, scale):
    keys = k.shape[0]
    s = nt(q, stacked(k, marks))
    parts = []
    for h in range(len(marks)):
        x = masked(s[:, h * keys : (h + 1) * keys] * (scale * LOG2E))
        parts.append(jnp.exp2(x - jnp.max(x, -1, keepdims=True)).astype(BF16))
    e = jnp.concatenate(parts, 1)
    width = q.shape[1]
    if width % 128:
        top, total = nn(e, stacked(v, marks)), nn(e, ones)
    else:
        both = nn(e, jnp.concatenate([stacked(v, marks), ones], 1))
        top, total = both[:, :width], both[:, width:]
    inverse = 1.0 / total
    return e, (top * inverse).astype(BF16), inverse


def attend_back(q, k, v, e, o, inverse, d_out, marks, marks32, rows32, ones, scale):
    keys = k.shape[0]
    width = q.shape[1]
    d_one = d_out.astype(F32) * inverse
    d_two = (d_one * o.astype(F32)).astype(BF16)
    d_one = d_one.astype(BF16)
    if width % 128:
        d_s = nt(d_one, stacked(v, marks)) - nt(d_two, ones)
    else:
        d_s = nt(
            jnp.concatenate([d_one, d_two], 1), jnp.concatenate([stacked(v, marks), -ones], 1)
        )
    dr = (e.astype(F32) * d_s * scale).astype(BF16)
    d_q = nn(dr, stacked(k, marks)).astype(BF16)
    if width % 128:
        d_k_all, d_v_all = tn(dr, q), tn(e, d_one)
        d_k = d_v = 0.0
        for h in range(len(marks)):
            cut = slice(h * keys, (h + 1) * keys)
            d_k += d_k_all[cut] * marks32[h]
            d_v += d_v_all[cut] * marks32[h]
        return d_q, d_k.astype(BF16), d_v.astype(BF16)
    d_k_all = nn(jnp.transpose(q), dr)
    d_v_all = nn(jnp.transpose(d_one), e)
    d_k = d_v = 0.0
    for h in range(len(marks)):
        cut = slice(h * keys, (h + 1) * keys)
        d_k += d_k_all[:, cut] * rows32[h]
        d_v += d_v_all[:, cut] * rows32[h]
    return d_q, jnp.transpose(d_k.astype(BF16)), jnp.transpose(d_v.astype(BF16))


def ones_per_head(keys, marks):
    return jnp.concatenate([jnp.broadcast_to(m, (keys, m.shape[1])) for m in marks], 0)


ENC_SIZE = D // HEADS
ENC_SCALE = ENC_SIZE ** -0.5
DEC_SIZE = DD // DHEADS
DEC_SCALE = DEC_SIZE ** -0.5


CH = 64
DEC_ROWS = 576
ENC_A = 768
ENC_B = 384
DEC_K = DEC_ROWS // CH
B_K = (DEC_ROWS + ENC_A + ENC_B) // CH
ALL_K = B_K + 1
A_TOP = DEC_ROWS
B_TOP = DEC_ROWS + ENC_A
S_TOP = B_TOP + ENC_B
EARLY = 4
XFIRST = True
EARLY_ROWS = EARLY * CH
LAG = 2
ORDER = (0, 1, 2, 3, 9, 10, 11, 12, 13, 14, 4, 15, 16, 17, 18, 5, 6, 19, 21, 20, 8, 22, 23, 24, 25, 27, 26, 7)
PIECES = (0, 2, 2, 2, 2, 2, 2, 2, 3, 3, 3, 10, 12, 12, 13, 13, 14, 14, 15, 15, 15, 16, 20)
LATE = ORDER.index(B_K)
WHOLE_LOW = 6
WHOLE_HIGH = 22
SMALL = 16


def tile_of(number):
    place = number // 3
    return place % 2, place // 2 * CH, number % 3 * 256


MESH = pl.DeviceIdType.MESH


def far(src, dst, send, recv, peer):
    return pltpu.make_async_remote_copy(
        src_ref=src, dst_ref=dst, send_sem=send, recv_sem=recv, device_id=peer, device_id_type=MESH
    )


def forward_and_decoder(
    wid, shifts, order, vis, pat, gains, offs, b_qv, b_up, b_dqv, b_dup,
    h_qkv, h_proj, h_up, h_down, h_dqkv, h_dproj, h_dup, h_ddown,
    cot_hbm, ew, evec, table, dgains, doffs,
    o_x, o_x1, o_a, o_u, o_y, o_gp, o_qkv, o_p, o_o, o_w, o_wproj, o_wup, o_wdown, o_dec,
    d_enc, d_qvb, d_upb, d_small, dec_out,
    w_qkv, w_proj, w_up, w_down, bias, biases, qkv, proj, up, down,
    ex, ea, eu, ey, egp, eqkv, ep, eo, ex1, epart, esend, erecv, esend2, erecv2, eown,
    cot, x0, x1, a, acts, probs, o, inverse, u, ut, y, gp, g32, gb, gt, acc, e_ref, hot, perm, buf, dsend, e_rc, e_rcy, e_rx, e_ry,
    load_s, out_s, cot_s, w_s, w_r, bias_s, bias_r, dw_s, dw_r, ex_s, ex_r, ex2_s, ex2_r, do_s, do_r, e_s, e_r,
):
    sec = lax.axis_index("section")
    lane = lax.axis_index("tensor")
    mate = lane + 1 - 2 * lax.rem(lane, 2)
    over = lax.rem(lane + 2, LANES)
    cross = lax.rem(mate + 2, LANES)
    me = sec * LANES + lane
    devices = 2 * LANES
    clip = me
    clips = (me, sec * LANES + over)

    def group_peer(step):
        peer = lax.rem(me + step, devices)
        return peer, {"section": lax.div(peer, LANES), "tensor": lax.rem(peer, LANES)}

    own = [
        pltpu.make_async_copy(src, dst.at[0], load_s.at[n])
        for n, (src, dst) in enumerate(
            ((h_qkv, w_qkv), (h_proj, w_proj), (h_up, w_up), (h_down, w_down))
        )
    ]

    def place(n, shard, part=None):
        thick = (128, 128, 512, 512)[n]
        base = shard * thick
        cut = pl.ds(pl.multiple_of(base, thick), thick)
        if part is None:
            return (qkv.at[:, :, cut], proj.at[cut, :], up.at[:, cut], down.at[cut, :])[n]
        some = span(part, (256, 64, 256, 256)[n])
        if n == 0:
            return qkv.at[:, some, cut]
        if n == 2:
            return up.at[some, cut]
        few = thick // 2
        rows = pl.ds(pl.multiple_of(base + part * few, few), few)
        return (proj if n == 1 else down).at[rows, :]

    shards = (h_dqkv, h_dproj, h_dup, h_ddown)
    keep = [
        pltpu.make_async_copy(shards[n], place(n, lane), load_s.at[4 + n]) for n in range(4)
    ]
    for copy in own + keep:
        copy.start()
    fetch = pltpu.make_async_copy(cot_hbm.at[clip], cot, cot_s)
    fetch.start()

    barrier = pltpu.get_barrier_semaphore()
    for step in range(1, devices):
        pl.semaphore_signal(barrier, inc=1, device_id_type=MESH, device_id=group_peer(step)[1])
    bias[...] = jnp.zeros_like(bias)
    half = w_proj.shape[1]
    bias[0:1, :] = b_up[...].astype(F32).reshape(1, -1)
    bias[1:3, 0:half] = b_qv[...].astype(F32)
    bias[3:4, 0:512] = b_dup[...].astype(F32).reshape(1, -1)
    bias[4:6, 0:128] = b_dqv[...].astype(F32)
    biases[lane] = bias[...]
    stride = pat.shape[0] // VIS
    for c in range(2):
        row = lax.broadcasted_iota(jnp.int32, (PAD, pat.shape[0]), 0)
        col = lax.broadcasted_iota(jnp.int32, (PAD, pat.shape[0]), 1)
        pick = (col == row * stride + clips[c]).astype(F32).astype(BF16)
        ex[c * PAD : (c + 1) * PAD, :] = nn(pick, pat[...])

    pl.semaphore_wait(barrier, devices - 1)

    def enc_weight(n):
        src = (h_qkv, h_proj, h_up, h_down)[n]
        dst = (w_qkv, w_proj, w_up, w_down)[n]
        return far(src, dst.at[1], w_s.at[n], w_r.at[n], {"tensor": mate})

    def bias_copy(step):
        return far(
            bias, biases.at[lane], bias_s.at[step], bias_r.at[step],
            {"tensor": lax.rem(lane + step, LANES)},
        )

    def half_of(n):
        some = span(sec, (256, 64, 256, 256)[n])
        return shards[n].at[:, some, :] if n == 0 else shards[n].at[some, :]

    def dec_weight(n, kind):
        peer = {"section": 1 - sec} if kind == 2 else {"tensor": over if kind == 0 else mate}
        if kind == 0:
            src, dst = half_of(n), place(n, lane, sec)
        elif kind == 1:
            src, dst = shards[n], place(n, lane)
        else:
            src = dst = place(n, over, 1 - sec if kind == 4 else sec)
        return far(src, dst, dw_s.at[5 * n + kind], dw_r.at[5 * n + kind], peer)

    enc_weight(0).start()
    for step in range(1, LANES):
        bias_copy(step).start()
    enc_weight(1).start()
    dec_weight(0, 0).start()
    enc_weight(2).start()
    enc_weight(3).start()
    for n in range(4):
        dec_weight(n, 1).start()

    def pass_on(n):
        dec_weight(n, 0).wait_recv()
        dec_weight(n, 2).start()
        dec_weight(n, 3).start()

    def pass_last(n):
        dec_weight(n, 2).wait_recv()
        dec_weight(n, 4).start()

    def arrived(n):
        keep[n].wait()
        dec_weight(n, 1).wait_recv()
        dec_weight(n, 3).wait_recv()
        dec_weight(n, 4).wait_recv()

    width = wid[clip]
    bits = jnp.where(width == WIDE, 3, 2)
    turn = shifts[0, clip] * width
    mod = GRID - 1
    spot = 0
    for i in range(order.shape[1]):
        spot = spot + jnp.where(order[0, i] == clip, i, 0)
    batch = spot // CM
    count = 0
    for i in range(order.shape[1]):
        count = count + jnp.where(batch == i // CM, wid[order[0, i]], 0)
    factor_rows = CM * GRID / (jnp.full((1, 1), count, jnp.int32) * GRID_ROWS).astype(F32)

    def slot_of(index):
        return (index - turn) & mod

    def code_of(slot):
        band = ((slot >> bits) + shifts[0, clip]) >> 2
        strip = ((slot & (width - 1)) + shifts[1, clip]) >> 2
        return band * 4 + strip

    def valid_rows():
        slot = slot_of(lax.broadcasted_iota(jnp.int32, (GRID, 1), 0))
        return (slot < GRID_ROWS * width).astype(F32)

    def clip_gradient():
        fetch.wait()
        rolled = slot_of(lax.broadcasted_iota(jnp.int32, (GRID, GRID), 0))
        column = lax.broadcasted_iota(jnp.int32, (GRID, GRID), 1)
        perm[...] = (rolled == column).astype(F32).astype(BF16)
        g = nn(perm[...], cot[...]) * valid_rows() * factor_rows
        g32[...] = g
        gb[...] = g.astype(BF16)
        gt[...] = jnp.transpose(g.astype(BF16))
        d_small[...] = jnp.zeros_like(d_small)
        d_small[5:6, :] = colsum(g)

    seen = vis[pl.ds(clip, 1), :]
    target = jnp.concatenate([(seen + turn) & mod, jnp.full((1, PAD - VIS), -1, jnp.int32)], 1)

    def places(i):
        r = span(i, PAD)
        index = lax.broadcasted_iota(jnp.int32, (PAD, PAD), 0) + i * PAD
        column = lax.broadcasted_iota(jnp.int32, (PAD, PAD), 1)
        hot[r, :] = (index == target).astype(F32).astype(BF16)
        slot = slot_of(index)
        by_row = ((slot >> bits) == column).astype(F32).astype(BF16)
        by_col = ((slot & (width - 1)) == column).astype(F32).astype(BF16)
        row_part = nn(by_row, table[0]) + nn(by_row, table[1])
        col_part = nn(by_col, table[0]) + nn(by_col, table[1])
        x0[r, :] = jnp.concatenate([row_part, col_part], 1)

    egain = gains[...].astype(F32)
    eoff = offs[...].astype(F32)
    emarks = head_marks(half, ENC_SIZE, BF16)
    key = lax.broadcasted_iota(jnp.int32, (PAD, PAD), 1)
    floor = jnp.where(key < VIS, NEG * LOG2E, -1e30)
    eones = ones_per_head(PAD, emarks)
    blocks = D // 256

    def give_part(i, side):
        cut = span(i, 256)
        return far(
            esend.at[(1 - side) * PAD : (2 - side) * PAD, cut],
            erecv.at[side * PAD : (side + 1) * PAD, cut],
            ex_s.at[2 * i + side], ex_r.at[2 * i + side], {"tensor": over},
        )

    for c in range(2):
        rows = slice(c * PAD, (c + 1) * PAD)
        hat, _ = normal(ex[rows, :])
        ea[rows, :] = (hat * egain[0:1] + eoff[0:1]).astype(BF16)
        limit = (VIS * wid[clips[c]]) // WIDE
        for g, shard in enumerate((lane, mate)):
            if c == 0 and g == 0:
                own[0].wait()
            if c == 0 and g == 1:
                enc_weight(0).wait_recv()
                for step in range(1, LANES):
                    bias_copy(step).wait_recv()
            if g == 0:
                bq, bv = bias[1:2, 0:half], bias[2:3, 0:half]
            else:
                bq, bv = biases[shard, 1:2, 0:half], biases[shard, 2:3, 0:half]
            eqkv[g, 0, rows] = (nt(ea[rows, :], w_qkv[g, 0]) + bq).astype(BF16)
            eqkv[g, 1, rows] = nt(ea[rows, :], w_qkv[g, 1]).astype(BF16)
            eqkv[g, 2, rows] = (nt(ea[rows, :], w_qkv[g, 2]) + bv).astype(BF16)
            p, out, _ = attend(
                eqkv[g, 0, rows], eqkv[g, 1, rows], eqkv[g, 2, rows], emarks, eones,
                lambda s: jnp.where(key < limit, s, floor), ENC_SCALE,
            )
            ep[g, c] = p
            eo[g, rows] = out
        if c == 0:
            own[1].wait()
            enc_weight(1).wait_recv()
        for i in range(blocks):
            cut = slice(i * 256, (i + 1) * 256)
            t = nn(eo[0, rows], w_proj[0, :, cut]) + nn(eo[1, rows], w_proj[1, :, cut])
            epart[rows, cut] = t
            esend[rows, cut] = t.astype(BF16)
            give_part(i, 1 - c).start()
    pass_on(0)
    clip_gradient()
    own[2].wait()
    enc_weight(2).wait_recv()

    def give_last(i):
        cut = span(i, 256)
        return far(
            esend2.at[:, cut], erecv2.at[:, cut], ex2_s.at[i], ex2_r.at[i], {"tensor": over}
        )

    for c in (1, 0):
        rows = slice(c * PAD, (c + 1) * PAD)
        for i in range(blocks):
            give_part(i, c).wait_recv()
        t = ex[rows, :] + epart[rows, :] + erecv[rows, :].astype(F32) + eoff[2:3]
        ex1[rows, :] = t
        hat, _ = normal(t)
        eu[rows, :] = (hat * egain[1:2] + eoff[1:2]).astype(BF16)
        for g, shard in enumerate((lane, mate)):

            def enc_ff(i, g=g, shard=shard, rows=rows):
                cut = span(i, 256)
                h = nn(eu[rows, :], w_up[g, :, cut]) + biases[shard, 0:1, cut]
                act, slope = gelu_both(h)
                ey[g, rows, cut] = act.astype(BF16)
                egp[g, rows, cut] = slope.astype(BF16)

            loop(w_up.shape[2] // 256, enc_ff, unroll=3)
        if c == 1:
            own[3].wait()
            enc_weight(3).wait_recv()
        for i in range(blocks):
            cut = slice(i * 256, (i + 1) * 256)
            t = nn(ey[0, rows], w_down[0, :, cut]) + nn(ey[1, rows], w_down[1, :, cut])
            if c == 0:
                eown[:, cut] = t
            else:
                esend2[:, cut] = t.astype(BF16)
                give_last(i).start()
        if c == 1:
            for n in (1, 2, 3):
                dec_weight(n, 0).start()
            pass_last(0)
    outs = [
        pltpu.make_async_copy(src, dst, out_s.at[n])
        for n, (src, dst) in enumerate(
            (
                (ex.at[0:PAD, :], o_x), (ex1, o_x1), (ea, o_a), (eu, o_u), (ey, o_y), (egp, o_gp),
                (eqkv, o_qkv), (ep, o_p), (eo, o_o), (w_qkv.at[1], o_w), (w_proj.at[1], o_wproj),
                (w_up.at[1], o_wup), (w_down.at[1], o_wdown),
            )
        )
    ]
    for copy in outs:
        copy.start()
    loop(GRID // PAD, places, unroll=2)
    for i in range(blocks):
        give_last(i).wait_recv()

    e_ref[...] = (ex1[0:PAD, :] + eown[...] + erecv2[...].astype(F32) + eoff[3:4]).astype(BF16)
    vec = evec[...].astype(F32)
    m = (nn(e_ref[...], ew[...]) + vec[0:1]).astype(BF16)
    gain = dgains[...].astype(F32)
    offsets = doffs[...].astype(F32)

    def start(i):
        r = span(i, PAD)
        oh = hot[r, :]
        hit = jnp.sum(oh.astype(F32), -1, keepdims=True)
        x = jnp.where(hit > 0, nn(oh, m), vec[1:2]).astype(BF16).astype(F32) + x0[r, :]
        x0[r, :] = x
        hat, _ = normal(x)
        a[r, :] = (hat * gain[0:1] + offsets[0:1]).astype(BF16)

    loop(GRID // PAD, start, unroll=2)
    arrived(0)

    def dec_bias(row, size):
        return jnp.concatenate([biases[k, row : row + 1, 0:size] for k in range(LANES)], 1)

    acts[0] = (nn(a[...], qkv[0]) + dec_bias(4, 128)).astype(BF16)
    acts[1] = nn(a[...], qkv[1]).astype(BF16)
    acts[2] = (nn(a[...], qkv[2]) + dec_bias(5, 128)).astype(BF16)
    pass_on(1)
    pass_on(2)
    marks = head_marks(128, DEC_SIZE, BF16)
    marks32 = head_marks(128, DEC_SIZE, F32)
    dim = lax.broadcasted_iota(jnp.int32, (128, 1), 0)
    rows32 = [
        ((dim >= h * DEC_SIZE) & (dim < (h + 1) * DEC_SIZE)).astype(F32) for h in range(len(marks))
    ]

    ones = ones_per_head(PAD, marks)

    def attention(i):
        r = span(i, PAD)
        row_slot = slot_of(lax.broadcasted_iota(jnp.int32, (PAD, PAD), 0) + i * PAD)
        key_slot = slot_of(lax.broadcasted_iota(jnp.int32, (PAD, PAD), 1) + i * PAD)
        allowed = (code_of(row_slot) == code_of(key_slot)) & (key_slot < GRID_ROWS * width)
        for g in range(DD // 128):
            c = slice(g * 128, (g + 1) * 128)
            probs[i, :, g * 512 : (g + 1) * 512], o[r, c], inverse[r, c] = attend(
                acts[0, r, c], acts[1, r, c], acts[2, r, c], marks, ones,
                lambda s: jnp.where(allowed, s, NEG * LOG2E), DEC_SCALE,
            )

    loop(GRID // PAD, attention, unroll=4)
    pass_last(1)
    pass_last(2)
    pass_on(3)
    arrived(1)

    def mix(i):
        r = span(i, 256)
        x = x0[r, :] + nn(o[r, :], proj[...]) + offsets[2:3]
        x1[r, :] = x
        hat, _ = normal(x)
        un = hat * gain[1:2] + offsets[1:2]
        u[r, :] = un.astype(BF16)
        ut[:, r] = jnp.transpose(un.astype(BF16))

    loop(2, mix)
    pass_last(3)
    arrived(2)

    def ff(i):
        c = span(i, 256)
        h = nn(u[...], up[:, c]) + biases[lax.div(i, 2), 3:4, span(lax.rem(i, 2), 256)]
        act, slope = gelu_both(h)
        y[:, c] = act.astype(BF16)
        gp[:, c] = slope.astype(BF16)

    loop(up.shape[1] // 256, ff, unroll=4)
    arrived(3)
    def out(i):
        c = span(i, 256)
        acc[:, c] = nn(y[...], down[:, c])

    loop(2, out)
    full = ((acc[...] + x1[...] + offsets[3:4]) * valid_rows()).astype(BF16)
    turned = tn(full, perm[...]).astype(BF16)
    for k in range(devices):
        dsend[k] = turned[k * dsend.shape[1] : (k + 1) * dsend.shape[1]]

    def decoded_copy(step):
        peer, spot = group_peer(step)
        return far(dsend.at[peer], dec_out.at[me], do_s.at[step], do_r.at[step], spot)

    for step in range(1, devices):
        decoded_copy(step).start()
    dec_out[me] = dsend[me]

    def ff_back(shard):
        for side in range(2):
            c = span(2 * shard + side, 256)
            d_down = nn(gt[...], y[:, c]).astype(BF16)
            dh = nt(gb[...], down[c, :]) * gp[:, c].astype(F32)
            d_upb[:, c] = colsum(dh)
            du = dh.astype(BF16)
            gp[:, c] = du
            d_up = nn(ut[...], du).astype(BF16)
            for block in range(GRID // CH):
                rows = slice(block * CH, (block + 1) * CH)
                h, top, col = tile_of(4 * block + side)
                buf[shard, h, top : top + CH, col : col + 256] = d_up[rows]
                h, top, col = tile_of(4 * block + 2 + side)
                buf[shard, h, top : top + CH, col : col + 256] = d_down[rows]

    def early_core(which):
        shard, land = ((mate, e_rc), (cross, e_rcy))[which]
        return far(
            buf.at[shard, :, 0:EARLY_ROWS, :], land, e_s.at[which], e_r.at[which], {"tensor": mate}
        )

    def early_x(which):
        return far(
            buf.at[(over, lane)[which], 1 - sec, 0:EARLY_ROWS, :], e_rx.at[which],
            e_s.at[2 + which], e_r.at[2 + which], {"section": 1 - sec},
        )

    def early_y():
        return far(
            buf.at[over, sec, 0:EARLY_ROWS, :], e_ry, e_s.at[4], e_r.at[4], {"tensor": over}
        )

    def early_add(shard, land):
        def body(i):
            r = span(i, CH)
            buf[shard, :, r, :] = buf[shard, :, r, :] + land[:, r, :]

        loop(EARLY_ROWS // CH, body)

    def early_half(shard, land):
        buf[shard, sec, 0:EARLY_ROWS, :] = buf[shard, sec, 0:EARLY_ROWS, :] + land

    def ff_step(i):
        ff_back(jnp.where(i == 0, cross, jnp.where(i == 1, over, jnp.where(i == 2, mate, lane))))

        @pl.when(i == 1)
        def _():
            early_core(1).start()

        @pl.when(i == 2)
        def _():
            early_core(0).start()

    loop(LANES, ff_step)
    early_core(1).wait_recv()
    early_add(over, e_rcy)
    early_x(0).start()

    def ff_in(i):
        c = span(i, 256)
        acc[:, c] = nt(gp[...], up[c, :])

    loop(2, ff_in)
    early_core(0).wait_recv()
    early_add(lane, e_rc)
    early_x(1).start()

    def mix_back(i):
        r = span(i, 256)
        hat, scale = normal(x1[r, :])
        da = acc[r, :]
        dx = g32[r, :] + normal_back(da, hat, scale, gain[1:2])
        d_small[1:2, :] += colsum(da * hat)
        d_small[3:4, :] += colsum(da)
        d_small[4:5, :] += colsum(dx)
        g32[r, :] = dx
        dxb = dx.astype(BF16)
        gb[r, :] = dxb
        u[r, :] = nt(dxb, proj[...]).astype(BF16)

    loop(2, mix_back)
    d_proj = tn(o[...], gb[...]).astype(BF16)
    for block in range(GRID // CH):
        h, top, col = tile_of(33 + 2 * block)
        side = slice(block // 2 * 128, (block // 2 + 1) * 128)
        for k in range(LANES):
            row = k * 128 + block % 2 * CH
            buf[k, h, top : top + CH, col + 128 : col + 256] = d_proj[row : row + CH, side]

    def attention_back(i):
        r = span(i, PAD)
        for k in range(DD // 128):
            c = slice(k * 128, (k + 1) * 128)
            acts[0, r, c], acts[1, r, c], acts[2, r, c] = attend_back(
                acts[0, r, c], acts[1, r, c], acts[2, r, c],
                probs[i, :, k * 512 : (k + 1) * 512], o[r, c], inverse[r, c], u[r, c],
                marks, marks32, rows32, ones, DEC_SCALE,
            )

    loop(GRID // PAD, attention_back, unroll=4)
    early_x(0).wait_recv()
    early_half(over, e_rx[0])
    early_y().start()
    d_qvb[0:1, :] = colsum(acts[0].astype(F32))
    d_qvb[1:2, :] = colsum(acts[2].astype(F32))

    def project_back(i):
        c = span(i, 256)
        acc[:, c] = (
            nt(acts[0], qkv[0, c, :]) + nt(acts[1], qkv[1, c, :]) + nt(acts[2], qkv[2, c, :])
        )

    loop(2, project_back)
    gt[...] = jnp.transpose(a[...])
    for j in range(3):
        d_qkv = nn(gt[...], acts[j]).astype(BF16)
        for block in range(GRID // CH):
            h, top, col = tile_of(32 + 2 * block + j // 2)
            col = col + j % 2 * 128
            rows = slice(block * CH, (block + 1) * CH)
            for k in range(LANES):
                buf[k, h, top : top + CH, col : col + 128] = d_qkv[rows, k * 128 : (k + 1) * 128]

    def start_back(i):
        r = span(i, PAD)
        hat, scale = normal(x0[r, :])
        da = acc[r, :]
        dx = g32[r, :] + normal_back(da, hat, scale, gain[0:1])
        d_small[0:1, :] += colsum(da * hat)
        d_small[2:3, :] += colsum(da)
        dg = dx.astype(BF16)
        gb[r, :] = dg
        hit = jnp.sum(hot[r, :].astype(F32), -1, keepdims=True)
        d_small[7:8, :] += colsum(jnp.where(hit > 0, 0.0, dg.astype(F32)))

    loop(GRID // PAD, start_back, unroll=2)
    dm = tn(hot[...], gb[...])
    d_small[6:7, :] = colsum(dm)
    dmb = dm.astype(BF16)
    d_enc[...] = nt(dmb, ew[...]).astype(BF16)
    d_ew = tn(e_ref[...], dmb).astype(BF16)
    for k in range(LANES):
        for h in range(2):
            top = k * 192 + h * 64
            buf[k, h, 512:576, 0:512] = d_ew[top : top + 64]
            buf[k, h, 512:576, 512:768] = d_ew[k * 192 + 128 : (k + 1) * 192, h * 256 : (h + 1) * 256]

    early_x(1).wait_recv()
    early_half(lane, e_rx[1])
    early_y().wait_recv()
    early_half(lane, e_ry[...])
    later = pl.ds(EARLY_ROWS, DEC_ROWS - EARLY_ROWS)
    rest = [pltpu.make_async_copy(buf.at[lane], o_dec.at[lane], out_s.at[13])] + [
        pltpu.make_async_copy(buf.at[k, :, later, :], o_dec.at[k, :, later, :], out_s.at[14 + n])
        for n, k in enumerate((mate, over, cross))
    ]
    for copy in rest:
        copy.start()
    for copy in outs + rest:
        copy.wait()
    for which in range(2):
        early_core(which).wait_send()
        early_x(which).wait_send()
    early_y().wait_send()
    for n in range(4):
        enc_weight(n).wait_send()
        for kind in range(5):
            dec_weight(n, kind).wait_send()
    for step in range(1, LANES):
        bias_copy(step).wait_send()
    for i in range(blocks):
        give_part(i, 0).wait_send()
        give_part(i, 1).wait_send()
        give_last(i).wait_send()
    for step in range(1, devices):
        decoded_copy(step).wait()


def forward_call(args, half, hid, dff):
    dma = lambda *s: pltpu.SemaphoreType.DMA(s)
    vm = lambda dtype, *shape: pltpu.VMEM(shape, dtype)
    rows = 2 * PAD
    keys = PAD * half // ENC_SIZE
    devices = 2 * LANES
    slab = DD // devices
    kept = [
        ((PAD, D), F32), ((rows, D), F32), ((rows, D), BF16), ((rows, D), BF16),
        ((2, rows, hid), BF16), ((2, rows, hid), BF16), ((2, 3, rows, half), BF16),
        ((2, 2, PAD, keys), BF16), ((2, rows, half), BF16),
        ((3, half, D), BF16), ((half, D), BF16), ((D, hid), BF16), ((hid, D), BF16),
        ((LANES, 2, DEC_ROWS, D), BF16),
    ]
    made = [
        ((PAD, D), BF16), ((2, DD), F32), ((1, dff), F32), ((8, DD), F32),
        ((devices, slab, GRID), BF16),
    ]
    return pl.pallas_call(
        forward_and_decoder,
        out_shape=[jax.ShapeDtypeStruct(s, d) for s, d in kept + made],
        in_specs=[SM, SM, SM] + [VM] * 8 + [ANY] * 9 + [VM] * 5,
        out_specs=[ANY] * len(kept) + [VM] * len(made),
        scratch_shapes=[
            vm(BF16, 2, 3, half, D), vm(BF16, 2, half, D), vm(BF16, 2, D, hid), vm(BF16, 2, hid, D),
            vm(F32, 8, D), vm(F32, LANES, 8, D),
            vm(BF16, 3, DD, DD), vm(BF16, DD, DD), vm(BF16, DD, dff), vm(BF16, dff, DD),
            vm(F32, rows, D), vm(BF16, rows, D), vm(BF16, rows, D), vm(BF16, 2, rows, hid),
            vm(BF16, 2, rows, hid), vm(BF16, 2, 3, rows, half), vm(BF16, 2, 2, PAD, keys),
            vm(BF16, 2, rows, half), vm(F32, rows, D), vm(F32, rows, D), vm(BF16, rows, D),
            vm(BF16, rows, D), vm(BF16, PAD, D), vm(BF16, PAD, D), vm(F32, PAD, D),
            vm(BF16, GRID, DD), vm(F32, GRID, DD), vm(F32, GRID, DD), vm(BF16, GRID, DD),
            vm(BF16, 3, GRID, DD), vm(BF16, GRID // PAD, PAD, DHEADS * PAD), vm(BF16, GRID, DD),
            vm(F32, GRID, DD),
            vm(BF16, GRID, DD), vm(BF16, DD, GRID), vm(BF16, GRID, dff), vm(BF16, GRID, dff),
            vm(F32, GRID, DD), vm(BF16, GRID, DD), vm(BF16, DD, GRID), vm(F32, GRID, DD),
            vm(BF16, PAD, D), vm(BF16, GRID, PAD), vm(BF16, GRID, GRID),
            vm(BF16, LANES, 2, DEC_ROWS, D),
            vm(BF16, devices, slab, GRID), *[vm(BF16, 2, EARLY_ROWS, D)] * 3, vm(BF16, EARLY_ROWS, D),
            dma(8), dma(17), pltpu.SemaphoreType.DMA, dma(4), dma(4), dma(LANES), dma(LANES),
            dma(20), dma(20), dma(6), dma(6), dma(3), dma(3), dma(devices), dma(devices),
            dma(5), dma(5),
        ],
        compiler_params=pltpu.CompilerParams(
            collective_id=0, has_side_effects=True, vmem_limit_bytes=VMEM_LIMIT
        ),
    )(*args)


def add(x, y):
    return x + y


def backward_and_sums(
    d_enc, gains,
    h_u, h_y, h_gp, h_down0, h_down1, h_up0, h_up1,
    h_x, h_x1, h_a, h_qkv, h_p, h_o, h_w0, h_w1, h_proj0, h_proj1,
    dec, dec_qvb, dec_upb, dec_small,
    total, emb, dx_out,
    gb, ut, part, send, recv, du, gx, dx1, d_o, d_acts, own, send1, recv1, dx32, dx,
    d_upb, d_qvb, d_small,
    acc, yacc, enc_mate, out, rcy, ry, land_x, land_l, land_r, small32, small,
    u, y, gp, down0, down1, up0, up1, x, x1, a, qkv, p, o, w0, w1, proj0, proj1, fetch_s,
    load_s, flush_s, ex_s, ex_r,
    core_s, core_r, corey_s, corey_r, y_s, y_r, x_s, x_r, z_s, zl_r, zr_r,
    bl_s, br_s, b_r, a_s, a_r, emb_s, emb_r, dx_s, dx_r,
):
    sec = lax.axis_index("section")
    lane = lax.axis_index("tensor")
    pos = lax.axis_index("dp")
    count = lax.axis_size("dp")
    mate = lane + 1 - 2 * lax.rem(lane, 2)
    over = lax.rem(lane + 2, LANES)
    cross = lax.rem(mate + 2, LANES)
    first = pos == 0
    last = pos == count - 1
    me = sec * LANES + lane
    devices = 2 * LANES

    def group_peer(step):
        peer = lax.rem(me + step, devices)
        return peer, {"section": lax.div(peer, LANES), "tensor": lax.rem(peer, LANES)}

    barrier = pltpu.get_barrier_semaphore()
    for step in range(1, devices):
        pl.semaphore_signal(barrier, inc=1, device_id_type=MESH, device_id=group_peer(step)[1])

    @pl.when(pos > 0)
    def _():
        pl.semaphore_signal(barrier, inc=1, device_id={"dp": pos - 1}, device_id_type=MESH)

    @pl.when(pos < count - 1)
    def _():
        pl.semaphore_signal(barrier, inc=1, device_id={"dp": pos + 1}, device_id_type=MESH)

    loads = [
        pltpu.make_async_copy(dec.at[lane], acc.at[:, 0:DEC_ROWS, :], load_s.at[0]),
        pltpu.make_async_copy(
            dec.at[over, :, EARLY_ROWS:DEC_ROWS, :], yacc.at[:, 0 : DEC_ROWS - EARLY_ROWS, :],
            load_s.at[1],
        ),
    ]
    for load in loads:
        load.start()
    fetches = [
        pltpu.make_async_copy(src, dst, fetch_s.at[n])
        for n, (src, dst) in enumerate(
            (
                (h_u, u), (h_y, y), (h_gp, gp), (h_down0, down0), (h_down1, down1), (h_up0, up0),
                (h_up1, up1), (h_x, x), (h_x1, x1), (h_a, a), (h_qkv, qkv), (h_p, p), (h_o, o),
                (h_w0, w0), (h_w1, w1), (h_proj0, proj0), (h_proj1, proj1),
            )
        )
    ]
    for fetch in fetches:
        fetch.start()
    small32[...] = jnp.zeros_like(small32)
    d_small[...] = jnp.zeros_like(d_small)
    gb[0:PAD, :] = d_enc[...]
    ends = jnp.where(first, 0, 1) + jnp.where(last, 0, 1)
    pl.semaphore_wait(barrier, devices - 1 + ends)

    gain = gains[...].astype(F32)
    width = w0.shape[1]
    marks = head_marks(width, ENC_SIZE, BF16)
    marks32 = head_marks(width, ENC_SIZE, F32)
    ones = ones_per_head(PAD, marks)

    def rows(k, size=CH):
        return pl.ds(pl.multiple_of(k * size, size), size)

    def give_enc():
        return far(d_enc, gb.at[PAD : 2 * PAD, :], ex_s.at[0], ex_r.at[0], {"tensor": over})

    def give_part(i, half):
        cut = rows(i, 256)
        n = 1 + 2 * i + half
        return far(
            send.at[(1 - half) * PAD : (2 - half) * PAD, cut],
            recv.at[half * PAD : (half + 1) * PAD, cut],
            ex_s.at[n], ex_r.at[n], {"tensor": over},
        )

    def give_last(i):
        cut = rows(i, 256)
        return far(send1.at[:, cut], recv1.at[:, cut], ex_s.at[7 + i], ex_r.at[7 + i], {"tensor": over})

    def ff_back(g, i, down):
        c = rows(i, 256)
        d_down = tn(y[g, :, c], gb[...]).astype(BF16)
        dh = nt(gb[...], down[c, :]) * gp[g, :, c].astype(F32)
        d_upb[g, :, c] = colsum(dh)
        dub = dh.astype(BF16)
        du[g, :, c] = dub
        d_up = nn(ut[...], dub).astype(BF16)
        if g == 0:
            acc[1, pl.ds(pl.multiple_of(A_TOP + i * 256, 64), 256), :] = d_down
            acc[0, A_TOP:B_TOP, c] = d_up
        else:
            enc_mate[1, c, :] = d_down
            enc_mate[0, 0:ENC_A, c] = d_up

    def ff_in(i):
        c = rows(i, 256)
        t = nt(du[0], up0[c, :]) + nt(du[1], up1[c, :])
        part[:, c] = t
        send[:, c] = t.astype(BF16)
        give_part(i, 0).start()
        give_part(i, 1).start()

    def norm_two():
        for fetch in fetches[7:]:
            fetch.wait()
        for k in range(D // 256):
            give_part(k, 0).wait_recv()
            give_part(k, 1).wait_recv()

        def body(j):
            r = rows(j, 64)
            da = part[r, :] + recv[r, :].astype(F32)
            hat, scale = normal(x1[r, :])
            g = gb[r, :].astype(F32)
            d = g + normal_back(da, hat, scale, gain[1:2])
            gx[r, :] = d.astype(BF16)
            dx1[r, :] = d

            @pl.when(j < 2)
            def _():
                d_small[1:2, :] += colsum(da * hat)
                d_small[3:4, :] += colsum(da)
                d_small[4:5, :] += colsum(d)
                d_small[5:6, :] += colsum(g)

        loop(2 * PAD // 64, body)

    def attention(g, c):
        if c == 0:
            d_proj = tn(o[g], gx[...]).astype(BF16)
            if g == 0:
                acc[1, B_TOP + width : S_TOP, :] = d_proj
            else:
                enc_mate[1, ENC_A + width : ENC_A + 2 * width, :] = d_proj
            d_o[...] = nt(gx[...], (proj0, proj1)[g][...]).astype(BF16)
        r = slice(c * PAD, (c + 1) * PAD)
        d_acts[g, 0, r], d_acts[g, 1, r], d_acts[g, 2, r] = attend_back(
            qkv[g, 0, r], qkv[g, 1, r], qkv[g, 2, r], p[g, c], o[g, r], 1.0 / nn(p[g, c], ones),
            d_o[r, :], marks, marks32, None, ones, ENC_SCALE,
        )
        if c == 1:
            d_qvb[g, 0:1, :] = colsum(d_acts[g, 0].astype(F32))
            d_qvb[g, 1:2, :] = colsum(d_acts[g, 2].astype(F32))

    def project_in(i):
        c = rows(i, 256)
        t = 0.0
        for g, w in enumerate((w0, w1)):
            for j in range(3):
                t += nn(d_acts[g, j], w[j, :, c])
        own[:, c] = t[:PAD]
        send1[:, c] = t[PAD:].astype(BF16)
        give_last(i).start()

    def project_grad(g):
        for j in range(3):
            row = (j % 2) * width
            d = tn(d_acts[g, j], a[...]).astype(BF16)
            if g == 0:
                acc[j // 2, B_TOP + row : B_TOP + row + width, :] = d
            else:
                enc_mate[j // 2, ENC_A + row : ENC_A + row + width, :] = d

    def norm_one():
        for k in range(D // 256):
            give_last(k).wait_recv()

        def body(j):
            r = rows(j, 64)
            da = own[r, :] + recv1[r, :].astype(F32)
            hat, scale = normal(x[r, :])
            d_small[0:1, :] += colsum(da * hat)
            d_small[2:3, :] += colsum(da)
            dx32[r, :] = dx1[r, :] + normal_back(da, hat, scale, gain[0:1])

        loop(PAD // 64, body)
        turned = jnp.transpose(dx32[...])
        cut = D // devices
        for k in range(devices):
            dx[k] = turned[k * cut : (k + 1) * cut, 0:VIS].astype(BF16)
        for r in range(LANES):
            small32[r, 8:9, 0:512] = dec_upb[:, r * 512 : (r + 1) * 512]
            small32[r, 9:10, 0:128] = dec_qvb[0:1, r * 128 : (r + 1) * 128]
            small32[r, 9:10, 128:256] = dec_qvb[1:2, r * 128 : (r + 1) * 128]
            small32[r, 0:8, 0:512] = dec_small[...]
            small32[r, 16:24, :] = d_small[...]
        for g, shard in enumerate((lane, mate)):
            small32[shard, 10:11, :] = d_upb[g]
            small32[shard, 11:12, 0:192] = d_qvb[g, 0:1]
            small32[shard, 11:12, 256:448] = d_qvb[g, 1:2]
        for r in range(LANES):
            for h in range(2):
                small[r, h] = small32[r, h * SMALL : (h + 1) * SMALL].astype(BF16)
        acc[:, S_TOP : S_TOP + SMALL, :] = small[lane]
        yacc[:, DEC_ROWS - EARLY_ROWS :, :] = small[over]
        core_copy(LATE, small.at[mate], SMALL).start()
        corey_copy(LATE, small.at[cross], SMALL).start()
        for step in range(1, devices):
            dx_copy(step).start()
        dx_out[me] = dx[me]

    def core_enc(lo, hi):
        def body(m):
            block = block_of(m)

            @pl.when((block >= lo) & (block < hi))
            def _():
                src = pl.ds(pl.multiple_of(block * CH - DEC_ROWS, CH), CH)
                core_copy(m, enc_mate.at[:, src, :]).start()

        loop(ALL_K, body)

    def first_piece():
        for fetch in fetches[:7]:
            fetch.wait()
        ut[...] = jnp.transpose(u[...])
        give_enc().wait_recv()

    def ff_step(k):
        for g, down in enumerate((down0, down1)):
            @pl.when(lax.rem(k, 2) == g)
            def _(g=g, down=down):
                ff_back(g, lax.div(k, 2), down)

    def run_pieces(n):
        def several(low, high, body):
            begin = sum(jnp.where(n > t, 1, 0) for t in PIECES[low:high])
            end = sum(jnp.where(n >= t, 1, 0) for t in PIECES[low:high])
            lax.fori_loop(begin, end, lambda k, c: (body(k), c)[1], 0)

        def single(k, body):
            @pl.when(n == PIECES[k])
            def _():
                body()

        single(0, first_piece)
        several(1, 7, ff_step)
        single(7, lambda: core_enc(DEC_K, DEC_K + ENC_A // CH))
        several(8, 11, ff_in)
        single(11, norm_two)
        for k in range(4):
            single(12 + k, lambda k=k: attention(k // 2, k % 2))
        several(16, 19, project_in)
        for g in range(2):
            single(19 + g, lambda g=g: project_grad(g))
        single(21, lambda: core_enc(DEC_K + ENC_A // CH, B_K))
        single(22, norm_one)

    def dx_copy(step):
        peer, place = group_peer(step)
        return far(dx.at[peer], dx_out.at[me], dx_s.at[step], dx_r.at[step], place)

    def emb_copy(step):
        return far(
            out.at[:, pl.ds(512, CH), :], emb.at[lane], emb_s.at[step], emb_r.at[step],
            {"tensor": lax.rem(lane + step, LANES)},
        )

    def block_of(m):
        shift = 0
        for k in range(1, ALL_K):
            if ORDER[k] - k != ORDER[k - 1] - k + 1:
                shift = jnp.where(m >= k, ORDER[k] - k, shift)
        return m + shift

    def is_dec(m):
        return (block_of(m) < DEC_K) & (m >= EARLY)

    def at(m, size=CH):
        return pl.ds(pl.multiple_of(block_of(m) * CH, CH), size)

    def slot(m, size=CH):
        return pl.ds(pl.multiple_of(m * CH, CH), size)

    def y_at(m, size=CH):
        return pl.ds(pl.multiple_of((jnp.minimum(block_of(m), DEC_K) - EARLY) * CH, CH), size)

    def core_copy(m, src, size=CH):
        return far(src, out.at[:, at(m, size), :], core_s.at[m], core_r.at[m], {"tensor": mate})

    def corey_copy(m, src, size=CH):
        return far(src, rcy.at[:, y_at(m, size), :], corey_s.at[m], corey_r.at[m], {"tensor": mate})

    def y_copy(m, size=CH):
        cut = y_at(m, size)
        return far(
            yacc.at[:, cut, :], ry.at[:, cut, :], y_s.at[m], y_r.at[m], {"tensor": over}
        )

    def x_copy(m, size=CH):
        return far(
            acc.at[1 - sec, at(m, size), :], land_x.at[0, slot(m, size), :], x_s.at[m], x_r.at[m],
            {"section": 1 - sec},
        )

    def xc_copy(m):
        return far(
            acc.at[:, at(m), :], land_x.at[:, slot(m), :], x_s.at[m], x_r.at[m],
            {"section": 1 - sec},
        )

    def z_copy(m, whole, right, size=CH):
        land = land_l if right else land_r
        if whole:
            src, dst = acc.at[:, at(m), :], land.at[:, slot(m), :]
        else:
            src, dst = acc.at[sec, at(m, size), :], land.at[0, slot(m, size), :]
        landed = zl_r if right else zr_r
        return far(src, dst, z_s.at[m], landed.at[m], {"dp": pos + 1 if right else pos - 1})

    def b_copy(m, whole, right, size=CH):
        place = out.at[:, at(m), :] if whole else out.at[sec, at(m, size), :]
        sent = br_s if right else bl_s
        return far(place, place, sent.at[m], b_r.at[m], {"dp": pos + 1 if right else pos - 1})

    def a_copy(m, size=CH):
        place = out.at[sec, at(m, size), :]
        return far(place, place, a_s.at[m], a_r.at[m], {"section": 1 - sec})

    def a_wait(m, size=CH):
        place = out.at[1 - sec, at(m, size), :]
        far(place, place, a_s.at[m], a_r.at[m], {"section": 1 - sec}).wait_recv()

    give_enc().start()

    def start_core(m):
        @pl.when(is_dec(m))
        def _():
            core_copy(m, dec.at[mate, :, at(m), :]).start()
            corey_copy(m, dec.at[cross, :, at(m), :]).start()

    loop(ALL_K, start_core)
    for load in loads:
        load.wait()

    def join_core(m, size):
        core_copy(m, out.at[:, at(m, size), :], size).wait_recv()
        acc[:, at(m, size), :] = add(acc[:, at(m, size), :], out[:, at(m, size), :])

    def join_core_y(m, size):
        corey_copy(m, rcy.at[:, y_at(m, size), :], size).wait_recv()
        yacc[:, y_at(m, size), :] = add(yacc[:, y_at(m, size), :], rcy[:, y_at(m, size), :])
        y_copy(m, size).start()

    def stage_c(m):
        @pl.when((m >= EARLY) & (m != LATE))
        def _():
            join_core(m, CH)

            @pl.when(is_dec(m))
            def _():
                join_core_y(m, CH)

        @pl.when(m == LATE)
        def _():
            join_core(m, SMALL)
            join_core_y(m, SMALL)

    def flush(m):
        return pltpu.make_async_copy(
            out.at[:, at(m), :], total.at[:, at(m), :], flush_s.at[m]
        )

    def finished(m):
        flush(m).start()

        @pl.when(block_of(m) == DEC_K - 1)
        def _():
            for step in range(1, LANES):
                emb_copy(step).start()
            emb[lane] = out[:, 512 : 512 + CH, :]

    def line_of(root, whole, size=CH):
        left = pos < root
        right = pos > root
        here = pos == root
        reach = max(root, count - 1 - root)
        level = jnp.where(left, pos, jnp.where(right, count - 1 - pos, reach))
        dist = jnp.where(left, root - pos, pos - root)

        def view(ref, m):
            return ref.at[:, at(m), :] if whole else ref.at[sec, at(m, size), :]

        def landed(ref, m):
            return ref.at[:, slot(m), :] if whole else ref.at[0, slot(m, size), :]

        def hop(m, rightward):
            return z_copy(m, whole, rightward, size)

        def back_hop(m, rightward):
            return b_copy(m, whole, rightward, size)

        def outer(m):
            @pl.when(left & first)
            def _():
                hop(m, True).start()

            @pl.when(right & last)
            def _():
                hop(m, False).start()

        def inward(m):
            @pl.when(left & (pos > 0))
            def _():
                hop(m, True).wait_recv()
                view(acc, m)[...] = add(view(acc, m)[...], landed(land_l, m)[...])
                hop(m, True).start()

            @pl.when(right & (pos < count - 1))
            def _():
                hop(m, False).wait_recv()
                view(acc, m)[...] = add(view(acc, m)[...], landed(land_r, m)[...])
                hop(m, False).start()

            @pl.when(here)
            def _():
                total = view(acc, m)[...].astype(F32)
                if root > 0:
                    hop(m, True).wait_recv()
                    total = total + landed(land_l, m)[...].astype(F32)
                if root < count - 1:
                    hop(m, False).wait_recv()
                    total = total + landed(land_r, m)[...].astype(F32)
                if whole:
                    view(acc, m)[...] = total.astype(BF16)
                    xc_copy(m).start()
                else:
                    view(out, m)[...] = total.astype(BF16)
                    spread(m)
                    a_copy(m, size).start()

        def spread(m):
            if root > 0:
                back_hop(m, False).start()
            if root < count - 1:
                back_hop(m, True).start()

        def crossed(m):
            xc_copy(m).wait_recv()
            view(out, m)[...] = add(view(acc, m)[...], landed(land_x, m)[...])
            spread(m)
            finished(m)

        def outward(m):
            back_hop(m, False).wait_recv()

            @pl.when(left & (pos > 0))
            def _():
                back_hop(m, False).start()

            @pl.when(right & (pos < count - 1))
            def _():
                back_hop(m, True).start()

            if whole:
                finished(m)
            else:
                a_copy(m, size).start()

        def sent(m):
            @pl.when(jnp.logical_not(here))
            def _():
                hop(m, True).wait_send()

            @pl.when((pos <= root) & (pos > 0))
            def _():
                back_hop(m, False).wait_send()

            @pl.when((pos >= root) & (pos < count - 1))
            def _():
                back_hop(m, True).wait_send()

            if whole:
                @pl.when(here)
                def _():
                    xc_copy(m).wait_send()
            else:
                a_copy(m, size).wait_send()

                @pl.when(crosses_first(m))
                def _():
                    x_copy(m, size).wait_send()

        def crosses_first(m):
            return m >= EARLY if XFIRST else m >= 0

        def set_off(m):
            if whole:
                outer(m)
            else:
                x_copy(m, size).start()

        def set_off_early(m):
            if XFIRST:
                outer(m)
            else:
                set_off(m)

        def add_y(m):
            def joined():
                y_copy(m, size).wait_recv()
                acc[:, at(m, size), :] = add(acc[:, at(m, size), :], ry[:, y_at(m, size), :])

            if size == CH:
                pl.when(is_dec(m))(joined)
            else:
                joined()
            set_off(m)

        def add_x(m):
            @pl.when(crosses_first(m))
            def _():
                x_copy(m, size).wait_recv()
                acc[sec, at(m, size), :] = add(
                    acc[sec, at(m, size), :], land_x[0, slot(m, size), :]
                )
                outer(m)

        def last_half(m):
            a_wait(m, size)
            finished(m)

        base = 1 if whole else 2
        back = base + reach + dist + (1 if whole else 0)
        steps = [(back, jnp.logical_not(here), outward), (base + level, level > 0, inward)]
        if whole:
            steps.append((base + reach + 1, here, crossed))
        else:
            steps += [(back + 1, True, last_half), (2, True, add_x)]
        return steps, sent, add_y, set_off_early

    low_root = (count - 1) // 2
    high_root = min(low_root + 1, count - 1)
    def is_whole(m):
        return (lax.rem(m, 2) == 0) & (m >= WHOLE_LOW) & (m < WHOLE_HIGH)

    roots = (high_root, count - 1, low_root, 0)
    lines = [
        (lambda m, part=part: is_whole(m) & (lax.rem(m, 8) == part), *line_of(root, True))
        for part, root in zip((0, 2, 4, 6), roots)
    ] + [
        (lambda m: jnp.logical_not(is_whole(m)) & (m != LATE), *line_of(low_root, False)),
        (lambda m: m == LATE, *line_of(low_root, False, SMALL)),
    ]

    def finish(m):
        @pl.when((m >= EARLY) & (m != LATE))
        def _():
            core_copy(m, out.at[:, at(m), :]).wait_send()

            @pl.when(is_dec(m))
            def _():
                corey_copy(m, rcy.at[:, y_at(m), :]).wait_send()
                y_copy(m).wait_send()

        @pl.when(m == LATE)
        def _():
            core_copy(m, out.at[:, at(m, SMALL), :], SMALL).wait_send()
            corey_copy(m, rcy.at[:, y_at(m, SMALL), :], SMALL).wait_send()
            y_copy(m, SMALL).wait_send()

        for mine, _, sent, _, _ in lines:
            @pl.when(mine(m))
            def _(sent=sent):
                sent(m)

    def set_off_early(m):
        for mine, _, _, _, set_off in lines:
            @pl.when(mine(m))
            def _(set_off=set_off):
                set_off(m)

    loop(EARLY, set_off_early)
    far_reach = max(max(root, count - 1 - root) for root in roots)
    depth = LAG * (3 + 2 * far_reach) + 1

    def tick(n):
        @pl.when(n <= PIECES[-1])
        def _():
            run_pieces(n)

        for mine, steps, _, add_y, _ in lines:
            m = n - LAG

            @pl.when((m >= EARLY) & (m < ALL_K))
            def _(m=m, mine=mine, add_y=add_y):
                @pl.when(mine(m))
                def _():
                    add_y(m)

            for offset, enabled, stage in steps:
                m = n - LAG * offset

                @pl.when((m >= 0) & (m < ALL_K) & enabled)
                def _(m=m, mine=mine, stage=stage):
                    @pl.when(mine(m))
                    def _():
                        stage(m)

        @pl.when(n < ALL_K)
        def _():
            stage_c(n)

        @pl.when(n >= depth)
        def _():
            finish(n - depth)

    loop(ALL_K + depth, tick)
    loop(ALL_K, lambda m: flush(m).wait())
    for step in range(1, devices):
        dx_copy(step).wait()
    for step in range(1, LANES):
        emb_copy(step).wait()
    give_enc().wait_send()
    for k in range(D // 256):
        give_part(k, 0).wait_send()
        give_part(k, 1).wait_send()
        give_last(k).wait_send()


def backward_call(args, half, hid):
    dma = lambda *s: pltpu.SemaphoreType.DMA(s)
    vm = pltpu.VMEM
    full = ALL_K * CH
    y_half = DEC_ROWS - EARLY_ROWS + SMALL
    k = ALL_K
    rows = 2 * PAD
    cut = D // (2 * LANES)
    specs = [VM, VM] + [ANY] * 18 + [VM] * 3
    return pl.pallas_call(
        backward_and_sums,
        out_shape=[
            jax.ShapeDtypeStruct((2, full, D), BF16),
            jax.ShapeDtypeStruct((LANES, 2, CH, D), BF16),
            jax.ShapeDtypeStruct((2 * LANES, cut, VIS), BF16),
        ],
        in_specs=specs,
        out_specs=[ANY, VM, VM],
        scratch_shapes=[
            vm((rows, D), BF16), vm((D, rows), BF16),
            vm((rows, D), F32), vm((rows, D), BF16), vm((rows, D), BF16),
            vm((2, rows, hid), BF16), vm((rows, D), BF16), vm((rows, D), F32),
            vm((rows, half), BF16), vm((2, 3, rows, half), BF16),
            vm((PAD, D), F32), vm((PAD, D), BF16), vm((PAD, D), BF16), vm((PAD, D), F32),
            vm((2 * LANES, cut, VIS), BF16),
            vm((2, 1, hid), F32), vm((2, 2, half), F32), vm((8, D), F32),
            vm((2, full, D), BF16), vm((2, y_half, D), BF16), vm((2, ENC_A + ENC_B, D), BF16),
            vm((2, full, D), BF16),
            vm((2, y_half, D), BF16), vm((2, y_half, D), BF16),
            *[vm((2, full, D), BF16)] * 3,
            vm((LANES, 32, D), F32), vm((LANES, 2, SMALL, D), BF16),
            *[vm(v.shape, v.dtype) for v in args[2:19]],
            dma(17), dma(2), dma(k), dma(10), dma(10),
            dma(k), dma(k), dma(k), dma(k), dma(k), dma(k),
            dma(k), dma(k), dma(k), dma(k), dma(k),
            dma(k), dma(k), dma(k), dma(k), dma(k), dma(LANES), dma(LANES),
            dma(2 * LANES), dma(2 * LANES),
        ],
        compiler_params=pltpu.CompilerParams(
            collective_id=1, has_side_effects=True, vmem_limit_bytes=VMEM_LIMIT
        ),
    )(*args)


def finish_grads(
    total, emb, decoded, dx, decoded_out, dx_out,
    e_qkv, e_qvb, e_proj, e_up, e_upb, e_down, e_gain, e_off,
    d_qkv, d_qvb, d_proj, d_up, d_upb, d_down, d_gain, d_off, d_ew, d_ev,
):
    half = e_proj.shape[0]
    decoded_out[...] = decoded[...]
    dx_out[...] = dx[...]
    e_up[...] = total[0, A_TOP:B_TOP, :].astype(F32)
    e_down[...] = total[1, A_TOP:B_TOP, :].astype(F32)
    e_qkv[0] = total[0, B_TOP : B_TOP + half, :].astype(F32)
    e_qkv[1] = total[0, B_TOP + half : S_TOP, :].astype(F32)
    e_qkv[2] = total[1, B_TOP : B_TOP + half, :].astype(F32)
    e_proj[...] = total[1, B_TOP + half : S_TOP, :].astype(F32)

    def raw(number):
        h, top, col = tile_of(number)
        return total[h, top : top + CH, col : col + 256]

    def tile(number):
        return raw(number).astype(F32)

    for block in range(GRID // CH):
        rows = slice(block * CH, (block + 1) * CH)
        side = slice(block // 2 * 128, (block // 2 + 1) * 128)
        for k in range(2):
            d_up[rows, k * 256 : (k + 1) * 256] = tile(4 * block + k)
            if block % 2:
                both = jnp.concatenate([raw(4 * block - 2 + k), raw(4 * block + 2 + k)], 0)
                d_down[k * 256 : (k + 1) * 256, side] = jnp.transpose(both).astype(F32)
        one, two = tile(32 + 2 * block), tile(33 + 2 * block)
        d_qkv[0, rows, :] = one[:, 0:128]
        d_qkv[1, rows, :] = one[:, 128:256]
        d_qkv[2, rows, :] = two[:, 0:128]
        d_proj[block % 2 * CH : (block % 2 + 1) * CH, side] = two[:, 128:256]
    for k in range(LANES):
        for h in range(2):
            top = k * 192 + h * 64
            d_ew[top : top + 64, :] = emb[k, h, :, 0:512].astype(F32)
            d_ew[k * 192 + 128 : (k + 1) * 192, h * 256 : (h + 1) * 256] = emb[
                k, h, :, 512:768
            ].astype(F32)
    little = total[0, S_TOP : S_TOP + SMALL, :].astype(F32)
    d_gain[...] = little[0:2, 0:512]
    d_off[...] = little[2:6, 0:512]
    d_ev[...] = little[6:8, 0:512]
    d_upb[...] = little[8, 0:512]
    d_qvb[0:1, :] = little[9:10, 0:128]
    d_qvb[1:2, :] = little[9:10, 128:256]
    e_upb[...] = little[10]
    e_qvb[0:1, :] = little[11:12, 0:192]
    e_qvb[1:2, :] = little[11:12, 256:448]
    little = total[1, S_TOP : S_TOP + SMALL, :].astype(F32)
    e_gain[...] = little[0:2]
    e_off[...] = little[2:6]


def call(kernel, specs, shapes, scratch, args):
    return pl.pallas_call(
        kernel,
        out_shape=[jax.ShapeDtypeStruct(s, d) for s, d in shapes],
        in_specs=specs,
        out_specs=[VM] * len(shapes),
        scratch_shapes=scratch,
        compiler_params=pltpu.CompilerParams(vmem_limit_bytes=VMEM_LIMIT),
    )(*args)


def position_rows():
    quarter = DD // 4
    freq = np.exp(np.arange(quarter, dtype=np.float32) * np.float32(-math.log(10000.0) / quarter))
    angle = np.arange(PAD, dtype=np.float32)[:, None] * freq[None, :].astype(np.float32)
    both = np.concatenate([np.sin(angle), np.cos(angle)], 1).astype(np.float32)
    high = both.astype(jnp.bfloat16)
    low = (both - high.astype(np.float32)).astype(jnp.bfloat16)
    return np.stack([high, low])


def per_device(
    patches, cotangent, widths, visible, window_shift, batch_order,
    encoder_qkv, encoder_qvbias, encoder_proj, encoder_up, encoder_upbias, encoder_down,
    encoder_gains, encoder_offsets,
    decoder_qkv, decoder_qvbias, decoder_proj, decoder_up, decoder_upbias, decoder_down,
    decoder_gains, decoder_offsets, embed_weight, embed_vectors,
):
    qkv0 = encoder_qkv.transpose(1, 2, 0)
    half = qkv0.shape[1]
    hid = encoder_up.shape[1]
    dff = decoder_up.shape[1] * LANES
    flat = patches.transpose(1, 0, 2).reshape(-1, D)
    (
        x, x1, a, u, y, gp, qkv, p, o, qkv1, proj1, up1, down1, dec_buf,
        d_enc, d_dqvb, d_dupb, d_dsmall, out_all,
    ) = forward_call(
        (
            widths, window_shift.T, batch_order, visible, flat, encoder_gains, encoder_offsets,
            encoder_qvbias, encoder_upbias, decoder_qvbias, decoder_upbias,
            qkv0, encoder_proj, encoder_up, encoder_down,
            decoder_qkv.transpose(1, 0, 2), decoder_proj, decoder_up, decoder_down,
            cotangent, embed_weight, embed_vectors, jnp.asarray(position_rows()),
            decoder_gains, decoder_offsets,
        ),
        half, hid, dff,
    )
    total, emb, dx_all = backward_call(
        (
            d_enc, encoder_gains, u, y, gp, encoder_down, down1, encoder_up, up1,
            x, x1, a, qkv, p, o, qkv0, qkv1, encoder_proj, proj1,
            dec_buf, d_dqvb, d_dupb, d_dsmall,
        ),
        half, hid,
    )
    f = lambda *shape: (shape, F32)
    out_all, dx_all, *grads = call(
        finish_grads, [VM] * 4,
        [
            (out_all.shape, BF16), (dx_all.shape, BF16), f(3, half, D), f(2, half), f(half, D), f(D, hid), f(hid), f(hid, D), f(2, D), f(4, D),
            f(3, DD, 128), f(2, 128), f(128, DD), f(DD, 512), f(512), f(512, DD), f(2, DD), f(4, DD),
            f(D, DD), f(2, DD),
        ],
        [], (total, emb, out_all, dx_all),
    )
    grads[0] = grads[0].transpose(2, 0, 1)
    grads[8] = grads[8].transpose(1, 0, 2)
    return (out_all.swapaxes(1, 2), dx_all.swapaxes(1, 2), *grads)


def solution(mesh):
    weights = (
        P(None, None, "tensor"), P(None, "tensor"), P("tensor", None), P(None, "tensor"),
        P("tensor"), P("tensor", None), P(), P(),
    )
    split = P("dp", None, ("section", "tensor"))
    return jax.shard_map(
        per_device,
        mesh=mesh,
        in_specs=(
            P("dp", None, None), P("dp", None, None), P("dp"), P("dp", None), P("dp", None),
            P("dp", None),
        ) + weights + weights + (P(), P()),
        out_specs=(split, split) + weights + weights + (P(), P()),
        check_vma=False,
    )
```

```python
import math

import jax
import jax.numpy as jnp
import numpy as np
from jax import lax
from jax.experimental import pallas as pl
from jax.experimental.pallas import tpu as pltpu
from jax.sharding import PartitionSpec as P

D = 768
HEADS = 12
DD = 512
DHEADS = 16
GRID_ROWS = 64
WIDE = 8
WIN = 4
VIS = 102
CM = 4
GRID = 512
LANES = 4
PAD = 128
EPS = 1e-06
NEG = -10000.0
F32 = jnp.float32
BF16 = jnp.bfloat16
VMEM_LIMIT = 60 * 1024 * 1024

VM = pl.BlockSpec(memory_space=pltpu.VMEM)
SM = pl.BlockSpec(memory_space=pltpu.SMEM)
ANY = pl.BlockSpec(memory_space=pl.ANY)


def nn(a, b):
    return lax.dot_general(a, b, (((1,), (0,)), ((), ())), preferred_element_type=F32)


def nt(a, b):
    return lax.dot_general(a, b, (((1,), (1,)), ((), ())), preferred_element_type=F32)


def tn(a, b):
    return lax.dot_general(a, b, (((0,), (0,)), ((), ())), preferred_element_type=F32)


def loop(count, body, unroll=1):
    def step(i, carry):
        body(i)
        return carry

    lax.fori_loop(0, count, step, 0, unroll=unroll)


def span(i, size):
    return pl.ds(pl.multiple_of(i * size, size), size)


def normal(x):
    center = x - jnp.mean(x, -1, keepdims=True)
    scale = lax.rsqrt(jnp.mean(center * center, -1, keepdims=True) + EPS)
    return center * scale, scale


def normal_back(dy, hat, scale, gain):
    d = dy * gain
    return scale * (
        d - jnp.mean(d, -1, keepdims=True) - hat * jnp.mean(d * hat, -1, keepdims=True)
    )


def gelu_both(h):
    phi = 0.5 * lax.erf(h * math.sqrt(0.5)) + 0.5
    bell = jnp.exp2(h * h * (-0.5 * math.log2(math.e)))
    return h * phi, phi + h * bell * (1.0 / math.sqrt(2.0 * math.pi))


def colsum(x):
    return jnp.sum(x, 0, keepdims=True)


def head_marks(width, size, dtype):
    lane = lax.broadcasted_iota(jnp.int32, (1, width), 1)
    return [((lane >= h * size) & (lane < (h + 1) * size)).astype(dtype) for h in range(width // size)]


def stacked(x, marks):
    return jnp.concatenate([x * m for m in marks], 0)


LOG2E = math.log2(math.e)


def attend(q, k, v, marks, ones, masked, scale):
    keys = k.shape[0]
    s = nt(q, stacked(k, marks))
    parts = []
    for h in range(len(marks)):
        x = masked(s[:, h * keys : (h + 1) * keys] * (scale * LOG2E))
        parts.append(jnp.exp2(x - jnp.max(x, -1, keepdims=True)).astype(BF16))
    e = jnp.concatenate(parts, 1)
    width = q.shape[1]
    if width % 128:
        top, total = nn(e, stacked(v, marks)), nn(e, ones)
    else:
        both = nn(e, jnp.concatenate([stacked(v, marks), ones], 1))
        top, total = both[:, :width], both[:, width:]
    inverse = 1.0 / total
    return e, (top * inverse).astype(BF16), inverse


def attend_back(q, k, v, e, o, inverse, d_out, marks, marks32, rows32, ones, scale):
    keys = k.shape[0]
    width = q.shape[1]
    d_one = d_out.astype(F32) * inverse
    d_two = (d_one * o.astype(F32)).astype(BF16)
    d_one = d_one.astype(BF16)
    if width % 128:
        d_s = nt(d_one, stacked(v, marks)) - nt(d_two, ones)
    else:
        d_s = nt(
            jnp.concatenate([d_one, d_two], 1), jnp.concatenate([stacked(v, marks), -ones], 1)
        )
    dr = (e.astype(F32) * d_s * scale).astype(BF16)
    d_q = nn(dr, stacked(k, marks)).astype(BF16)
    if width % 128:
        d_k_all, d_v_all = tn(dr, q), tn(e, d_one)
        d_k = d_v = 0.0
        for h in range(len(marks)):
            cut = slice(h * keys, (h + 1) * keys)
            d_k += d_k_all[cut] * marks32[h]
            d_v += d_v_all[cut] * marks32[h]
        return d_q, d_k.astype(BF16), d_v.astype(BF16)
    d_k_all = nn(jnp.transpose(q), dr)
    d_v_all = nn(jnp.transpose(d_one), e)
    d_k = d_v = 0.0
    for h in range(len(marks)):
        cut = slice(h * keys, (h + 1) * keys)
        d_k += d_k_all[:, cut] * rows32[h]
        d_v += d_v_all[:, cut] * rows32[h]
    return d_q, jnp.transpose(d_k.astype(BF16)), jnp.transpose(d_v.astype(BF16))


def ones_per_head(keys, marks):
    return jnp.concatenate([jnp.broadcast_to(m, (keys, m.shape[1])) for m in marks], 0)


ENC_SIZE = D // HEADS
ENC_SCALE = ENC_SIZE ** -0.5
DEC_SIZE = DD // DHEADS
DEC_SCALE = DEC_SIZE ** -0.5


CH = 64
DEC_ROWS = 576
ENC_A = 768
ENC_B = 384
DEC_K = DEC_ROWS // CH
B_K = (DEC_ROWS + ENC_A + ENC_B) // CH
ALL_K = B_K + 1
A_TOP = DEC_ROWS
B_TOP = DEC_ROWS + ENC_A
S_TOP = B_TOP + ENC_B
EARLY = 4
XFIRST = True
EARLY_ROWS = EARLY * CH
LAG = 2
ORDER = (0, 1, 2, 3, 9, 10, 11, 12, 13, 14, 4, 15, 16, 17, 18, 5, 6, 19, 21, 20, 8, 22, 23, 24, 25, 27, 26, 7)
PIECES = (0, 2, 2, 2, 2, 2, 2, 2, 3, 3, 3, 10, 12, 12, 13, 13, 14, 14, 15, 15, 15, 16, 20)
LATE = ORDER.index(B_K)
WHOLE_LOW = 6
WHOLE_HIGH = 22
SMALL = 16


def tile_of(number):
    place = number // 3
    return place % 2, place // 2 * CH, number % 3 * 256


MESH = pl.DeviceIdType.MESH


def far(src, dst, send, recv, peer):
    return pltpu.make_async_remote_copy(
        src_ref=src, dst_ref=dst, send_sem=send, recv_sem=recv, device_id=peer, device_id_type=MESH
    )


def forward_and_decoder(
    wid, shifts, order, vis, pat, gains, offs, b_qv, b_up, b_dqv, b_dup,
    h_qkv, h_proj, h_up, h_down, h_dqkv, h_dproj, h_dup, h_ddown,
    cot_hbm, ew, evec, table, dgains, doffs,
    o_x, o_x1, o_a, o_u, o_y, o_gp, o_qkv, o_p, o_o, o_w, o_wproj, o_wup, o_wdown, o_dec,
    d_enc, d_qvb, d_upb, d_small, dec_out,
    w_qkv, w_proj, w_up, w_down, bias, biases, qkv, proj, up, down,
    ex, ea, eu, ey, egp, eqkv, ep, eo, ex1, epart, esend, erecv, esend2, erecv2, eown,
    cot, x0, x1, a, acts, probs, o, inverse, u, ut, y, gp, g32, gb, gt, acc, e_ref, hot, perm, buf, dsend, e_rc, e_rcy, e_rx, e_ry,
    load_s, out_s, cot_s, w_s, w_r, bias_s, bias_r, dw_s, dw_r, ex_s, ex_r, ex2_s, ex2_r, do_s, do_r, e_s, e_r,
):
    sec = lax.axis_index("section")
    lane = lax.axis_index("tensor")
    mate = lane + 1 - 2 * lax.rem(lane, 2)
    over = lax.rem(lane + 2, LANES)
    cross = lax.rem(mate + 2, LANES)
    me = sec * LANES + lane
    devices = 2 * LANES
    clip = me
    clips = (me, sec * LANES + over)

    def group_peer(step):
        peer = lax.rem(me + step, devices)
        return peer, {"section": lax.div(peer, LANES), "tensor": lax.rem(peer, LANES)}

    own = [
        pltpu.make_async_copy(src, dst.at[0], load_s.at[n])
        for n, (src, dst) in enumerate(
            ((h_qkv, w_qkv), (h_proj, w_proj), (h_up, w_up), (h_down, w_down))
        )
    ]

    def place(n, shard, part=None):
        thick = (128, 128, 512, 512)[n]
        base = shard * thick
        cut = pl.ds(pl.multiple_of(base, thick), thick)
        if part is None:
            return (qkv.at[:, :, cut], proj.at[cut, :], up.at[:, cut], down.at[cut, :])[n]
        some = span(part, (256, 64, 256, 256)[n])
        if n == 0:
            return qkv.at[:, some, cut]
        if n == 2:
            return up.at[some, cut]
        few = thick // 2
        rows = pl.ds(pl.multiple_of(base + part * few, few), few)
        return (proj if n == 1 else down).at[rows, :]

    shards = (h_dqkv, h_dproj, h_dup, h_ddown)
    keep = [
        pltpu.make_async_copy(shards[n], place(n, lane), load_s.at[4 + n]) for n in range(4)
    ]
    for copy in own + keep:
        copy.start()
    fetch = pltpu.make_async_copy(cot_hbm.at[clip], cot, cot_s)
    fetch.start()

    barrier = pltpu.get_barrier_semaphore()
    for step in range(1, devices):
        pl.semaphore_signal(barrier, inc=1, device_id_type=MESH, device_id=group_peer(step)[1])
    bias[...] = jnp.zeros_like(bias)
    half = w_proj.shape[1]
    bias[0:1, :] = b_up[...].astype(F32).reshape(1, -1)
    bias[1:3, 0:half] = b_qv[...].astype(F32)
    bias[3:4, 0:512] = b_dup[...].astype(F32).reshape(1, -1)
    bias[4:6, 0:128] = b_dqv[...].astype(F32)
    biases[lane] = bias[...]
    stride = pat.shape[0] // VIS
    for c in range(2):
        row = lax.broadcasted_iota(jnp.int32, (PAD, pat.shape[0]), 0)
        col = lax.broadcasted_iota(jnp.int32, (PAD, pat.shape[0]), 1)
        pick = (col == row * stride + clips[c]).astype(F32).astype(BF16)
        ex[c * PAD : (c + 1) * PAD, :] = nn(pick, pat[...])

    pl.semaphore_wait(barrier, devices - 1)

    def enc_weight(n):
        src = (h_qkv, h_proj, h_up, h_down)[n]
        dst = (w_qkv, w_proj, w_up, w_down)[n]
        return far(src, dst.at[1], w_s.at[n], w_r.at[n], {"tensor": mate})

    def bias_copy(step):
        return far(
            bias, biases.at[lane], bias_s.at[step], bias_r.at[step],
            {"tensor": lax.rem(lane + step, LANES)},
        )

    def half_of(n):
        some = span(sec, (256, 64, 256, 256)[n])
        return shards[n].at[:, some, :] if n == 0 else shards[n].at[some, :]

    def dec_weight(n, kind):
        peer = {"section": 1 - sec} if kind == 2 else {"tensor": over if kind == 0 else mate}
        if kind == 0:
            src, dst = half_of(n), place(n, lane, sec)
        elif kind == 1:
            src, dst = shards[n], place(n, lane)
        else:
            src = dst = place(n, over, 1 - sec if kind == 4 else sec)
        return far(src, dst, dw_s.at[5 * n + kind], dw_r.at[5 * n + kind], peer)

    enc_weight(0).start()
    for step in range(1, LANES):
        bias_copy(step).start()
    enc_weight(1).start()
    dec_weight(0, 0).start()
    enc_weight(2).start()
    enc_weight(3).start()
    for n in range(4):
        dec_weight(n, 1).start()

    def pass_on(n):
        dec_weight(n, 0).wait_recv()
        dec_weight(n, 2).start()
        dec_weight(n, 3).start()

    def pass_last(n):
        dec_weight(n, 2).wait_recv()
        dec_weight(n, 4).start()

    def arrived(n):
        keep[n].wait()
        dec_weight(n, 1).wait_recv()
        dec_weight(n, 3).wait_recv()
        dec_weight(n, 4).wait_recv()

    width = wid[clip]
    bits = jnp.where(width == WIDE, 3, 2)
    turn = shifts[0, clip] * width
    mod = GRID - 1
    spot = 0
    for i in range(order.shape[1]):
        spot = spot + jnp.where(order[0, i] == clip, i, 0)
    batch = spot // CM
    count = 0
    for i in range(order.shape[1]):
        count = count + jnp.where(batch == i // CM, wid[order[0, i]], 0)
    factor_rows = CM * GRID / (jnp.full((1, 1), count, jnp.int32) * GRID_ROWS).astype(F32)

    def slot_of(index):
        return (index - turn) & mod

    def code_of(slot):
        band = ((slot >> bits) + shifts[0, clip]) >> 2
        strip = ((slot & (width - 1)) + shifts[1, clip]) >> 2
        return band * 4 + strip

    def valid_rows():
        slot = slot_of(lax.broadcasted_iota(jnp.int32, (GRID, 1), 0))
        return (slot < GRID_ROWS * width).astype(F32)

    def clip_gradient():
        fetch.wait()
        rolled = slot_of(lax.broadcasted_iota(jnp.int32, (GRID, GRID), 0))
        column = lax.broadcasted_iota(jnp.int32, (GRID, GRID), 1)
        perm[...] = (rolled == column).astype(F32).astype(BF16)
        g = nn(perm[...], cot[...]) * valid_rows() * factor_rows
        g32[...] = g
        gb[...] = g.astype(BF16)
        gt[...] = jnp.transpose(g.astype(BF16))
        d_small[...] = jnp.zeros_like(d_small)
        d_small[5:6, :] = colsum(g)

    seen = vis[pl.ds(clip, 1), :]
    target = jnp.concatenate([(seen + turn) & mod, jnp.full((1, PAD - VIS), -1, jnp.int32)], 1)

    def places(i):
        r = span(i, PAD)
        index = lax.broadcasted_iota(jnp.int32, (PAD, PAD), 0) + i * PAD
        column = lax.broadcasted_iota(jnp.int32, (PAD, PAD), 1)
        hot[r, :] = (index == target).astype(F32).astype(BF16)
        slot = slot_of(index)
        by_row = ((slot >> bits) == column).astype(F32).astype(BF16)
        by_col = ((slot & (width - 1)) == column).astype(F32).astype(BF16)
        row_part = nn(by_row, table[0]) + nn(by_row, table[1])
        col_part = nn(by_col, table[0]) + nn(by_col, table[1])
        x0[r, :] = jnp.concatenate([row_part, col_part], 1)

    egain = gains[...].astype(F32)
    eoff = offs[...].astype(F32)
    emarks = head_marks(half, ENC_SIZE, BF16)
    key = lax.broadcasted_iota(jnp.int32, (PAD, PAD), 1)
    floor = jnp.where(key < VIS, NEG * LOG2E, -1e30)
    eones = ones_per_head(PAD, emarks)
    blocks = D // 256

    def give_part(i, side):
        cut = span(i, 256)
        return far(
            esend.at[(1 - side) * PAD : (2 - side) * PAD, cut],
            erecv.at[side * PAD : (side + 1) * PAD, cut],
            ex_s.at[2 * i + side], ex_r.at[2 * i + side], {"tensor": over},
        )

    for c in range(2):
        rows = slice(c * PAD, (c + 1) * PAD)
        hat, _ = normal(ex[rows, :])
        ea[rows, :] = (hat * egain[0:1] + eoff[0:1]).astype(BF16)
        limit = (VIS * wid[clips[c]]) // WIDE
        for g, shard in enumerate((lane, mate)):
            if c == 0 and g == 0:
                own[0].wait()
            if c == 0 and g == 1:
                enc_weight(0).wait_recv()
                for step in range(1, LANES):
                    bias_copy(step).wait_recv()
            if g == 0:
                bq, bv = bias[1:2, 0:half], bias[2:3, 0:half]
            else:
                bq, bv = biases[shard, 1:2, 0:half], biases[shard, 2:3, 0:half]
            eqkv[g, 0, rows] = (nt(ea[rows, :], w_qkv[g, 0]) + bq).astype(BF16)
            eqkv[g, 1, rows] = nt(ea[rows, :], w_qkv[g, 1]).astype(BF16)
            eqkv[g, 2, rows] = (nt(ea[rows, :], w_qkv[g, 2]) + bv).astype(BF16)
            p, out, _ = attend(
                eqkv[g, 0, rows], eqkv[g, 1, rows], eqkv[g, 2, rows], emarks, eones,
                lambda s: jnp.where(key < limit, s, floor), ENC_SCALE,
            )
            ep[g, c] = p
            eo[g, rows] = out
        if c == 0:
            own[1].wait()
            enc_weight(1).wait_recv()
        for i in range(blocks):
            cut = slice(i * 256, (i + 1) * 256)
            t = nn(eo[0, rows], w_proj[0, :, cut]) + nn(eo[1, rows], w_proj[1, :, cut])
            epart[rows, cut] = t
            esend[rows, cut] = t.astype(BF16)
            give_part(i, 1 - c).start()
    pass_on(0)
    clip_gradient()
    own[2].wait()
    enc_weight(2).wait_recv()

    def give_last(i):
        cut = span(i, 256)
        return far(
            esend2.at[:, cut], erecv2.at[:, cut], ex2_s.at[i], ex2_r.at[i], {"tensor": over}
        )

    for c in (1, 0):
        rows = slice(c * PAD, (c + 1) * PAD)
        for i in range(blocks):
            give_part(i, c).wait_recv()
        t = ex[rows, :] + epart[rows, :] + erecv[rows, :].astype(F32) + eoff[2:3]
        ex1[rows, :] = t
        hat, _ = normal(t)
        eu[rows, :] = (hat * egain[1:2] + eoff[1:2]).astype(BF16)
        for g, shard in enumerate((lane, mate)):

            def enc_ff(i, g=g, shard=shard, rows=rows):
                cut = span(i, 256)
                h = nn(eu[rows, :], w_up[g, :, cut]) + biases[shard, 0:1, cut]
                act, slope = gelu_both(h)
                ey[g, rows, cut] = act.astype(BF16)
                egp[g, rows, cut] = slope.astype(BF16)

            loop(w_up.shape[2] // 256, enc_ff, unroll=3)
        if c == 1:
            own[3].wait()
            enc_weight(3).wait_recv()
        for i in range(blocks):
            cut = slice(i * 256, (i + 1) * 256)
            t = nn(ey[0, rows], w_down[0, :, cut]) + nn(ey[1, rows], w_down[1, :, cut])
            if c == 0:
                eown[:, cut] = t
            else:
                esend2[:, cut] = t.astype(BF16)
                give_last(i).start()
        if c == 1:
            for n in (1, 2, 3):
                dec_weight(n, 0).start()
            pass_last(0)
    outs = [
        pltpu.make_async_copy(src, dst, out_s.at[n])
        for n, (src, dst) in enumerate(
            (
                (ex.at[0:PAD, :], o_x), (ex1, o_x1), (ea, o_a), (eu, o_u), (ey, o_y), (egp, o_gp),
                (eqkv, o_qkv), (ep, o_p), (eo, o_o), (w_qkv.at[1], o_w), (w_proj.at[1], o_wproj),
                (w_up.at[1], o_wup), (w_down.at[1], o_wdown),
            )
        )
    ]
    for copy in outs:
        copy.start()
    loop(GRID // PAD, places, unroll=2)
    for i in range(blocks):
        give_last(i).wait_recv()

    e_ref[...] = (ex1[0:PAD, :] + eown[...] + erecv2[...].astype(F32) + eoff[3:4]).astype(BF16)
    vec = evec[...].astype(F32)
    m = (nn(e_ref[...], ew[...]) + vec[0:1]).astype(BF16)
    gain = dgains[...].astype(F32)
    offsets = doffs[...].astype(F32)

    def start(i):
        r = span(i, PAD)
        oh = hot[r, :]
        hit = jnp.sum(oh.astype(F32), -1, keepdims=True)
        x = jnp.where(hit > 0, nn(oh, m), vec[1:2]).astype(BF16).astype(F32) + x0[r, :]
        x0[r, :] = x
        hat, _ = normal(x)
        a[r, :] = (hat * gain[0:1] + offsets[0:1]).astype(BF16)

    loop(GRID // PAD, start, unroll=2)
    arrived(0)

    def dec_bias(row, size):
        return jnp.concatenate([biases[k, row : row + 1, 0:size] for k in range(LANES)], 1)

    acts[0] = (nn(a[...], qkv[0]) + dec_bias(4, 128)).astype(BF16)
    acts[1] = nn(a[...], qkv[1]).astype(BF16)
    acts[2] = (nn(a[...], qkv[2]) + dec_bias(5, 128)).astype(BF16)
    pass_on(1)
    pass_on(2)
    marks = head_marks(128, DEC_SIZE, BF16)
    marks32 = head_marks(128, DEC_SIZE, F32)
    dim = lax.broadcasted_iota(jnp.int32, (128, 1), 0)
    rows32 = [
        ((dim >= h * DEC_SIZE) & (dim < (h + 1) * DEC_SIZE)).astype(F32) for h in range(len(marks))
    ]

    ones = ones_per_head(PAD, marks)

    def attention(i):
        r = span(i, PAD)
        row_slot = slot_of(lax.broadcasted_iota(jnp.int32, (PAD, PAD), 0) + i * PAD)
        key_slot = slot_of(lax.broadcasted_iota(jnp.int32, (PAD, PAD), 1) + i * PAD)
        allowed = (code_of(row_slot) == code_of(key_slot)) & (key_slot < GRID_ROWS * width)
        for g in range(DD // 128):
            c = slice(g * 128, (g + 1) * 128)
            probs[i, :, g * 512 : (g + 1) * 512], o[r, c], inverse[r, c] = attend(
                acts[0, r, c], acts[1, r, c], acts[2, r, c], marks, ones,
                lambda s: jnp.where(allowed, s, NEG * LOG2E), DEC_SCALE,
            )

    loop(GRID // PAD, attention, unroll=4)
    pass_last(1)
    pass_last(2)
    pass_on(3)
    arrived(1)

    def mix(i):
        r = span(i, 256)
        x = x0[r, :] + nn(o[r, :], proj[...]) + offsets[2:3]
        x1[r, :] = x
        hat, _ = normal(x)
        un = hat * gain[1:2] + offsets[1:2]
        u[r, :] = un.astype(BF16)
        ut[:, r] = jnp.transpose(un.astype(BF16))

    loop(2, mix)
    pass_last(3)
    arrived(2)

    def ff(i):
        c = span(i, 256)
        h = nn(u[...], up[:, c]) + biases[lax.div(i, 2), 3:4, span(lax.rem(i, 2), 256)]
        act, slope = gelu_both(h)
        y[:, c] = act.astype(BF16)
        gp[:, c] = slope.astype(BF16)

    loop(up.shape[1] // 256, ff, unroll=4)
    arrived(3)
    def out(i):
        c = span(i, 256)
        acc[:, c] = nn(y[...], down[:, c])

    loop(2, out)
    full = ((acc[...] + x1[...] + offsets[3:4]) * valid_rows()).astype(BF16)
    turned = tn(full, perm[...]).astype(BF16)
    for k in range(devices):
        dsend[k] = turned[k * dsend.shape[1] : (k + 1) * dsend.shape[1]]

    def decoded_copy(step):
        peer, spot = group_peer(step)
        return far(dsend.at[peer], dec_out.at[me], do_s.at[step], do_r.at[step], spot)

    for step in range(1, devices):
        decoded_copy(step).start()
    dec_out[me] = dsend[me]

    def ff_back(shard):
        for side in range(2):
            c = span(2 * shard + side, 256)
            d_down = nn(gt[...], y[:, c]).astype(BF16)
            dh = nt(gb[...], down[c, :]) * gp[:, c].astype(F32)
            d_upb[:, c] = colsum(dh)
            du = dh.astype(BF16)
            gp[:, c] = du
            d_up = nn(ut[...], du).astype(BF16)
            for block in range(GRID // CH):
                rows = slice(block * CH, (block + 1) * CH)
                h, top, col = tile_of(4 * block + side)
                buf[shard, h, top : top + CH, col : col + 256] = d_up[rows]
                h, top, col = tile_of(4 * block + 2 + side)
                buf[shard, h, top : top + CH, col : col + 256] = d_down[rows]

    def early_core(which):
        shard, land = ((mate, e_rc), (cross, e_rcy))[which]
        return far(
            buf.at[shard, :, 0:EARLY_ROWS, :], land, e_s.at[which], e_r.at[which], {"tensor": mate}
        )

    def early_x(which):
        return far(
            buf.at[(over, lane)[which], 1 - sec, 0:EARLY_ROWS, :], e_rx.at[which],
            e_s.at[2 + which], e_r.at[2 + which], {"section": 1 - sec},
        )

    def early_y():
        return far(
            buf.at[over, sec, 0:EARLY_ROWS, :], e_ry, e_s.at[4], e_r.at[4], {"tensor": over}
        )

    def early_add(shard, land):
        def body(i):
            r = span(i, CH)
            buf[shard, :, r, :] = buf[shard, :, r, :] + land[:, r, :]

        loop(EARLY_ROWS // CH, body)

    def early_half(shard, land):
        buf[shard, sec, 0:EARLY_ROWS, :] = buf[shard, sec, 0:EARLY_ROWS, :] + land

    def ff_step(i):
        ff_back(jnp.where(i == 0, cross, jnp.where(i == 1, over, jnp.where(i == 2, mate, lane))))

        @pl.when(i == 1)
        def _():
            early_core(1).start()

        @pl.when(i == 2)
        def _():
            early_core(0).start()

    loop(LANES, ff_step)
    early_core(1).wait_recv()
    early_add(over, e_rcy)
    early_x(0).start()

    def ff_in(i):
        c = span(i, 256)
        acc[:, c] = nt(gp[...], up[c, :])

    loop(2, ff_in)
    early_core(0).wait_recv()
    early_add(lane, e_rc)
    early_x(1).start()

    def mix_back(i):
        r = span(i, 256)
        hat, scale = normal(x1[r, :])
        da = acc[r, :]
        dx = g32[r, :] + normal_back(da, hat, scale, gain[1:2])
        d_small[1:2, :] += colsum(da * hat)
        d_small[3:4, :] += colsum(da)
        d_small[4:5, :] += colsum(dx)
        g32[r, :] = dx
        dxb = dx.astype(BF16)
        gb[r, :] = dxb
        u[r, :] = nt(dxb, proj[...]).astype(BF16)

    loop(2, mix_back)
    d_proj = tn(o[...], gb[...]).astype(BF16)
    for block in range(GRID // CH):
        h, top, col = tile_of(33 + 2 * block)
        side = slice(block // 2 * 128, (block // 2 + 1) * 128)
        for k in range(LANES):
            row = k * 128 + block % 2 * CH
            buf[k, h, top : top + CH, col + 128 : col + 256] = d_proj[row : row + CH, side]

    def attention_back(i):
        r = span(i, PAD)
        for k in range(DD // 128):
            c = slice(k * 128, (k + 1) * 128)
            acts[0, r, c], acts[1, r, c], acts[2, r, c] = attend_back(
                acts[0, r, c], acts[1, r, c], acts[2, r, c],
                probs[i, :, k * 512 : (k + 1) * 512], o[r, c], inverse[r, c], u[r, c],
                marks, marks32, rows32, ones, DEC_SCALE,
            )

    loop(GRID // PAD, attention_back, unroll=4)
    early_x(0).wait_recv()
    early_half(over, e_rx[0])
    early_y().start()
    d_qvb[0:1, :] = colsum(acts[0].astype(F32))
    d_qvb[1:2, :] = colsum(acts[2].astype(F32))

    def project_back(i):
        c = span(i, 256)
        acc[:, c] = (
            nt(acts[0], qkv[0, c, :]) + nt(acts[1], qkv[1, c, :]) + nt(acts[2], qkv[2, c, :])
        )

    loop(2, project_back)
    gt[...] = jnp.transpose(a[...])
    for j in range(3):
        d_qkv = nn(gt[...], acts[j]).astype(BF16)
        for block in range(GRID // CH):
            h, top, col = tile_of(32 + 2 * block + j // 2)
            col = col + j % 2 * 128
            rows = slice(block * CH, (block + 1) * CH)
            for k in range(LANES):
                buf[k, h, top : top + CH, col : col + 128] = d_qkv[rows, k * 128 : (k + 1) * 128]

    def start_back(i):
        r = span(i, PAD)
        hat, scale = normal(x0[r, :])
        da = acc[r, :]
        dx = g32[r, :] + normal_back(da, hat, scale, gain[0:1])
        d_small[0:1, :] += colsum(da * hat)
        d_small[2:3, :] += colsum(da)
        dg = dx.astype(BF16)
        gb[r, :] = dg
        hit = jnp.sum(hot[r, :].astype(F32), -1, keepdims=True)
        d_small[7:8, :] += colsum(jnp.where(hit > 0, 0.0, dg.astype(F32)))

    loop(GRID // PAD, start_back, unroll=2)
    dm = tn(hot[...], gb[...])
    d_small[6:7, :] = colsum(dm)
    dmb = dm.astype(BF16)
    d_enc[...] = nt(dmb, ew[...]).astype(BF16)
    d_ew = tn(e_ref[...], dmb).astype(BF16)
    for k in range(LANES):
        for h in range(2):
            top = k * 192 + h * 64
            buf[k, h, 512:576, 0:512] = d_ew[top : top + 64]
            buf[k, h, 512:576, 512:768] = d_ew[k * 192 + 128 : (k + 1) * 192, h * 256 : (h + 1) * 256]

    early_x(1).wait_recv()
    early_half(lane, e_rx[1])
    early_y().wait_recv()
    early_half(lane, e_ry[...])
    later = pl.ds(EARLY_ROWS, DEC_ROWS - EARLY_ROWS)
    rest = [pltpu.make_async_copy(buf.at[lane], o_dec.at[lane], out_s.at[13])] + [
        pltpu.make_async_copy(buf.at[k, :, later, :], o_dec.at[k, :, later, :], out_s.at[14 + n])
        for n, k in enumerate((mate, over, cross))
    ]
    for copy in rest:
        copy.start()
    for copy in outs + rest:
        copy.wait()
    for which in range(2):
        early_core(which).wait_send()
        early_x(which).wait_send()
    early_y().wait_send()
    for n in range(4):
        enc_weight(n).wait_send()
        for kind in range(5):
            dec_weight(n, kind).wait_send()
    for step in range(1, LANES):
        bias_copy(step).wait_send()
    for i in range(blocks):
        give_part(i, 0).wait_send()
        give_part(i, 1).wait_send()
        give_last(i).wait_send()
    for step in range(1, devices):
        decoded_copy(step).wait()


def forward_call(args, half, hid, dff):
    dma = lambda *s: pltpu.SemaphoreType.DMA(s)
    vm = lambda dtype, *shape: pltpu.VMEM(shape, dtype)
    rows = 2 * PAD
    keys = PAD * half // ENC_SIZE
    devices = 2 * LANES
    slab = DD // devices
    kept = [
        ((PAD, D), F32), ((rows, D), F32), ((rows, D), BF16), ((rows, D), BF16),
        ((2, rows, hid), BF16), ((2, rows, hid), BF16), ((2, 3, rows, half), BF16),
        ((2, 2, PAD, keys), BF16), ((2, rows, half), BF16),
        ((3, half, D), BF16), ((half, D), BF16), ((D, hid), BF16), ((hid, D), BF16),
        ((LANES, 2, DEC_ROWS, D), BF16),
    ]
    made = [
        ((PAD, D), BF16), ((2, DD), F32), ((1, dff), F32), ((8, DD), F32),
        ((devices, slab, GRID), BF16),
    ]
    return pl.pallas_call(
        forward_and_decoder,
        out_shape=[jax.ShapeDtypeStruct(s, d) for s, d in kept + made],
        in_specs=[SM, SM, SM] + [VM] * 8 + [ANY] * 9 + [VM] * 5,
        out_specs=[ANY] * len(kept) + [VM] * len(made),
        scratch_shapes=[
            vm(BF16, 2, 3, half, D), vm(BF16, 2, half, D), vm(BF16, 2, D, hid), vm(BF16, 2, hid, D),
            vm(F32, 8, D), vm(F32, LANES, 8, D),
            vm(BF16, 3, DD, DD), vm(BF16, DD, DD), vm(BF16, DD, dff), vm(BF16, dff, DD),
            vm(F32, rows, D), vm(BF16, rows, D), vm(BF16, rows, D), vm(BF16, 2, rows, hid),
            vm(BF16, 2, rows, hid), vm(BF16, 2, 3, rows, half), vm(BF16, 2, 2, PAD, keys),
            vm(BF16, 2, rows, half), vm(F32, rows, D), vm(F32, rows, D), vm(BF16, rows, D),
            vm(BF16, rows, D), vm(BF16, PAD, D), vm(BF16, PAD, D), vm(F32, PAD, D),
            vm(BF16, GRID, DD), vm(F32, GRID, DD), vm(F32, GRID, DD), vm(BF16, GRID, DD),
            vm(BF16, 3, GRID, DD), vm(BF16, GRID // PAD, PAD, DHEADS * PAD), vm(BF16, GRID, DD),
            vm(F32, GRID, DD),
            vm(BF16, GRID, DD), vm(BF16, DD, GRID), vm(BF16, GRID, dff), vm(BF16, GRID, dff),
            vm(F32, GRID, DD), vm(BF16, GRID, DD), vm(BF16, DD, GRID), vm(F32, GRID, DD),
            vm(BF16, PAD, D), vm(BF16, GRID, PAD), vm(BF16, GRID, GRID),
            vm(BF16, LANES, 2, DEC_ROWS, D),
            vm(BF16, devices, slab, GRID), *[vm(BF16, 2, EARLY_ROWS, D)] * 3, vm(BF16, EARLY_ROWS, D),
            dma(8), dma(17), pltpu.SemaphoreType.DMA, dma(4), dma(4), dma(LANES), dma(LANES),
            dma(20), dma(20), dma(6), dma(6), dma(3), dma(3), dma(devices), dma(devices),
            dma(5), dma(5),
        ],
        compiler_params=pltpu.CompilerParams(
            collective_id=0, has_side_effects=True, vmem_limit_bytes=VMEM_LIMIT
        ),
    )(*args)


def add(x, y):
    return x + y


def backward_and_sums(
    d_enc, gains,
    h_u, h_y, h_gp, h_down0, h_down1, h_up0, h_up1,
    h_x, h_x1, h_a, h_qkv, h_p, h_o, h_w0, h_w1, h_proj0, h_proj1,
    dec, dec_qvb, dec_upb, dec_small,
    total, emb, dx_out,
    gb, ut, part, send, recv, du, gx, dx1, d_o, d_acts, own, send1, recv1, dx32, dx,
    d_upb, d_qvb, d_small,
    acc, yacc, enc_mate, out, rcy, ry, land_x, land_l, land_r, small32, small,
    u, y, gp, down0, down1, up0, up1, x, x1, a, qkv, p, o, w0, w1, proj0, proj1, fetch_s,
    load_s, flush_s, ex_s, ex_r,
    core_s, core_r, corey_s, corey_r, y_s, y_r, x_s, x_r, z_s, zl_r, zr_r,
    bl_s, br_s, b_r, a_s, a_r, emb_s, emb_r, dx_s, dx_r,
):
    sec = lax.axis_index("section")
    lane = lax.axis_index("tensor")
    pos = lax.axis_index("dp")
    count = lax.axis_size("dp")
    mate = lane + 1 - 2 * lax.rem(lane, 2)
    over = lax.rem(lane + 2, LANES)
    cross = lax.rem(mate + 2, LANES)
    first = pos == 0
    last = pos == count - 1
    me = sec * LANES + lane
    devices = 2 * LANES

    def group_peer(step):
        peer = lax.rem(me + step, devices)
        return peer, {"section": lax.div(peer, LANES), "tensor": lax.rem(peer, LANES)}

    barrier = pltpu.get_barrier_semaphore()
    for step in range(1, devices):
        pl.semaphore_signal(barrier, inc=1, device_id_type=MESH, device_id=group_peer(step)[1])

    @pl.when(pos > 0)
    def _():
        pl.semaphore_signal(barrier, inc=1, device_id={"dp": pos - 1}, device_id_type=MESH)

    @pl.when(pos < count - 1)
    def _():
        pl.semaphore_signal(barrier, inc=1, device_id={"dp": pos + 1}, device_id_type=MESH)

    loads = [
        pltpu.make_async_copy(dec.at[lane], acc.at[:, 0:DEC_ROWS, :], load_s.at[0]),
        pltpu.make_async_copy(
            dec.at[over, :, EARLY_ROWS:DEC_ROWS, :], yacc.at[:, 0 : DEC_ROWS - EARLY_ROWS, :],
            load_s.at[1],
        ),
    ]
    for load in loads:
        load.start()
    fetches = [
        pltpu.make_async_copy(src, dst, fetch_s.at[n])
        for n, (src, dst) in enumerate(
            (
                (h_u, u), (h_y, y), (h_gp, gp), (h_down0, down0), (h_down1, down1), (h_up0, up0),
                (h_up1, up1), (h_x, x), (h_x1, x1), (h_a, a), (h_qkv, qkv), (h_p, p), (h_o, o),
                (h_w0, w0), (h_w1, w1), (h_proj0, proj0), (h_proj1, proj1),
            )
        )
    ]
    for fetch in fetches:
        fetch.start()
    small32[...] = jnp.zeros_like(small32)
    d_small[...] = jnp.zeros_like(d_small)
    gb[0:PAD, :] = d_enc[...]
    ends = jnp.where(first, 0, 1) + jnp.where(last, 0, 1)
    pl.semaphore_wait(barrier, devices - 1 + ends)

    gain = gains[...].astype(F32)
    width = w0.shape[1]
    marks = head_marks(width, ENC_SIZE, BF16)
    marks32 = head_marks(width, ENC_SIZE, F32)
    ones = ones_per_head(PAD, marks)

    def rows(k, size=CH):
        return pl.ds(pl.multiple_of(k * size, size), size)

    def give_enc():
        return far(d_enc, gb.at[PAD : 2 * PAD, :], ex_s.at[0], ex_r.at[0], {"tensor": over})

    def give_part(i, half):
        cut = rows(i, 256)
        n = 1 + 2 * i + half
        return far(
            send.at[(1 - half) * PAD : (2 - half) * PAD, cut],
            recv.at[half * PAD : (half + 1) * PAD, cut],
            ex_s.at[n], ex_r.at[n], {"tensor": over},
        )

    def give_last(i):
        cut = rows(i, 256)
        return far(send1.at[:, cut], recv1.at[:, cut], ex_s.at[7 + i], ex_r.at[7 + i], {"tensor": over})

    def ff_back(g, i, down):
        c = rows(i, 256)
        d_down = tn(y[g, :, c], gb[...]).astype(BF16)
        dh = nt(gb[...], down[c, :]) * gp[g, :, c].astype(F32)
        d_upb[g, :, c] = colsum(dh)
        dub = dh.astype(BF16)
        du[g, :, c] = dub
        d_up = nn(ut[...], dub).astype(BF16)
        if g == 0:
            acc[1, pl.ds(pl.multiple_of(A_TOP + i * 256, 64), 256), :] = d_down
            acc[0, A_TOP:B_TOP, c] = d_up
        else:
            enc_mate[1, c, :] = d_down
            enc_mate[0, 0:ENC_A, c] = d_up

    def ff_in(i):
        c = rows(i, 256)
        t = nt(du[0], up0[c, :]) + nt(du[1], up1[c, :])
        part[:, c] = t
        send[:, c] = t.astype(BF16)
        give_part(i, 0).start()
        give_part(i, 1).start()

    def norm_two():
        for fetch in fetches[7:]:
            fetch.wait()
        for k in range(D // 256):
            give_part(k, 0).wait_recv()
            give_part(k, 1).wait_recv()

        def body(j):
            r = rows(j, 64)
            da = part[r, :] + recv[r, :].astype(F32)
            hat, scale = normal(x1[r, :])
            g = gb[r, :].astype(F32)
            d = g + normal_back(da, hat, scale, gain[1:2])
            gx[r, :] = d.astype(BF16)
            dx1[r, :] = d

            @pl.when(j < 2)
            def _():
                d_small[1:2, :] += colsum(da * hat)
                d_small[3:4, :] += colsum(da)
                d_small[4:5, :] += colsum(d)
                d_small[5:6, :] += colsum(g)

        loop(2 * PAD // 64, body)

    def attention(g, c):
        if c == 0:
            d_proj = tn(o[g], gx[...]).astype(BF16)
            if g == 0:
                acc[1, B_TOP + width : S_TOP, :] = d_proj
            else:
                enc_mate[1, ENC_A + width : ENC_A + 2 * width, :] = d_proj
            d_o[...] = nt(gx[...], (proj0, proj1)[g][...]).astype(BF16)
        r = slice(c * PAD, (c + 1) * PAD)
        d_acts[g, 0, r], d_acts[g, 1, r], d_acts[g, 2, r] = attend_back(
            qkv[g, 0, r], qkv[g, 1, r], qkv[g, 2, r], p[g, c], o[g, r], 1.0 / nn(p[g, c], ones),
            d_o[r, :], marks, marks32, None, ones, ENC_SCALE,
        )
        if c == 1:
            d_qvb[g, 0:1, :] = colsum(d_acts[g, 0].astype(F32))
            d_qvb[g, 1:2, :] = colsum(d_acts[g, 2].astype(F32))

    def project_in(i):
        c = rows(i, 256)
        t = 0.0
        for g, w in enumerate((w0, w1)):
            for j in range(3):
                t += nn(d_acts[g, j], w[j, :, c])
        own[:, c] = t[:PAD]
        send1[:, c] = t[PAD:].astype(BF16)
        give_last(i).start()

    def project_grad(g):
        for j in range(3):
            row = (j % 2) * width
            d = tn(d_acts[g, j], a[...]).astype(BF16)
            if g == 0:
                acc[j // 2, B_TOP + row : B_TOP + row + width, :] = d
            else:
                enc_mate[j // 2, ENC_A + row : ENC_A + row + width, :] = d

    def norm_one():
        for k in range(D // 256):
            give_last(k).wait_recv()

        def body(j):
            r = rows(j, 64)
            da = own[r, :] + recv1[r, :].astype(F32)
            hat, scale = normal(x[r, :])
            d_small[0:1, :] += colsum(da * hat)
            d_small[2:3, :] += colsum(da)
            dx32[r, :] = dx1[r, :] + normal_back(da, hat, scale, gain[0:1])

        loop(PAD // 64, body)
        turned = jnp.transpose(dx32[...])
        cut = D // devices
        for k in range(devices):
            dx[k] = turned[k * cut : (k + 1) * cut, 0:VIS].astype(BF16)
        for r in range(LANES):
            small32[r, 8:9, 0:512] = dec_upb[:, r * 512 : (r + 1) * 512]
            small32[r, 9:10, 0:128] = dec_qvb[0:1, r * 128 : (r + 1) * 128]
            small32[r, 9:10, 128:256] = dec_qvb[1:2, r * 128 : (r + 1) * 128]
            small32[r, 0:8, 0:512] = dec_small[...]
            small32[r, 16:24, :] = d_small[...]
        for g, shard in enumerate((lane, mate)):
            small32[shard, 10:11, :] = d_upb[g]
            small32[shard, 11:12, 0:192] = d_qvb[g, 0:1]
            small32[shard, 11:12, 256:448] = d_qvb[g, 1:2]
        for r in range(LANES):
            for h in range(2):
                small[r, h] = small32[r, h * SMALL : (h + 1) * SMALL].astype(BF16)
        acc[:, S_TOP : S_TOP + SMALL, :] = small[lane]
        yacc[:, DEC_ROWS - EARLY_ROWS :, :] = small[over]
        core_copy(LATE, small.at[mate], SMALL).start()
        corey_copy(LATE, small.at[cross], SMALL).start()
        for step in range(1, devices):
            dx_copy(step).start()
        dx_out[me] = dx[me]

    def core_enc(lo, hi):
        def body(m):
            block = block_of(m)

            @pl.when((block >= lo) & (block < hi))
            def _():
                src = pl.ds(pl.multiple_of(block * CH - DEC_ROWS, CH), CH)
                core_copy(m, enc_mate.at[:, src, :]).start()

        loop(ALL_K, body)

    def first_piece():
        for fetch in fetches[:7]:
            fetch.wait()
        ut[...] = jnp.transpose(u[...])
        give_enc().wait_recv()

    def ff_step(k):
        for g, down in enumerate((down0, down1)):
            @pl.when(lax.rem(k, 2) == g)
            def _(g=g, down=down):
                ff_back(g, lax.div(k, 2), down)

    def run_pieces(n):
        def several(low, high, body):
            begin = sum(jnp.where(n > t, 1, 0) for t in PIECES[low:high])
            end = sum(jnp.where(n >= t, 1, 0) for t in PIECES[low:high])
            lax.fori_loop(begin, end, lambda k, c: (body(k), c)[1], 0)

        def single(k, body):
            @pl.when(n == PIECES[k])
            def _():
                body()

        single(0, first_piece)
        several(1, 7, ff_step)
        single(7, lambda: core_enc(DEC_K, DEC_K + ENC_A // CH))
        several(8, 11, ff_in)
        single(11, norm_two)
        for k in range(4):
            single(12 + k, lambda k=k: attention(k // 2, k % 2))
        several(16, 19, project_in)
        for g in range(2):
            single(19 + g, lambda g=g: project_grad(g))
        single(21, lambda: core_enc(DEC_K + ENC_A // CH, B_K))
        single(22, norm_one)

    def dx_copy(step):
        peer, place = group_peer(step)
        return far(dx.at[peer], dx_out.at[me], dx_s.at[step], dx_r.at[step], place)

    def emb_copy(step):
        return far(
            out.at[:, pl.ds(512, CH), :], emb.at[lane], emb_s.at[step], emb_r.at[step],
            {"tensor": lax.rem(lane + step, LANES)},
        )

    def block_of(m):
        shift = 0
        for k in range(1, ALL_K):
            if ORDER[k] - k != ORDER[k - 1] - k + 1:
                shift = jnp.where(m >= k, ORDER[k] - k, shift)
        return m + shift

    def is_dec(m):
        return (block_of(m) < DEC_K) & (m >= EARLY)

    def at(m, size=CH):
        return pl.ds(pl.multiple_of(block_of(m) * CH, CH), size)

    def slot(m, size=CH):
        return pl.ds(pl.multiple_of(m * CH, CH), size)

    def y_at(m, size=CH):
        return pl.ds(pl.multiple_of((jnp.minimum(block_of(m), DEC_K) - EARLY) * CH, CH), size)

    def core_copy(m, src, size=CH):
        return far(src, out.at[:, at(m, size), :], core_s.at[m], core_r.at[m], {"tensor": mate})

    def corey_copy(m, src, size=CH):
        return far(src, rcy.at[:, y_at(m, size), :], corey_s.at[m], corey_r.at[m], {"tensor": mate})

    def y_copy(m, size=CH):
        cut = y_at(m, size)
        return far(
            yacc.at[:, cut, :], ry.at[:, cut, :], y_s.at[m], y_r.at[m], {"tensor": over}
        )

    def x_copy(m, size=CH):
        return far(
            acc.at[1 - sec, at(m, size), :], land_x.at[0, slot(m, size), :], x_s.at[m], x_r.at[m],
            {"section": 1 - sec},
        )

    def xc_copy(m):
        return far(
            acc.at[:, at(m), :], land_x.at[:, slot(m), :], x_s.at[m], x_r.at[m],
            {"section": 1 - sec},
        )

    def z_copy(m, whole, right, size=CH):
        land = land_l if right else land_r
        if whole:
            src, dst = acc.at[:, at(m), :], land.at[:, slot(m), :]
        else:
            src, dst = acc.at[sec, at(m, size), :], land.at[0, slot(m, size), :]
        landed = zl_r if right else zr_r
        return far(src, dst, z_s.at[m], landed.at[m], {"dp": pos + 1 if right else pos - 1})

    def b_copy(m, whole, right, size=CH):
        place = out.at[:, at(m), :] if whole else out.at[sec, at(m, size), :]
        sent = br_s if right else bl_s
        return far(place, place, sent.at[m], b_r.at[m], {"dp": pos + 1 if right else pos - 1})

    def a_copy(m, size=CH):
        place = out.at[sec, at(m, size), :]
        return far(place, place, a_s.at[m], a_r.at[m], {"section": 1 - sec})

    def a_wait(m, size=CH):
        place = out.at[1 - sec, at(m, size), :]
        far(place, place, a_s.at[m], a_r.at[m], {"section": 1 - sec}).wait_recv()

    give_enc().start()

    def start_core(m):
        @pl.when(is_dec(m))
        def _():
            core_copy(m, dec.at[mate, :, at(m), :]).start()
            corey_copy(m, dec.at[cross, :, at(m), :]).start()

    loop(ALL_K, start_core)
    for load in loads:
        load.wait()

    def join_core(m, size):
        core_copy(m, out.at[:, at(m, size), :], size).wait_recv()
        acc[:, at(m, size), :] = add(acc[:, at(m, size), :], out[:, at(m, size), :])

    def join_core_y(m, size):
        corey_copy(m, rcy.at[:, y_at(m, size), :], size).wait_recv()
        yacc[:, y_at(m, size), :] = add(yacc[:, y_at(m, size), :], rcy[:, y_at(m, size), :])
        y_copy(m, size).start()

    def stage_c(m):
        @pl.when((m >= EARLY) & (m != LATE))
        def _():
            join_core(m, CH)

            @pl.when(is_dec(m))
            def _():
                join_core_y(m, CH)

        @pl.when(m == LATE)
        def _():
            join_core(m, SMALL)
            join_core_y(m, SMALL)

    def flush(m):
        return pltpu.make_async_copy(
            out.at[:, at(m), :], total.at[:, at(m), :], flush_s.at[m]
        )

    def finished(m):
        flush(m).start()

        @pl.when(block_of(m) == DEC_K - 1)
        def _():
            for step in range(1, LANES):
                emb_copy(step).start()
            emb[lane] = out[:, 512 : 512 + CH, :]

    def line_of(root, whole, size=CH):
        left = pos < root
        right = pos > root
        here = pos == root
        reach = max(root, count - 1 - root)
        level = jnp.where(left, pos, jnp.where(right, count - 1 - pos, reach))
        dist = jnp.where(left, root - pos, pos - root)

        def view(ref, m):
            return ref.at[:, at(m), :] if whole else ref.at[sec, at(m, size), :]

        def landed(ref, m):
            return ref.at[:, slot(m), :] if whole else ref.at[0, slot(m, size), :]

        def hop(m, rightward):
            return z_copy(m, whole, rightward, size)

        def back_hop(m, rightward):
            return b_copy(m, whole, rightward, size)

        def outer(m):
            @pl.when(left & first)
            def _():
                hop(m, True).start()

            @pl.when(right & last)
            def _():
                hop(m, False).start()

        def inward(m):
            @pl.when(left & (pos > 0))
            def _():
                hop(m, True).wait_recv()
                view(acc, m)[...] = add(view(acc, m)[...], landed(land_l, m)[...])
                hop(m, True).start()

            @pl.when(right & (pos < count - 1))
            def _():
                hop(m, False).wait_recv()
                view(acc, m)[...] = add(view(acc, m)[...], landed(land_r, m)[...])
                hop(m, False).start()

            @pl.when(here)
            def _():
                total = view(acc, m)[...].astype(F32)
                if root > 0:
                    hop(m, True).wait_recv()
                    total = total + landed(land_l, m)[...].astype(F32)
                if root < count - 1:
                    hop(m, False).wait_recv()
                    total = total + landed(land_r, m)[...].astype(F32)
                if whole:
                    view(acc, m)[...] = total.astype(BF16)
                    xc_copy(m).start()
                else:
                    view(out, m)[...] = total.astype(BF16)
                    spread(m)
                    a_copy(m, size).start()

        def spread(m):
            if root > 0:
                back_hop(m, False).start()
            if root < count - 1:
                back_hop(m, True).start()

        def crossed(m):
            xc_copy(m).wait_recv()
            view(out, m)[...] = add(view(acc, m)[...], landed(land_x, m)[...])
            spread(m)
            finished(m)

        def outward(m):
            back_hop(m, False).wait_recv()

            @pl.when(left & (pos > 0))
            def _():
                back_hop(m, False).start()

            @pl.when(right & (pos < count - 1))
            def _():
                back_hop(m, True).start()

            if whole:
                finished(m)
            else:
                a_copy(m, size).start()

        def sent(m):
            @pl.when(jnp.logical_not(here))
            def _():
                hop(m, True).wait_send()

            @pl.when((pos <= root) & (pos > 0))
            def _():
                back_hop(m, False).wait_send()

            @pl.when((pos >= root) & (pos < count - 1))
            def _():
                back_hop(m, True).wait_send()

            if whole:
                @pl.when(here)
                def _():
                    xc_copy(m).wait_send()
            else:
                a_copy(m, size).wait_send()

                @pl.when(crosses_first(m))
                def _():
                    x_copy(m, size).wait_send()

        def crosses_first(m):
            return m >= EARLY if XFIRST else m >= 0

        def set_off(m):
            if whole:
                outer(m)
            else:
                x_copy(m, size).start()

        def set_off_early(m):
            if XFIRST:
                outer(m)
            else:
                set_off(m)

        def add_y(m):
            def joined():
                y_copy(m, size).wait_recv()
                acc[:, at(m, size), :] = add(acc[:, at(m, size), :], ry[:, y_at(m, size), :])

            if size == CH:
                pl.when(is_dec(m))(joined)
            else:
                joined()
            set_off(m)

        def add_x(m):
            @pl.when(crosses_first(m))
            def _():
                x_copy(m, size).wait_recv()
                acc[sec, at(m, size), :] = add(
                    acc[sec, at(m, size), :], land_x[0, slot(m, size), :]
                )
                outer(m)

        def last_half(m):
            a_wait(m, size)
            finished(m)

        base = 1 if whole else 2
        back = base + reach + dist + (1 if whole else 0)
        steps = [(back, jnp.logical_not(here), outward), (base + level, level > 0, inward)]
        if whole:
            steps.append((base + reach + 1, here, crossed))
        else:
            steps += [(back + 1, True, last_half), (2, True, add_x)]
        return steps, sent, add_y, set_off_early

    low_root = (count - 1) // 2
    high_root = min(low_root + 1, count - 1)
    def is_whole(m):
        return (lax.rem(m, 2) == 0) & (m >= WHOLE_LOW) & (m < WHOLE_HIGH)

    roots = (high_root, count - 1, low_root, 0)
    lines = [
        (lambda m, part=part: is_whole(m) & (lax.rem(m, 8) == part), *line_of(root, True))
        for part, root in zip((0, 2, 4, 6), roots)
    ] + [
        (lambda m: jnp.logical_not(is_whole(m)) & (m != LATE), *line_of(low_root, False)),
        (lambda m: m == LATE, *line_of(low_root, False, SMALL)),
    ]

    def finish(m):
        @pl.when((m >= EARLY) & (m != LATE))
        def _():
            core_copy(m, out.at[:, at(m), :]).wait_send()

            @pl.when(is_dec(m))
            def _():
                corey_copy(m, rcy.at[:, y_at(m), :]).wait_send()
                y_copy(m).wait_send()

        @pl.when(m == LATE)
        def _():
            core_copy(m, out.at[:, at(m, SMALL), :], SMALL).wait_send()
            corey_copy(m, rcy.at[:, y_at(m, SMALL), :], SMALL).wait_send()
            y_copy(m, SMALL).wait_send()

        for mine, _, sent, _, _ in lines:
            @pl.when(mine(m))
            def _(sent=sent):
                sent(m)

    def set_off_early(m):
        for mine, _, _, _, set_off in lines:
            @pl.when(mine(m))
            def _(set_off=set_off):
                set_off(m)

    loop(EARLY, set_off_early)
    far_reach = max(max(root, count - 1 - root) for root in roots)
    depth = LAG * (3 + 2 * far_reach) + 1

    def tick(n):
        @pl.when(n <= PIECES[-1])
        def _():
            run_pieces(n)

        def run_line(line):
            mine, steps, _, add_y, _ = line
            m = n - LAG

            @pl.when((m >= EARLY) & (m < ALL_K))
            def _(m=m):
                @pl.when(mine(m))
                def _():
                    add_y(m)

            for offset, enabled, stage in steps:
                m = n - LAG * offset

                @pl.when((m >= 0) & (m < ALL_K) & enabled)
                def _(m=m, stage=stage):
                    @pl.when(mine(m))
                    def _():
                        stage(m)

        run_line(lines[-2])

        @pl.when((lax.rem(n, 2) == 0) & (n >= WHOLE_LOW) & (n < WHOLE_HIGH + depth))
        def _():
            for line in lines[:-2]:
                run_line(line)

        @pl.when((n >= LATE) & (n < LATE + depth))
        def _():
            run_line(lines[-1])

        @pl.when(n < ALL_K)
        def _():
            stage_c(n)

        @pl.when(n >= depth)
        def _():
            finish(n - depth)

    loop(ALL_K + depth, tick)
    loop(ALL_K, lambda m: flush(m).wait())
    for step in range(1, devices):
        dx_copy(step).wait()
    for step in range(1, LANES):
        emb_copy(step).wait()
    give_enc().wait_send()
    for k in range(D // 256):
        give_part(k, 0).wait_send()
        give_part(k, 1).wait_send()
        give_last(k).wait_send()


def backward_call(args, half, hid):
    dma = lambda *s: pltpu.SemaphoreType.DMA(s)
    vm = pltpu.VMEM
    full = ALL_K * CH
    y_half = DEC_ROWS - EARLY_ROWS + SMALL
    k = ALL_K
    rows = 2 * PAD
    cut = D // (2 * LANES)
    specs = [VM, VM] + [ANY] * 18 + [VM] * 3
    return pl.pallas_call(
        backward_and_sums,
        out_shape=[
            jax.ShapeDtypeStruct((2, full, D), BF16),
            jax.ShapeDtypeStruct((LANES, 2, CH, D), BF16),
            jax.ShapeDtypeStruct((2 * LANES, cut, VIS), BF16),
        ],
        in_specs=specs,
        out_specs=[ANY, VM, VM],
        scratch_shapes=[
            vm((rows, D), BF16), vm((D, rows), BF16),
            vm((rows, D), F32), vm((rows, D), BF16), vm((rows, D), BF16),
            vm((2, rows, hid), BF16), vm((rows, D), BF16), vm((rows, D), F32),
            vm((rows, half), BF16), vm((2, 3, rows, half), BF16),
            vm((PAD, D), F32), vm((PAD, D), BF16), vm((PAD, D), BF16), vm((PAD, D), F32),
            vm((2 * LANES, cut, VIS), BF16),
            vm((2, 1, hid), F32), vm((2, 2, half), F32), vm((8, D), F32),
            vm((2, full, D), BF16), vm((2, y_half, D), BF16), vm((2, ENC_A + ENC_B, D), BF16),
            vm((2, full, D), BF16),
            vm((2, y_half, D), BF16), vm((2, y_half, D), BF16),
            *[vm((2, full, D), BF16)] * 3,
            vm((LANES, 32, D), F32), vm((LANES, 2, SMALL, D), BF16),
            *[vm(v.shape, v.dtype) for v in args[2:19]],
            dma(17), dma(2), dma(k), dma(10), dma(10),
            dma(k), dma(k), dma(k), dma(k), dma(k), dma(k),
            dma(k), dma(k), dma(k), dma(k), dma(k),
            dma(k), dma(k), dma(k), dma(k), dma(k), dma(LANES), dma(LANES),
            dma(2 * LANES), dma(2 * LANES),
        ],
        compiler_params=pltpu.CompilerParams(
            collective_id=1, has_side_effects=True, vmem_limit_bytes=VMEM_LIMIT
        ),
    )(*args)


def finish_grads(
    total, emb, decoded, dx, decoded_out, dx_out,
    e_qkv, e_qvb, e_proj, e_up, e_upb, e_down, e_gain, e_off,
    d_qkv, d_qvb, d_proj, d_up, d_upb, d_down, d_gain, d_off, d_ew, d_ev,
):
    half = e_proj.shape[0]
    decoded_out[...] = decoded[...]
    dx_out[...] = dx[...]
    e_up[...] = total[0, A_TOP:B_TOP, :].astype(F32)
    e_down[...] = total[1, A_TOP:B_TOP, :].astype(F32)
    e_qkv[0] = total[0, B_TOP : B_TOP + half, :].astype(F32)
    e_qkv[1] = total[0, B_TOP + half : S_TOP, :].astype(F32)
    e_qkv[2] = total[1, B_TOP : B_TOP + half, :].astype(F32)
    e_proj[...] = total[1, B_TOP + half : S_TOP, :].astype(F32)

    def raw(number):
        h, top, col = tile_of(number)
        return total[h, top : top + CH, col : col + 256]

    def tile(number):
        return raw(number).astype(F32)

    for block in range(GRID // CH):
        rows = slice(block * CH, (block + 1) * CH)
        side = slice(block // 2 * 128, (block // 2 + 1) * 128)
        for k in range(2):
            d_up[rows, k * 256 : (k + 1) * 256] = tile(4 * block + k)
            if block % 2:
                both = jnp.concatenate([raw(4 * block - 2 + k), raw(4 * block + 2 + k)], 0)
                d_down[k * 256 : (k + 1) * 256, side] = jnp.transpose(both).astype(F32)
        one, two = tile(32 + 2 * block), tile(33 + 2 * block)
        d_qkv[0, rows, :] = one[:, 0:128]
        d_qkv[1, rows, :] = one[:, 128:256]
        d_qkv[2, rows, :] = two[:, 0:128]
        d_proj[block % 2 * CH : (block % 2 + 1) * CH, side] = two[:, 128:256]
    for k in range(LANES):
        for h in range(2):
            top = k * 192 + h * 64
            d_ew[top : top + 64, :] = emb[k, h, :, 0:512].astype(F32)
            d_ew[k * 192 + 128 : (k + 1) * 192, h * 256 : (h + 1) * 256] = emb[
                k, h, :, 512:768
            ].astype(F32)
    little = total[0, S_TOP : S_TOP + SMALL, :].astype(F32)
    d_gain[...] = little[0:2, 0:512]
    d_off[...] = little[2:6, 0:512]
    d_ev[...] = little[6:8, 0:512]
    d_upb[...] = little[8, 0:512]
    d_qvb[0:1, :] = little[9:10, 0:128]
    d_qvb[1:2, :] = little[9:10, 128:256]
    e_upb[...] = little[10]
    e_qvb[0:1, :] = little[11:12, 0:192]
    e_qvb[1:2, :] = little[11:12, 256:448]
    little = total[1, S_TOP : S_TOP + SMALL, :].astype(F32)
    e_gain[...] = little[0:2]
    e_off[...] = little[2:6]


def call(kernel, specs, shapes, scratch, args):
    return pl.pallas_call(
        kernel,
        out_shape=[jax.ShapeDtypeStruct(s, d) for s, d in shapes],
        in_specs=specs,
        out_specs=[VM] * len(shapes),
        scratch_shapes=scratch,
        compiler_params=pltpu.CompilerParams(vmem_limit_bytes=VMEM_LIMIT),
    )(*args)


def position_rows():
    quarter = DD // 4
    freq = np.exp(np.arange(quarter, dtype=np.float32) * np.float32(-math.log(10000.0) / quarter))
    angle = np.arange(PAD, dtype=np.float32)[:, None] * freq[None, :].astype(np.float32)
    both = np.concatenate([np.sin(angle), np.cos(angle)], 1).astype(np.float32)
    high = both.astype(jnp.bfloat16)
    low = (both - high.astype(np.float32)).astype(jnp.bfloat16)
    return np.stack([high, low])


def per_device(
    patches, cotangent, widths, visible, window_shift, batch_order,
    encoder_qkv, encoder_qvbias, encoder_proj, encoder_up, encoder_upbias, encoder_down,
    encoder_gains, encoder_offsets,
    decoder_qkv, decoder_qvbias, decoder_proj, decoder_up, decoder_upbias, decoder_down,
    decoder_gains, decoder_offsets, embed_weight, embed_vectors,
):
    qkv0 = encoder_qkv.transpose(1, 2, 0)
    half = qkv0.shape[1]
    hid = encoder_up.shape[1]
    dff = decoder_up.shape[1] * LANES
    flat = patches.transpose(1, 0, 2).reshape(-1, D)
    (
        x, x1, a, u, y, gp, qkv, p, o, qkv1, proj1, up1, down1, dec_buf,
        d_enc, d_dqvb, d_dupb, d_dsmall, out_all,
    ) = forward_call(
        (
            widths, window_shift.T, batch_order, visible, flat, encoder_gains, encoder_offsets,
            encoder_qvbias, encoder_upbias, decoder_qvbias, decoder_upbias,
            qkv0, encoder_proj, encoder_up, encoder_down,
            decoder_qkv.transpose(1, 0, 2), decoder_proj, decoder_up, decoder_down,
            cotangent, embed_weight, embed_vectors, jnp.asarray(position_rows()),
            decoder_gains, decoder_offsets,
        ),
        half, hid, dff,
    )
    total, emb, dx_all = backward_call(
        (
            d_enc, encoder_gains, u, y, gp, encoder_down, down1, encoder_up, up1,
            x, x1, a, qkv, p, o, qkv0, qkv1, encoder_proj, proj1,
            dec_buf, d_dqvb, d_dupb, d_dsmall,
        ),
        half, hid,
    )
    f = lambda *shape: (shape, F32)
    out_all, dx_all, *grads = call(
        finish_grads, [VM] * 4,
        [
            (out_all.shape, BF16), (dx_all.shape, BF16), f(3, half, D), f(2, half), f(half, D), f(D, hid), f(hid), f(hid, D), f(2, D), f(4, D),
            f(3, DD, 128), f(2, 128), f(128, DD), f(DD, 512), f(512), f(512, DD), f(2, DD), f(4, DD),
            f(D, DD), f(2, DD),
        ],
        [], (total, emb, out_all, dx_all),
    )
    grads[0] = grads[0].transpose(2, 0, 1)
    grads[8] = grads[8].transpose(1, 0, 2)
    return (out_all.swapaxes(1, 2), dx_all.swapaxes(1, 2), *grads)


def solution(mesh):
    weights = (
        P(None, None, "tensor"), P(None, "tensor"), P("tensor", None), P(None, "tensor"),
        P("tensor"), P("tensor", None), P(), P(),
    )
    split = P("dp", None, ("section", "tensor"))
    return jax.shard_map(
        per_device,
        mesh=mesh,
        in_specs=(
            P("dp", None, None), P("dp", None, None), P("dp"), P("dp", None), P("dp", None),
            P("dp", None),
        ) + weights + weights + (P(), P()),
        out_specs=(split, split) + weights + weights + (P(), P()),
        check_vma=False,
    )
```

```python
import math

import jax
import jax.numpy as jnp
import numpy as np
from jax import lax
from jax.experimental import pallas as pl
from jax.experimental.pallas import tpu as pltpu
from jax.sharding import PartitionSpec as P

D = 768
HEADS = 12
DD = 512
DHEADS = 16
GRID_ROWS = 64
WIDE = 8
WIN = 4
VIS = 102
CM = 4
GRID = 512
LANES = 4
PAD = 128
EPS = 1e-06
NEG = -10000.0
F32 = jnp.float32
BF16 = jnp.bfloat16
VMEM_LIMIT = 60 * 1024 * 1024

VM = pl.BlockSpec(memory_space=pltpu.VMEM)
SM = pl.BlockSpec(memory_space=pltpu.SMEM)
ANY = pl.BlockSpec(memory_space=pl.ANY)


def nn(a, b):
    return lax.dot_general(a, b, (((1,), (0,)), ((), ())), preferred_element_type=F32)


def nt(a, b):
    return lax.dot_general(a, b, (((1,), (1,)), ((), ())), preferred_element_type=F32)


def tn(a, b):
    return lax.dot_general(a, b, (((0,), (0,)), ((), ())), preferred_element_type=F32)


def loop(count, body, unroll=1):
    def step(i, carry):
        body(i)
        return carry

    lax.fori_loop(0, count, step, 0, unroll=unroll)


def span(i, size):
    return pl.ds(pl.multiple_of(i * size, size), size)


def normal(x):
    center = x - jnp.mean(x, -1, keepdims=True)
    scale = lax.rsqrt(jnp.mean(center * center, -1, keepdims=True) + EPS)
    return center * scale, scale


def normal_back(dy, hat, scale, gain):
    d = dy * gain
    return scale * (
        d - jnp.mean(d, -1, keepdims=True) - hat * jnp.mean(d * hat, -1, keepdims=True)
    )


def gelu_both(h):
    phi = 0.5 * lax.erf(h * math.sqrt(0.5)) + 0.5
    bell = jnp.exp2(h * h * (-0.5 * math.log2(math.e)))
    return h * phi, phi + h * bell * (1.0 / math.sqrt(2.0 * math.pi))


def colsum(x):
    return jnp.sum(x, 0, keepdims=True)


def head_marks(width, size, dtype):
    lane = lax.broadcasted_iota(jnp.int32, (1, width), 1)
    return [((lane >= h * size) & (lane < (h + 1) * size)).astype(dtype) for h in range(width // size)]


def stacked(x, marks):
    return jnp.concatenate([x * m for m in marks], 0)


LOG2E = math.log2(math.e)


def attend(q, k, v, marks, ones, masked, scale):
    keys = k.shape[0]
    s = nt(q, stacked(k, marks))
    parts = []
    for h in range(len(marks)):
        x = masked(s[:, h * keys : (h + 1) * keys] * (scale * LOG2E))
        parts.append(jnp.exp2(x - jnp.max(x, -1, keepdims=True)).astype(BF16))
    e = jnp.concatenate(parts, 1)
    width = q.shape[1]
    if width % 128:
        top, total = nn(e, stacked(v, marks)), nn(e, ones)
    else:
        both = nn(e, jnp.concatenate([stacked(v, marks), ones], 1))
        top, total = both[:, :width], both[:, width:]
    inverse = 1.0 / total
    return e, (top * inverse).astype(BF16), inverse


def attend_back(q, k, v, e, o, inverse, d_out, marks, marks32, rows32, ones, scale):
    keys = k.shape[0]
    width = q.shape[1]
    d_one = d_out.astype(F32) * inverse
    d_two = (d_one * o.astype(F32)).astype(BF16)
    d_one = d_one.astype(BF16)
    if width % 128:
        d_s = nt(d_one, stacked(v, marks)) - nt(d_two, ones)
    else:
        d_s = nt(
            jnp.concatenate([d_one, d_two], 1), jnp.concatenate([stacked(v, marks), -ones], 1)
        )
    dr = (e.astype(F32) * d_s * scale).astype(BF16)
    d_q = nn(dr, stacked(k, marks)).astype(BF16)
    if width % 128:
        d_k_all, d_v_all = tn(dr, q), tn(e, d_one)
        d_k = d_v = 0.0
        for h in range(len(marks)):
            cut = slice(h * keys, (h + 1) * keys)
            d_k += d_k_all[cut] * marks32[h]
            d_v += d_v_all[cut] * marks32[h]
        return d_q, d_k.astype(BF16), d_v.astype(BF16)
    d_k_all = nn(jnp.transpose(q), dr)
    d_v_all = nn(jnp.transpose(d_one), e)
    d_k = d_v = 0.0
    for h in range(len(marks)):
        cut = slice(h * keys, (h + 1) * keys)
        d_k += d_k_all[:, cut] * rows32[h]
        d_v += d_v_all[:, cut] * rows32[h]
    return d_q, jnp.transpose(d_k.astype(BF16)), jnp.transpose(d_v.astype(BF16))


def ones_per_head(keys, marks):
    return jnp.concatenate([jnp.broadcast_to(m, (keys, m.shape[1])) for m in marks], 0)


ENC_SIZE = D // HEADS
ENC_SCALE = ENC_SIZE ** -0.5
DEC_SIZE = DD // DHEADS
DEC_SCALE = DEC_SIZE ** -0.5


CH = 64
DEC_ROWS = 576
ENC_A = 768
ENC_B = 384
DEC_K = DEC_ROWS // CH
B_K = (DEC_ROWS + ENC_A + ENC_B) // CH
ALL_K = B_K + 1
A_TOP = DEC_ROWS
B_TOP = DEC_ROWS + ENC_A
S_TOP = B_TOP + ENC_B
EARLY = 4
XFIRST = True
EARLY_ROWS = EARLY * CH
LAG = 2
ORDER = (0, 1, 2, 3, 9, 10, 11, 12, 13, 14, 4, 15, 16, 17, 18, 5, 6, 19, 21, 20, 8, 22, 23, 24, 25, 27, 26, 7)
PIECES = (0, 2, 2, 2, 2, 2, 2, 2, 3, 3, 3, 10, 12, 12, 13, 13, 14, 14, 15, 15, 15, 16, 20)
LATE = ORDER.index(B_K)
WHOLE_LOW = 6
WHOLE_HIGH = 22
SMALL = 16


def tile_of(number):
    place = number // 3
    return place % 2, place // 2 * CH, number % 3 * 256


MESH = pl.DeviceIdType.MESH


def far(src, dst, send, recv, peer):
    return pltpu.make_async_remote_copy(
        src_ref=src, dst_ref=dst, send_sem=send, recv_sem=recv, device_id=peer, device_id_type=MESH
    )


def forward_and_decoder(
    wid, shifts, order, vis, pat, gains, offs, b_qv, b_up, b_dqv, b_dup,
    h_qkv, h_proj, h_up, h_down, h_dqkv, h_dproj, h_dup, h_ddown,
    cot_hbm, ew, evec, table, dgains, doffs,
    o_x, o_x1, o_a, o_u, o_y, o_gp, o_qkv, o_p, o_o, o_w, o_wproj, o_wup, o_wdown, o_dec,
    d_enc, d_qvb, d_upb, d_small, dec_out,
    w_qkv, w_proj, w_up, w_down, bias, biases, qkv, proj, up, down,
    ex, ea, eu, ey, egp, eqkv, ep, eo, ex1, epart, esend, erecv, esend2, erecv2, eown,
    cot, x0, x1, a, acts, probs, o, inverse, u, ut, y, gp, g32, gb, gt, acc, e_ref, hot, perm, buf, dsend, e_rc, e_rcy, e_rx, e_ry,
    load_s, out_s, cot_s, w_s, w_r, bias_s, bias_r, dw_s, dw_r, ex_s, ex_r, ex2_s, ex2_r, do_s, do_r, e_s, e_r,
):
    sec = lax.axis_index("section")
    lane = lax.axis_index("tensor")
    mate = lane + 1 - 2 * lax.rem(lane, 2)
    over = lax.rem(lane + 2, LANES)
    cross = lax.rem(mate + 2, LANES)
    me = sec * LANES + lane
    devices = 2 * LANES
    clip = me
    clips = (me, sec * LANES + over)

    def group_peer(step):
        peer = lax.rem(me + step, devices)
        return peer, {"section": lax.div(peer, LANES), "tensor": lax.rem(peer, LANES)}

    own = [
        pltpu.make_async_copy(src, dst.at[0], load_s.at[n])
        for n, (src, dst) in enumerate(
            ((h_qkv, w_qkv), (h_proj, w_proj), (h_up, w_up), (h_down, w_down))
        )
    ]

    def place(n, shard, part=None):
        thick = (128, 128, 512, 512)[n]
        base = shard * thick
        cut = pl.ds(pl.multiple_of(base, thick), thick)
        if part is None:
            return (qkv.at[:, :, cut], proj.at[cut, :], up.at[:, cut], down.at[cut, :])[n]
        some = span(part, (256, 64, 256, 256)[n])
        if n == 0:
            return qkv.at[:, some, cut]
        if n == 2:
            return up.at[some, cut]
        few = thick // 2
        rows = pl.ds(pl.multiple_of(base + part * few, few), few)
        return (proj if n == 1 else down).at[rows, :]

    shards = (h_dqkv, h_dproj, h_dup, h_ddown)
    keep = [
        pltpu.make_async_copy(shards[n], place(n, lane), load_s.at[4 + n]) for n in range(4)
    ]
    for copy in own + keep:
        copy.start()
    fetch = pltpu.make_async_copy(cot_hbm.at[clip], cot, cot_s)
    fetch.start()

    barrier = pltpu.get_barrier_semaphore()
    for step in range(1, devices):
        pl.semaphore_signal(barrier, inc=1, device_id_type=MESH, device_id=group_peer(step)[1])
    bias[...] = jnp.zeros_like(bias)
    half = w_proj.shape[1]
    bias[0:1, :] = b_up[...].astype(F32).reshape(1, -1)
    bias[1:3, 0:half] = b_qv[...].astype(F32)
    bias[3:4, 0:512] = b_dup[...].astype(F32).reshape(1, -1)
    bias[4:6, 0:128] = b_dqv[...].astype(F32)
    biases[lane] = bias[...]
    stride = pat.shape[0] // VIS
    for c in range(2):
        row = lax.broadcasted_iota(jnp.int32, (PAD, pat.shape[0]), 0)
        col = lax.broadcasted_iota(jnp.int32, (PAD, pat.shape[0]), 1)
        pick = (col == row * stride + clips[c]).astype(F32).astype(BF16)
        ex[c * PAD : (c + 1) * PAD, :] = nn(pick, pat[...])

    pl.semaphore_wait(barrier, devices - 1)

    def enc_weight(n):
        src = (h_qkv, h_proj, h_up, h_down)[n]
        dst = (w_qkv, w_proj, w_up, w_down)[n]
        return far(src, dst.at[1], w_s.at[n], w_r.at[n], {"tensor": mate})

    def bias_copy(step):
        return far(
            bias, biases.at[lane], bias_s.at[step], bias_r.at[step],
            {"tensor": lax.rem(lane + step, LANES)},
        )

    def half_of(n):
        some = span(sec, (256, 64, 256, 256)[n])
        return shards[n].at[:, some, :] if n == 0 else shards[n].at[some, :]

    def dec_weight(n, kind):
        peer = {"section": 1 - sec} if kind == 2 else {"tensor": over if kind == 0 else mate}
        if kind == 0:
            src, dst = half_of(n), place(n, lane, sec)
        elif kind == 1:
            src, dst = shards[n], place(n, lane)
        else:
            src = dst = place(n, over, 1 - sec if kind == 4 else sec)
        return far(src, dst, dw_s.at[5 * n + kind], dw_r.at[5 * n + kind], peer)

    enc_weight(0).start()
    for step in range(1, LANES):
        bias_copy(step).start()
    enc_weight(1).start()
    dec_weight(0, 0).start()
    enc_weight(2).start()
    enc_weight(3).start()
    for n in range(4):
        dec_weight(n, 1).start()

    def pass_on(n):
        dec_weight(n, 0).wait_recv()
        dec_weight(n, 2).start()
        dec_weight(n, 3).start()

    def pass_last(n):
        dec_weight(n, 2).wait_recv()
        dec_weight(n, 4).start()

    def arrived(n):
        keep[n].wait()
        dec_weight(n, 1).wait_recv()
        dec_weight(n, 3).wait_recv()
        dec_weight(n, 4).wait_recv()

    width = wid[clip]
    bits = jnp.where(width == WIDE, 3, 2)
    turn = shifts[0, clip] * width
    mod = GRID - 1
    spot = 0
    for i in range(order.shape[1]):
        spot = spot + jnp.where(order[0, i] == clip, i, 0)
    batch = spot // CM
    count = 0
    for i in range(order.shape[1]):
        count = count + jnp.where(batch == i // CM, wid[order[0, i]], 0)
    factor_rows = CM * GRID / (jnp.full((1, 1), count, jnp.int32) * GRID_ROWS).astype(F32)

    def slot_of(index):
        return (index - turn) & mod

    def code_of(slot):
        band = ((slot >> bits) + shifts[0, clip]) >> 2
        strip = ((slot & (width - 1)) + shifts[1, clip]) >> 2
        return band * 4 + strip

    def valid_rows():
        slot = slot_of(lax.broadcasted_iota(jnp.int32, (GRID, 1), 0))
        return (slot < GRID_ROWS * width).astype(F32)

    def clip_gradient():
        fetch.wait()
        rolled = slot_of(lax.broadcasted_iota(jnp.int32, (GRID, GRID), 0))
        column = lax.broadcasted_iota(jnp.int32, (GRID, GRID), 1)
        perm[...] = (rolled == column).astype(F32).astype(BF16)
        g = nn(perm[...], cot[...]) * valid_rows() * factor_rows
        g32[...] = g
        gb[...] = g.astype(BF16)
        gt[...] = jnp.transpose(g.astype(BF16))
        d_small[...] = jnp.zeros_like(d_small)
        d_small[5:6, :] = colsum(g)

    seen = vis[pl.ds(clip, 1), :]
    target = jnp.concatenate([(seen + turn) & mod, jnp.full((1, PAD - VIS), -1, jnp.int32)], 1)

    def places(i):
        r = span(i, PAD)
        index = lax.broadcasted_iota(jnp.int32, (PAD, PAD), 0) + i * PAD
        column = lax.broadcasted_iota(jnp.int32, (PAD, PAD), 1)
        hot[r, :] = (index == target).astype(F32).astype(BF16)
        slot = slot_of(index)
        by_row = ((slot >> bits) == column).astype(F32).astype(BF16)
        by_col = ((slot & (width - 1)) == column).astype(F32).astype(BF16)
        row_part = nn(by_row, table[0]) + nn(by_row, table[1])
        col_part = nn(by_col, table[0]) + nn(by_col, table[1])
        x0[r, :] = jnp.concatenate([row_part, col_part], 1)

    egain = gains[...].astype(F32)
    eoff = offs[...].astype(F32)
    emarks = head_marks(half, ENC_SIZE, BF16)
    key = lax.broadcasted_iota(jnp.int32, (PAD, PAD), 1)
    floor = jnp.where(key < VIS, NEG * LOG2E, -1e30)
    eones = ones_per_head(PAD, emarks)
    blocks = D // 256

    def give_part(i, side):
        cut = span(i, 256)
        return far(
            esend.at[(1 - side) * PAD : (2 - side) * PAD, cut],
            erecv.at[side * PAD : (side + 1) * PAD, cut],
            ex_s.at[2 * i + side], ex_r.at[2 * i + side], {"tensor": over},
        )

    for c in range(2):
        rows = slice(c * PAD, (c + 1) * PAD)
        hat, _ = normal(ex[rows, :])
        ea[rows, :] = (hat * egain[0:1] + eoff[0:1]).astype(BF16)
        limit = (VIS * wid[clips[c]]) // WIDE
        for g, shard in enumerate((lane, mate)):
            if c == 0 and g == 0:
                own[0].wait()
            if c == 0 and g == 1:
                enc_weight(0).wait_recv()
                for step in range(1, LANES):
                    bias_copy(step).wait_recv()
            if g == 0:
                bq, bv = bias[1:2, 0:half], bias[2:3, 0:half]
            else:
                bq, bv = biases[shard, 1:2, 0:half], biases[shard, 2:3, 0:half]
            eqkv[g, 0, rows] = (nt(ea[rows, :], w_qkv[g, 0]) + bq).astype(BF16)
            eqkv[g, 1, rows] = nt(ea[rows, :], w_qkv[g, 1]).astype(BF16)
            eqkv[g, 2, rows] = (nt(ea[rows, :], w_qkv[g, 2]) + bv).astype(BF16)
            p, out, _ = attend(
                eqkv[g, 0, rows], eqkv[g, 1, rows], eqkv[g, 2, rows], emarks, eones,
                lambda s: jnp.where(key < limit, s, floor), ENC_SCALE,
            )
            ep[g, c] = p
            eo[g, rows] = out
        if c == 0:
            own[1].wait()
            enc_weight(1).wait_recv()
        for i in range(blocks):
            cut = slice(i * 256, (i + 1) * 256)
            t = nn(eo[0, rows], w_proj[0, :, cut]) + nn(eo[1, rows], w_proj[1, :, cut])
            epart[rows, cut] = t
            esend[rows, cut] = t.astype(BF16)
            give_part(i, 1 - c).start()
    pass_on(0)
    clip_gradient()
    own[2].wait()
    enc_weight(2).wait_recv()

    def give_last(i):
        cut = span(i, 256)
        return far(
            esend2.at[:, cut], erecv2.at[:, cut], ex2_s.at[i], ex2_r.at[i], {"tensor": over}
        )

    for c in (1, 0):
        rows = slice(c * PAD, (c + 1) * PAD)
        for i in range(blocks):
            give_part(i, c).wait_recv()
        t = ex[rows, :] + epart[rows, :] + erecv[rows, :].astype(F32) + eoff[2:3]
        ex1[rows, :] = t
        hat, _ = normal(t)
        eu[rows, :] = (hat * egain[1:2] + eoff[1:2]).astype(BF16)
        for g, shard in enumerate((lane, mate)):

            def enc_ff(i, g=g, shard=shard, rows=rows):
                cut = span(i, 256)
                h = nn(eu[rows, :], w_up[g, :, cut]) + biases[shard, 0:1, cut]
                act, slope = gelu_both(h)
                ey[g, rows, cut] = act.astype(BF16)
                egp[g, rows, cut] = slope.astype(BF16)

            loop(w_up.shape[2] // 256, enc_ff, unroll=3)
        if c == 1:
            own[3].wait()
            enc_weight(3).wait_recv()
        for i in range(blocks):
            cut = slice(i * 256, (i + 1) * 256)
            t = nn(ey[0, rows], w_down[0, :, cut]) + nn(ey[1, rows], w_down[1, :, cut])
            if c == 0:
                eown[:, cut] = t
            else:
                esend2[:, cut] = t.astype(BF16)
                give_last(i).start()
        if c == 1:
            for n in (1, 2, 3):
                dec_weight(n, 0).start()
            pass_last(0)
    outs = [
        pltpu.make_async_copy(src, dst, out_s.at[n])
        for n, (src, dst) in enumerate(
            (
                (ex.at[0:PAD, :], o_x), (ex1, o_x1), (ea, o_a), (eu, o_u), (ey, o_y), (egp, o_gp),
                (eqkv, o_qkv), (ep, o_p), (eo, o_o), (w_qkv.at[1], o_w), (w_proj.at[1], o_wproj),
                (w_up.at[1], o_wup), (w_down.at[1], o_wdown),
            )
        )
    ]
    for copy in outs:
        copy.start()
    loop(GRID // PAD, places, unroll=2)
    for i in range(blocks):
        give_last(i).wait_recv()

    e_ref[...] = (ex1[0:PAD, :] + eown[...] + erecv2[...].astype(F32) + eoff[3:4]).astype(BF16)
    vec = evec[...].astype(F32)
    m = (nn(e_ref[...], ew[...]) + vec[0:1]).astype(BF16)
    gain = dgains[...].astype(F32)
    offsets = doffs[...].astype(F32)

    def start(i):
        r = span(i, PAD)
        oh = hot[r, :]
        hit = jnp.sum(oh.astype(F32), -1, keepdims=True)
        x = jnp.where(hit > 0, nn(oh, m), vec[1:2]).astype(BF16).astype(F32) + x0[r, :]
        x0[r, :] = x
        hat, _ = normal(x)
        a[r, :] = (hat * gain[0:1] + offsets[0:1]).astype(BF16)

    loop(GRID // PAD, start, unroll=2)
    arrived(0)

    def dec_bias(row, size):
        return jnp.concatenate([biases[k, row : row + 1, 0:size] for k in range(LANES)], 1)

    acts[0] = (nn(a[...], qkv[0]) + dec_bias(4, 128)).astype(BF16)
    acts[1] = nn(a[...], qkv[1]).astype(BF16)
    acts[2] = (nn(a[...], qkv[2]) + dec_bias(5, 128)).astype(BF16)
    pass_on(1)
    pass_on(2)
    marks = head_marks(128, DEC_SIZE, BF16)
    marks32 = head_marks(128, DEC_SIZE, F32)
    dim = lax.broadcasted_iota(jnp.int32, (128, 1), 0)
    rows32 = [
        ((dim >= h * DEC_SIZE) & (dim < (h + 1) * DEC_SIZE)).astype(F32) for h in range(len(marks))
    ]

    ones = ones_per_head(PAD, marks)

    def attention(i):
        r = span(i, PAD)
        row_slot = slot_of(lax.broadcasted_iota(jnp.int32, (PAD, PAD), 0) + i * PAD)
        key_slot = slot_of(lax.broadcasted_iota(jnp.int32, (PAD, PAD), 1) + i * PAD)
        allowed = (code_of(row_slot) == code_of(key_slot)) & (key_slot < GRID_ROWS * width)
        for g in range(DD // 128):
            c = slice(g * 128, (g + 1) * 128)
            probs[i, :, g * 512 : (g + 1) * 512], o[r, c], inverse[r, c] = attend(
                acts[0, r, c], acts[1, r, c], acts[2, r, c], marks, ones,
                lambda s: jnp.where(allowed, s, NEG * LOG2E), DEC_SCALE,
            )

    loop(GRID // PAD, attention, unroll=4)
    pass_last(1)
    pass_last(2)
    pass_on(3)
    arrived(1)

    def mix(i):
        r = span(i, 256)
        x = x0[r, :] + nn(o[r, :], proj[...]) + offsets[2:3]
        x1[r, :] = x
        hat, _ = normal(x)
        un = hat * gain[1:2] + offsets[1:2]
        u[r, :] = un.astype(BF16)
        ut[:, r] = jnp.transpose(un.astype(BF16))

    loop(2, mix)
    pass_last(3)
    arrived(2)

    def ff(i):
        c = span(i, 256)
        h = nn(u[...], up[:, c]) + biases[lax.div(i, 2), 3:4, span(lax.rem(i, 2), 256)]
        act, slope = gelu_both(h)
        y[:, c] = act.astype(BF16)
        gp[:, c] = slope.astype(BF16)

    loop(up.shape[1] // 256, ff, unroll=4)
    arrived(3)
    def out(i):
        c = span(i, 256)
        acc[:, c] = nn(y[...], down[:, c])

    loop(2, out)
    full = ((acc[...] + x1[...] + offsets[3:4]) * valid_rows()).astype(BF16)
    turned = tn(full, perm[...]).astype(BF16)
    for k in range(devices):
        dsend[k] = turned[k * dsend.shape[1] : (k + 1) * dsend.shape[1]]

    def decoded_copy(step):
        peer, spot = group_peer(step)
        return far(dsend.at[peer], dec_out.at[me], do_s.at[step], do_r.at[step], spot)

    for step in range(1, devices):
        decoded_copy(step).start()
    dec_out[me] = dsend[me]

    def ff_back(shard):
        for side in range(2):
            c = span(2 * shard + side, 256)
            d_down = nn(gt[...], y[:, c]).astype(BF16)
            dh = nt(gb[...], down[c, :]) * gp[:, c].astype(F32)
            d_upb[:, c] = colsum(dh)
            du = dh.astype(BF16)
            gp[:, c] = du
            d_up = nn(ut[...], du).astype(BF16)
            for block in range(GRID // CH):
                rows = slice(block * CH, (block + 1) * CH)
                h, top, col = tile_of(4 * block + side)
                buf[shard, h, top : top + CH, col : col + 256] = d_up[rows]
                h, top, col = tile_of(4 * block + 2 + side)
                buf[shard, h, top : top + CH, col : col + 256] = d_down[rows]

    def early_core(which):
        shard, land = ((mate, e_rc), (cross, e_rcy))[which]
        return far(
            buf.at[shard, :, 0:EARLY_ROWS, :], land, e_s.at[which], e_r.at[which], {"tensor": mate}
        )

    def early_x(which):
        return far(
            buf.at[(over, lane)[which], 1 - sec, 0:EARLY_ROWS, :], e_rx.at[which],
            e_s.at[2 + which], e_r.at[2 + which], {"section": 1 - sec},
        )

    def early_y():
        return far(
            buf.at[over, sec, 0:EARLY_ROWS, :], e_ry, e_s.at[4], e_r.at[4], {"tensor": over}
        )

    def early_add(shard, land):
        def body(i):
            r = span(i, CH)
            buf[shard, :, r, :] = buf[shard, :, r, :] + land[:, r, :]

        loop(EARLY_ROWS // CH, body)

    def early_half(shard, land):
        buf[shard, sec, 0:EARLY_ROWS, :] = buf[shard, sec, 0:EARLY_ROWS, :] + land

    def ff_step(i):
        ff_back(jnp.where(i == 0, cross, jnp.where(i == 1, over, jnp.where(i == 2, mate, lane))))

        @pl.when(i == 1)
        def _():
            early_core(1).start()

        @pl.when(i == 2)
        def _():
            early_core(0).start()

    loop(LANES, ff_step)
    early_core(1).wait_recv()
    early_add(over, e_rcy)
    early_x(0).start()

    def ff_in(i):
        c = span(i, 256)
        acc[:, c] = nt(gp[...], up[c, :])

    loop(2, ff_in)
    early_core(0).wait_recv()
    early_add(lane, e_rc)
    early_x(1).start()

    def mix_back(i):
        r = span(i, 256)
        hat, scale = normal(x1[r, :])
        da = acc[r, :]
        dx = g32[r, :] + normal_back(da, hat, scale, gain[1:2])
        d_small[1:2, :] += colsum(da * hat)
        d_small[3:4, :] += colsum(da)
        d_small[4:5, :] += colsum(dx)
        g32[r, :] = dx
        dxb = dx.astype(BF16)
        gb[r, :] = dxb
        u[r, :] = nt(dxb, proj[...]).astype(BF16)

    loop(2, mix_back)
    d_proj = tn(o[...], gb[...]).astype(BF16)
    for block in range(GRID // CH):
        h, top, col = tile_of(33 + 2 * block)
        side = slice(block // 2 * 128, (block // 2 + 1) * 128)
        for k in range(LANES):
            row = k * 128 + block % 2 * CH
            buf[k, h, top : top + CH, col + 128 : col + 256] = d_proj[row : row + CH, side]

    def attention_back(i):
        r = span(i, PAD)
        for k in range(DD // 128):
            c = slice(k * 128, (k + 1) * 128)
            acts[0, r, c], acts[1, r, c], acts[2, r, c] = attend_back(
                acts[0, r, c], acts[1, r, c], acts[2, r, c],
                probs[i, :, k * 512 : (k + 1) * 512], o[r, c], inverse[r, c], u[r, c],
                marks, marks32, rows32, ones, DEC_SCALE,
            )

    loop(GRID // PAD, attention_back, unroll=4)
    early_x(0).wait_recv()
    early_half(over, e_rx[0])
    early_y().start()
    d_qvb[0:1, :] = colsum(acts[0].astype(F32))
    d_qvb[1:2, :] = colsum(acts[2].astype(F32))

    def project_back(i):
        c = span(i, 256)
        acc[:, c] = (
            nt(acts[0], qkv[0, c, :]) + nt(acts[1], qkv[1, c, :]) + nt(acts[2], qkv[2, c, :])
        )

    loop(2, project_back)
    gt[...] = jnp.transpose(a[...])
    for j in range(3):
        d_qkv = nn(gt[...], acts[j]).astype(BF16)
        for block in range(GRID // CH):
            h, top, col = tile_of(32 + 2 * block + j // 2)
            col = col + j % 2 * 128
            rows = slice(block * CH, (block + 1) * CH)
            for k in range(LANES):
                buf[k, h, top : top + CH, col : col + 128] = d_qkv[rows, k * 128 : (k + 1) * 128]

    def start_back(i):
        r = span(i, PAD)
        hat, scale = normal(x0[r, :])
        da = acc[r, :]
        dx = g32[r, :] + normal_back(da, hat, scale, gain[0:1])
        d_small[0:1, :] += colsum(da * hat)
        d_small[2:3, :] += colsum(da)
        dg = dx.astype(BF16)
        gb[r, :] = dg
        hit = jnp.sum(hot[r, :].astype(F32), -1, keepdims=True)
        d_small[7:8, :] += colsum(jnp.where(hit > 0, 0.0, dg.astype(F32)))

    loop(GRID // PAD, start_back, unroll=2)
    dm = tn(hot[...], gb[...])
    d_small[6:7, :] = colsum(dm)
    dmb = dm.astype(BF16)
    d_enc[...] = nt(dmb, ew[...]).astype(BF16)
    d_ew = tn(e_ref[...], dmb).astype(BF16)
    for k in range(LANES):
        for h in range(2):
            top = k * 192 + h * 64
            buf[k, h, 512:576, 0:512] = d_ew[top : top + 64]
            buf[k, h, 512:576, 512:768] = d_ew[k * 192 + 128 : (k + 1) * 192, h * 256 : (h + 1) * 256]

    early_x(1).wait_recv()
    early_half(lane, e_rx[1])
    early_y().wait_recv()
    early_half(lane, e_ry[...])
    later = pl.ds(EARLY_ROWS, DEC_ROWS - EARLY_ROWS)
    rest = [pltpu.make_async_copy(buf.at[lane], o_dec.at[lane], out_s.at[13])] + [
        pltpu.make_async_copy(buf.at[k, :, later, :], o_dec.at[k, :, later, :], out_s.at[14 + n])
        for n, k in enumerate((mate, over, cross))
    ]
    for copy in rest:
        copy.start()
    for copy in outs + rest:
        copy.wait()
    for which in range(2):
        early_core(which).wait_send()
        early_x(which).wait_send()
    early_y().wait_send()
    for n in range(4):
        enc_weight(n).wait_send()
        for kind in range(5):
            dec_weight(n, kind).wait_send()
    for step in range(1, LANES):
        bias_copy(step).wait_send()
    for i in range(blocks):
        give_part(i, 0).wait_send()
        give_part(i, 1).wait_send()
        give_last(i).wait_send()
    for step in range(1, devices):
        decoded_copy(step).wait()


def forward_call(args, half, hid, dff):
    dma = lambda *s: pltpu.SemaphoreType.DMA(s)
    vm = lambda dtype, *shape: pltpu.VMEM(shape, dtype)
    rows = 2 * PAD
    keys = PAD * half // ENC_SIZE
    devices = 2 * LANES
    slab = DD // devices
    kept = [
        ((PAD, D), F32), ((rows, D), F32), ((rows, D), BF16), ((rows, D), BF16),
        ((2, rows, hid), BF16), ((2, rows, hid), BF16), ((2, 3, rows, half), BF16),
        ((2, 2, PAD, keys), BF16), ((2, rows, half), BF16),
        ((3, half, D), BF16), ((half, D), BF16), ((D, hid), BF16), ((hid, D), BF16),
        ((LANES, 2, DEC_ROWS, D), BF16),
    ]
    made = [
        ((PAD, D), BF16), ((2, DD), F32), ((1, dff), F32), ((8, DD), F32),
        ((devices, slab, GRID), BF16),
    ]
    return pl.pallas_call(
        forward_and_decoder,
        out_shape=[jax.ShapeDtypeStruct(s, d) for s, d in kept + made],
        in_specs=[SM, SM, SM] + [VM] * 8 + [ANY] * 9 + [VM] * 5,
        out_specs=[ANY] * len(kept) + [VM] * len(made),
        scratch_shapes=[
            vm(BF16, 2, 3, half, D), vm(BF16, 2, half, D), vm(BF16, 2, D, hid), vm(BF16, 2, hid, D),
            vm(F32, 8, D), vm(F32, LANES, 8, D),
            vm(BF16, 3, DD, DD), vm(BF16, DD, DD), vm(BF16, DD, dff), vm(BF16, dff, DD),
            vm(F32, rows, D), vm(BF16, rows, D), vm(BF16, rows, D), vm(BF16, 2, rows, hid),
            vm(BF16, 2, rows, hid), vm(BF16, 2, 3, rows, half), vm(BF16, 2, 2, PAD, keys),
            vm(BF16, 2, rows, half), vm(F32, rows, D), vm(F32, rows, D), vm(BF16, rows, D),
            vm(BF16, rows, D), vm(BF16, PAD, D), vm(BF16, PAD, D), vm(F32, PAD, D),
            vm(BF16, GRID, DD), vm(F32, GRID, DD), vm(F32, GRID, DD), vm(BF16, GRID, DD),
            vm(BF16, 3, GRID, DD), vm(BF16, GRID // PAD, PAD, DHEADS * PAD), vm(BF16, GRID, DD),
            vm(F32, GRID, DD),
            vm(BF16, GRID, DD), vm(BF16, DD, GRID), vm(BF16, GRID, dff), vm(BF16, GRID, dff),
            vm(F32, GRID, DD), vm(BF16, GRID, DD), vm(BF16, DD, GRID), vm(F32, GRID, DD),
            vm(BF16, PAD, D), vm(BF16, GRID, PAD), vm(BF16, GRID, GRID),
            vm(BF16, LANES, 2, DEC_ROWS, D),
            vm(BF16, devices, slab, GRID), *[vm(BF16, 2, EARLY_ROWS, D)] * 3, vm(BF16, EARLY_ROWS, D),
            dma(8), dma(17), pltpu.SemaphoreType.DMA, dma(4), dma(4), dma(LANES), dma(LANES),
            dma(20), dma(20), dma(6), dma(6), dma(3), dma(3), dma(devices), dma(devices),
            dma(5), dma(5),
        ],
        compiler_params=pltpu.CompilerParams(
            collective_id=0, has_side_effects=True, vmem_limit_bytes=VMEM_LIMIT
        ),
    )(*args)


def add(x, y):
    return x + y


def backward_and_sums(
    d_enc, gains,
    h_u, h_y, h_gp, h_down0, h_down1, h_up0, h_up1,
    h_x, h_x1, h_a, h_qkv, h_p, h_o, h_w0, h_w1, h_proj0, h_proj1,
    dec, dec_qvb, dec_upb, dec_small,
    total, emb, dx_out,
    gb, ut, part, send, recv, du, gx, dx1, d_o, d_acts, own, send1, recv1, dx32, dx,
    d_upb, d_qvb, d_small,
    acc, yacc, enc_mate, out, rcy, ry, land_x, land_l, land_r, small32, small,
    u, y, gp, down0, down1, up0, up1, x, x1, a, qkv, p, o, w0, w1, proj0, proj1, fetch_s,
    load_s, flush_s, ex_s, ex_r,
    core_s, core_r, corey_s, corey_r, y_s, y_r, x_s, x_r, z_s, zl_r, zr_r,
    bl_s, br_s, b_r, a_s, a_r, emb_s, emb_r, dx_s, dx_r,
):
    sec = lax.axis_index("section")
    lane = lax.axis_index("tensor")
    pos = lax.axis_index("dp")
    count = lax.axis_size("dp")
    mate = lane + 1 - 2 * lax.rem(lane, 2)
    over = lax.rem(lane + 2, LANES)
    cross = lax.rem(mate + 2, LANES)
    first = pos == 0
    last = pos == count - 1
    me = sec * LANES + lane
    devices = 2 * LANES

    def group_peer(step):
        peer = lax.rem(me + step, devices)
        return peer, {"section": lax.div(peer, LANES), "tensor": lax.rem(peer, LANES)}

    barrier = pltpu.get_barrier_semaphore()
    for step in range(1, devices):
        pl.semaphore_signal(barrier, inc=1, device_id_type=MESH, device_id=group_peer(step)[1])

    @pl.when(pos > 0)
    def _():
        pl.semaphore_signal(barrier, inc=1, device_id={"dp": pos - 1}, device_id_type=MESH)

    @pl.when(pos < count - 1)
    def _():
        pl.semaphore_signal(barrier, inc=1, device_id={"dp": pos + 1}, device_id_type=MESH)

    loads = [
        pltpu.make_async_copy(dec.at[lane], acc.at[:, 0:DEC_ROWS, :], load_s.at[0]),
        pltpu.make_async_copy(
            dec.at[over, :, EARLY_ROWS:DEC_ROWS, :], yacc.at[:, 0 : DEC_ROWS - EARLY_ROWS, :],
            load_s.at[1],
        ),
    ]
    for load in loads:
        load.start()
    fetches = [
        pltpu.make_async_copy(src, dst, fetch_s.at[n])
        for n, (src, dst) in enumerate(
            (
                (h_u, u), (h_y, y), (h_gp, gp), (h_down0, down0), (h_down1, down1), (h_up0, up0),
                (h_up1, up1), (h_x, x), (h_x1, x1), (h_a, a), (h_qkv, qkv), (h_p, p), (h_o, o),
                (h_w0, w0), (h_w1, w1), (h_proj0, proj0), (h_proj1, proj1),
            )
        )
    ]
    for fetch in fetches:
        fetch.start()
    small32[...] = jnp.zeros_like(small32)
    d_small[...] = jnp.zeros_like(d_small)
    gb[0:PAD, :] = d_enc[...]
    ends = jnp.where(first, 0, 1) + jnp.where(last, 0, 1)
    pl.semaphore_wait(barrier, devices - 1 + ends)

    gain = gains[...].astype(F32)
    width = w0.shape[1]
    marks = head_marks(width, ENC_SIZE, BF16)
    marks32 = head_marks(width, ENC_SIZE, F32)
    ones = ones_per_head(PAD, marks)

    def rows(k, size=CH):
        return pl.ds(pl.multiple_of(k * size, size), size)

    def give_enc():
        return far(d_enc, gb.at[PAD : 2 * PAD, :], ex_s.at[0], ex_r.at[0], {"tensor": over})

    def give_part(i, half):
        cut = rows(i, 256)
        n = 1 + 2 * i + half
        return far(
            send.at[(1 - half) * PAD : (2 - half) * PAD, cut],
            recv.at[half * PAD : (half + 1) * PAD, cut],
            ex_s.at[n], ex_r.at[n], {"tensor": over},
        )

    def give_last(i):
        cut = rows(i, 256)
        return far(send1.at[:, cut], recv1.at[:, cut], ex_s.at[7 + i], ex_r.at[7 + i], {"tensor": over})

    def ff_back(g, i, down):
        c = rows(i, 256)
        d_down = tn(y[g, :, c], gb[...]).astype(BF16)
        dh = nt(gb[...], down[c, :]) * gp[g, :, c].astype(F32)
        d_upb[g, :, c] = colsum(dh)
        dub = dh.astype(BF16)
        du[g, :, c] = dub
        d_up = nn(ut[...], dub).astype(BF16)
        if g == 0:
            acc[1, pl.ds(pl.multiple_of(A_TOP + i * 256, 64), 256), :] = d_down
            acc[0, A_TOP:B_TOP, c] = d_up
        else:
            enc_mate[1, c, :] = d_down
            enc_mate[0, 0:ENC_A, c] = d_up

    def ff_in(i):
        c = rows(i, 256)
        t = nt(du[0], up0[c, :]) + nt(du[1], up1[c, :])
        part[:, c] = t
        send[:, c] = t.astype(BF16)
        give_part(i, 0).start()
        give_part(i, 1).start()

    def norm_two():
        for fetch in fetches[7:]:
            fetch.wait()
        for k in range(D // 256):
            give_part(k, 0).wait_recv()
            give_part(k, 1).wait_recv()

        def body(j):
            r = rows(j, 64)
            da = part[r, :] + recv[r, :].astype(F32)
            hat, scale = normal(x1[r, :])
            g = gb[r, :].astype(F32)
            d = g + normal_back(da, hat, scale, gain[1:2])
            gx[r, :] = d.astype(BF16)
            dx1[r, :] = d

            @pl.when(j < 2)
            def _():
                d_small[1:2, :] += colsum(da * hat)
                d_small[3:4, :] += colsum(da)
                d_small[4:5, :] += colsum(d)
                d_small[5:6, :] += colsum(g)

        loop(2 * PAD // 64, body)

    def attention(g, c):
        if c == 0:
            d_proj = tn(o[g], gx[...]).astype(BF16)
            if g == 0:
                acc[1, B_TOP + width : S_TOP, :] = d_proj
            else:
                enc_mate[1, ENC_A + width : ENC_A + 2 * width, :] = d_proj
            d_o[...] = nt(gx[...], (proj0, proj1)[g][...]).astype(BF16)
        r = slice(c * PAD, (c + 1) * PAD)
        d_acts[g, 0, r], d_acts[g, 1, r], d_acts[g, 2, r] = attend_back(
            qkv[g, 0, r], qkv[g, 1, r], qkv[g, 2, r], p[g, c], o[g, r], 1.0 / nn(p[g, c], ones),
            d_o[r, :], marks, marks32, None, ones, ENC_SCALE,
        )
        if c == 1:
            d_qvb[g, 0:1, :] = colsum(d_acts[g, 0].astype(F32))
            d_qvb[g, 1:2, :] = colsum(d_acts[g, 2].astype(F32))

    def project_in(i):
        c = rows(i, 256)
        t = 0.0
        for g, w in enumerate((w0, w1)):
            for j in range(3):
                t += nn(d_acts[g, j], w[j, :, c])
        own[:, c] = t[:PAD]
        send1[:, c] = t[PAD:].astype(BF16)
        give_last(i).start()

    def project_grad(g):
        for j in range(3):
            row = (j % 2) * width
            d = tn(d_acts[g, j], a[...]).astype(BF16)
            if g == 0:
                acc[j // 2, B_TOP + row : B_TOP + row + width, :] = d
            else:
                enc_mate[j // 2, ENC_A + row : ENC_A + row + width, :] = d

    def norm_one():
        for k in range(D // 256):
            give_last(k).wait_recv()

        def body(j):
            r = rows(j, 64)
            da = own[r, :] + recv1[r, :].astype(F32)
            hat, scale = normal(x[r, :])
            d_small[0:1, :] += colsum(da * hat)
            d_small[2:3, :] += colsum(da)
            dx32[r, :] = dx1[r, :] + normal_back(da, hat, scale, gain[0:1])

        loop(PAD // 64, body)
        turned = jnp.transpose(dx32[...])
        cut = D // devices
        for k in range(devices):
            dx[k] = turned[k * cut : (k + 1) * cut, 0:VIS].astype(BF16)
        for r in range(LANES):
            small32[r, 8:9, 0:512] = dec_upb[:, r * 512 : (r + 1) * 512]
            small32[r, 9:10, 0:128] = dec_qvb[0:1, r * 128 : (r + 1) * 128]
            small32[r, 9:10, 128:256] = dec_qvb[1:2, r * 128 : (r + 1) * 128]
            small32[r, 0:8, 0:512] = dec_small[...]
            small32[r, 16:24, :] = d_small[...]
        for g, shard in enumerate((lane, mate)):
            small32[shard, 10:11, :] = d_upb[g]
            small32[shard, 11:12, 0:192] = d_qvb[g, 0:1]
            small32[shard, 11:12, 256:448] = d_qvb[g, 1:2]
        for r in range(LANES):
            for h in range(2):
                small[r, h] = small32[r, h * SMALL : (h + 1) * SMALL].astype(BF16)
        acc[:, S_TOP : S_TOP + SMALL, :] = small[lane]
        yacc[:, DEC_ROWS - EARLY_ROWS :, :] = small[over]
        core_copy(LATE, small.at[mate], SMALL).start()
        corey_copy(LATE, small.at[cross], SMALL).start()
        for step in range(1, devices):
            dx_copy(step).start()
        dx_out[me] = dx[me]

    def core_enc(lo, hi):
        for m, block in enumerate(ORDER):
            if lo <= block < hi:
                src = pl.ds(block * CH - DEC_ROWS, CH)
                core_copy(m, enc_mate.at[:, src, :]).start()

    def first_piece():
        for fetch in fetches[:7]:
            fetch.wait()
        ut[...] = jnp.transpose(u[...])
        give_enc().wait_recv()

    def ff_step(k):
        for g, down in enumerate((down0, down1)):
            @pl.when(lax.rem(k, 2) == g)
            def _(g=g, down=down):
                ff_back(g, lax.div(k, 2), down)

    def run_pieces(n):
        def several(low, high, body):
            begin = sum(jnp.where(n > t, 1, 0) for t in PIECES[low:high])
            end = sum(jnp.where(n >= t, 1, 0) for t in PIECES[low:high])
            lax.fori_loop(begin, end, lambda k, c: (body(k), c)[1], 0)

        def single(k, body):
            @pl.when(n == PIECES[k])
            def _():
                body()

        single(0, first_piece)
        several(1, 7, ff_step)
        single(7, lambda: core_enc(DEC_K, DEC_K + ENC_A // CH))
        several(8, 11, ff_in)
        single(11, norm_two)
        for k in range(4):
            single(12 + k, lambda k=k: attention(k // 2, k % 2))
        several(16, 19, project_in)
        for g in range(2):
            single(19 + g, lambda g=g: project_grad(g))
        single(21, lambda: core_enc(DEC_K + ENC_A // CH, B_K))
        single(22, norm_one)

    def dx_copy(step):
        peer, place = group_peer(step)
        return far(dx.at[peer], dx_out.at[me], dx_s.at[step], dx_r.at[step], place)

    def emb_copy(step):
        return far(
            out.at[:, pl.ds(512, CH), :], emb.at[lane], emb_s.at[step], emb_r.at[step],
            {"tensor": lax.rem(lane + step, LANES)},
        )

    def block_of(m):
        if isinstance(m, int):
            return ORDER[m]
        shift = 0
        for k in range(1, ALL_K):
            if ORDER[k] - k != ORDER[k - 1] - k + 1:
                shift = jnp.where(m >= k, ORDER[k] - k, shift)
        return m + shift

    def is_dec(m):
        return (block_of(m) < DEC_K) & (m >= EARLY)

    def at(m, size=CH):
        if isinstance(m, int):
            return pl.ds(ORDER[m] * CH, size)
        return pl.ds(pl.multiple_of(block_of(m) * CH, CH), size)

    def slot(m, size=CH):
        if isinstance(m, int):
            return pl.ds(m * CH, size)
        return pl.ds(pl.multiple_of(m * CH, CH), size)

    def y_at(m, size=CH):
        if isinstance(m, int):
            return pl.ds((min(ORDER[m], DEC_K) - EARLY) * CH, size)
        return pl.ds(pl.multiple_of((jnp.minimum(block_of(m), DEC_K) - EARLY) * CH, CH), size)

    def core_copy(m, src, size=CH):
        return far(src, out.at[:, at(m, size), :], core_s.at[m], core_r.at[m], {"tensor": mate})

    def corey_copy(m, src, size=CH):
        return far(src, rcy.at[:, y_at(m, size), :], corey_s.at[m], corey_r.at[m], {"tensor": mate})

    def y_copy(m, size=CH):
        cut = y_at(m, size)
        return far(
            yacc.at[:, cut, :], ry.at[:, cut, :], y_s.at[m], y_r.at[m], {"tensor": over}
        )

    def x_copy(m, size=CH):
        return far(
            acc.at[1 - sec, at(m, size), :], land_x.at[0, slot(m, size), :], x_s.at[m], x_r.at[m],
            {"section": 1 - sec},
        )

    def xc_copy(m):
        return far(
            acc.at[:, at(m), :], land_x.at[:, slot(m), :], x_s.at[m], x_r.at[m],
            {"section": 1 - sec},
        )

    def z_copy(m, whole, right, size=CH):
        land = land_l if right else land_r
        if whole:
            src, dst = acc.at[:, at(m), :], land.at[:, slot(m), :]
        else:
            src, dst = acc.at[sec, at(m, size), :], land.at[0, slot(m, size), :]
        landed = zl_r if right else zr_r
        return far(src, dst, z_s.at[m], landed.at[m], {"dp": pos + 1 if right else pos - 1})

    def b_copy(m, whole, right, size=CH):
        place = out.at[:, at(m), :] if whole else out.at[sec, at(m, size), :]
        sent = br_s if right else bl_s
        return far(place, place, sent.at[m], b_r.at[m], {"dp": pos + 1 if right else pos - 1})

    def a_copy(m, size=CH):
        place = out.at[sec, at(m, size), :]
        return far(place, place, a_s.at[m], a_r.at[m], {"section": 1 - sec})

    def a_wait(m, size=CH):
        place = out.at[1 - sec, at(m, size), :]
        far(place, place, a_s.at[m], a_r.at[m], {"section": 1 - sec}).wait_recv()

    give_enc().start()

    for m in range(EARLY, ALL_K):
        if ORDER[m] < DEC_K:
            core_copy(m, dec.at[mate, :, at(m), :]).start()
            corey_copy(m, dec.at[cross, :, at(m), :]).start()
    for load in loads:
        load.wait()

    def join_core(m, size):
        core_copy(m, out.at[:, at(m, size), :], size).wait_recv()
        acc[:, at(m, size), :] = add(acc[:, at(m, size), :], out[:, at(m, size), :])

    def join_core_y(m, size):
        corey_copy(m, rcy.at[:, y_at(m, size), :], size).wait_recv()
        yacc[:, y_at(m, size), :] = add(yacc[:, y_at(m, size), :], rcy[:, y_at(m, size), :])
        y_copy(m, size).start()

    def stage_c(m):
        @pl.when((m >= EARLY) & (m != LATE))
        def _():
            join_core(m, CH)

            @pl.when(is_dec(m))
            def _():
                join_core_y(m, CH)

        @pl.when(m == LATE)
        def _():
            join_core(m, SMALL)
            join_core_y(m, SMALL)

    def flush(m):
        return pltpu.make_async_copy(
            out.at[:, at(m), :], total.at[:, at(m), :], flush_s.at[m]
        )

    def finished(m):
        flush(m).start()

        @pl.when(block_of(m) == DEC_K - 1)
        def _():
            for step in range(1, LANES):
                emb_copy(step).start()
            emb[lane] = out[:, 512 : 512 + CH, :]

    def line_of(root, whole, size=CH):
        left = pos < root
        right = pos > root
        here = pos == root
        reach = max(root, count - 1 - root)
        level = jnp.where(left, pos, jnp.where(right, count - 1 - pos, reach))
        dist = jnp.where(left, root - pos, pos - root)

        def view(ref, m):
            return ref.at[:, at(m), :] if whole else ref.at[sec, at(m, size), :]

        def landed(ref, m):
            return ref.at[:, slot(m), :] if whole else ref.at[0, slot(m, size), :]

        def hop(m, rightward):
            return z_copy(m, whole, rightward, size)

        def back_hop(m, rightward):
            return b_copy(m, whole, rightward, size)

        def outer(m):
            @pl.when(left & first)
            def _():
                hop(m, True).start()

            @pl.when(right & last)
            def _():
                hop(m, False).start()

        def inward(m):
            @pl.when(left & (pos > 0))
            def _():
                hop(m, True).wait_recv()
                view(acc, m)[...] = add(view(acc, m)[...], landed(land_l, m)[...])
                hop(m, True).start()

            @pl.when(right & (pos < count - 1))
            def _():
                hop(m, False).wait_recv()
                view(acc, m)[...] = add(view(acc, m)[...], landed(land_r, m)[...])
                hop(m, False).start()

            @pl.when(here)
            def _():
                total = view(acc, m)[...].astype(F32)
                if root > 0:
                    hop(m, True).wait_recv()
                    total = total + landed(land_l, m)[...].astype(F32)
                if root < count - 1:
                    hop(m, False).wait_recv()
                    total = total + landed(land_r, m)[...].astype(F32)
                if whole:
                    view(acc, m)[...] = total.astype(BF16)
                    xc_copy(m).start()
                else:
                    view(out, m)[...] = total.astype(BF16)
                    spread(m)
                    a_copy(m, size).start()

        def spread(m):
            if root > 0:
                back_hop(m, False).start()
            if root < count - 1:
                back_hop(m, True).start()

        def crossed(m):
            xc_copy(m).wait_recv()
            view(out, m)[...] = add(view(acc, m)[...], landed(land_x, m)[...])
            spread(m)
            finished(m)

        def outward(m):
            back_hop(m, False).wait_recv()

            @pl.when(left & (pos > 0))
            def _():
                back_hop(m, False).start()

            @pl.when(right & (pos < count - 1))
            def _():
                back_hop(m, True).start()

            if whole:
                finished(m)
            else:
                a_copy(m, size).start()

        def sent(m):
            @pl.when(jnp.logical_not(here))
            def _():
                hop(m, True).wait_send()

            @pl.when((pos <= root) & (pos > 0))
            def _():
                back_hop(m, False).wait_send()

            @pl.when((pos >= root) & (pos < count - 1))
            def _():
                back_hop(m, True).wait_send()

            if whole:
                @pl.when(here)
                def _():
                    xc_copy(m).wait_send()
            else:
                a_copy(m, size).wait_send()

                @pl.when(crosses_first(m))
                def _():
                    x_copy(m, size).wait_send()

        def crosses_first(m):
            return m >= EARLY if XFIRST else m >= 0

        def set_off(m):
            if whole:
                outer(m)
            else:
                x_copy(m, size).start()

        def set_off_early(m):
            if XFIRST:
                outer(m)
            else:
                set_off(m)

        def add_y(m):
            def joined():
                y_copy(m, size).wait_recv()
                acc[:, at(m, size), :] = add(acc[:, at(m, size), :], ry[:, y_at(m, size), :])

            if size == CH:
                pl.when(is_dec(m))(joined)
            else:
                joined()
            set_off(m)

        def add_x(m):
            @pl.when(crosses_first(m))
            def _():
                x_copy(m, size).wait_recv()
                acc[sec, at(m, size), :] = add(
                    acc[sec, at(m, size), :], land_x[0, slot(m, size), :]
                )
                outer(m)

        def last_half(m):
            a_wait(m, size)
            finished(m)

        base = 1 if whole else 2
        back = base + reach + dist + (1 if whole else 0)
        steps = [(back, jnp.logical_not(here), outward), (base + level, level > 0, inward)]
        if whole:
            steps.append((base + reach + 1, here, crossed))
        else:
            steps += [(back + 1, True, last_half), (2, True, add_x)]
        return steps, sent, add_y, set_off_early

    low_root = (count - 1) // 2
    high_root = min(low_root + 1, count - 1)
    def is_whole(m):
        return (lax.rem(m, 2) == 0) & (m >= WHOLE_LOW) & (m < WHOLE_HIGH)

    roots = (high_root, count - 1, low_root, 0)
    lines = [
        (lambda m, part=part: is_whole(m) & (lax.rem(m, 8) == part), *line_of(root, True))
        for part, root in zip((0, 2, 4, 6), roots)
    ] + [
        (lambda m: jnp.logical_not(is_whole(m)) & (m != LATE), *line_of(low_root, False)),
        (lambda m: m == LATE, *line_of(low_root, False, SMALL)),
    ]

    def finish(m):
        @pl.when((m >= EARLY) & (m != LATE))
        def _():
            core_copy(m, out.at[:, at(m), :]).wait_send()

            @pl.when(is_dec(m))
            def _():
                corey_copy(m, rcy.at[:, y_at(m), :]).wait_send()
                y_copy(m).wait_send()

        @pl.when(m == LATE)
        def _():
            core_copy(m, out.at[:, at(m, SMALL), :], SMALL).wait_send()
            corey_copy(m, rcy.at[:, y_at(m, SMALL), :], SMALL).wait_send()
            y_copy(m, SMALL).wait_send()

        for mine, _, sent, _, _ in lines:
            @pl.when(mine(m))
            def _(sent=sent):
                sent(m)

    for m in range(EARLY):
        lines[-2][-1](m)
    far_reach = max(max(root, count - 1 - root) for root in roots)
    depth = LAG * (3 + 2 * far_reach) + 1

    def tick(n):
        @pl.when(n <= PIECES[-1])
        def _():
            run_pieces(n)

        def run_line(line):
            mine, steps, _, add_y, _ = line
            m = n - LAG

            @pl.when((m >= EARLY) & (m < ALL_K))
            def _(m=m):
                @pl.when(mine(m))
                def _():
                    add_y(m)

            for offset, enabled, stage in steps:
                m = n - LAG * offset

                @pl.when((m >= 0) & (m < ALL_K) & enabled)
                def _(m=m, stage=stage):
                    @pl.when(mine(m))
                    def _():
                        stage(m)

        @pl.when((lax.rem(n, 2) == 0) & (n >= WHOLE_LOW) & (n < WHOLE_HIGH + depth))
        def _():
            for line in lines[:-2]:
                run_line(line)

        run_line(lines[-2])

        @pl.when((n >= LATE) & (n < LATE + depth))
        def _():
            run_line(lines[-1])

        @pl.when(n < ALL_K)
        def _():
            stage_c(n)

        @pl.when(n >= depth)
        def _():
            finish(n - depth)

    loop(ALL_K + depth, tick)
    loop(ALL_K, lambda m: flush(m).wait())
    for step in range(1, devices):
        dx_copy(step).wait()
    for step in range(1, LANES):
        emb_copy(step).wait()
    give_enc().wait_send()
    for k in range(D // 256):
        give_part(k, 0).wait_send()
        give_part(k, 1).wait_send()
        give_last(k).wait_send()


def backward_call(args, half, hid):
    dma = lambda *s: pltpu.SemaphoreType.DMA(s)
    vm = pltpu.VMEM
    full = ALL_K * CH
    y_half = DEC_ROWS - EARLY_ROWS + SMALL
    k = ALL_K
    rows = 2 * PAD
    cut = D // (2 * LANES)
    specs = [VM, VM] + [ANY] * 18 + [VM] * 3
    return pl.pallas_call(
        backward_and_sums,
        out_shape=[
            jax.ShapeDtypeStruct((2, full, D), BF16),
            jax.ShapeDtypeStruct((LANES, 2, CH, D), BF16),
            jax.ShapeDtypeStruct((2 * LANES, cut, VIS), BF16),
        ],
        in_specs=specs,
        out_specs=[ANY, VM, VM],
        scratch_shapes=[
            vm((rows, D), BF16), vm((D, rows), BF16),
            vm((rows, D), F32), vm((rows, D), BF16), vm((rows, D), BF16),
            vm((2, rows, hid), BF16), vm((rows, D), BF16), vm((rows, D), F32),
            vm((rows, half), BF16), vm((2, 3, rows, half), BF16),
            vm((PAD, D), F32), vm((PAD, D), BF16), vm((PAD, D), BF16), vm((PAD, D), F32),
            vm((2 * LANES, cut, VIS), BF16),
            vm((2, 1, hid), F32), vm((2, 2, half), F32), vm((8, D), F32),
            vm((2, full, D), BF16), vm((2, y_half, D), BF16), vm((2, ENC_A + ENC_B, D), BF16),
            vm((2, full, D), BF16),
            vm((2, y_half, D), BF16), vm((2, y_half, D), BF16),
            *[vm((2, full, D), BF16)] * 3,
            vm((LANES, 32, D), F32), vm((LANES, 2, SMALL, D), BF16),
            *[vm(v.shape, v.dtype) for v in args[2:19]],
            dma(17), dma(2), dma(k), dma(10), dma(10),
            dma(k), dma(k), dma(k), dma(k), dma(k), dma(k),
            dma(k), dma(k), dma(k), dma(k), dma(k),
            dma(k), dma(k), dma(k), dma(k), dma(k), dma(LANES), dma(LANES),
            dma(2 * LANES), dma(2 * LANES),
        ],
        compiler_params=pltpu.CompilerParams(
            collective_id=1, has_side_effects=True, vmem_limit_bytes=VMEM_LIMIT
        ),
    )(*args)


def finish_grads(
    total, emb, decoded, dx, decoded_out, dx_out,
    e_qkv, e_qvb, e_proj, e_up, e_upb, e_down, e_gain, e_off,
    d_qkv, d_qvb, d_proj, d_up, d_upb, d_down, d_gain, d_off, d_ew, d_ev,
):
    half = e_proj.shape[0]
    decoded_out[...] = decoded[...]
    dx_out[...] = dx[...]
    e_up[...] = total[0, A_TOP:B_TOP, :].astype(F32)
    e_down[...] = total[1, A_TOP:B_TOP, :].astype(F32)
    e_qkv[0] = total[0, B_TOP : B_TOP + half, :].astype(F32)
    e_qkv[1] = total[0, B_TOP + half : S_TOP, :].astype(F32)
    e_qkv[2] = total[1, B_TOP : B_TOP + half, :].astype(F32)
    e_proj[...] = total[1, B_TOP + half : S_TOP, :].astype(F32)

    def raw(number):
        h, top, col = tile_of(number)
        return total[h, top : top + CH, col : col + 256]

    def tile(number):
        return raw(number).astype(F32)

    for block in range(GRID // CH):
        rows = slice(block * CH, (block + 1) * CH)
        side = slice(block // 2 * 128, (block // 2 + 1) * 128)
        for k in range(2):
            d_up[rows, k * 256 : (k + 1) * 256] = tile(4 * block + k)
            if block % 2:
                both = jnp.concatenate([raw(4 * block - 2 + k), raw(4 * block + 2 + k)], 0)
                d_down[k * 256 : (k + 1) * 256, side] = jnp.transpose(both).astype(F32)
        one, two = tile(32 + 2 * block), tile(33 + 2 * block)
        d_qkv[0, rows, :] = one[:, 0:128]
        d_qkv[1, rows, :] = one[:, 128:256]
        d_qkv[2, rows, :] = two[:, 0:128]
        d_proj[block % 2 * CH : (block % 2 + 1) * CH, side] = two[:, 128:256]
    for k in range(LANES):
        for h in range(2):
            top = k * 192 + h * 64
            d_ew[top : top + 64, :] = emb[k, h, :, 0:512].astype(F32)
            d_ew[k * 192 + 128 : (k + 1) * 192, h * 256 : (h + 1) * 256] = emb[
                k, h, :, 512:768
            ].astype(F32)
    little = total[0, S_TOP : S_TOP + SMALL, :].astype(F32)
    d_gain[...] = little[0:2, 0:512]
    d_off[...] = little[2:6, 0:512]
    d_ev[...] = little[6:8, 0:512]
    d_upb[...] = little[8, 0:512]
    d_qvb[0:1, :] = little[9:10, 0:128]
    d_qvb[1:2, :] = little[9:10, 128:256]
    e_upb[...] = little[10]
    e_qvb[0:1, :] = little[11:12, 0:192]
    e_qvb[1:2, :] = little[11:12, 256:448]
    little = total[1, S_TOP : S_TOP + SMALL, :].astype(F32)
    e_gain[...] = little[0:2]
    e_off[...] = little[2:6]


def call(kernel, specs, shapes, scratch, args):
    return pl.pallas_call(
        kernel,
        out_shape=[jax.ShapeDtypeStruct(s, d) for s, d in shapes],
        in_specs=specs,
        out_specs=[VM] * len(shapes),
        scratch_shapes=scratch,
        compiler_params=pltpu.CompilerParams(vmem_limit_bytes=VMEM_LIMIT),
    )(*args)


def position_rows():
    quarter = DD // 4
    freq = np.exp(np.arange(quarter, dtype=np.float32) * np.float32(-math.log(10000.0) / quarter))
    angle = np.arange(PAD, dtype=np.float32)[:, None] * freq[None, :].astype(np.float32)
    both = np.concatenate([np.sin(angle), np.cos(angle)], 1).astype(np.float32)
    high = both.astype(jnp.bfloat16)
    low = (both - high.astype(np.float32)).astype(jnp.bfloat16)
    return np.stack([high, low])


def per_device(
    patches, cotangent, widths, visible, window_shift, batch_order,
    encoder_qkv, encoder_qvbias, encoder_proj, encoder_up, encoder_upbias, encoder_down,
    encoder_gains, encoder_offsets,
    decoder_qkv, decoder_qvbias, decoder_proj, decoder_up, decoder_upbias, decoder_down,
    decoder_gains, decoder_offsets, embed_weight, embed_vectors,
):
    qkv0 = encoder_qkv.transpose(1, 2, 0)
    half = qkv0.shape[1]
    hid = encoder_up.shape[1]
    dff = decoder_up.shape[1] * LANES
    flat = patches.transpose(1, 0, 2).reshape(-1, D)
    (
        x, x1, a, u, y, gp, qkv, p, o, qkv1, proj1, up1, down1, dec_buf,
        d_enc, d_dqvb, d_dupb, d_dsmall, out_all,
    ) = forward_call(
        (
            widths, window_shift.T, batch_order, visible, flat, encoder_gains, encoder_offsets,
            encoder_qvbias, encoder_upbias, decoder_qvbias, decoder_upbias,
            qkv0, encoder_proj, encoder_up, encoder_down,
            decoder_qkv.transpose(1, 0, 2), decoder_proj, decoder_up, decoder_down,
            cotangent, embed_weight, embed_vectors, jnp.asarray(position_rows()),
            decoder_gains, decoder_offsets,
        ),
        half, hid, dff,
    )
    total, emb, dx_all = backward_call(
        (
            d_enc, encoder_gains, u, y, gp, encoder_down, down1, encoder_up, up1,
            x, x1, a, qkv, p, o, qkv0, qkv1, encoder_proj, proj1,
            dec_buf, d_dqvb, d_dupb, d_dsmall,
        ),
        half, hid,
    )
    f = lambda *shape: (shape, F32)
    out_all, dx_all, *grads = call(
        finish_grads, [VM] * 4,
        [
            (out_all.shape, BF16), (dx_all.shape, BF16), f(3, half, D), f(2, half), f(half, D), f(D, hid), f(hid), f(hid, D), f(2, D), f(4, D),
            f(3, DD, 128), f(2, 128), f(128, DD), f(DD, 512), f(512), f(512, DD), f(2, DD), f(4, DD),
            f(D, DD), f(2, DD),
        ],
        [], (total, emb, out_all, dx_all),
    )
    grads[0] = grads[0].transpose(2, 0, 1)
    grads[8] = grads[8].transpose(1, 0, 2)
    return (out_all.swapaxes(1, 2), dx_all.swapaxes(1, 2), *grads)


def solution(mesh):
    weights = (
        P(None, None, "tensor"), P(None, "tensor"), P("tensor", None), P(None, "tensor"),
        P("tensor"), P("tensor", None), P(), P(),
    )
    split = P("dp", None, ("section", "tensor"))
    return jax.shard_map(
        per_device,
        mesh=mesh,
        in_specs=(
            P("dp", None, None), P("dp", None, None), P("dp"), P("dp", None), P("dp", None),
            P("dp", None),
        ) + weights + weights + (P(), P()),
        out_specs=(split, split) + weights + weights + (P(), P()),
        check_vma=False,
    )
```

```python
import math

import jax
import jax.numpy as jnp
import numpy as np
from jax import lax
from jax.experimental import pallas as pl
from jax.experimental.pallas import tpu as pltpu
from jax.sharding import PartitionSpec as P

D = 768
HEADS = 12
DD = 512
DHEADS = 16
GRID_ROWS = 64
WIDE = 8
WIN = 4
VIS = 102
CM = 4
GRID = 512
LANES = 4
PAD = 128
EPS = 1e-06
NEG = -10000.0
F32 = jnp.float32
BF16 = jnp.bfloat16
VMEM_LIMIT = 60 * 1024 * 1024

VM = pl.BlockSpec(memory_space=pltpu.VMEM)
SM = pl.BlockSpec(memory_space=pltpu.SMEM)
ANY = pl.BlockSpec(memory_space=pl.ANY)


def nn(a, b):
    return lax.dot_general(a, b, (((1,), (0,)), ((), ())), preferred_element_type=F32)


def nt(a, b):
    return lax.dot_general(a, b, (((1,), (1,)), ((), ())), preferred_element_type=F32)


def tn(a, b):
    return lax.dot_general(a, b, (((0,), (0,)), ((), ())), preferred_element_type=F32)


def loop(count, body, unroll=1):
    def step(i, carry):
        body(i)
        return carry

    lax.fori_loop(0, count, step, 0, unroll=unroll)


def span(i, size):
    return pl.ds(pl.multiple_of(i * size, size), size)


def normal(x):
    center = x - jnp.mean(x, -1, keepdims=True)
    scale = lax.rsqrt(jnp.mean(center * center, -1, keepdims=True) + EPS)
    return center * scale, scale


def normal_back(dy, hat, scale, gain):
    d = dy * gain
    return scale * (
        d - jnp.mean(d, -1, keepdims=True) - hat * jnp.mean(d * hat, -1, keepdims=True)
    )


def gelu_both(h):
    phi = 0.5 * lax.erf(h * math.sqrt(0.5)) + 0.5
    bell = jnp.exp2(h * h * (-0.5 * math.log2(math.e)))
    return h * phi, phi + h * bell * (1.0 / math.sqrt(2.0 * math.pi))


def colsum(x):
    return jnp.sum(x, 0, keepdims=True)


def head_marks(width, size, dtype):
    lane = lax.broadcasted_iota(jnp.int32, (1, width), 1)
    return [((lane >= h * size) & (lane < (h + 1) * size)).astype(dtype) for h in range(width // size)]


def stacked(x, marks):
    return jnp.concatenate([x * m for m in marks], 0)


LOG2E = math.log2(math.e)


def attend(q, k, v, marks, ones, masked, scale):
    keys = k.shape[0]
    s = nt(q, stacked(k, marks))
    parts = []
    for h in range(len(marks)):
        x = masked(s[:, h * keys : (h + 1) * keys] * (scale * LOG2E))
        parts.append(jnp.exp2(x - jnp.max(x, -1, keepdims=True)).astype(BF16))
    e = jnp.concatenate(parts, 1)
    width = q.shape[1]
    if width % 128:
        top, total = nn(e, stacked(v, marks)), nn(e, ones)
    else:
        both = nn(e, jnp.concatenate([stacked(v, marks), ones], 1))
        top, total = both[:, :width], both[:, width:]
    inverse = 1.0 / total
    return e, (top * inverse).astype(BF16), inverse


def attend_back(q, k, v, e, o, inverse, d_out, marks, marks32, rows32, ones, scale):
    keys = k.shape[0]
    width = q.shape[1]
    d_one = d_out.astype(F32) * inverse
    d_two = (d_one * o.astype(F32)).astype(BF16)
    d_one = d_one.astype(BF16)
    if width % 128:
        d_s = nt(d_one, stacked(v, marks)) - nt(d_two, ones)
    else:
        d_s = nt(
            jnp.concatenate([d_one, d_two], 1), jnp.concatenate([stacked(v, marks), -ones], 1)
        )
    dr = (e.astype(F32) * d_s * scale).astype(BF16)
    d_q = nn(dr, stacked(k, marks)).astype(BF16)
    if width % 128:
        d_k_all, d_v_all = tn(dr, q), tn(e, d_one)
        d_k = d_v = 0.0
        for h in range(len(marks)):
            cut = slice(h * keys, (h + 1) * keys)
            d_k += d_k_all[cut] * marks32[h]
            d_v += d_v_all[cut] * marks32[h]
        return d_q, d_k.astype(BF16), d_v.astype(BF16)
    d_k_all = nn(jnp.transpose(q), dr)
    d_v_all = nn(jnp.transpose(d_one), e)
    d_k = d_v = 0.0
    for h in range(len(marks)):
        cut = slice(h * keys, (h + 1) * keys)
        d_k += d_k_all[:, cut] * rows32[h]
        d_v += d_v_all[:, cut] * rows32[h]
    return d_q, jnp.transpose(d_k.astype(BF16)), jnp.transpose(d_v.astype(BF16))


def ones_per_head(keys, marks):
    return jnp.concatenate([jnp.broadcast_to(m, (keys, m.shape[1])) for m in marks], 0)


ENC_SIZE = D // HEADS
ENC_SCALE = ENC_SIZE ** -0.5
DEC_SIZE = DD // DHEADS
DEC_SCALE = DEC_SIZE ** -0.5


CH = 64
DEC_ROWS = 576
ENC_A = 768
ENC_B = 384
DEC_K = DEC_ROWS // CH
B_K = (DEC_ROWS + ENC_A + ENC_B) // CH
ALL_K = B_K + 1
A_TOP = DEC_ROWS
B_TOP = DEC_ROWS + ENC_A
S_TOP = B_TOP + ENC_B
EARLY = 4
XFIRST = True
EARLY_ROWS = EARLY * CH
LAG = 2
ORDER = (0, 1, 2, 3, 9, 10, 11, 12, 13, 14, 4, 15, 16, 17, 18, 5, 6, 19, 21, 20, 8, 22, 23, 24, 25, 27, 26, 7)
PIECES = (0, 2, 2, 2, 2, 2, 2, 2, 3, 3, 3, 10, 12, 12, 13, 13, 14, 14, 15, 15, 15, 16, 20)
LATE = ORDER.index(B_K)
WHOLE_LOW = 6
WHOLE_HIGH = 22
SMALL = 16


def tile_of(number):
    place = number // 3
    return place % 2, place // 2 * CH, number % 3 * 256


MESH = pl.DeviceIdType.MESH


def far(src, dst, send, recv, peer):
    return pltpu.make_async_remote_copy(
        src_ref=src, dst_ref=dst, send_sem=send, recv_sem=recv, device_id=peer, device_id_type=MESH
    )


def forward_and_decoder(
    wid, shifts, order, vis, pat, gains, offs, b_qv, b_up, b_dqv, b_dup,
    h_qkv, h_proj, h_up, h_down, h_dqkv, h_dproj, h_dup, h_ddown,
    cot_hbm, ew, evec, table, dgains, doffs,
    o_x, o_x1, o_a, o_u, o_y, o_gp, o_qkv, o_p, o_o, o_w, o_wproj, o_wup, o_wdown, o_dec,
    d_enc, d_qvb, d_upb, d_small, dec_out,
    w_qkv, w_proj, w_up, w_down, bias, biases, qkv, proj, up, down,
    ex, ea, eu, ey, egp, eqkv, ep, eo, ex1, epart, esend, erecv, esend2, erecv2, eown,
    cot, x0, x1, a, acts, probs, o, inverse, u, ut, y, gp, g32, gb, gt, acc, e_ref, hot, perm, buf, dsend, e_rc, e_rcy, e_rx, e_ry,
    load_s, out_s, cot_s, w_s, w_r, bias_s, bias_r, dw_s, dw_r, ex_s, ex_r, ex2_s, ex2_r, do_s, do_r, e_s, e_r,
):
    sec = lax.axis_index("section")
    lane = lax.axis_index("tensor")
    mate = lane + 1 - 2 * lax.rem(lane, 2)
    over = lax.rem(lane + 2, LANES)
    cross = lax.rem(mate + 2, LANES)
    me = sec * LANES + lane
    devices = 2 * LANES
    clip = me
    clips = (me, sec * LANES + over)

    def group_peer(step):
        peer = lax.rem(me + step, devices)
        return peer, {"section": lax.div(peer, LANES), "tensor": lax.rem(peer, LANES)}

    own = [
        pltpu.make_async_copy(src, dst.at[0], load_s.at[n])
        for n, (src, dst) in enumerate(
            ((h_qkv, w_qkv), (h_proj, w_proj), (h_up, w_up), (h_down, w_down))
        )
    ]

    def place(n, shard, part=None):
        thick = (128, 128, 512, 512)[n]
        base = shard * thick
        cut = pl.ds(pl.multiple_of(base, thick), thick)
        if part is None:
            return (qkv.at[:, :, cut], proj.at[cut, :], up.at[:, cut], down.at[cut, :])[n]
        some = span(part, (256, 64, 256, 256)[n])
        if n == 0:
            return qkv.at[:, some, cut]
        if n == 2:
            return up.at[some, cut]
        few = thick // 2
        rows = pl.ds(pl.multiple_of(base + part * few, few), few)
        return (proj if n == 1 else down).at[rows, :]

    shards = (h_dqkv, h_dproj, h_dup, h_ddown)
    keep = [
        pltpu.make_async_copy(shards[n], place(n, lane), load_s.at[4 + n]) for n in range(4)
    ]
    for copy in own + keep:
        copy.start()
    fetch = pltpu.make_async_copy(cot_hbm.at[clip], cot, cot_s)
    fetch.start()

    barrier = pltpu.get_barrier_semaphore()
    for step in range(1, devices):
        pl.semaphore_signal(barrier, inc=1, device_id_type=MESH, device_id=group_peer(step)[1])
    bias[...] = jnp.zeros_like(bias)
    half = w_proj.shape[1]
    bias[0:1, :] = b_up[...].astype(F32).reshape(1, -1)
    bias[1:3, 0:half] = b_qv[...].astype(F32)
    bias[3:4, 0:512] = b_dup[...].astype(F32).reshape(1, -1)
    bias[4:6, 0:128] = b_dqv[...].astype(F32)
    biases[lane] = bias[...]
    stride = pat.shape[0] // VIS
    for c in range(2):
        row = lax.broadcasted_iota(jnp.int32, (PAD, pat.shape[0]), 0)
        col = lax.broadcasted_iota(jnp.int32, (PAD, pat.shape[0]), 1)
        pick = (col == row * stride + clips[c]).astype(F32).astype(BF16)
        ex[c * PAD : (c + 1) * PAD, :] = nn(pick, pat[...])

    pl.semaphore_wait(barrier, devices - 1)

    def enc_weight(n):
        src = (h_qkv, h_proj, h_up, h_down)[n]
        dst = (w_qkv, w_proj, w_up, w_down)[n]
        return far(src, dst.at[1], w_s.at[n], w_r.at[n], {"tensor": mate})

    def bias_copy(step):
        return far(
            bias, biases.at[lane], bias_s.at[step], bias_r.at[step],
            {"tensor": lax.rem(lane + step, LANES)},
        )

    def half_of(n):
        some = span(sec, (256, 64, 256, 256)[n])
        return shards[n].at[:, some, :] if n == 0 else shards[n].at[some, :]

    def dec_weight(n, kind):
        peer = {"section": 1 - sec} if kind == 2 else {"tensor": over if kind == 0 else mate}
        if kind == 0:
            src, dst = half_of(n), place(n, lane, sec)
        elif kind == 1:
            src, dst = shards[n], place(n, lane)
        else:
            src = dst = place(n, over, 1 - sec if kind == 4 else sec)
        return far(src, dst, dw_s.at[5 * n + kind], dw_r.at[5 * n + kind], peer)

    enc_weight(0).start()
    for step in range(1, LANES):
        bias_copy(step).start()
    enc_weight(1).start()
    dec_weight(0, 0).start()
    enc_weight(2).start()
    enc_weight(3).start()
    for n in range(4):
        dec_weight(n, 1).start()

    def pass_on(n):
        dec_weight(n, 0).wait_recv()
        dec_weight(n, 2).start()
        dec_weight(n, 3).start()

    def pass_last(n):
        dec_weight(n, 2).wait_recv()
        dec_weight(n, 4).start()

    def arrived(n):
        keep[n].wait()
        dec_weight(n, 1).wait_recv()
        dec_weight(n, 3).wait_recv()
        dec_weight(n, 4).wait_recv()

    width = wid[clip]
    bits = jnp.where(width == WIDE, 3, 2)
    turn = shifts[0, clip] * width
    mod = GRID - 1
    spot = 0
    for i in range(order.shape[1]):
        spot = spot + jnp.where(order[0, i] == clip, i, 0)
    batch = spot // CM
    count = 0
    for i in range(order.shape[1]):
        count = count + jnp.where(batch == i // CM, wid[order[0, i]], 0)
    factor_rows = CM * GRID / (jnp.full((1, 1), count, jnp.int32) * GRID_ROWS).astype(F32)

    def slot_of(index):
        return (index - turn) & mod

    def code_of(slot):
        band = ((slot >> bits) + shifts[0, clip]) >> 2
        strip = ((slot & (width - 1)) + shifts[1, clip]) >> 2
        return band * 4 + strip

    def valid_rows():
        slot = slot_of(lax.broadcasted_iota(jnp.int32, (GRID, 1), 0))
        return (slot < GRID_ROWS * width).astype(F32)

    def clip_gradient():
        fetch.wait()
        rolled = slot_of(lax.broadcasted_iota(jnp.int32, (GRID, GRID), 0))
        column = lax.broadcasted_iota(jnp.int32, (GRID, GRID), 1)
        perm[...] = (rolled == column).astype(F32).astype(BF16)
        g = nn(perm[...], cot[...]) * valid_rows() * factor_rows
        g32[...] = g
        gb[...] = g.astype(BF16)
        gt[...] = jnp.transpose(g.astype(BF16))
        d_small[...] = jnp.zeros_like(d_small)
        d_small[5:6, :] = colsum(g)

    seen = vis[pl.ds(clip, 1), :]
    target = jnp.concatenate([(seen + turn) & mod, jnp.full((1, PAD - VIS), -1, jnp.int32)], 1)

    def places(i):
        r = span(i, PAD)
        index = lax.broadcasted_iota(jnp.int32, (PAD, PAD), 0) + i * PAD
        column = lax.broadcasted_iota(jnp.int32, (PAD, PAD), 1)
        hot[r, :] = (index == target).astype(F32).astype(BF16)
        slot = slot_of(index)
        by_row = ((slot >> bits) == column).astype(F32).astype(BF16)
        by_col = ((slot & (width - 1)) == column).astype(F32).astype(BF16)
        row_part = nn(by_row, table[0]) + nn(by_row, table[1])
        col_part = nn(by_col, table[0]) + nn(by_col, table[1])
        x0[r, :] = jnp.concatenate([row_part, col_part], 1)

    egain = gains[...].astype(F32)
    eoff = offs[...].astype(F32)
    emarks = head_marks(half, ENC_SIZE, BF16)
    key = lax.broadcasted_iota(jnp.int32, (PAD, PAD), 1)
    floor = jnp.where(key < VIS, NEG * LOG2E, -1e30)
    eones = ones_per_head(PAD, emarks)
    blocks = D // 256

    def give_part(i, side):
        cut = span(i, 256)
        return far(
            esend.at[(1 - side) * PAD : (2 - side) * PAD, cut],
            erecv.at[side * PAD : (side + 1) * PAD, cut],
            ex_s.at[2 * i + side], ex_r.at[2 * i + side], {"tensor": over},
        )

    for c in range(2):
        rows = slice(c * PAD, (c + 1) * PAD)
        hat, _ = normal(ex[rows, :])
        ea[rows, :] = (hat * egain[0:1] + eoff[0:1]).astype(BF16)
        limit = (VIS * wid[clips[c]]) // WIDE
        for g, shard in enumerate((lane, mate)):
            if c == 0 and g == 0:
                own[0].wait()
            if c == 0 and g == 1:
                enc_weight(0).wait_recv()
                for step in range(1, LANES):
                    bias_copy(step).wait_recv()
            if g == 0:
                bq, bv = bias[1:2, 0:half], bias[2:3, 0:half]
            else:
                bq, bv = biases[shard, 1:2, 0:half], biases[shard, 2:3, 0:half]
            eqkv[g, 0, rows] = (nt(ea[rows, :], w_qkv[g, 0]) + bq).astype(BF16)
            eqkv[g, 1, rows] = nt(ea[rows, :], w_qkv[g, 1]).astype(BF16)
            eqkv[g, 2, rows] = (nt(ea[rows, :], w_qkv[g, 2]) + bv).astype(BF16)
            p, out, _ = attend(
                eqkv[g, 0, rows], eqkv[g, 1, rows], eqkv[g, 2, rows], emarks, eones,
                lambda s: jnp.where(key < limit, s, floor), ENC_SCALE,
            )
            ep[g, c] = p
            eo[g, rows] = out
        if c == 0:
            own[1].wait()
            enc_weight(1).wait_recv()
        for i in range(blocks):
            cut = slice(i * 256, (i + 1) * 256)
            t = nn(eo[0, rows], w_proj[0, :, cut]) + nn(eo[1, rows], w_proj[1, :, cut])
            epart[rows, cut] = t
            esend[rows, cut] = t.astype(BF16)
            give_part(i, 1 - c).start()
    pass_on(0)
    clip_gradient()
    own[2].wait()
    enc_weight(2).wait_recv()

    def give_last(i):
        cut = span(i, 256)
        return far(
            esend2.at[:, cut], erecv2.at[:, cut], ex2_s.at[i], ex2_r.at[i], {"tensor": over}
        )

    for c in (1, 0):
        rows = slice(c * PAD, (c + 1) * PAD)
        for i in range(blocks):
            give_part(i, c).wait_recv()
        t = ex[rows, :] + epart[rows, :] + erecv[rows, :].astype(F32) + eoff[2:3]
        ex1[rows, :] = t
        hat, _ = normal(t)
        eu[rows, :] = (hat * egain[1:2] + eoff[1:2]).astype(BF16)
        for g, shard in enumerate((lane, mate)):

            def enc_ff(i, g=g, shard=shard, rows=rows):
                cut = span(i, 256)
                h = nn(eu[rows, :], w_up[g, :, cut]) + biases[shard, 0:1, cut]
                act, slope = gelu_both(h)
                ey[g, rows, cut] = act.astype(BF16)
                egp[g, rows, cut] = slope.astype(BF16)

            loop(w_up.shape[2] // 256, enc_ff, unroll=3)
        if c == 1:
            own[3].wait()
            enc_weight(3).wait_recv()
        for i in range(blocks):
            cut = slice(i * 256, (i + 1) * 256)
            t = nn(ey[0, rows], w_down[0, :, cut]) + nn(ey[1, rows], w_down[1, :, cut])
            if c == 0:
                eown[:, cut] = t
            else:
                esend2[:, cut] = t.astype(BF16)
                give_last(i).start()
        if c == 1:
            for n in (1, 2, 3):
                dec_weight(n, 0).start()
            pass_last(0)
    outs = [
        pltpu.make_async_copy(src, dst, out_s.at[n])
        for n, (src, dst) in enumerate(
            (
                (ex.at[0:PAD, :], o_x), (ex1, o_x1), (ea, o_a), (eu, o_u), (ey, o_y), (egp, o_gp),
                (eqkv, o_qkv), (ep, o_p), (eo, o_o), (w_qkv.at[1], o_w), (w_proj.at[1], o_wproj),
                (w_up.at[1], o_wup), (w_down.at[1], o_wdown),
            )
        )
    ]
    for copy in outs:
        copy.start()
    loop(GRID // PAD, places, unroll=2)
    for i in range(blocks):
        give_last(i).wait_recv()

    e_ref[...] = (ex1[0:PAD, :] + eown[...] + erecv2[...].astype(F32) + eoff[3:4]).astype(BF16)
    vec = evec[...].astype(F32)
    m = (nn(e_ref[...], ew[...]) + vec[0:1]).astype(BF16)
    gain = dgains[...].astype(F32)
    offsets = doffs[...].astype(F32)

    def start(i):
        r = span(i, PAD)
        oh = hot[r, :]
        hit = jnp.sum(oh.astype(F32), -1, keepdims=True)
        x = jnp.where(hit > 0, nn(oh, m), vec[1:2]).astype(BF16).astype(F32) + x0[r, :]
        x0[r, :] = x
        hat, _ = normal(x)
        a[r, :] = (hat * gain[0:1] + offsets[0:1]).astype(BF16)

    loop(GRID // PAD, start, unroll=2)
    arrived(0)

    def dec_bias(row, size):
        return jnp.concatenate([biases[k, row : row + 1, 0:size] for k in range(LANES)], 1)

    acts[0] = (nn(a[...], qkv[0]) + dec_bias(4, 128)).astype(BF16)
    acts[1] = nn(a[...], qkv[1]).astype(BF16)
    acts[2] = (nn(a[...], qkv[2]) + dec_bias(5, 128)).astype(BF16)
    pass_on(1)
    pass_on(2)
    marks = head_marks(128, DEC_SIZE, BF16)
    marks32 = head_marks(128, DEC_SIZE, F32)
    dim = lax.broadcasted_iota(jnp.int32, (128, 1), 0)
    rows32 = [
        ((dim >= h * DEC_SIZE) & (dim < (h + 1) * DEC_SIZE)).astype(F32) for h in range(len(marks))
    ]

    ones = ones_per_head(PAD, marks)

    def attention(i):
        r = span(i, PAD)
        row_slot = slot_of(lax.broadcasted_iota(jnp.int32, (PAD, PAD), 0) + i * PAD)
        key_slot = slot_of(lax.broadcasted_iota(jnp.int32, (PAD, PAD), 1) + i * PAD)
        allowed = (code_of(row_slot) == code_of(key_slot)) & (key_slot < GRID_ROWS * width)
        for g in range(DD // 128):
            c = slice(g * 128, (g + 1) * 128)
            probs[i, :, g * 512 : (g + 1) * 512], o[r, c], inverse[r, c] = attend(
                acts[0, r, c], acts[1, r, c], acts[2, r, c], marks, ones,
                lambda s: jnp.where(allowed, s, NEG * LOG2E), DEC_SCALE,
            )

    loop(GRID // PAD, attention, unroll=4)
    pass_last(1)
    pass_last(2)
    pass_on(3)
    arrived(1)

    def mix(i):
        r = span(i, 256)
        x = x0[r, :] + nn(o[r, :], proj[...]) + offsets[2:3]
        x1[r, :] = x
        hat, _ = normal(x)
        un = hat * gain[1:2] + offsets[1:2]
        u[r, :] = un.astype(BF16)
        ut[:, r] = jnp.transpose(un.astype(BF16))

    loop(2, mix)
    pass_last(3)
    arrived(2)

    def ff(i):
        c = span(i, 256)
        h = nn(u[...], up[:, c]) + biases[lax.div(i, 2), 3:4, span(lax.rem(i, 2), 256)]
        act, slope = gelu_both(h)
        y[:, c] = act.astype(BF16)
        gp[:, c] = slope.astype(BF16)

    loop(up.shape[1] // 256, ff, unroll=4)
    arrived(3)
    def out(i):
        c = span(i, 256)
        acc[:, c] = nn(y[...], down[:, c])

    loop(2, out)
    full = ((acc[...] + x1[...] + offsets[3:4]) * valid_rows()).astype(BF16)
    turned = tn(full, perm[...]).astype(BF16)
    for k in range(devices):
        dsend[k] = turned[k * dsend.shape[1] : (k + 1) * dsend.shape[1]]

    def decoded_copy(step):
        peer, spot = group_peer(step)
        return far(dsend.at[peer], dec_out.at[me], do_s.at[step], do_r.at[step], spot)

    for step in range(1, devices):
        decoded_copy(step).start()
    dec_out[me] = dsend[me]

    def ff_back(shard):
        for side in range(2):
            c = span(2 * shard + side, 256)
            d_down = nn(gt[...], y[:, c]).astype(BF16)
            dh = nt(gb[...], down[c, :]) * gp[:, c].astype(F32)
            d_upb[:, c] = colsum(dh)
            du = dh.astype(BF16)
            gp[:, c] = du
            d_up = nn(ut[...], du).astype(BF16)
            for block in range(GRID // CH):
                rows = slice(block * CH, (block + 1) * CH)
                h, top, col = tile_of(4 * block + side)
                buf[shard, h, top : top + CH, col : col + 256] = d_up[rows]
                h, top, col = tile_of(4 * block + 2 + side)
                buf[shard, h, top : top + CH, col : col + 256] = d_down[rows]

    def early_core(which):
        shard, land = ((mate, e_rc), (cross, e_rcy))[which]
        return far(
            buf.at[shard, :, 0:EARLY_ROWS, :], land, e_s.at[which], e_r.at[which], {"tensor": mate}
        )

    def early_x(which):
        return far(
            buf.at[(over, lane)[which], 1 - sec, 0:EARLY_ROWS, :], e_rx.at[which],
            e_s.at[2 + which], e_r.at[2 + which], {"section": 1 - sec},
        )

    def early_y():
        return far(
            buf.at[over, sec, 0:EARLY_ROWS, :], e_ry, e_s.at[4], e_r.at[4], {"tensor": over}
        )

    def early_add(shard, land):
        def body(i):
            r = span(i, CH)
            buf[shard, :, r, :] = buf[shard, :, r, :] + land[:, r, :]

        loop(EARLY_ROWS // CH, body)

    def early_half(shard, land):
        buf[shard, sec, 0:EARLY_ROWS, :] = buf[shard, sec, 0:EARLY_ROWS, :] + land

    def ff_step(i):
        ff_back(jnp.where(i == 0, cross, jnp.where(i == 1, over, jnp.where(i == 2, mate, lane))))

        @pl.when(i == 1)
        def _():
            early_core(1).start()

        @pl.when(i == 2)
        def _():
            early_core(0).start()

    loop(LANES, ff_step)
    early_core(1).wait_recv()
    early_add(over, e_rcy)
    early_x(0).start()

    def ff_in(i):
        c = span(i, 256)
        acc[:, c] = nt(gp[...], up[c, :])

    loop(2, ff_in)
    early_core(0).wait_recv()
    early_add(lane, e_rc)
    early_x(1).start()

    def mix_back(i):
        r = span(i, 256)
        hat, scale = normal(x1[r, :])
        da = acc[r, :]
        dx = g32[r, :] + normal_back(da, hat, scale, gain[1:2])
        d_small[1:2, :] += colsum(da * hat)
        d_small[3:4, :] += colsum(da)
        d_small[4:5, :] += colsum(dx)
        g32[r, :] = dx
        dxb = dx.astype(BF16)
        gb[r, :] = dxb
        u[r, :] = nt(dxb, proj[...]).astype(BF16)

    loop(2, mix_back)
    d_proj = tn(o[...], gb[...]).astype(BF16)
    for block in range(GRID // CH):
        h, top, col = tile_of(33 + 2 * block)
        side = slice(block // 2 * 128, (block // 2 + 1) * 128)
        for k in range(LANES):
            row = k * 128 + block % 2 * CH
            buf[k, h, top : top + CH, col + 128 : col + 256] = d_proj[row : row + CH, side]

    def attention_back(i):
        r = span(i, PAD)
        for k in range(DD // 128):
            c = slice(k * 128, (k + 1) * 128)
            acts[0, r, c], acts[1, r, c], acts[2, r, c] = attend_back(
                acts[0, r, c], acts[1, r, c], acts[2, r, c],
                probs[i, :, k * 512 : (k + 1) * 512], o[r, c], inverse[r, c], u[r, c],
                marks, marks32, rows32, ones, DEC_SCALE,
            )

    loop(GRID // PAD, attention_back, unroll=4)
    early_x(0).wait_recv()
    early_half(over, e_rx[0])
    early_y().start()
    d_qvb[0:1, :] = colsum(acts[0].astype(F32))
    d_qvb[1:2, :] = colsum(acts[2].astype(F32))

    def project_back(i):
        c = span(i, 256)
        acc[:, c] = (
            nt(acts[0], qkv[0, c, :]) + nt(acts[1], qkv[1, c, :]) + nt(acts[2], qkv[2, c, :])
        )

    loop(2, project_back)
    gt[...] = jnp.transpose(a[...])
    for j in range(3):
        d_qkv = nn(gt[...], acts[j]).astype(BF16)
        for block in range(GRID // CH):
            h, top, col = tile_of(32 + 2 * block + j // 2)
            col = col + j % 2 * 128
            rows = slice(block * CH, (block + 1) * CH)
            for k in range(LANES):
                buf[k, h, top : top + CH, col : col + 128] = d_qkv[rows, k * 128 : (k + 1) * 128]

    def start_back(i):
        r = span(i, PAD)
        hat, scale = normal(x0[r, :])
        da = acc[r, :]
        dx = g32[r, :] + normal_back(da, hat, scale, gain[0:1])
        d_small[0:1, :] += colsum(da * hat)
        d_small[2:3, :] += colsum(da)
        dg = dx.astype(BF16)
        gb[r, :] = dg
        hit = jnp.sum(hot[r, :].astype(F32), -1, keepdims=True)
        d_small[7:8, :] += colsum(jnp.where(hit > 0, 0.0, dg.astype(F32)))

    loop(GRID // PAD, start_back, unroll=2)
    dm = tn(hot[...], gb[...])
    d_small[6:7, :] = colsum(dm)
    dmb = dm.astype(BF16)
    d_enc[...] = nt(dmb, ew[...]).astype(BF16)
    d_ew = tn(e_ref[...], dmb).astype(BF16)
    for k in range(LANES):
        for h in range(2):
            top = k * 192 + h * 64
            buf[k, h, 512:576, 0:512] = d_ew[top : top + 64]
            buf[k, h, 512:576, 512:768] = d_ew[k * 192 + 128 : (k + 1) * 192, h * 256 : (h + 1) * 256]

    early_x(1).wait_recv()
    early_half(lane, e_rx[1])
    early_y().wait_recv()
    early_half(lane, e_ry[...])
    later = pl.ds(EARLY_ROWS, DEC_ROWS - EARLY_ROWS)
    rest = [pltpu.make_async_copy(buf.at[lane], o_dec.at[lane], out_s.at[13])] + [
        pltpu.make_async_copy(buf.at[k, :, later, :], o_dec.at[k, :, later, :], out_s.at[14 + n])
        for n, k in enumerate((mate, over, cross))
    ]
    for copy in rest:
        copy.start()
    for copy in outs + rest:
        copy.wait()
    for which in range(2):
        early_core(which).wait_send()
        early_x(which).wait_send()
    early_y().wait_send()
    for n in range(4):
        enc_weight(n).wait_send()
        for kind in range(5):
            dec_weight(n, kind).wait_send()
    for step in range(1, LANES):
        bias_copy(step).wait_send()
    for i in range(blocks):
        give_part(i, 0).wait_send()
        give_part(i, 1).wait_send()
        give_last(i).wait_send()
    for step in range(1, devices):
        decoded_copy(step).wait()


def forward_call(args, half, hid, dff):
    dma = lambda *s: pltpu.SemaphoreType.DMA(s)
    vm = lambda dtype, *shape: pltpu.VMEM(shape, dtype)
    rows = 2 * PAD
    keys = PAD * half // ENC_SIZE
    devices = 2 * LANES
    slab = DD // devices
    kept = [
        ((PAD, D), F32), ((rows, D), F32), ((rows, D), BF16), ((rows, D), BF16),
        ((2, rows, hid), BF16), ((2, rows, hid), BF16), ((2, 3, rows, half), BF16),
        ((2, 2, PAD, keys), BF16), ((2, rows, half), BF16),
        ((3, half, D), BF16), ((half, D), BF16), ((D, hid), BF16), ((hid, D), BF16),
        ((LANES, 2, DEC_ROWS, D), BF16),
    ]
    made = [
        ((PAD, D), BF16), ((2, DD), F32), ((1, dff), F32), ((8, DD), F32),
        ((devices, slab, GRID), BF16),
    ]
    return pl.pallas_call(
        forward_and_decoder,
        out_shape=[jax.ShapeDtypeStruct(s, d) for s, d in kept + made],
        in_specs=[SM, SM, SM] + [VM] * 8 + [ANY] * 9 + [VM] * 5,
        out_specs=[ANY] * len(kept) + [VM] * len(made),
        scratch_shapes=[
            vm(BF16, 2, 3, half, D), vm(BF16, 2, half, D), vm(BF16, 2, D, hid), vm(BF16, 2, hid, D),
            vm(F32, 8, D), vm(F32, LANES, 8, D),
            vm(BF16, 3, DD, DD), vm(BF16, DD, DD), vm(BF16, DD, dff), vm(BF16, dff, DD),
            vm(F32, rows, D), vm(BF16, rows, D), vm(BF16, rows, D), vm(BF16, 2, rows, hid),
            vm(BF16, 2, rows, hid), vm(BF16, 2, 3, rows, half), vm(BF16, 2, 2, PAD, keys),
            vm(BF16, 2, rows, half), vm(F32, rows, D), vm(F32, rows, D), vm(BF16, rows, D),
            vm(BF16, rows, D), vm(BF16, PAD, D), vm(BF16, PAD, D), vm(F32, PAD, D),
            vm(BF16, GRID, DD), vm(F32, GRID, DD), vm(F32, GRID, DD), vm(BF16, GRID, DD),
            vm(BF16, 3, GRID, DD), vm(BF16, GRID // PAD, PAD, DHEADS * PAD), vm(BF16, GRID, DD),
            vm(F32, GRID, DD),
            vm(BF16, GRID, DD), vm(BF16, DD, GRID), vm(BF16, GRID, dff), vm(BF16, GRID, dff),
            vm(F32, GRID, DD), vm(BF16, GRID, DD), vm(BF16, DD, GRID), vm(F32, GRID, DD),
            vm(BF16, PAD, D), vm(BF16, GRID, PAD), vm(BF16, GRID, GRID),
            vm(BF16, LANES, 2, DEC_ROWS, D),
            vm(BF16, devices, slab, GRID), *[vm(BF16, 2, EARLY_ROWS, D)] * 3, vm(BF16, EARLY_ROWS, D),
            dma(8), dma(17), pltpu.SemaphoreType.DMA, dma(4), dma(4), dma(LANES), dma(LANES),
            dma(20), dma(20), dma(6), dma(6), dma(3), dma(3), dma(devices), dma(devices),
            dma(5), dma(5),
        ],
        compiler_params=pltpu.CompilerParams(
            collective_id=0, has_side_effects=True, vmem_limit_bytes=VMEM_LIMIT
        ),
    )(*args)


def add(x, y):
    return x + y


def backward_and_sums(
    d_enc, gains,
    h_u, h_y, h_gp, h_down0, h_down1, h_up0, h_up1,
    h_x, h_x1, h_a, h_qkv, h_p, h_o, h_w0, h_w1, h_proj0, h_proj1,
    dec, dec_qvb, dec_upb, dec_small,
    total, emb, dx_out,
    gb, ut, part, send, recv, du, gx, dx1, d_o, d_acts, own, send1, recv1, dx32, dx,
    d_upb, d_qvb, d_small,
    acc, yacc, enc_mate, out, rcy, ry, land_x, land_l, land_r, small32, small,
    u, y, gp, down0, down1, up0, up1, x, x1, a, qkv, p, o, w0, w1, proj0, proj1, fetch_s,
    load_s, flush_s, ex_s, ex_r,
    core_s, core_r, corey_s, corey_r, y_s, y_r, x_s, x_r, z_s, zl_r, zr_r,
    bl_s, br_s, b_r, a_s, a_r, emb_s, emb_r, dx_s, dx_r,
):
    sec = lax.axis_index("section")
    lane = lax.axis_index("tensor")
    pos = lax.axis_index("dp")
    count = lax.axis_size("dp")
    mate = lane + 1 - 2 * lax.rem(lane, 2)
    over = lax.rem(lane + 2, LANES)
    cross = lax.rem(mate + 2, LANES)
    first = pos == 0
    last = pos == count - 1
    me = sec * LANES + lane
    devices = 2 * LANES

    def group_peer(step):
        peer = lax.rem(me + step, devices)
        return peer, {"section": lax.div(peer, LANES), "tensor": lax.rem(peer, LANES)}

    barrier = pltpu.get_barrier_semaphore()
    for step in range(1, devices):
        pl.semaphore_signal(barrier, inc=1, device_id_type=MESH, device_id=group_peer(step)[1])

    @pl.when(pos > 0)
    def _():
        pl.semaphore_signal(barrier, inc=1, device_id={"dp": pos - 1}, device_id_type=MESH)

    @pl.when(pos < count - 1)
    def _():
        pl.semaphore_signal(barrier, inc=1, device_id={"dp": pos + 1}, device_id_type=MESH)

    loads = [
        pltpu.make_async_copy(dec.at[lane], acc.at[:, 0:DEC_ROWS, :], load_s.at[0]),
        pltpu.make_async_copy(
            dec.at[over, :, EARLY_ROWS:DEC_ROWS, :], yacc.at[:, 0 : DEC_ROWS - EARLY_ROWS, :],
            load_s.at[1],
        ),
    ]
    for load in loads:
        load.start()
    fetches = [
        pltpu.make_async_copy(src, dst, fetch_s.at[n])
        for n, (src, dst) in enumerate(
            (
                (h_u, u), (h_y, y), (h_gp, gp), (h_down0, down0), (h_down1, down1), (h_up0, up0),
                (h_up1, up1), (h_x, x), (h_x1, x1), (h_a, a), (h_qkv, qkv), (h_p, p), (h_o, o),
                (h_w0, w0), (h_w1, w1), (h_proj0, proj0), (h_proj1, proj1),
            )
        )
    ]
    for fetch in fetches:
        fetch.start()
    small32[...] = jnp.zeros_like(small32)
    d_small[...] = jnp.zeros_like(d_small)
    gb[0:PAD, :] = d_enc[...]
    ends = jnp.where(first, 0, 1) + jnp.where(last, 0, 1)
    pl.semaphore_wait(barrier, devices - 1 + ends)

    gain = gains[...].astype(F32)
    width = w0.shape[1]
    marks = head_marks(width, ENC_SIZE, BF16)
    marks32 = head_marks(width, ENC_SIZE, F32)
    ones = ones_per_head(PAD, marks)

    def rows(k, size=CH):
        return pl.ds(pl.multiple_of(k * size, size), size)

    def give_enc():
        return far(d_enc, gb.at[PAD : 2 * PAD, :], ex_s.at[0], ex_r.at[0], {"tensor": over})

    def give_part(i, half):
        cut = rows(i, 256)
        n = 1 + 2 * i + half
        return far(
            send.at[(1 - half) * PAD : (2 - half) * PAD, cut],
            recv.at[half * PAD : (half + 1) * PAD, cut],
            ex_s.at[n], ex_r.at[n], {"tensor": over},
        )

    def give_last(i):
        cut = rows(i, 256)
        return far(send1.at[:, cut], recv1.at[:, cut], ex_s.at[7 + i], ex_r.at[7 + i], {"tensor": over})

    def ff_back(g, i, down):
        c = rows(i, 256)
        d_down = tn(y[g, :, c], gb[...]).astype(BF16)
        dh = nt(gb[...], down[c, :]) * gp[g, :, c].astype(F32)
        d_upb[g, :, c] = colsum(dh)
        dub = dh.astype(BF16)
        du[g, :, c] = dub
        d_up = nn(ut[...], dub).astype(BF16)
        if g == 0:
            acc[1, pl.ds(pl.multiple_of(A_TOP + i * 256, 64), 256), :] = d_down
            acc[0, A_TOP:B_TOP, c] = d_up
        else:
            enc_mate[1, c, :] = d_down
            enc_mate[0, 0:ENC_A, c] = d_up

    def ff_in(i):
        c = rows(i, 256)
        t = nt(du[0], up0[c, :]) + nt(du[1], up1[c, :])
        part[:, c] = t
        send[:, c] = t.astype(BF16)
        give_part(i, 0).start()
        give_part(i, 1).start()

    def norm_two():
        for fetch in fetches[7:]:
            fetch.wait()
        for k in range(D // 256):
            give_part(k, 0).wait_recv()
            give_part(k, 1).wait_recv()

        def body(j):
            r = rows(j, 64)
            da = part[r, :] + recv[r, :].astype(F32)
            hat, scale = normal(x1[r, :])
            g = gb[r, :].astype(F32)
            d = g + normal_back(da, hat, scale, gain[1:2])
            gx[r, :] = d.astype(BF16)
            dx1[r, :] = d

            @pl.when(j < 2)
            def _():
                d_small[1:2, :] += colsum(da * hat)
                d_small[3:4, :] += colsum(da)
                d_small[4:5, :] += colsum(d)
                d_small[5:6, :] += colsum(g)

        loop(2 * PAD // 64, body)

    def attention(g, c):
        if c == 0:
            d_proj = tn(o[g], gx[...]).astype(BF16)
            if g == 0:
                acc[1, B_TOP + width : S_TOP, :] = d_proj
            else:
                enc_mate[1, ENC_A + width : ENC_A + 2 * width, :] = d_proj
            d_o[...] = nt(gx[...], (proj0, proj1)[g][...]).astype(BF16)
        r = slice(c * PAD, (c + 1) * PAD)
        d_acts[g, 0, r], d_acts[g, 1, r], d_acts[g, 2, r] = attend_back(
            qkv[g, 0, r], qkv[g, 1, r], qkv[g, 2, r], p[g, c], o[g, r], 1.0 / nn(p[g, c], ones),
            d_o[r, :], marks, marks32, None, ones, ENC_SCALE,
        )
        if c == 1:
            d_qvb[g, 0:1, :] = colsum(d_acts[g, 0].astype(F32))
            d_qvb[g, 1:2, :] = colsum(d_acts[g, 2].astype(F32))

    def project_in(i):
        c = rows(i, 256)
        t = 0.0
        for g, w in enumerate((w0, w1)):
            for j in range(3):
                t += nn(d_acts[g, j], w[j, :, c])
        own[:, c] = t[:PAD]
        send1[:, c] = t[PAD:].astype(BF16)
        give_last(i).start()

    def project_grad(g):
        for j in range(3):
            row = (j % 2) * width
            d = tn(d_acts[g, j], a[...]).astype(BF16)
            if g == 0:
                acc[j // 2, B_TOP + row : B_TOP + row + width, :] = d
            else:
                enc_mate[j // 2, ENC_A + row : ENC_A + row + width, :] = d

    def norm_one():
        for k in range(D // 256):
            give_last(k).wait_recv()

        def body(j):
            r = rows(j, 64)
            da = own[r, :] + recv1[r, :].astype(F32)
            hat, scale = normal(x[r, :])
            d_small[0:1, :] += colsum(da * hat)
            d_small[2:3, :] += colsum(da)
            dx32[r, :] = dx1[r, :] + normal_back(da, hat, scale, gain[0:1])

        loop(PAD // 64, body)
        turned = jnp.transpose(dx32[...])
        cut = D // devices
        for k in range(devices):
            dx[k] = turned[k * cut : (k + 1) * cut, 0:VIS].astype(BF16)
        for r in range(LANES):
            small32[r, 8:9, 0:512] = dec_upb[:, r * 512 : (r + 1) * 512]
            small32[r, 9:10, 0:128] = dec_qvb[0:1, r * 128 : (r + 1) * 128]
            small32[r, 9:10, 128:256] = dec_qvb[1:2, r * 128 : (r + 1) * 128]
            small32[r, 0:8, 0:512] = dec_small[...]
            small32[r, 16:24, :] = d_small[...]
        for g, shard in enumerate((lane, mate)):
            small32[shard, 10:11, :] = d_upb[g]
            small32[shard, 11:12, 0:192] = d_qvb[g, 0:1]
            small32[shard, 11:12, 256:448] = d_qvb[g, 1:2]
        for r in range(LANES):
            for h in range(2):
                small[r, h] = small32[r, h * SMALL : (h + 1) * SMALL].astype(BF16)
        acc[:, S_TOP : S_TOP + SMALL, :] = small[lane]
        yacc[:, DEC_ROWS - EARLY_ROWS :, :] = small[over]
        core_copy(LATE, small.at[mate], SMALL).start()
        corey_copy(LATE, small.at[cross], SMALL).start()
        for step in range(1, devices):
            dx_copy(step).start()
        dx_out[me] = dx[me]

    def core_enc(lo, hi):
        for m, block in enumerate(ORDER):
            if lo <= block < hi:
                src = pl.ds(block * CH - DEC_ROWS, CH)
                core_copy(m, enc_mate.at[:, src, :]).start()

    def first_piece():
        for fetch in fetches[:7]:
            fetch.wait()
        ut[...] = jnp.transpose(u[...])
        give_enc().wait_recv()

    def ff_step(k):
        for g, down in enumerate((down0, down1)):
            @pl.when(lax.rem(k, 2) == g)
            def _(g=g, down=down):
                ff_back(g, lax.div(k, 2), down)

    def run_pieces(n):
        def several(low, high, body):
            begin = sum(jnp.where(n > t, 1, 0) for t in PIECES[low:high])
            end = sum(jnp.where(n >= t, 1, 0) for t in PIECES[low:high])
            lax.fori_loop(begin, end, lambda k, c: (body(k), c)[1], 0)

        def single(k, body):
            @pl.when(n == PIECES[k])
            def _():
                body()

        single(0, first_piece)
        several(1, 7, ff_step)
        single(7, lambda: core_enc(DEC_K, DEC_K + ENC_A // CH))
        several(8, 11, ff_in)
        single(11, norm_two)
        for k in range(4):
            single(12 + k, lambda k=k: attention(k // 2, k % 2))
        several(16, 19, project_in)
        for g in range(2):
            single(19 + g, lambda g=g: project_grad(g))
        single(21, lambda: core_enc(DEC_K + ENC_A // CH, B_K))
        single(22, norm_one)

    def dx_copy(step):
        peer, place = group_peer(step)
        return far(dx.at[peer], dx_out.at[me], dx_s.at[step], dx_r.at[step], place)

    def emb_copy(step):
        return far(
            out.at[:, pl.ds(512, CH), :], emb.at[lane], emb_s.at[step], emb_r.at[step],
            {"tensor": lax.rem(lane + step, LANES)},
        )

    def block_of(m):
        if isinstance(m, int):
            return ORDER[m]
        shift = 0
        for k in range(1, ALL_K):
            if ORDER[k] - k != ORDER[k - 1] - k + 1:
                shift = jnp.where(m >= k, ORDER[k] - k, shift)
        return m + shift

    def is_dec(m):
        return (block_of(m) < DEC_K) & (m >= EARLY)

    def at(m, size=CH):
        if isinstance(m, int):
            return pl.ds(ORDER[m] * CH, size)
        return pl.ds(pl.multiple_of(block_of(m) * CH, CH), size)

    def slot(m, size=CH):
        if isinstance(m, int):
            return pl.ds(m * CH, size)
        return pl.ds(pl.multiple_of(m * CH, CH), size)

    def y_at(m, size=CH):
        if isinstance(m, int):
            return pl.ds((min(ORDER[m], DEC_K) - EARLY) * CH, size)
        return pl.ds(pl.multiple_of((jnp.minimum(block_of(m), DEC_K) - EARLY) * CH, CH), size)

    def core_copy(m, src, size=CH):
        return far(src, out.at[:, at(m, size), :], core_s.at[m], core_r.at[m], {"tensor": mate})

    def corey_copy(m, src, size=CH):
        return far(src, rcy.at[:, y_at(m, size), :], corey_s.at[m], corey_r.at[m], {"tensor": mate})

    def y_copy(m, size=CH):
        cut = y_at(m, size)
        return far(
            yacc.at[:, cut, :], ry.at[:, cut, :], y_s.at[m], y_r.at[m], {"tensor": over}
        )

    def x_copy(m, size=CH):
        return far(
            acc.at[1 - sec, at(m, size), :], land_x.at[0, slot(m, size), :], x_s.at[m], x_r.at[m],
            {"section": 1 - sec},
        )

    def xc_copy(m):
        return far(
            acc.at[:, at(m), :], land_x.at[:, slot(m), :], x_s.at[m], x_r.at[m],
            {"section": 1 - sec},
        )

    def z_copy(m, whole, right, size=CH):
        land = land_l if right else land_r
        if whole:
            src, dst = acc.at[:, at(m), :], land.at[:, slot(m), :]
        else:
            src, dst = acc.at[sec, at(m, size), :], land.at[0, slot(m, size), :]
        landed = zl_r if right else zr_r
        return far(src, dst, z_s.at[m], landed.at[m], {"dp": pos + 1 if right else pos - 1})

    def b_copy(m, whole, right, size=CH):
        place = out.at[:, at(m), :] if whole else out.at[sec, at(m, size), :]
        sent = br_s if right else bl_s
        return far(place, place, sent.at[m], b_r.at[m], {"dp": pos + 1 if right else pos - 1})

    def a_copy(m, size=CH):
        place = out.at[sec, at(m, size), :]
        return far(place, place, a_s.at[m], a_r.at[m], {"section": 1 - sec})

    def a_wait(m, size=CH):
        place = out.at[1 - sec, at(m, size), :]
        far(place, place, a_s.at[m], a_r.at[m], {"section": 1 - sec}).wait_recv()

    give_enc().start()

    for m in range(EARLY, ALL_K):
        if ORDER[m] < DEC_K:
            core_copy(m, dec.at[mate, :, at(m), :]).start()
            corey_copy(m, dec.at[cross, :, at(m), :]).start()
    for load in loads:
        load.wait()

    def join_core(m, size):
        core_copy(m, out.at[:, at(m, size), :], size).wait_recv()
        acc[:, at(m, size), :] = add(acc[:, at(m, size), :], out[:, at(m, size), :])

    def join_core_y(m, size):
        corey_copy(m, rcy.at[:, y_at(m, size), :], size).wait_recv()
        yacc[:, y_at(m, size), :] = add(yacc[:, y_at(m, size), :], rcy[:, y_at(m, size), :])
        y_copy(m, size).start()

    def stage_c(m):
        @pl.when((m >= EARLY) & (m != LATE))
        def _():
            join_core(m, CH)

            @pl.when(is_dec(m))
            def _():
                join_core_y(m, CH)

        @pl.when(m == LATE)
        def _():
            join_core(m, SMALL)
            join_core_y(m, SMALL)

    def flush(m):
        return pltpu.make_async_copy(
            out.at[:, at(m), :], total.at[:, at(m), :], flush_s.at[m]
        )

    def finished(m):
        flush(m).start()

        @pl.when(block_of(m) == DEC_K - 1)
        def _():
            for step in range(1, LANES):
                emb_copy(step).start()
            emb[lane] = out[:, 512 : 512 + CH, :]

    def line_of(root, whole, size=CH):
        left = pos < root
        right = pos > root
        here = pos == root
        reach = max(root, count - 1 - root)
        level = jnp.where(left, pos, jnp.where(right, count - 1 - pos, reach))
        dist = jnp.where(left, root - pos, pos - root)

        def view(ref, m):
            return ref.at[:, at(m), :] if whole else ref.at[sec, at(m, size), :]

        def landed(ref, m):
            return ref.at[:, slot(m), :] if whole else ref.at[0, slot(m, size), :]

        def hop(m, rightward):
            return z_copy(m, whole, rightward, size)

        def back_hop(m, rightward):
            return b_copy(m, whole, rightward, size)

        def outer(m):
            @pl.when(left & first)
            def _():
                hop(m, True).start()

            @pl.when(right & last)
            def _():
                hop(m, False).start()

        def inward(m):
            @pl.when(left & (pos > 0))
            def _():
                hop(m, True).wait_recv()
                view(acc, m)[...] = add(view(acc, m)[...], landed(land_l, m)[...])
                hop(m, True).start()

            @pl.when(right & (pos < count - 1))
            def _():
                hop(m, False).wait_recv()
                view(acc, m)[...] = add(view(acc, m)[...], landed(land_r, m)[...])
                hop(m, False).start()

            @pl.when(here)
            def _():
                total = view(acc, m)[...].astype(F32)
                if root > 0:
                    hop(m, True).wait_recv()
                    total = total + landed(land_l, m)[...].astype(F32)
                if root < count - 1:
                    hop(m, False).wait_recv()
                    total = total + landed(land_r, m)[...].astype(F32)
                if whole:
                    view(acc, m)[...] = total.astype(BF16)
                    xc_copy(m).start()
                else:
                    view(out, m)[...] = total.astype(BF16)
                    spread(m)
                    a_copy(m, size).start()

        def spread(m):
            if root > 0:
                back_hop(m, False).start()
            if root < count - 1:
                back_hop(m, True).start()

        def crossed(m):
            xc_copy(m).wait_recv()
            view(out, m)[...] = add(view(acc, m)[...], landed(land_x, m)[...])
            spread(m)
            finished(m)

        def outward(m):
            back_hop(m, False).wait_recv()

            @pl.when(left & (pos > 0))
            def _():
                back_hop(m, False).start()

            @pl.when(right & (pos < count - 1))
            def _():
                back_hop(m, True).start()

            if whole:
                finished(m)
            else:
                a_copy(m, size).start()

        def sent(m):
            @pl.when(jnp.logical_not(here))
            def _():
                hop(m, True).wait_send()

            @pl.when((pos <= root) & (pos > 0))
            def _():
                back_hop(m, False).wait_send()

            @pl.when((pos >= root) & (pos < count - 1))
            def _():
                back_hop(m, True).wait_send()

            if whole:
                @pl.when(here)
                def _():
                    xc_copy(m).wait_send()
            else:
                a_copy(m, size).wait_send()

                @pl.when(crosses_first(m))
                def _():
                    x_copy(m, size).wait_send()

        def crosses_first(m):
            return m >= EARLY if XFIRST else m >= 0

        def set_off(m):
            if whole:
                outer(m)
            else:
                x_copy(m, size).start()

        def set_off_early(m):
            if XFIRST:
                outer(m)
            else:
                set_off(m)

        def add_y(m):
            def joined():
                y_copy(m, size).wait_recv()
                acc[:, at(m, size), :] = add(acc[:, at(m, size), :], ry[:, y_at(m, size), :])

            if size == CH:
                pl.when(is_dec(m))(joined)
            else:
                joined()
            set_off(m)

        def add_x(m):
            @pl.when(crosses_first(m))
            def _():
                x_copy(m, size).wait_recv()
                acc[sec, at(m, size), :] = add(
                    acc[sec, at(m, size), :], land_x[0, slot(m, size), :]
                )
                outer(m)

        def last_half(m):
            a_wait(m, size)
            finished(m)

        base = 1 if whole else 2
        back = base + reach + dist + (1 if whole else 0)
        steps = {
            "outward": (back, jnp.logical_not(here), outward),
            "inward": (base + level, level > 0, inward),
            "add_y": (1, True, add_y),
        }
        if whole:
            steps["crossed"] = (base + reach + 1, here, crossed)
        else:
            steps["last"] = (back + 1, True, last_half)
            steps["add_x"] = (2, True, add_x)
        return steps, sent, set_off_early

    low_root = (count - 1) // 2
    high_root = min(low_root + 1, count - 1)
    def is_whole(m):
        return (lax.rem(m, 2) == 0) & (m >= WHOLE_LOW) & (m < WHOLE_HIGH)

    roots = (high_root, count - 1, low_root, 0)
    lines = [
        (lambda m, part=part: is_whole(m) & (lax.rem(m, 8) == part), *line_of(root, True))
        for part, root in zip((0, 2, 4, 6), roots)
    ] + [
        (lambda m: jnp.logical_not(is_whole(m)) & (m != LATE), *line_of(low_root, False)),
        (lambda m: m == LATE, *line_of(low_root, False, SMALL)),
    ]

    def finish(m):
        @pl.when((m >= EARLY) & (m != LATE))
        def _():
            core_copy(m, out.at[:, at(m), :]).wait_send()

            @pl.when(is_dec(m))
            def _():
                corey_copy(m, rcy.at[:, y_at(m), :]).wait_send()
                y_copy(m).wait_send()

        @pl.when(m == LATE)
        def _():
            core_copy(m, out.at[:, at(m, SMALL), :], SMALL).wait_send()
            corey_copy(m, rcy.at[:, y_at(m, SMALL), :], SMALL).wait_send()
            y_copy(m, SMALL).wait_send()

        for mine, _, sent, _ in lines:
            @pl.when(mine(m))
            def _(sent=sent):
                sent(m)

    for m in range(EARLY):
        lines[-2][-1](m)
    far_reach = max(max(root, count - 1 - root) for root in roots)
    depth = LAG * (3 + 2 * far_reach) + 1

    def tick(n):
        @pl.when(n <= PIECES[-1])
        def _():
            run_pieces(n)

        def run(line, name):
            mine, steps, _, _ = line
            if name not in steps:
                return
            offset, enabled, stage = steps[name]
            m = n - LAG * offset
            least = EARLY if name == "add_y" else 0

            @pl.when((m >= least) & (m < ALL_K) & enabled)
            def _():
                @pl.when(mine(m))
                def _():
                    stage(m)

        for name in ("last", "outward", "crossed", "inward", "add_x", "add_y"):
            if name not in ("last", "add_x"):
                @pl.when((lax.rem(n, 2) == 0) & (n >= WHOLE_LOW) & (n < WHOLE_HIGH + depth))
                def _(name=name):
                    for line in lines[:-2]:
                        run(line, name)

            run(lines[-2], name)
            if name != "crossed":
                @pl.when((n >= LATE) & (n < LATE + depth))
                def _(name=name):
                    run(lines[-1], name)

        @pl.when(n < ALL_K)
        def _():
            stage_c(n)

        @pl.when(n >= depth)
        def _():
            finish(n - depth)

    loop(ALL_K + depth, tick)
    loop(ALL_K, lambda m: flush(m).wait())
    for step in range(1, devices):
        dx_copy(step).wait()
    for step in range(1, LANES):
        emb_copy(step).wait()
    give_enc().wait_send()
    for k in range(D // 256):
        give_part(k, 0).wait_send()
        give_part(k, 1).wait_send()
        give_last(k).wait_send()


def backward_call(args, half, hid):
    dma = lambda *s: pltpu.SemaphoreType.DMA(s)
    vm = pltpu.VMEM
    full = ALL_K * CH
    y_half = DEC_ROWS - EARLY_ROWS + SMALL
    k = ALL_K
    rows = 2 * PAD
    cut = D // (2 * LANES)
    specs = [VM, VM] + [ANY] * 18 + [VM] * 3
    return pl.pallas_call(
        backward_and_sums,
        out_shape=[
            jax.ShapeDtypeStruct((2, full, D), BF16),
            jax.ShapeDtypeStruct((LANES, 2, CH, D), BF16),
            jax.ShapeDtypeStruct((2 * LANES, cut, VIS), BF16),
        ],
        in_specs=specs,
        out_specs=[ANY, VM, VM],
        scratch_shapes=[
            vm((rows, D), BF16), vm((D, rows), BF16),
            vm((rows, D), F32), vm((rows, D), BF16), vm((rows, D), BF16),
            vm((2, rows, hid), BF16), vm((rows, D), BF16), vm((rows, D), F32),
            vm((rows, half), BF16), vm((2, 3, rows, half), BF16),
            vm((PAD, D), F32), vm((PAD, D), BF16), vm((PAD, D), BF16), vm((PAD, D), F32),
            vm((2 * LANES, cut, VIS), BF16),
            vm((2, 1, hid), F32), vm((2, 2, half), F32), vm((8, D), F32),
            vm((2, full, D), BF16), vm((2, y_half, D), BF16), vm((2, ENC_A + ENC_B, D), BF16),
            vm((2, full, D), BF16),
            vm((2, y_half, D), BF16), vm((2, y_half, D), BF16),
            *[vm((2, full, D), BF16)] * 3,
            vm((LANES, 32, D), F32), vm((LANES, 2, SMALL, D), BF16),
            *[vm(v.shape, v.dtype) for v in args[2:19]],
            dma(17), dma(2), dma(k), dma(10), dma(10),
            dma(k), dma(k), dma(k), dma(k), dma(k), dma(k),
            dma(k), dma(k), dma(k), dma(k), dma(k),
            dma(k), dma(k), dma(k), dma(k), dma(k), dma(LANES), dma(LANES),
            dma(2 * LANES), dma(2 * LANES),
        ],
        compiler_params=pltpu.CompilerParams(
            collective_id=1, has_side_effects=True, vmem_limit_bytes=VMEM_LIMIT
        ),
    )(*args)


def finish_grads(
    total, emb, decoded, dx, decoded_out, dx_out,
    e_qkv, e_qvb, e_proj, e_up, e_upb, e_down, e_gain, e_off,
    d_qkv, d_qvb, d_proj, d_up, d_upb, d_down, d_gain, d_off, d_ew, d_ev,
):
    half = e_proj.shape[0]
    decoded_out[...] = decoded[...]
    dx_out[...] = dx[...]
    e_up[...] = total[0, A_TOP:B_TOP, :].astype(F32)
    e_down[...] = total[1, A_TOP:B_TOP, :].astype(F32)
    e_qkv[0] = total[0, B_TOP : B_TOP + half, :].astype(F32)
    e_qkv[1] = total[0, B_TOP + half : S_TOP, :].astype(F32)
    e_qkv[2] = total[1, B_TOP : B_TOP + half, :].astype(F32)
    e_proj[...] = total[1, B_TOP + half : S_TOP, :].astype(F32)

    def raw(number):
        h, top, col = tile_of(number)
        return total[h, top : top + CH, col : col + 256]

    def tile(number):
        return raw(number).astype(F32)

    for block in range(GRID // CH):
        rows = slice(block * CH, (block + 1) * CH)
        side = slice(block // 2 * 128, (block // 2 + 1) * 128)
        for k in range(2):
            d_up[rows, k * 256 : (k + 1) * 256] = tile(4 * block + k)
            if block % 2:
                both = jnp.concatenate([raw(4 * block - 2 + k), raw(4 * block + 2 + k)], 0)
                d_down[k * 256 : (k + 1) * 256, side] = jnp.transpose(both).astype(F32)
        one, two = tile(32 + 2 * block), tile(33 + 2 * block)
        d_qkv[0, rows, :] = one[:, 0:128]
        d_qkv[1, rows, :] = one[:, 128:256]
        d_qkv[2, rows, :] = two[:, 0:128]
        d_proj[block % 2 * CH : (block % 2 + 1) * CH, side] = two[:, 128:256]
    for k in range(LANES):
        for h in range(2):
            top = k * 192 + h * 64
            d_ew[top : top + 64, :] = emb[k, h, :, 0:512].astype(F32)
            d_ew[k * 192 + 128 : (k + 1) * 192, h * 256 : (h + 1) * 256] = emb[
                k, h, :, 512:768
            ].astype(F32)
    little = total[0, S_TOP : S_TOP + SMALL, :].astype(F32)
    d_gain[...] = little[0:2, 0:512]
    d_off[...] = little[2:6, 0:512]
    d_ev[...] = little[6:8, 0:512]
    d_upb[...] = little[8, 0:512]
    d_qvb[0:1, :] = little[9:10, 0:128]
    d_qvb[1:2, :] = little[9:10, 128:256]
    e_upb[...] = little[10]
    e_qvb[0:1, :] = little[11:12, 0:192]
    e_qvb[1:2, :] = little[11:12, 256:448]
    little = total[1, S_TOP : S_TOP + SMALL, :].astype(F32)
    e_gain[...] = little[0:2]
    e_off[...] = little[2:6]


def call(kernel, specs, shapes, scratch, args):
    return pl.pallas_call(
        kernel,
        out_shape=[jax.ShapeDtypeStruct(s, d) for s, d in shapes],
        in_specs=specs,
        out_specs=[VM] * len(shapes),
        scratch_shapes=scratch,
        compiler_params=pltpu.CompilerParams(vmem_limit_bytes=VMEM_LIMIT),
    )(*args)


def position_rows():
    quarter = DD // 4
    freq = np.exp(np.arange(quarter, dtype=np.float32) * np.float32(-math.log(10000.0) / quarter))
    angle = np.arange(PAD, dtype=np.float32)[:, None] * freq[None, :].astype(np.float32)
    both = np.concatenate([np.sin(angle), np.cos(angle)], 1).astype(np.float32)
    high = both.astype(jnp.bfloat16)
    low = (both - high.astype(np.float32)).astype(jnp.bfloat16)
    return np.stack([high, low])


def per_device(
    patches, cotangent, widths, visible, window_shift, batch_order,
    encoder_qkv, encoder_qvbias, encoder_proj, encoder_up, encoder_upbias, encoder_down,
    encoder_gains, encoder_offsets,
    decoder_qkv, decoder_qvbias, decoder_proj, decoder_up, decoder_upbias, decoder_down,
    decoder_gains, decoder_offsets, embed_weight, embed_vectors,
):
    qkv0 = encoder_qkv.transpose(1, 2, 0)
    half = qkv0.shape[1]
    hid = encoder_up.shape[1]
    dff = decoder_up.shape[1] * LANES
    flat = patches.transpose(1, 0, 2).reshape(-1, D)
    (
        x, x1, a, u, y, gp, qkv, p, o, qkv1, proj1, up1, down1, dec_buf,
        d_enc, d_dqvb, d_dupb, d_dsmall, out_all,
    ) = forward_call(
        (
            widths, window_shift.T, batch_order, visible, flat, encoder_gains, encoder_offsets,
            encoder_qvbias, encoder_upbias, decoder_qvbias, decoder_upbias,
            qkv0, encoder_proj, encoder_up, encoder_down,
            decoder_qkv.transpose(1, 0, 2), decoder_proj, decoder_up, decoder_down,
            cotangent, embed_weight, embed_vectors, jnp.asarray(position_rows()),
            decoder_gains, decoder_offsets,
        ),
        half, hid, dff,
    )
    total, emb, dx_all = backward_call(
        (
            d_enc, encoder_gains, u, y, gp, encoder_down, down1, encoder_up, up1,
            x, x1, a, qkv, p, o, qkv0, qkv1, encoder_proj, proj1,
            dec_buf, d_dqvb, d_dupb, d_dsmall,
        ),
        half, hid,
    )
    f = lambda *shape: (shape, F32)
    out_all, dx_all, *grads = call(
        finish_grads, [VM] * 4,
        [
            (out_all.shape, BF16), (dx_all.shape, BF16), f(3, half, D), f(2, half), f(half, D), f(D, hid), f(hid), f(hid, D), f(2, D), f(4, D),
            f(3, DD, 128), f(2, 128), f(128, DD), f(DD, 512), f(512), f(512, DD), f(2, DD), f(4, DD),
            f(D, DD), f(2, DD),
        ],
        [], (total, emb, out_all, dx_all),
    )
    grads[0] = grads[0].transpose(2, 0, 1)
    grads[8] = grads[8].transpose(1, 0, 2)
    return (out_all.swapaxes(1, 2), dx_all.swapaxes(1, 2), *grads)


def solution(mesh):
    weights = (
        P(None, None, "tensor"), P(None, "tensor"), P("tensor", None), P(None, "tensor"),
        P("tensor"), P("tensor", None), P(), P(),
    )
    split = P("dp", None, ("section", "tensor"))
    return jax.shard_map(
        per_device,
        mesh=mesh,
        in_specs=(
            P("dp", None, None), P("dp", None, None), P("dp"), P("dp", None), P("dp", None),
            P("dp", None),
        ) + weights + weights + (P(), P()),
        out_specs=(split, split) + weights + weights + (P(), P()),
        check_vma=False,
    )
```

```python
import math

import jax
import jax.numpy as jnp
import numpy as np
from jax import lax
from jax.experimental import pallas as pl
from jax.experimental.pallas import tpu as pltpu
from jax.sharding import PartitionSpec as P

D = 768
HEADS = 12
DD = 512
DHEADS = 16
GRID_ROWS = 64
WIDE = 8
WIN = 4
VIS = 102
CM = 4
GRID = 512
LANES = 4
PAD = 128
EPS = 1e-06
NEG = -10000.0
F32 = jnp.float32
BF16 = jnp.bfloat16
VMEM_LIMIT = 60 * 1024 * 1024

VM = pl.BlockSpec(memory_space=pltpu.VMEM)
SM = pl.BlockSpec(memory_space=pltpu.SMEM)
ANY = pl.BlockSpec(memory_space=pl.ANY)


def nn(a, b):
    return lax.dot_general(a, b, (((1,), (0,)), ((), ())), preferred_element_type=F32)


def nt(a, b):
    return lax.dot_general(a, b, (((1,), (1,)), ((), ())), preferred_element_type=F32)


def tn(a, b):
    return lax.dot_general(a, b, (((0,), (0,)), ((), ())), preferred_element_type=F32)


def loop(count, body, unroll=1):
    def step(i, carry):
        body(i)
        return carry

    lax.fori_loop(0, count, step, 0, unroll=unroll)


def span(i, size):
    return pl.ds(pl.multiple_of(i * size, size), size)


def normal(x):
    center = x - jnp.mean(x, -1, keepdims=True)
    scale = lax.rsqrt(jnp.mean(center * center, -1, keepdims=True) + EPS)
    return center * scale, scale


def normal_back(dy, hat, scale, gain):
    d = dy * gain
    return scale * (
        d - jnp.mean(d, -1, keepdims=True) - hat * jnp.mean(d * hat, -1, keepdims=True)
    )


def gelu_both(h):
    phi = 0.5 * lax.erf(h * math.sqrt(0.5)) + 0.5
    bell = jnp.exp2(h * h * (-0.5 * math.log2(math.e)))
    return h * phi, phi + h * bell * (1.0 / math.sqrt(2.0 * math.pi))


def colsum(x):
    return jnp.sum(x, 0, keepdims=True)


def head_marks(width, size, dtype):
    lane = lax.broadcasted_iota(jnp.int32, (1, width), 1)
    return [((lane >= h * size) & (lane < (h + 1) * size)).astype(dtype) for h in range(width // size)]


def stacked(x, marks):
    return jnp.concatenate([x * m for m in marks], 0)


LOG2E = math.log2(math.e)


def attend(q, k, v, marks, ones, masked, scale):
    keys = k.shape[0]
    s = nt(q, stacked(k, marks))
    parts = []
    for h in range(len(marks)):
        x = masked(s[:, h * keys : (h + 1) * keys] * (scale * LOG2E))
        parts.append(jnp.exp2(x - jnp.max(x, -1, keepdims=True)).astype(BF16))
    e = jnp.concatenate(parts, 1)
    width = q.shape[1]
    if width % 128:
        top, total = nn(e, stacked(v, marks)), nn(e, ones)
    else:
        both = nn(e, jnp.concatenate([stacked(v, marks), ones], 1))
        top, total = both[:, :width], both[:, width:]
    inverse = 1.0 / total
    return e, (top * inverse).astype(BF16), inverse


def attend_back(q, k, v, e, o, inverse, d_out, marks, marks32, rows32, ones, scale):
    keys = k.shape[0]
    width = q.shape[1]
    d_one = d_out.astype(F32) * inverse
    d_two = (d_one * o.astype(F32)).astype(BF16)
    d_one = d_one.astype(BF16)
    if width % 128:
        d_s = nt(d_one, stacked(v, marks)) - nt(d_two, ones)
    else:
        d_s = nt(
            jnp.concatenate([d_one, d_two], 1), jnp.concatenate([stacked(v, marks), -ones], 1)
        )
    dr = (e.astype(F32) * d_s * scale).astype(BF16)
    d_q = nn(dr, stacked(k, marks)).astype(BF16)
    if width % 128:
        d_k_all, d_v_all = tn(dr, q), tn(e, d_one)
        d_k = d_v = 0.0
        for h in range(len(marks)):
            cut = slice(h * keys, (h + 1) * keys)
            d_k += d_k_all[cut] * marks32[h]
            d_v += d_v_all[cut] * marks32[h]
        return d_q, d_k.astype(BF16), d_v.astype(BF16)
    d_k_all = nn(jnp.transpose(q), dr)
    d_v_all = nn(jnp.transpose(d_one), e)
    d_k = d_v = 0.0
    for h in range(len(marks)):
        cut = slice(h * keys, (h + 1) * keys)
        d_k += d_k_all[:, cut] * rows32[h]
        d_v += d_v_all[:, cut] * rows32[h]
    return d_q, jnp.transpose(d_k.astype(BF16)), jnp.transpose(d_v.astype(BF16))


def ones_per_head(keys, marks):
    return jnp.concatenate([jnp.broadcast_to(m, (keys, m.shape[1])) for m in marks], 0)


ENC_SIZE = D // HEADS
ENC_SCALE = ENC_SIZE ** -0.5
DEC_SIZE = DD // DHEADS
DEC_SCALE = DEC_SIZE ** -0.5


CH = 64
DEC_ROWS = 576
ENC_A = 768
ENC_B = 384
DEC_K = DEC_ROWS // CH
B_K = (DEC_ROWS + ENC_A + ENC_B) // CH
ALL_K = B_K + 1
A_TOP = DEC_ROWS
B_TOP = DEC_ROWS + ENC_A
S_TOP = B_TOP + ENC_B
EARLY = 4
XFIRST = True
EARLY_ROWS = EARLY * CH
LAG = 2
ORDER = (0, 1, 2, 3, 9, 10, 11, 12, 13, 14, 4, 15, 16, 17, 18, 5, 6, 19, 21, 20, 8, 22, 23, 24, 25, 27, 26, 7)
PIECES = (0, 2, 2, 2, 2, 2, 2, 2, 3, 3, 3, 10, 12, 12, 13, 13, 14, 14, 15, 15, 15, 16, 20)
LATE = ORDER.index(B_K)
WHOLE_LOW = 6
WHOLE_HIGH = 22
SMALL = 16


def tile_of(number):
    place = number // 3
    return place % 2, place // 2 * CH, number % 3 * 256


MESH = pl.DeviceIdType.MESH


def far(src, dst, send, recv, peer):
    return pltpu.make_async_remote_copy(
        src_ref=src, dst_ref=dst, send_sem=send, recv_sem=recv, device_id=peer, device_id_type=MESH
    )


def forward_and_decoder(
    wid, shifts, order, vis, pat, gains, offs, b_qv, b_up, b_dqv, b_dup,
    h_qkv, h_proj, h_up, h_down, h_dqkv, h_dproj, h_dup, h_ddown,
    cot_hbm, ew, evec, table, dgains, doffs,
    o_x, o_x1, o_a, o_u, o_y, o_gp, o_qkv, o_p, o_o, o_w, o_wproj, o_wup, o_wdown, o_dec,
    d_enc, d_qvb, d_upb, d_small, dec_out,
    w_qkv, w_proj, w_up, w_down, bias, biases, qkv, proj, up, down,
    ex, ea, eu, ey, egp, eqkv, ep, eo, ex1, epart, esend, erecv, esend2, erecv2, eown,
    cot, x0, x1, a, acts, probs, o, inverse, u, ut, y, gp, g32, gb, gt, acc, e_ref, hot, perm, buf, dsend, e_rc, e_rcy, e_rx, e_ry,
    load_s, out_s, cot_s, w_s, w_r, bias_s, bias_r, dw_s, dw_r, ex_s, ex_r, ex2_s, ex2_r, do_s, do_r, e_s, e_r,
):
    sec = lax.axis_index("section")
    lane = lax.axis_index("tensor")
    mate = lane + 1 - 2 * lax.rem(lane, 2)
    over = lax.rem(lane + 2, LANES)
    cross = lax.rem(mate + 2, LANES)
    me = sec * LANES + lane
    devices = 2 * LANES
    clip = me
    clips = (me, sec * LANES + over)

    def group_peer(step):
        peer = lax.rem(me + step, devices)
        return peer, {"section": lax.div(peer, LANES), "tensor": lax.rem(peer, LANES)}

    own = [
        pltpu.make_async_copy(src, dst.at[0], load_s.at[n])
        for n, (src, dst) in enumerate(
            ((h_qkv, w_qkv), (h_proj, w_proj), (h_up, w_up), (h_down, w_down))
        )
    ]

    def place(n, shard, part=None):
        thick = (128, 128, 512, 512)[n]
        base = shard * thick
        cut = pl.ds(pl.multiple_of(base, thick), thick)
        if part is None:
            return (qkv.at[:, :, cut], proj.at[cut, :], up.at[:, cut], down.at[cut, :])[n]
        some = span(part, (256, 64, 256, 256)[n])
        if n == 0:
            return qkv.at[:, some, cut]
        if n == 2:
            return up.at[some, cut]
        few = thick // 2
        rows = pl.ds(pl.multiple_of(base + part * few, few), few)
        return (proj if n == 1 else down).at[rows, :]

    shards = (h_dqkv, h_dproj, h_dup, h_ddown)
    keep = [
        pltpu.make_async_copy(shards[n], place(n, lane), load_s.at[4 + n]) for n in range(4)
    ]
    for copy in own + keep:
        copy.start()
    fetch = pltpu.make_async_copy(cot_hbm.at[clip], cot, cot_s)
    fetch.start()

    barrier = pltpu.get_barrier_semaphore()
    for step in range(1, devices):
        pl.semaphore_signal(barrier, inc=1, device_id_type=MESH, device_id=group_peer(step)[1])
    bias[...] = jnp.zeros_like(bias)
    half = w_proj.shape[1]
    bias[0:1, :] = b_up[...].astype(F32).reshape(1, -1)
    bias[1:3, 0:half] = b_qv[...].astype(F32)
    bias[3:4, 0:512] = b_dup[...].astype(F32).reshape(1, -1)
    bias[4:6, 0:128] = b_dqv[...].astype(F32)
    biases[lane] = bias[...]
    stride = pat.shape[0] // VIS
    for c in range(2):
        row = lax.broadcasted_iota(jnp.int32, (PAD, pat.shape[0]), 0)
        col = lax.broadcasted_iota(jnp.int32, (PAD, pat.shape[0]), 1)
        pick = (col == row * stride + clips[c]).astype(F32).astype(BF16)
        ex[c * PAD : (c + 1) * PAD, :] = nn(pick, pat[...])

    pl.semaphore_wait(barrier, devices - 1)

    def enc_weight(n):
        src = (h_qkv, h_proj, h_up, h_down)[n]
        dst = (w_qkv, w_proj, w_up, w_down)[n]
        return far(src, dst.at[1], w_s.at[n], w_r.at[n], {"tensor": mate})

    def bias_copy(step):
        return far(
            bias, biases.at[lane], bias_s.at[step], bias_r.at[step],
            {"tensor": lax.rem(lane + step, LANES)},
        )

    def half_of(n):
        some = span(sec, (256, 64, 256, 256)[n])
        return shards[n].at[:, some, :] if n == 0 else shards[n].at[some, :]

    def dec_weight(n, kind):
        peer = {"section": 1 - sec} if kind == 2 else {"tensor": over if kind == 0 else mate}
        if kind == 0:
            src, dst = half_of(n), place(n, lane, sec)
        elif kind == 1:
            src, dst = shards[n], place(n, lane)
        else:
            src = dst = place(n, over, 1 - sec if kind == 4 else sec)
        return far(src, dst, dw_s.at[5 * n + kind], dw_r.at[5 * n + kind], peer)

    enc_weight(0).start()
    for step in range(1, LANES):
        bias_copy(step).start()
    enc_weight(1).start()
    dec_weight(0, 0).start()
    enc_weight(2).start()
    enc_weight(3).start()
    for n in range(4):
        dec_weight(n, 1).start()

    def pass_on(n):
        dec_weight(n, 0).wait_recv()
        dec_weight(n, 2).start()
        dec_weight(n, 3).start()

    def pass_last(n):
        dec_weight(n, 2).wait_recv()
        dec_weight(n, 4).start()

    def arrived(n):
        keep[n].wait()
        dec_weight(n, 1).wait_recv()
        dec_weight(n, 3).wait_recv()
        dec_weight(n, 4).wait_recv()

    width = wid[clip]
    bits = jnp.where(width == WIDE, 3, 2)
    turn = shifts[0, clip] * width
    mod = GRID - 1
    spot = 0
    for i in range(order.shape[1]):
        spot = spot + jnp.where(order[0, i] == clip, i, 0)
    batch = spot // CM
    count = 0
    for i in range(order.shape[1]):
        count = count + jnp.where(batch == i // CM, wid[order[0, i]], 0)
    factor_rows = CM * GRID / (jnp.full((1, 1), count, jnp.int32) * GRID_ROWS).astype(F32)

    def slot_of(index):
        return (index - turn) & mod

    def code_of(slot):
        band = ((slot >> bits) + shifts[0, clip]) >> 2
        strip = ((slot & (width - 1)) + shifts[1, clip]) >> 2
        return band * 4 + strip

    def valid_rows():
        slot = slot_of(lax.broadcasted_iota(jnp.int32, (GRID, 1), 0))
        return (slot < GRID_ROWS * width).astype(F32)

    def clip_gradient():
        fetch.wait()
        rolled = slot_of(lax.broadcasted_iota(jnp.int32, (GRID, GRID), 0))
        column = lax.broadcasted_iota(jnp.int32, (GRID, GRID), 1)
        perm[...] = (rolled == column).astype(F32).astype(BF16)
        g = nn(perm[...], cot[...]) * valid_rows() * factor_rows
        g32[...] = g
        gb[...] = g.astype(BF16)
        gt[...] = jnp.transpose(g.astype(BF16))
        d_small[...] = jnp.zeros_like(d_small)
        d_small[5:6, :] = colsum(g)

    seen = vis[pl.ds(clip, 1), :]
    target = jnp.concatenate([(seen + turn) & mod, jnp.full((1, PAD - VIS), -1, jnp.int32)], 1)

    def places(i):
        r = span(i, PAD)
        index = lax.broadcasted_iota(jnp.int32, (PAD, PAD), 0) + i * PAD
        column = lax.broadcasted_iota(jnp.int32, (PAD, PAD), 1)
        hot[r, :] = (index == target).astype(F32).astype(BF16)
        slot = slot_of(index)
        by_row = ((slot >> bits) == column).astype(F32).astype(BF16)
        by_col = ((slot & (width - 1)) == column).astype(F32).astype(BF16)
        row_part = nn(by_row, table[0]) + nn(by_row, table[1])
        col_part = nn(by_col, table[0]) + nn(by_col, table[1])
        x0[r, :] = jnp.concatenate([row_part, col_part], 1)

    egain = gains[...].astype(F32)
    eoff = offs[...].astype(F32)
    emarks = head_marks(half, ENC_SIZE, BF16)
    key = lax.broadcasted_iota(jnp.int32, (PAD, PAD), 1)
    floor = jnp.where(key < VIS, NEG * LOG2E, -1e30)
    eones = ones_per_head(PAD, emarks)
    blocks = D // 256

    def give_part(i, side):
        cut = span(i, 256)
        return far(
            esend.at[(1 - side) * PAD : (2 - side) * PAD, cut],
            erecv.at[side * PAD : (side + 1) * PAD, cut],
            ex_s.at[2 * i + side], ex_r.at[2 * i + side], {"tensor": over},
        )

    for c in range(2):
        rows = slice(c * PAD, (c + 1) * PAD)
        hat, _ = normal(ex[rows, :])
        ea[rows, :] = (hat * egain[0:1] + eoff[0:1]).astype(BF16)
        limit = (VIS * wid[clips[c]]) // WIDE
        for g, shard in enumerate((lane, mate)):
            if c == 0 and g == 0:
                own[0].wait()
            if c == 0 and g == 1:
                enc_weight(0).wait_recv()
                for step in range(1, LANES):
                    bias_copy(step).wait_recv()
            if g == 0:
                bq, bv = bias[1:2, 0:half], bias[2:3, 0:half]
            else:
                bq, bv = biases[shard, 1:2, 0:half], biases[shard, 2:3, 0:half]
            eqkv[g, 0, rows] = (nt(ea[rows, :], w_qkv[g, 0]) + bq).astype(BF16)
            eqkv[g, 1, rows] = nt(ea[rows, :], w_qkv[g, 1]).astype(BF16)
            eqkv[g, 2, rows] = (nt(ea[rows, :], w_qkv[g, 2]) + bv).astype(BF16)
            p, out, _ = attend(
                eqkv[g, 0, rows], eqkv[g, 1, rows], eqkv[g, 2, rows], emarks, eones,
                lambda s: jnp.where(key < limit, s, floor), ENC_SCALE,
            )
            ep[g, c] = p
            eo[g, rows] = out
        if c == 0:
            own[1].wait()
            enc_weight(1).wait_recv()
        for i in range(blocks):
            cut = slice(i * 256, (i + 1) * 256)
            t = nn(eo[0, rows], w_proj[0, :, cut]) + nn(eo[1, rows], w_proj[1, :, cut])
            epart[rows, cut] = t
            esend[rows, cut] = t.astype(BF16)
            give_part(i, 1 - c).start()
    pass_on(0)
    clip_gradient()
    own[2].wait()
    enc_weight(2).wait_recv()

    def give_last(i):
        cut = span(i, 256)
        return far(
            esend2.at[:, cut], erecv2.at[:, cut], ex2_s.at[i], ex2_r.at[i], {"tensor": over}
        )

    for c in (1, 0):
        rows = slice(c * PAD, (c + 1) * PAD)
        for i in range(blocks):
            give_part(i, c).wait_recv()
        t = ex[rows, :] + epart[rows, :] + erecv[rows, :].astype(F32) + eoff[2:3]
        ex1[rows, :] = t
        hat, _ = normal(t)
        eu[rows, :] = (hat * egain[1:2] + eoff[1:2]).astype(BF16)
        for g, shard in enumerate((lane, mate)):

            def enc_ff(i, g=g, shard=shard, rows=rows):
                cut = span(i, 256)
                h = nn(eu[rows, :], w_up[g, :, cut]) + biases[shard, 0:1, cut]
                act, slope = gelu_both(h)
                ey[g, rows, cut] = act.astype(BF16)
                egp[g, rows, cut] = slope.astype(BF16)

            loop(w_up.shape[2] // 256, enc_ff, unroll=3)
        if c == 1:
            own[3].wait()
            enc_weight(3).wait_recv()
        for i in range(blocks):
            cut = slice(i * 256, (i + 1) * 256)
            t = nn(ey[0, rows], w_down[0, :, cut]) + nn(ey[1, rows], w_down[1, :, cut])
            if c == 0:
                eown[:, cut] = t
            else:
                esend2[:, cut] = t.astype(BF16)
                give_last(i).start()
        if c == 1:
            for n in (1, 2, 3):
                dec_weight(n, 0).start()
            pass_last(0)
    outs = [
        pltpu.make_async_copy(src, dst, out_s.at[n])
        for n, (src, dst) in enumerate(
            (
                (ex.at[0:PAD, :], o_x), (ex1, o_x1), (ea, o_a), (eu, o_u), (ey, o_y), (egp, o_gp),
                (eqkv, o_qkv), (ep, o_p), (eo, o_o), (w_qkv.at[1], o_w), (w_proj.at[1], o_wproj),
                (w_up.at[1], o_wup), (w_down.at[1], o_wdown),
            )
        )
    ]
    for copy in outs:
        copy.start()
    loop(GRID // PAD, places, unroll=2)
    for i in range(blocks):
        give_last(i).wait_recv()

    e_ref[...] = (ex1[0:PAD, :] + eown[...] + erecv2[...].astype(F32) + eoff[3:4]).astype(BF16)
    vec = evec[...].astype(F32)
    m = (nn(e_ref[...], ew[...]) + vec[0:1]).astype(BF16)
    gain = dgains[...].astype(F32)
    offsets = doffs[...].astype(F32)

    def start(i):
        r = span(i, PAD)
        oh = hot[r, :]
        hit = jnp.sum(oh.astype(F32), -1, keepdims=True)
        x = jnp.where(hit > 0, nn(oh, m), vec[1:2]).astype(BF16).astype(F32) + x0[r, :]
        x0[r, :] = x
        hat, _ = normal(x)
        a[r, :] = (hat * gain[0:1] + offsets[0:1]).astype(BF16)

    loop(GRID // PAD, start, unroll=2)
    arrived(0)

    def dec_bias(row, size):
        return jnp.concatenate([biases[k, row : row + 1, 0:size] for k in range(LANES)], 1)

    acts[0] = (nn(a[...], qkv[0]) + dec_bias(4, 128)).astype(BF16)
    acts[1] = nn(a[...], qkv[1]).astype(BF16)
    acts[2] = (nn(a[...], qkv[2]) + dec_bias(5, 128)).astype(BF16)
    pass_on(1)
    pass_on(2)
    marks = head_marks(128, DEC_SIZE, BF16)
    marks32 = head_marks(128, DEC_SIZE, F32)
    dim = lax.broadcasted_iota(jnp.int32, (128, 1), 0)
    rows32 = [
        ((dim >= h * DEC_SIZE) & (dim < (h + 1) * DEC_SIZE)).astype(F32) for h in range(len(marks))
    ]

    ones = ones_per_head(PAD, marks)

    def attention(i):
        r = span(i, PAD)
        row_slot = slot_of(lax.broadcasted_iota(jnp.int32, (PAD, PAD), 0) + i * PAD)
        key_slot = slot_of(lax.broadcasted_iota(jnp.int32, (PAD, PAD), 1) + i * PAD)
        allowed = (code_of(row_slot) == code_of(key_slot)) & (key_slot < GRID_ROWS * width)
        for g in range(DD // 128):
            c = slice(g * 128, (g + 1) * 128)
            probs[i, :, g * 512 : (g + 1) * 512], o[r, c], inverse[r, c] = attend(
                acts[0, r, c], acts[1, r, c], acts[2, r, c], marks, ones,
                lambda s: jnp.where(allowed, s, NEG * LOG2E), DEC_SCALE,
            )

    loop(GRID // PAD, attention, unroll=4)
    pass_last(1)
    pass_last(2)
    pass_on(3)
    arrived(1)

    def mix(i):
        r = span(i, 256)
        x = x0[r, :] + nn(o[r, :], proj[...]) + offsets[2:3]
        x1[r, :] = x
        hat, _ = normal(x)
        un = hat * gain[1:2] + offsets[1:2]
        u[r, :] = un.astype(BF16)
        ut[:, r] = jnp.transpose(un.astype(BF16))

    loop(2, mix)
    pass_last(3)
    arrived(2)

    def ff(i):
        c = span(i, 256)
        h = nn(u[...], up[:, c]) + biases[lax.div(i, 2), 3:4, span(lax.rem(i, 2), 256)]
        act, slope = gelu_both(h)
        y[:, c] = act.astype(BF16)
        gp[:, c] = slope.astype(BF16)

    loop(up.shape[1] // 256, ff, unroll=4)
    arrived(3)
    def out(i):
        c = span(i, 256)
        acc[:, c] = nn(y[...], down[:, c])

    loop(2, out)
    full = ((acc[...] + x1[...] + offsets[3:4]) * valid_rows()).astype(BF16)
    turned = tn(full, perm[...]).astype(BF16)
    for k in range(devices):
        dsend[k] = turned[k * dsend.shape[1] : (k + 1) * dsend.shape[1]]

    def decoded_copy(step):
        peer, spot = group_peer(step)
        return far(dsend.at[peer], dec_out.at[me], do_s.at[step], do_r.at[step], spot)

    for step in range(1, devices):
        decoded_copy(step).start()
    dec_out[me] = dsend[me]

    def ff_back(shard):
        for side in range(2):
            c = span(2 * shard + side, 256)
            d_down = nn(gt[...], y[:, c]).astype(BF16)
            dh = nt(gb[...], down[c, :]) * gp[:, c].astype(F32)
            d_upb[:, c] = colsum(dh)
            du = dh.astype(BF16)
            gp[:, c] = du
            d_up = nn(ut[...], du).astype(BF16)
            for block in range(GRID // CH):
                rows = slice(block * CH, (block + 1) * CH)
                h, top, col = tile_of(4 * block + side)
                buf[shard, h, top : top + CH, col : col + 256] = d_up[rows]
                h, top, col = tile_of(4 * block + 2 + side)
                buf[shard, h, top : top + CH, col : col + 256] = d_down[rows]

    def early_core(which):
        shard, land = ((mate, e_rc), (cross, e_rcy))[which]
        return far(
            buf.at[shard, :, 0:EARLY_ROWS, :], land, e_s.at[which], e_r.at[which], {"tensor": mate}
        )

    def early_x(which):
        return far(
            buf.at[(over, lane)[which], 1 - sec, 0:EARLY_ROWS, :], e_rx.at[which],
            e_s.at[2 + which], e_r.at[2 + which], {"section": 1 - sec},
        )

    def early_y():
        return far(
            buf.at[over, sec, 0:EARLY_ROWS, :], e_ry, e_s.at[4], e_r.at[4], {"tensor": over}
        )

    def early_add(shard, land):
        def body(i):
            r = span(i, CH)
            buf[shard, :, r, :] = buf[shard, :, r, :] + land[:, r, :]

        loop(EARLY_ROWS // CH, body)

    def early_half(shard, land):
        buf[shard, sec, 0:EARLY_ROWS, :] = buf[shard, sec, 0:EARLY_ROWS, :] + land

    def ff_step(i):
        ff_back(jnp.where(i == 0, cross, jnp.where(i == 1, over, jnp.where(i == 2, mate, lane))))

        @pl.when(i == 1)
        def _():
            early_core(1).start()

        @pl.when(i == 2)
        def _():
            early_core(0).start()

    loop(LANES, ff_step)
    early_core(1).wait_recv()
    early_add(over, e_rcy)
    early_x(0).start()

    def ff_in(i):
        c = span(i, 256)
        acc[:, c] = nt(gp[...], up[c, :])

    loop(2, ff_in)
    early_core(0).wait_recv()
    early_add(lane, e_rc)
    early_x(1).start()

    def mix_back(i):
        r = span(i, 256)
        hat, scale = normal(x1[r, :])
        da = acc[r, :]
        dx = g32[r, :] + normal_back(da, hat, scale, gain[1:2])
        d_small[1:2, :] += colsum(da * hat)
        d_small[3:4, :] += colsum(da)
        d_small[4:5, :] += colsum(dx)
        g32[r, :] = dx
        dxb = dx.astype(BF16)
        gb[r, :] = dxb
        u[r, :] = nt(dxb, proj[...]).astype(BF16)

    loop(2, mix_back)
    d_proj = tn(o[...], gb[...]).astype(BF16)
    for block in range(GRID // CH):
        h, top, col = tile_of(33 + 2 * block)
        side = slice(block // 2 * 128, (block // 2 + 1) * 128)
        for k in range(LANES):
            row = k * 128 + block % 2 * CH
            buf[k, h, top : top + CH, col + 128 : col + 256] = d_proj[row : row + CH, side]

    def attention_back(i):
        r = span(i, PAD)
        for k in range(DD // 128):
            c = slice(k * 128, (k + 1) * 128)
            acts[0, r, c], acts[1, r, c], acts[2, r, c] = attend_back(
                acts[0, r, c], acts[1, r, c], acts[2, r, c],
                probs[i, :, k * 512 : (k + 1) * 512], o[r, c], inverse[r, c], u[r, c],
                marks, marks32, rows32, ones, DEC_SCALE,
            )

    loop(GRID // PAD, attention_back, unroll=4)
    early_x(0).wait_recv()
    early_half(over, e_rx[0])
    early_y().start()
    d_qvb[0:1, :] = colsum(acts[0].astype(F32))
    d_qvb[1:2, :] = colsum(acts[2].astype(F32))

    def project_back(i):
        c = span(i, 256)
        acc[:, c] = (
            nt(acts[0], qkv[0, c, :]) + nt(acts[1], qkv[1, c, :]) + nt(acts[2], qkv[2, c, :])
        )

    loop(2, project_back)
    gt[...] = jnp.transpose(a[...])
    for j in range(3):
        d_qkv = nn(gt[...], acts[j]).astype(BF16)
        for block in range(GRID // CH):
            h, top, col = tile_of(32 + 2 * block + j // 2)
            col = col + j % 2 * 128
            rows = slice(block * CH, (block + 1) * CH)
            for k in range(LANES):
                buf[k, h, top : top + CH, col : col + 128] = d_qkv[rows, k * 128 : (k + 1) * 128]

    def start_back(i):
        r = span(i, PAD)
        hat, scale = normal(x0[r, :])
        da = acc[r, :]
        dx = g32[r, :] + normal_back(da, hat, scale, gain[0:1])
        d_small[0:1, :] += colsum(da * hat)
        d_small[2:3, :] += colsum(da)
        dg = dx.astype(BF16)
        gb[r, :] = dg
        hit = jnp.sum(hot[r, :].astype(F32), -1, keepdims=True)
        d_small[7:8, :] += colsum(jnp.where(hit > 0, 0.0, dg.astype(F32)))

    loop(GRID // PAD, start_back, unroll=2)
    dm = tn(hot[...], gb[...])
    d_small[6:7, :] = colsum(dm)
    dmb = dm.astype(BF16)
    d_enc[...] = nt(dmb, ew[...]).astype(BF16)
    d_ew = tn(e_ref[...], dmb).astype(BF16)
    for k in range(LANES):
        for h in range(2):
            top = k * 192 + h * 64
            buf[k, h, 512:576, 0:512] = d_ew[top : top + 64]
            buf[k, h, 512:576, 512:768] = d_ew[k * 192 + 128 : (k + 1) * 192, h * 256 : (h + 1) * 256]

    early_x(1).wait_recv()
    early_half(lane, e_rx[1])
    early_y().wait_recv()
    early_half(lane, e_ry[...])
    later = pl.ds(EARLY_ROWS, DEC_ROWS - EARLY_ROWS)
    rest = [pltpu.make_async_copy(buf.at[lane], o_dec.at[lane], out_s.at[13])] + [
        pltpu.make_async_copy(buf.at[k, :, later, :], o_dec.at[k, :, later, :], out_s.at[14 + n])
        for n, k in enumerate((mate, over, cross))
    ]
    for copy in rest:
        copy.start()
    for copy in outs + rest:
        copy.wait()
    for which in range(2):
        early_core(which).wait_send()
        early_x(which).wait_send()
    early_y().wait_send()
    for n in range(4):
        enc_weight(n).wait_send()
        for kind in range(5):
            dec_weight(n, kind).wait_send()
    for step in range(1, LANES):
        bias_copy(step).wait_send()
    for i in range(blocks):
        give_part(i, 0).wait_send()
        give_part(i, 1).wait_send()
        give_last(i).wait_send()
    for step in range(1, devices):
        decoded_copy(step).wait()


def forward_call(args, half, hid, dff):
    dma = lambda *s: pltpu.SemaphoreType.DMA(s)
    vm = lambda dtype, *shape: pltpu.VMEM(shape, dtype)
    rows = 2 * PAD
    keys = PAD * half // ENC_SIZE
    devices = 2 * LANES
    slab = DD // devices
    kept = [
        ((PAD, D), F32), ((rows, D), F32), ((rows, D), BF16), ((rows, D), BF16),
        ((2, rows, hid), BF16), ((2, rows, hid), BF16), ((2, 3, rows, half), BF16),
        ((2, 2, PAD, keys), BF16), ((2, rows, half), BF16),
        ((3, half, D), BF16), ((half, D), BF16), ((D, hid), BF16), ((hid, D), BF16),
        ((LANES, 2, DEC_ROWS, D), BF16),
    ]
    made = [
        ((PAD, D), BF16), ((2, DD), F32), ((1, dff), F32), ((8, DD), F32),
        ((devices, slab, GRID), BF16),
    ]
    return pl.pallas_call(
        forward_and_decoder,
        out_shape=[jax.ShapeDtypeStruct(s, d) for s, d in kept + made],
        in_specs=[SM, SM, SM] + [VM] * 8 + [ANY] * 9 + [VM] * 5,
        out_specs=[ANY] * len(kept) + [VM] * len(made),
        scratch_shapes=[
            vm(BF16, 2, 3, half, D), vm(BF16, 2, half, D), vm(BF16, 2, D, hid), vm(BF16, 2, hid, D),
            vm(F32, 8, D), vm(F32, LANES, 8, D),
            vm(BF16, 3, DD, DD), vm(BF16, DD, DD), vm(BF16, DD, dff), vm(BF16, dff, DD),
            vm(F32, rows, D), vm(BF16, rows, D), vm(BF16, rows, D), vm(BF16, 2, rows, hid),
            vm(BF16, 2, rows, hid), vm(BF16, 2, 3, rows, half), vm(BF16, 2, 2, PAD, keys),
            vm(BF16, 2, rows, half), vm(F32, rows, D), vm(F32, rows, D), vm(BF16, rows, D),
            vm(BF16, rows, D), vm(BF16, PAD, D), vm(BF16, PAD, D), vm(F32, PAD, D),
            vm(BF16, GRID, DD), vm(F32, GRID, DD), vm(F32, GRID, DD), vm(BF16, GRID, DD),
            vm(BF16, 3, GRID, DD), vm(BF16, GRID // PAD, PAD, DHEADS * PAD), vm(BF16, GRID, DD),
            vm(F32, GRID, DD),
            vm(BF16, GRID, DD), vm(BF16, DD, GRID), vm(BF16, GRID, dff), vm(BF16, GRID, dff),
            vm(F32, GRID, DD), vm(BF16, GRID, DD), vm(BF16, DD, GRID), vm(F32, GRID, DD),
            vm(BF16, PAD, D), vm(BF16, GRID, PAD), vm(BF16, GRID, GRID),
            vm(BF16, LANES, 2, DEC_ROWS, D),
            vm(BF16, devices, slab, GRID), *[vm(BF16, 2, EARLY_ROWS, D)] * 3, vm(BF16, EARLY_ROWS, D),
            dma(8), dma(17), pltpu.SemaphoreType.DMA, dma(4), dma(4), dma(LANES), dma(LANES),
            dma(20), dma(20), dma(6), dma(6), dma(3), dma(3), dma(devices), dma(devices),
            dma(5), dma(5),
        ],
        compiler_params=pltpu.CompilerParams(
            collective_id=0, has_side_effects=True, vmem_limit_bytes=VMEM_LIMIT
        ),
    )(*args)


def add(x, y):
    return x + y


def backward_and_sums(
    d_enc, gains,
    h_u, h_y, h_gp, h_down0, h_down1, h_up0, h_up1,
    h_x, h_x1, h_a, h_qkv, h_p, h_o, h_w0, h_w1, h_proj0, h_proj1,
    dec, dec_qvb, dec_upb, dec_small,
    total, emb, dx_out,
    gb, ut, part, send, recv, du, gx, dx1, d_o, d_acts, own, send1, recv1, dx32, dx,
    d_upb, d_qvb, d_small,
    acc, yacc, enc_mate, out, rcy, ry, land_x, land_l, land_r, small32, small,
    u, y, gp, down0, down1, up0, up1, x, x1, a, qkv, p, o, w0, w1, proj0, proj1, fetch_s,
    load_s, flush_s, ex_s, ex_r,
    core_s, core_r, corey_s, corey_r, y_s, y_r, x_s, x_r, z_s, zl_r, zr_r,
    bl_s, br_s, b_r, a_s, a_r, emb_s, emb_r, dx_s, dx_r,
):
    sec = lax.axis_index("section")
    lane = lax.axis_index("tensor")
    pos = lax.axis_index("dp")
    count = lax.axis_size("dp")
    mate = lane + 1 - 2 * lax.rem(lane, 2)
    over = lax.rem(lane + 2, LANES)
    cross = lax.rem(mate + 2, LANES)
    first = pos == 0
    last = pos == count - 1
    me = sec * LANES + lane
    devices = 2 * LANES

    def group_peer(step):
        peer = lax.rem(me + step, devices)
        return peer, {"section": lax.div(peer, LANES), "tensor": lax.rem(peer, LANES)}

    barrier = pltpu.get_barrier_semaphore()
    for step in range(1, devices):
        pl.semaphore_signal(barrier, inc=1, device_id_type=MESH, device_id=group_peer(step)[1])

    @pl.when(pos > 0)
    def _():
        pl.semaphore_signal(barrier, inc=1, device_id={"dp": pos - 1}, device_id_type=MESH)

    @pl.when(pos < count - 1)
    def _():
        pl.semaphore_signal(barrier, inc=1, device_id={"dp": pos + 1}, device_id_type=MESH)

    loads = [
        pltpu.make_async_copy(dec.at[lane], acc.at[:, 0:DEC_ROWS, :], load_s.at[0]),
        pltpu.make_async_copy(
            dec.at[over, :, EARLY_ROWS:DEC_ROWS, :], yacc.at[:, 0 : DEC_ROWS - EARLY_ROWS, :],
            load_s.at[1],
        ),
    ]
    for load in loads:
        load.start()
    fetches = [
        pltpu.make_async_copy(src, dst, fetch_s.at[n])
        for n, (src, dst) in enumerate(
            (
                (h_u, u), (h_y, y), (h_gp, gp), (h_down0, down0), (h_down1, down1), (h_up0, up0),
                (h_up1, up1), (h_x, x), (h_x1, x1), (h_a, a), (h_qkv, qkv), (h_p, p), (h_o, o),
                (h_w0, w0), (h_w1, w1), (h_proj0, proj0), (h_proj1, proj1),
            )
        )
    ]
    for fetch in fetches:
        fetch.start()
    small32[...] = jnp.zeros_like(small32)
    d_small[...] = jnp.zeros_like(d_small)
    gb[0:PAD, :] = d_enc[...]
    ends = jnp.where(first, 0, 1) + jnp.where(last, 0, 1)
    pl.semaphore_wait(barrier, devices - 1 + ends)

    gain = gains[...].astype(F32)
    width = w0.shape[1]
    marks = head_marks(width, ENC_SIZE, BF16)
    marks32 = head_marks(width, ENC_SIZE, F32)
    ones = ones_per_head(PAD, marks)

    def rows(k, size=CH):
        return pl.ds(pl.multiple_of(k * size, size), size)

    def give_enc():
        return far(d_enc, gb.at[PAD : 2 * PAD, :], ex_s.at[0], ex_r.at[0], {"tensor": over})

    def give_part(i, half):
        cut = rows(i, 256)
        n = 1 + 2 * i + half
        return far(
            send.at[(1 - half) * PAD : (2 - half) * PAD, cut],
            recv.at[half * PAD : (half + 1) * PAD, cut],
            ex_s.at[n], ex_r.at[n], {"tensor": over},
        )

    def give_last(i):
        cut = rows(i, 256)
        return far(send1.at[:, cut], recv1.at[:, cut], ex_s.at[7 + i], ex_r.at[7 + i], {"tensor": over})

    def ff_back(g, i, down):
        c = rows(i, 256)
        d_down = tn(y[g, :, c], gb[...]).astype(BF16)
        dh = nt(gb[...], down[c, :]) * gp[g, :, c].astype(F32)
        d_upb[g, :, c] = colsum(dh)
        dub = dh.astype(BF16)
        du[g, :, c] = dub
        d_up = nn(ut[...], dub).astype(BF16)
        if g == 0:
            acc[1, pl.ds(pl.multiple_of(A_TOP + i * 256, 64), 256), :] = d_down
            acc[0, A_TOP:B_TOP, c] = d_up
        else:
            enc_mate[1, c, :] = d_down
            enc_mate[0, 0:ENC_A, c] = d_up

    def ff_in(i):
        c = rows(i, 256)
        t = nt(du[0], up0[c, :]) + nt(du[1], up1[c, :])
        part[:, c] = t
        send[:, c] = t.astype(BF16)
        give_part(i, 0).start()
        give_part(i, 1).start()

    def norm_two():
        for fetch in fetches[7:]:
            fetch.wait()
        for k in range(D // 256):
            give_part(k, 0).wait_recv()
            give_part(k, 1).wait_recv()

        def body(j):
            r = rows(j, 64)
            da = part[r, :] + recv[r, :].astype(F32)
            hat, scale = normal(x1[r, :])
            g = gb[r, :].astype(F32)
            d = g + normal_back(da, hat, scale, gain[1:2])
            gx[r, :] = d.astype(BF16)
            dx1[r, :] = d

            @pl.when(j < 2)
            def _():
                d_small[1:2, :] += colsum(da * hat)
                d_small[3:4, :] += colsum(da)
                d_small[4:5, :] += colsum(d)
                d_small[5:6, :] += colsum(g)

        loop(2 * PAD // 64, body)

    def attention(g, c):
        if c == 0:
            d_proj = tn(o[g], gx[...]).astype(BF16)
            if g == 0:
                acc[1, B_TOP + width : S_TOP, :] = d_proj
            else:
                enc_mate[1, ENC_A + width : ENC_A + 2 * width, :] = d_proj
            d_o[...] = nt(gx[...], (proj0, proj1)[g][...]).astype(BF16)
        r = slice(c * PAD, (c + 1) * PAD)
        d_acts[g, 0, r], d_acts[g, 1, r], d_acts[g, 2, r] = attend_back(
            qkv[g, 0, r], qkv[g, 1, r], qkv[g, 2, r], p[g, c], o[g, r], 1.0 / nn(p[g, c], ones),
            d_o[r, :], marks, marks32, None, ones, ENC_SCALE,
        )
        if c == 1:
            d_qvb[g, 0:1, :] = colsum(d_acts[g, 0].astype(F32))
            d_qvb[g, 1:2, :] = colsum(d_acts[g, 2].astype(F32))

    def project_in(i):
        c = rows(i, 256)
        t = 0.0
        for g, w in enumerate((w0, w1)):
            for j in range(3):
                t += nn(d_acts[g, j], w[j, :, c])
        own[:, c] = t[:PAD]
        send1[:, c] = t[PAD:].astype(BF16)
        give_last(i).start()

    def project_grad(g):
        for j in range(3):
            row = (j % 2) * width
            d = tn(d_acts[g, j], a[...]).astype(BF16)
            if g == 0:
                acc[j // 2, B_TOP + row : B_TOP + row + width, :] = d
            else:
                enc_mate[j // 2, ENC_A + row : ENC_A + row + width, :] = d

    def norm_one():
        for k in range(D // 256):
            give_last(k).wait_recv()

        def body(j):
            r = rows(j, 64)
            da = own[r, :] + recv1[r, :].astype(F32)
            hat, scale = normal(x[r, :])
            d_small[0:1, :] += colsum(da * hat)
            d_small[2:3, :] += colsum(da)
            dx32[r, :] = dx1[r, :] + normal_back(da, hat, scale, gain[0:1])

        loop(PAD // 64, body)
        turned = jnp.transpose(dx32[...])
        cut = D // devices
        for k in range(devices):
            dx[k] = turned[k * cut : (k + 1) * cut, 0:VIS].astype(BF16)
        for r in range(LANES):
            small32[r, 8:9, 0:512] = dec_upb[:, r * 512 : (r + 1) * 512]
            small32[r, 9:10, 0:128] = dec_qvb[0:1, r * 128 : (r + 1) * 128]
            small32[r, 9:10, 128:256] = dec_qvb[1:2, r * 128 : (r + 1) * 128]
            small32[r, 0:8, 0:512] = dec_small[...]
            small32[r, 16:24, :] = d_small[...]
        for g, shard in enumerate((lane, mate)):
            small32[shard, 10:11, :] = d_upb[g]
            small32[shard, 11:12, 0:192] = d_qvb[g, 0:1]
            small32[shard, 11:12, 256:448] = d_qvb[g, 1:2]
        for r in range(LANES):
            for h in range(2):
                small[r, h] = small32[r, h * SMALL : (h + 1) * SMALL].astype(BF16)
        acc[:, S_TOP : S_TOP + SMALL, :] = small[lane]
        yacc[:, DEC_ROWS - EARLY_ROWS :, :] = small[over]
        core_copy(LATE, small.at[mate], SMALL).start()
        corey_copy(LATE, small.at[cross], SMALL).start()
        for step in range(1, devices):
            dx_copy(step).start()
        dx_out[me] = dx[me]

    def core_enc(lo, hi):
        for m, block in enumerate(ORDER):
            if lo <= block < hi:
                src = pl.ds(block * CH - DEC_ROWS, CH)
                core_copy(m, enc_mate.at[:, src, :]).start()

    def first_piece():
        for fetch in fetches[:7]:
            fetch.wait()
        ut[...] = jnp.transpose(u[...])
        give_enc().wait_recv()

    def ff_step(k):
        for g, down in enumerate((down0, down1)):
            @pl.when(lax.rem(k, 2) == g)
            def _(g=g, down=down):
                ff_back(g, lax.div(k, 2), down)

    def run_pieces(n):
        def several(low, high, body):
            begin = sum(jnp.where(n > t, 1, 0) for t in PIECES[low:high])
            end = sum(jnp.where(n >= t, 1, 0) for t in PIECES[low:high])
            lax.fori_loop(begin, end, lambda k, c: (body(k), c)[1], 0)

        def single(k, body):
            @pl.when(n == PIECES[k])
            def _():
                body()

        single(0, first_piece)
        several(1, 7, ff_step)
        single(7, lambda: core_enc(DEC_K, DEC_K + ENC_A // CH))
        several(8, 11, ff_in)
        single(11, norm_two)
        for k in range(4):
            single(12 + k, lambda k=k: attention(k // 2, k % 2))
        several(16, 19, project_in)
        for g in range(2):
            single(19 + g, lambda g=g: project_grad(g))
        single(21, lambda: core_enc(DEC_K + ENC_A // CH, B_K))
        single(22, norm_one)

    def dx_copy(step):
        peer, place = group_peer(step)
        return far(dx.at[peer], dx_out.at[me], dx_s.at[step], dx_r.at[step], place)

    def emb_copy(step):
        return far(
            out.at[:, pl.ds(512, CH), :], emb.at[lane], emb_s.at[step], emb_r.at[step],
            {"tensor": lax.rem(lane + step, LANES)},
        )

    def block_of(m):
        if isinstance(m, int):
            return ORDER[m]
        shift = 0
        for k in range(1, ALL_K):
            if ORDER[k] - k != ORDER[k - 1] - k + 1:
                shift = jnp.where(m >= k, ORDER[k] - k, shift)
        return m + shift

    def is_dec(m):
        return (block_of(m) < DEC_K) & (m >= EARLY)

    def at(m, size=CH):
        if isinstance(m, int):
            return pl.ds(ORDER[m] * CH, size)
        return pl.ds(pl.multiple_of(block_of(m) * CH, CH), size)

    def slot(m, size=CH):
        if isinstance(m, int):
            return pl.ds(m * CH, size)
        return pl.ds(pl.multiple_of(m * CH, CH), size)

    def y_at(m, size=CH):
        if isinstance(m, int):
            return pl.ds((min(ORDER[m], DEC_K) - EARLY) * CH, size)
        return pl.ds(pl.multiple_of((jnp.minimum(block_of(m), DEC_K) - EARLY) * CH, CH), size)

    def core_copy(m, src, size=CH):
        return far(src, out.at[:, at(m, size), :], core_s.at[m], core_r.at[m], {"tensor": mate})

    def corey_copy(m, src, size=CH):
        return far(src, rcy.at[:, y_at(m, size), :], corey_s.at[m], corey_r.at[m], {"tensor": mate})

    def y_copy(m, size=CH):
        cut = y_at(m, size)
        return far(
            yacc.at[:, cut, :], ry.at[:, cut, :], y_s.at[m], y_r.at[m], {"tensor": over}
        )

    def x_copy(m, size=CH):
        return far(
            acc.at[1 - sec, at(m, size), :], land_x.at[0, slot(m, size), :], x_s.at[m], x_r.at[m],
            {"section": 1 - sec},
        )

    def xc_copy(m):
        return far(
            acc.at[:, at(m), :], land_x.at[:, slot(m), :], x_s.at[m], x_r.at[m],
            {"section": 1 - sec},
        )

    def z_copy(m, whole, right, size=CH):
        land = land_l if right else land_r
        if whole:
            src, dst = acc.at[:, at(m), :], land.at[:, slot(m), :]
        else:
            src, dst = acc.at[sec, at(m, size), :], land.at[0, slot(m, size), :]
        landed = zl_r if right else zr_r
        return far(src, dst, z_s.at[m], landed.at[m], {"dp": pos + 1 if right else pos - 1})

    def b_copy(m, whole, right, size=CH):
        place = out.at[:, at(m), :] if whole else out.at[sec, at(m, size), :]
        sent = br_s if right else bl_s
        return far(place, place, sent.at[m], b_r.at[m], {"dp": pos + 1 if right else pos - 1})

    def a_copy(m, size=CH):
        place = out.at[sec, at(m, size), :]
        return far(place, place, a_s.at[m], a_r.at[m], {"section": 1 - sec})

    def a_wait(m, size=CH):
        place = out.at[1 - sec, at(m, size), :]
        far(place, place, a_s.at[m], a_r.at[m], {"section": 1 - sec}).wait_recv()

    give_enc().start()

    for m in range(EARLY, ALL_K):
        if ORDER[m] < DEC_K:
            core_copy(m, dec.at[mate, :, at(m), :]).start()
            corey_copy(m, dec.at[cross, :, at(m), :]).start()
    for load in loads:
        load.wait()

    def join_core(m, size):
        core_copy(m, out.at[:, at(m, size), :], size).wait_recv()
        acc[:, at(m, size), :] = add(acc[:, at(m, size), :], out[:, at(m, size), :])

    def join_core_y(m, size):
        corey_copy(m, rcy.at[:, y_at(m, size), :], size).wait_recv()
        yacc[:, y_at(m, size), :] = add(yacc[:, y_at(m, size), :], rcy[:, y_at(m, size), :])
        y_copy(m, size).start()

    def stage_c(m):
        @pl.when((m >= EARLY) & (m != LATE))
        def _():
            join_core(m, CH)

            @pl.when(is_dec(m))
            def _():
                join_core_y(m, CH)

        @pl.when(m == LATE)
        def _():
            join_core(m, SMALL)
            join_core_y(m, SMALL)

    def flush(m):
        return pltpu.make_async_copy(
            out.at[:, at(m), :], total.at[:, at(m), :], flush_s.at[m]
        )

    def finished(m):
        flush(m).start()

        @pl.when(block_of(m) == DEC_K - 1)
        def _():
            for step in range(1, LANES):
                emb_copy(step).start()
            emb[lane] = out[:, 512 : 512 + CH, :]

    def line_of(root, whole, size=CH):
        left = pos < root
        right = pos > root
        here = pos == root
        reach = max(root, count - 1 - root)
        level = jnp.where(left, pos, jnp.where(right, count - 1 - pos, reach))
        dist = jnp.where(left, root - pos, pos - root)

        def view(ref, m):
            return ref.at[:, at(m), :] if whole else ref.at[sec, at(m, size), :]

        def landed(ref, m):
            return ref.at[:, slot(m), :] if whole else ref.at[0, slot(m, size), :]

        def hop(m, rightward):
            return z_copy(m, whole, rightward, size)

        def back_hop(m, rightward):
            return b_copy(m, whole, rightward, size)

        def outer(m):
            @pl.when(left & first)
            def _():
                hop(m, True).start()

            @pl.when(right & last)
            def _():
                hop(m, False).start()

        def inward(m):
            @pl.when(left & (pos > 0))
            def _():
                hop(m, True).wait_recv()
                view(acc, m)[...] = add(view(acc, m)[...], landed(land_l, m)[...])
                hop(m, True).start()

            @pl.when(right & (pos < count - 1))
            def _():
                hop(m, False).wait_recv()
                view(acc, m)[...] = add(view(acc, m)[...], landed(land_r, m)[...])
                hop(m, False).start()

            @pl.when(here)
            def _():
                total = view(acc, m)[...].astype(F32)
                if root > 0:
                    hop(m, True).wait_recv()
                    total = total + landed(land_l, m)[...].astype(F32)
                if root < count - 1:
                    hop(m, False).wait_recv()
                    total = total + landed(land_r, m)[...].astype(F32)
                if whole:
                    view(acc, m)[...] = total.astype(BF16)
                    xc_copy(m).start()
                else:
                    view(out, m)[...] = total.astype(BF16)
                    spread(m)
                    a_copy(m, size).start()

        def spread(m):
            if root > 0:
                back_hop(m, False).start()
            if root < count - 1:
                back_hop(m, True).start()

        def crossed(m):
            xc_copy(m).wait_recv()
            view(out, m)[...] = add(view(acc, m)[...], landed(land_x, m)[...])
            spread(m)
            finished(m)

        def outward(m):
            back_hop(m, False).wait_recv()

            @pl.when(left & (pos > 0))
            def _():
                back_hop(m, False).start()

            @pl.when(right & (pos < count - 1))
            def _():
                back_hop(m, True).start()

            if whole:
                finished(m)
            else:
                a_copy(m, size).start()

        def sent(m):
            @pl.when(jnp.logical_not(here))
            def _():
                hop(m, True).wait_send()

            @pl.when((pos <= root) & (pos > 0))
            def _():
                back_hop(m, False).wait_send()

            @pl.when((pos >= root) & (pos < count - 1))
            def _():
                back_hop(m, True).wait_send()

            if whole:
                @pl.when(here)
                def _():
                    xc_copy(m).wait_send()
            else:
                a_copy(m, size).wait_send()

                @pl.when(crosses_first(m))
                def _():
                    x_copy(m, size).wait_send()

        def crosses_first(m):
            return m >= EARLY if XFIRST else m >= 0

        def set_off(m):
            if whole:
                outer(m)
            else:
                x_copy(m, size).start()

        def set_off_early(m):
            if XFIRST:
                outer(m)
            else:
                set_off(m)

        def add_y(m):
            def joined():
                y_copy(m, size).wait_recv()
                acc[:, at(m, size), :] = add(acc[:, at(m, size), :], ry[:, y_at(m, size), :])

            if size == CH:
                pl.when(is_dec(m))(joined)
            else:
                joined()
            set_off(m)

        def add_x(m):
            @pl.when(crosses_first(m))
            def _():
                x_copy(m, size).wait_recv()
                acc[sec, at(m, size), :] = add(
                    acc[sec, at(m, size), :], land_x[0, slot(m, size), :]
                )
                outer(m)

        def last_half(m):
            a_wait(m, size)
            finished(m)

        base = 1 if whole else 2
        back = base + reach + dist + (1 if whole else 0)
        steps = {
            "outward": (back, jnp.logical_not(here), outward),
            "inward": (base + level, level > 0, inward),
            "add_y": (1, True, add_y),
        }
        if whole:
            steps["crossed"] = (base + reach + 1, here, crossed)
        else:
            steps["last"] = (back + 1, True, last_half)
            steps["add_x"] = (2, True, add_x)
        return steps, sent, set_off_early

    low_root = (count - 1) // 2
    high_root = min(low_root + 1, count - 1)
    def is_whole(m):
        return (lax.rem(m, 2) == 0) & (m >= WHOLE_LOW) & (m < WHOLE_HIGH)

    roots = (high_root, count - 1, low_root, 0)
    lines = [
        (lambda m, part=part: is_whole(m) & (lax.rem(m, 8) == part), *line_of(root, True))
        for part, root in zip((0, 2, 4, 6), roots)
    ] + [
        (lambda m: jnp.logical_not(is_whole(m)) & (m != LATE), *line_of(low_root, False)),
        (lambda m: m == LATE, *line_of(low_root, False, SMALL)),
    ]

    def finish(m):
        @pl.when((m >= EARLY) & (m != LATE))
        def _():
            core_copy(m, out.at[:, at(m), :]).wait_send()

            @pl.when(is_dec(m))
            def _():
                corey_copy(m, rcy.at[:, y_at(m), :]).wait_send()
                y_copy(m).wait_send()

        @pl.when(m == LATE)
        def _():
            core_copy(m, out.at[:, at(m, SMALL), :], SMALL).wait_send()
            corey_copy(m, rcy.at[:, y_at(m, SMALL), :], SMALL).wait_send()
            y_copy(m, SMALL).wait_send()

        for mine, _, sent, _ in lines:
            @pl.when(mine(m))
            def _(sent=sent):
                sent(m)

    for m in range(EARLY):
        lines[-2][-1](m)
    far_reach = max(max(root, count - 1 - root) for root in roots)
    depth = LAG * (3 + 2 * far_reach) + 1

    def tick(n):
        @pl.when(n <= PIECES[-1])
        def _():
            run_pieces(n)

        def run(line, name):
            mine, steps, _, _ = line
            if name not in steps:
                return
            offset, enabled, stage = steps[name]
            m = n - LAG * offset
            least = EARLY if name == "add_y" else 0

            @pl.when((m >= least) & (m < ALL_K) & enabled)
            def _():
                @pl.when(mine(m))
                def _():
                    stage(m)

        for name in ("add_y", "add_x", "inward", "crossed", "outward", "last"):
            if name not in ("last", "add_x"):
                @pl.when((lax.rem(n, 2) == 0) & (n >= WHOLE_LOW) & (n < WHOLE_HIGH + depth))
                def _(name=name):
                    for line in lines[:-2]:
                        run(line, name)

            run(lines[-2], name)
            if name != "crossed":
                @pl.when((n >= LATE) & (n < LATE + depth))
                def _(name=name):
                    run(lines[-1], name)

        @pl.when(n < ALL_K)
        def _():
            stage_c(n)

        @pl.when(n >= depth)
        def _():
            finish(n - depth)

    loop(ALL_K + depth, tick)
    loop(ALL_K, lambda m: flush(m).wait())
    for step in range(1, devices):
        dx_copy(step).wait()
    for step in range(1, LANES):
        emb_copy(step).wait()
    give_enc().wait_send()
    for k in range(D // 256):
        give_part(k, 0).wait_send()
        give_part(k, 1).wait_send()
        give_last(k).wait_send()


def backward_call(args, half, hid):
    dma = lambda *s: pltpu.SemaphoreType.DMA(s)
    vm = pltpu.VMEM
    full = ALL_K * CH
    y_half = DEC_ROWS - EARLY_ROWS + SMALL
    k = ALL_K
    rows = 2 * PAD
    cut = D // (2 * LANES)
    specs = [VM, VM] + [ANY] * 18 + [VM] * 3
    return pl.pallas_call(
        backward_and_sums,
        out_shape=[
            jax.ShapeDtypeStruct((2, full, D), BF16),
            jax.ShapeDtypeStruct((LANES, 2, CH, D), BF16),
            jax.ShapeDtypeStruct((2 * LANES, cut, VIS), BF16),
        ],
        in_specs=specs,
        out_specs=[ANY, VM, VM],
        scratch_shapes=[
            vm((rows, D), BF16), vm((D, rows), BF16),
            vm((rows, D), F32), vm((rows, D), BF16), vm((rows, D), BF16),
            vm((2, rows, hid), BF16), vm((rows, D), BF16), vm((rows, D), F32),
            vm((rows, half), BF16), vm((2, 3, rows, half), BF16),
            vm((PAD, D), F32), vm((PAD, D), BF16), vm((PAD, D), BF16), vm((PAD, D), F32),
            vm((2 * LANES, cut, VIS), BF16),
            vm((2, 1, hid), F32), vm((2, 2, half), F32), vm((8, D), F32),
            vm((2, full, D), BF16), vm((2, y_half, D), BF16), vm((2, ENC_A + ENC_B, D), BF16),
            vm((2, full, D), BF16),
            vm((2, y_half, D), BF16), vm((2, y_half, D), BF16),
            *[vm((2, full, D), BF16)] * 3,
            vm((LANES, 32, D), F32), vm((LANES, 2, SMALL, D), BF16),
            *[vm(v.shape, v.dtype) for v in args[2:19]],
            dma(17), dma(2), dma(k), dma(10), dma(10),
            dma(k), dma(k), dma(k), dma(k), dma(k), dma(k),
            dma(k), dma(k), dma(k), dma(k), dma(k),
            dma(k), dma(k), dma(k), dma(k), dma(k), dma(LANES), dma(LANES),
            dma(2 * LANES), dma(2 * LANES),
        ],
        compiler_params=pltpu.CompilerParams(
            collective_id=1, has_side_effects=True, vmem_limit_bytes=VMEM_LIMIT
        ),
    )(*args)


def finish_grads(
    total, emb, decoded, dx, decoded_out, dx_out,
    e_qkv, e_qvb, e_proj, e_up, e_upb, e_down, e_gain, e_off,
    d_qkv, d_qvb, d_proj, d_up, d_upb, d_down, d_gain, d_off, d_ew, d_ev,
):
    half = e_proj.shape[0]
    decoded_out[...] = decoded[...]
    dx_out[...] = dx[...]
    e_up[...] = total[0, A_TOP:B_TOP, :].astype(F32)
    e_down[...] = total[1, A_TOP:B_TOP, :].astype(F32)
    e_qkv[0] = total[0, B_TOP : B_TOP + half, :].astype(F32)
    e_qkv[1] = total[0, B_TOP + half : S_TOP, :].astype(F32)
    e_qkv[2] = total[1, B_TOP : B_TOP + half, :].astype(F32)
    e_proj[...] = total[1, B_TOP + half : S_TOP, :].astype(F32)

    def raw(number):
        h, top, col = tile_of(number)
        return total[h, top : top + CH, col : col + 256]

    def tile(number):
        return raw(number).astype(F32)

    for block in range(GRID // CH):
        rows = slice(block * CH, (block + 1) * CH)
        side = slice(block // 2 * 128, (block // 2 + 1) * 128)
        for k in range(2):
            d_up[rows, k * 256 : (k + 1) * 256] = tile(4 * block + k)
            if block % 2:
                both = jnp.concatenate([raw(4 * block - 2 + k), raw(4 * block + 2 + k)], 0)
                d_down[k * 256 : (k + 1) * 256, side] = jnp.transpose(both).astype(F32)
        one, two = tile(32 + 2 * block), tile(33 + 2 * block)
        d_qkv[0, rows, :] = one[:, 0:128]
        d_qkv[1, rows, :] = one[:, 128:256]
        d_qkv[2, rows, :] = two[:, 0:128]
        d_proj[block % 2 * CH : (block % 2 + 1) * CH, side] = two[:, 128:256]
    for k in range(LANES):
        for h in range(2):
            top = k * 192 + h * 64
            d_ew[top : top + 64, :] = emb[k, h, :, 0:512].astype(F32)
            d_ew[k * 192 + 128 : (k + 1) * 192, h * 256 : (h + 1) * 256] = emb[
                k, h, :, 512:768
            ].astype(F32)
    little = total[0, S_TOP : S_TOP + SMALL, :].astype(F32)
    d_gain[...] = little[0:2, 0:512]
    d_off[...] = little[2:6, 0:512]
    d_ev[...] = little[6:8, 0:512]
    d_upb[...] = little[8, 0:512]
    d_qvb[0:1, :] = little[9:10, 0:128]
    d_qvb[1:2, :] = little[9:10, 128:256]
    e_upb[...] = little[10]
    e_qvb[0:1, :] = little[11:12, 0:192]
    e_qvb[1:2, :] = little[11:12, 256:448]
    little = total[1, S_TOP : S_TOP + SMALL, :].astype(F32)
    e_gain[...] = little[0:2]
    e_off[...] = little[2:6]


def call(kernel, specs, shapes, scratch, args):
    return pl.pallas_call(
        kernel,
        out_shape=[jax.ShapeDtypeStruct(s, d) for s, d in shapes],
        in_specs=specs,
        out_specs=[VM] * len(shapes),
        scratch_shapes=scratch,
        compiler_params=pltpu.CompilerParams(vmem_limit_bytes=VMEM_LIMIT),
    )(*args)


def position_rows():
    quarter = DD // 4
    freq = np.exp(np.arange(quarter, dtype=np.float32) * np.float32(-math.log(10000.0) / quarter))
    angle = np.arange(PAD, dtype=np.float32)[:, None] * freq[None, :].astype(np.float32)
    both = np.concatenate([np.sin(angle), np.cos(angle)], 1).astype(np.float32)
    high = both.astype(jnp.bfloat16)
    low = (both - high.astype(np.float32)).astype(jnp.bfloat16)
    return np.stack([high, low])


def per_device(
    patches, cotangent, widths, visible, window_shift, batch_order,
    encoder_qkv, encoder_qvbias, encoder_proj, encoder_up, encoder_upbias, encoder_down,
    encoder_gains, encoder_offsets,
    decoder_qkv, decoder_qvbias, decoder_proj, decoder_up, decoder_upbias, decoder_down,
    decoder_gains, decoder_offsets, embed_weight, embed_vectors,
):
    qkv0 = encoder_qkv.transpose(1, 2, 0)
    half = qkv0.shape[1]
    hid = encoder_up.shape[1]
    dff = decoder_up.shape[1] * LANES
    flat = patches.transpose(1, 0, 2).reshape(-1, D)
    (
        x, x1, a, u, y, gp, qkv, p, o, qkv1, proj1, up1, down1, dec_buf,
        d_enc, d_dqvb, d_dupb, d_dsmall, out_all,
    ) = forward_call(
        (
            widths, window_shift.T, batch_order, visible, flat, encoder_gains, encoder_offsets,
            encoder_qvbias, encoder_upbias, decoder_qvbias, decoder_upbias,
            qkv0, encoder_proj, encoder_up, encoder_down,
            decoder_qkv.transpose(1, 0, 2), decoder_proj, decoder_up, decoder_down,
            cotangent, embed_weight, embed_vectors, jnp.asarray(position_rows()),
            decoder_gains, decoder_offsets,
        ),
        half, hid, dff,
    )
    total, emb, dx_all = backward_call(
        (
            d_enc, encoder_gains, u, y, gp, encoder_down, down1, encoder_up, up1,
            x, x1, a, qkv, p, o, qkv0, qkv1, encoder_proj, proj1,
            dec_buf, d_dqvb, d_dupb, d_dsmall,
        ),
        half, hid,
    )
    f = lambda *shape: (shape, F32)
    out_all, dx_all, *grads = call(
        finish_grads, [VM] * 4,
        [
            (out_all.shape, BF16), (dx_all.shape, BF16), f(3, half, D), f(2, half), f(half, D), f(D, hid), f(hid), f(hid, D), f(2, D), f(4, D),
            f(3, DD, 128), f(2, 128), f(128, DD), f(DD, 512), f(512), f(512, DD), f(2, DD), f(4, DD),
            f(D, DD), f(2, DD),
        ],
        [], (total, emb, out_all, dx_all),
    )
    grads[0] = grads[0].transpose(2, 0, 1)
    grads[8] = grads[8].transpose(1, 0, 2)
    return (out_all.swapaxes(1, 2), dx_all.swapaxes(1, 2), *grads)


def solution(mesh):
    weights = (
        P(None, None, "tensor"), P(None, "tensor"), P("tensor", None), P(None, "tensor"),
        P("tensor"), P("tensor", None), P(), P(),
    )
    split = P("dp", None, ("section", "tensor"))
    return jax.shard_map(
        per_device,
        mesh=mesh,
        in_specs=(
            P("dp", None, None), P("dp", None, None), P("dp"), P("dp", None), P("dp", None),
            P("dp", None),
        ) + weights + weights + (P(), P()),
        out_specs=(split, split) + weights + weights + (P(), P()),
        check_vma=False,
    )
```
